32 devices in a mesh: space: 8 (over y, x, core), vel: 4 (over z).
Axes of the slice: x: 2, y: 2, z: 4, core: 2. Of those that a mesh axis runs over, the one named last changes fastest.
Arguments:
- particle_profile: float32 [64, 262144], P('space', 'vel'), as said below
- neighbors: int32 [6, 64], P(None, 'space'), may hold values from -1 to 63, as said below
- face_vectors: float32 [3, 6, 64], P(None, None, 'space'), may hold values from -0.8 to 0.8, as said below
- volumes: float32 [64], P('space'), may hold values from 2 to 4
- wall_temp: float32 [64], P('space'), may hold values from 0.5 to 1.5
Outputs:
- evolved: float32 [64, 262144], P('space', 'vel')
- macro_quantities: float32 [8, 64], P(None, 'space')
The draws below stay inside these ranges and needn't reach their ends.
Inputs may be any that keep to these rules, and one draw needn't show every extreme that they name: neighbors[k, g] is -1 or a cell other than g at most 3 cells away from g in cell order; face 0 of an even cell points 3 cells ahead and of an odd cell 3 cells behind, or is -1 where that leaves the mesh. `face_vectors`: every component has a magnitude between 0.3 and 0.8. `particle_profile`: positive.
All inputs are finite; a program needn't handle non-finite values.
Results may differ from the reference program's by a relative error of at most 0.00015.
Values sent between devices are 32-bit elements; how exact they have to be, the bound alone decides.
No kernel may reach another device: no remote copies, remote signals or barrier semaphores. Data moves between devices by JAX's collectives and lax.ppermute only.
A program may use at most 64 MiB of HBM per device.

```python
import math
import jax
import jax.numpy as jnp
from jax import lax

NV = 64
MESH_SITE_COUNT = 64
FACES = 6
REACH = 3
STEPS = 2


def draw_particle_profile(key, part):
    key = jax.random.fold_in(key, 11)
    stochastic_seeds = jax.random.split(key, 5)
    particle_concentration = jax.random.uniform(stochastic_seeds[0], (MESH_SITE_COUNT, 1), jnp.float32, 0.5, 2.0)
    average_drift = jax.random.uniform(stochastic_seeds[1], (3, MESH_SITE_COUNT, 1), jnp.float32, -0.4, 0.4)
    kinetic_warmth = jax.random.uniform(stochastic_seeds[2], (MESH_SITE_COUNT, 1), jnp.float32, 0.7, 1.4)
    skew = jax.random.uniform(stochastic_seeds[4], (3, MESH_SITE_COUNT, 1), jnp.float32, -0.3, 0.3)
    warmth_sqrt = jnp.sqrt(kinetic_warmth)
    spacing = 12.0 / NV
    flat_index = jnp.arange(NV * NV * NV, dtype=jnp.int32)
    axes_index = [flat_index // (NV * NV), flat_index // NV % NV, flat_index % NV]
    magnitude_square = jnp.zeros((MESH_SITE_COUNT, NV * NV * NV), jnp.float32)
    projected_motion = jnp.zeros((MESH_SITE_COUNT, NV * NV * NV), jnp.float32)
    for direction_label in range(3):
        position_entry = -6.0 + (axes_index[direction_label].astype(jnp.float32) + 0.5) * spacing
        normalized_entry = (position_entry[None, :] - average_drift[direction_label]) / warmth_sqrt
        magnitude_square = magnitude_square + normalized_entry * normalized_entry
        projected_motion = projected_motion + normalized_entry * skew[direction_label]
    shape_coefficient = 1.0 + 0.6 * jnp.tanh(0.5 * projected_motion * (magnitude_square - 5.0))
    accommodation_share = jax.random.uniform(stochastic_seeds[3], (MESH_SITE_COUNT, NV * NV * NV), jnp.float32, 0.5, 1.5)
    return particle_concentration * kinetic_warmth ** (-1.5) * jnp.exp(-0.5 * magnitude_square) * shape_coefficient * accommodation_share


def draw_neighbors(key, part):
    key = jax.random.fold_in(key, 23)
    stochastic_seeds = jax.random.split(key, 3)
    cell_ids = jnp.arange(MESH_SITE_COUNT, dtype=jnp.int32)[None, :]
    distance = jax.random.randint(stochastic_seeds[0], (FACES, MESH_SITE_COUNT), 1, REACH + 1)
    signs = jax.random.randint(stochastic_seeds[1], (FACES, MESH_SITE_COUNT), 0, 2) * 2 - 1
    first_face = jnp.where(cell_ids % 2 == 0, REACH, -REACH)
    offsets = jnp.concatenate([first_face, (distance * signs)[1:]], axis=0)
    walls = jax.random.randint(stochastic_seeds[2], (FACES, MESH_SITE_COUNT), 0, 8) == 0
    walls = jnp.concatenate([jnp.zeros((1, MESH_SITE_COUNT), dtype=walls.dtype), walls[1:]], axis=0)
    relaxed_state = cell_ids + offsets
    outside = (relaxed_state < 0) | (relaxed_state >= MESH_SITE_COUNT)
    return jnp.where(outside | walls, -1, relaxed_state).astype(jnp.int32)


def draw_face_vectors(key, part):
    key = jax.random.fold_in(key, 37)
    first_key, second_key = jax.random.split(key)
    magnitude = jax.random.uniform(first_key, (3, FACES, MESH_SITE_COUNT), jnp.float32, 0.3, 0.8)
    signs = jax.random.randint(second_key, (3, FACES, MESH_SITE_COUNT), 0, 2) * 2 - 1
    return magnitude * signs.astype(jnp.float32)


def block_scale(stream_key, extent, cuts, smallest, high):
    gain, own = 1.0, jax.random.fold_in(stream_key, 6)
    for axis_at, parts in cuts:
        steps = jnp.exp(jax.random.uniform(jax.random.fold_in(own, axis_at), (parts,), jnp.float32, smallest / len(cuts), high / len(cuts)))
        gain = gain * jnp.repeat(steps, extent[axis_at] // parts).reshape([-1 if axis == axis_at else 1 for axis in range(len(extent))])
    return gain


def setup_inputs(seed: int = 0) -> dict:
    seeds = jax.random.split(jax.random.key(seed), 6)
    particle_profile = draw_particle_profile(jax.random.fold_in(seeds[5], 71), 0)
    neighbors = draw_neighbors(jax.random.fold_in(seeds[5], 71), 0)
    face_vectors = draw_face_vectors(jax.random.fold_in(seeds[5], 71), 0)
    volumes = jnp.clip(2.0 + 2.0 * jax.random.uniform(seeds[3], (MESH_SITE_COUNT,), jnp.float32) ** block_scale(seeds[3], (MESH_SITE_COUNT,), ((0, 8),), -0.2, 0.2), 2.0, 4.0)
    wall_temp = jnp.clip(0.5 + 1.0 * jax.random.uniform(seeds[4], (MESH_SITE_COUNT,), jnp.float32) ** block_scale(seeds[4], (MESH_SITE_COUNT,), ((0, 8),), -0.2, 0.2), 0.5, 1.5)
    return {"particle_profile": particle_profile, "neighbors": neighbors, "face_vectors": face_vectors, "volumes": volumes, "wall_temp": wall_temp}


speed_limit = 6.0
time_step = 0.015
baseline_shear_coefficient = 0.1
power_law_index = 0.81
diffusivity_ratio = 2.0 / 3.0


def velocity_grid(first_plane, plane_count, points):
    spacing = 2.0 * speed_limit / points
    flat_index = jnp.arange(plane_count * points * points, dtype=jnp.int32)
    first_axis = flat_index // (points * points) + first_plane
    second_axis = (flat_index // points) % points
    third_axis = flat_index % points
    stacked = jnp.stack([first_axis, second_axis, third_axis]).astype(jnp.float32)
    return -speed_limit + (stacked + 0.5) * spacing


def quadrature_weight(points):
    spacing = 2.0 * speed_limit / points
    return spacing ** 3 * (2.0 * math.pi) ** -1.5


def face_speed(vectors, abscissa_nodes):
    return vectors[0][:, None] * abscissa_nodes[0][None, :] + vectors[1][:, None] * abscissa_nodes[1][None, :] + vectors[2][:, None] * abscissa_nodes[2][None, :]


def corrected_relaxed_state(particle_concentration, average_drift, kinetic_warmth, energy_current, abscissa_nodes):
    peculiar = [abscissa_nodes[direction_label][None, :] - average_drift[direction_label][:, None] for direction_label in range(3)]
    magnitude_square = peculiar[0] ** 2 + peculiar[1] ** 2 + peculiar[2] ** 2
    reciprocal_warmth = 1.0 / kinetic_warmth[:, None]
    gaussian_state = particle_concentration[:, None] * reciprocal_warmth ** 1.5 * jnp.exp(-0.5 * magnitude_square * reciprocal_warmth)
    isotropic_stress = particle_concentration * kinetic_warmth
    projected_motion = peculiar[0] * energy_current[0][:, None] + peculiar[1] * energy_current[1][:, None] + peculiar[2] * energy_current[2][:, None]
    leading_coefficient = 1.0 + (1.0 - diffusivity_ratio) * projected_motion / (5.0 * isotropic_stress * kinetic_warmth)[:, None] * (magnitude_square * reciprocal_warmth - 5.0)
    return gaussian_state * leading_coefficient


def integral_quantities(particle_profile, abscissa_nodes, quadrature_coefficients):
    particle_concentration = quadrature_coefficients * jnp.sum(particle_profile, axis=1)
    average_drift = quadrature_coefficients * jnp.einsum("iv,cv->ic", abscissa_nodes, particle_profile, precision=lax.Precision.HIGHEST) / particle_concentration
    peculiar = [abscissa_nodes[direction_label][None, :] - average_drift[direction_label][:, None] for direction_label in range(3)]
    magnitude_square = peculiar[0] ** 2 + peculiar[1] ** 2 + peculiar[2] ** 2
    kinetic_warmth = quadrature_coefficients * jnp.sum(particle_profile * magnitude_square, axis=1) / (3.0 * particle_concentration)
    energy_current = 0.5 * jnp.stack([quadrature_coefficients * jnp.sum(particle_profile * magnitude_square * component, axis=1) for component in peculiar])
    return particle_concentration, average_drift, kinetic_warmth, energy_current


def advance(particle_profile, neighbors, face_vectors, volumes, wall_temp, abscissa_nodes, quadrature_coefficients):
    particle_concentration, average_drift, kinetic_warmth, energy_current = integral_quantities(particle_profile, abscissa_nodes, quadrature_coefficients)
    relaxed_state = corrected_relaxed_state(particle_concentration, average_drift, kinetic_warmth, energy_current, abscissa_nodes)
    relaxation_rate = particle_concentration * kinetic_warmth / (baseline_shear_coefficient * kinetic_warmth ** power_law_index)
    squared_speed = jnp.sum(abscissa_nodes * abscissa_nodes, axis=0)
    wall_shape = wall_temp[:, None] ** -1.5 * jnp.exp(-0.5 * squared_speed[None, :] / wall_temp[:, None])
    flux_sum = jnp.zeros_like(particle_profile)
    for face_id in range(FACES):
        normal_speed = face_speed(face_vectors[:, face_id], abscissa_nodes)
        outgoing = jnp.maximum(normal_speed, 0.0)
        incoming = jnp.minimum(normal_speed, 0.0)
        wall_release_rate = quadrature_coefficients * jnp.sum(outgoing * particle_profile, axis=1)
        wall_intake_rate = -quadrature_coefficients * jnp.sum(incoming * wall_shape, axis=1)
        link_ids = neighbors[face_id]
        across = jnp.take(particle_profile, jnp.maximum(link_ids, 0), axis=0)
        arriving = jnp.where((link_ids < 0)[:, None], (wall_release_rate / wall_intake_rate)[:, None] * wall_shape, across)
        flux_sum = flux_sum + outgoing * particle_profile + incoming * arriving
    return particle_profile - (time_step / volumes)[:, None] * flux_sum + time_step * relaxation_rate[:, None] * (relaxed_state - particle_profile)


def reference(particle_profile, neighbors, face_vectors, volumes, wall_temp):
    abscissa_nodes = velocity_grid(0, NV, NV)
    quadrature_coefficients = quadrature_weight(NV)
    for step_id in range(STEPS):
        particle_profile = advance(particle_profile, neighbors, face_vectors, volumes, wall_temp, abscissa_nodes, quadrature_coefficients)
    particle_concentration, average_drift, kinetic_warmth, energy_current = integral_quantities(particle_profile, abscissa_nodes, quadrature_coefficients)
    macro_quantities = jnp.concatenate([particle_concentration[None], average_drift, kinetic_warmth[None], energy_current])
    return particle_profile, macro_quantities
```

```python
import math

import jax
import jax.numpy as jnp
from jax import lax
from jax.experimental import pallas as pl
from jax.experimental.pallas import tpu as pltpu
from jax.sharding import PartitionSpec as P

NV = 64
FACES = 6
REACH = 3
STEPS = 2
LANES = 128
SUB = 8

TIME_STEP = 0.015
SHEAR = 0.1
POWER = 0.81
SPEED_LIMIT = 6.0
H = 2.0 * SPEED_LIMIT / NV
WEIGHT = H**3 * (2.0 * math.pi) ** (-1.5)

CHUNKS = NV * NV // LANES
TILES = CHUNKS // SUB

FV, VOL, WT, WALL = 0, 18, 19, 20
GEO = 26
EMIT, ABSORB = 13, 19
SUMS = 25

F32 = jnp.float32
VMEM_LIMIT = 40 * 1024 * 1024


def lane_iota():
    return lax.broadcasted_iota(jnp.int32, (SUB, LANES), 1)


def sub_iota():
    return lax.broadcasted_iota(jnp.int32, (SUB, LANES), 0)


def half_of(lane):
    return (lane >= NV).astype(F32)


def third_component(lane):
    c = jnp.where(lane >= NV, lane - NV, lane).astype(F32)
    return -SPEED_LIMIT + (c + 0.5) * H


def tile_nodes(t):
    lane = lane_iota()
    b = (2 * SUB * t + 2 * sub_iota()).astype(F32) + half_of(lane)
    return -SPEED_LIMIT + (b + 0.5) * H, third_component(lane)


def plane_node(first_plane, a):
    return -SPEED_LIMIT + ((first_plane + a).astype(F32) + 0.5) * H


def column(tile, p):
    return jnp.broadcast_to(tile[:, p : p + 1], (SUB, LANES))


def splat(ref, i, g):
    return jnp.broadcast_to(ref[i, pl.ds(g, 1), :], (SUB, LANES))


def total(tile):
    return jnp.broadcast_to(jnp.sum(tile, axis=1, keepdims=True), (SUB, LANES))


def polynomial_sums(native_ref, planes, first_plane):
    half = CHUNKS // 2

    def plane(a, acc):
        xa = plane_node(first_plane, a)
        base = a * CHUNKS
        b0 = b1 = b2 = b3 = None
        for i in range(half):
            y = (2 * i + 1) * H
            hi = native_ref[pl.ds(pl.multiple_of((base + half + i) * SUB, SUB), SUB), :]
            lo = native_ref[pl.ds(pl.multiple_of((base + half - 1 - i) * SUB, SUB), SUB), :]
            s, d = hi + lo, hi - lo
            terms = (s, y * d, (y * y) * s, (y * y * y) * d)
            if i == 0:
                b0, b1, b2, b3 = terms
            else:
                b0, b1, b2, b3 = b0 + terms[0], b1 + terms[1], b2 + terms[2], b3 + terms[3]
        a0, a1, a2 = xa * b0, xa * b1, xa * b2
        aa0, aa1 = xa * a0, xa * a1
        new = (b0, b1, b2, b3, a0, a1, a2, aa0, aa1, xa * aa0)
        return tuple(x + y for x, y in zip(acc, new))

    zero = jnp.zeros((SUB, LANES), F32)
    g00, g01, g02, g03, g10, g11, g12, g20, g21, g30 = lax.fori_loop(0, planes, plane, (zero,) * 10)
    lane = lane_iota()
    e = (half_of(lane) - 0.5) * H
    c = third_component(lane)
    h00, h10, h20, h30 = g00, g10, g20, g30
    h01 = g01 + e * g00
    h11 = g11 + e * g10
    h21 = g21 + e * g20
    h02 = g02 + e * (2.0 * g01 + e * g00)
    h12 = g12 + e * (2.0 * g11 + e * g10)
    h03 = g03 + e * (3.0 * g02 + e * (3.0 * g01 + e * g00))
    return (
        h00,
        h10,
        h01,
        c * h00,
        h20,
        h02,
        c * c * h00,
        h11,
        c * h10,
        c * h01,
        h30 + h12 + c * c * h10,
        h21 + h03 + c * c * h01,
        c * (h20 + h02 + c * c * h00),
    )


def pack_sums(arrays, start):
    lane = lane_iota()
    out = jnp.zeros((SUB, LANES), F32)
    for p, x in enumerate(arrays):
        out = jnp.where(lane == start + p, total(x), out)
    return out


def face_sums(ref, k):
    out = ref[k, pl.ds(0, SUB, stride=SUB), :]
    for s in range(1, SUB):
        out = out + ref[k, pl.ds(s, SUB, stride=SUB), :]
    return out


def wall_tiles(wall_temp):
    rt = 1.0 / wall_temp
    scale = rt * jnp.sqrt(rt)
    out = []
    for t in range(TILES):
        xb, xc = tile_nodes(t)
        out.append(scale * jnp.exp(-0.5 * (xb * xb + xc * xc) * rt))
    return out


def emitted_sums(f_ref, first_row, planes, first_plane, nbr_ref, geo_ref, sums_ref, with_absorbed):
    sums_ref[...] = jnp.zeros_like(sums_ref)

    def cell(g, _):
        for k in range(FACES):

            @pl.when(nbr_ref[k, g] < 0)
            def _():
                v0, v1, v2 = [splat(geo_ref, FV + FACES * i + k, g) for i in range(3)]
                base = []
                for t in range(TILES):
                    xb, xc = tile_nodes(t)
                    base.append(v1 * xb + v2 * xc)
                if with_absorbed:
                    wt = splat(geo_ref, WT, g)
                    shape = wall_tiles(wt)

                def plane(a, acc):
                    out, back = acc
                    xa = plane_node(first_plane, a)
                    sa = v0 * xa
                    if with_absorbed:
                        wa = jnp.exp(-0.5 * xa * xa / wt)
                    for t in range(TILES):
                        s = sa + base[t]
                        f = f_ref[first_row + g, pl.ds(pl.multiple_of((a * TILES + t) * SUB, SUB), SUB), :]
                        out = out + jnp.maximum(s, 0.0) * f
                        if with_absorbed:
                            back = back + jnp.maximum(-s, 0.0) * (wa * shape[t])
                    return out, back

                zero = jnp.zeros((SUB, LANES), F32)
                out, back = lax.fori_loop(0, planes, plane, (zero, zero))
                at = pl.ds(pl.multiple_of(g * SUB, SUB), SUB)
                sums_ref[k, at, :] = out
                if with_absorbed:
                    sums_ref[FACES + k, at, :] = back

        return 0

    lax.fori_loop(0, SUB, cell, 0)


def unpack_geo(geo_in, geo_ref):
    tile = geo_in[...]
    for p in range(GEO):
        geo_ref[p] = column(tile, p)


def split_kernel(native_ref, f_ref, up_ref, down_ref):
    groups = native_ref.shape[0] // (SUB * SUB)

    def group(j, _):
        for g in range(SUB):
            x = native_ref[pl.ds(j * SUB * SUB + g, SUB, stride=SUB), :]
            at = pl.ds(pl.multiple_of(j * SUB, SUB), SUB)
            f_ref[g, at, :] = x
            if g < REACH:
                down_ref[g, at, :] = x
            if g >= SUB - REACH:
                up_ref[g - (SUB - REACH), at, :] = x
        return 0

    lax.fori_loop(0, groups, group, 0, unroll=2)


def split_profile(native):
    rows = native.shape[0] // SUB
    block = rows // 8
    spec = lambda n: pl.BlockSpec((n, block, LANES), lambda i: (0, i, 0))
    return pl.pallas_call(
        split_kernel,
        grid=(8,),
        in_specs=[pl.BlockSpec((block * SUB, LANES), lambda i: (i, 0))],
        out_specs=[spec(SUB), spec(REACH), spec(REACH)],
        out_shape=[
            jax.ShapeDtypeStruct((SUB, rows, LANES), F32),
            jax.ShapeDtypeStruct((REACH, rows, LANES), F32),
            jax.ShapeDtypeStruct((REACH, rows, LANES), F32),
        ],
        compiler_params=pltpu.CompilerParams(vmem_limit_bytes=VMEM_LIMIT),
        name="split_profile",
    )(native)


def first_sums_kernel(meta_ref, nbr_ref, geo_in, native_ref, f_ref, sums_out, out_ref, geo_ref, face_ref):
    rows = f_ref.shape[1]
    planes = rows // CHUNKS
    first_plane = meta_ref[1]
    unpack_geo(geo_in, geo_ref)
    packed = pack_sums(polynomial_sums(native_ref, planes, first_plane), 0)
    emitted_sums(f_ref, 0, planes, first_plane, nbr_ref, geo_ref, face_ref, True)
    packed = packed + pack_sums([face_sums(face_ref, k) for k in range(2 * FACES)], EMIT)
    sums_out[...] = packed

    def cell(g, _):
        scale = TIME_STEP / splat(geo_ref, VOL, g)
        v0, v1, v2 = [[scale * splat(geo_ref, FV + FACES * i + k, g) for k in range(FACES)] for i in range(3)]
        for t in range(TILES):
            xb, xc = tile_nodes(t)
            base = [v1[k] * xb + v2[k] * xc for k in range(FACES)]

            def plane(a, _):
                xa = plane_node(first_plane, a)
                acc = None
                for k in range(FACES):
                    term = jnp.maximum(v0[k] * xa + base[k], 0.0)
                    acc = term if acc is None else acc + term
                out_ref[g, pl.ds(pl.multiple_of((a * TILES + t) * SUB, SUB), SUB), :] = acc
                return 0

            lax.fori_loop(0, planes, plane, 0, unroll=4)
        return 0

    lax.fori_loop(0, SUB, cell, 0)


def first_sums(meta, nbr, geo, native, f):
    rows = f.shape[1]
    return pl.pallas_call(
        first_sums_kernel,
        in_specs=[
            pl.BlockSpec(memory_space=pltpu.SMEM),
            pl.BlockSpec(memory_space=pltpu.SMEM),
            pl.BlockSpec(memory_space=pltpu.VMEM),
            pl.BlockSpec(memory_space=pltpu.VMEM),
            pl.BlockSpec(memory_space=pltpu.VMEM),
        ],
        out_specs=[pl.BlockSpec(memory_space=pltpu.VMEM)] * 2,
        out_shape=[
            jax.ShapeDtypeStruct((SUB, LANES), F32),
            jax.ShapeDtypeStruct((SUB, rows, LANES), F32),
        ],
        scratch_shapes=[
            pltpu.VMEM((GEO, SUB, LANES), F32),
            pltpu.VMEM((2 * FACES, SUB * SUB, LANES), F32),
        ],
        compiler_params=pltpu.CompilerParams(vmem_limit_bytes=VMEM_LIMIT),
        name="first_sums",
    )(meta, nbr, geo, native, f)


def quantities(tile):
    m = [WEIGHT * column(tile, p) for p in range(13)]
    n = m[0]
    rn = 1.0 / n
    u = [m[1 + i] * rn for i in range(3)]
    uu = u[0] * u[0] + u[1] * u[1] + u[2] * u[2]
    trace = m[4] + m[5] + m[6]
    width = trace - n * uu
    temperature = width * rn * (1.0 / 3.0)
    second = [[m[4], m[7], m[8]], [m[7], m[5], m[9]], [m[8], m[9], m[6]]]
    q = []
    for i in range(3):
        across = u[0] * second[i][0] + u[1] * second[i][1] + u[2] * second[i][2]
        q.append(0.5 * (m[10 + i] - 2.0 * across - u[i] * trace + 2.0 * uu * m[1 + i]))
    return n, u, temperature, q


def macro_kernel(sums_ref, out_ref):
    n, u, temperature, q = quantities(sums_ref[...])
    lane, sub = lane_iota(), sub_iota()
    for i, x in enumerate((n, *u, temperature, *q)):
        row = jnp.sum(jnp.where(lane == sub, x, 0.0), axis=0, keepdims=True)
        out_ref[pl.ds(i, 1), :] = row[:, :SUB]


def macro(sums):
    return pl.pallas_call(
        macro_kernel,
        in_specs=[pl.BlockSpec(memory_space=pltpu.VMEM)],
        out_specs=pl.BlockSpec(memory_space=pltpu.VMEM),
        out_shape=jax.ShapeDtypeStruct((8, SUB), F32),
        name="macro",
    )(sums)


def step_kernel(
    last,
    meta_ref,
    nbr_ref,
    geo_in,
    sums_in,
    absorbed_in,
    f_any,
    before_any,
    after_any,
    out_any,
    *refs,
):
    if last:
        native_ref, sums_out, ext, outflow, geo_ref, ta, coef, sems = refs
    else:
        f_out, up_out, down_out, sums_out, native_ref, ext, outflow, face_ref, geo_ref, ta, coef, sems = refs
    rows = ext.shape[1]
    planes = rows // CHUNKS
    first_plane = meta_ref[1]
    copies = [
        pltpu.make_async_copy(before_any, ext.at[pl.ds(0, REACH)], sems.at[0]),
        pltpu.make_async_copy(f_any, ext.at[pl.ds(REACH, SUB)], sems.at[1]),
        pltpu.make_async_copy(after_any, ext.at[pl.ds(REACH + SUB, REACH)], sems.at[2]),
        pltpu.make_async_copy(out_any, outflow, sems.at[3]),
    ]
    for c in copies:
        c.start()

    unpack_geo(geo_in, geo_ref)
    sums = sums_in[...]
    absorbed = absorbed_in[...]
    n, u, temperature, q = quantities(sums)
    rt = 1.0 / temperature
    rate = TIME_STEP * n * temperature / (SHEAR * jnp.exp(POWER * jnp.log(temperature)))
    height = rate * n * rt * jnp.sqrt(rt)
    slope = (1.0 / 3.0) / (5.0 * n * temperature * temperature)
    scale = -TIME_STEP / geo_ref[VOL]
    coef[0] = rate
    coef[1] = rt
    coef[2], coef[3] = u[1], u[2]
    coef[4], coef[5] = slope * q[1], slope * q[2]
    for k in range(FACES):
        wall = geo_ref[WALL + k] > 0.5
        ratio = jnp.where(
            wall, column(sums, EMIT + k) / jnp.where(wall, column(absorbed, ABSORB + k), 1.0), 1.0
        )
        for i in range(3):
            coef[6 + FACES * i + k] = scale * ratio * geo_ref[FV + FACES * i + k]

    def plane_table(a, _):
        ca = plane_node(first_plane, a) - u[0]
        za = ca * ca * rt
        ta[0, a] = height * jnp.exp(-0.5 * za)
        ta[1, a] = slope * q[0] * ca
        ta[2, a] = za - 5.0
        return 0

    lax.fori_loop(0, planes, plane_table, 0)

    def wall_row(g, _):
        walls = nbr_ref[0, g] < 0
        for k in range(1, FACES):
            walls = jnp.logical_or(walls, nbr_ref[k, g] < 0)

        @pl.when(walls)
        def _():
            wt = splat(geo_ref, WT, g)
            shape = wall_tiles(wt)

            def plane(a, _):
                xa = plane_node(first_plane, a)
                wa = jnp.exp(-0.5 * xa * xa / wt)
                for t in range(TILES):
                    at = pl.ds(pl.multiple_of((a * TILES + t) * SUB, SUB), SUB)
                    ext[2 * REACH + SUB + g, at, :] = wa * shape[t]
                return 0

            lax.fori_loop(0, planes, plane, 0)

        return 0

    lax.fori_loop(0, SUB, wall_row, 0)
    for c in copies:
        c.wait()

    def cell(g, _):
        base_row = meta_ref[0]
        source = []
        for k in range(FACES):
            j = nbr_ref[k, g]
            source.append(jnp.where(j < 0, 2 * REACH + SUB + g, j - base_row))
        keep = 1.0 - splat(coef, 0, g)
        rtg = splat(coef, 1, g)
        ub, uc = splat(coef, 2, g), splat(coef, 3, g)
        qb, qc = splat(coef, 4, g), splat(coef, 5, g)
        v0 = [splat(coef, 6 + k, g) for k in range(FACES)]
        for pair in range(TILES // 2):
            base, bell, heat, zz = [], [], [], []
            for t in (2 * pair, 2 * pair + 1):
                xb, xc = tile_nodes(t)
                cb, cc = xb - ub, xc - uc
                z = (cb * cb + cc * cc) * rtg
                bell.append(jnp.exp(-0.5 * z))
                heat.append(cb * qb + cc * qc)
                zz.append(z)
                base.append(
                    [splat(coef, 12 + k, g) * xb + splat(coef, 18 + k, g) * xc for k in range(FACES)]
                )

            def plane(a, _):
                xa = plane_node(first_plane, a)
                height_a = jnp.broadcast_to(ta[0, a, pl.ds(g, 1), :], (SUB, LANES))
                heat_a = jnp.broadcast_to(ta[1, a, pl.ds(g, 1), :], (SUB, LANES))
                z_a = jnp.broadcast_to(ta[2, a, pl.ds(g, 1), :], (SUB, LANES))
                sa = [v0[k] * xa for k in range(FACES)]
                for i in range(2):
                    tile = a * TILES + 2 * pair + i
                    at = pl.ds(pl.multiple_of(tile * SUB, SUB), SUB)
                    f = ext[REACH + g, at, :]
                    acc = f * (keep - outflow[g, at, :])
                    for k in range(FACES):
                        acc = acc + jnp.maximum(sa[k] + base[i][k], 0.0) * ext[source[k], at, :]
                    target = (height_a * bell[i]) * (1.0 + (heat_a + heat[i]) * (z_a + zz[i]))
                    new = acc + target
                    native_ref[pl.ds(tile * SUB * SUB + g, SUB, stride=SUB), :] = new
                    if not last:
                        f_out[g, at, :] = new
                return 0

            lax.fori_loop(0, planes, plane, 0, unroll=2)
        return 0

    lax.fori_loop(0, SUB, cell, 0)

    if not last:

        def spread(j, _):
            at = pl.ds(pl.multiple_of(j * SUB, SUB), SUB)
            for i in range(REACH):
                down_out[i, at, :] = f_out[i, at, :]
                up_out[i, at, :] = f_out[SUB - REACH + i, at, :]
            return 0

        lax.fori_loop(0, rows // SUB, spread, 0, unroll=4)

    packed = pack_sums(polynomial_sums(native_ref, planes, first_plane), 0)
    if not last:
        emitted_sums(f_out, 0, planes, first_plane, nbr_ref, geo_ref, face_ref, False)
        packed = packed + pack_sums([face_sums(face_ref, k) for k in range(FACES)], EMIT)
    sums_out[...] = packed


def step(last, meta, nbr, geo, sums, absorbed, f, before, after, outflow):
    rows = f.shape[1]
    planes = rows // CHUNKS
    vmem, smem, anywhere = (
        pl.BlockSpec(memory_space=pltpu.VMEM),
        pl.BlockSpec(memory_space=pltpu.SMEM),
        pl.BlockSpec(memory_space=pl.ANY),
    )
    array = lambda *shape: jax.ShapeDtypeStruct(shape, F32)
    native = (SUB * rows, LANES)
    if last:
        out_shape = [array(*native), array(SUB, LANES)]
        scratch = []
    else:
        out_shape = [array(SUB, rows, LANES), array(REACH, rows, LANES), array(REACH, rows, LANES), array(SUB, LANES)]
        scratch = [pltpu.VMEM(native, F32)]
    scratch += [
        pltpu.VMEM((2 * REACH + 2 * SUB, rows, LANES), F32),
        pltpu.VMEM((SUB, rows, LANES), F32),
    ]
    if not last:
        scratch.append(pltpu.VMEM((FACES, SUB * SUB, LANES), F32))
    scratch += [
        pltpu.VMEM((GEO, SUB, LANES), F32),
        pltpu.VMEM((3, planes, SUB, LANES), F32),
        pltpu.VMEM((6 + 3 * FACES, SUB, LANES), F32),
        pltpu.SemaphoreType.DMA((4,)),
    ]

    def kernel(*refs):
        step_kernel(last, *refs)

    return pl.pallas_call(
        kernel,
        in_specs=[smem, smem, vmem, vmem, vmem, anywhere, anywhere, anywhere, anywhere],
        out_specs=[vmem] * len(out_shape),
        out_shape=out_shape,
        scratch_shapes=scratch,
        compiler_params=pltpu.CompilerParams(vmem_limit_bytes=VMEM_LIMIT),
        name="last_step" if last else "step",
    )(meta, nbr, geo, sums, absorbed, f, before, after, outflow)


def exchange(up, down):
    size = lax.axis_size("space")
    forward = [(i, i + 1) for i in range(size - 1)]
    backward = [(i + 1, i) for i in range(size - 1)]
    return lax.ppermute(up, "space", forward), lax.ppermute(down, "space", backward)


def per_device(particle_profile, neighbors, face_vectors, volumes, wall_temp):
    cells, points = particle_profile.shape
    rows = points // LANES
    plane_count = NV // lax.axis_size("vel")
    native = particle_profile.reshape(cells, rows, LANES).transpose(1, 0, 2).reshape(cells * rows, LANES)
    meta = jnp.stack([lax.axis_index("space") * cells - REACH, lax.axis_index("vel") * plane_count])
    geo = jnp.concatenate(
        [face_vectors.reshape(3 * FACES, cells), volumes[None], wall_temp[None], (neighbors < 0).astype(F32)]
    )
    geo = jnp.pad(geo.T, ((0, 0), (0, LANES - GEO)))
    f, up, down = split_profile(native)
    before, after = exchange(up, down)
    sums0, outflow = first_sums(meta, neighbors, geo, native, f)
    sums0 = lax.psum(sums0, "vel")
    f, up, down, sums1 = step(False, meta, neighbors, geo, sums0, sums0, f, before, after, outflow)
    before, after = exchange(up, down)
    sums1 = lax.psum(sums1, "vel")
    native, sums2 = step(True, meta, neighbors, geo, sums1, sums0, f, before, after, outflow)
    macro_quantities = macro(lax.psum(sums2, "vel"))
    evolved = native.reshape(rows, cells, LANES).transpose(1, 0, 2).reshape(cells, points)
    return evolved, macro_quantities


def solution(mesh):
    return jax.shard_map(
        per_device,
        mesh=mesh,
        in_specs=(
            P("space", "vel"),
            P(None, "space"),
            P(None, None, "space"),
            P("space"),
            P("space"),
        ),
        out_specs=(P("space", "vel"), P(None, "space")),
        check_vma=False,
    )
```

```python
import functools
import math

import jax
import jax.numpy as jnp
from jax import lax
from jax.experimental import pallas as pl
from jax.experimental.pallas import tpu as pltpu
from jax.sharding import PartitionSpec as P

NV = 64
FACES = 6
REACH = 3
STEPS = 2
LANES = 128
SUB = 8

TIME_STEP = 0.015
SHEAR = 0.1
POWER = 0.81
SPEED_LIMIT = 6.0
H = 2.0 * SPEED_LIMIT / NV
WEIGHT = H**3 * (2.0 * math.pi) ** (-1.5)

CHUNKS = NV * NV // LANES
TILES = CHUNKS // SUB

FV, VOL, WT, WALL, LOCAL, FIRST = 0, 18, 19, 20, 26, 32
GEO = 33
WALL_LINK = -64
BEFORE_PAIRS = tuple((g, r) for g in range(REACH) for r in range(g, REACH))
EMIT, ABSORB = 13, 19
SUMS = 25

F32 = jnp.float32
VMEM_LIMIT = 16 * 1024 * 1024


def lane_iota():
    return lax.broadcasted_iota(jnp.int32, (SUB, LANES), 1)


def sub_iota():
    return lax.broadcasted_iota(jnp.int32, (SUB, LANES), 0)


def half_of(lane):
    return (lane >= NV).astype(F32)


def third_component(lane):
    c = jnp.where(lane >= NV, lane - NV, lane).astype(F32)
    return -SPEED_LIMIT + (c + 0.5) * H


def tile_nodes(t):
    lane = lane_iota()
    b = (2 * SUB * t + 2 * sub_iota()).astype(F32) + half_of(lane)
    return -SPEED_LIMIT + (b + 0.5) * H, third_component(lane)


def column(tile, p):
    return jnp.broadcast_to(tile[:, p : p + 1], (SUB, LANES))


def splat(ref, i, g):
    return jnp.broadcast_to(ref[i, pl.ds(g, 1), :], (SUB, LANES))


def total(tile):
    return jnp.broadcast_to(jnp.sum(tile, axis=1, keepdims=True), (SUB, LANES))


def face_coefficients(geo_ref, k, g):
    return [splat(geo_ref, FV + FACES * i + k, g) for i in range(3)]


def at_rows(start, size=SUB):
    return pl.ds(pl.multiple_of(start, SUB), size)


def wall_tiles(wall_temp):
    rt = 1.0 / wall_temp
    scale = rt * jnp.sqrt(rt)
    out = []
    for t in range(TILES):
        xb, xc = tile_nodes(t)
        out.append(scale * jnp.exp(-0.5 * (xb * xb + xc * xc) * rt))
    return out


def unpack_geo(geo_in, geo_ref):
    tile = geo_in[...]
    for p in range(GEO):
        geo_ref[p] = column(tile, p)


def pack_sums(arrays, start):
    lane = lane_iota()
    out = jnp.zeros((SUB, LANES), F32)
    for p, x in enumerate(arrays):
        out = jnp.where(lane == start + p, total(x), out)
    return out


def over_sublanes(ref, k):
    out = ref[k, pl.ds(0, SUB, stride=SUB), :]
    for s in range(1, SUB):
        out = out + ref[k, pl.ds(s, SUB, stride=SUB), :]
    return out


def finish_polynomials(y, first, planes):
    y0, y1, y2, y3, by0, by1, by2, bby0, bby1, bbby0 = y
    m = first + 0.5 * (planes - 1) * H
    c = third_component(lane_iota())
    cc = c * c
    a = y1 + m * y0
    aa = y2 + m * (2.0 * y1 + m * y0)
    aaa = y3 + m * (3.0 * y2 + m * (3.0 * y1 + m * y0))
    ab = by1 + m * by0
    aab = by2 + m * (2.0 * by1 + m * by0)
    abb = bby1 + m * bby0
    return (
        y0,
        a,
        by0,
        c * y0,
        aa,
        bby0,
        cc * y0,
        ab,
        c * a,
        c * by0,
        aaa + abb + cc * a,
        aab + bbby0 + cc * by0,
        c * (aa + bby0 + cc * y0),
    )


def polynomial_sums(f_ref, planes, parts_ref):
    half = planes // 2

    def cell(g, _):
        out = [None] * 10
        for t in range(TILES):
            y0 = y1 = y2 = y3 = None
            for i in range(half):
                d = (i + 0.5) * H
                hi = f_ref[g, pl.ds(((half + i) * TILES + t) * SUB, SUB), :]
                lo = f_ref[g, pl.ds(((half - 1 - i) * TILES + t) * SUB, SUB), :]
                s, r = hi + lo, hi - lo
                if i == 0:
                    y0, y1, y2, y3 = s, d * r, (d * d) * s, (d * d * d) * r
                else:
                    y0, y1, y2, y3 = y0 + s, y1 + d * r, y2 + (d * d) * s, y3 + (d * d * d) * r
            b, _c = tile_nodes(t)
            bb = b * b
            terms = (y0, y1, y2, y3, b * y0, b * y1, b * y2, bb * y0, bb * y1, bb * (b * y0))
            out = [x if o is None else o + x for o, x in zip(out, terms)]
        for p in range(10):
            parts_ref[p, at_rows(g * SUB), :] = out[p]
        return 0

    lax.fori_loop(0, SUB, cell, 0)
    return [over_sublanes(parts_ref, p) for p in range(10)]


def native_polynomial_sums(native_ref, planes):
    half, side = planes // 2, CHUNKS // 2
    zero = jnp.zeros((SUB, LANES), F32)
    acc = [zero] * 10

    def plane(a, acc):
        xa = (a.astype(F32) - 0.5 * (planes - 1)) * H
        b0 = b1 = b2 = b3 = None
        for i in range(side):
            y = (2 * i + 1) * H
            hi = native_ref[at_rows((a * CHUNKS + side + i) * SUB), :]
            lo = native_ref[at_rows((a * CHUNKS + side - 1 - i) * SUB), :]
            s, d = hi + lo, hi - lo
            terms = (s, y * d, (y * y) * s, (y * y * y) * d)
            if i == 0:
                b0, b1, b2, b3 = terms
            else:
                b0, b1, b2, b3 = b0 + terms[0], b1 + terms[1], b2 + terms[2], b3 + terms[3]
        a0, a1, a2 = xa * b0, xa * b1, xa * b2
        aa0 = xa * a0
        new = (b0, a0, aa0, xa * aa0, b1, a1, xa * a1, b2, a2, b3)
        return tuple(x + z for x, z in zip(acc, new))

    g0, a0, aa0, aaa0, g1, a1, aa1, g2, a2, g3 = lax.fori_loop(0, planes, plane, tuple(acc))
    e = (half_of(lane_iota()) - 0.5) * H
    return [
        g0,
        a0,
        aa0,
        aaa0,
        g1 + e * g0,
        a1 + e * a0,
        aa1 + e * aa0,
        g2 + e * (2.0 * g1 + e * g0),
        a2 + e * (2.0 * a1 + e * a0),
        g3 + e * (3.0 * g2 + e * (3.0 * g1 + e * g0)),
    ]


def wall_sums(f_ref, planes, links_ref, geo_ref, sums_ref, with_absorbed):
    sums_ref[...] = jnp.zeros_like(sums_ref)

    def cell(g, _):
        for k in range(FACES):

            @pl.when(links_ref[k, g] == WALL_LINK)
            def _():
                v0, v1, v2 = face_coefficients(geo_ref, k, g)
                first = splat(geo_ref, FIRST, g)
                base = []
                for t in range(TILES):
                    xb, xc = tile_nodes(t)
                    base.append(v1 * xb + v2 * xc)
                if with_absorbed:
                    wt = splat(geo_ref, WT, g)
                    shape = wall_tiles(wt)

                def plane(a, acc):
                    out, back = acc
                    xa = first + a.astype(F32) * H
                    sa = v0 * xa
                    if with_absorbed:
                        wa = jnp.exp(-0.5 * xa * xa / wt)
                    for t in range(TILES):
                        s = sa + base[t]
                        f = f_ref[g, at_rows((a * TILES + t) * SUB), :]
                        out = out + jnp.maximum(s, 0.0) * f
                        if with_absorbed:
                            back = back + jnp.maximum(-s, 0.0) * (wa * shape[t])
                    return out, back

                zero = jnp.zeros((SUB, LANES), F32)
                out, back = lax.fori_loop(0, planes, plane, (zero, zero), unroll=2)
                at = at_rows(g * SUB)
                sums_ref[k, at, :] = out
                if with_absorbed:
                    sums_ref[FACES + k, at, :] = back

        return 0

    lax.fori_loop(0, SUB, cell, 0)


def sums_kernel(with_absorbed, links_ref, geo_in, f_ref, sums_out, geo_ref, parts_ref, face_ref):
    planes = f_ref.shape[1] // CHUNKS
    unpack_geo(geo_in, geo_ref)
    first = geo_ref[FIRST]
    y = polynomial_sums(f_ref, planes, parts_ref)
    packed = pack_sums(finish_polynomials(y, first, planes), 0)
    wall_sums(f_ref, planes, links_ref, geo_ref, face_ref, with_absorbed)
    faces = 2 * FACES if with_absorbed else FACES
    sums_out[...] = packed + pack_sums([over_sublanes(face_ref, k) for k in range(faces)], EMIT)


def spec(space):
    return pl.BlockSpec(memory_space=space)


def array(*shape):
    return jax.ShapeDtypeStruct(shape, F32)


def params():
    return pltpu.CompilerParams(vmem_limit_bytes=VMEM_LIMIT)


def local_sums(with_absorbed, links, geo, f):
    return pl.pallas_call(
        functools.partial(sums_kernel, with_absorbed),
        in_specs=[spec(pltpu.SMEM), spec(pltpu.VMEM), spec(pltpu.VMEM)],
        out_specs=spec(pltpu.VMEM),
        out_shape=array(SUB, LANES),
        scratch_shapes=[
            pltpu.VMEM((GEO, SUB, LANES), F32),
            pltpu.VMEM((10, SUB * SUB, LANES), F32),
            pltpu.VMEM(((2 if with_absorbed else 1) * FACES, SUB * SUB, LANES), F32),
        ],
        compiler_params=params(),
        name="local_sums",
    )(links, geo, f)


SPLIT_PARTS = 4


def split_kernel(native_hbm, f_ref, up_ref, down_ref, native_ref, sems):
    rows = native_ref.shape[0]
    part = rows // SPLIT_PARTS
    copies = [
        pltpu.make_async_copy(
            native_hbm.at[pl.ds(i * part, part)], native_ref.at[pl.ds(i * part, part)], sems.at[i]
        )
        for i in range(SPLIT_PARTS)
    ]
    for c in copies:
        c.start()
    groups = part // (SUB * SUB)

    for i, c in enumerate(copies):
        c.wait()

        def group(j, _):
            for g in range(SUB):
                x = native_ref[pl.ds(j * SUB * SUB + g, SUB, stride=SUB), :]
                at = at_rows(j * SUB)
                f_ref[g, at, :] = x
                if g < REACH:
                    down_ref[g, at, :] = x
                if g >= SUB - REACH:
                    up_ref[g - (SUB - REACH), at, :] = x
            return 0

        lax.fori_loop(i * groups, (i + 1) * groups, group, 0, unroll=2)


def split_profile(native):
    rows = native.shape[0] // SUB
    return pl.pallas_call(
        split_kernel,
        in_specs=[spec(pltpu.HBM)],
        out_specs=[spec(pltpu.VMEM)] * 3,
        out_shape=[array(SUB, rows, LANES), array(REACH, rows, LANES), array(REACH, rows, LANES)],
        scratch_shapes=[pltpu.VMEM((SUB * rows, LANES), F32), pltpu.SemaphoreType.DMA((SPLIT_PARTS,))],
        compiler_params=params(),
        name="split_profile",
    )(native)


def geometry_kernel(links_ref, geo_in, outflow_ref, pairs_ref, geo_ref):
    rows = outflow_ref.shape[1]
    planes = rows // CHUNKS
    unpack_geo(geo_in, geo_ref)
    first = splat(geo_ref, FIRST, 0)

    def clear(j, _):
        for p in range(pairs_ref.shape[0]):
            pairs_ref[p, at_rows(j * SUB), :] = jnp.zeros((SUB, LANES), F32)
        return 0

    lax.fori_loop(0, rows // SUB, clear, 0)

    def cell(g, _):
        scale = TIME_STEP / splat(geo_ref, VOL, g)
        v = [[scale * x for x in face_coefficients(geo_ref, k, g)] for k in range(FACES)]
        for t in range(TILES):
            xb, xc = tile_nodes(t)
            base = [v[k][1] * xb + v[k][2] * xc for k in range(FACES)]

            def plane(a, _):
                xa = first + a.astype(F32) * H
                acc = None
                for k in range(FACES):
                    term = jnp.maximum(v[k][0] * xa + base[k], 0.0)
                    acc = term if acc is None else acc + term
                outflow_ref[g, at_rows((a * TILES + t) * SUB), :] = acc
                return 0

            lax.fori_loop(0, planes, plane, 0, unroll=4)

        edge = g - (SUB - REACH)
        for k in range(FACES):
            j = links_ref[k, g]
            is_before = jnp.logical_and(j < 0, j != WALL_LINK)

            @pl.when(jnp.logical_or(is_before, j >= SUB))
            def _():
                r = j + REACH
                before = g * REACH - g * (g - 1) // 2 + r - g
                after = len(BEFORE_PAIRS) + edge * (edge + 1) // 2 + j - SUB
                at_pair = jnp.where(is_before, before, after)
                for t in range(TILES):
                    xb, xc = tile_nodes(t)
                    base = v[k][1] * xb + v[k][2] * xc

                    def plane(a, _):
                        xa = first + a.astype(F32) * H
                        at = at_rows((a * TILES + t) * SUB)
                        weight = jnp.maximum(-(v[k][0] * xa + base), 0.0)
                        pairs_ref[at_pair, at, :] = pairs_ref[at_pair, at, :] + weight
                        return 0

                    lax.fori_loop(0, planes, plane, 0, unroll=4)

        return 0

    lax.fori_loop(0, SUB, cell, 0)


def geometry(links, geo, rows):
    return pl.pallas_call(
        geometry_kernel,
        in_specs=[spec(pltpu.SMEM), spec(pltpu.VMEM)],
        out_specs=[spec(pltpu.VMEM)] * 2,
        out_shape=[array(SUB, rows, LANES), array(2 * len(BEFORE_PAIRS), rows, LANES)],
        scratch_shapes=[pltpu.VMEM((GEO, SUB, LANES), F32)],
        compiler_params=params(),
        name="geometry",
    )(links, geo)


def gather_sums(tile):
    size = lax.axis_size("vel")
    if size not in (2, 4):
        return [lax.psum(tile, "vel")]
    others = [lax.ppermute(tile, "vel", [(i, i ^ s) for i in range(size)]) for s in range(1, size)]
    return [tile, *others]


def add_tiles(refs):
    tiles = [r[...] for r in refs]
    while len(tiles) > 1:
        tiles = [tiles[i] + tiles[i + 1] for i in range(0, len(tiles), 2)]
    return tiles[0]


def quantities(tile):
    m = [WEIGHT * column(tile, p) for p in range(13)]
    n = m[0]
    rn = 1.0 / n
    u = [m[1 + i] * rn for i in range(3)]
    uu = u[0] * u[0] + u[1] * u[1] + u[2] * u[2]
    trace = m[4] + m[5] + m[6]
    width = trace - n * uu
    temperature = width * rn * (1.0 / 3.0)
    second = [[m[4], m[7], m[8]], [m[7], m[5], m[9]], [m[8], m[9], m[6]]]
    q = []
    for i in range(3):
        across = u[0] * second[i][0] + u[1] * second[i][1] + u[2] * second[i][2]
        q.append(0.5 * (m[10 + i] - 2.0 * across - u[i] * trace + 2.0 * uu * m[1 + i]))
    return n, u, temperature, q


def macro_kernel(*refs):
    out_ref = refs[-1]
    n, u, temperature, q = quantities(add_tiles(refs[:-1]))
    lane, sub = lane_iota(), sub_iota()
    for i, x in enumerate((n, *u, temperature, *q)):
        row = jnp.sum(jnp.where(lane == sub, x, 0.0), axis=0, keepdims=True)
        out_ref[pl.ds(i, 1), :] = row[:, :SUB]


def macro(tiles):
    return pl.pallas_call(
        macro_kernel,
        in_specs=[spec(pltpu.VMEM)] * len(tiles),
        out_specs=spec(pltpu.VMEM),
        out_shape=array(8, SUB),
        name="macro",
    )(*tiles)


def inner_kernel(last, count, links_ref, geo_in, absorbed_in, *refs):
    sums_refs, (f_ref, outflow_ref, out_ref, sum_out, geo_ref, ta, coef) = refs[:count], refs[count:]
    planes = f_ref.shape[1] // CHUNKS
    unpack_geo(geo_in, geo_ref)
    sums = add_tiles(sums_refs)
    sum_out[...] = sums
    absorbed = sums if absorbed_in is None else absorbed_in[...]
    n, u, temperature, q = quantities(sums)
    rt = 1.0 / temperature
    rate = TIME_STEP * n * temperature / (SHEAR * jnp.exp(POWER * jnp.log(temperature)))
    height = rate * n * rt * jnp.sqrt(rt)
    slope = (1.0 / 3.0) / (5.0 * n * temperature * temperature)
    scale = -TIME_STEP / geo_ref[VOL]
    coef[0] = rate
    coef[1] = rt
    coef[2], coef[3] = u[1], u[2]
    coef[4], coef[5] = slope * q[1], slope * q[2]
    for k in range(FACES):
        wall = geo_ref[WALL + k] > 0.5
        ratio = column(sums, EMIT + k) / jnp.where(wall, column(absorbed, ABSORB + k), 1.0)
        factor = scale * jnp.where(wall, ratio, geo_ref[LOCAL + k])
        for i in range(3):
            coef[6 + FACES * i + k] = factor * geo_ref[FV + FACES * i + k]

    first = geo_ref[FIRST]

    def plane_table(a, _):
        ca = first + a.astype(F32) * H - u[0]
        za = ca * ca * rt
        ta[0, a] = height * jnp.exp(-0.5 * za)
        ta[1, a] = slope * q[0] * ca
        ta[2, a] = za - 5.0
        return 0

    lax.fori_loop(0, planes, plane_table, 0)

    def place(g, tile):
        if last:
            return (pl.ds(tile * SUB * SUB + g, SUB, stride=SUB), slice(None))
        return (g, at_rows(tile * SUB), slice(None))

    def cell(g, _):
        source, weight = [], []
        for k in range(FACES):
            j = links_ref[k, g]
            own = jnp.logical_and(j >= 0, j < SUB)
            source.append(jnp.where(own, j, g))
            weight.append([splat(coef, 6 + FACES * i + k, g) * splat(geo_ref, LOCAL + k, g) for i in range(3)])
        keep = 1.0 - splat(coef, 0, g)
        rtg = splat(coef, 1, g)
        ub, uc = splat(coef, 2, g), splat(coef, 3, g)
        qb, qc = splat(coef, 4, g), splat(coef, 5, g)
        x0 = splat(geo_ref, FIRST, g)
        for pair in range(TILES // 2):
            base, bell, heat, zz = [], [], [], []
            for t in (2 * pair, 2 * pair + 1):
                xb, xc = tile_nodes(t)
                cb, cc = xb - ub, xc - uc
                z = (cb * cb + cc * cc) * rtg
                bell.append(jnp.exp(-0.5 * z))
                heat.append(cb * qb + cc * qc)
                zz.append(z)
                base.append([weight[k][1] * xb + weight[k][2] * xc for k in range(FACES)])

            def plane(a, _):
                xa = x0 + a.astype(F32) * H
                height_a, heat_a, z_a = [
                    jnp.broadcast_to(ta[i, a, pl.ds(g, 1), :], (SUB, LANES)) for i in range(3)
                ]
                sa = [weight[k][0] * xa for k in range(FACES)]
                for i in range(2):
                    tile = a * TILES + 2 * pair + i
                    at = at_rows(tile * SUB)
                    acc = f_ref[g, at, :] * (keep - outflow_ref[g, at, :])
                    for k in range(FACES):
                        acc = acc + jnp.maximum(sa[k] + base[i][k], 0.0) * f_ref[source[k], at, :]
                    target = (height_a * bell[i]) * (1.0 + (heat_a + heat[i]) * (z_a + zz[i]))
                    out_ref[place(g, tile)] = acc + target
                return 0

            lax.fori_loop(0, planes, plane, 0, unroll=2)

        for k in range(FACES):

            @pl.when(links_ref[k, g] == WALL_LINK)
            def _():
                wt = splat(geo_ref, WT, g)
                shape = wall_tiles(wt)
                v0, v1, v2 = [splat(coef, 6 + FACES * i + k, g) for i in range(3)]
                base = []
                for t in range(TILES):
                    xb, xc = tile_nodes(t)
                    base.append(v1 * xb + v2 * xc)

                def plane(a, _):
                    xa = x0 + a.astype(F32) * H
                    wa = jnp.exp(-0.5 * xa * xa / wt)
                    sa = v0 * xa
                    for t in range(TILES):
                        where = place(g, a * TILES + t)
                        out_ref[where] = out_ref[where] + jnp.maximum(sa + base[t], 0.0) * (wa * shape[t])
                    return 0

                lax.fori_loop(0, planes, plane, 0, unroll=2)

        return 0

    lax.fori_loop(0, SUB, cell, 0)


def inner(last, links, geo, absorbed, tiles, f, outflow):
    rows = f.shape[1]
    vmem = spec(pltpu.VMEM)
    given = [links, geo] + ([] if absorbed is None else [absorbed]) + list(tiles) + [f, outflow]

    def kernel(links_ref, geo_in, *refs):
        if absorbed is None:
            inner_kernel(last, len(tiles), links_ref, geo_in, None, *refs)
        else:
            inner_kernel(last, len(tiles), links_ref, geo_in, *refs)

    return pl.pallas_call(
        kernel,
        in_specs=[spec(pltpu.SMEM)] + [vmem] * (len(given) - 1),
        out_specs=[vmem] * 2,
        out_shape=[
            array(SUB * rows, LANES) if last else array(SUB, rows, LANES),
            array(SUB, LANES),
        ],
        scratch_shapes=[
            pltpu.VMEM((GEO, SUB, LANES), F32),
            pltpu.VMEM((3, rows // CHUNKS, SUB, LANES), F32),
            pltpu.VMEM((6 + 3 * FACES, SUB, LANES), F32),
        ],
        compiler_params=params(),
        name="inner",
    )(*given)


def halo_terms(pairs_ref, before_ref, after_ref, at):
    count = len(BEFORE_PAIRS)
    low, high = [None] * REACH, [None] * REACH
    rows = [before_ref[r, at, :] for r in range(REACH)]
    for p, (g, r) in enumerate(BEFORE_PAIRS):
        term = pairs_ref[p, at, :] * rows[r]
        low[g] = term if low[g] is None else low[g] + term
    rows = [after_ref[r, at, :] for r in range(REACH)]
    p = count
    for e in range(REACH):
        for r in range(e + 1):
            term = pairs_ref[p, at, :] * rows[r]
            high[e] = term if high[e] is None else high[e] + term
            p += 1
    return low, high


def edge_kernel(pairs_ref, before_ref, after_ref, part_ref, f_ref, up_ref, down_ref):
    def group(j, _):
        at = at_rows(j * SUB)
        low, high = halo_terms(pairs_ref, before_ref, after_ref, at)
        for g in range(SUB):
            x = part_ref[g, at, :]
            if g < REACH:
                x = x + low[g]
                down_ref[g, at, :] = x
            e = g - (SUB - REACH)
            if e >= 0:
                x = x + high[e]
                up_ref[e, at, :] = x
            f_ref[g, at, :] = x
        return 0

    lax.fori_loop(0, part_ref.shape[1] // SUB, group, 0)


def edge(pairs, before, after, part):
    rows = part.shape[1]
    return pl.pallas_call(
        edge_kernel,
        in_specs=[spec(pltpu.VMEM)] * 4,
        out_specs=[spec(pltpu.VMEM)] * 3,
        out_shape=[array(SUB, rows, LANES), array(REACH, rows, LANES), array(REACH, rows, LANES)],
        compiler_params=params(),
        name="edge",
    )(pairs, before, after, part)


def last_edge_kernel(geo_in, pairs_ref, before_ref, after_ref, part_ref, out_hbm, sums_out, native_ref, sems):
    rows = part_ref.shape[0] // SUB
    planes = rows // CHUNKS
    tiles = rows // SUB
    part = tiles // LAST_PARTS
    copies = []
    for i in range(LAST_PARTS):

        def group(j, _):
            at = at_rows(j * SUB)
            low, high = halo_terms(pairs_ref, before_ref, after_ref, at)
            terms = low + [None] * (SUB - 2 * REACH) + high
            for g in range(SUB):
                where = (pl.ds(j * SUB * SUB + g, SUB, stride=SUB), slice(None))
                x = part_ref[where]
                native_ref[where] = x if terms[g] is None else x + terms[g]
            return 0

        lax.fori_loop(i * part, (i + 1) * part, group, 0)
        at = pl.ds(i * part * SUB * SUB, part * SUB * SUB)
        copies.append(pltpu.make_async_copy(native_ref.at[at], out_hbm.at[at], sems.at[i]))
        copies[-1].start()
    y = native_polynomial_sums(native_ref, planes)
    sums_out[...] = pack_sums(finish_polynomials(y, column(geo_in[...], FIRST), planes), 0)
    for c in copies:
        c.wait()


LAST_PARTS = 4


def last_edge(geo, pairs, before, after, part):
    return pl.pallas_call(
        last_edge_kernel,
        in_specs=[spec(pltpu.VMEM)] * 5,
        out_specs=[spec(pltpu.HBM), spec(pltpu.VMEM)],
        out_shape=[array(*part.shape), array(SUB, LANES)],
        scratch_shapes=[pltpu.VMEM(part.shape, F32), pltpu.SemaphoreType.DMA((LAST_PARTS,))],
        compiler_params=params(),
        name="last_edge",
    )(geo, pairs, before, after, part)


def exchange(up, down):
    size = lax.axis_size("space")
    forward = [(i, i + 1) for i in range(size - 1)]
    backward = [(i + 1, i) for i in range(size - 1)]
    return lax.ppermute(up, "space", forward), lax.ppermute(down, "space", backward)


def per_device(particle_profile, neighbors, face_vectors, volumes, wall_temp):
    cells, points = particle_profile.shape
    rows = points // LANES
    plane_count = NV // lax.axis_size("vel")
    native = particle_profile.reshape(cells, rows, LANES).transpose(1, 0, 2).reshape(cells * rows, LANES)
    wall = neighbors < 0
    links = jnp.where(wall, WALL_LINK, neighbors - lax.axis_index("space") * cells)
    own = (links >= 0) & (links < cells)
    first = -SPEED_LIMIT + ((lax.axis_index("vel") * plane_count).astype(F32) + 0.5) * H
    geo = jnp.concatenate(
        [
            face_vectors.reshape(3 * FACES, cells),
            volumes[None],
            wall_temp[None],
            wall.astype(F32),
            own.astype(F32),
            jnp.full((1, cells), first, F32),
        ]
    )
    geo = jnp.pad(geo.T, ((0, 0), (0, LANES - GEO)))
    f, up, down = split_profile(pltpu.with_memory_space_constraint(native, pltpu.HBM))
    before, after = exchange(up, down)
    tiles = gather_sums(local_sums(True, links, geo, f))
    outflow, pairs = geometry(links, geo, rows)
    part, absorbed = inner(False, links, geo, None, tiles, f, outflow)
    f, up, down = edge(pairs, before, after, part)
    before, after = exchange(up, down)
    tiles = gather_sums(local_sums(False, links, geo, f))
    part, _ = inner(True, links, geo, absorbed, tiles, f, outflow)
    native, sums = last_edge(geo, pairs, before, after, part)
    macro_quantities = macro(gather_sums(sums))
    evolved = native.reshape(rows, cells, LANES).transpose(1, 0, 2).reshape(cells, points)
    return evolved, macro_quantities


def solution(mesh):
    return jax.shard_map(
        per_device,
        mesh=mesh,
        in_specs=(
            P("space", "vel"),
            P(None, "space"),
            P(None, None, "space"),
            P("space"),
            P("space"),
        ),
        out_specs=(P("space", "vel"), P(None, "space")),
        check_vma=False,
    )
```

```python
import functools
import math

import jax
import jax.numpy as jnp
from jax import lax
from jax.experimental import pallas as pl
from jax.experimental.pallas import tpu as pltpu
from jax.sharding import PartitionSpec as P

NV = 64
FACES = 6
REACH = 3
STEPS = 2
LANES = 128
SUB = 8

TIME_STEP = 0.015
SHEAR = 0.1
POWER = 0.81
SPEED_LIMIT = 6.0
H = 2.0 * SPEED_LIMIT / NV
WEIGHT = H**3 * (2.0 * math.pi) ** (-1.5)

CHUNKS = NV * NV // LANES
TILES = CHUNKS // SUB

FV, VOL, WT, WALL, LOCAL, FIRST = 0, 18, 19, 20, 26, 32
GEO = 33
WALL_LINK = -64
BEFORE_PAIRS = tuple((g, r) for g in range(REACH) for r in range(g, REACH))
EMIT, ABSORB = 13, 19
SUMS = 25

F32 = jnp.float32
VMEM_LIMIT = 16 * 1024 * 1024


def lane_iota():
    return lax.broadcasted_iota(jnp.int32, (SUB, LANES), 1)


def sub_iota():
    return lax.broadcasted_iota(jnp.int32, (SUB, LANES), 0)


def half_of(lane):
    return (lane >= NV).astype(F32)


def third_component(lane):
    c = jnp.where(lane >= NV, lane - NV, lane).astype(F32)
    return -SPEED_LIMIT + (c + 0.5) * H


def tile_nodes(t):
    lane = lane_iota()
    b = (2 * SUB * t + 2 * sub_iota()).astype(F32) + half_of(lane)
    return -SPEED_LIMIT + (b + 0.5) * H, third_component(lane)


def column(tile, p):
    return jnp.broadcast_to(tile[:, p : p + 1], (SUB, LANES))


def splat(ref, i, g):
    return jnp.broadcast_to(ref[i, pl.ds(g, 1), :], (SUB, LANES))


def total(tile):
    return jnp.broadcast_to(jnp.sum(tile, axis=1, keepdims=True), (SUB, LANES))


def face_coefficients(geo_ref, k, g):
    return [splat(geo_ref, FV + FACES * i + k, g) for i in range(3)]


def at_rows(start, size=SUB):
    return pl.ds(pl.multiple_of(start, SUB), size)


def wall_tiles(wall_temp):
    rt = 1.0 / wall_temp
    scale = rt * jnp.sqrt(rt)
    out = []
    for t in range(TILES):
        xb, xc = tile_nodes(t)
        out.append(scale * jnp.exp(-0.5 * (xb * xb + xc * xc) * rt))
    return out


def unpack_geo(geo_in, geo_ref):
    tile = geo_in[...]
    for p in range(GEO):
        geo_ref[p] = column(tile, p)


def pack_sums(arrays, start):
    lane = lane_iota()
    out = jnp.zeros((SUB, LANES), F32)
    for p, x in enumerate(arrays):
        out = jnp.where(lane == start + p, total(x), out)
    return out


def over_sublanes(ref, k):
    out = ref[k, pl.ds(0, SUB, stride=SUB), :]
    for s in range(1, SUB):
        out = out + ref[k, pl.ds(s, SUB, stride=SUB), :]
    return out


def finish_polynomials(y, first, planes):
    y0, y1, y2, y3, by0, by1, by2, bby0, bby1, bbby0 = y
    m = first + 0.5 * (planes - 1) * H
    c = third_component(lane_iota())
    cc = c * c
    a = y1 + m * y0
    aa = y2 + m * (2.0 * y1 + m * y0)
    aaa = y3 + m * (3.0 * y2 + m * (3.0 * y1 + m * y0))
    ab = by1 + m * by0
    aab = by2 + m * (2.0 * by1 + m * by0)
    abb = bby1 + m * bby0
    return (
        y0,
        a,
        by0,
        c * y0,
        aa,
        bby0,
        cc * y0,
        ab,
        c * a,
        c * by0,
        aaa + abb + cc * a,
        aab + bbby0 + cc * by0,
        c * (aa + bby0 + cc * y0),
    )


def polynomial_sums(f_ref, planes, parts_ref):
    half = planes // 2

    def cell(g, _):
        out = [None] * 10
        for t in range(TILES):
            y0 = y1 = y2 = y3 = None
            for i in range(half):
                d = (i + 0.5) * H
                hi = f_ref[g, pl.ds(((half + i) * TILES + t) * SUB, SUB), :]
                lo = f_ref[g, pl.ds(((half - 1 - i) * TILES + t) * SUB, SUB), :]
                s, r = hi + lo, hi - lo
                if i == 0:
                    y0, y1, y2, y3 = s, d * r, (d * d) * s, (d * d * d) * r
                else:
                    y0, y1, y2, y3 = y0 + s, y1 + d * r, y2 + (d * d) * s, y3 + (d * d * d) * r
            b, _c = tile_nodes(t)
            bb = b * b
            terms = (y0, y1, y2, y3, b * y0, b * y1, b * y2, bb * y0, bb * y1, bb * (b * y0))
            out = [x if o is None else o + x for o, x in zip(out, terms)]
        for p in range(10):
            parts_ref[p, at_rows(g * SUB), :] = out[p]
        return 0

    lax.fori_loop(0, SUB, cell, 0)
    return [over_sublanes(parts_ref, p) for p in range(10)]


def native_polynomial_sums(native_ref, planes):
    half, side = planes // 2, CHUNKS // 2
    zero = jnp.zeros((SUB, LANES), F32)
    acc = [zero] * 10

    def plane(a, acc):
        xa = (a.astype(F32) - 0.5 * (planes - 1)) * H
        b0 = b1 = b2 = b3 = None
        for i in range(side):
            y = (2 * i + 1) * H
            hi = native_ref[at_rows((a * CHUNKS + side + i) * SUB), :]
            lo = native_ref[at_rows((a * CHUNKS + side - 1 - i) * SUB), :]
            s, d = hi + lo, hi - lo
            terms = (s, y * d, (y * y) * s, (y * y * y) * d)
            if i == 0:
                b0, b1, b2, b3 = terms
            else:
                b0, b1, b2, b3 = b0 + terms[0], b1 + terms[1], b2 + terms[2], b3 + terms[3]
        a0, a1, a2 = xa * b0, xa * b1, xa * b2
        aa0 = xa * a0
        new = (b0, a0, aa0, xa * aa0, b1, a1, xa * a1, b2, a2, b3)
        return tuple(x + z for x, z in zip(acc, new))

    g0, a0, aa0, aaa0, g1, a1, aa1, g2, a2, g3 = lax.fori_loop(0, planes, plane, tuple(acc))
    e = (half_of(lane_iota()) - 0.5) * H
    return [
        g0,
        a0,
        aa0,
        aaa0,
        g1 + e * g0,
        a1 + e * a0,
        aa1 + e * aa0,
        g2 + e * (2.0 * g1 + e * g0),
        a2 + e * (2.0 * a1 + e * a0),
        g3 + e * (3.0 * g2 + e * (3.0 * g1 + e * g0)),
    ]


def wall_sums(f_ref, planes, links_ref, geo_ref, sums_ref, with_absorbed):
    sums_ref[...] = jnp.zeros_like(sums_ref)

    def cell(g, _):
        for k in range(FACES):

            @pl.when(links_ref[k, g] == WALL_LINK)
            def _():
                v0, v1, v2 = face_coefficients(geo_ref, k, g)
                first = splat(geo_ref, FIRST, g)
                base = []
                for t in range(TILES):
                    xb, xc = tile_nodes(t)
                    base.append(v1 * xb + v2 * xc)
                if with_absorbed:
                    wt = splat(geo_ref, WT, g)
                    shape = wall_tiles(wt)

                def plane(a, acc):
                    out, back = acc
                    xa = first + a.astype(F32) * H
                    sa = v0 * xa
                    if with_absorbed:
                        wa = jnp.exp(-0.5 * xa * xa / wt)
                    for t in range(TILES):
                        s = sa + base[t]
                        f = f_ref[g, at_rows((a * TILES + t) * SUB), :]
                        out = out + jnp.maximum(s, 0.0) * f
                        if with_absorbed:
                            back = back + jnp.maximum(-s, 0.0) * (wa * shape[t])
                    return out, back

                zero = jnp.zeros((SUB, LANES), F32)
                out, back = lax.fori_loop(0, planes, plane, (zero, zero), unroll=2)
                at = at_rows(g * SUB)
                sums_ref[k, at, :] = out
                if with_absorbed:
                    sums_ref[FACES + k, at, :] = back

        return 0

    lax.fori_loop(0, SUB, cell, 0)


def sums_kernel(with_absorbed, links_ref, geo_in, f_ref, sums_out, geo_ref, parts_ref, face_ref):
    planes = f_ref.shape[1] // CHUNKS
    unpack_geo(geo_in, geo_ref)
    first = geo_ref[FIRST]
    y = polynomial_sums(f_ref, planes, parts_ref)
    packed = pack_sums(finish_polynomials(y, first, planes), 0)
    wall_sums(f_ref, planes, links_ref, geo_ref, face_ref, with_absorbed)
    faces = 2 * FACES if with_absorbed else FACES
    sums_out[...] = packed + pack_sums([over_sublanes(face_ref, k) for k in range(faces)], EMIT)


def spec(space):
    return pl.BlockSpec(memory_space=space)


def array(*shape):
    return jax.ShapeDtypeStruct(shape, F32)


def params():
    return pltpu.CompilerParams(vmem_limit_bytes=VMEM_LIMIT)


def local_sums(with_absorbed, links, geo, f):
    return pl.pallas_call(
        functools.partial(sums_kernel, with_absorbed),
        in_specs=[spec(pltpu.SMEM), spec(pltpu.VMEM), spec(pltpu.VMEM)],
        out_specs=spec(pltpu.VMEM),
        out_shape=array(SUB, LANES),
        scratch_shapes=[
            pltpu.VMEM((GEO, SUB, LANES), F32),
            pltpu.VMEM((10, SUB * SUB, LANES), F32),
            pltpu.VMEM(((2 if with_absorbed else 1) * FACES, SUB * SUB, LANES), F32),
        ],
        compiler_params=params(),
        name="local_sums",
    )(links, geo, f)


SPLIT_PARTS = 4


def split_kernel(native_hbm, f_ref, up_ref, down_ref, native_ref, sems):
    rows = native_ref.shape[0]
    part = rows // SPLIT_PARTS
    copies = [
        pltpu.make_async_copy(
            native_hbm.at[pl.ds(i * part, part)], native_ref.at[pl.ds(i * part, part)], sems.at[i]
        )
        for i in range(SPLIT_PARTS)
    ]
    for c in copies:
        c.start()
    groups = part // (SUB * SUB)

    for i, c in enumerate(copies):
        c.wait()

        def group(j, _):
            for g in range(SUB):
                x = native_ref[pl.ds(j * SUB * SUB + g, SUB, stride=SUB), :]
                at = at_rows(j * SUB)
                f_ref[g, at, :] = x
                if g < REACH:
                    down_ref[g, at, :] = x
                if g >= SUB - REACH:
                    up_ref[g - (SUB - REACH), at, :] = x
            return 0

        lax.fori_loop(i * groups, (i + 1) * groups, group, 0, unroll=2)


def split_profile(native):
    rows = native.shape[0] // SUB
    return pl.pallas_call(
        split_kernel,
        in_specs=[spec(pltpu.HBM)],
        out_specs=[spec(pltpu.VMEM)] * 3,
        out_shape=[array(SUB, rows, LANES), array(REACH, rows, LANES), array(REACH, rows, LANES)],
        scratch_shapes=[pltpu.VMEM((SUB * rows, LANES), F32), pltpu.SemaphoreType.DMA((SPLIT_PARTS,))],
        compiler_params=params(),
        name="split_profile",
    )(native)


def geometry_kernel(links_ref, geo_in, pairs_ref, geo_ref):
    rows = pairs_ref.shape[1]
    planes = rows // CHUNKS
    unpack_geo(geo_in, geo_ref)
    first = splat(geo_ref, FIRST, 0)

    def clear(j, _):
        for p in range(pairs_ref.shape[0]):
            pairs_ref[p, at_rows(j * SUB), :] = jnp.zeros((SUB, LANES), F32)
        return 0

    lax.fori_loop(0, rows // SUB, clear, 0, unroll=2)

    def cell(g, _):
        edge = g - (SUB - REACH)
        for k in range(FACES):
            j = links_ref[k, g]
            is_before = jnp.logical_and(j < 0, j != WALL_LINK)

            @pl.when(jnp.logical_or(is_before, j >= SUB))
            def _():
                before = g * REACH - g * (g - 1) // 2 + (j + REACH) - g
                after = len(BEFORE_PAIRS) + edge * (edge + 1) // 2 + j - SUB
                at_pair = jnp.where(is_before, before, after)
                scale = -TIME_STEP / splat(geo_ref, VOL, g)
                v0, v1, v2 = [scale * x for x in face_coefficients(geo_ref, k, g)]
                base = []
                for t in range(TILES):
                    xb, xc = tile_nodes(t)
                    base.append(v1 * xb + v2 * xc)

                def plane(a, _):
                    sa = v0 * (first + a.astype(F32) * H)
                    for t in range(TILES):
                        at = at_rows((a * TILES + t) * SUB)
                        pairs_ref[at_pair, at, :] = pairs_ref[at_pair, at, :] + jnp.maximum(sa + base[t], 0.0)
                    return 0

                lax.fori_loop(0, planes, plane, 0, unroll=4)

        return 0

    lax.fori_loop(0, SUB, cell, 0)


def geometry(links, geo, rows):
    return pl.pallas_call(
        geometry_kernel,
        in_specs=[spec(pltpu.SMEM), spec(pltpu.VMEM)],
        out_specs=spec(pltpu.VMEM),
        out_shape=array(2 * len(BEFORE_PAIRS), rows, LANES),
        scratch_shapes=[pltpu.VMEM((GEO, SUB, LANES), F32)],
        compiler_params=params(),
        name="geometry",
    )(links, geo)


def gather_sums(tile):
    size = lax.axis_size("vel")
    if size not in (2, 4):
        return [lax.psum(tile, "vel")]
    others = [lax.ppermute(tile, "vel", [(i, i ^ s) for i in range(size)]) for s in range(1, size)]
    return [tile, *others]


def add_tiles(refs):
    tiles = [r[...] for r in refs]
    while len(tiles) > 1:
        tiles = [tiles[i] + tiles[i + 1] for i in range(0, len(tiles), 2)]
    return tiles[0]


def quantities(tile):
    m = [WEIGHT * column(tile, p) for p in range(13)]
    n = m[0]
    rn = 1.0 / n
    u = [m[1 + i] * rn for i in range(3)]
    uu = u[0] * u[0] + u[1] * u[1] + u[2] * u[2]
    trace = m[4] + m[5] + m[6]
    width = trace - n * uu
    temperature = width * rn * (1.0 / 3.0)
    second = [[m[4], m[7], m[8]], [m[7], m[5], m[9]], [m[8], m[9], m[6]]]
    q = []
    for i in range(3):
        across = u[0] * second[i][0] + u[1] * second[i][1] + u[2] * second[i][2]
        q.append(0.5 * (m[10 + i] - 2.0 * across - u[i] * trace + 2.0 * uu * m[1 + i]))
    return n, u, temperature, q


def macro_kernel(*refs):
    out_ref = refs[-1]
    n, u, temperature, q = quantities(add_tiles(refs[:-1]))
    lane, sub = lane_iota(), sub_iota()
    for i, x in enumerate((n, *u, temperature, *q)):
        row = jnp.sum(jnp.where(lane == sub, x, 0.0), axis=0, keepdims=True)
        out_ref[pl.ds(i, 1), :] = row[:, :SUB]


def macro(tiles):
    return pl.pallas_call(
        macro_kernel,
        in_specs=[spec(pltpu.VMEM)] * len(tiles),
        out_specs=spec(pltpu.VMEM),
        out_shape=array(8, SUB),
        name="macro",
    )(*tiles)


def inner_kernel(last, count, links_ref, geo_in, absorbed_in, *refs):
    sums_refs, (f_ref, out_ref, sum_out, geo_ref, ta, coef) = refs[:count], refs[count:]
    planes = f_ref.shape[1] // CHUNKS
    unpack_geo(geo_in, geo_ref)
    sums = add_tiles(sums_refs)
    sum_out[...] = sums
    absorbed = sums if absorbed_in is None else absorbed_in[...]
    n, u, temperature, q = quantities(sums)
    rt = 1.0 / temperature
    rate = TIME_STEP * n * temperature / (SHEAR * jnp.exp(POWER * jnp.log(temperature)))
    height = rate * n * rt * jnp.sqrt(rt)
    slope = (1.0 / 3.0) / (5.0 * n * temperature * temperature)
    scale = -TIME_STEP / geo_ref[VOL]
    coef[0] = 1.0 - rate
    coef[1] = rt
    coef[2], coef[3] = u[1], u[2]
    coef[4], coef[5] = slope * q[1], slope * q[2]
    for i in range(3):
        whole = None
        for k in range(FACES):
            x = scale * geo_ref[FV + FACES * i + k]
            coef[6 + FACES * i + k] = x
            whole = x if whole is None else whole + x
        coef[24 + i] = whole
    for k in range(FACES):
        wall = geo_ref[WALL + k] > 0.5
        coef[27 + k] = column(sums, EMIT + k) / jnp.where(wall, column(absorbed, ABSORB + k), 1.0)

    first = geo_ref[FIRST]

    def plane_table(a, _):
        ca = first + a.astype(F32) * H - u[0]
        za = ca * ca * rt
        ta[0, a] = height * jnp.exp(-0.5 * za)
        ta[1, a] = slope * q[0] * ca
        ta[2, a] = za - 5.0
        return 0

    lax.fori_loop(0, planes, plane_table, 0, unroll=4)

    def place(g, tile):
        if last:
            return (pl.ds(tile * SUB * SUB + g, SUB, stride=SUB), slice(None))
        return (g, at_rows(tile * SUB), slice(None))

    def cell(g, _):
        source, weight = [], []
        for k in range(FACES):
            j = links_ref[k, g]
            own = jnp.logical_and(j >= 0, j < SUB)
            source.append(jnp.where(own, j, g))
            weight.append([splat(coef, 6 + FACES * i + k, g) * splat(geo_ref, LOCAL + k, g) for i in range(3)])
        keep, rtg = splat(coef, 0, g), splat(coef, 1, g)
        ub, uc = splat(coef, 2, g), splat(coef, 3, g)
        qb, qc = splat(coef, 4, g), splat(coef, 5, g)
        whole = [splat(coef, 24 + i, g) for i in range(3)]
        x0 = splat(geo_ref, FIRST, g)
        for pair in range(TILES // 2):
            base, bell, heat, zz, stay = [], [], [], [], []
            for t in (2 * pair, 2 * pair + 1):
                xb, xc = tile_nodes(t)
                cb, cc = xb - ub, xc - uc
                z = (cb * cb + cc * cc) * rtg
                bell.append(jnp.exp(-0.5 * z))
                heat.append(cb * qb + cc * qc)
                zz.append(z)
                base.append([weight[k][1] * xb + weight[k][2] * xc for k in range(FACES)])
                stay.append(keep + whole[1] * xb + whole[2] * xc)

            def plane(a, _):
                xa = x0 + a.astype(F32) * H
                height_a, heat_a, z_a = [
                    jnp.broadcast_to(ta[i, a, pl.ds(g, 1), :], (SUB, LANES)) for i in range(3)
                ]
                sa = [weight[k][0] * xa for k in range(FACES)]
                stay_a = whole[0] * xa
                for i in range(2):
                    tile = a * TILES + 2 * pair + i
                    at = at_rows(tile * SUB)
                    f = f_ref[g, at, :]
                    terms = [
                        jnp.maximum(sa[k] + base[i][k], 0.0) * (f_ref[source[k], at, :] - f)
                        for k in range(FACES)
                    ]
                    target = (height_a * bell[i]) * (1.0 + (heat_a + heat[i]) * (z_a + zz[i]))
                    inflow = (terms[0] + terms[1]) + (terms[2] + terms[3]) + (terms[4] + terms[5])
                    out_ref[place(g, tile)] = (f * (stay_a + stay[i]) + target) + inflow
                return 0

            lax.fori_loop(0, planes, plane, 0, unroll=4)

        for k in range(FACES):

            @pl.when(links_ref[k, g] == WALL_LINK)
            def _():
                wt = splat(geo_ref, WT, g)
                ratio = splat(coef, 27 + k, g)
                shape = [ratio * x for x in wall_tiles(wt)]
                v0, v1, v2 = [splat(coef, 6 + FACES * i + k, g) for i in range(3)]
                base = []
                for t in range(TILES):
                    xb, xc = tile_nodes(t)
                    base.append(v1 * xb + v2 * xc)

                def plane(a, _):
                    xa = x0 + a.astype(F32) * H
                    wa = jnp.exp(-0.5 * xa * xa / wt)
                    sa = v0 * xa
                    for t in range(TILES):
                        tile = a * TILES + t
                        where = place(g, tile)
                        f = f_ref[g, at_rows(tile * SUB), :]
                        out_ref[where] = out_ref[where] + jnp.maximum(sa + base[t], 0.0) * (wa * shape[t] - f)
                    return 0

                lax.fori_loop(0, planes, plane, 0, unroll=4)

        return 0

    lax.fori_loop(0, SUB, cell, 0)


def inner(last, links, geo, absorbed, tiles, f):
    rows = f.shape[1]
    vmem = spec(pltpu.VMEM)
    given = [links, geo] + ([] if absorbed is None else [absorbed]) + list(tiles) + [f]

    def kernel(links_ref, geo_in, *refs):
        if absorbed is None:
            inner_kernel(last, len(tiles), links_ref, geo_in, None, *refs)
        else:
            inner_kernel(last, len(tiles), links_ref, geo_in, *refs)

    return pl.pallas_call(
        kernel,
        in_specs=[spec(pltpu.SMEM)] + [vmem] * (len(given) - 1),
        out_specs=[vmem] * 2,
        out_shape=[
            array(SUB * rows, LANES) if last else array(SUB, rows, LANES),
            array(SUB, LANES),
        ],
        scratch_shapes=[
            pltpu.VMEM((GEO, SUB, LANES), F32),
            pltpu.VMEM((3, rows // CHUNKS, SUB, LANES), F32),
            pltpu.VMEM((27 + FACES, SUB, LANES), F32),
        ],
        compiler_params=params(),
        name="inner",
    )(*given)


def halo_terms(pairs_ref, before_ref, after_ref, f_ref, at):
    low, high = [None] * REACH, [None] * REACH
    rows = [before_ref[r, at, :] for r in range(REACH)]
    own = [f_ref[g, at, :] for g in range(REACH)]
    for p, (g, r) in enumerate(BEFORE_PAIRS):
        term = pairs_ref[p, at, :] * (rows[r] - own[g])
        low[g] = term if low[g] is None else low[g] + term
    rows = [after_ref[r, at, :] for r in range(REACH)]
    own = [f_ref[SUB - REACH + e, at, :] for e in range(REACH)]
    p = len(BEFORE_PAIRS)
    for e in range(REACH):
        for r in range(e + 1):
            term = pairs_ref[p, at, :] * (rows[r] - own[e])
            high[e] = term if high[e] is None else high[e] + term
            p += 1
    return low, high


def edge_kernel(pairs_ref, before_ref, after_ref, old_ref, part_ref, f_ref, up_ref, down_ref):
    def group(j, _):
        at = at_rows(j * SUB)
        low, high = halo_terms(pairs_ref, before_ref, after_ref, old_ref, at)
        for g in range(REACH):
            x = part_ref[g, at, :] + low[g]
            down_ref[g, at, :] = x
            f_ref[g, at, :] = x
            e = SUB - REACH + g
            x = part_ref[e, at, :] + high[g]
            up_ref[g, at, :] = x
            f_ref[e, at, :] = x
        return 0

    lax.fori_loop(0, part_ref.shape[1] // SUB, group, 0, unroll=2)


def edge(pairs, before, after, old, part):
    rows = part.shape[1]
    return pl.pallas_call(
        edge_kernel,
        in_specs=[spec(pltpu.VMEM)] * 5,
        out_specs=[spec(pltpu.VMEM)] * 3,
        out_shape=[array(SUB, rows, LANES), array(REACH, rows, LANES), array(REACH, rows, LANES)],
        input_output_aliases={4: 0},
        compiler_params=params(),
        name="edge",
    )(pairs, before, after, old, part)


def last_edge_kernel(
    geo_in, pairs_ref, before_ref, after_ref, f_ref, part_ref, out_hbm, sums_out, native_ref, sems
):
    rows = part_ref.shape[0] // SUB
    planes = rows // CHUNKS
    tiles = rows // SUB
    part = tiles // LAST_PARTS
    copies = []
    for i in range(LAST_PARTS):

        def group(j, _):
            at = at_rows(j * SUB)
            low, high = halo_terms(pairs_ref, before_ref, after_ref, f_ref, at)
            terms = low + [None] * (SUB - 2 * REACH) + high
            for g in range(SUB):
                where = (pl.ds(j * SUB * SUB + g, SUB, stride=SUB), slice(None))
                x = part_ref[where]
                native_ref[where] = x if terms[g] is None else x + terms[g]
            return 0

        lax.fori_loop(i * part, (i + 1) * part, group, 0, unroll=2)
        at = pl.ds(i * part * SUB * SUB, part * SUB * SUB)
        copies.append(pltpu.make_async_copy(native_ref.at[at], out_hbm.at[at], sems.at[i]))
        copies[-1].start()
    y = native_polynomial_sums(native_ref, planes)
    sums_out[...] = pack_sums(finish_polynomials(y, column(geo_in[...], FIRST), planes), 0)
    for c in copies:
        c.wait()


LAST_PARTS = 4


def last_edge(geo, pairs, before, after, f, part):
    return pl.pallas_call(
        last_edge_kernel,
        in_specs=[spec(pltpu.VMEM)] * 6,
        out_specs=[spec(pltpu.HBM), spec(pltpu.VMEM)],
        out_shape=[array(*part.shape), array(SUB, LANES)],
        scratch_shapes=[pltpu.VMEM(part.shape, F32), pltpu.SemaphoreType.DMA((LAST_PARTS,))],
        compiler_params=params(),
        name="last_edge",
    )(geo, pairs, before, after, f, part)


def exchange(up, down):
    size = lax.axis_size("space")
    forward = [(i, i + 1) for i in range(size - 1)]
    backward = [(i + 1, i) for i in range(size - 1)]
    return lax.ppermute(up, "space", forward), lax.ppermute(down, "space", backward)


def per_device(particle_profile, neighbors, face_vectors, volumes, wall_temp):
    cells, points = particle_profile.shape
    rows = points // LANES
    plane_count = NV // lax.axis_size("vel")
    native = particle_profile.reshape(cells, rows, LANES).transpose(1, 0, 2).reshape(cells * rows, LANES)
    wall = neighbors < 0
    links = jnp.where(wall, WALL_LINK, neighbors - lax.axis_index("space") * cells)
    own = (links >= 0) & (links < cells)
    first = -SPEED_LIMIT + ((lax.axis_index("vel") * plane_count).astype(F32) + 0.5) * H
    geo = jnp.concatenate(
        [
            face_vectors.reshape(3 * FACES, cells),
            volumes[None],
            wall_temp[None],
            wall.astype(F32),
            own.astype(F32),
            jnp.full((1, cells), first, F32),
        ]
    )
    geo = jnp.pad(geo.T, ((0, 0), (0, LANES - GEO)))
    f, up, down = split_profile(pltpu.with_memory_space_constraint(native, pltpu.HBM))
    before, after = exchange(up, down)
    tiles = gather_sums(local_sums(True, links, geo, f))
    pairs = geometry(links, geo, rows)
    part, absorbed = inner(False, links, geo, None, tiles, f)
    f, up, down = edge(pairs, before, after, f, part)
    before, after = exchange(up, down)
    tiles = gather_sums(local_sums(False, links, geo, f))
    part, _ = inner(True, links, geo, absorbed, tiles, f)
    native, sums = last_edge(geo, pairs, before, after, f, part)
    macro_quantities = macro(gather_sums(sums))
    evolved = native.reshape(rows, cells, LANES).transpose(1, 0, 2).reshape(cells, points)
    return evolved, macro_quantities


def solution(mesh):
    return jax.shard_map(
        per_device,
        mesh=mesh,
        in_specs=(
            P("space", "vel"),
            P(None, "space"),
            P(None, None, "space"),
            P("space"),
            P("space"),
        ),
        out_specs=(P("space", "vel"), P(None, "space")),
        check_vma=False,
    )
```

```python
import functools
import math

import jax
import jax.numpy as jnp
from jax import lax
from jax.experimental import pallas as pl
from jax.experimental.pallas import tpu as pltpu
from jax.sharding import PartitionSpec as P

NV = 64
FACES = 6
REACH = 3
STEPS = 2
LANES = 128
SUB = 8

TIME_STEP = 0.015
SHEAR = 0.1
POWER = 0.81
SPEED_LIMIT = 6.0
H = 2.0 * SPEED_LIMIT / NV
WEIGHT = H**3 * (2.0 * math.pi) ** (-1.5)

CHUNKS = NV * NV // LANES
TILES = CHUNKS // SUB

FV, VOL, WT, WALL, LOCAL, FIRST = 0, 18, 19, 20, 26, 32
GEO = 33
WALL_LINK = -64
BEFORE_PAIRS = tuple((g, r) for g in range(REACH) for r in range(g, REACH))
EMIT, ABSORB = 13, 19
SUMS = 25

F32 = jnp.float32
VMEM_LIMIT = 16 * 1024 * 1024


def lane_iota():
    return lax.broadcasted_iota(jnp.int32, (SUB, LANES), 1)


def sub_iota():
    return lax.broadcasted_iota(jnp.int32, (SUB, LANES), 0)


def half_of(lane):
    return (lane >= NV).astype(F32)


def third_component(lane):
    c = jnp.where(lane >= NV, lane - NV, lane).astype(F32)
    return -SPEED_LIMIT + (c + 0.5) * H


def tile_nodes(t):
    lane = lane_iota()
    b = (2 * SUB * t + 2 * sub_iota()).astype(F32) + half_of(lane)
    return -SPEED_LIMIT + (b + 0.5) * H, third_component(lane)


def column(tile, p):
    return jnp.broadcast_to(tile[:, p : p + 1], (SUB, LANES))


def splat(ref, i, g):
    return jnp.broadcast_to(ref[i, pl.ds(g, 1), :], (SUB, LANES))


def total(tile):
    return jnp.broadcast_to(jnp.sum(tile, axis=1, keepdims=True), (SUB, LANES))


def face_coefficients(geo_ref, k, g):
    return [splat(geo_ref, FV + FACES * i + k, g) for i in range(3)]


def at_rows(start, size=SUB):
    return pl.ds(pl.multiple_of(start, SUB), size)


def wall_tiles(wall_temp):
    rt = 1.0 / wall_temp
    scale = rt * jnp.sqrt(rt)
    out = []
    for t in range(TILES):
        xb, xc = tile_nodes(t)
        out.append(scale * jnp.exp(-0.5 * (xb * xb + xc * xc) * rt))
    return out


def unpack_geo(geo_in, geo_ref):
    tile = geo_in[...]
    for p in range(GEO):
        geo_ref[p] = column(tile, p)


def pack_sums(arrays, start):
    lane = lane_iota()
    out = jnp.zeros((SUB, LANES), F32)
    for p, x in enumerate(arrays):
        out = jnp.where(lane == start + p, total(x), out)
    return out


def over_sublanes(ref, k):
    out = ref[k, pl.ds(0, SUB, stride=SUB), :]
    for s in range(1, SUB):
        out = out + ref[k, pl.ds(s, SUB, stride=SUB), :]
    return out


def finish_polynomials(y, first, planes):
    y0, y1, y2, y3, by0, by1, by2, bby0, bby1, bbby0 = y
    m = first + 0.5 * (planes - 1) * H
    c = third_component(lane_iota())
    cc = c * c
    a = y1 + m * y0
    aa = y2 + m * (2.0 * y1 + m * y0)
    aaa = y3 + m * (3.0 * y2 + m * (3.0 * y1 + m * y0))
    ab = by1 + m * by0
    aab = by2 + m * (2.0 * by1 + m * by0)
    abb = bby1 + m * bby0
    return (
        y0,
        a,
        by0,
        c * y0,
        aa,
        bby0,
        cc * y0,
        ab,
        c * a,
        c * by0,
        aaa + abb + cc * a,
        aab + bbby0 + cc * by0,
        c * (aa + bby0 + cc * y0),
    )


def polynomial_sums(f_ref, planes, parts_ref):
    half = planes // 2

    def cell(g, _):
        out = [None] * 10
        for t in range(TILES):
            y0 = y1 = y2 = y3 = None
            for i in range(half):
                d = (i + 0.5) * H
                hi = f_ref[g, pl.ds(((half + i) * TILES + t) * SUB, SUB), :]
                lo = f_ref[g, pl.ds(((half - 1 - i) * TILES + t) * SUB, SUB), :]
                s, r = hi + lo, hi - lo
                if i == 0:
                    y0, y1, y2, y3 = s, d * r, (d * d) * s, (d * d * d) * r
                else:
                    y0, y1, y2, y3 = y0 + s, y1 + d * r, y2 + (d * d) * s, y3 + (d * d * d) * r
            b, _c = tile_nodes(t)
            bb = b * b
            terms = (y0, y1, y2, y3, b * y0, b * y1, b * y2, bb * y0, bb * y1, bb * (b * y0))
            out = [x if o is None else o + x for o, x in zip(out, terms)]
        for p in range(10):
            parts_ref[p, at_rows(g * SUB), :] = out[p]
        return 0

    lax.fori_loop(0, SUB, cell, 0)
    return [over_sublanes(parts_ref, p) for p in range(10)]


def native_polynomial_sums(native_ref, planes):
    half, side = planes // 2, CHUNKS // 2
    zero = jnp.zeros((SUB, LANES), F32)
    acc = [zero] * 10

    def plane(a, acc):
        xa = (a.astype(F32) - 0.5 * (planes - 1)) * H
        b0 = b1 = b2 = b3 = None
        for i in range(side):
            y = (2 * i + 1) * H
            hi = native_ref[at_rows((a * CHUNKS + side + i) * SUB), :]
            lo = native_ref[at_rows((a * CHUNKS + side - 1 - i) * SUB), :]
            s, d = hi + lo, hi - lo
            terms = (s, y * d, (y * y) * s, (y * y * y) * d)
            if i == 0:
                b0, b1, b2, b3 = terms
            else:
                b0, b1, b2, b3 = b0 + terms[0], b1 + terms[1], b2 + terms[2], b3 + terms[3]
        a0, a1, a2 = xa * b0, xa * b1, xa * b2
        aa0 = xa * a0
        new = (b0, a0, aa0, xa * aa0, b1, a1, xa * a1, b2, a2, b3)
        return tuple(x + z for x, z in zip(acc, new))

    g0, a0, aa0, aaa0, g1, a1, aa1, g2, a2, g3 = lax.fori_loop(0, planes, plane, tuple(acc))
    e = (half_of(lane_iota()) - 0.5) * H
    return [
        g0,
        a0,
        aa0,
        aaa0,
        g1 + e * g0,
        a1 + e * a0,
        aa1 + e * aa0,
        g2 + e * (2.0 * g1 + e * g0),
        a2 + e * (2.0 * a1 + e * a0),
        g3 + e * (3.0 * g2 + e * (3.0 * g1 + e * g0)),
    ]


def wall_sums(f_ref, planes, links_ref, geo_ref, sums_ref, with_absorbed):
    sums_ref[...] = jnp.zeros_like(sums_ref)

    def cell(g, _):
        for k in range(FACES):

            @pl.when(links_ref[k, g] == WALL_LINK)
            def _():
                v0, v1, v2 = face_coefficients(geo_ref, k, g)
                first = splat(geo_ref, FIRST, g)
                base = []
                for t in range(TILES):
                    xb, xc = tile_nodes(t)
                    base.append(v1 * xb + v2 * xc)
                if with_absorbed:
                    wt = splat(geo_ref, WT, g)
                    shape = wall_tiles(wt)

                def plane(a, acc):
                    out, back = list(acc[0]), list(acc[1])
                    xa = first + a.astype(F32) * H
                    sa = v0 * xa
                    if with_absorbed:
                        wa = jnp.exp(-0.5 * xa * xa / wt)
                    for t in range(TILES):
                        s = sa + base[t]
                        f = f_ref[g, at_rows((a * TILES + t) * SUB), :]
                        out[t] = out[t] + jnp.maximum(s, 0.0) * f
                        if with_absorbed:
                            back[t] = back[t] + jnp.maximum(-s, 0.0) * (wa * shape[t])
                    return tuple(out), tuple(back)

                zeros = (jnp.zeros((SUB, LANES), F32),) * TILES
                out, back = lax.fori_loop(0, planes, plane, (zeros, zeros), unroll=4)
                out = (out[0] + out[1]) + (out[2] + out[3])
                back = (back[0] + back[1]) + (back[2] + back[3])
                at = at_rows(g * SUB)
                sums_ref[k, at, :] = out
                if with_absorbed:
                    sums_ref[FACES + k, at, :] = back

        return 0

    lax.fori_loop(0, SUB, cell, 0)


def sums_kernel(links_ref, geo_in, f_ref, sums_out, geo_ref, parts_ref, face_ref):
    planes = f_ref.shape[1] // CHUNKS
    unpack_geo(geo_in, geo_ref)
    y = polynomial_sums(f_ref, planes, parts_ref)
    packed = pack_sums(finish_polynomials(y, geo_ref[FIRST], planes), 0)
    wall_sums(f_ref, planes, links_ref, geo_ref, face_ref, False)
    sums_out[...] = packed + pack_sums([over_sublanes(face_ref, k) for k in range(FACES)], EMIT)


def first_sums_kernel(links_ref, geo_in, native_ref, f_ref, sums_out, geo_ref, face_ref):
    rows = f_ref.shape[1]
    planes = rows // CHUNKS
    unpack_geo(geo_in, geo_ref)

    def group(j, _):
        for g in range(SUB):
            f_ref[g, at_rows(j * SUB), :] = native_ref[pl.ds(j * SUB * SUB + g, SUB, stride=SUB), :]
        return 0

    lax.fori_loop(0, rows // SUB, group, 0, unroll=2)
    y = native_polynomial_sums(native_ref, planes)
    packed = pack_sums(finish_polynomials(y, geo_ref[FIRST], planes), 0)
    wall_sums(f_ref, planes, links_ref, geo_ref, face_ref, True)
    sums_out[...] = packed + pack_sums([over_sublanes(face_ref, k) for k in range(2 * FACES)], EMIT)


def spec(space):
    return pl.BlockSpec(memory_space=space)


def array(*shape):
    return jax.ShapeDtypeStruct(shape, F32)


def params():
    return pltpu.CompilerParams(vmem_limit_bytes=VMEM_LIMIT)


def local_sums(links, geo, f):
    return pl.pallas_call(
        sums_kernel,
        in_specs=[spec(pltpu.SMEM), spec(pltpu.VMEM), spec(pltpu.VMEM)],
        out_specs=spec(pltpu.VMEM),
        out_shape=array(SUB, LANES),
        scratch_shapes=[
            pltpu.VMEM((GEO, SUB, LANES), F32),
            pltpu.VMEM((10, SUB * SUB, LANES), F32),
            pltpu.VMEM((FACES, SUB * SUB, LANES), F32),
        ],
        compiler_params=params(),
        name="local_sums",
    )(links, geo, f)


def first_sums(links, geo, native):
    rows = native.shape[0] // SUB
    return pl.pallas_call(
        first_sums_kernel,
        in_specs=[spec(pltpu.SMEM), spec(pltpu.VMEM), spec(pltpu.VMEM)],
        out_specs=[spec(pltpu.VMEM)] * 2,
        out_shape=[array(SUB, rows, LANES), array(SUB, LANES)],
        scratch_shapes=[
            pltpu.VMEM((GEO, SUB, LANES), F32),
            pltpu.VMEM((2 * FACES, SUB * SUB, LANES), F32),
        ],
        compiler_params=params(),
        name="first_sums",
    )(links, geo, native)


SPLIT_PARTS = 4


def is_odd():
    return lax.rem(lax.axis_index("space"), 2) == 1


def first_rows_kernel(native_hbm, native_ref, far_ref, near_ref, sems):
    rows = native_ref.shape[0]
    part = rows // SPLIT_PARTS
    copies = [
        pltpu.make_async_copy(
            native_hbm.at[pl.ds(i * part, part)], native_ref.at[pl.ds(i * part, part)], sems.at[i]
        )
        for i in range(SPLIT_PARTS)
    ]
    for c in copies:
        c.start()
    odd = is_odd()
    far = jnp.where(odd, SUB - REACH, 0)
    near = jnp.where(odd, 0, SUB - REACH)
    groups = part // (SUB * SUB)

    for i, c in enumerate(copies):
        c.wait()

        def group(j, _):
            for r in range(REACH):
                at = at_rows(j * SUB)
                far_ref[r, at, :] = native_ref[pl.ds(j * SUB * SUB + far + r, SUB, stride=SUB), :]
                near_ref[r, at, :] = native_ref[pl.ds(j * SUB * SUB + near + r, SUB, stride=SUB), :]
            return 0

        lax.fori_loop(i * groups, (i + 1) * groups, group, 0, unroll=4)


def first_rows(native):
    rows = native.shape[0] // SUB
    return pl.pallas_call(
        first_rows_kernel,
        in_specs=[spec(pltpu.HBM)],
        out_specs=[spec(pltpu.VMEM)] * 3,
        out_shape=[array(*native.shape), array(REACH, rows, LANES), array(REACH, rows, LANES)],
        scratch_shapes=[pltpu.SemaphoreType.DMA((SPLIT_PARTS,))],
        compiler_params=params(),
        name="first_rows",
    )(pltpu.with_memory_space_constraint(native, pltpu.HBM))


def geometry_kernel(links_ref, geo_in, pairs_ref, geo_ref):
    rows = pairs_ref.shape[1]
    planes = rows // CHUNKS
    unpack_geo(geo_in, geo_ref)
    first = splat(geo_ref, FIRST, 0)

    def clear(j, _):
        for p in range(pairs_ref.shape[0]):
            pairs_ref[p, at_rows(j * SUB), :] = jnp.zeros((SUB, LANES), F32)
        return 0

    lax.fori_loop(0, rows // SUB, clear, 0, unroll=2)

    def cell(g, _):
        edge = g - (SUB - REACH)
        for k in range(FACES):
            j = links_ref[k, g]
            is_before = jnp.logical_and(j < 0, j != WALL_LINK)

            @pl.when(jnp.logical_or(is_before, j >= SUB))
            def _():
                before = g * REACH - g * (g - 1) // 2 + (j + REACH) - g
                after = len(BEFORE_PAIRS) + edge * (edge + 1) // 2 + j - SUB
                at_pair = jnp.where(is_before, before, after)
                scale = -TIME_STEP / splat(geo_ref, VOL, g)
                v0, v1, v2 = [scale * x for x in face_coefficients(geo_ref, k, g)]
                base = []
                for t in range(TILES):
                    xb, xc = tile_nodes(t)
                    base.append(v1 * xb + v2 * xc)

                def plane(a, _):
                    sa = v0 * (first + a.astype(F32) * H)
                    for t in range(TILES):
                        at = at_rows((a * TILES + t) * SUB)
                        pairs_ref[at_pair, at, :] = pairs_ref[at_pair, at, :] + jnp.maximum(sa + base[t], 0.0)
                    return 0

                lax.fori_loop(0, planes, plane, 0, unroll=4)

        return 0

    lax.fori_loop(0, SUB, cell, 0)


def geometry(links, geo, rows):
    return pl.pallas_call(
        geometry_kernel,
        in_specs=[spec(pltpu.SMEM), spec(pltpu.VMEM)],
        out_specs=spec(pltpu.VMEM),
        out_shape=array(2 * len(BEFORE_PAIRS), rows, LANES),
        scratch_shapes=[pltpu.VMEM((GEO, SUB, LANES), F32)],
        compiler_params=params(),
        name="geometry",
    )(links, geo)


def gather_sums(tile):
    size = lax.axis_size("vel")
    if size not in (2, 4):
        return [lax.psum(tile, "vel")]
    others = [lax.ppermute(tile, "vel", [(i, i ^ s) for i in range(size)]) for s in range(1, size)]
    return [tile, *others]


def add_tiles(refs):
    tiles = [r[...] for r in refs]
    while len(tiles) > 1:
        tiles = [tiles[i] + tiles[i + 1] for i in range(0, len(tiles), 2)]
    return tiles[0]


def quantities(tile):
    m = [WEIGHT * column(tile, p) for p in range(13)]
    n = m[0]
    rn = 1.0 / n
    u = [m[1 + i] * rn for i in range(3)]
    uu = u[0] * u[0] + u[1] * u[1] + u[2] * u[2]
    trace = m[4] + m[5] + m[6]
    width = trace - n * uu
    temperature = width * rn * (1.0 / 3.0)
    second = [[m[4], m[7], m[8]], [m[7], m[5], m[9]], [m[8], m[9], m[6]]]
    q = []
    for i in range(3):
        across = u[0] * second[i][0] + u[1] * second[i][1] + u[2] * second[i][2]
        q.append(0.5 * (m[10 + i] - 2.0 * across - u[i] * trace + 2.0 * uu * m[1 + i]))
    return n, u, temperature, q


def macro_kernel(*refs):
    out_ref = refs[-1]
    n, u, temperature, q = quantities(add_tiles(refs[:-1]))
    lane, sub = lane_iota(), sub_iota()
    for i, x in enumerate((n, *u, temperature, *q)):
        row = jnp.sum(jnp.where(lane == sub, x, 0.0), axis=0, keepdims=True)
        out_ref[pl.ds(i, 1), :] = row[:, :SUB]


def macro(tiles):
    return pl.pallas_call(
        macro_kernel,
        in_specs=[spec(pltpu.VMEM)] * len(tiles),
        out_specs=spec(pltpu.VMEM),
        out_shape=array(8, SUB),
        name="macro",
    )(*tiles)


def placer(native):
    def place(g, tile):
        if native:
            return (pl.ds(tile * SUB * SUB + g, SUB, stride=SUB), slice(None))
        return (g, at_rows(tile * SUB), slice(None))

    return place


def flux_kernel(native, links_ref, geo_in, f_ref, out_ref, geo_ref, coef):
    planes = f_ref.shape[1] // CHUNKS
    place = placer(native)
    unpack_geo(geo_in, geo_ref)
    scale = -TIME_STEP / geo_ref[VOL]
    for i in range(3):
        whole = None
        for k in range(FACES):
            x = scale * geo_ref[FV + FACES * i + k]
            coef[FACES * i + k] = x * geo_ref[LOCAL + k]
            whole = x if whole is None else whole + x
        coef[3 * FACES + i] = whole

    def cell(g, _):
        source = []
        for k in range(FACES):
            j = links_ref[k, g]
            source.append(jnp.where(jnp.logical_and(j >= 0, j < SUB), j, g))
        weight = [[splat(coef, FACES * i + k, g) for i in range(3)] for k in range(FACES)]
        whole = [splat(coef, 3 * FACES + i, g) for i in range(3)]
        x0 = splat(geo_ref, FIRST, g)
        for pair in range(TILES // 2):
            base, stay = [], []
            for t in (2 * pair, 2 * pair + 1):
                xb, xc = tile_nodes(t)
                base.append([weight[k][1] * xb + weight[k][2] * xc for k in range(FACES)])
                stay.append(1.0 + whole[1] * xb + whole[2] * xc)

            def plane(a, _):
                xa = x0 + a.astype(F32) * H
                sa = [weight[k][0] * xa for k in range(FACES)]
                stay_a = whole[0] * xa
                for i in range(2):
                    tile = a * TILES + 2 * pair + i
                    at = at_rows(tile * SUB)
                    f = f_ref[g, at, :]
                    terms = [
                        jnp.maximum(sa[k] + base[i][k], 0.0) * (f_ref[source[k], at, :] - f)
                        for k in range(FACES)
                    ]
                    inflow = (terms[0] + terms[1]) + (terms[2] + terms[3]) + (terms[4] + terms[5])
                    out_ref[place(g, tile)] = f * (stay_a + stay[i]) + inflow
                return 0

            lax.fori_loop(0, planes, plane, 0, unroll=4)
        return 0

    lax.fori_loop(0, SUB, cell, 0)


def flux(native, links, geo, f):
    rows = f.shape[1]
    return pl.pallas_call(
        functools.partial(flux_kernel, native),
        in_specs=[spec(pltpu.SMEM), spec(pltpu.VMEM), spec(pltpu.VMEM)],
        out_specs=spec(pltpu.VMEM),
        out_shape=array(SUB * rows, LANES) if native else array(SUB, rows, LANES),
        scratch_shapes=[
            pltpu.VMEM((GEO, SUB, LANES), F32),
            pltpu.VMEM((3 * FACES + 3, SUB, LANES), F32),
        ],
        compiler_params=params(),
        name="flux",
    )(links, geo, f)


def target_kernel(native, count, links_ref, geo_in, absorbed_in, *refs):
    sums_refs, (f_ref, part_ref, out_ref, sum_out, geo_ref, ta, coef) = refs[:count], refs[count:]
    planes = f_ref.shape[1] // CHUNKS
    place = placer(native)
    unpack_geo(geo_in, geo_ref)
    sums = add_tiles(sums_refs)
    sum_out[...] = sums
    absorbed = sums if absorbed_in is None else absorbed_in[...]
    n, u, temperature, q = quantities(sums)
    rt = 1.0 / temperature
    rate = TIME_STEP * n * temperature / (SHEAR * jnp.exp(POWER * jnp.log(temperature)))
    height = rate * n * rt * jnp.sqrt(rt)
    slope = (1.0 / 3.0) / (5.0 * n * temperature * temperature)
    coef[0] = rate
    coef[1] = rt
    coef[2], coef[3] = u[1], u[2]
    coef[4], coef[5] = slope * q[1], slope * q[2]
    for k in range(FACES):
        wall = geo_ref[WALL + k] > 0.5
        coef[6 + k] = column(sums, EMIT + k) / jnp.where(wall, column(absorbed, ABSORB + k), 1.0)
    first = geo_ref[FIRST]

    def plane_table(a, _):
        ca = first + a.astype(F32) * H - u[0]
        za = ca * ca * rt
        ta[0, a] = height * jnp.exp(-0.5 * za)
        ta[1, a] = slope * q[0] * ca
        ta[2, a] = za - 5.0
        return 0

    lax.fori_loop(0, planes, plane_table, 0, unroll=4)

    def cell(g, _):
        rate_g, rtg = splat(coef, 0, g), splat(coef, 1, g)
        ub, uc = splat(coef, 2, g), splat(coef, 3, g)
        qb, qc = splat(coef, 4, g), splat(coef, 5, g)
        x0 = splat(geo_ref, FIRST, g)
        bell, heat, zz = [], [], []
        for t in range(TILES):
            xb, xc = tile_nodes(t)
            cb, cc = xb - ub, xc - uc
            z = (cb * cb + cc * cc) * rtg
            bell.append(jnp.exp(-0.5 * z))
            heat.append(cb * qb + cc * qc)
            zz.append(z)

        def plane(a, _):
            height_a, heat_a, z_a = [
                jnp.broadcast_to(ta[i, a, pl.ds(g, 1), :], (SUB, LANES)) for i in range(3)
            ]
            for t in range(TILES):
                tile = a * TILES + t
                where = place(g, tile)
                f = f_ref[g, at_rows(tile * SUB), :]
                target = (height_a * bell[t]) * (1.0 + (heat_a + heat[t]) * (z_a + zz[t]))
                out_ref[where] = (part_ref[where] - rate_g * f) + target
            return 0

        lax.fori_loop(0, planes, plane, 0, unroll=4)

        for k in range(FACES):

            @pl.when(links_ref[k, g] == WALL_LINK)
            def _():
                wt = splat(geo_ref, WT, g)
                ratio = splat(coef, 6 + k, g)
                shape = [ratio * x for x in wall_tiles(wt)]
                scale = -TIME_STEP / splat(geo_ref, VOL, g)
                v0, v1, v2 = [scale * x for x in face_coefficients(geo_ref, k, g)]
                base = []
                for t in range(TILES):
                    xb, xc = tile_nodes(t)
                    base.append(v1 * xb + v2 * xc)

                def plane(a, _):
                    xa = x0 + a.astype(F32) * H
                    wa = jnp.exp(-0.5 * xa * xa / wt)
                    sa = v0 * xa
                    for t in range(TILES):
                        tile = a * TILES + t
                        where = place(g, tile)
                        f = f_ref[g, at_rows(tile * SUB), :]
                        out_ref[where] = out_ref[where] + jnp.maximum(sa + base[t], 0.0) * (wa * shape[t] - f)
                    return 0

                lax.fori_loop(0, planes, plane, 0, unroll=4)

        return 0

    lax.fori_loop(0, SUB, cell, 0)


def add_target(native, links, geo, absorbed, tiles, f, part):
    rows = f.shape[1]
    vmem = spec(pltpu.VMEM)
    given = [links, geo] + ([] if absorbed is None else [absorbed]) + list(tiles) + [f, part]

    def kernel(links_ref, geo_in, *refs):
        if absorbed is None:
            target_kernel(native, len(tiles), links_ref, geo_in, None, *refs)
        else:
            target_kernel(native, len(tiles), links_ref, geo_in, *refs)

    return pl.pallas_call(
        kernel,
        in_specs=[spec(pltpu.SMEM)] + [vmem] * (len(given) - 1),
        out_specs=[vmem] * 2,
        out_shape=[array(*part.shape), array(SUB, LANES)],
        input_output_aliases={len(given) - 1: 0},
        scratch_shapes=[
            pltpu.VMEM((GEO, SUB, LANES), F32),
            pltpu.VMEM((3, rows // CHUNKS, SUB, LANES), F32),
            pltpu.VMEM((6 + FACES, SUB, LANES), F32),
        ],
        compiler_params=params(),
        name="add_target",
    )(*given)


def halo_terms(pairs_ref, before_ref, after_ref, f_ref, at):
    low, high = [None] * REACH, [None] * REACH
    rows = [before_ref[r, at, :] for r in range(REACH)]
    own = [f_ref[g, at, :] for g in range(REACH)]
    for p, (g, r) in enumerate(BEFORE_PAIRS):
        term = pairs_ref[p, at, :] * (rows[r] - own[g])
        low[g] = term if low[g] is None else low[g] + term
    rows = [after_ref[r, at, :] for r in range(REACH)]
    own = [f_ref[SUB - REACH + e, at, :] for e in range(REACH)]
    p = len(BEFORE_PAIRS)
    for e in range(REACH):
        for r in range(e + 1):
            term = pairs_ref[p, at, :] * (rows[r] - own[e])
            high[e] = term if high[e] is None else high[e] + term
            p += 1
    return low, high


def by_side(far_ref, near_ref, run):
    odd = is_odd()

    @pl.when(odd)
    def _():
        run(near_ref, far_ref)

    @pl.when(jnp.logical_not(odd))
    def _():
        run(far_ref, near_ref)


def edge_kernel(pairs_ref, far_in, near_in, old_ref, part_ref, f_ref, far_out, near_out):
    def run(before_ref, after_ref):
        down_out, up_out = (near_out, far_out) if after_ref is far_in else (far_out, near_out)

        def group(j, _):
            at = at_rows(j * SUB)
            low, high = halo_terms(pairs_ref, before_ref, after_ref, old_ref, at)
            for g in range(REACH):
                x = part_ref[g, at, :] + low[g]
                down_out[g, at, :] = x
                f_ref[g, at, :] = x
                e = SUB - REACH + g
                x = part_ref[e, at, :] + high[g]
                up_out[g, at, :] = x
                f_ref[e, at, :] = x
            return 0

        lax.fori_loop(0, part_ref.shape[1] // SUB, group, 0, unroll=2)

    by_side(far_in, near_in, run)


def edge(pairs, far, near, old, part):
    rows = part.shape[1]
    return pl.pallas_call(
        edge_kernel,
        in_specs=[spec(pltpu.VMEM)] * 5,
        out_specs=[spec(pltpu.VMEM)] * 3,
        out_shape=[array(SUB, rows, LANES), array(REACH, rows, LANES), array(REACH, rows, LANES)],
        input_output_aliases={4: 0},
        compiler_params=params(),
        name="edge",
    )(pairs, far, near, old, part)


def last_edge_kernel(
    geo_in, pairs_ref, far_ref, near_ref, f_ref, part_ref, out_hbm, sums_out, native_ref, sems
):
    rows = part_ref.shape[0] // SUB
    planes = rows // CHUNKS
    part = rows // SUB // LAST_PARTS

    def copy(i):
        at = pl.ds(i * part * SUB * SUB, part * SUB * SUB)
        return pltpu.make_async_copy(native_ref.at[at], out_hbm.at[at], sems.at[i])

    def run(before_ref, after_ref):
        for i in range(LAST_PARTS):

            def group(j, _):
                at = at_rows(j * SUB)
                low, high = halo_terms(pairs_ref, before_ref, after_ref, f_ref, at)
                terms = low + [None] * (SUB - 2 * REACH) + high
                for g in range(SUB):
                    where = (pl.ds(j * SUB * SUB + g, SUB, stride=SUB), slice(None))
                    x = part_ref[where]
                    native_ref[where] = x if terms[g] is None else x + terms[g]
                return 0

            lax.fori_loop(i * part, (i + 1) * part, group, 0, unroll=2)
            copy(i).start()

    by_side(far_ref, near_ref, run)
    y = native_polynomial_sums(native_ref, planes)
    sums_out[...] = pack_sums(finish_polynomials(y, column(geo_in[...], FIRST), planes), 0)
    for i in range(LAST_PARTS):
        copy(i).wait()


LAST_PARTS = 4


def last_edge(geo, pairs, far, near, f, part):
    return pl.pallas_call(
        last_edge_kernel,
        in_specs=[spec(pltpu.VMEM)] * 6,
        out_specs=[spec(pltpu.HBM), spec(pltpu.VMEM)],
        out_shape=[array(*part.shape), array(SUB, LANES)],
        scratch_shapes=[pltpu.VMEM(part.shape, F32), pltpu.SemaphoreType.DMA((LAST_PARTS,))],
        compiler_params=params(),
        name="last_edge",
    )(geo, pairs, far, near, f, part)


def exchange(far, near):
    size = lax.axis_size("space")
    out = []
    for x, start in ((far, 1), (near, 0)):
        pairs = [(i, i + 1) for i in range(start, size - 1, 2)]
        out.append(lax.ppermute(x, "space", pairs + [(j, i) for i, j in pairs]))
    return out


def per_device(particle_profile, neighbors, face_vectors, volumes, wall_temp):
    cells, points = particle_profile.shape
    rows = points // LANES
    plane_count = NV // lax.axis_size("vel")
    native = particle_profile.reshape(cells, rows, LANES).transpose(1, 0, 2).reshape(cells * rows, LANES)
    wall = neighbors < 0
    links = jnp.where(wall, WALL_LINK, neighbors - lax.axis_index("space") * cells)
    own = (links >= 0) & (links < cells)
    first = -SPEED_LIMIT + ((lax.axis_index("vel") * plane_count).astype(F32) + 0.5) * H
    geo = jnp.concatenate(
        [
            face_vectors.reshape(3 * FACES, cells),
            volumes[None],
            wall_temp[None],
            wall.astype(F32),
            own.astype(F32),
            jnp.full((1, cells), first, F32),
        ]
    )
    geo = jnp.pad(geo.T, ((0, 0), (0, LANES - GEO)))
    native, far, near = first_rows(native)
    far, near = exchange(far, near)
    f, sums = first_sums(links, geo, native)
    tiles = gather_sums(sums)
    pairs = geometry(links, geo, rows)
    part = flux(False, links, geo, f)
    part, absorbed = add_target(False, links, geo, None, tiles, f, part)
    f, far, near = edge(pairs, far, near, f, part)
    far, near = exchange(far, near)
    tiles = gather_sums(local_sums(links, geo, f))
    part = flux(True, links, geo, f)
    part, _ = add_target(True, links, geo, absorbed, tiles, f, part)
    native, sums = last_edge(geo, pairs, far, near, f, part)
    macro_quantities = macro(gather_sums(sums))
    evolved = native.reshape(rows, cells, LANES).transpose(1, 0, 2).reshape(cells, points)
    return evolved, macro_quantities


def solution(mesh):
    return jax.shard_map(
        per_device,
        mesh=mesh,
        in_specs=(
            P("space", "vel"),
            P(None, "space"),
            P(None, None, "space"),
            P("space"),
            P("space"),
        ),
        out_specs=(P("space", "vel"), P(None, "space")),
        check_vma=False,
    )
```

```python
import functools
import math

import jax
import jax.numpy as jnp
from jax import lax
from jax.experimental import pallas as pl
from jax.experimental.pallas import tpu as pltpu
from jax.sharding import PartitionSpec as P

NV = 64
FACES = 6
REACH = 3
STEPS = 2
LANES = 128
SUB = 8

TIME_STEP = 0.015
SHEAR = 0.1
POWER = 0.81
SPEED_LIMIT = 6.0
H = 2.0 * SPEED_LIMIT / NV
WEIGHT = H**3 * (2.0 * math.pi) ** (-1.5)

CHUNKS = NV * NV // LANES
TILES = CHUNKS // SUB

FV, VOL, WT, WALL, LOCAL, FIRST = 0, 18, 19, 20, 26, 32
GEO = 33
WALL_LINK = -64
BEFORE_PAIRS = tuple((g, r) for g in range(REACH) for r in range(g, REACH))
EMIT, ABSORB = 13, 19
SUMS = 25

F32 = jnp.float32
VMEM_LIMIT = 16 * 1024 * 1024


def lane_iota():
    return lax.broadcasted_iota(jnp.int32, (SUB, LANES), 1)


def sub_iota():
    return lax.broadcasted_iota(jnp.int32, (SUB, LANES), 0)


def half_of(lane):
    return (lane >= NV).astype(F32)


def third_component(lane):
    c = jnp.where(lane >= NV, lane - NV, lane).astype(F32)
    return -SPEED_LIMIT + (c + 0.5) * H


def tile_nodes(t):
    lane = lane_iota()
    b = (2 * SUB * t + 2 * sub_iota()).astype(F32) + half_of(lane)
    return -SPEED_LIMIT + (b + 0.5) * H, third_component(lane)


def column(tile, p):
    return jnp.broadcast_to(tile[:, p : p + 1], (SUB, LANES))


def splat(ref, i, g):
    return jnp.broadcast_to(ref[i, pl.ds(g, 1), :], (SUB, LANES))


def total(tile):
    return jnp.broadcast_to(jnp.sum(tile, axis=1, keepdims=True), (SUB, LANES))


def face_coefficients(geo_ref, k, g):
    return [splat(geo_ref, FV + FACES * i + k, g) for i in range(3)]


def at_rows(start, size=SUB):
    return pl.ds(pl.multiple_of(start, SUB), size)


def wall_tiles(wall_temp):
    rt = 1.0 / wall_temp
    scale = rt * jnp.sqrt(rt)
    out = []
    for t in range(TILES):
        xb, xc = tile_nodes(t)
        out.append(scale * jnp.exp(-0.5 * (xb * xb + xc * xc) * rt))
    return out


def unpack_geo(geo_in, geo_ref):
    tile = geo_in[...]
    for p in range(GEO):
        geo_ref[p] = column(tile, p)


def pack_sums(arrays, start):
    lane = lane_iota()
    out = jnp.zeros((SUB, LANES), F32)
    for p, x in enumerate(arrays):
        out = jnp.where(lane == start + p, total(x), out)
    return out


def over_sublanes(ref, k):
    out = ref[k, pl.ds(0, SUB, stride=SUB), :]
    for s in range(1, SUB):
        out = out + ref[k, pl.ds(s, SUB, stride=SUB), :]
    return out


def finish_polynomials(y, first, planes):
    y0, y1, y2, y3, by0, by1, by2, bby0, bby1, bbby0 = y
    m = first + 0.5 * (planes - 1) * H
    c = third_component(lane_iota())
    cc = c * c
    a = y1 + m * y0
    aa = y2 + m * (2.0 * y1 + m * y0)
    aaa = y3 + m * (3.0 * y2 + m * (3.0 * y1 + m * y0))
    ab = by1 + m * by0
    aab = by2 + m * (2.0 * by1 + m * by0)
    abb = bby1 + m * bby0
    return (
        y0,
        a,
        by0,
        c * y0,
        aa,
        bby0,
        cc * y0,
        ab,
        c * a,
        c * by0,
        aaa + abb + cc * a,
        aab + bbby0 + cc * by0,
        c * (aa + bby0 + cc * y0),
    )


def polynomial_sums(f_ref, planes, parts_ref):
    half = planes // 2

    def cell(g, _):
        out = [None] * 10
        for t in range(TILES):
            y0 = y1 = y2 = y3 = None
            for i in range(half):
                d = (i + 0.5) * H
                hi = f_ref[g, pl.ds(((half + i) * TILES + t) * SUB, SUB), :]
                lo = f_ref[g, pl.ds(((half - 1 - i) * TILES + t) * SUB, SUB), :]
                s, r = hi + lo, hi - lo
                if i == 0:
                    y0, y1, y2, y3 = s, d * r, (d * d) * s, (d * d * d) * r
                else:
                    y0, y1, y2, y3 = y0 + s, y1 + d * r, y2 + (d * d) * s, y3 + (d * d * d) * r
            b, _c = tile_nodes(t)
            bb = b * b
            terms = (y0, y1, y2, y3, b * y0, b * y1, b * y2, bb * y0, bb * y1, bb * (b * y0))
            out = [x if o is None else o + x for o, x in zip(out, terms)]
        for p in range(10):
            parts_ref[p, at_rows(g * SUB), :] = out[p]
        return 0

    lax.fori_loop(0, SUB, cell, 0)
    return [over_sublanes(parts_ref, p) for p in range(10)]


def native_polynomial_sums(native_ref, planes):
    half, side = planes // 2, CHUNKS // 2
    zero = jnp.zeros((SUB, LANES), F32)
    acc = [zero] * 10

    def plane(a, acc):
        xa = (a.astype(F32) - 0.5 * (planes - 1)) * H
        b0 = b1 = b2 = b3 = None
        for i in range(side):
            y = (2 * i + 1) * H
            hi = native_ref[at_rows((a * CHUNKS + side + i) * SUB), :]
            lo = native_ref[at_rows((a * CHUNKS + side - 1 - i) * SUB), :]
            s, d = hi + lo, hi - lo
            terms = (s, y * d, (y * y) * s, (y * y * y) * d)
            if i == 0:
                b0, b1, b2, b3 = terms
            else:
                b0, b1, b2, b3 = b0 + terms[0], b1 + terms[1], b2 + terms[2], b3 + terms[3]
        a0, a1, a2 = xa * b0, xa * b1, xa * b2
        aa0 = xa * a0
        new = (b0, a0, aa0, xa * aa0, b1, a1, xa * a1, b2, a2, b3)
        return tuple(x + z for x, z in zip(acc, new))

    g0, a0, aa0, aaa0, g1, a1, aa1, g2, a2, g3 = lax.fori_loop(0, planes, plane, tuple(acc))
    e = (half_of(lane_iota()) - 0.5) * H
    return [
        g0,
        a0,
        aa0,
        aaa0,
        g1 + e * g0,
        a1 + e * a0,
        aa1 + e * aa0,
        g2 + e * (2.0 * g1 + e * g0),
        a2 + e * (2.0 * a1 + e * a0),
        g3 + e * (3.0 * g2 + e * (3.0 * g1 + e * g0)),
    ]


def wall_sums(f_ref, planes, links_ref, geo_ref, sums_ref, with_absorbed):
    sums_ref[...] = jnp.zeros_like(sums_ref)

    def cell(g, _):
        for k in range(FACES):

            @pl.when(links_ref[k, g] == WALL_LINK)
            def _():
                v0, v1, v2 = face_coefficients(geo_ref, k, g)
                first = splat(geo_ref, FIRST, g)
                base = []
                for t in range(TILES):
                    xb, xc = tile_nodes(t)
                    base.append(v1 * xb + v2 * xc)
                if with_absorbed:
                    wt = splat(geo_ref, WT, g)
                    shape = wall_tiles(wt)

                def plane(a, acc):
                    out, back = list(acc[0]), list(acc[1])
                    xa = first + a.astype(F32) * H
                    sa = v0 * xa
                    if with_absorbed:
                        wa = jnp.exp(-0.5 * xa * xa / wt)
                    for t in range(TILES):
                        s = sa + base[t]
                        f = f_ref[g, at_rows((a * TILES + t) * SUB), :]
                        out[t] = out[t] + jnp.maximum(s, 0.0) * f
                        if with_absorbed:
                            back[t] = back[t] + jnp.maximum(-s, 0.0) * (wa * shape[t])
                    return tuple(out), tuple(back)

                zeros = (jnp.zeros((SUB, LANES), F32),) * TILES
                out, back = lax.fori_loop(0, planes, plane, (zeros, zeros), unroll=4)
                out = (out[0] + out[1]) + (out[2] + out[3])
                back = (back[0] + back[1]) + (back[2] + back[3])
                at = at_rows(g * SUB)
                sums_ref[k, at, :] = out
                if with_absorbed:
                    sums_ref[FACES + k, at, :] = back

        return 0

    lax.fori_loop(0, SUB, cell, 0)


def sums_kernel(links_ref, geo_in, f_ref, sums_out, geo_ref, parts_ref, face_ref):
    planes = f_ref.shape[1] // CHUNKS
    unpack_geo(geo_in, geo_ref)
    y = polynomial_sums(f_ref, planes, parts_ref)
    packed = pack_sums(finish_polynomials(y, geo_ref[FIRST], planes), 0)
    wall_sums(f_ref, planes, links_ref, geo_ref, face_ref, False)
    sums_out[...] = packed + pack_sums([over_sublanes(face_ref, k) for k in range(FACES)], EMIT)


def first_sums_kernel(links_ref, geo_in, native_ref, f_ref, sums_out, geo_ref, face_ref):
    rows = f_ref.shape[1]
    planes = rows // CHUNKS
    unpack_geo(geo_in, geo_ref)

    def group(j, _):
        for g in range(SUB):
            f_ref[g, at_rows(j * SUB), :] = native_ref[pl.ds(j * SUB * SUB + g, SUB, stride=SUB), :]
        return 0

    lax.fori_loop(0, rows // SUB, group, 0, unroll=2)
    y = native_polynomial_sums(native_ref, planes)
    packed = pack_sums(finish_polynomials(y, geo_ref[FIRST], planes), 0)
    wall_sums(f_ref, planes, links_ref, geo_ref, face_ref, True)
    sums_out[...] = packed + pack_sums([over_sublanes(face_ref, k) for k in range(2 * FACES)], EMIT)


def spec(space):
    return pl.BlockSpec(memory_space=space)


def array(*shape):
    return jax.ShapeDtypeStruct(shape, F32)


def params():
    return pltpu.CompilerParams(vmem_limit_bytes=VMEM_LIMIT)


def local_sums(links, geo, f):
    return pl.pallas_call(
        sums_kernel,
        in_specs=[spec(pltpu.SMEM), spec(pltpu.VMEM), spec(pltpu.VMEM)],
        out_specs=spec(pltpu.VMEM),
        out_shape=array(SUB, LANES),
        scratch_shapes=[
            pltpu.VMEM((GEO, SUB, LANES), F32),
            pltpu.VMEM((10, SUB * SUB, LANES), F32),
            pltpu.VMEM((FACES, SUB * SUB, LANES), F32),
        ],
        compiler_params=params(),
        name="local_sums",
    )(links, geo, f)


def first_sums(links, geo, native):
    rows = native.shape[0] // SUB
    return pl.pallas_call(
        first_sums_kernel,
        in_specs=[spec(pltpu.SMEM), spec(pltpu.VMEM), spec(pltpu.VMEM)],
        out_specs=[spec(pltpu.VMEM)] * 2,
        out_shape=[array(SUB, rows, LANES), array(SUB, LANES)],
        scratch_shapes=[
            pltpu.VMEM((GEO, SUB, LANES), F32),
            pltpu.VMEM((2 * FACES, SUB * SUB, LANES), F32),
        ],
        compiler_params=params(),
        name="first_sums",
    )(links, geo, native)


SPLIT_PARTS = 4


def is_odd():
    return lax.rem(lax.axis_index("space"), 2) == 1


def first_rows_kernel(native_hbm, native_ref, far1_ref, far2_ref, near_ref, sems):
    rows = native_ref.shape[0]
    part = rows // SPLIT_PARTS
    copies = [
        pltpu.make_async_copy(
            native_hbm.at[pl.ds(i * part, part)], native_ref.at[pl.ds(i * part, part)], sems.at[i]
        )
        for i in range(SPLIT_PARTS)
    ]
    for c in copies:
        c.start()
    odd = is_odd()
    far = jnp.where(odd, SUB - REACH, 0)
    near = jnp.where(odd, 0, SUB - REACH)
    groups = part // (SUB * SUB)

    for i, c in enumerate(copies):
        c.wait()

        far_ref = (far1_ref, far2_ref)[2 * i // SPLIT_PARTS]
        begin = far_ref.shape[1] // SUB * (2 * i // SPLIT_PARTS)

        def group(j, _):
            for r in range(REACH):
                x = native_ref[pl.ds(j * SUB * SUB + far + r, SUB, stride=SUB), :]
                far_ref[r, at_rows((j - begin) * SUB), :] = x
                x = native_ref[pl.ds(j * SUB * SUB + near + r, SUB, stride=SUB), :]
                near_ref[r, at_rows(j * SUB), :] = x
            return 0

        lax.fori_loop(i * groups, (i + 1) * groups, group, 0, unroll=4)


def halo_arrays(rows):
    return [array(REACH, rows // 2, LANES), array(REACH, rows // 2, LANES), array(REACH, rows, LANES)]


def first_rows(native):
    rows = native.shape[0] // SUB
    return pl.pallas_call(
        first_rows_kernel,
        in_specs=[spec(pltpu.HBM)],
        out_specs=[spec(pltpu.VMEM)] * 4,
        out_shape=[array(*native.shape)] + halo_arrays(rows),
        scratch_shapes=[pltpu.SemaphoreType.DMA((SPLIT_PARTS,))],
        compiler_params=params(),
        name="first_rows",
    )(pltpu.with_memory_space_constraint(native, pltpu.HBM))


def geometry_kernel(links_ref, geo_in, pairs_ref, geo_ref):
    rows = pairs_ref.shape[1]
    planes = rows // CHUNKS
    unpack_geo(geo_in, geo_ref)
    first = splat(geo_ref, FIRST, 0)

    def clear(j, _):
        for p in range(pairs_ref.shape[0]):
            pairs_ref[p, at_rows(j * SUB), :] = jnp.zeros((SUB, LANES), F32)
        return 0

    lax.fori_loop(0, rows // SUB, clear, 0, unroll=2)

    def cell(g, _):
        edge = g - (SUB - REACH)
        for k in range(FACES):
            j = links_ref[k, g]
            is_before = jnp.logical_and(j < 0, j != WALL_LINK)

            @pl.when(jnp.logical_or(is_before, j >= SUB))
            def _():
                before = g * REACH - g * (g - 1) // 2 + (j + REACH) - g
                after = len(BEFORE_PAIRS) + edge * (edge + 1) // 2 + j - SUB
                at_pair = jnp.where(is_before, before, after)
                scale = -TIME_STEP / splat(geo_ref, VOL, g)
                v0, v1, v2 = [scale * x for x in face_coefficients(geo_ref, k, g)]
                base = []
                for t in range(TILES):
                    xb, xc = tile_nodes(t)
                    base.append(v1 * xb + v2 * xc)

                def plane(a, _):
                    sa = v0 * (first + a.astype(F32) * H)
                    for t in range(TILES):
                        at = at_rows((a * TILES + t) * SUB)
                        pairs_ref[at_pair, at, :] = pairs_ref[at_pair, at, :] + jnp.maximum(sa + base[t], 0.0)
                    return 0

                lax.fori_loop(0, planes, plane, 0, unroll=4)

        return 0

    lax.fori_loop(0, SUB, cell, 0)


def geometry(links, geo, rows):
    return pl.pallas_call(
        geometry_kernel,
        in_specs=[spec(pltpu.SMEM), spec(pltpu.VMEM)],
        out_specs=spec(pltpu.VMEM),
        out_shape=array(2 * len(BEFORE_PAIRS), rows, LANES),
        scratch_shapes=[pltpu.VMEM((GEO, SUB, LANES), F32)],
        compiler_params=params(),
        name="geometry",
    )(links, geo)


def gather_sums(tile):
    size = lax.axis_size("vel")
    if size not in (2, 4):
        return [lax.psum(tile, "vel")]
    others = [lax.ppermute(tile, "vel", [(i, i ^ s) for i in range(size)]) for s in range(1, size)]
    return [tile, *others]


def add_tiles(refs):
    tiles = [r[...] for r in refs]
    while len(tiles) > 1:
        tiles = [tiles[i] + tiles[i + 1] for i in range(0, len(tiles), 2)]
    return tiles[0]


def quantities(tile):
    m = [WEIGHT * column(tile, p) for p in range(13)]
    n = m[0]
    rn = 1.0 / n
    u = [m[1 + i] * rn for i in range(3)]
    uu = u[0] * u[0] + u[1] * u[1] + u[2] * u[2]
    trace = m[4] + m[5] + m[6]
    width = trace - n * uu
    temperature = width * rn * (1.0 / 3.0)
    second = [[m[4], m[7], m[8]], [m[7], m[5], m[9]], [m[8], m[9], m[6]]]
    q = []
    for i in range(3):
        across = u[0] * second[i][0] + u[1] * second[i][1] + u[2] * second[i][2]
        q.append(0.5 * (m[10 + i] - 2.0 * across - u[i] * trace + 2.0 * uu * m[1 + i]))
    return n, u, temperature, q


def macro_kernel(*refs):
    out_ref = refs[-1]
    n, u, temperature, q = quantities(add_tiles(refs[:-1]))
    lane, sub = lane_iota(), sub_iota()
    for i, x in enumerate((n, *u, temperature, *q)):
        row = jnp.sum(jnp.where(lane == sub, x, 0.0), axis=0, keepdims=True)
        out_ref[pl.ds(i, 1), :] = row[:, :SUB]


def macro(tiles):
    return pl.pallas_call(
        macro_kernel,
        in_specs=[spec(pltpu.VMEM)] * len(tiles),
        out_specs=spec(pltpu.VMEM),
        out_shape=array(8, SUB),
        name="macro",
    )(*tiles)


def placer(native):
    def place(g, tile):
        if native:
            return (pl.ds(tile * SUB * SUB + g, SUB, stride=SUB), slice(None))
        return (g, at_rows(tile * SUB), slice(None))

    return place


def flux_kernel(native, links_ref, geo_in, f_ref, out_ref, geo_ref, coef):
    planes = f_ref.shape[1] // CHUNKS
    place = placer(native)
    unpack_geo(geo_in, geo_ref)
    scale = -TIME_STEP / geo_ref[VOL]
    for i in range(3):
        whole = None
        for k in range(FACES):
            x = scale * geo_ref[FV + FACES * i + k]
            coef[FACES * i + k] = x * geo_ref[LOCAL + k]
            whole = x if whole is None else whole + x
        coef[3 * FACES + i] = whole

    def cell(g, _):
        source = []
        for k in range(FACES):
            j = links_ref[k, g]
            source.append(jnp.where(jnp.logical_and(j >= 0, j < SUB), j, g))
        weight = [[splat(coef, FACES * i + k, g) for i in range(3)] for k in range(FACES)]
        whole = [splat(coef, 3 * FACES + i, g) for i in range(3)]
        x0 = splat(geo_ref, FIRST, g)
        for pair in range(TILES // 2):
            base, stay = [], []
            for t in (2 * pair, 2 * pair + 1):
                xb, xc = tile_nodes(t)
                base.append([weight[k][1] * xb + weight[k][2] * xc for k in range(FACES)])
                stay.append(1.0 + whole[1] * xb + whole[2] * xc)

            def plane(a, _):
                xa = x0 + a.astype(F32) * H
                sa = [weight[k][0] * xa for k in range(FACES)]
                stay_a = whole[0] * xa
                for i in range(2):
                    tile = a * TILES + 2 * pair + i
                    at = at_rows(tile * SUB)
                    f = f_ref[g, at, :]
                    terms = [
                        jnp.maximum(sa[k] + base[i][k], 0.0) * (f_ref[source[k], at, :] - f)
                        for k in range(FACES)
                    ]
                    inflow = (terms[0] + terms[1]) + (terms[2] + terms[3]) + (terms[4] + terms[5])
                    out_ref[place(g, tile)] = f * (stay_a + stay[i]) + inflow
                return 0

            lax.fori_loop(0, planes, plane, 0, unroll=4)
        return 0

    lax.fori_loop(0, SUB, cell, 0)


def flux(native, links, geo, f):
    rows = f.shape[1]
    return pl.pallas_call(
        functools.partial(flux_kernel, native),
        in_specs=[spec(pltpu.SMEM), spec(pltpu.VMEM), spec(pltpu.VMEM)],
        out_specs=spec(pltpu.VMEM),
        out_shape=array(SUB * rows, LANES) if native else array(SUB, rows, LANES),
        scratch_shapes=[
            pltpu.VMEM((GEO, SUB, LANES), F32),
            pltpu.VMEM((3 * FACES + 3, SUB, LANES), F32),
        ],
        compiler_params=params(),
        name="flux",
    )(links, geo, f)


def target_kernel(native, count, links_ref, geo_in, absorbed_in, *refs):
    sums_refs, (f_ref, part_ref, out_ref, sum_out, geo_ref, ta, coef) = refs[:count], refs[count:]
    planes = f_ref.shape[1] // CHUNKS
    place = placer(native)
    unpack_geo(geo_in, geo_ref)
    sums = add_tiles(sums_refs)
    sum_out[...] = sums
    absorbed = sums if absorbed_in is None else absorbed_in[...]
    n, u, temperature, q = quantities(sums)
    rt = 1.0 / temperature
    rate = TIME_STEP * n * temperature / (SHEAR * jnp.exp(POWER * jnp.log(temperature)))
    height = rate * n * rt * jnp.sqrt(rt)
    slope = (1.0 / 3.0) / (5.0 * n * temperature * temperature)
    coef[0] = rate
    coef[1] = rt
    coef[2], coef[3] = u[1], u[2]
    coef[4], coef[5] = slope * q[1], slope * q[2]
    for k in range(FACES):
        wall = geo_ref[WALL + k] > 0.5
        coef[6 + k] = column(sums, EMIT + k) / jnp.where(wall, column(absorbed, ABSORB + k), 1.0)
    first = geo_ref[FIRST]

    def plane_table(a, _):
        ca = first + a.astype(F32) * H - u[0]
        za = ca * ca * rt
        ta[0, a] = height * jnp.exp(-0.5 * za)
        ta[1, a] = slope * q[0] * ca
        ta[2, a] = za - 5.0
        return 0

    lax.fori_loop(0, planes, plane_table, 0, unroll=4)

    def cell(g, _):
        rate_g, rtg = splat(coef, 0, g), splat(coef, 1, g)
        ub, uc = splat(coef, 2, g), splat(coef, 3, g)
        qb, qc = splat(coef, 4, g), splat(coef, 5, g)
        x0 = splat(geo_ref, FIRST, g)
        bell, heat, zz = [], [], []
        for t in range(TILES):
            xb, xc = tile_nodes(t)
            cb, cc = xb - ub, xc - uc
            z = (cb * cb + cc * cc) * rtg
            bell.append(jnp.exp(-0.5 * z))
            heat.append(cb * qb + cc * qc)
            zz.append(z)

        def plane(a, _):
            height_a, heat_a, z_a = [
                jnp.broadcast_to(ta[i, a, pl.ds(g, 1), :], (SUB, LANES)) for i in range(3)
            ]
            for t in range(TILES):
                tile = a * TILES + t
                where = place(g, tile)
                f = f_ref[g, at_rows(tile * SUB), :]
                target = (height_a * bell[t]) * (1.0 + (heat_a + heat[t]) * (z_a + zz[t]))
                out_ref[where] = (part_ref[where] - rate_g * f) + target
            return 0

        lax.fori_loop(0, planes, plane, 0, unroll=4)

        for k in range(FACES):

            @pl.when(links_ref[k, g] == WALL_LINK)
            def _():
                wt = splat(geo_ref, WT, g)
                ratio = splat(coef, 6 + k, g)
                shape = [ratio * x for x in wall_tiles(wt)]
                scale = -TIME_STEP / splat(geo_ref, VOL, g)
                v0, v1, v2 = [scale * x for x in face_coefficients(geo_ref, k, g)]
                base = []
                for t in range(TILES):
                    xb, xc = tile_nodes(t)
                    base.append(v1 * xb + v2 * xc)

                def plane(a, _):
                    xa = x0 + a.astype(F32) * H
                    wa = jnp.exp(-0.5 * xa * xa / wt)
                    sa = v0 * xa
                    for t in range(TILES):
                        tile = a * TILES + t
                        where = place(g, tile)
                        f = f_ref[g, at_rows(tile * SUB), :]
                        out_ref[where] = out_ref[where] + jnp.maximum(sa + base[t], 0.0) * (wa * shape[t] - f)
                    return 0

                lax.fori_loop(0, planes, plane, 0, unroll=4)

        return 0

    lax.fori_loop(0, SUB, cell, 0)


def add_target(native, links, geo, absorbed, tiles, f, part):
    rows = f.shape[1]
    vmem = spec(pltpu.VMEM)
    given = [links, geo] + ([] if absorbed is None else [absorbed]) + list(tiles) + [f, part]

    def kernel(links_ref, geo_in, *refs):
        if absorbed is None:
            target_kernel(native, len(tiles), links_ref, geo_in, None, *refs)
        else:
            target_kernel(native, len(tiles), links_ref, geo_in, *refs)

    return pl.pallas_call(
        kernel,
        in_specs=[spec(pltpu.SMEM)] + [vmem] * (len(given) - 1),
        out_specs=[vmem] * 2,
        out_shape=[array(*part.shape), array(SUB, LANES)],
        input_output_aliases={len(given) - 1: 0},
        scratch_shapes=[
            pltpu.VMEM((GEO, SUB, LANES), F32),
            pltpu.VMEM((3, rows // CHUNKS, SUB, LANES), F32),
            pltpu.VMEM((6 + FACES, SUB, LANES), F32),
        ],
        compiler_params=params(),
        name="add_target",
    )(*given)


def halo_terms(pairs_ref, before, after, f_ref, at):
    low, high = [None] * REACH, [None] * REACH
    own = [f_ref[g, at, :] for g in range(REACH)]
    for p, (g, r) in enumerate(BEFORE_PAIRS):
        term = pairs_ref[p, at, :] * (before[r] - own[g])
        low[g] = term if low[g] is None else low[g] + term
    own = [f_ref[SUB - REACH + e, at, :] for e in range(REACH)]
    p = len(BEFORE_PAIRS)
    for e in range(REACH):
        for r in range(e + 1):
            term = pairs_ref[p, at, :] * (after[r] - own[e])
            high[e] = term if high[e] is None else high[e] + term
            p += 1
    return low, high


def over_halves(halo, groups, run):
    far1_ref, far2_ref, near_ref = halo[:3]

    def variant(half, odd, far_ref):
        begin = half * (groups // 2)

        def load(j):
            far_at, near_at = at_rows((j - begin) * SUB), at_rows(j * SUB)
            far = [far_ref[r, far_at, :] for r in range(REACH)]
            near = [near_ref[r, near_at, :] for r in range(REACH)]
            return (near, far) if odd else (far, near)

        run(half, odd, load)

    def choose(half, far_ref, wanted):
        odd = is_odd()
        for side in (True, False):

            @pl.when(jnp.logical_and(odd == side, wanted))
            def _():
                variant(half, side, far_ref)

    choose(0, far1_ref, True)
    if len(halo) == 3:
        choose(1, far2_ref, True)
    else:
        me = lax.axis_index("space")
        relayed = me < 0
        for _first, _between, last in RELAYS:
            relayed = jnp.logical_or(relayed, me == last)
        choose(1, halo[3], relayed)
        choose(1, far2_ref, jnp.logical_not(relayed))


def edge_kernel(count, pairs_ref, *refs):
    halo, (old_ref, part_ref, f_ref, far1_out, far2_out, near_out) = refs[:count], refs[count:]
    groups = part_ref.shape[1] // SUB

    def run(half, odd, load):
        far_out = (far1_out, far2_out)[half]
        begin = half * (groups // 2)

        def group(j, _):
            at, far_at = at_rows(j * SUB), at_rows((j - begin) * SUB)
            low, high = halo_terms(pairs_ref, *load(j), old_ref, at)
            for g in range(REACH):
                x = part_ref[g, at, :] + low[g]
                f_ref[g, at, :] = x
                e = SUB - REACH + g
                y = part_ref[e, at, :] + high[g]
                f_ref[e, at, :] = y
                far_out[g, far_at, :] = y if odd else x
                near_out[g, at, :] = x if odd else y
            return 0

        lax.fori_loop(begin, begin + groups // 2, group, 0, unroll=2)

    over_halves(halo, groups, run)


def edge(pairs, halo, old, part):
    rows = part.shape[1]
    return pl.pallas_call(
        functools.partial(edge_kernel, len(halo)),
        in_specs=[spec(pltpu.VMEM)] * (3 + len(halo)),
        out_specs=[spec(pltpu.VMEM)] * 4,
        out_shape=[array(SUB, rows, LANES)] + halo_arrays(rows),
        input_output_aliases={2 + len(halo): 0},
        compiler_params=params(),
        name="edge",
    )(pairs, *halo, old, part)


def last_edge_kernel(count, geo_in, pairs_ref, *refs):
    halo, (f_ref, part_ref, out_hbm, sums_out, native_ref, sems) = refs[:count], refs[count:]
    rows = part_ref.shape[0] // SUB
    planes = rows // CHUNKS
    groups = rows // SUB
    part = groups // LAST_PARTS

    def copy(i):
        at = pl.ds(i * part * SUB * SUB, part * SUB * SUB)
        return pltpu.make_async_copy(native_ref.at[at], out_hbm.at[at], sems.at[i])

    def run(half, odd, load):
        for i in range(half * LAST_PARTS // 2, (half + 1) * LAST_PARTS // 2):

            def group(j, _):
                low, high = halo_terms(pairs_ref, *load(j), f_ref, at_rows(j * SUB))
                terms = low + [None] * (SUB - 2 * REACH) + high
                for g in range(SUB):
                    where = (pl.ds(j * SUB * SUB + g, SUB, stride=SUB), slice(None))
                    x = part_ref[where]
                    native_ref[where] = x if terms[g] is None else x + terms[g]
                return 0

            lax.fori_loop(i * part, (i + 1) * part, group, 0, unroll=2)
            copy(i).start()

    over_halves(halo, groups, run)
    y = native_polynomial_sums(native_ref, planes)
    sums_out[...] = pack_sums(finish_polynomials(y, column(geo_in[...], FIRST), planes), 0)
    for i in range(LAST_PARTS):
        copy(i).wait()


LAST_PARTS = 4


def last_edge(geo, pairs, halo, f, part):
    return pl.pallas_call(
        functools.partial(last_edge_kernel, len(halo)),
        in_specs=[spec(pltpu.VMEM)] * (4 + len(halo)),
        out_specs=[spec(pltpu.HBM), spec(pltpu.VMEM)],
        out_shape=[array(*part.shape), array(SUB, LANES)],
        scratch_shapes=[pltpu.VMEM(part.shape, F32), pltpu.SemaphoreType.DMA((LAST_PARTS,))],
        compiler_params=params(),
        name="last_edge",
    )(geo, pairs, *halo, f, part)


RELAY_SLABS = 8
RELAYS = ((3, 7, 4), (4, 0, 3))


def both_ways(pairs):
    return pairs + [(j, i) for i, j in pairs]


def exchange(far1, far2, near):
    size = lax.axis_size("space")
    far_pairs = both_ways([(i, i + 1) for i in range(1, size - 1, 2)])
    near_pairs = both_ways([(i, i + 1) for i in range(0, size - 1, 2)])
    relays = RELAYS if size == RELAY_SLABS else ()
    direct = [p for p in far_pairs if p not in [(first, last) for first, _, last in relays]]
    far2 = lax.ppermute(far2, "space", direct + [(first, between) for first, between, _ in relays])
    out = [lax.ppermute(far1, "space", far_pairs), far2, lax.ppermute(near, "space", near_pairs)]
    if relays:
        out.append(lax.ppermute(far2, "space", [(between, last) for _, between, last in relays]))
    return out


def per_device(particle_profile, neighbors, face_vectors, volumes, wall_temp):
    cells, points = particle_profile.shape
    rows = points // LANES
    plane_count = NV // lax.axis_size("vel")
    native = particle_profile.reshape(cells, rows, LANES).transpose(1, 0, 2).reshape(cells * rows, LANES)
    wall = neighbors < 0
    links = jnp.where(wall, WALL_LINK, neighbors - lax.axis_index("space") * cells)
    own = (links >= 0) & (links < cells)
    first = -SPEED_LIMIT + ((lax.axis_index("vel") * plane_count).astype(F32) + 0.5) * H
    geo = jnp.concatenate(
        [
            face_vectors.reshape(3 * FACES, cells),
            volumes[None],
            wall_temp[None],
            wall.astype(F32),
            own.astype(F32),
            jnp.full((1, cells), first, F32),
        ]
    )
    geo = jnp.pad(geo.T, ((0, 0), (0, LANES - GEO)))
    native, *halo = first_rows(native)
    halo = exchange(*halo)
    f, sums = first_sums(links, geo, native)
    tiles = gather_sums(sums)
    pairs = geometry(links, geo, rows)
    part = flux(False, links, geo, f)
    part, absorbed = add_target(False, links, geo, None, tiles, f, part)
    f, *halo = edge(pairs, halo, f, part)
    halo = exchange(*halo)
    tiles = gather_sums(local_sums(links, geo, f))
    part = flux(True, links, geo, f)
    part, _ = add_target(True, links, geo, absorbed, tiles, f, part)
    native, sums = last_edge(geo, pairs, halo, f, part)
    macro_quantities = macro(gather_sums(sums))
    evolved = native.reshape(rows, cells, LANES).transpose(1, 0, 2).reshape(cells, points)
    return evolved, macro_quantities


def solution(mesh):
    return jax.shard_map(
        per_device,
        mesh=mesh,
        in_specs=(
            P("space", "vel"),
            P(None, "space"),
            P(None, None, "space"),
            P("space"),
            P("space"),
        ),
        out_specs=(P("space", "vel"), P(None, "space")),
        check_vma=False,
    )
```

```python
import functools
import math

import jax
import jax.numpy as jnp
from jax import lax
from jax.experimental import pallas as pl
from jax.experimental.pallas import tpu as pltpu
from jax.sharding import PartitionSpec as P

NV = 64
FACES = 6
REACH = 3
STEPS = 2
LANES = 128
SUB = 8

TIME_STEP = 0.015
SHEAR = 0.1
POWER = 0.81
SPEED_LIMIT = 6.0
H = 2.0 * SPEED_LIMIT / NV
WEIGHT = H**3 * (2.0 * math.pi) ** (-1.5)

CHUNKS = NV * NV // LANES
TILES = CHUNKS // SUB

FV, VOL, WT, WALL, LOCAL, FIRST = 0, 18, 19, 20, 26, 32
GEO = 33
WALL_LINK = -64
BEFORE_PAIRS = tuple((g, r) for g in range(REACH) for r in range(g, REACH))
EMIT, ABSORB = 13, 19
SUMS = 25

F32 = jnp.float32
VMEM_LIMIT = 16 * 1024 * 1024


def lane_iota():
    return lax.broadcasted_iota(jnp.int32, (SUB, LANES), 1)


def sub_iota():
    return lax.broadcasted_iota(jnp.int32, (SUB, LANES), 0)


def half_of(lane):
    return (lane >= NV).astype(F32)


def third_component(lane):
    c = jnp.where(lane >= NV, lane - NV, lane).astype(F32)
    return -SPEED_LIMIT + (c + 0.5) * H


def tile_nodes(t):
    lane = lane_iota()
    b = (2 * SUB * t + 2 * sub_iota()).astype(F32) + half_of(lane)
    return -SPEED_LIMIT + (b + 0.5) * H, third_component(lane)


def column(tile, p):
    return jnp.broadcast_to(tile[:, p : p + 1], (SUB, LANES))


def splat(ref, i, g):
    return jnp.broadcast_to(ref[i, pl.ds(g, 1), :], (SUB, LANES))


def total(tile):
    return jnp.broadcast_to(jnp.sum(tile, axis=1, keepdims=True), (SUB, LANES))


def face_coefficients(geo_ref, k, g):
    return [splat(geo_ref, FV + FACES * i + k, g) for i in range(3)]


def at_rows(start, size=SUB):
    return pl.ds(pl.multiple_of(start, SUB), size)


def wall_tiles(wall_temp):
    rt = 1.0 / wall_temp
    scale = rt * jnp.sqrt(rt)
    out = []
    for t in range(TILES):
        xb, xc = tile_nodes(t)
        out.append(scale * jnp.exp(-0.5 * (xb * xb + xc * xc) * rt))
    return out


def unpack_geo(geo_in, geo_ref):
    tile = geo_in[...]
    for p in range(GEO):
        geo_ref[p] = column(tile, p)


def pack_sums(arrays, start):
    lane = lane_iota()
    out = jnp.zeros((SUB, LANES), F32)
    for p, x in enumerate(arrays):
        out = jnp.where(lane == start + p, total(x), out)
    return out


def over_sublanes(ref, k):
    out = ref[k, pl.ds(0, SUB, stride=SUB), :]
    for s in range(1, SUB):
        out = out + ref[k, pl.ds(s, SUB, stride=SUB), :]
    return out


def finish_polynomials(y, first, planes):
    y0, y1, y2, y3, by0, by1, by2, bby0, bby1, bbby0 = y
    m = first + 0.5 * (planes - 1) * H
    c = third_component(lane_iota())
    cc = c * c
    a = y1 + m * y0
    aa = y2 + m * (2.0 * y1 + m * y0)
    aaa = y3 + m * (3.0 * y2 + m * (3.0 * y1 + m * y0))
    ab = by1 + m * by0
    aab = by2 + m * (2.0 * by1 + m * by0)
    abb = bby1 + m * bby0
    return (
        y0,
        a,
        by0,
        c * y0,
        aa,
        bby0,
        cc * y0,
        ab,
        c * a,
        c * by0,
        aaa + abb + cc * a,
        aab + bbby0 + cc * by0,
        c * (aa + bby0 + cc * y0),
    )


def polynomial_sums(f_ref, planes, parts_ref):
    half = planes // 2

    def cell(g, _):
        out = [None] * 10
        for t in range(TILES):
            y0 = y1 = y2 = y3 = None
            for i in range(half):
                d = (i + 0.5) * H
                hi = f_ref[g, pl.ds(((half + i) * TILES + t) * SUB, SUB), :]
                lo = f_ref[g, pl.ds(((half - 1 - i) * TILES + t) * SUB, SUB), :]
                s, r = hi + lo, hi - lo
                if i == 0:
                    y0, y1, y2, y3 = s, d * r, (d * d) * s, (d * d * d) * r
                else:
                    y0, y1, y2, y3 = y0 + s, y1 + d * r, y2 + (d * d) * s, y3 + (d * d * d) * r
            b, _c = tile_nodes(t)
            bb = b * b
            terms = (y0, y1, y2, y3, b * y0, b * y1, b * y2, bb * y0, bb * y1, bb * (b * y0))
            out = [x if o is None else o + x for o, x in zip(out, terms)]
        for p in range(10):
            parts_ref[p, at_rows(g * SUB), :] = out[p]
        return 0

    lax.fori_loop(0, SUB, cell, 0)
    return [over_sublanes(parts_ref, p) for p in range(10)]


def native_polynomial_sums(native_ref, planes):
    half, side = planes // 2, CHUNKS // 2
    zero = jnp.zeros((SUB, LANES), F32)
    acc = [zero] * 10

    def plane(a, acc):
        xa = (a.astype(F32) - 0.5 * (planes - 1)) * H
        b0 = b1 = b2 = b3 = None
        for i in range(side):
            y = (2 * i + 1) * H
            hi = native_ref[at_rows((a * CHUNKS + side + i) * SUB), :]
            lo = native_ref[at_rows((a * CHUNKS + side - 1 - i) * SUB), :]
            s, d = hi + lo, hi - lo
            terms = (s, y * d, (y * y) * s, (y * y * y) * d)
            if i == 0:
                b0, b1, b2, b3 = terms
            else:
                b0, b1, b2, b3 = b0 + terms[0], b1 + terms[1], b2 + terms[2], b3 + terms[3]
        a0, a1, a2 = xa * b0, xa * b1, xa * b2
        aa0 = xa * a0
        new = (b0, a0, aa0, xa * aa0, b1, a1, xa * a1, b2, a2, b3)
        return tuple(x + z for x, z in zip(acc, new))

    g0, a0, aa0, aaa0, g1, a1, aa1, g2, a2, g3 = lax.fori_loop(0, planes, plane, tuple(acc))
    e = (half_of(lane_iota()) - 0.5) * H
    return [
        g0,
        a0,
        aa0,
        aaa0,
        g1 + e * g0,
        a1 + e * a0,
        aa1 + e * aa0,
        g2 + e * (2.0 * g1 + e * g0),
        a2 + e * (2.0 * a1 + e * a0),
        g3 + e * (3.0 * g2 + e * (3.0 * g1 + e * g0)),
    ]


def wall_sums(f_ref, planes, links_ref, geo_ref, sums_ref, with_absorbed):
    sums_ref[...] = jnp.zeros_like(sums_ref)

    def cell(g, _):
        for k in range(FACES):

            @pl.when(links_ref[k, g] == WALL_LINK)
            def _():
                v0, v1, v2 = face_coefficients(geo_ref, k, g)
                first = splat(geo_ref, FIRST, g)
                base = []
                for t in range(TILES):
                    xb, xc = tile_nodes(t)
                    base.append(v1 * xb + v2 * xc)
                if with_absorbed:
                    wt = splat(geo_ref, WT, g)
                    shape = wall_tiles(wt)

                def plane(a, acc):
                    out, back = list(acc[0]), list(acc[1])
                    xa = first + a.astype(F32) * H
                    sa = v0 * xa
                    if with_absorbed:
                        wa = jnp.exp(-0.5 * xa * xa / wt)
                    for t in range(TILES):
                        s = sa + base[t]
                        f = f_ref[g, at_rows((a * TILES + t) * SUB), :]
                        out[t] = out[t] + jnp.maximum(s, 0.0) * f
                        if with_absorbed:
                            back[t] = back[t] + jnp.maximum(-s, 0.0) * (wa * shape[t])
                    return tuple(out), tuple(back)

                zeros = (jnp.zeros((SUB, LANES), F32),) * TILES
                out, back = lax.fori_loop(0, planes, plane, (zeros, zeros), unroll=4)
                out = (out[0] + out[1]) + (out[2] + out[3])
                back = (back[0] + back[1]) + (back[2] + back[3])
                at = at_rows(g * SUB)
                sums_ref[k, at, :] = out
                if with_absorbed:
                    sums_ref[FACES + k, at, :] = back

        return 0

    lax.fori_loop(0, SUB, cell, 0)


def sums_kernel(links_ref, geo_in, f_ref, sums_out, geo_ref, parts_ref, face_ref):
    planes = f_ref.shape[1] // CHUNKS
    unpack_geo(geo_in, geo_ref)
    y = polynomial_sums(f_ref, planes, parts_ref)
    packed = pack_sums(finish_polynomials(y, geo_ref[FIRST], planes), 0)
    wall_sums(f_ref, planes, links_ref, geo_ref, face_ref, False)
    sums_out[...] = packed + pack_sums([over_sublanes(face_ref, k) for k in range(FACES)], EMIT)


def first_sums_kernel(links_ref, geo_in, native_ref, f_ref, sums_out, geo_ref, face_ref):
    rows = f_ref.shape[1]
    planes = rows // CHUNKS
    unpack_geo(geo_in, geo_ref)

    def group(j, _):
        for g in range(SUB):
            f_ref[g, at_rows(j * SUB), :] = native_ref[pl.ds(j * SUB * SUB + g, SUB, stride=SUB), :]
        return 0

    lax.fori_loop(0, rows // SUB, group, 0, unroll=2)
    y = native_polynomial_sums(native_ref, planes)
    packed = pack_sums(finish_polynomials(y, geo_ref[FIRST], planes), 0)
    wall_sums(f_ref, planes, links_ref, geo_ref, face_ref, True)
    sums_out[...] = packed + pack_sums([over_sublanes(face_ref, k) for k in range(2 * FACES)], EMIT)


def spec(space):
    return pl.BlockSpec(memory_space=space)


def array(*shape):
    return jax.ShapeDtypeStruct(shape, F32)


def params():
    return pltpu.CompilerParams(vmem_limit_bytes=VMEM_LIMIT)


def traffic(rows, profiles):
    size = SUB * rows * LANES
    return pl.CostEstimate(flops=8 * profiles * size, bytes_accessed=4 * profiles * size, transcendentals=0)


def local_sums(links, geo, f):
    return pl.pallas_call(
        sums_kernel,
        in_specs=[spec(pltpu.SMEM), spec(pltpu.VMEM), spec(pltpu.VMEM)],
        out_specs=spec(pltpu.VMEM),
        out_shape=array(SUB, LANES),
        scratch_shapes=[
            pltpu.VMEM((GEO, SUB, LANES), F32),
            pltpu.VMEM((10, SUB * SUB, LANES), F32),
            pltpu.VMEM((FACES, SUB * SUB, LANES), F32),
        ],
        compiler_params=params(),
        cost_estimate=traffic(f.shape[1], 4),
        name="local_sums",
    )(links, geo, f)


def first_sums(links, geo, native):
    rows = native.shape[0] // SUB
    return pl.pallas_call(
        first_sums_kernel,
        in_specs=[spec(pltpu.SMEM), spec(pltpu.VMEM), spec(pltpu.VMEM)],
        out_specs=[spec(pltpu.VMEM)] * 2,
        out_shape=[array(SUB, rows, LANES), array(SUB, LANES)],
        scratch_shapes=[
            pltpu.VMEM((GEO, SUB, LANES), F32),
            pltpu.VMEM((2 * FACES, SUB * SUB, LANES), F32),
        ],
        compiler_params=params(),
        cost_estimate=traffic(rows, 5),
        name="first_sums",
    )(links, geo, native)


SPLIT_PARTS = 4


def is_odd():
    return lax.rem(lax.axis_index("space"), 2) == 1


def first_rows_kernel(native_hbm, native_ref, far1_ref, far2_ref, near_ref, sems):
    rows = native_ref.shape[0]
    part = rows // SPLIT_PARTS
    copies = [
        pltpu.make_async_copy(
            native_hbm.at[pl.ds(i * part, part)], native_ref.at[pl.ds(i * part, part)], sems.at[i]
        )
        for i in range(SPLIT_PARTS)
    ]
    for c in copies:
        c.start()
    odd = is_odd()
    far = jnp.where(odd, SUB - REACH, 0)
    near = jnp.where(odd, 0, SUB - REACH)
    groups = part // (SUB * SUB)

    for i, c in enumerate(copies):
        c.wait()

        far_ref = (far1_ref, far2_ref)[2 * i // SPLIT_PARTS]
        begin = far_ref.shape[1] // SUB * (2 * i // SPLIT_PARTS)

        def group(j, _):
            for r in range(REACH):
                x = native_ref[pl.ds(j * SUB * SUB + far + r, SUB, stride=SUB), :]
                far_ref[r, at_rows((j - begin) * SUB), :] = x
                x = native_ref[pl.ds(j * SUB * SUB + near + r, SUB, stride=SUB), :]
                near_ref[r, at_rows(j * SUB), :] = x
            return 0

        lax.fori_loop(i * groups, (i + 1) * groups, group, 0, unroll=4)


def halo_arrays(rows):
    return [array(REACH, rows // 2, LANES), array(REACH, rows // 2, LANES), array(REACH, rows, LANES)]


def first_rows(native):
    rows = native.shape[0] // SUB
    return pl.pallas_call(
        first_rows_kernel,
        in_specs=[spec(pltpu.HBM)],
        out_specs=[spec(pltpu.VMEM)] * 4,
        out_shape=[array(*native.shape)] + halo_arrays(rows),
        scratch_shapes=[pltpu.SemaphoreType.DMA((SPLIT_PARTS,))],
        compiler_params=params(),
        cost_estimate=traffic(rows, 4),
        name="first_rows",
    )(pltpu.with_memory_space_constraint(native, pltpu.HBM))


def geometry_kernel(links_ref, geo_in, pairs_ref, geo_ref):
    rows = pairs_ref.shape[1]
    planes = rows // CHUNKS
    unpack_geo(geo_in, geo_ref)
    first = splat(geo_ref, FIRST, 0)

    def clear(j, _):
        for p in range(pairs_ref.shape[0]):
            pairs_ref[p, at_rows(j * SUB), :] = jnp.zeros((SUB, LANES), F32)
        return 0

    lax.fori_loop(0, rows // SUB, clear, 0, unroll=2)

    def cell(g, _):
        edge = g - (SUB - REACH)
        for k in range(FACES):
            j = links_ref[k, g]
            is_before = jnp.logical_and(j < 0, j != WALL_LINK)

            @pl.when(jnp.logical_or(is_before, j >= SUB))
            def _():
                before = g * REACH - g * (g - 1) // 2 + (j + REACH) - g
                after = len(BEFORE_PAIRS) + edge * (edge + 1) // 2 + j - SUB
                at_pair = jnp.where(is_before, before, after)
                scale = -TIME_STEP / splat(geo_ref, VOL, g)
                v0, v1, v2 = [scale * x for x in face_coefficients(geo_ref, k, g)]
                base = []
                for t in range(TILES):
                    xb, xc = tile_nodes(t)
                    base.append(v1 * xb + v2 * xc)

                def plane(a, _):
                    sa = v0 * (first + a.astype(F32) * H)
                    for t in range(TILES):
                        at = at_rows((a * TILES + t) * SUB)
                        pairs_ref[at_pair, at, :] = pairs_ref[at_pair, at, :] + jnp.maximum(sa + base[t], 0.0)
                    return 0

                lax.fori_loop(0, planes, plane, 0, unroll=4)

        return 0

    lax.fori_loop(0, SUB, cell, 0)


def geometry(links, geo, rows):
    return pl.pallas_call(
        geometry_kernel,
        in_specs=[spec(pltpu.SMEM), spec(pltpu.VMEM)],
        out_specs=spec(pltpu.VMEM),
        out_shape=array(2 * len(BEFORE_PAIRS), rows, LANES),
        scratch_shapes=[pltpu.VMEM((GEO, SUB, LANES), F32)],
        compiler_params=params(),
        cost_estimate=traffic(rows, 4),
        name="geometry",
    )(links, geo)


def gather_sums(tile):
    size = lax.axis_size("vel")
    if size not in (2, 4):
        return [lax.psum(tile, "vel")]
    others = [lax.ppermute(tile, "vel", [(i, i ^ s) for i in range(size)]) for s in range(1, size)]
    return [tile, *others]


def add_tiles(refs):
    tiles = [r[...] for r in refs]
    while len(tiles) > 1:
        tiles = [tiles[i] + tiles[i + 1] for i in range(0, len(tiles), 2)]
    return tiles[0]


def quantities(tile):
    m = [WEIGHT * column(tile, p) for p in range(13)]
    n = m[0]
    rn = 1.0 / n
    u = [m[1 + i] * rn for i in range(3)]
    uu = u[0] * u[0] + u[1] * u[1] + u[2] * u[2]
    trace = m[4] + m[5] + m[6]
    width = trace - n * uu
    temperature = width * rn * (1.0 / 3.0)
    second = [[m[4], m[7], m[8]], [m[7], m[5], m[9]], [m[8], m[9], m[6]]]
    q = []
    for i in range(3):
        across = u[0] * second[i][0] + u[1] * second[i][1] + u[2] * second[i][2]
        q.append(0.5 * (m[10 + i] - 2.0 * across - u[i] * trace + 2.0 * uu * m[1 + i]))
    return n, u, temperature, q


def macro_kernel(*refs):
    out_ref = refs[-1]
    n, u, temperature, q = quantities(add_tiles(refs[:-1]))
    lane, sub = lane_iota(), sub_iota()
    for i, x in enumerate((n, *u, temperature, *q)):
        row = jnp.sum(jnp.where(lane == sub, x, 0.0), axis=0, keepdims=True)
        out_ref[pl.ds(i, 1), :] = row[:, :SUB]


def macro(tiles):
    return pl.pallas_call(
        macro_kernel,
        in_specs=[spec(pltpu.VMEM)] * len(tiles),
        out_specs=spec(pltpu.VMEM),
        out_shape=array(8, SUB),
        name="macro",
    )(*tiles)


def placer(native):
    def place(g, tile):
        if native:
            return (pl.ds(tile * SUB * SUB + g, SUB, stride=SUB), slice(None))
        return (g, at_rows(tile * SUB), slice(None))

    return place


def flux_kernel(native, links_ref, geo_in, f_ref, out_ref, geo_ref, coef):
    planes = f_ref.shape[1] // CHUNKS
    place = placer(native)
    unpack_geo(geo_in, geo_ref)
    scale = -TIME_STEP / geo_ref[VOL]
    for i in range(3):
        whole = None
        for k in range(FACES):
            x = scale * geo_ref[FV + FACES * i + k]
            coef[FACES * i + k] = x * geo_ref[LOCAL + k]
            whole = x if whole is None else whole + x
        coef[3 * FACES + i] = whole

    def cell(g, _):
        source = []
        for k in range(FACES):
            j = links_ref[k, g]
            source.append(jnp.where(jnp.logical_and(j >= 0, j < SUB), j, g))
        weight = [[splat(coef, FACES * i + k, g) for i in range(3)] for k in range(FACES)]
        whole = [splat(coef, 3 * FACES + i, g) for i in range(3)]
        x0 = splat(geo_ref, FIRST, g)
        for pair in range(TILES // 2):
            base, stay = [], []
            for t in (2 * pair, 2 * pair + 1):
                xb, xc = tile_nodes(t)
                base.append([weight[k][1] * xb + weight[k][2] * xc for k in range(FACES)])
                stay.append(1.0 + whole[1] * xb + whole[2] * xc)

            def plane(a, _):
                xa = x0 + a.astype(F32) * H
                sa = [weight[k][0] * xa for k in range(FACES)]
                stay_a = whole[0] * xa
                for i in range(2):
                    tile = a * TILES + 2 * pair + i
                    at = at_rows(tile * SUB)
                    f = f_ref[g, at, :]
                    terms = [
                        jnp.maximum(sa[k] + base[i][k], 0.0) * (f_ref[source[k], at, :] - f)
                        for k in range(FACES)
                    ]
                    inflow = (terms[0] + terms[1]) + (terms[2] + terms[3]) + (terms[4] + terms[5])
                    out_ref[place(g, tile)] = f * (stay_a + stay[i]) + inflow
                return 0

            lax.fori_loop(0, planes, plane, 0, unroll=4)
        return 0

    lax.fori_loop(0, SUB, cell, 0)


def flux(native, links, geo, f):
    rows = f.shape[1]
    return pl.pallas_call(
        functools.partial(flux_kernel, native),
        in_specs=[spec(pltpu.SMEM), spec(pltpu.VMEM), spec(pltpu.VMEM)],
        out_specs=spec(pltpu.VMEM),
        out_shape=array(SUB * rows, LANES) if native else array(SUB, rows, LANES),
        scratch_shapes=[
            pltpu.VMEM((GEO, SUB, LANES), F32),
            pltpu.VMEM((3 * FACES + 3, SUB, LANES), F32),
        ],
        compiler_params=params(),
        cost_estimate=traffic(rows, 7),
        name="flux",
    )(links, geo, f)


def target_kernel(native, count, links_ref, geo_in, absorbed_in, *refs):
    sums_refs, (f_ref, part_ref, out_ref, sum_out, geo_ref, ta, coef) = refs[:count], refs[count:]
    planes = f_ref.shape[1] // CHUNKS
    place = placer(native)
    unpack_geo(geo_in, geo_ref)
    sums = add_tiles(sums_refs)
    sum_out[...] = sums
    absorbed = sums if absorbed_in is None else absorbed_in[...]
    n, u, temperature, q = quantities(sums)
    rt = 1.0 / temperature
    rate = TIME_STEP * n * temperature / (SHEAR * jnp.exp(POWER * jnp.log(temperature)))
    height = rate * n * rt * jnp.sqrt(rt)
    slope = (1.0 / 3.0) / (5.0 * n * temperature * temperature)
    coef[0] = rate
    coef[1] = rt
    coef[2], coef[3] = u[1], u[2]
    coef[4], coef[5] = slope * q[1], slope * q[2]
    for k in range(FACES):
        wall = geo_ref[WALL + k] > 0.5
        coef[6 + k] = column(sums, EMIT + k) / jnp.where(wall, column(absorbed, ABSORB + k), 1.0)
    first = geo_ref[FIRST]

    def plane_table(a, _):
        ca = first + a.astype(F32) * H - u[0]
        za = ca * ca * rt
        ta[0, a] = height * jnp.exp(-0.5 * za)
        ta[1, a] = slope * q[0] * ca
        ta[2, a] = za - 5.0
        return 0

    lax.fori_loop(0, planes, plane_table, 0, unroll=4)

    def cell(g, _):
        rate_g, rtg = splat(coef, 0, g), splat(coef, 1, g)
        ub, uc = splat(coef, 2, g), splat(coef, 3, g)
        qb, qc = splat(coef, 4, g), splat(coef, 5, g)
        x0 = splat(geo_ref, FIRST, g)
        bell, heat, zz = [], [], []
        for t in range(TILES):
            xb, xc = tile_nodes(t)
            cb, cc = xb - ub, xc - uc
            z = (cb * cb + cc * cc) * rtg
            bell.append(jnp.exp(-0.5 * z))
            heat.append(cb * qb + cc * qc)
            zz.append(z)

        def plane(a, _):
            height_a, heat_a, z_a = [
                jnp.broadcast_to(ta[i, a, pl.ds(g, 1), :], (SUB, LANES)) for i in range(3)
            ]
            for t in range(TILES):
                tile = a * TILES + t
                where = place(g, tile)
                f = f_ref[g, at_rows(tile * SUB), :]
                target = (height_a * bell[t]) * (1.0 + (heat_a + heat[t]) * (z_a + zz[t]))
                out_ref[where] = (part_ref[where] - rate_g * f) + target
            return 0

        lax.fori_loop(0, planes, plane, 0, unroll=4)

        for k in range(FACES):

            @pl.when(links_ref[k, g] == WALL_LINK)
            def _():
                wt = splat(geo_ref, WT, g)
                ratio = splat(coef, 6 + k, g)
                shape = [ratio * x for x in wall_tiles(wt)]
                scale = -TIME_STEP / splat(geo_ref, VOL, g)
                v0, v1, v2 = [scale * x for x in face_coefficients(geo_ref, k, g)]
                base = []
                for t in range(TILES):
                    xb, xc = tile_nodes(t)
                    base.append(v1 * xb + v2 * xc)

                def plane(a, _):
                    xa = x0 + a.astype(F32) * H
                    wa = jnp.exp(-0.5 * xa * xa / wt)
                    sa = v0 * xa
                    for t in range(TILES):
                        tile = a * TILES + t
                        where = place(g, tile)
                        f = f_ref[g, at_rows(tile * SUB), :]
                        out_ref[where] = out_ref[where] + jnp.maximum(sa + base[t], 0.0) * (wa * shape[t] - f)
                    return 0

                lax.fori_loop(0, planes, plane, 0, unroll=4)

        return 0

    lax.fori_loop(0, SUB, cell, 0)


def add_target(native, links, geo, absorbed, tiles, f, part):
    rows = f.shape[1]
    vmem = spec(pltpu.VMEM)
    given = [links, geo] + ([] if absorbed is None else [absorbed]) + list(tiles) + [f, part]

    def kernel(links_ref, geo_in, *refs):
        if absorbed is None:
            target_kernel(native, len(tiles), links_ref, geo_in, None, *refs)
        else:
            target_kernel(native, len(tiles), links_ref, geo_in, *refs)

    return pl.pallas_call(
        kernel,
        in_specs=[spec(pltpu.SMEM)] + [vmem] * (len(given) - 1),
        out_specs=[vmem] * 2,
        out_shape=[array(*part.shape), array(SUB, LANES)],
        input_output_aliases={len(given) - 1: 0},
        scratch_shapes=[
            pltpu.VMEM((GEO, SUB, LANES), F32),
            pltpu.VMEM((3, rows // CHUNKS, SUB, LANES), F32),
            pltpu.VMEM((6 + FACES, SUB, LANES), F32),
        ],
        compiler_params=params(),
        cost_estimate=traffic(rows, 7),
        name="add_target",
    )(*given)


def halo_terms(pairs_ref, before, after, f_ref, at):
    low, high = [None] * REACH, [None] * REACH
    own = [f_ref[g, at, :] for g in range(REACH)]
    for p, (g, r) in enumerate(BEFORE_PAIRS):
        term = pairs_ref[p, at, :] * (before[r] - own[g])
        low[g] = term if low[g] is None else low[g] + term
    own = [f_ref[SUB - REACH + e, at, :] for e in range(REACH)]
    p = len(BEFORE_PAIRS)
    for e in range(REACH):
        for r in range(e + 1):
            term = pairs_ref[p, at, :] * (after[r] - own[e])
            high[e] = term if high[e] is None else high[e] + term
            p += 1
    return low, high


def over_halves(halo, groups, run):
    far1_ref, far2_ref, near_ref = halo[:3]

    def variant(half, odd, far_ref):
        begin = half * (groups // 2)

        def load(j):
            far_at, near_at = at_rows((j - begin) * SUB), at_rows(j * SUB)
            far = [far_ref[r, far_at, :] for r in range(REACH)]
            near = [near_ref[r, near_at, :] for r in range(REACH)]
            return (near, far) if odd else (far, near)

        run(half, odd, load)

    def choose(half, far_ref, wanted):
        odd = is_odd()
        for side in (True, False):

            @pl.when(jnp.logical_and(odd == side, wanted))
            def _():
                variant(half, side, far_ref)

    choose(0, far1_ref, True)
    if len(halo) == 3:
        choose(1, far2_ref, True)
    else:
        me = lax.axis_index("space")
        relayed = me < 0
        for _first, _between, last in RELAYS:
            relayed = jnp.logical_or(relayed, me == last)
        choose(1, halo[3], relayed)
        choose(1, far2_ref, jnp.logical_not(relayed))


def edge_kernel(count, pairs_ref, *refs):
    halo, (old_ref, part_ref, f_ref, far1_out, far2_out, near_out) = refs[:count], refs[count:]
    groups = part_ref.shape[1] // SUB

    def run(half, odd, load):
        far_out = (far1_out, far2_out)[half]
        begin = half * (groups // 2)

        def group(j, _):
            at, far_at = at_rows(j * SUB), at_rows((j - begin) * SUB)
            low, high = halo_terms(pairs_ref, *load(j), old_ref, at)
            for g in range(REACH):
                x = part_ref[g, at, :] + low[g]
                f_ref[g, at, :] = x
                e = SUB - REACH + g
                y = part_ref[e, at, :] + high[g]
                f_ref[e, at, :] = y
                far_out[g, far_at, :] = y if odd else x
                near_out[g, at, :] = x if odd else y
            return 0

        lax.fori_loop(begin, begin + groups // 2, group, 0, unroll=2)

    over_halves(halo, groups, run)


def edge(pairs, halo, old, part):
    rows = part.shape[1]
    return pl.pallas_call(
        functools.partial(edge_kernel, len(halo)),
        in_specs=[spec(pltpu.VMEM)] * (3 + len(halo)),
        out_specs=[spec(pltpu.VMEM)] * 4,
        out_shape=[array(SUB, rows, LANES)] + halo_arrays(rows),
        input_output_aliases={2 + len(halo): 0},
        compiler_params=params(),
        cost_estimate=traffic(rows, 4),
        name="edge",
    )(pairs, *halo, old, part)


def last_edge_kernel(count, geo_in, pairs_ref, *refs):
    halo, (f_ref, part_ref, out_hbm, sums_out, native_ref, sems) = refs[:count], refs[count:]
    rows = part_ref.shape[0] // SUB
    planes = rows // CHUNKS
    groups = rows // SUB
    part = groups // LAST_PARTS

    def copy(i):
        at = pl.ds(i * part * SUB * SUB, part * SUB * SUB)
        return pltpu.make_async_copy(native_ref.at[at], out_hbm.at[at], sems.at[i])

    def run(half, odd, load):
        for i in range(half * LAST_PARTS // 2, (half + 1) * LAST_PARTS // 2):

            def group(j, _):
                low, high = halo_terms(pairs_ref, *load(j), f_ref, at_rows(j * SUB))
                terms = low + [None] * (SUB - 2 * REACH) + high
                for g in range(SUB):
                    where = (pl.ds(j * SUB * SUB + g, SUB, stride=SUB), slice(None))
                    x = part_ref[where]
                    native_ref[where] = x if terms[g] is None else x + terms[g]
                return 0

            lax.fori_loop(i * part, (i + 1) * part, group, 0, unroll=2)
            copy(i).start()

    over_halves(halo, groups, run)
    y = native_polynomial_sums(native_ref, planes)
    sums_out[...] = pack_sums(finish_polynomials(y, column(geo_in[...], FIRST), planes), 0)
    for i in range(LAST_PARTS):
        copy(i).wait()


LAST_PARTS = 4


def last_edge(geo, pairs, halo, f, part):
    return pl.pallas_call(
        functools.partial(last_edge_kernel, len(halo)),
        in_specs=[spec(pltpu.VMEM)] * (4 + len(halo)),
        out_specs=[spec(pltpu.HBM), spec(pltpu.VMEM)],
        out_shape=[array(*part.shape), array(SUB, LANES)],
        scratch_shapes=[pltpu.VMEM(part.shape, F32), pltpu.SemaphoreType.DMA((LAST_PARTS,))],
        compiler_params=params(),
        cost_estimate=traffic(part.shape[0] // SUB, 4),
        name="last_edge",
    )(geo, pairs, *halo, f, part)


RELAY_SLABS = 8
RELAYS = ((3, 7, 4), (4, 0, 3))


def both_ways(pairs):
    return pairs + [(j, i) for i, j in pairs]


def exchange(far1, far2, near):
    size = lax.axis_size("space")
    far_pairs = both_ways([(i, i + 1) for i in range(1, size - 1, 2)])
    near_pairs = both_ways([(i, i + 1) for i in range(0, size - 1, 2)])
    relays = RELAYS if size == RELAY_SLABS else ()
    direct = [p for p in far_pairs if p not in [(first, last) for first, _, last in relays]]
    far2 = lax.ppermute(far2, "space", direct + [(first, between) for first, between, _ in relays])
    return [lax.ppermute(far1, "space", far_pairs), far2, lax.ppermute(near, "space", near_pairs)]


def pass_on(halo, after):
    size = lax.axis_size("space")
    if size != RELAY_SLABS:
        return halo
    rows, _ = lax.optimization_barrier((halo[1], after))
    return [*halo, lax.ppermute(rows, "space", [(between, last) for _, between, last in RELAYS])]


def per_device(particle_profile, neighbors, face_vectors, volumes, wall_temp):
    cells, points = particle_profile.shape
    rows = points // LANES
    plane_count = NV // lax.axis_size("vel")
    native = particle_profile.reshape(cells, rows, LANES).transpose(1, 0, 2).reshape(cells * rows, LANES)
    wall = neighbors < 0
    links = jnp.where(wall, WALL_LINK, neighbors - lax.axis_index("space") * cells)
    own = (links >= 0) & (links < cells)
    first = -SPEED_LIMIT + ((lax.axis_index("vel") * plane_count).astype(F32) + 0.5) * H
    geo = jnp.concatenate(
        [
            face_vectors.reshape(3 * FACES, cells),
            volumes[None],
            wall_temp[None],
            wall.astype(F32),
            own.astype(F32),
            jnp.full((1, cells), first, F32),
        ]
    )
    geo = jnp.pad(geo.T, ((0, 0), (0, LANES - GEO)))
    native, *halo = first_rows(native)
    halo = exchange(*halo)
    f, sums = first_sums(links, geo, native)
    halo = pass_on(halo, sums)
    tiles = gather_sums(sums)
    pairs = geometry(links, geo, rows)
    part = flux(False, links, geo, f)
    part, absorbed = add_target(False, links, geo, None, tiles, f, part)
    f, *halo = edge(pairs, halo, f, part)
    halo = exchange(*halo)
    sums = local_sums(links, geo, f)
    halo = pass_on(halo, sums)
    tiles = gather_sums(sums)
    part = flux(True, links, geo, f)
    part, _ = add_target(True, links, geo, absorbed, tiles, f, part)
    native, sums = last_edge(geo, pairs, halo, f, part)
    macro_quantities = macro(gather_sums(sums))
    evolved = native.reshape(rows, cells, LANES).transpose(1, 0, 2).reshape(cells, points)
    return evolved, macro_quantities


def solution(mesh):
    return jax.shard_map(
        per_device,
        mesh=mesh,
        in_specs=(
            P("space", "vel"),
            P(None, "space"),
            P(None, None, "space"),
            P("space"),
            P("space"),
        ),
        out_specs=(P("space", "vel"), P(None, "space")),
        check_vma=False,
    )
```

```python
import functools
import math

import jax
import jax.numpy as jnp
from jax import lax
from jax.experimental import pallas as pl
from jax.experimental.pallas import tpu as pltpu
from jax.sharding import PartitionSpec as P

NV = 64
FACES = 6
REACH = 3
STEPS = 2
LANES = 128
SUB = 8

TIME_STEP = 0.015
SHEAR = 0.1
POWER = 0.81
SPEED_LIMIT = 6.0
H = 2.0 * SPEED_LIMIT / NV
WEIGHT = H**3 * (2.0 * math.pi) ** (-1.5)

CHUNKS = NV * NV // LANES
TILES = CHUNKS // SUB

FV, VOL, WT, WALL, LOCAL, FIRST = 0, 18, 19, 20, 26, 32
GEO = 33
WALL_LINK = -64
BEFORE_PAIRS = tuple((g, r) for g in range(REACH) for r in range(g, REACH))
EMIT, ABSORB = 13, 19
SUMS = 25

F32 = jnp.float32
VMEM_LIMIT = 16 * 1024 * 1024


def lane_iota():
    return lax.broadcasted_iota(jnp.int32, (SUB, LANES), 1)


def sub_iota():
    return lax.broadcasted_iota(jnp.int32, (SUB, LANES), 0)


def half_of(lane):
    return (lane >= NV).astype(F32)


def third_component(lane):
    c = jnp.where(lane >= NV, lane - NV, lane).astype(F32)
    return -SPEED_LIMIT + (c + 0.5) * H


def tile_nodes(t):
    lane = lane_iota()
    b = (2 * SUB * t + 2 * sub_iota()).astype(F32) + half_of(lane)
    return -SPEED_LIMIT + (b + 0.5) * H, third_component(lane)


def column(tile, p):
    return jnp.broadcast_to(tile[:, p : p + 1], (SUB, LANES))


def splat(ref, i, g):
    return jnp.broadcast_to(ref[i, pl.ds(g, 1), :], (SUB, LANES))


def total(tile):
    return jnp.broadcast_to(jnp.sum(tile, axis=1, keepdims=True), (SUB, LANES))


def face_coefficients(geo_ref, k, g):
    return [splat(geo_ref, FV + FACES * i + k, g) for i in range(3)]


def at_rows(start, size=SUB):
    return pl.ds(pl.multiple_of(start, SUB), size)


def wall_tiles(wall_temp):
    rt = 1.0 / wall_temp
    scale = rt * jnp.sqrt(rt)
    out = []
    for t in range(TILES):
        xb, xc = tile_nodes(t)
        out.append(scale * jnp.exp(-0.5 * (xb * xb + xc * xc) * rt))
    return out


def unpack_geo(geo_in, geo_ref):
    tile = geo_in[...]
    for p in range(GEO):
        geo_ref[p] = column(tile, p)


def pack_sums(arrays, start):
    lane = lane_iota()
    out = jnp.zeros((SUB, LANES), F32)
    for p, x in enumerate(arrays):
        out = jnp.where(lane == start + p, total(x), out)
    return out


def over_sublanes(ref, k):
    out = ref[k, pl.ds(0, SUB, stride=SUB), :]
    for s in range(1, SUB):
        out = out + ref[k, pl.ds(s, SUB, stride=SUB), :]
    return out


def finish_polynomials(y, first, planes):
    y0, y1, y2, y3, by0, by1, by2, bby0, bby1, bbby0 = y
    m = first + 0.5 * (planes - 1) * H
    c = third_component(lane_iota())
    cc = c * c
    a = y1 + m * y0
    aa = y2 + m * (2.0 * y1 + m * y0)
    aaa = y3 + m * (3.0 * y2 + m * (3.0 * y1 + m * y0))
    ab = by1 + m * by0
    aab = by2 + m * (2.0 * by1 + m * by0)
    abb = bby1 + m * bby0
    return (
        y0,
        a,
        by0,
        c * y0,
        aa,
        bby0,
        cc * y0,
        ab,
        c * a,
        c * by0,
        aaa + abb + cc * a,
        aab + bbby0 + cc * by0,
        c * (aa + bby0 + cc * y0),
    )


def polynomial_sums(f_ref, planes, parts_ref):
    half = planes // 2

    def cell(g, _):
        out = [None] * 10
        for t in range(TILES):
            y0 = y1 = y2 = y3 = None
            for i in range(half):
                d = (i + 0.5) * H
                hi = f_ref[g, pl.ds(((half + i) * TILES + t) * SUB, SUB), :]
                lo = f_ref[g, pl.ds(((half - 1 - i) * TILES + t) * SUB, SUB), :]
                s, r = hi + lo, hi - lo
                if i == 0:
                    y0, y1, y2, y3 = s, d * r, (d * d) * s, (d * d * d) * r
                else:
                    y0, y1, y2, y3 = y0 + s, y1 + d * r, y2 + (d * d) * s, y3 + (d * d * d) * r
            b, _c = tile_nodes(t)
            bb = b * b
            terms = (y0, y1, y2, y3, b * y0, b * y1, b * y2, bb * y0, bb * y1, bb * (b * y0))
            out = [x if o is None else o + x for o, x in zip(out, terms)]
        for p in range(10):
            parts_ref[p, at_rows(g * SUB), :] = out[p]
        return 0

    lax.fori_loop(0, SUB, cell, 0)
    return [over_sublanes(parts_ref, p) for p in range(10)]


def native_polynomial_sums(native_ref, planes):
    half, side = planes // 2, CHUNKS // 2
    zero = jnp.zeros((SUB, LANES), F32)
    acc = [zero] * 10

    def plane(a, acc):
        xa = (a.astype(F32) - 0.5 * (planes - 1)) * H
        b0 = b1 = b2 = b3 = None
        for i in range(side):
            y = (2 * i + 1) * H
            hi = native_ref[at_rows((a * CHUNKS + side + i) * SUB), :]
            lo = native_ref[at_rows((a * CHUNKS + side - 1 - i) * SUB), :]
            s, d = hi + lo, hi - lo
            terms = (s, y * d, (y * y) * s, (y * y * y) * d)
            if i == 0:
                b0, b1, b2, b3 = terms
            else:
                b0, b1, b2, b3 = b0 + terms[0], b1 + terms[1], b2 + terms[2], b3 + terms[3]
        a0, a1, a2 = xa * b0, xa * b1, xa * b2
        aa0 = xa * a0
        new = (b0, a0, aa0, xa * aa0, b1, a1, xa * a1, b2, a2, b3)
        return tuple(x + z for x, z in zip(acc, new))

    g0, a0, aa0, aaa0, g1, a1, aa1, g2, a2, g3 = lax.fori_loop(0, planes, plane, tuple(acc))
    e = (half_of(lane_iota()) - 0.5) * H
    return [
        g0,
        a0,
        aa0,
        aaa0,
        g1 + e * g0,
        a1 + e * a0,
        aa1 + e * aa0,
        g2 + e * (2.0 * g1 + e * g0),
        a2 + e * (2.0 * a1 + e * a0),
        g3 + e * (3.0 * g2 + e * (3.0 * g1 + e * g0)),
    ]


def wall_sums(f_ref, planes, links_ref, geo_ref, sums_ref, with_absorbed):
    sums_ref[...] = jnp.zeros_like(sums_ref)

    def cell(g, _):
        for k in range(FACES):

            @pl.when(links_ref[k, g] == WALL_LINK)
            def _():
                v0, v1, v2 = face_coefficients(geo_ref, k, g)
                first = splat(geo_ref, FIRST, g)
                base = []
                for t in range(TILES):
                    xb, xc = tile_nodes(t)
                    base.append(v1 * xb + v2 * xc)
                if with_absorbed:
                    wt = splat(geo_ref, WT, g)
                    shape = wall_tiles(wt)

                def plane(a, acc):
                    out, back = list(acc[0]), list(acc[1])
                    xa = first + a.astype(F32) * H
                    sa = v0 * xa
                    if with_absorbed:
                        wa = jnp.exp(-0.5 * xa * xa / wt)
                    for t in range(TILES):
                        s = sa + base[t]
                        f = f_ref[g, at_rows((a * TILES + t) * SUB), :]
                        out[t] = out[t] + jnp.maximum(s, 0.0) * f
                        if with_absorbed:
                            back[t] = back[t] + jnp.maximum(-s, 0.0) * (wa * shape[t])
                    return tuple(out), tuple(back)

                zeros = (jnp.zeros((SUB, LANES), F32),) * TILES
                out, back = lax.fori_loop(0, planes, plane, (zeros, zeros), unroll=4)
                out = (out[0] + out[1]) + (out[2] + out[3])
                back = (back[0] + back[1]) + (back[2] + back[3])
                at = at_rows(g * SUB)
                sums_ref[k, at, :] = out
                if with_absorbed:
                    sums_ref[FACES + k, at, :] = back

        return 0

    lax.fori_loop(0, SUB, cell, 0)


def sums_kernel(links_ref, geo_in, f_ref, sums_out, geo_ref, parts_ref, face_ref):
    planes = f_ref.shape[1] // CHUNKS
    unpack_geo(geo_in, geo_ref)
    y = polynomial_sums(f_ref, planes, parts_ref)
    packed = pack_sums(finish_polynomials(y, geo_ref[FIRST], planes), 0)
    wall_sums(f_ref, planes, links_ref, geo_ref, face_ref, False)
    sums_out[...] = packed + pack_sums([over_sublanes(face_ref, k) for k in range(FACES)], EMIT)


def first_sums_kernel(links_ref, geo_in, native_ref, f_ref, sums_out, geo_ref, face_ref):
    rows = f_ref.shape[1]
    planes = rows // CHUNKS
    unpack_geo(geo_in, geo_ref)

    def group(j, _):
        for g in range(SUB):
            f_ref[g, at_rows(j * SUB), :] = native_ref[pl.ds(j * SUB * SUB + g, SUB, stride=SUB), :]
        return 0

    lax.fori_loop(0, rows // SUB, group, 0, unroll=2)
    y = native_polynomial_sums(native_ref, planes)
    packed = pack_sums(finish_polynomials(y, geo_ref[FIRST], planes), 0)
    wall_sums(f_ref, planes, links_ref, geo_ref, face_ref, True)
    sums_out[...] = packed + pack_sums([over_sublanes(face_ref, k) for k in range(2 * FACES)], EMIT)


def spec(space):
    return pl.BlockSpec(memory_space=space)


def array(*shape):
    return jax.ShapeDtypeStruct(shape, F32)


def params():
    return pltpu.CompilerParams(vmem_limit_bytes=VMEM_LIMIT)


def local_sums(links, geo, f):
    return pl.pallas_call(
        sums_kernel,
        in_specs=[spec(pltpu.SMEM), spec(pltpu.VMEM), spec(pltpu.VMEM)],
        out_specs=spec(pltpu.VMEM),
        out_shape=array(SUB, LANES),
        scratch_shapes=[
            pltpu.VMEM((GEO, SUB, LANES), F32),
            pltpu.VMEM((10, SUB * SUB, LANES), F32),
            pltpu.VMEM((FACES, SUB * SUB, LANES), F32),
        ],
        compiler_params=params(),
        name="local_sums",
    )(links, geo, f)


def first_sums(links, geo, native):
    rows = native.shape[0] // SUB
    return pl.pallas_call(
        first_sums_kernel,
        in_specs=[spec(pltpu.SMEM), spec(pltpu.VMEM), spec(pltpu.VMEM)],
        out_specs=[spec(pltpu.VMEM)] * 2,
        out_shape=[array(SUB, rows, LANES), array(SUB, LANES)],
        scratch_shapes=[
            pltpu.VMEM((GEO, SUB, LANES), F32),
            pltpu.VMEM((2 * FACES, SUB * SUB, LANES), F32),
        ],
        compiler_params=params(),
        name="first_sums",
    )(links, geo, native)


SPLIT_PARTS = 4


def is_odd():
    return lax.rem(lax.axis_index("space"), 2) == 1


def first_rows_kernel(native_hbm, native_ref, far_ref, near_ref, sems):
    rows = native_ref.shape[0]
    part = rows // SPLIT_PARTS
    copies = [
        pltpu.make_async_copy(
            native_hbm.at[pl.ds(i * part, part)], native_ref.at[pl.ds(i * part, part)], sems.at[i]
        )
        for i in range(SPLIT_PARTS)
    ]
    for c in copies:
        c.start()
    odd = is_odd()
    far = jnp.where(odd, SUB - REACH, 0)
    near = jnp.where(odd, 0, SUB - REACH)
    groups = part // (SUB * SUB)

    for i, c in enumerate(copies):
        c.wait()

        def group(j, _):
            for r in range(REACH):
                at = at_rows(j * SUB)
                far_ref[r, at, :] = native_ref[pl.ds(j * SUB * SUB + far + r, SUB, stride=SUB), :]
                near_ref[r, at, :] = native_ref[pl.ds(j * SUB * SUB + near + r, SUB, stride=SUB), :]
            return 0

        lax.fori_loop(i * groups, (i + 1) * groups, group, 0, unroll=4)


def first_rows(native):
    rows = native.shape[0] // SUB
    return pl.pallas_call(
        first_rows_kernel,
        in_specs=[spec(pltpu.HBM)],
        out_specs=[spec(pltpu.VMEM)] * 3,
        out_shape=[array(*native.shape), array(REACH, rows, LANES), array(REACH, rows, LANES)],
        scratch_shapes=[pltpu.SemaphoreType.DMA((SPLIT_PARTS,))],
        compiler_params=params(),
        name="first_rows",
    )(pltpu.with_memory_space_constraint(native, pltpu.HBM))


def geometry_kernel(links_ref, geo_in, pairs_ref, geo_ref):
    rows = pairs_ref.shape[1]
    planes = rows // CHUNKS
    unpack_geo(geo_in, geo_ref)
    first = splat(geo_ref, FIRST, 0)

    def clear(j, _):
        for p in range(pairs_ref.shape[0]):
            pairs_ref[p, at_rows(j * SUB), :] = jnp.zeros((SUB, LANES), F32)
        return 0

    lax.fori_loop(0, rows // SUB, clear, 0, unroll=2)

    def cell(g, _):
        edge = g - (SUB - REACH)
        for k in range(FACES):
            j = links_ref[k, g]
            is_before = jnp.logical_and(j < 0, j != WALL_LINK)

            @pl.when(jnp.logical_or(is_before, j >= SUB))
            def _():
                before = g * REACH - g * (g - 1) // 2 + (j + REACH) - g
                after = len(BEFORE_PAIRS) + edge * (edge + 1) // 2 + j - SUB
                at_pair = jnp.where(is_before, before, after)
                scale = -TIME_STEP / splat(geo_ref, VOL, g)
                v0, v1, v2 = [scale * x for x in face_coefficients(geo_ref, k, g)]
                base = []
                for t in range(TILES):
                    xb, xc = tile_nodes(t)
                    base.append(v1 * xb + v2 * xc)

                def plane(a, _):
                    sa = v0 * (first + a.astype(F32) * H)
                    for t in range(TILES):
                        at = at_rows((a * TILES + t) * SUB)
                        pairs_ref[at_pair, at, :] = pairs_ref[at_pair, at, :] + jnp.maximum(sa + base[t], 0.0)
                    return 0

                lax.fori_loop(0, planes, plane, 0, unroll=4)

        return 0

    lax.fori_loop(0, SUB, cell, 0)


def geometry(links, geo, rows):
    return pl.pallas_call(
        geometry_kernel,
        in_specs=[spec(pltpu.SMEM), spec(pltpu.VMEM)],
        out_specs=spec(pltpu.VMEM),
        out_shape=array(2 * len(BEFORE_PAIRS), rows, LANES),
        scratch_shapes=[pltpu.VMEM((GEO, SUB, LANES), F32)],
        compiler_params=params(),
        name="geometry",
    )(links, geo)


def gather_sums(tile):
    return lax.all_gather(tile, "vel")


def add_tiles(ref):
    out = ref[0]
    for i in range(1, ref.shape[0]):
        out = out + ref[i]
    return out


def quantities(tile):
    m = [WEIGHT * column(tile, p) for p in range(13)]
    n = m[0]
    rn = 1.0 / n
    u = [m[1 + i] * rn for i in range(3)]
    uu = u[0] * u[0] + u[1] * u[1] + u[2] * u[2]
    trace = m[4] + m[5] + m[6]
    width = trace - n * uu
    temperature = width * rn * (1.0 / 3.0)
    second = [[m[4], m[7], m[8]], [m[7], m[5], m[9]], [m[8], m[9], m[6]]]
    q = []
    for i in range(3):
        across = u[0] * second[i][0] + u[1] * second[i][1] + u[2] * second[i][2]
        q.append(0.5 * (m[10 + i] - 2.0 * across - u[i] * trace + 2.0 * uu * m[1 + i]))
    return n, u, temperature, q


def macro_kernel(sums_ref, out_ref):
    n, u, temperature, q = quantities(add_tiles(sums_ref))
    lane, sub = lane_iota(), sub_iota()
    for i, x in enumerate((n, *u, temperature, *q)):
        row = jnp.sum(jnp.where(lane == sub, x, 0.0), axis=0, keepdims=True)
        out_ref[pl.ds(i, 1), :] = row[:, :SUB]


def macro(tiles):
    return pl.pallas_call(
        macro_kernel,
        in_specs=[spec(pltpu.VMEM)],
        out_specs=spec(pltpu.VMEM),
        out_shape=array(8, SUB),
        name="macro",
    )(tiles)


def placer(native):
    def place(g, tile):
        if native:
            return (pl.ds(tile * SUB * SUB + g, SUB, stride=SUB), slice(None))
        return (g, at_rows(tile * SUB), slice(None))

    return place


def flux_kernel(native, links_ref, geo_in, f_ref, out_ref, geo_ref, coef):
    planes = f_ref.shape[1] // CHUNKS
    place = placer(native)
    unpack_geo(geo_in, geo_ref)
    scale = -TIME_STEP / geo_ref[VOL]
    for i in range(3):
        whole = None
        for k in range(FACES):
            x = scale * geo_ref[FV + FACES * i + k]
            coef[FACES * i + k] = x * geo_ref[LOCAL + k]
            whole = x if whole is None else whole + x
        coef[3 * FACES + i] = whole

    def cell(g, _):
        source = []
        for k in range(FACES):
            j = links_ref[k, g]
            source.append(jnp.where(jnp.logical_and(j >= 0, j < SUB), j, g))
        weight = [[splat(coef, FACES * i + k, g) for i in range(3)] for k in range(FACES)]
        whole = [splat(coef, 3 * FACES + i, g) for i in range(3)]
        x0 = splat(geo_ref, FIRST, g)
        for pair in range(TILES // 2):
            base, stay = [], []
            for t in (2 * pair, 2 * pair + 1):
                xb, xc = tile_nodes(t)
                base.append([weight[k][1] * xb + weight[k][2] * xc for k in range(FACES)])
                stay.append(1.0 + whole[1] * xb + whole[2] * xc)

            def plane(a, _):
                xa = x0 + a.astype(F32) * H
                sa = [weight[k][0] * xa for k in range(FACES)]
                stay_a = whole[0] * xa
                for i in range(2):
                    tile = a * TILES + 2 * pair + i
                    at = at_rows(tile * SUB)
                    f = f_ref[g, at, :]
                    terms = [
                        jnp.maximum(sa[k] + base[i][k], 0.0) * (f_ref[source[k], at, :] - f)
                        for k in range(FACES)
                    ]
                    inflow = (terms[0] + terms[1]) + (terms[2] + terms[3]) + (terms[4] + terms[5])
                    out_ref[place(g, tile)] = f * (stay_a + stay[i]) + inflow
                return 0

            lax.fori_loop(0, planes, plane, 0, unroll=4)
        return 0

    lax.fori_loop(0, SUB, cell, 0)


def flux(native, links, geo, f):
    rows = f.shape[1]
    return pl.pallas_call(
        functools.partial(flux_kernel, native),
        in_specs=[spec(pltpu.SMEM), spec(pltpu.VMEM), spec(pltpu.VMEM)],
        out_specs=spec(pltpu.VMEM),
        out_shape=array(SUB * rows, LANES) if native else array(SUB, rows, LANES),
        scratch_shapes=[
            pltpu.VMEM((GEO, SUB, LANES), F32),
            pltpu.VMEM((3 * FACES + 3, SUB, LANES), F32),
        ],
        compiler_params=params(),
        name="flux",
    )(links, geo, f)


def target_kernel(native, links_ref, geo_in, absorbed_in, *refs):
    tiles_ref, f_ref, part_ref, out_ref, sum_out, geo_ref, ta, coef = refs
    planes = f_ref.shape[1] // CHUNKS
    place = placer(native)
    unpack_geo(geo_in, geo_ref)
    sums = add_tiles(tiles_ref)
    sum_out[...] = sums
    absorbed = sums if absorbed_in is None else absorbed_in[...]
    n, u, temperature, q = quantities(sums)
    rt = 1.0 / temperature
    rate = TIME_STEP * n * temperature / (SHEAR * jnp.exp(POWER * jnp.log(temperature)))
    height = rate * n * rt * jnp.sqrt(rt)
    slope = (1.0 / 3.0) / (5.0 * n * temperature * temperature)
    coef[0] = rate
    coef[1] = rt
    coef[2], coef[3] = u[1], u[2]
    coef[4], coef[5] = slope * q[1], slope * q[2]
    for k in range(FACES):
        wall = geo_ref[WALL + k] > 0.5
        coef[6 + k] = column(sums, EMIT + k) / jnp.where(wall, column(absorbed, ABSORB + k), 1.0)
    first = geo_ref[FIRST]

    def plane_table(a, _):
        ca = first + a.astype(F32) * H - u[0]
        za = ca * ca * rt
        ta[0, a] = height * jnp.exp(-0.5 * za)
        ta[1, a] = slope * q[0] * ca
        ta[2, a] = za - 5.0
        return 0

    lax.fori_loop(0, planes, plane_table, 0, unroll=4)

    def cell(g, _):
        rate_g, rtg = splat(coef, 0, g), splat(coef, 1, g)
        ub, uc = splat(coef, 2, g), splat(coef, 3, g)
        qb, qc = splat(coef, 4, g), splat(coef, 5, g)
        x0 = splat(geo_ref, FIRST, g)
        bell, heat, zz = [], [], []
        for t in range(TILES):
            xb, xc = tile_nodes(t)
            cb, cc = xb - ub, xc - uc
            z = (cb * cb + cc * cc) * rtg
            bell.append(jnp.exp(-0.5 * z))
            heat.append(cb * qb + cc * qc)
            zz.append(z)

        def plane(a, _):
            height_a, heat_a, z_a = [
                jnp.broadcast_to(ta[i, a, pl.ds(g, 1), :], (SUB, LANES)) for i in range(3)
            ]
            for t in range(TILES):
                tile = a * TILES + t
                where = place(g, tile)
                f = f_ref[g, at_rows(tile * SUB), :]
                target = (height_a * bell[t]) * (1.0 + (heat_a + heat[t]) * (z_a + zz[t]))
                out_ref[where] = (part_ref[where] - rate_g * f) + target
            return 0

        lax.fori_loop(0, planes, plane, 0, unroll=4)

        for k in range(FACES):

            @pl.when(links_ref[k, g] == WALL_LINK)
            def _():
                wt = splat(geo_ref, WT, g)
                ratio = splat(coef, 6 + k, g)
                shape = [ratio * x for x in wall_tiles(wt)]
                scale = -TIME_STEP / splat(geo_ref, VOL, g)
                v0, v1, v2 = [scale * x for x in face_coefficients(geo_ref, k, g)]
                base = []
                for t in range(TILES):
                    xb, xc = tile_nodes(t)
                    base.append(v1 * xb + v2 * xc)

                def plane(a, _):
                    xa = x0 + a.astype(F32) * H
                    wa = jnp.exp(-0.5 * xa * xa / wt)
                    sa = v0 * xa
                    for t in range(TILES):
                        tile = a * TILES + t
                        where = place(g, tile)
                        f = f_ref[g, at_rows(tile * SUB), :]
                        out_ref[where] = out_ref[where] + jnp.maximum(sa + base[t], 0.0) * (wa * shape[t] - f)
                    return 0

                lax.fori_loop(0, planes, plane, 0, unroll=4)

        return 0

    lax.fori_loop(0, SUB, cell, 0)


def add_target(native, links, geo, absorbed, tiles, f, part):
    rows = f.shape[1]
    vmem = spec(pltpu.VMEM)
    given = [links, geo] + ([] if absorbed is None else [absorbed]) + [tiles, f, part]

    def kernel(links_ref, geo_in, *refs):
        if absorbed is None:
            target_kernel(native, links_ref, geo_in, None, *refs)
        else:
            target_kernel(native, links_ref, geo_in, *refs)

    return pl.pallas_call(
        kernel,
        in_specs=[spec(pltpu.SMEM)] + [vmem] * (len(given) - 1),
        out_specs=[vmem] * 2,
        out_shape=[array(*part.shape), array(SUB, LANES)],
        input_output_aliases={len(given) - 1: 0},
        scratch_shapes=[
            pltpu.VMEM((GEO, SUB, LANES), F32),
            pltpu.VMEM((3, rows // CHUNKS, SUB, LANES), F32),
            pltpu.VMEM((6 + FACES, SUB, LANES), F32),
        ],
        compiler_params=params(),
        name="add_target",
    )(*given)


def halo_terms(pairs_ref, before_ref, after_ref, f_ref, at):
    low, high = [None] * REACH, [None] * REACH
    rows = [before_ref[r, at, :] for r in range(REACH)]
    own = [f_ref[g, at, :] for g in range(REACH)]
    for p, (g, r) in enumerate(BEFORE_PAIRS):
        term = pairs_ref[p, at, :] * (rows[r] - own[g])
        low[g] = term if low[g] is None else low[g] + term
    rows = [after_ref[r, at, :] for r in range(REACH)]
    own = [f_ref[SUB - REACH + e, at, :] for e in range(REACH)]
    p = len(BEFORE_PAIRS)
    for e in range(REACH):
        for r in range(e + 1):
            term = pairs_ref[p, at, :] * (rows[r] - own[e])
            high[e] = term if high[e] is None else high[e] + term
            p += 1
    return low, high


def by_side(far_ref, near_ref, run):
    odd = is_odd()

    @pl.when(odd)
    def _():
        run(near_ref, far_ref)

    @pl.when(jnp.logical_not(odd))
    def _():
        run(far_ref, near_ref)


def edge_kernel(pairs_ref, far_in, near_in, old_ref, part_ref, f_ref, far_out, near_out):
    def run(before_ref, after_ref):
        down_out, up_out = (near_out, far_out) if after_ref is far_in else (far_out, near_out)

        def group(j, _):
            at = at_rows(j * SUB)
            low, high = halo_terms(pairs_ref, before_ref, after_ref, old_ref, at)
            for g in range(REACH):
                x = part_ref[g, at, :] + low[g]
                down_out[g, at, :] = x
                f_ref[g, at, :] = x
                e = SUB - REACH + g
                x = part_ref[e, at, :] + high[g]
                up_out[g, at, :] = x
                f_ref[e, at, :] = x
            return 0

        lax.fori_loop(0, part_ref.shape[1] // SUB, group, 0, unroll=2)

    by_side(far_in, near_in, run)


def edge(pairs, far, near, old, part):
    rows = part.shape[1]
    return pl.pallas_call(
        edge_kernel,
        in_specs=[spec(pltpu.VMEM)] * 5,
        out_specs=[spec(pltpu.VMEM)] * 3,
        out_shape=[array(SUB, rows, LANES), array(REACH, rows, LANES), array(REACH, rows, LANES)],
        input_output_aliases={4: 0},
        compiler_params=params(),
        name="edge",
    )(pairs, far, near, old, part)


def last_edge_kernel(
    geo_in, pairs_ref, far_ref, near_ref, f_ref, part_ref, out_hbm, sums_out, native_ref, sems
):
    rows = part_ref.shape[0] // SUB
    planes = rows // CHUNKS
    part = rows // SUB // LAST_PARTS

    def copy(i):
        at = pl.ds(i * part * SUB * SUB, part * SUB * SUB)
        return pltpu.make_async_copy(native_ref.at[at], out_hbm.at[at], sems.at[i])

    def run(before_ref, after_ref):
        for i in range(LAST_PARTS):

            def group(j, _):
                at = at_rows(j * SUB)
                low, high = halo_terms(pairs_ref, before_ref, after_ref, f_ref, at)
                terms = low + [None] * (SUB - 2 * REACH) + high
                for g in range(SUB):
                    where = (pl.ds(j * SUB * SUB + g, SUB, stride=SUB), slice(None))
                    x = part_ref[where]
                    native_ref[where] = x if terms[g] is None else x + terms[g]
                return 0

            lax.fori_loop(i * part, (i + 1) * part, group, 0, unroll=2)
            copy(i).start()

    by_side(far_ref, near_ref, run)
    y = native_polynomial_sums(native_ref, planes)
    sums_out[...] = pack_sums(finish_polynomials(y, column(geo_in[...], FIRST), planes), 0)
    for i in range(LAST_PARTS):
        copy(i).wait()


LAST_PARTS = 4


def last_edge(geo, pairs, far, near, f, part):
    return pl.pallas_call(
        last_edge_kernel,
        in_specs=[spec(pltpu.VMEM)] * 6,
        out_specs=[spec(pltpu.HBM), spec(pltpu.VMEM)],
        out_shape=[array(*part.shape), array(SUB, LANES)],
        scratch_shapes=[pltpu.VMEM(part.shape, F32), pltpu.SemaphoreType.DMA((LAST_PARTS,))],
        compiler_params=params(),
        name="last_edge",
    )(geo, pairs, far, near, f, part)


def exchange(far, near):
    size = lax.axis_size("space")
    out = []
    for x, start in ((far, 1), (near, 0)):
        pairs = [(i, i + 1) for i in range(start, size - 1, 2)]
        out.append(lax.ppermute(x, "space", pairs + [(j, i) for i, j in pairs]))
    return out


def per_device(particle_profile, neighbors, face_vectors, volumes, wall_temp):
    cells, points = particle_profile.shape
    rows = points // LANES
    plane_count = NV // lax.axis_size("vel")
    native = particle_profile.reshape(cells, rows, LANES).transpose(1, 0, 2).reshape(cells * rows, LANES)
    wall = neighbors < 0
    links = jnp.where(wall, WALL_LINK, neighbors - lax.axis_index("space") * cells)
    own = (links >= 0) & (links < cells)
    first = -SPEED_LIMIT + ((lax.axis_index("vel") * plane_count).astype(F32) + 0.5) * H
    geo = jnp.concatenate(
        [
            face_vectors.reshape(3 * FACES, cells),
            volumes[None],
            wall_temp[None],
            wall.astype(F32),
            own.astype(F32),
            jnp.full((1, cells), first, F32),
        ]
    )
    geo = jnp.pad(geo.T, ((0, 0), (0, LANES - GEO)))
    native, far, near = first_rows(native)
    far, near = exchange(far, near)
    f, sums = first_sums(links, geo, native)
    tiles = gather_sums(sums)
    pairs = geometry(links, geo, rows)
    part = flux(False, links, geo, f)
    part, absorbed = add_target(False, links, geo, None, tiles, f, part)
    f, far, near = edge(pairs, far, near, f, part)
    far, near = exchange(far, near)
    tiles = gather_sums(local_sums(links, geo, f))
    part = flux(True, links, geo, f)
    part, _ = add_target(True, links, geo, absorbed, tiles, f, part)
    native, sums = last_edge(geo, pairs, far, near, f, part)
    macro_quantities = macro(gather_sums(sums))
    evolved = native.reshape(rows, cells, LANES).transpose(1, 0, 2).reshape(cells, points)
    return evolved, macro_quantities


def solution(mesh):
    return jax.shard_map(
        per_device,
        mesh=mesh,
        in_specs=(
            P("space", "vel"),
            P(None, "space"),
            P(None, None, "space"),
            P("space"),
            P("space"),
        ),
        out_specs=(P("space", "vel"), P(None, "space")),
        check_vma=False,
    )
```

```python
import functools
import math

import jax
import jax.numpy as jnp
from jax import lax
from jax.experimental import pallas as pl
from jax.experimental.pallas import tpu as pltpu
from jax.sharding import PartitionSpec as P

NV = 64
FACES = 6
REACH = 3
STEPS = 2
LANES = 128
SUB = 8

TIME_STEP = 0.015
SHEAR = 0.1
POWER = 0.81
SPEED_LIMIT = 6.0
H = 2.0 * SPEED_LIMIT / NV
WEIGHT = H**3 * (2.0 * math.pi) ** (-1.5)

CHUNKS = NV * NV // LANES
TILES = CHUNKS // SUB

FV, VOL, WT, WALL, LOCAL, FIRST = 0, 18, 19, 20, 26, 32
GEO = 33
WALL_LINK = -64
BEFORE_PAIRS = tuple((g, r) for g in range(REACH) for r in range(g, REACH))
EMIT, ABSORB = 13, 19
SUMS = 25

F32 = jnp.float32
VMEM_LIMIT = 16 * 1024 * 1024


def lane_iota():
    return lax.broadcasted_iota(jnp.int32, (SUB, LANES), 1)


def sub_iota():
    return lax.broadcasted_iota(jnp.int32, (SUB, LANES), 0)


def half_of(lane):
    return (lane >= NV).astype(F32)


def third_component(lane):
    c = jnp.where(lane >= NV, lane - NV, lane).astype(F32)
    return -SPEED_LIMIT + (c + 0.5) * H


def tile_nodes(t):
    lane = lane_iota()
    b = (2 * SUB * t + 2 * sub_iota()).astype(F32) + half_of(lane)
    return -SPEED_LIMIT + (b + 0.5) * H, third_component(lane)


def column(tile, p):
    return jnp.broadcast_to(tile[:, p : p + 1], (SUB, LANES))


def splat(ref, i, g):
    return jnp.broadcast_to(ref[i, pl.ds(g, 1), :], (SUB, LANES))


def total(tile):
    return jnp.broadcast_to(jnp.sum(tile, axis=1, keepdims=True), (SUB, LANES))


def face_coefficients(geo_ref, k, g):
    return [splat(geo_ref, FV + FACES * i + k, g) for i in range(3)]


def at_rows(start, size=SUB):
    return pl.ds(pl.multiple_of(start, SUB), size)


def wall_tiles(wall_temp):
    rt = 1.0 / wall_temp
    scale = rt * jnp.sqrt(rt)
    out = []
    for t in range(TILES):
        xb, xc = tile_nodes(t)
        out.append(scale * jnp.exp(-0.5 * (xb * xb + xc * xc) * rt))
    return out


def pack_sums(arrays, start):
    lane = lane_iota()
    out = jnp.zeros((SUB, LANES), F32)
    for p, x in enumerate(arrays):
        out = jnp.where(lane == start + p, total(x), out)
    return out


def over_sublanes(ref, k):
    out = ref[k, pl.ds(0, SUB, stride=SUB), :]
    for s in range(1, SUB):
        out = out + ref[k, pl.ds(s, SUB, stride=SUB), :]
    return out


def finish_polynomials(y, first, planes):
    y0, y1, y2, y3, by0, by1, by2, bby0, bby1, bbby0 = y
    m = first + 0.5 * (planes - 1) * H
    c = third_component(lane_iota())
    cc = c * c
    a = y1 + m * y0
    aa = y2 + m * (2.0 * y1 + m * y0)
    aaa = y3 + m * (3.0 * y2 + m * (3.0 * y1 + m * y0))
    ab = by1 + m * by0
    aab = by2 + m * (2.0 * by1 + m * by0)
    abb = bby1 + m * bby0
    return (
        y0,
        a,
        by0,
        c * y0,
        aa,
        bby0,
        cc * y0,
        ab,
        c * a,
        c * by0,
        aaa + abb + cc * a,
        aab + bbby0 + cc * by0,
        c * (aa + bby0 + cc * y0),
    )


def polynomial_sums(f_ref, planes, parts_ref):
    half = planes // 2

    def cell(g, _):
        out = [None] * 10
        for t in range(TILES):
            y0 = y1 = y2 = y3 = None
            for i in range(half):
                d = (i + 0.5) * H
                hi = f_ref[g, pl.ds(((half + i) * TILES + t) * SUB, SUB), :]
                lo = f_ref[g, pl.ds(((half - 1 - i) * TILES + t) * SUB, SUB), :]
                s, r = hi + lo, hi - lo
                if i == 0:
                    y0, y1, y2, y3 = s, d * r, (d * d) * s, (d * d * d) * r
                else:
                    y0, y1, y2, y3 = y0 + s, y1 + d * r, y2 + (d * d) * s, y3 + (d * d * d) * r
            b, _c = tile_nodes(t)
            bb = b * b
            terms = (y0, y1, y2, y3, b * y0, b * y1, b * y2, bb * y0, bb * y1, bb * (b * y0))
            out = [x if o is None else o + x for o, x in zip(out, terms)]
        for p in range(10):
            parts_ref[p, at_rows(g * SUB), :] = out[p]
        return 0

    lax.fori_loop(0, SUB, cell, 0)
    return [over_sublanes(parts_ref, p) for p in range(10)]


def native_polynomial_sums(native_ref, planes):
    half, side = planes // 2, CHUNKS // 2
    zero = jnp.zeros((SUB, LANES), F32)
    acc = [zero] * 10

    def plane(a, acc):
        xa = (a.astype(F32) - 0.5 * (planes - 1)) * H
        b0 = b1 = b2 = b3 = None
        for i in range(side):
            y = (2 * i + 1) * H
            hi = native_ref[at_rows((a * CHUNKS + side + i) * SUB), :]
            lo = native_ref[at_rows((a * CHUNKS + side - 1 - i) * SUB), :]
            s, d = hi + lo, hi - lo
            terms = (s, y * d, (y * y) * s, (y * y * y) * d)
            if i == 0:
                b0, b1, b2, b3 = terms
            else:
                b0, b1, b2, b3 = b0 + terms[0], b1 + terms[1], b2 + terms[2], b3 + terms[3]
        a0, a1, a2 = xa * b0, xa * b1, xa * b2
        aa0 = xa * a0
        new = (b0, a0, aa0, xa * aa0, b1, a1, xa * a1, b2, a2, b3)
        return tuple(x + z for x, z in zip(acc, new))

    g0, a0, aa0, aaa0, g1, a1, aa1, g2, a2, g3 = lax.fori_loop(0, planes, plane, tuple(acc))
    e = (half_of(lane_iota()) - 0.5) * H
    return [
        g0,
        a0,
        aa0,
        aaa0,
        g1 + e * g0,
        a1 + e * a0,
        aa1 + e * aa0,
        g2 + e * (2.0 * g1 + e * g0),
        a2 + e * (2.0 * a1 + e * a0),
        g3 + e * (3.0 * g2 + e * (3.0 * g1 + e * g0)),
    ]


def wall_sums(f_ref, planes, links_ref, geo_ref, sums_ref, with_absorbed):
    sums_ref[...] = jnp.zeros_like(sums_ref)

    def cell(g, _):
        for k in range(FACES):

            @pl.when(links_ref[k, g] == WALL_LINK)
            def _():
                v0, v1, v2 = face_coefficients(geo_ref, k, g)
                first = splat(geo_ref, FIRST, g)
                base = []
                for t in range(TILES):
                    xb, xc = tile_nodes(t)
                    base.append(v1 * xb + v2 * xc)
                if with_absorbed:
                    wt = splat(geo_ref, WT, g)
                    shape = wall_tiles(wt)

                def plane(a, acc):
                    out, back = list(acc[0]), list(acc[1])
                    xa = first + a.astype(F32) * H
                    sa = v0 * xa
                    if with_absorbed:
                        wa = jnp.exp(-0.5 * xa * xa / wt)
                    for t in range(TILES):
                        s = sa + base[t]
                        f = f_ref[g, at_rows((a * TILES + t) * SUB), :]
                        out[t] = out[t] + jnp.maximum(s, 0.0) * f
                        if with_absorbed:
                            back[t] = back[t] + jnp.maximum(-s, 0.0) * (wa * shape[t])
                    return tuple(out), tuple(back)

                zeros = (jnp.zeros((SUB, LANES), F32),) * TILES
                out, back = lax.fori_loop(0, planes, plane, (zeros, zeros), unroll=4)
                out = (out[0] + out[1]) + (out[2] + out[3])
                back = (back[0] + back[1]) + (back[2] + back[3])
                at = at_rows(g * SUB)
                sums_ref[k, at, :] = out
                if with_absorbed:
                    sums_ref[FACES + k, at, :] = back

        return 0

    lax.fori_loop(0, SUB, cell, 0)


def sums_kernel(links_ref, geo_ref, f_ref, sums_out, parts_ref, face_ref):
    planes = f_ref.shape[1] // CHUNKS
    y = polynomial_sums(f_ref, planes, parts_ref)
    packed = pack_sums(finish_polynomials(y, geo_ref[FIRST], planes), 0)
    wall_sums(f_ref, planes, links_ref, geo_ref, face_ref, False)
    sums_out[...] = packed + pack_sums([over_sublanes(face_ref, k) for k in range(FACES)], EMIT)


def first_sums_kernel(links_ref, geo_ref, native_ref, f_ref, sums_out, face_ref):
    rows = f_ref.shape[1]
    planes = rows // CHUNKS

    def group(j, _):
        for g in range(SUB):
            f_ref[g, at_rows(j * SUB), :] = native_ref[pl.ds(j * SUB * SUB + g, SUB, stride=SUB), :]
        return 0

    lax.fori_loop(0, rows // SUB, group, 0, unroll=2)
    y = native_polynomial_sums(native_ref, planes)
    packed = pack_sums(finish_polynomials(y, geo_ref[FIRST], planes), 0)
    wall_sums(f_ref, planes, links_ref, geo_ref, face_ref, True)
    sums_out[...] = packed + pack_sums([over_sublanes(face_ref, k) for k in range(2 * FACES)], EMIT)


def spec(space):
    return pl.BlockSpec(memory_space=space)


def array(*shape):
    return jax.ShapeDtypeStruct(shape, F32)


def params():
    return pltpu.CompilerParams(vmem_limit_bytes=VMEM_LIMIT)


def traffic(rows, profiles):
    size = SUB * rows * LANES
    return pl.CostEstimate(flops=8 * profiles * size, bytes_accessed=4 * profiles * size, transcendentals=0)


def local_sums(links, geo, f):
    return pl.pallas_call(
        sums_kernel,
        in_specs=[spec(pltpu.SMEM), spec(pltpu.VMEM), spec(pltpu.VMEM)],
        out_specs=spec(pltpu.VMEM),
        out_shape=array(SUB, LANES),
        scratch_shapes=[
                pltpu.VMEM((10, SUB * SUB, LANES), F32),
            pltpu.VMEM((FACES, SUB * SUB, LANES), F32),
        ],
        compiler_params=params(),
        cost_estimate=traffic(f.shape[1], 4),
        name="local_sums",
    )(links, geo, f)


def first_sums(links, geo, native):
    rows = native.shape[0] // SUB
    return pl.pallas_call(
        first_sums_kernel,
        in_specs=[spec(pltpu.SMEM), spec(pltpu.VMEM), spec(pltpu.VMEM)],
        out_specs=[spec(pltpu.VMEM)] * 2,
        out_shape=[array(SUB, rows, LANES), array(SUB, LANES)],
        scratch_shapes=[
                pltpu.VMEM((2 * FACES, SUB * SUB, LANES), F32),
        ],
        compiler_params=params(),
        cost_estimate=traffic(rows, 5),
        name="first_sums",
    )(links, geo, native)


SPLIT_PARTS = 4


def is_odd():
    return lax.rem(lax.axis_index("space"), 2) == 1


def first_rows_kernel(native_hbm, native_ref, far_ref, near_ref, sems):
    rows = native_ref.shape[0]
    part = rows // SPLIT_PARTS
    copies = [
        pltpu.make_async_copy(
            native_hbm.at[pl.ds(i * part, part)], native_ref.at[pl.ds(i * part, part)], sems.at[i]
        )
        for i in range(SPLIT_PARTS)
    ]
    for c in copies:
        c.start()
    odd = is_odd()
    far = jnp.where(odd, SUB - REACH, 0)
    near = jnp.where(odd, 0, SUB - REACH)
    groups = part // (SUB * SUB)

    for i, c in enumerate(copies):
        c.wait()

        def group(j, _):
            for r in range(REACH):
                at = at_rows(j * SUB)
                far_ref[r, at, :] = native_ref[pl.ds(j * SUB * SUB + far + r, SUB, stride=SUB), :]
                near_ref[r, at, :] = native_ref[pl.ds(j * SUB * SUB + near + r, SUB, stride=SUB), :]
            return 0

        lax.fori_loop(i * groups, (i + 1) * groups, group, 0, unroll=4)


def first_rows(native):
    rows = native.shape[0] // SUB
    return pl.pallas_call(
        first_rows_kernel,
        in_specs=[spec(pltpu.HBM)],
        out_specs=[spec(pltpu.VMEM)] * 3,
        out_shape=[array(*native.shape), array(REACH, rows, LANES), array(REACH, rows, LANES)],
        scratch_shapes=[pltpu.SemaphoreType.DMA((SPLIT_PARTS,))],
        compiler_params=params(),
        cost_estimate=traffic(rows, 4),
        name="first_rows",
    )(pltpu.with_memory_space_constraint(native, pltpu.HBM))


def geometry_kernel(links_ref, geo_ref, pairs_ref):
    rows = pairs_ref.shape[1]
    planes = rows // CHUNKS
    first = splat(geo_ref, FIRST, 0)

    def clear(j, _):
        for p in range(pairs_ref.shape[0]):
            pairs_ref[p, at_rows(j * SUB), :] = jnp.zeros((SUB, LANES), F32)
        return 0

    lax.fori_loop(0, rows // SUB, clear, 0, unroll=2)

    def cell(g, _):
        edge = g - (SUB - REACH)
        for k in range(FACES):
            j = links_ref[k, g]
            is_before = jnp.logical_and(j < 0, j != WALL_LINK)

            @pl.when(jnp.logical_or(is_before, j >= SUB))
            def _():
                before = g * REACH - g * (g - 1) // 2 + (j + REACH) - g
                after = len(BEFORE_PAIRS) + edge * (edge + 1) // 2 + j - SUB
                at_pair = jnp.where(is_before, before, after)
                scale = -TIME_STEP / splat(geo_ref, VOL, g)
                v0, v1, v2 = [scale * x for x in face_coefficients(geo_ref, k, g)]
                base = []
                for t in range(TILES):
                    xb, xc = tile_nodes(t)
                    base.append(v1 * xb + v2 * xc)

                def plane(a, _):
                    sa = v0 * (first + a.astype(F32) * H)
                    for t in range(TILES):
                        at = at_rows((a * TILES + t) * SUB)
                        pairs_ref[at_pair, at, :] = pairs_ref[at_pair, at, :] + jnp.maximum(sa + base[t], 0.0)
                    return 0

                lax.fori_loop(0, planes, plane, 0, unroll=4)

        return 0

    lax.fori_loop(0, SUB, cell, 0)


def geometry(links, geo, rows):
    return pl.pallas_call(
        geometry_kernel,
        in_specs=[spec(pltpu.SMEM), spec(pltpu.VMEM)],
        out_specs=spec(pltpu.VMEM),
        out_shape=array(2 * len(BEFORE_PAIRS), rows, LANES),
        compiler_params=params(),
        cost_estimate=traffic(rows, 4),
        name="geometry",
    )(links, geo)


def gather_sums(tile):
    size = lax.axis_size("vel")
    if size not in (2, 4):
        return [lax.psum(tile, "vel")]
    others = [lax.ppermute(tile, "vel", [(i, i ^ s) for i in range(size)]) for s in range(1, size)]
    return [tile, *others]


def add_tiles(refs):
    tiles = [r[...] for r in refs]
    while len(tiles) > 1:
        tiles = [tiles[i] + tiles[i + 1] for i in range(0, len(tiles), 2)]
    return tiles[0]


def quantities(tile):
    m = [WEIGHT * column(tile, p) for p in range(13)]
    n = m[0]
    rn = 1.0 / n
    u = [m[1 + i] * rn for i in range(3)]
    uu = u[0] * u[0] + u[1] * u[1] + u[2] * u[2]
    trace = m[4] + m[5] + m[6]
    width = trace - n * uu
    temperature = width * rn * (1.0 / 3.0)
    second = [[m[4], m[7], m[8]], [m[7], m[5], m[9]], [m[8], m[9], m[6]]]
    q = []
    for i in range(3):
        across = u[0] * second[i][0] + u[1] * second[i][1] + u[2] * second[i][2]
        q.append(0.5 * (m[10 + i] - 2.0 * across - u[i] * trace + 2.0 * uu * m[1 + i]))
    return n, u, temperature, q


def macro_kernel(*refs):
    out_ref = refs[-1]
    n, u, temperature, q = quantities(add_tiles(refs[:-1]))
    lane, sub = lane_iota(), sub_iota()
    for i, x in enumerate((n, *u, temperature, *q)):
        row = jnp.sum(jnp.where(lane == sub, x, 0.0), axis=0, keepdims=True)
        out_ref[pl.ds(i, 1), :] = row[:, :SUB]


def macro(tiles):
    return pl.pallas_call(
        macro_kernel,
        in_specs=[spec(pltpu.VMEM)] * len(tiles),
        out_specs=spec(pltpu.VMEM),
        out_shape=array(8, SUB),
        name="macro",
    )(*tiles)


def flux_kernel(links_ref, geo_ref, f_ref, out_ref, coef, source, face):
    planes = f_ref.shape[1] // CHUNKS
    scale = -TIME_STEP / geo_ref[VOL]
    for i in range(3):
        whole = None
        for k in range(FACES):
            x = scale * geo_ref[FV + FACES * i + k]
            coef[FACES * i + k] = x
            whole = x if whole is None else whole + x
        coef[3 * FACES + i] = whole

    def cell(g, _):
        count = 0
        for k in range(FACES):
            j = links_ref[k, g]
            source[count] = j
            face[count] = k
            count = count + jnp.logical_and(j >= 0, j < SUB).astype(jnp.int32)
        for n in range(FACES + 1):

            @pl.when(count == n)
            def _():
                own_faces(g, n)

        return 0

    def own_faces(g, n):
        at_source = [source[i] for i in range(n)]
        weight = [[splat(coef, FACES * i + face[k], g) for i in range(3)] for k in range(n)]
        whole = [splat(coef, 3 * FACES + i, g) for i in range(3)]
        x0 = splat(geo_ref, FIRST, g)
        for pair in range(TILES // 2):
            base, stay = [], []
            for t in (2 * pair, 2 * pair + 1):
                xb, xc = tile_nodes(t)
                base.append([w[1] * xb + w[2] * xc for w in weight])
                stay.append(1.0 + whole[1] * xb + whole[2] * xc)

            def plane(a, _):
                xa = x0 + a.astype(F32) * H
                sa = [w[0] * xa for w in weight]
                stay_a = whole[0] * xa
                for i in range(2):
                    at = at_rows((a * TILES + 2 * pair + i) * SUB)
                    f = f_ref[g, at, :]
                    acc = f * (stay_a + stay[i])
                    for k in range(n):
                        acc = acc + jnp.maximum(sa[k] + base[i][k], 0.0) * (f_ref[at_source[k], at, :] - f)
                    out_ref[g, at, :] = acc
                return 0

            lax.fori_loop(0, planes, plane, 0, unroll=math.gcd(planes, 8))

    lax.fori_loop(0, SUB, cell, 0)


def flux(links, geo, f):
    return pl.pallas_call(
        flux_kernel,
        in_specs=[spec(pltpu.SMEM), spec(pltpu.VMEM), spec(pltpu.VMEM)],
        out_specs=spec(pltpu.VMEM),
        out_shape=array(*f.shape),
        scratch_shapes=[
            pltpu.VMEM((3 * FACES + 3, SUB, LANES), F32),
            pltpu.SMEM((FACES + 1,), jnp.int32),
            pltpu.SMEM((FACES + 1,), jnp.int32),
        ],
        compiler_params=params(),
        cost_estimate=traffic(f.shape[1], 7),
        name="flux",
    )(links, geo, f)


def target_kernel(count, links_ref, geo_ref, absorbed_in, *refs):
    sums_refs, (f_ref, part_ref, out_ref, sum_out, ta, coef) = refs[:count], refs[count:]
    planes = f_ref.shape[1] // CHUNKS
    sums = add_tiles(sums_refs)
    sum_out[...] = sums
    absorbed = sums if absorbed_in is None else absorbed_in[...]
    n, u, temperature, q = quantities(sums)
    rt = 1.0 / temperature
    rate = TIME_STEP * n * temperature / (SHEAR * jnp.exp(POWER * jnp.log(temperature)))
    height = rate * n * rt * jnp.sqrt(rt)
    slope = (1.0 / 3.0) / (5.0 * n * temperature * temperature)
    coef[0] = rate
    coef[1] = rt
    coef[2], coef[3] = u[1], u[2]
    coef[4], coef[5] = slope * q[1], slope * q[2]
    for k in range(FACES):
        wall = geo_ref[WALL + k] > 0.5
        coef[6 + k] = column(sums, EMIT + k) / jnp.where(wall, column(absorbed, ABSORB + k), 1.0)
    first = geo_ref[FIRST]

    def plane_table(a, _):
        ca = first + a.astype(F32) * H - u[0]
        za = ca * ca * rt
        ta[0, a] = height * jnp.exp(-0.5 * za)
        ta[1, a] = slope * q[0] * ca
        ta[2, a] = za - 5.0
        return 0

    lax.fori_loop(0, planes, plane_table, 0, unroll=4)

    def cell(g, _):
        rate_g, rtg = splat(coef, 0, g), splat(coef, 1, g)
        ub, uc = splat(coef, 2, g), splat(coef, 3, g)
        qb, qc = splat(coef, 4, g), splat(coef, 5, g)
        x0 = splat(geo_ref, FIRST, g)
        bell, heat, zz = [], [], []
        for t in range(TILES):
            xb, xc = tile_nodes(t)
            cb, cc = xb - ub, xc - uc
            z = (cb * cb + cc * cc) * rtg
            bell.append(jnp.exp(-0.5 * z))
            heat.append(cb * qb + cc * qc)
            zz.append(z)

        def plane(a, _):
            height_a, heat_a, z_a = [
                jnp.broadcast_to(ta[i, a, pl.ds(g, 1), :], (SUB, LANES)) for i in range(3)
            ]
            for t in range(TILES):
                where = (g, at_rows((a * TILES + t) * SUB), slice(None))
                f = f_ref[where]
                target = (height_a * bell[t]) * (1.0 + (heat_a + heat[t]) * (z_a + zz[t]))
                out_ref[where] = (part_ref[where] - rate_g * f) + target
            return 0

        lax.fori_loop(0, planes, plane, 0, unroll=math.gcd(planes, 8))

        for k in range(FACES):

            @pl.when(links_ref[k, g] == WALL_LINK)
            def _():
                wt = splat(geo_ref, WT, g)
                ratio = splat(coef, 6 + k, g)
                shape = [ratio * x for x in wall_tiles(wt)]
                scale = -TIME_STEP / splat(geo_ref, VOL, g)
                v0, v1, v2 = [scale * x for x in face_coefficients(geo_ref, k, g)]
                base = []
                for t in range(TILES):
                    xb, xc = tile_nodes(t)
                    base.append(v1 * xb + v2 * xc)

                def plane(a, _):
                    xa = x0 + a.astype(F32) * H
                    wa = jnp.exp(-0.5 * xa * xa / wt)
                    sa = v0 * xa
                    for t in range(TILES):
                        where = (g, at_rows((a * TILES + t) * SUB), slice(None))
                        f = f_ref[where]
                        out_ref[where] = out_ref[where] + jnp.maximum(sa + base[t], 0.0) * (wa * shape[t] - f)
                    return 0

                lax.fori_loop(0, planes, plane, 0, unroll=4)

        return 0

    lax.fori_loop(0, SUB, cell, 0)


def add_target(links, geo, absorbed, tiles, f, part):
    rows = f.shape[1]
    vmem = spec(pltpu.VMEM)
    given = [links, geo] + ([] if absorbed is None else [absorbed]) + list(tiles) + [f, part]

    def kernel(links_ref, geo_in, *refs):
        if absorbed is None:
            target_kernel(len(tiles), links_ref, geo_in, None, *refs)
        else:
            target_kernel(len(tiles), links_ref, geo_in, *refs)

    return pl.pallas_call(
        kernel,
        in_specs=[spec(pltpu.SMEM)] + [vmem] * (len(given) - 1),
        out_specs=[vmem] * 2,
        out_shape=[array(*part.shape), array(SUB, LANES)],
        input_output_aliases={len(given) - 1: 0},
        scratch_shapes=[
                pltpu.VMEM((3, rows // CHUNKS, SUB, LANES), F32),
            pltpu.VMEM((6 + FACES, SUB, LANES), F32),
        ],
        compiler_params=params(),
        cost_estimate=traffic(rows, 7),
        name="add_target",
    )(*given)


def halo_terms(pairs_ref, before_ref, after_ref, f_ref, at):
    low, high = [None] * REACH, [None] * REACH
    rows = [before_ref[r, at, :] for r in range(REACH)]
    own = [f_ref[g, at, :] for g in range(REACH)]
    for p, (g, r) in enumerate(BEFORE_PAIRS):
        term = pairs_ref[p, at, :] * (rows[r] - own[g])
        low[g] = term if low[g] is None else low[g] + term
    rows = [after_ref[r, at, :] for r in range(REACH)]
    own = [f_ref[SUB - REACH + e, at, :] for e in range(REACH)]
    p = len(BEFORE_PAIRS)
    for e in range(REACH):
        for r in range(e + 1):
            term = pairs_ref[p, at, :] * (rows[r] - own[e])
            high[e] = term if high[e] is None else high[e] + term
            p += 1
    return low, high


def by_side(far_ref, near_ref, run):
    odd = is_odd()

    @pl.when(odd)
    def _():
        run(near_ref, far_ref)

    @pl.when(jnp.logical_not(odd))
    def _():
        run(far_ref, near_ref)


def edge_kernel(pairs_ref, far_in, near_in, old_ref, part_ref, f_ref, far_out, near_out):
    def run(before_ref, after_ref):
        down_out, up_out = (near_out, far_out) if after_ref is far_in else (far_out, near_out)

        def group(j, _):
            at = at_rows(j * SUB)
            low, high = halo_terms(pairs_ref, before_ref, after_ref, old_ref, at)
            for g in range(REACH):
                x = part_ref[g, at, :] + low[g]
                down_out[g, at, :] = x
                f_ref[g, at, :] = x
                e = SUB - REACH + g
                x = part_ref[e, at, :] + high[g]
                up_out[g, at, :] = x
                f_ref[e, at, :] = x
            return 0

        lax.fori_loop(0, part_ref.shape[1] // SUB, group, 0, unroll=2)

    by_side(far_in, near_in, run)


def edge(pairs, far, near, old, part):
    rows = part.shape[1]
    return pl.pallas_call(
        edge_kernel,
        in_specs=[spec(pltpu.VMEM)] * 5,
        out_specs=[spec(pltpu.VMEM)] * 3,
        out_shape=[array(SUB, rows, LANES), array(REACH, rows, LANES), array(REACH, rows, LANES)],
        input_output_aliases={4: 0},
        compiler_params=params(),
        cost_estimate=traffic(rows, 4),
        name="edge",
    )(pairs, far, near, old, part)


def last_edge_kernel(
    geo_ref, pairs_ref, far_ref, near_ref, f_ref, part_ref, out_hbm, sums_out, native_ref, sems
):
    rows = part_ref.shape[1]
    planes = rows // CHUNKS
    part = rows // SUB // LAST_PARTS

    def copy(i):
        at = pl.ds(i * part * SUB * SUB, part * SUB * SUB)
        return pltpu.make_async_copy(native_ref.at[at], out_hbm.at[at], sems.at[i])

    def run(before_ref, after_ref):
        for i in range(LAST_PARTS):

            def group(j, _):
                at = at_rows(j * SUB)
                low, high = halo_terms(pairs_ref, before_ref, after_ref, f_ref, at)
                terms = low + [None] * (SUB - 2 * REACH) + high
                for g in range(SUB):
                    x = part_ref[g, at, :]
                    where = (pl.ds(j * SUB * SUB + g, SUB, stride=SUB), slice(None))
                    native_ref[where] = x if terms[g] is None else x + terms[g]
                return 0

            lax.fori_loop(i * part, (i + 1) * part, group, 0, unroll=2)
            copy(i).start()

    by_side(far_ref, near_ref, run)
    y = native_polynomial_sums(native_ref, planes)
    sums_out[...] = pack_sums(finish_polynomials(y, geo_ref[FIRST], planes), 0)
    for i in range(LAST_PARTS):
        copy(i).wait()


LAST_PARTS = 4


def last_edge(geo, pairs, far, near, f, part):
    native = (SUB * part.shape[1], LANES)
    return pl.pallas_call(
        last_edge_kernel,
        in_specs=[spec(pltpu.VMEM)] * 6,
        out_specs=[spec(pltpu.HBM), spec(pltpu.VMEM)],
        out_shape=[array(*native), array(SUB, LANES)],
        scratch_shapes=[pltpu.VMEM(native, F32), pltpu.SemaphoreType.DMA((LAST_PARTS,))],
        compiler_params=params(),
        cost_estimate=traffic(part.shape[1], 4),
        name="last_edge",
    )(geo, pairs, far, near, f, part)


def exchange(far, near):
    size = lax.axis_size("space")
    out = []
    for x, start in ((far, 1), (near, 0)):
        pairs = [(i, i + 1) for i in range(start, size - 1, 2)]
        out.append(lax.ppermute(x, "space", pairs + [(j, i) for i, j in pairs]))
    return out


def per_device(particle_profile, neighbors, face_vectors, volumes, wall_temp):
    cells, points = particle_profile.shape
    rows = points // LANES
    plane_count = NV // lax.axis_size("vel")
    native = particle_profile.reshape(cells, rows, LANES).transpose(1, 0, 2).reshape(cells * rows, LANES)
    wall = neighbors < 0
    links = jnp.where(wall, WALL_LINK, neighbors - lax.axis_index("space") * cells)
    own = (links >= 0) & (links < cells)
    first = -SPEED_LIMIT + ((lax.axis_index("vel") * plane_count).astype(F32) + 0.5) * H
    geo = jnp.concatenate(
        [
            face_vectors.reshape(3 * FACES, cells),
            volumes[None],
            wall_temp[None],
            wall.astype(F32),
            own.astype(F32),
            jnp.full((1, cells), first, F32),
        ]
    )
    geo = jnp.broadcast_to(geo[:, :, None], (GEO, cells, LANES))
    native, far, near = first_rows(native)
    far, near = exchange(far, near)
    f, sums = first_sums(links, geo, native)
    tiles = gather_sums(sums)
    pairs = geometry(links, geo, rows)
    part = flux(links, geo, f)
    part, absorbed = add_target(links, geo, None, tiles, f, part)
    f, far, near = edge(pairs, far, near, f, part)
    far, near = exchange(far, near)
    tiles = gather_sums(local_sums(links, geo, f))
    part = flux(links, geo, f)
    part, _ = add_target(links, geo, absorbed, tiles, f, part)
    native, sums = last_edge(geo, pairs, far, near, f, part)
    macro_quantities = macro(gather_sums(sums))
    evolved = native.reshape(rows, cells, LANES).transpose(1, 0, 2).reshape(cells, points)
    return evolved, macro_quantities


def solution(mesh):
    return jax.shard_map(
        per_device,
        mesh=mesh,
        in_specs=(
            P("space", "vel"),
            P(None, "space"),
            P(None, None, "space"),
            P("space"),
            P("space"),
        ),
        out_specs=(P("space", "vel"), P(None, "space")),
        check_vma=False,
    )
```

```python
import functools
import math

import jax
import jax.numpy as jnp
from jax import lax
from jax.experimental import pallas as pl
from jax.experimental.pallas import tpu as pltpu
from jax.sharding import PartitionSpec as P

NV = 64
FACES = 6
REACH = 3
STEPS = 2
LANES = 128
SUB = 8

TIME_STEP = 0.015
SHEAR = 0.1
POWER = 0.81
SPEED_LIMIT = 6.0
H = 2.0 * SPEED_LIMIT / NV
WEIGHT = H**3 * (2.0 * math.pi) ** (-1.5)

CHUNKS = NV * NV // LANES
TILES = CHUNKS // SUB

FV, VOL, WT, WALL, LOCAL, FIRST = 0, 18, 19, 20, 26, 32
GEO = 33
WALL_LINK = -64
BEFORE_PAIRS = tuple((g, r) for g in range(REACH) for r in range(g, REACH))
EMIT, ABSORB = 13, 19
SUMS = 25

F32 = jnp.float32


def lane_iota():
    return lax.broadcasted_iota(jnp.int32, (SUB, LANES), 1)


def sub_iota():
    return lax.broadcasted_iota(jnp.int32, (SUB, LANES), 0)


def half_of(lane):
    return (lane >= NV).astype(F32)


def third_component(lane):
    c = jnp.where(lane >= NV, lane - NV, lane).astype(F32)
    return -SPEED_LIMIT + (c + 0.5) * H


def tile_nodes(t):
    lane = lane_iota()
    b = (2 * SUB * t + 2 * sub_iota()).astype(F32) + half_of(lane)
    return -SPEED_LIMIT + (b + 0.5) * H, third_component(lane)


def column(tile, p):
    return jnp.broadcast_to(tile[:, p : p + 1], (SUB, LANES))


def splat(ref, i, g):
    return jnp.broadcast_to(ref[i, pl.ds(g, 1), :], (SUB, LANES))


def total(tile):
    return jnp.broadcast_to(jnp.sum(tile, axis=1, keepdims=True), (SUB, LANES))


def face_coefficients(geo_ref, k, g):
    return [splat(geo_ref, FV + FACES * i + k, g) for i in range(3)]


def at_rows(start, size=SUB):
    return pl.ds(pl.multiple_of(start, SUB), size)


def wall_tiles(wall_temp):
    rt = 1.0 / wall_temp
    scale = rt * jnp.sqrt(rt)
    out = []
    for t in range(TILES):
        xb, xc = tile_nodes(t)
        out.append(scale * jnp.exp(-0.5 * (xb * xb + xc * xc) * rt))
    return out


def pack_sums(arrays, start):
    lane = lane_iota()
    out = jnp.zeros((SUB, LANES), F32)
    for p, x in enumerate(arrays):
        out = jnp.where(lane == start + p, total(x), out)
    return out


def over_sublanes(ref, k):
    out = ref[k, pl.ds(0, SUB, stride=SUB), :]
    for s in range(1, SUB):
        out = out + ref[k, pl.ds(s, SUB, stride=SUB), :]
    return out


def finish_polynomials(y, first, planes):
    y0, y1, y2, y3, by0, by1, by2, bby0, bby1, bbby0 = y
    m = first + 0.5 * (planes - 1) * H
    c = third_component(lane_iota())
    cc = c * c
    a = y1 + m * y0
    aa = y2 + m * (2.0 * y1 + m * y0)
    aaa = y3 + m * (3.0 * y2 + m * (3.0 * y1 + m * y0))
    ab = by1 + m * by0
    aab = by2 + m * (2.0 * by1 + m * by0)
    abb = bby1 + m * bby0
    return (
        y0,
        a,
        by0,
        c * y0,
        aa,
        bby0,
        cc * y0,
        ab,
        c * a,
        c * by0,
        aaa + abb + cc * a,
        aab + bbby0 + cc * by0,
        c * (aa + bby0 + cc * y0),
    )


def polynomial_sums(f_ref, planes, parts_ref):
    half = planes // 2

    def cell(g, _):
        out = [None] * 10
        for t in range(TILES):
            y0 = y1 = y2 = y3 = None
            for i in range(half):
                d = (i + 0.5) * H
                hi = f_ref[g, pl.ds(((half + i) * TILES + t) * SUB, SUB), :]
                lo = f_ref[g, pl.ds(((half - 1 - i) * TILES + t) * SUB, SUB), :]
                s, r = hi + lo, hi - lo
                if i == 0:
                    y0, y1, y2, y3 = s, d * r, (d * d) * s, (d * d * d) * r
                else:
                    y0, y1, y2, y3 = y0 + s, y1 + d * r, y2 + (d * d) * s, y3 + (d * d * d) * r
            b, _c = tile_nodes(t)
            bb = b * b
            terms = (y0, y1, y2, y3, b * y0, b * y1, b * y2, bb * y0, bb * y1, bb * (b * y0))
            out = [x if o is None else o + x for o, x in zip(out, terms)]
        for p in range(10):
            parts_ref[p, at_rows(g * SUB), :] = out[p]
        return 0

    lax.fori_loop(0, SUB, cell, 0)
    return [over_sublanes(parts_ref, p) for p in range(10)]


def native_polynomial_sums(native_ref, planes):
    half, side = planes // 2, CHUNKS // 2
    zero = jnp.zeros((SUB, LANES), F32)
    acc = [zero] * 10

    def plane(a, acc):
        xa = (a.astype(F32) - 0.5 * (planes - 1)) * H
        b0 = b1 = b2 = b3 = None
        for i in range(side):
            y = (2 * i + 1) * H
            hi = native_ref[at_rows((a * CHUNKS + side + i) * SUB), :]
            lo = native_ref[at_rows((a * CHUNKS + side - 1 - i) * SUB), :]
            s, d = hi + lo, hi - lo
            terms = (s, y * d, (y * y) * s, (y * y * y) * d)
            if i == 0:
                b0, b1, b2, b3 = terms
            else:
                b0, b1, b2, b3 = b0 + terms[0], b1 + terms[1], b2 + terms[2], b3 + terms[3]
        a0, a1, a2 = xa * b0, xa * b1, xa * b2
        aa0 = xa * a0
        new = (b0, a0, aa0, xa * aa0, b1, a1, xa * a1, b2, a2, b3)
        return tuple(x + z for x, z in zip(acc, new))

    g0, a0, aa0, aaa0, g1, a1, aa1, g2, a2, g3 = lax.fori_loop(0, planes, plane, tuple(acc))
    e = (half_of(lane_iota()) - 0.5) * H
    return [
        g0,
        a0,
        aa0,
        aaa0,
        g1 + e * g0,
        a1 + e * a0,
        aa1 + e * aa0,
        g2 + e * (2.0 * g1 + e * g0),
        a2 + e * (2.0 * a1 + e * a0),
        g3 + e * (3.0 * g2 + e * (3.0 * g1 + e * g0)),
    ]


def wall_sums(f_ref, planes, links_ref, geo_ref, sums_ref, with_absorbed):
    sums_ref[...] = jnp.zeros_like(sums_ref)

    def cell(g, _):
        for k in range(FACES):

            @pl.when(links_ref[k, g] == WALL_LINK)
            def _():
                v0, v1, v2 = face_coefficients(geo_ref, k, g)
                first = splat(geo_ref, FIRST, g)
                base = []
                for t in range(TILES):
                    xb, xc = tile_nodes(t)
                    base.append(v1 * xb + v2 * xc)
                if with_absorbed:
                    wt = splat(geo_ref, WT, g)
                    shape = wall_tiles(wt)

                def plane(a, acc):
                    out, back = list(acc[0]), list(acc[1])
                    xa = first + a.astype(F32) * H
                    sa = v0 * xa
                    if with_absorbed:
                        wa = jnp.exp(-0.5 * xa * xa / wt)
                    for t in range(TILES):
                        s = sa + base[t]
                        f = f_ref[g, at_rows((a * TILES + t) * SUB), :]
                        out[t] = out[t] + jnp.maximum(s, 0.0) * f
                        if with_absorbed:
                            back[t] = back[t] + jnp.maximum(-s, 0.0) * (wa * shape[t])
                    return tuple(out), tuple(back)

                zeros = (jnp.zeros((SUB, LANES), F32),) * TILES
                out, back = lax.fori_loop(0, planes, plane, (zeros, zeros), unroll=4)
                out = (out[0] + out[1]) + (out[2] + out[3])
                back = (back[0] + back[1]) + (back[2] + back[3])
                at = at_rows(g * SUB)
                sums_ref[k, at, :] = out
                if with_absorbed:
                    sums_ref[FACES + k, at, :] = back

        return 0

    lax.fori_loop(0, SUB, cell, 0)


def sums_kernel(links_ref, geo_ref, f_ref, sums_out, parts_ref, face_ref):
    planes = f_ref.shape[1] // CHUNKS
    y = polynomial_sums(f_ref, planes, parts_ref)
    packed = pack_sums(finish_polynomials(y, geo_ref[FIRST], planes), 0)
    wall_sums(f_ref, planes, links_ref, geo_ref, face_ref, False)
    sums_out[...] = packed + pack_sums([over_sublanes(face_ref, k) for k in range(FACES)], EMIT)


def first_sums_kernel(links_ref, geo_ref, native_ref, f_ref, sums_out, face_ref):
    rows = f_ref.shape[1]
    planes = rows // CHUNKS

    def group(j, _):
        for g in range(SUB):
            f_ref[g, at_rows(j * SUB), :] = native_ref[pl.ds(j * SUB * SUB + g, SUB, stride=SUB), :]
        return 0

    lax.fori_loop(0, rows // SUB, group, 0, unroll=2)
    y = native_polynomial_sums(native_ref, planes)
    packed = pack_sums(finish_polynomials(y, geo_ref[FIRST], planes), 0)
    wall_sums(f_ref, planes, links_ref, geo_ref, face_ref, True)
    sums_out[...] = packed + pack_sums([over_sublanes(face_ref, k) for k in range(2 * FACES)], EMIT)


def spec(space):
    return pl.BlockSpec(memory_space=space)


def array(*shape):
    return jax.ShapeDtypeStruct(shape, F32)


def params(mib=16):
    return pltpu.CompilerParams(vmem_limit_bytes=mib * 1024 * 1024)


def traffic(rows, profiles):
    size = SUB * rows * LANES
    return pl.CostEstimate(flops=8 * profiles * size, bytes_accessed=4 * profiles * size, transcendentals=0)


def local_sums(links, geo, f):
    return pl.pallas_call(
        sums_kernel,
        in_specs=[spec(pltpu.SMEM), spec(pltpu.VMEM), spec(pltpu.VMEM)],
        out_specs=spec(pltpu.VMEM),
        out_shape=array(SUB, LANES),
        scratch_shapes=[
                pltpu.VMEM((10, SUB * SUB, LANES), F32),
            pltpu.VMEM((FACES, SUB * SUB, LANES), F32),
        ],
        compiler_params=params(),
        cost_estimate=traffic(f.shape[1], 4),
        name="local_sums",
    )(links, geo, f)


def first_sums(links, geo, native):
    rows = native.shape[0] // SUB
    return pl.pallas_call(
        first_sums_kernel,
        in_specs=[spec(pltpu.SMEM), spec(pltpu.VMEM), spec(pltpu.VMEM)],
        out_specs=[spec(pltpu.VMEM)] * 2,
        out_shape=[array(SUB, rows, LANES), array(SUB, LANES)],
        scratch_shapes=[
                pltpu.VMEM((2 * FACES, SUB * SUB, LANES), F32),
        ],
        compiler_params=params(),
        cost_estimate=traffic(rows, 5),
        name="first_sums",
    )(links, geo, native)


SPLIT_PARTS = 4


def is_odd():
    return lax.rem(lax.axis_index("space"), 2) == 1


def first_rows_kernel(native_hbm, native_ref, far_ref, near_ref, sems):
    rows = native_ref.shape[0]
    part = rows // SPLIT_PARTS
    copies = [
        pltpu.make_async_copy(
            native_hbm.at[pl.ds(i * part, part)], native_ref.at[pl.ds(i * part, part)], sems.at[i]
        )
        for i in range(SPLIT_PARTS)
    ]
    for c in copies:
        c.start()
    odd = is_odd()
    far = jnp.where(odd, SUB - REACH, 0)
    near = jnp.where(odd, 0, SUB - REACH)
    groups = part // (SUB * SUB)

    for i, c in enumerate(copies):
        c.wait()

        def group(j, _):
            for r in range(REACH):
                at = at_rows(j * SUB)
                far_ref[r, at, :] = native_ref[pl.ds(j * SUB * SUB + far + r, SUB, stride=SUB), :]
                near_ref[r, at, :] = native_ref[pl.ds(j * SUB * SUB + near + r, SUB, stride=SUB), :]
            return 0

        lax.fori_loop(i * groups, (i + 1) * groups, group, 0, unroll=4)


def first_rows(native):
    rows = native.shape[0] // SUB
    return pl.pallas_call(
        first_rows_kernel,
        in_specs=[spec(pltpu.HBM)],
        out_specs=[spec(pltpu.VMEM)] * 3,
        out_shape=[pltpu.VMEM(native.shape, F32)] + [pltpu.VMEM((REACH, rows, LANES), F32)] * 2,
        scratch_shapes=[pltpu.SemaphoreType.DMA((SPLIT_PARTS,))],
        compiler_params=params(),
        cost_estimate=traffic(rows, 4),
        name="first_rows",
    )(pltpu.with_memory_space_constraint(native, pltpu.HBM))


def geometry_kernel(links_ref, geo_ref, pairs_ref):
    rows = pairs_ref.shape[1]
    planes = rows // CHUNKS
    first = splat(geo_ref, FIRST, 0)

    def clear(j, _):
        for p in range(pairs_ref.shape[0]):
            pairs_ref[p, at_rows(j * SUB), :] = jnp.zeros((SUB, LANES), F32)
        return 0

    lax.fori_loop(0, rows // SUB, clear, 0, unroll=2)

    def cell(g, _):
        edge = g - (SUB - REACH)
        for k in range(FACES):
            j = links_ref[k, g]
            is_before = jnp.logical_and(j < 0, j != WALL_LINK)

            @pl.when(jnp.logical_or(is_before, j >= SUB))
            def _():
                before = g * REACH - g * (g - 1) // 2 + (j + REACH) - g
                after = len(BEFORE_PAIRS) + edge * (edge + 1) // 2 + j - SUB
                at_pair = jnp.where(is_before, before, after)
                scale = -TIME_STEP / splat(geo_ref, VOL, g)
                v0, v1, v2 = [scale * x for x in face_coefficients(geo_ref, k, g)]
                base = []
                for t in range(TILES):
                    xb, xc = tile_nodes(t)
                    base.append(v1 * xb + v2 * xc)

                def plane(a, _):
                    sa = v0 * (first + a.astype(F32) * H)
                    for t in range(TILES):
                        at = at_rows((a * TILES + t) * SUB)
                        pairs_ref[at_pair, at, :] = pairs_ref[at_pair, at, :] + jnp.maximum(sa + base[t], 0.0)
                    return 0

                lax.fori_loop(0, planes, plane, 0, unroll=4)

        return 0

    lax.fori_loop(0, SUB, cell, 0)


def geometry(links, geo, rows):
    return pl.pallas_call(
        geometry_kernel,
        in_specs=[spec(pltpu.SMEM), spec(pltpu.VMEM)],
        out_specs=spec(pltpu.VMEM),
        out_shape=array(2 * len(BEFORE_PAIRS), rows, LANES),
        compiler_params=params(),
        cost_estimate=traffic(rows, 4),
        name="geometry",
    )(links, geo)


def gather_sums(tile):
    size = lax.axis_size("vel")
    if size not in (2, 4):
        return [lax.psum(tile, "vel")]
    others = [lax.ppermute(tile, "vel", [(i, i ^ s) for i in range(size)]) for s in range(1, size)]
    return [tile, *others]


def doubling_sums(tile):
    size = lax.axis_size("vel")
    if size != 4:
        return gather_sums(tile)
    pair = tile + lax.ppermute(tile, "vel", [(i, i ^ 1) for i in range(size)])
    return [pair, lax.ppermute(pair, "vel", [(i, i ^ 2) for i in range(size)])]


def add_tiles(refs):
    tiles = [r[...] for r in refs]
    while len(tiles) > 1:
        tiles = [tiles[i] + tiles[i + 1] for i in range(0, len(tiles), 2)]
    return tiles[0]


def quantities(tile):
    m = [WEIGHT * column(tile, p) for p in range(13)]
    n = m[0]
    rn = 1.0 / n
    u = [m[1 + i] * rn for i in range(3)]
    uu = u[0] * u[0] + u[1] * u[1] + u[2] * u[2]
    trace = m[4] + m[5] + m[6]
    width = trace - n * uu
    temperature = width * rn * (1.0 / 3.0)
    second = [[m[4], m[7], m[8]], [m[7], m[5], m[9]], [m[8], m[9], m[6]]]
    q = []
    for i in range(3):
        across = u[0] * second[i][0] + u[1] * second[i][1] + u[2] * second[i][2]
        q.append(0.5 * (m[10 + i] - 2.0 * across - u[i] * trace + 2.0 * uu * m[1 + i]))
    return n, u, temperature, q


def macro_kernel(*refs):
    out_ref = refs[-1]
    n, u, temperature, q = quantities(add_tiles(refs[:-1]))
    lane, sub = lane_iota(), sub_iota()
    for i, x in enumerate((n, *u, temperature, *q)):
        row = jnp.sum(jnp.where(lane == sub, x, 0.0), axis=0, keepdims=True)
        out_ref[pl.ds(i, 1), :] = row[:, :SUB]


def macro(tiles):
    return pl.pallas_call(
        macro_kernel,
        in_specs=[spec(pltpu.VMEM)] * len(tiles),
        out_specs=spec(pltpu.VMEM),
        out_shape=array(8, SUB),
        compiler_params=params(1),
        name="macro",
    )(*tiles)


def flux_kernel(links_ref, geo_ref, f_ref, out_ref, coef, source, face):
    planes = f_ref.shape[1] // CHUNKS
    scale = -TIME_STEP / geo_ref[VOL]
    for i in range(3):
        whole = None
        for k in range(FACES):
            x = scale * geo_ref[FV + FACES * i + k]
            coef[FACES * i + k] = x
            whole = x if whole is None else whole + x
        coef[3 * FACES + i] = whole

    def cell(g, _):
        count = 0
        for k in range(FACES):
            j = links_ref[k, g]
            source[count] = j
            face[count] = k
            count = count + jnp.logical_and(j >= 0, j < SUB).astype(jnp.int32)
        for n in range(FACES + 1):

            @pl.when(count == n)
            def _():
                own_faces(g, n)

        return 0

    def own_faces(g, n):
        at_source = [source[i] for i in range(n)]
        weight = [[splat(coef, FACES * i + face[k], g) for i in range(3)] for k in range(n)]
        whole = [splat(coef, 3 * FACES + i, g) for i in range(3)]
        x0 = splat(geo_ref, FIRST, g)
        for pair in range(TILES // 2):
            base, stay = [], []
            for t in (2 * pair, 2 * pair + 1):
                xb, xc = tile_nodes(t)
                base.append([w[1] * xb + w[2] * xc for w in weight])
                stay.append(1.0 + whole[1] * xb + whole[2] * xc)

            def plane(a, _):
                xa = x0 + a.astype(F32) * H
                sa = [w[0] * xa for w in weight]
                stay_a = whole[0] * xa
                for i in range(2):
                    at = at_rows((a * TILES + 2 * pair + i) * SUB)
                    f = f_ref[g, at, :]
                    acc = f * (stay_a + stay[i])
                    for k in range(n):
                        acc = acc + jnp.maximum(sa[k] + base[i][k], 0.0) * (f_ref[at_source[k], at, :] - f)
                    out_ref[g, at, :] = acc
                return 0

            lax.fori_loop(0, planes, plane, 0, unroll=math.gcd(planes, 8))

    lax.fori_loop(0, SUB, cell, 0)


def flux(links, geo, f):
    return pl.pallas_call(
        flux_kernel,
        in_specs=[spec(pltpu.SMEM), spec(pltpu.VMEM), spec(pltpu.VMEM)],
        out_specs=spec(pltpu.VMEM),
        out_shape=array(*f.shape),
        scratch_shapes=[
            pltpu.VMEM((3 * FACES + 3, SUB, LANES), F32),
            pltpu.SMEM((FACES + 1,), jnp.int32),
            pltpu.SMEM((FACES + 1,), jnp.int32),
        ],
        compiler_params=params(),
        cost_estimate=traffic(f.shape[1], 7),
        name="flux",
    )(links, geo, f)


def target_kernel(count, links_ref, geo_ref, absorbed_in, *refs):
    sums_refs, (f_ref, part_ref, out_ref, sum_out, ta, coef) = refs[:count], refs[count:]
    planes = f_ref.shape[1] // CHUNKS
    sums = add_tiles(sums_refs)
    sum_out[...] = sums
    absorbed = sums if absorbed_in is None else absorbed_in[...]
    n, u, temperature, q = quantities(sums)
    rt = 1.0 / temperature
    rate = TIME_STEP * n * temperature / (SHEAR * jnp.exp(POWER * jnp.log(temperature)))
    height = rate * n * rt * jnp.sqrt(rt)
    slope = (1.0 / 3.0) / (5.0 * n * temperature * temperature)
    coef[0] = rate
    coef[1] = rt
    coef[2], coef[3] = u[1], u[2]
    coef[4], coef[5] = slope * q[1], slope * q[2]
    for k in range(FACES):
        wall = geo_ref[WALL + k] > 0.5
        coef[6 + k] = column(sums, EMIT + k) / jnp.where(wall, column(absorbed, ABSORB + k), 1.0)
    first = geo_ref[FIRST]

    def plane_table(a, _):
        ca = first + a.astype(F32) * H - u[0]
        za = ca * ca * rt
        ta[0, a] = height * jnp.exp(-0.5 * za)
        ta[1, a] = slope * q[0] * ca
        ta[2, a] = za - 5.0
        return 0

    lax.fori_loop(0, planes, plane_table, 0, unroll=4)

    def cell(g, _):
        rate_g, rtg = splat(coef, 0, g), splat(coef, 1, g)
        ub, uc = splat(coef, 2, g), splat(coef, 3, g)
        qb, qc = splat(coef, 4, g), splat(coef, 5, g)
        x0 = splat(geo_ref, FIRST, g)
        bell, heat, zz = [], [], []
        for t in range(TILES):
            xb, xc = tile_nodes(t)
            cb, cc = xb - ub, xc - uc
            z = (cb * cb + cc * cc) * rtg
            bell.append(jnp.exp(-0.5 * z))
            heat.append(cb * qb + cc * qc)
            zz.append(z)

        def plane(a, _):
            height_a, heat_a, z_a = [
                jnp.broadcast_to(ta[i, a, pl.ds(g, 1), :], (SUB, LANES)) for i in range(3)
            ]
            for t in range(TILES):
                where = (g, at_rows((a * TILES + t) * SUB), slice(None))
                f = f_ref[where]
                target = (height_a * bell[t]) * (1.0 + (heat_a + heat[t]) * (z_a + zz[t]))
                out_ref[where] = (part_ref[where] - rate_g * f) + target
            return 0

        lax.fori_loop(0, planes, plane, 0, unroll=math.gcd(planes, 8))

        for k in range(FACES):

            @pl.when(links_ref[k, g] == WALL_LINK)
            def _():
                wt = splat(geo_ref, WT, g)
                ratio = splat(coef, 6 + k, g)
                shape = [ratio * x for x in wall_tiles(wt)]
                scale = -TIME_STEP / splat(geo_ref, VOL, g)
                v0, v1, v2 = [scale * x for x in face_coefficients(geo_ref, k, g)]
                base = []
                for t in range(TILES):
                    xb, xc = tile_nodes(t)
                    base.append(v1 * xb + v2 * xc)

                def plane(a, _):
                    xa = x0 + a.astype(F32) * H
                    wa = jnp.exp(-0.5 * xa * xa / wt)
                    sa = v0 * xa
                    for t in range(TILES):
                        where = (g, at_rows((a * TILES + t) * SUB), slice(None))
                        f = f_ref[where]
                        out_ref[where] = out_ref[where] + jnp.maximum(sa + base[t], 0.0) * (wa * shape[t] - f)
                    return 0

                lax.fori_loop(0, planes, plane, 0, unroll=4)

        return 0

    lax.fori_loop(0, SUB, cell, 0)


def add_target(links, geo, absorbed, tiles, f, part):
    rows = f.shape[1]
    vmem = spec(pltpu.VMEM)
    given = [links, geo] + ([] if absorbed is None else [absorbed]) + list(tiles) + [f, part]

    def kernel(links_ref, geo_in, *refs):
        if absorbed is None:
            target_kernel(len(tiles), links_ref, geo_in, None, *refs)
        else:
            target_kernel(len(tiles), links_ref, geo_in, *refs)

    return pl.pallas_call(
        kernel,
        in_specs=[spec(pltpu.SMEM)] + [vmem] * (len(given) - 1),
        out_specs=[vmem] * 2,
        out_shape=[array(*part.shape), array(SUB, LANES)],
        input_output_aliases={len(given) - 1: 0},
        scratch_shapes=[
                pltpu.VMEM((3, rows // CHUNKS, SUB, LANES), F32),
            pltpu.VMEM((6 + FACES, SUB, LANES), F32),
        ],
        compiler_params=params(),
        cost_estimate=traffic(rows, 7),
        name="add_target",
    )(*given)


def halo_terms(pairs_ref, before_ref, after_ref, f_ref, at):
    low, high = [None] * REACH, [None] * REACH
    rows = [before_ref[r, at, :] for r in range(REACH)]
    own = [f_ref[g, at, :] for g in range(REACH)]
    for p, (g, r) in enumerate(BEFORE_PAIRS):
        term = pairs_ref[p, at, :] * (rows[r] - own[g])
        low[g] = term if low[g] is None else low[g] + term
    rows = [after_ref[r, at, :] for r in range(REACH)]
    own = [f_ref[SUB - REACH + e, at, :] for e in range(REACH)]
    p = len(BEFORE_PAIRS)
    for e in range(REACH):
        for r in range(e + 1):
            term = pairs_ref[p, at, :] * (rows[r] - own[e])
            high[e] = term if high[e] is None else high[e] + term
            p += 1
    return low, high


def by_side(far_ref, near_ref, run):
    odd = is_odd()

    @pl.when(odd)
    def _():
        run(near_ref, far_ref)

    @pl.when(jnp.logical_not(odd))
    def _():
        run(far_ref, near_ref)


def edge_kernel(pairs_ref, far_in, near_in, old_ref, part_ref, f_ref, far_out, near_out):
    def run(before_ref, after_ref):
        down_out, up_out = (near_out, far_out) if after_ref is far_in else (far_out, near_out)

        def group(j, _):
            at = at_rows(j * SUB)
            low, high = halo_terms(pairs_ref, before_ref, after_ref, old_ref, at)
            for g in range(REACH):
                x = part_ref[g, at, :] + low[g]
                down_out[g, at, :] = x
                f_ref[g, at, :] = x
                e = SUB - REACH + g
                x = part_ref[e, at, :] + high[g]
                up_out[g, at, :] = x
                f_ref[e, at, :] = x
            return 0

        lax.fori_loop(0, part_ref.shape[1] // SUB, group, 0, unroll=2)

    by_side(far_in, near_in, run)


def edge(pairs, far, near, old, part):
    rows = part.shape[1]
    return pl.pallas_call(
        edge_kernel,
        in_specs=[spec(pltpu.VMEM)] * 5,
        out_specs=[spec(pltpu.VMEM)] * 3,
        out_shape=[array(SUB, rows, LANES), array(REACH, rows, LANES), array(REACH, rows, LANES)],
        input_output_aliases={4: 0},
        compiler_params=params(),
        cost_estimate=traffic(rows, 4),
        name="edge",
    )(pairs, far, near, old, part)


def last_edge_kernel(
    geo_ref, pairs_ref, far_ref, near_ref, f_ref, part_ref, out_hbm, sums_out, native_ref, sems
):
    rows = part_ref.shape[1]
    planes = rows // CHUNKS
    part = rows // SUB // LAST_PARTS

    def copy(i):
        at = pl.ds(i * part * SUB * SUB, part * SUB * SUB)
        return pltpu.make_async_copy(native_ref.at[at], out_hbm.at[at], sems.at[i])

    def run(before_ref, after_ref):
        for i in range(LAST_PARTS):

            def group(j, _):
                at = at_rows(j * SUB)
                low, high = halo_terms(pairs_ref, before_ref, after_ref, f_ref, at)
                terms = low + [None] * (SUB - 2 * REACH) + high
                for g in range(SUB):
                    x = part_ref[g, at, :]
                    where = (pl.ds(j * SUB * SUB + g, SUB, stride=SUB), slice(None))
                    native_ref[where] = x if terms[g] is None else x + terms[g]
                return 0

            lax.fori_loop(i * part, (i + 1) * part, group, 0, unroll=2)
            copy(i).start()

    by_side(far_ref, near_ref, run)
    y = native_polynomial_sums(native_ref, planes)
    sums_out[...] = pack_sums(finish_polynomials(y, geo_ref[FIRST], planes), 0)
    for i in range(LAST_PARTS):
        copy(i).wait()


LAST_PARTS = 4


def last_edge(geo, pairs, far, near, f, part):
    native = (SUB * part.shape[1], LANES)
    return pl.pallas_call(
        last_edge_kernel,
        in_specs=[spec(pltpu.VMEM)] * 6,
        out_specs=[spec(pltpu.HBM), spec(pltpu.VMEM)],
        out_shape=[array(*native), array(SUB, LANES)],
        scratch_shapes=[pltpu.VMEM(native, F32), pltpu.SemaphoreType.DMA((LAST_PARTS,))],
        compiler_params=params(),
        cost_estimate=traffic(part.shape[1], 4),
        name="last_edge",
    )(geo, pairs, far, near, f, part)


def exchange(far, near):
    size = lax.axis_size("space")
    out = []
    for x, start in ((far, 1), (near, 0)):
        pairs = [(i, i + 1) for i in range(start, size - 1, 2)]
        out.append(lax.ppermute(x, "space", pairs + [(j, i) for i, j in pairs]))
    return out


def per_device(particle_profile, neighbors, face_vectors, volumes, wall_temp):
    cells, points = particle_profile.shape
    rows = points // LANES
    plane_count = NV // lax.axis_size("vel")
    native = particle_profile.reshape(cells, rows, LANES).transpose(1, 0, 2).reshape(cells * rows, LANES)
    wall = neighbors < 0
    links = jnp.where(wall, WALL_LINK, neighbors - lax.axis_index("space") * cells)
    own = (links >= 0) & (links < cells)
    first = -SPEED_LIMIT + ((lax.axis_index("vel") * plane_count).astype(F32) + 0.5) * H
    geo = jnp.concatenate(
        [
            face_vectors.reshape(3 * FACES, cells),
            volumes[None],
            wall_temp[None],
            wall.astype(F32),
            own.astype(F32),
            jnp.full((1, cells), first, F32),
        ]
    )
    geo = jnp.broadcast_to(geo[:, :, None], (GEO, cells, LANES))
    native, far, near = first_rows(native)
    far, near = exchange(far, near)
    f, sums = first_sums(links, geo, native)
    tiles = gather_sums(sums)
    pairs = geometry(links, geo, rows)
    part = flux(links, geo, f)
    part, absorbed = add_target(links, geo, None, tiles, f, part)
    f, far, near = edge(pairs, far, near, f, part)
    far, near = exchange(far, near)
    tiles = gather_sums(local_sums(links, geo, f))
    part = flux(links, geo, f)
    part, _ = add_target(links, geo, absorbed, tiles, f, part)
    native, sums = last_edge(geo, pairs, far, near, f, part)
    macro_quantities = macro(doubling_sums(sums))
    evolved = native.reshape(rows, cells, LANES).transpose(1, 0, 2).reshape(cells, points)
    return evolved, macro_quantities


def solution(mesh):
    return jax.shard_map(
        per_device,
        mesh=mesh,
        in_specs=(
            P("space", "vel"),
            P(None, "space"),
            P(None, None, "space"),
            P("space"),
            P("space"),
        ),
        out_specs=(P("space", "vel"), P(None, "space")),
        check_vma=False,
    )
```

```python
import functools
import math

import jax
import jax.numpy as jnp
from jax import lax
from jax.experimental import pallas as pl
from jax.experimental.pallas import tpu as pltpu
from jax.sharding import PartitionSpec as P

NV = 64
FACES = 6
REACH = 3
STEPS = 2
LANES = 128
SUB = 8

TIME_STEP = 0.015
SHEAR = 0.1
POWER = 0.81
SPEED_LIMIT = 6.0
H = 2.0 * SPEED_LIMIT / NV
WEIGHT = H**3 * (2.0 * math.pi) ** (-1.5)

CHUNKS = NV * NV // LANES
TILES = CHUNKS // SUB

FV, VOL, WT, WALL, LOCAL, FIRST = 0, 18, 19, 20, 26, 32
GEO = 33
WALL_LINK = -64
BEFORE_PAIRS = tuple((g, r) for g in range(REACH) for r in range(g, REACH))
EMIT, ABSORB = 13, 19
SUMS = 25

F32 = jnp.float32


def lane_iota():
    return lax.broadcasted_iota(jnp.int32, (SUB, LANES), 1)


def sub_iota():
    return lax.broadcasted_iota(jnp.int32, (SUB, LANES), 0)


def half_of(lane):
    return (lane >= NV).astype(F32)


def third_component(lane):
    c = jnp.where(lane >= NV, lane - NV, lane).astype(F32)
    return -SPEED_LIMIT + (c + 0.5) * H


def tile_nodes(t):
    lane = lane_iota()
    b = (2 * SUB * t + 2 * sub_iota()).astype(F32) + half_of(lane)
    return -SPEED_LIMIT + (b + 0.5) * H, third_component(lane)


def column(tile, p):
    return jnp.broadcast_to(tile[:, p : p + 1], (SUB, LANES))


def splat(ref, i, g):
    return jnp.broadcast_to(ref[i, pl.ds(g, 1), :], (SUB, LANES))


def total(tile):
    return jnp.broadcast_to(jnp.sum(tile, axis=1, keepdims=True), (SUB, LANES))


def face_coefficients(geo_ref, k, g):
    return [splat(geo_ref, FV + FACES * i + k, g) for i in range(3)]


def at_rows(start, size=SUB):
    return pl.ds(pl.multiple_of(start, SUB), size)


def wall_tiles(wall_temp):
    rt = 1.0 / wall_temp
    scale = rt * jnp.sqrt(rt)
    out = []
    for t in range(TILES):
        xb, xc = tile_nodes(t)
        out.append(scale * jnp.exp(-0.5 * (xb * xb + xc * xc) * rt))
    return out


def pack_sums(arrays, start):
    lane = lane_iota()
    out = jnp.zeros((SUB, LANES), F32)
    for p, x in enumerate(arrays):
        out = jnp.where(lane == start + p, total(x), out)
    return out


def over_sublanes(ref, k):
    out = ref[k, pl.ds(0, SUB, stride=SUB), :]
    for s in range(1, SUB):
        out = out + ref[k, pl.ds(s, SUB, stride=SUB), :]
    return out


def list_faces(links_ref, wanted, cell_ref, face_ref):
    def cell(g, count):
        for k in range(FACES):
            cell_ref[count] = g
            face_ref[count] = k
            count = count + wanted(links_ref[k, g]).astype(jnp.int32)
        return count

    return lax.fori_loop(0, SUB, cell, 0)


def is_wall(j):
    return j == WALL_LINK


def is_remote(j):
    return jnp.logical_or(j >= SUB, jnp.logical_and(j < 0, j != WALL_LINK))


def face_lists():
    return [pltpu.SMEM((FACES * SUB + 1,), jnp.int32)] * 2


def unroll(planes, most):
    return math.gcd(planes, most)


def finish_polynomials(y, first, planes):
    y0, y1, y2, y3, by0, by1, by2, bby0, bby1, bbby0 = y
    m = first + 0.5 * (planes - 1) * H
    c = third_component(lane_iota())
    cc = c * c
    a = y1 + m * y0
    aa = y2 + m * (2.0 * y1 + m * y0)
    aaa = y3 + m * (3.0 * y2 + m * (3.0 * y1 + m * y0))
    ab = by1 + m * by0
    aab = by2 + m * (2.0 * by1 + m * by0)
    abb = bby1 + m * bby0
    return (
        y0,
        a,
        by0,
        c * y0,
        aa,
        bby0,
        cc * y0,
        ab,
        c * a,
        c * by0,
        aaa + abb + cc * a,
        aab + bbby0 + cc * by0,
        c * (aa + bby0 + cc * y0),
    )


def polynomial_sums(f_ref, planes, parts_ref):
    half = planes // 2

    def cell(g, _):
        out = [None] * 10
        for t in range(TILES):
            y0 = y1 = y2 = y3 = None
            for i in range(half):
                d = (i + 0.5) * H
                hi = f_ref[g, pl.ds(((half + i) * TILES + t) * SUB, SUB), :]
                lo = f_ref[g, pl.ds(((half - 1 - i) * TILES + t) * SUB, SUB), :]
                s, r = hi + lo, hi - lo
                if i == 0:
                    y0, y1, y2, y3 = s, d * r, (d * d) * s, (d * d * d) * r
                else:
                    y0, y1, y2, y3 = y0 + s, y1 + d * r, y2 + (d * d) * s, y3 + (d * d * d) * r
            b, _c = tile_nodes(t)
            bb = b * b
            terms = (y0, y1, y2, y3, b * y0, b * y1, b * y2, bb * y0, bb * y1, bb * (b * y0))
            out = [x if o is None else o + x for o, x in zip(out, terms)]
        for p in range(10):
            parts_ref[p, at_rows(g * SUB), :] = out[p]
        return 0

    lax.fori_loop(0, SUB, cell, 0)
    return [over_sublanes(parts_ref, p) for p in range(10)]


def native_polynomial_sums(native_ref, planes):
    half, side = planes // 2, CHUNKS // 2
    zero = jnp.zeros((SUB, LANES), F32)
    acc = [zero] * 10

    def plane(a, acc):
        xa = (a.astype(F32) - 0.5 * (planes - 1)) * H
        b0 = b1 = b2 = b3 = None
        for i in range(side):
            y = (2 * i + 1) * H
            hi = native_ref[at_rows((a * CHUNKS + side + i) * SUB), :]
            lo = native_ref[at_rows((a * CHUNKS + side - 1 - i) * SUB), :]
            s, d = hi + lo, hi - lo
            terms = (s, y * d, (y * y) * s, (y * y * y) * d)
            if i == 0:
                b0, b1, b2, b3 = terms
            else:
                b0, b1, b2, b3 = b0 + terms[0], b1 + terms[1], b2 + terms[2], b3 + terms[3]
        a0, a1, a2 = xa * b0, xa * b1, xa * b2
        aa0 = xa * a0
        new = (b0, a0, aa0, xa * aa0, b1, a1, xa * a1, b2, a2, b3)
        return tuple(x + z for x, z in zip(acc, new))

    g0, a0, aa0, aaa0, g1, a1, aa1, g2, a2, g3 = lax.fori_loop(0, planes, plane, tuple(acc))
    e = (half_of(lane_iota()) - 0.5) * H
    return [
        g0,
        a0,
        aa0,
        aaa0,
        g1 + e * g0,
        a1 + e * a0,
        aa1 + e * aa0,
        g2 + e * (2.0 * g1 + e * g0),
        a2 + e * (2.0 * a1 + e * a0),
        g3 + e * (3.0 * g2 + e * (3.0 * g1 + e * g0)),
    ]


def wall_sums(f_ref, planes, links_ref, geo_ref, sums_ref, cells, faces, with_absorbed):
    sums_ref[...] = jnp.zeros_like(sums_ref)

    def wall(i, _):
        g, k = cells[i], faces[i]
        v0, v1, v2 = face_coefficients(geo_ref, k, g)
        first = splat(geo_ref, FIRST, g)
        base = []
        for t in range(TILES):
            xb, xc = tile_nodes(t)
            base.append(v1 * xb + v2 * xc)
        if with_absorbed:
            wt = splat(geo_ref, WT, g)
            shape = wall_tiles(wt)

        def plane(a, acc):
            out, back = list(acc[0]), list(acc[1])
            xa = first + a.astype(F32) * H
            sa = v0 * xa
            if with_absorbed:
                wa = jnp.exp(-0.5 * xa * xa / wt)
            for t in range(TILES):
                s = sa + base[t]
                f = f_ref[g, at_rows((a * TILES + t) * SUB), :]
                out[t] = out[t] + jnp.maximum(s, 0.0) * f
                if with_absorbed:
                    back[t] = back[t] + jnp.maximum(-s, 0.0) * (wa * shape[t])
            return tuple(out), tuple(back)

        zeros = (jnp.zeros((SUB, LANES), F32),) * TILES
        out, back = lax.fori_loop(0, planes, plane, (zeros, zeros), unroll=unroll(planes, 16))
        at = at_rows(g * SUB)
        sums_ref[k, at, :] = (out[0] + out[1]) + (out[2] + out[3])
        if with_absorbed:
            sums_ref[FACES + k, at, :] = (back[0] + back[1]) + (back[2] + back[3])
        return 0

    lax.fori_loop(0, list_faces(links_ref, is_wall, cells, faces), wall, 0)


def sums_kernel(links_ref, geo_ref, f_ref, sums_out, parts_ref, face_ref, cells, faces):
    planes = f_ref.shape[1] // CHUNKS
    y = polynomial_sums(f_ref, planes, parts_ref)
    packed = pack_sums(finish_polynomials(y, geo_ref[FIRST], planes), 0)
    wall_sums(f_ref, planes, links_ref, geo_ref, face_ref, cells, faces, False)
    sums_out[...] = packed + pack_sums([over_sublanes(face_ref, k) for k in range(FACES)], EMIT)


def first_sums_kernel(links_ref, geo_ref, native_ref, f_ref, sums_out, face_ref, cells, faces):
    rows = f_ref.shape[1]
    planes = rows // CHUNKS

    def group(j, _):
        for g in range(SUB):
            f_ref[g, at_rows(j * SUB), :] = native_ref[pl.ds(j * SUB * SUB + g, SUB, stride=SUB), :]
        return 0

    lax.fori_loop(0, rows // SUB, group, 0, unroll=2)
    y = native_polynomial_sums(native_ref, planes)
    packed = pack_sums(finish_polynomials(y, geo_ref[FIRST], planes), 0)
    wall_sums(f_ref, planes, links_ref, geo_ref, face_ref, cells, faces, True)
    sums_out[...] = packed + pack_sums([over_sublanes(face_ref, k) for k in range(2 * FACES)], EMIT)


def spec(space):
    return pl.BlockSpec(memory_space=space)


def array(*shape):
    return jax.ShapeDtypeStruct(shape, F32)


def params(mib=8):
    return pltpu.CompilerParams(vmem_limit_bytes=mib * 1024 * 1024)


def traffic(rows, profiles):
    size = SUB * rows * LANES
    return pl.CostEstimate(flops=8 * profiles * size, bytes_accessed=4 * profiles * size, transcendentals=0)


def local_sums(links, geo, f):
    return pl.pallas_call(
        sums_kernel,
        in_specs=[spec(pltpu.SMEM), spec(pltpu.VMEM), spec(pltpu.VMEM)],
        out_specs=spec(pltpu.VMEM),
        out_shape=array(SUB, LANES),
        scratch_shapes=[
                pltpu.VMEM((10, SUB * SUB, LANES), F32),
            pltpu.VMEM((FACES, SUB * SUB, LANES), F32),
            *face_lists(),
        ],
        compiler_params=params(),
        cost_estimate=traffic(f.shape[1], 4),
        name="local_sums",
    )(links, geo, f)


def first_sums(links, geo, native):
    rows = native.shape[0] // SUB
    return pl.pallas_call(
        first_sums_kernel,
        in_specs=[spec(pltpu.SMEM), spec(pltpu.VMEM), spec(pltpu.VMEM)],
        out_specs=[spec(pltpu.VMEM)] * 2,
        out_shape=[array(SUB, rows, LANES), array(SUB, LANES)],
        scratch_shapes=[
                pltpu.VMEM((2 * FACES, SUB * SUB, LANES), F32),
            *face_lists(),
        ],
        compiler_params=params(),
        cost_estimate=traffic(rows, 5),
        name="first_sums",
    )(links, geo, native)


SPLIT_PARTS = 4


def is_odd():
    return lax.rem(lax.axis_index("space"), 2) == 1


def first_rows_kernel(native_hbm, native_ref, far_any, near_any, far_ref, near_ref, sems, far_sems, near_sems):
    rows = native_ref.shape[0]
    part = rows // SPLIT_PARTS
    copies = [
        pltpu.make_async_copy(
            native_hbm.at[pl.ds(i * part, part)], native_ref.at[pl.ds(i * part, part)], sems.at[i]
        )
        for i in range(SPLIT_PARTS)
    ]
    for c in copies:
        c.start()
    odd = is_odd()
    far = jnp.where(odd, SUB - REACH, 0)
    near = jnp.where(odd, 0, SUB - REACH)
    groups = part // (SUB * SUB)
    out = []

    for i, c in enumerate(copies):
        c.wait()

        def group(j, _):
            for r in range(REACH):
                at = at_rows(j * SUB)
                far_ref[r, at, :] = native_ref[pl.ds(j * SUB * SUB + far + r, SUB, stride=SUB), :]
                near_ref[r, at, :] = native_ref[pl.ds(j * SUB * SUB + near + r, SUB, stride=SUB), :]
            return 0

        lax.fori_loop(i * groups, (i + 1) * groups, group, 0, unroll=unroll(groups, 8))
        at = pl.ds(i * groups * SUB, groups * SUB)
        out.append(pltpu.make_async_copy(far_ref.at[:, at], far_any.at[:, at], far_sems.at[i]))
        out.append(pltpu.make_async_copy(near_ref.at[:, at], near_any.at[:, at], near_sems.at[i]))
        out[-2].start()
        out[-1].start()
    for c in out:
        c.wait()


def first_rows(native):
    rows = native.shape[0] // SUB
    halo = (REACH, rows, LANES)
    return pl.pallas_call(
        first_rows_kernel,
        in_specs=[spec(pltpu.HBM)],
        out_specs=[spec(pltpu.VMEM), spec(pl.ANY), spec(pl.ANY)],
        out_shape=[array(*native.shape), array(*halo), array(*halo)],
        scratch_shapes=[pltpu.VMEM(halo, F32)] * 2 + [pltpu.SemaphoreType.DMA((SPLIT_PARTS,))] * 3,
        compiler_params=params(),
        cost_estimate=traffic(rows, 4),
        name="first_rows",
    )(pltpu.with_memory_space_constraint(native, pltpu.HBM))


def geometry_kernel(links_ref, geo_ref, pairs_ref, cells, faces):
    rows = pairs_ref.shape[1]
    planes = rows // CHUNKS
    first = splat(geo_ref, FIRST, 0)

    def clear(j, _):
        for p in range(pairs_ref.shape[0]):
            pairs_ref[p, at_rows(j * SUB), :] = jnp.zeros((SUB, LANES), F32)
        return 0

    lax.fori_loop(0, rows // SUB, clear, 0, unroll=4)

    def remote(i, _):
        g, k = cells[i], faces[i]
        j = links_ref[k, g]
        edge = g - (SUB - REACH)
        before = g * REACH - g * (g - 1) // 2 + (j + REACH) - g
        after = len(BEFORE_PAIRS) + edge * (edge + 1) // 2 + j - SUB
        at_pair = jnp.where(j < 0, before, after)
        scale = -TIME_STEP / splat(geo_ref, VOL, g)
        v0, v1, v2 = [scale * x for x in face_coefficients(geo_ref, k, g)]
        base = []
        for t in range(TILES):
            xb, xc = tile_nodes(t)
            base.append(v1 * xb + v2 * xc)

        def plane(a, _):
            sa = v0 * (first + a.astype(F32) * H)
            for t in range(TILES):
                at = at_rows((a * TILES + t) * SUB)
                pairs_ref[at_pair, at, :] = pairs_ref[at_pair, at, :] + jnp.maximum(sa + base[t], 0.0)
            return 0

        lax.fori_loop(0, planes, plane, 0, unroll=unroll(planes, 8))
        return 0

    lax.fori_loop(0, list_faces(links_ref, is_remote, cells, faces), remote, 0)


def geometry(links, geo, rows):
    return pl.pallas_call(
        geometry_kernel,
        in_specs=[spec(pltpu.SMEM), spec(pltpu.VMEM)],
        out_specs=spec(pltpu.VMEM),
        out_shape=array(2 * len(BEFORE_PAIRS), rows, LANES),
        scratch_shapes=face_lists(),
        compiler_params=params(),
        cost_estimate=traffic(rows, 4),
        name="geometry",
    )(links, geo)


def gather_sums(tile):
    size = lax.axis_size("vel")
    if size not in (2, 4):
        return [lax.psum(tile, "vel")]
    others = [lax.ppermute(tile, "vel", [(i, i ^ s) for i in range(size)]) for s in range(1, size)]
    return [tile, *others]


def doubling_sums(tile):
    size = lax.axis_size("vel")
    if size != 4:
        return gather_sums(tile)
    pair = tile + lax.ppermute(tile, "vel", [(i, i ^ 1) for i in range(size)])
    return [pair, lax.ppermute(pair, "vel", [(i, i ^ 2) for i in range(size)])]


def add_tiles(refs):
    tiles = [r[...] for r in refs]
    while len(tiles) > 1:
        tiles = [tiles[i] + tiles[i + 1] for i in range(0, len(tiles), 2)]
    return tiles[0]


def quantities(tile):
    m = [WEIGHT * column(tile, p) for p in range(13)]
    n = m[0]
    rn = 1.0 / n
    u = [m[1 + i] * rn for i in range(3)]
    uu = u[0] * u[0] + u[1] * u[1] + u[2] * u[2]
    trace = m[4] + m[5] + m[6]
    width = trace - n * uu
    temperature = width * rn * (1.0 / 3.0)
    second = [[m[4], m[7], m[8]], [m[7], m[5], m[9]], [m[8], m[9], m[6]]]
    q = []
    for i in range(3):
        across = u[0] * second[i][0] + u[1] * second[i][1] + u[2] * second[i][2]
        q.append(0.5 * (m[10 + i] - 2.0 * across - u[i] * trace + 2.0 * uu * m[1 + i]))
    return n, u, temperature, q


def macro_kernel(*refs):
    out_ref = refs[-1]
    n, u, temperature, q = quantities(add_tiles(refs[:-1]))
    lane, sub = lane_iota(), sub_iota()
    for i, x in enumerate((n, *u, temperature, *q)):
        row = jnp.sum(jnp.where(lane == sub, x, 0.0), axis=0, keepdims=True)
        out_ref[pl.ds(i, 1), :] = row[:, :SUB]


def macro(tiles):
    return pl.pallas_call(
        macro_kernel,
        in_specs=[spec(pltpu.VMEM)] * len(tiles),
        out_specs=spec(pltpu.VMEM),
        out_shape=array(8, SUB),
        compiler_params=params(1),
        name="macro",
    )(*tiles)


def flux_kernel(links_ref, geo_ref, f_ref, out_ref, coef, source, face):
    planes = f_ref.shape[1] // CHUNKS
    scale = -TIME_STEP / geo_ref[VOL]
    for i in range(3):
        whole = None
        for k in range(FACES):
            x = scale * geo_ref[FV + FACES * i + k]
            coef[FACES * i + k] = x
            whole = x if whole is None else whole + x
        coef[3 * FACES + i] = whole

    def cell(g, _):
        count = 0
        for k in range(FACES):
            j = links_ref[k, g]
            source[count] = j
            face[count] = k
            count = count + jnp.logical_and(j >= 0, j < SUB).astype(jnp.int32)
        for n in range(FACES + 1):

            @pl.when(count == n)
            def _():
                own_faces(g, n)

        return 0

    def own_faces(g, n):
        at_source = [source[i] for i in range(n)]
        weight = [[splat(coef, FACES * i + face[k], g) for i in range(3)] for k in range(n)]
        whole = [splat(coef, 3 * FACES + i, g) for i in range(3)]
        x0 = splat(geo_ref, FIRST, g)
        base, stay = [], []
        for t in range(TILES):
            xb, xc = tile_nodes(t)
            base.append([w[1] * xb + w[2] * xc for w in weight])
            stay.append(1.0 + whole[1] * xb + whole[2] * xc)

        def plane(a, _):
            xa = x0 + a.astype(F32) * H
            sa = [w[0] * xa for w in weight]
            stay_a = whole[0] * xa
            for t in range(TILES):
                at = at_rows((a * TILES + t) * SUB)
                f = f_ref[g, at, :]
                acc = f * (stay_a + stay[t])
                for k in range(n):
                    acc = acc + jnp.maximum(sa[k] + base[t][k], 0.0) * (f_ref[at_source[k], at, :] - f)
                out_ref[g, at, :] = acc
            return 0

        lax.fori_loop(0, planes, plane, 0, unroll=unroll(planes, 8))

    lax.fori_loop(0, SUB, cell, 0)


def flux(links, geo, f):
    return pl.pallas_call(
        flux_kernel,
        in_specs=[spec(pltpu.SMEM), spec(pltpu.VMEM), spec(pltpu.VMEM)],
        out_specs=spec(pltpu.VMEM),
        out_shape=array(*f.shape),
        scratch_shapes=[
            pltpu.VMEM((3 * FACES + 3, SUB, LANES), F32),
            pltpu.SMEM((FACES + 1,), jnp.int32),
            pltpu.SMEM((FACES + 1,), jnp.int32),
        ],
        compiler_params=params(),
        cost_estimate=traffic(f.shape[1], 7),
        name="flux",
    )(links, geo, f)


def target_kernel(count, links_ref, geo_ref, absorbed_in, *refs):
    sums_refs, (f_ref, part_ref, out_ref, sum_out, ta, coef, cells, faces) = refs[:count], refs[count:]
    planes = f_ref.shape[1] // CHUNKS
    sums = add_tiles(sums_refs)
    sum_out[...] = sums
    absorbed = sums if absorbed_in is None else absorbed_in[...]
    n, u, temperature, q = quantities(sums)
    rt = 1.0 / temperature
    rate = TIME_STEP * n * temperature / (SHEAR * jnp.exp(POWER * jnp.log(temperature)))
    height = rate * n * rt * jnp.sqrt(rt)
    slope = (1.0 / 3.0) / (5.0 * n * temperature * temperature)
    coef[0] = rate
    coef[1] = rt
    coef[2], coef[3] = u[1], u[2]
    coef[4], coef[5] = slope * q[1], slope * q[2]
    for k in range(FACES):
        wall = geo_ref[WALL + k] > 0.5
        coef[6 + k] = column(sums, EMIT + k) / jnp.where(wall, column(absorbed, ABSORB + k), 1.0)
    first = geo_ref[FIRST]

    def plane_table(a, _):
        ca = first + a.astype(F32) * H - u[0]
        za = ca * ca * rt
        ta[0, a] = height * jnp.exp(-0.5 * za)
        ta[1, a] = slope * q[0] * ca
        ta[2, a] = za - 5.0
        return 0

    lax.fori_loop(0, planes, plane_table, 0, unroll=4)

    def cell(g, _):
        rate_g, rtg = splat(coef, 0, g), splat(coef, 1, g)
        ub, uc = splat(coef, 2, g), splat(coef, 3, g)
        qb, qc = splat(coef, 4, g), splat(coef, 5, g)
        bell, heat, zz = [], [], []
        for t in range(TILES):
            xb, xc = tile_nodes(t)
            cb, cc = xb - ub, xc - uc
            z = (cb * cb + cc * cc) * rtg
            bell.append(jnp.exp(-0.5 * z))
            heat.append(cb * qb + cc * qc)
            zz.append(z)

        def plane(a, _):
            height_a, heat_a, z_a = [
                jnp.broadcast_to(ta[i, a, pl.ds(g, 1), :], (SUB, LANES)) for i in range(3)
            ]
            for t in range(TILES):
                where = (g, at_rows((a * TILES + t) * SUB), slice(None))
                f = f_ref[where]
                target = (height_a * bell[t]) * (1.0 + (heat_a + heat[t]) * (z_a + zz[t]))
                out_ref[where] = (part_ref[where] - rate_g * f) + target
            return 0

        lax.fori_loop(0, planes, plane, 0, unroll=unroll(planes, 16))
        return 0

    lax.fori_loop(0, SUB, cell, 0)

    def wall(i, _):
        g, k = cells[i], faces[i]
        x0 = splat(geo_ref, FIRST, g)
        wt = splat(geo_ref, WT, g)
        ratio = splat(coef, 6 + k, g)
        shape = [ratio * x for x in wall_tiles(wt)]
        scale = -TIME_STEP / splat(geo_ref, VOL, g)
        v0, v1, v2 = [scale * x for x in face_coefficients(geo_ref, k, g)]
        base = []
        for t in range(TILES):
            xb, xc = tile_nodes(t)
            base.append(v1 * xb + v2 * xc)

        def plane(a, _):
            xa = x0 + a.astype(F32) * H
            wa = jnp.exp(-0.5 * xa * xa / wt)
            sa = v0 * xa
            for t in range(TILES):
                where = (g, at_rows((a * TILES + t) * SUB), slice(None))
                f = f_ref[where]
                out_ref[where] = out_ref[where] + jnp.maximum(sa + base[t], 0.0) * (wa * shape[t] - f)
            return 0

        lax.fori_loop(0, planes, plane, 0, unroll=unroll(planes, 8))
        return 0

    lax.fori_loop(0, list_faces(links_ref, is_wall, cells, faces), wall, 0)


def add_target(links, geo, absorbed, tiles, f, part):
    rows = f.shape[1]
    vmem = spec(pltpu.VMEM)
    given = [links, geo] + ([] if absorbed is None else [absorbed]) + list(tiles) + [f, part]

    def kernel(links_ref, geo_in, *refs):
        if absorbed is None:
            target_kernel(len(tiles), links_ref, geo_in, None, *refs)
        else:
            target_kernel(len(tiles), links_ref, geo_in, *refs)

    return pl.pallas_call(
        kernel,
        in_specs=[spec(pltpu.SMEM)] + [vmem] * (len(given) - 1),
        out_specs=[vmem] * 2,
        out_shape=[array(*part.shape), array(SUB, LANES)],
        input_output_aliases={len(given) - 1: 0},
        scratch_shapes=[
                pltpu.VMEM((3, rows // CHUNKS, SUB, LANES), F32),
            pltpu.VMEM((6 + FACES, SUB, LANES), F32),
            *face_lists(),
        ],
        compiler_params=params(),
        cost_estimate=traffic(rows, 7),
        name="add_target",
    )(*given)


def halo_terms(pairs_ref, before_ref, after_ref, f_ref, at):
    low, high = [None] * REACH, [None] * REACH
    rows = [before_ref[r, at, :] for r in range(REACH)]
    own = [f_ref[g, at, :] for g in range(REACH)]
    for p, (g, r) in enumerate(BEFORE_PAIRS):
        term = pairs_ref[p, at, :] * (rows[r] - own[g])
        low[g] = term if low[g] is None else low[g] + term
    rows = [after_ref[r, at, :] for r in range(REACH)]
    own = [f_ref[SUB - REACH + e, at, :] for e in range(REACH)]
    p = len(BEFORE_PAIRS)
    for e in range(REACH):
        for r in range(e + 1):
            term = pairs_ref[p, at, :] * (rows[r] - own[e])
            high[e] = term if high[e] is None else high[e] + term
            p += 1
    return low, high


def by_side(far_ref, near_ref, run):
    odd = is_odd()

    @pl.when(odd)
    def _():
        run(near_ref, far_ref)

    @pl.when(jnp.logical_not(odd))
    def _():
        run(far_ref, near_ref)


def edge_kernel(pairs_ref, far_in, near_in, old_ref, part_ref, f_ref, far_out, near_out):
    def run(before_ref, after_ref):
        down_out, up_out = (near_out, far_out) if after_ref is far_in else (far_out, near_out)

        def group(j, _):
            at = at_rows(j * SUB)
            low, high = halo_terms(pairs_ref, before_ref, after_ref, old_ref, at)
            for g in range(REACH):
                x = part_ref[g, at, :] + low[g]
                down_out[g, at, :] = x
                f_ref[g, at, :] = x
                e = SUB - REACH + g
                x = part_ref[e, at, :] + high[g]
                up_out[g, at, :] = x
                f_ref[e, at, :] = x
            return 0

        lax.fori_loop(0, part_ref.shape[1] // SUB, group, 0, unroll=4)

    by_side(far_in, near_in, run)


def edge(pairs, far, near, old, part):
    rows = part.shape[1]
    return pl.pallas_call(
        edge_kernel,
        in_specs=[spec(pltpu.VMEM)] * 5,
        out_specs=[spec(pltpu.VMEM)] * 3,
        out_shape=[array(SUB, rows, LANES), array(REACH, rows, LANES), array(REACH, rows, LANES)],
        input_output_aliases={4: 0},
        compiler_params=params(),
        cost_estimate=traffic(rows, 4),
        name="edge",
    )(pairs, far, near, old, part)


def last_edge_kernel(
    geo_ref, pairs_ref, far_ref, near_ref, f_ref, part_ref, out_hbm, sums_out, native_ref, sems
):
    rows = part_ref.shape[1]
    planes = rows // CHUNKS
    part = rows // SUB // LAST_PARTS

    def copy(i):
        at = pl.ds(i * part * SUB * SUB, part * SUB * SUB)
        return pltpu.make_async_copy(native_ref.at[at], out_hbm.at[at], sems.at[i])

    def run(before_ref, after_ref):
        for i in range(LAST_PARTS):

            def group(j, _):
                at = at_rows(j * SUB)
                low, high = halo_terms(pairs_ref, before_ref, after_ref, f_ref, at)
                terms = low + [None] * (SUB - 2 * REACH) + high
                for g in range(SUB):
                    x = part_ref[g, at, :]
                    where = (pl.ds(j * SUB * SUB + g, SUB, stride=SUB), slice(None))
                    native_ref[where] = x if terms[g] is None else x + terms[g]
                return 0

            lax.fori_loop(i * part, (i + 1) * part, group, 0, unroll=2)
            copy(i).start()

    by_side(far_ref, near_ref, run)
    y = native_polynomial_sums(native_ref, planes)
    sums_out[...] = pack_sums(finish_polynomials(y, geo_ref[FIRST], planes), 0)
    for i in range(LAST_PARTS):
        copy(i).wait()


LAST_PARTS = 4


def last_edge(geo, pairs, far, near, f, part):
    native = (SUB * part.shape[1], LANES)
    return pl.pallas_call(
        last_edge_kernel,
        in_specs=[spec(pltpu.VMEM)] * 6,
        out_specs=[spec(pltpu.HBM), spec(pltpu.VMEM)],
        out_shape=[array(*native), array(SUB, LANES)],
        scratch_shapes=[pltpu.VMEM(native, F32), pltpu.SemaphoreType.DMA((LAST_PARTS,))],
        compiler_params=params(),
        cost_estimate=traffic(part.shape[1], 4),
        name="last_edge",
    )(geo, pairs, far, near, f, part)


def exchange(far, near):
    size = lax.axis_size("space")
    out = []
    for x, start in ((far, 1), (near, 0)):
        pairs = [(i, i + 1) for i in range(start, size - 1, 2)]
        out.append(lax.ppermute(x, "space", pairs + [(j, i) for i, j in pairs]))
    return out


def per_device(particle_profile, neighbors, face_vectors, volumes, wall_temp):
    cells, points = particle_profile.shape
    rows = points // LANES
    plane_count = NV // lax.axis_size("vel")
    native = particle_profile.reshape(cells, rows, LANES).transpose(1, 0, 2).reshape(cells * rows, LANES)
    wall = neighbors < 0
    links = jnp.where(wall, WALL_LINK, neighbors - lax.axis_index("space") * cells)
    own = (links >= 0) & (links < cells)
    first = -SPEED_LIMIT + ((lax.axis_index("vel") * plane_count).astype(F32) + 0.5) * H
    geo = jnp.concatenate(
        [
            face_vectors.reshape(3 * FACES, cells),
            volumes[None],
            wall_temp[None],
            wall.astype(F32),
            own.astype(F32),
            jnp.full((1, cells), first, F32),
        ]
    )
    geo = jnp.broadcast_to(geo[:, :, None], (GEO, cells, LANES))
    native, far, near = first_rows(native)
    far, near = exchange(far, near)
    f, sums = first_sums(links, geo, native)
    tiles = gather_sums(sums)
    pairs = geometry(links, geo, rows)
    part = flux(links, geo, f)
    part, absorbed = add_target(links, geo, None, tiles, f, part)
    f, far, near = edge(pairs, far, near, f, part)
    far, near = exchange(far, near)
    tiles = gather_sums(local_sums(links, geo, f))
    part = flux(links, geo, f)
    part, _ = add_target(links, geo, absorbed, tiles, f, part)
    native, sums = last_edge(geo, pairs, far, near, f, part)
    macro_quantities = macro(doubling_sums(sums))
    evolved = native.reshape(rows, cells, LANES).transpose(1, 0, 2).reshape(cells, points)
    return evolved, macro_quantities


def solution(mesh):
    return jax.shard_map(
        per_device,
        mesh=mesh,
        in_specs=(
            P("space", "vel"),
            P(None, "space"),
            P(None, None, "space"),
            P("space"),
            P("space"),
        ),
        out_specs=(P("space", "vel"), P(None, "space")),
        check_vma=False,
    )
```

```python
import functools
import math

import jax
import jax.numpy as jnp
from jax import lax
from jax.experimental import pallas as pl
from jax.experimental.pallas import tpu as pltpu
from jax.sharding import PartitionSpec as P

NV = 64
FACES = 6
REACH = 3
STEPS = 2
LANES = 128
SUB = 8

TIME_STEP = 0.015
SHEAR = 0.1
POWER = 0.81
SPEED_LIMIT = 6.0
H = 2.0 * SPEED_LIMIT / NV
WEIGHT = H**3 * (2.0 * math.pi) ** (-1.5)

CHUNKS = NV * NV // LANES
TILES = CHUNKS // SUB

FV, VOL, WT, WALL, LOCAL, FIRST = 0, 18, 19, 20, 26, 32
GEO = 33
WALL_LINK = -64
BEFORE_PAIRS = tuple((g, r) for g in range(REACH) for r in range(g, REACH))
EMIT, ABSORB = 13, 19
SUMS = 25

F32 = jnp.float32


def lane_iota():
    return lax.broadcasted_iota(jnp.int32, (SUB, LANES), 1)


def sub_iota():
    return lax.broadcasted_iota(jnp.int32, (SUB, LANES), 0)


def half_of(lane):
    return (lane >= NV).astype(F32)


def third_component(lane):
    c = jnp.where(lane >= NV, lane - NV, lane).astype(F32)
    return -SPEED_LIMIT + (c + 0.5) * H


def tile_nodes(t):
    lane = lane_iota()
    b = (2 * SUB * t + 2 * sub_iota()).astype(F32) + half_of(lane)
    return -SPEED_LIMIT + (b + 0.5) * H, third_component(lane)


def column(tile, p):
    return jnp.broadcast_to(tile[:, p : p + 1], (SUB, LANES))


def splat(ref, i, g):
    return jnp.broadcast_to(ref[i, pl.ds(g, 1), :], (SUB, LANES))


def total(tile):
    return jnp.broadcast_to(jnp.sum(tile, axis=1, keepdims=True), (SUB, LANES))


def face_coefficients(geo_ref, k, g):
    return [splat(geo_ref, FV + FACES * i + k, g) for i in range(3)]


def at_rows(start, size=SUB):
    return pl.ds(pl.multiple_of(start, SUB), size)


def wall_tiles(wall_temp):
    rt = 1.0 / wall_temp
    scale = rt * jnp.sqrt(rt)
    out = []
    for t in range(TILES):
        xb, xc = tile_nodes(t)
        out.append(scale * jnp.exp(-0.5 * (xb * xb + xc * xc) * rt))
    return out


def pack_sums(arrays, start):
    lane = lane_iota()
    out = jnp.zeros((SUB, LANES), F32)
    for p, x in enumerate(arrays):
        out = jnp.where(lane == start + p, total(x), out)
    return out


def over_sublanes(ref, k):
    out = ref[k, pl.ds(0, SUB, stride=SUB), :]
    for s in range(1, SUB):
        out = out + ref[k, pl.ds(s, SUB, stride=SUB), :]
    return out


def list_faces(links_ref, wanted, cell_ref, face_ref):
    def cell(g, count):
        for k in range(FACES):
            cell_ref[count] = g
            face_ref[count] = k
            count = count + wanted(links_ref[k, g]).astype(jnp.int32)
        return count

    return lax.fori_loop(0, SUB, cell, 0)


def is_wall(j):
    return j == WALL_LINK


def is_remote(j):
    return jnp.logical_or(j >= SUB, jnp.logical_and(j < 0, j != WALL_LINK))


def face_lists():
    return [pltpu.SMEM((FACES * SUB + 1,), jnp.int32)] * 2


def unroll(planes, most):
    return math.gcd(planes, most)


def finish_polynomials(y, first, planes):
    y0, y1, y2, y3, by0, by1, by2, bby0, bby1, bbby0 = y
    m = first + 0.5 * (planes - 1) * H
    c = third_component(lane_iota())
    cc = c * c
    a = y1 + m * y0
    aa = y2 + m * (2.0 * y1 + m * y0)
    aaa = y3 + m * (3.0 * y2 + m * (3.0 * y1 + m * y0))
    ab = by1 + m * by0
    aab = by2 + m * (2.0 * by1 + m * by0)
    abb = bby1 + m * bby0
    return (
        y0,
        a,
        by0,
        c * y0,
        aa,
        bby0,
        cc * y0,
        ab,
        c * a,
        c * by0,
        aaa + abb + cc * a,
        aab + bbby0 + cc * by0,
        c * (aa + bby0 + cc * y0),
    )


def polynomial_sums(f_ref, planes, parts_ref):
    half = planes // 2

    def cell(g, _):
        out = [None] * 10
        for t in range(TILES):
            y0 = y1 = y2 = y3 = None
            for i in range(half):
                d = (i + 0.5) * H
                hi = f_ref[g, pl.ds(((half + i) * TILES + t) * SUB, SUB), :]
                lo = f_ref[g, pl.ds(((half - 1 - i) * TILES + t) * SUB, SUB), :]
                s, r = hi + lo, hi - lo
                if i == 0:
                    y0, y1, y2, y3 = s, d * r, (d * d) * s, (d * d * d) * r
                else:
                    y0, y1, y2, y3 = y0 + s, y1 + d * r, y2 + (d * d) * s, y3 + (d * d * d) * r
            b, _c = tile_nodes(t)
            bb = b * b
            terms = (y0, y1, y2, y3, b * y0, b * y1, b * y2, bb * y0, bb * y1, bb * (b * y0))
            out = [x if o is None else o + x for o, x in zip(out, terms)]
        for p in range(10):
            parts_ref[p, at_rows(g * SUB), :] = out[p]
        return 0

    lax.fori_loop(0, SUB, cell, 0)
    return [over_sublanes(parts_ref, p) for p in range(10)]


def native_polynomial_sums(native_ref, planes):
    half, side = planes // 2, CHUNKS // 2
    zero = jnp.zeros((SUB, LANES), F32)
    acc = [zero] * 10

    def plane(a, acc):
        xa = (a.astype(F32) - 0.5 * (planes - 1)) * H
        b0 = b1 = b2 = b3 = None
        for i in range(side):
            y = (2 * i + 1) * H
            hi = native_ref[at_rows((a * CHUNKS + side + i) * SUB), :]
            lo = native_ref[at_rows((a * CHUNKS + side - 1 - i) * SUB), :]
            s, d = hi + lo, hi - lo
            terms = (s, y * d, (y * y) * s, (y * y * y) * d)
            if i == 0:
                b0, b1, b2, b3 = terms
            else:
                b0, b1, b2, b3 = b0 + terms[0], b1 + terms[1], b2 + terms[2], b3 + terms[3]
        a0, a1, a2 = xa * b0, xa * b1, xa * b2
        aa0 = xa * a0
        new = (b0, a0, aa0, xa * aa0, b1, a1, xa * a1, b2, a2, b3)
        return tuple(x + z for x, z in zip(acc, new))

    g0, a0, aa0, aaa0, g1, a1, aa1, g2, a2, g3 = lax.fori_loop(0, planes, plane, tuple(acc))
    e = (half_of(lane_iota()) - 0.5) * H
    return [
        g0,
        a0,
        aa0,
        aaa0,
        g1 + e * g0,
        a1 + e * a0,
        aa1 + e * aa0,
        g2 + e * (2.0 * g1 + e * g0),
        a2 + e * (2.0 * a1 + e * a0),
        g3 + e * (3.0 * g2 + e * (3.0 * g1 + e * g0)),
    ]


def wall_sums(f_ref, planes, links_ref, geo_ref, sums_ref, cells, faces, with_absorbed):
    sums_ref[...] = jnp.zeros_like(sums_ref)

    def wall(i, _):
        g, k = cells[i], faces[i]
        v0, v1, v2 = face_coefficients(geo_ref, k, g)
        first = splat(geo_ref, FIRST, g)
        base = []
        for t in range(TILES):
            xb, xc = tile_nodes(t)
            base.append(v1 * xb + v2 * xc)
        if with_absorbed:
            wt = splat(geo_ref, WT, g)
            shape = wall_tiles(wt)

        def plane(a, acc):
            out, back = list(acc[0]), list(acc[1])
            xa = first + a.astype(F32) * H
            sa = v0 * xa
            if with_absorbed:
                wa = jnp.exp(-0.5 * xa * xa / wt)
            for t in range(TILES):
                s = sa + base[t]
                f = f_ref[g, at_rows((a * TILES + t) * SUB), :]
                out[t] = out[t] + jnp.maximum(s, 0.0) * f
                if with_absorbed:
                    back[t] = back[t] + jnp.maximum(-s, 0.0) * (wa * shape[t])
            return tuple(out), tuple(back)

        zeros = (jnp.zeros((SUB, LANES), F32),) * TILES
        out, back = lax.fori_loop(0, planes, plane, (zeros, zeros), unroll=unroll(planes, 16))
        at = at_rows(g * SUB)
        sums_ref[k, at, :] = (out[0] + out[1]) + (out[2] + out[3])
        if with_absorbed:
            sums_ref[FACES + k, at, :] = (back[0] + back[1]) + (back[2] + back[3])
        return 0

    lax.fori_loop(0, list_faces(links_ref, is_wall, cells, faces), wall, 0)


def sums_kernel(links_ref, geo_ref, f_ref, sums_out, parts_ref, face_ref, cells, faces):
    planes = f_ref.shape[1] // CHUNKS
    y = polynomial_sums(f_ref, planes, parts_ref)
    packed = pack_sums(finish_polynomials(y, geo_ref[FIRST], planes), 0)
    wall_sums(f_ref, planes, links_ref, geo_ref, face_ref, cells, faces, False)
    sums_out[...] = packed + pack_sums([over_sublanes(face_ref, k) for k in range(FACES)], EMIT)


def first_sums_kernel(links_ref, geo_ref, native_ref, f_ref, sums_out, face_ref, cells, faces):
    rows = f_ref.shape[1]
    planes = rows // CHUNKS

    def group(j, _):
        for g in range(SUB):
            f_ref[g, at_rows(j * SUB), :] = native_ref[pl.ds(j * SUB * SUB + g, SUB, stride=SUB), :]
        return 0

    lax.fori_loop(0, rows // SUB, group, 0, unroll=2)
    y = native_polynomial_sums(native_ref, planes)
    packed = pack_sums(finish_polynomials(y, geo_ref[FIRST], planes), 0)
    wall_sums(f_ref, planes, links_ref, geo_ref, face_ref, cells, faces, True)
    sums_out[...] = packed + pack_sums([over_sublanes(face_ref, k) for k in range(2 * FACES)], EMIT)


def spec(space):
    return pl.BlockSpec(memory_space=space)


def array(*shape):
    return jax.ShapeDtypeStruct(shape, F32)


def params(mib=8):
    return pltpu.CompilerParams(vmem_limit_bytes=mib * 1024 * 1024)


def traffic(rows, profiles):
    size = SUB * rows * LANES
    return pl.CostEstimate(flops=8 * profiles * size, bytes_accessed=4 * profiles * size, transcendentals=0)


def local_sums(links, geo, f):
    return pl.pallas_call(
        sums_kernel,
        in_specs=[spec(pltpu.SMEM), spec(pltpu.VMEM), spec(pltpu.VMEM)],
        out_specs=spec(pltpu.VMEM),
        out_shape=array(SUB, LANES),
        scratch_shapes=[
                pltpu.VMEM((10, SUB * SUB, LANES), F32),
            pltpu.VMEM((FACES, SUB * SUB, LANES), F32),
            *face_lists(),
        ],
        compiler_params=params(),
        cost_estimate=traffic(f.shape[1], 4),
        name="local_sums",
    )(links, geo, f)


def first_sums(links, geo, native):
    rows = native.shape[0] // SUB
    return pl.pallas_call(
        first_sums_kernel,
        in_specs=[spec(pltpu.SMEM), spec(pltpu.VMEM), spec(pltpu.VMEM)],
        out_specs=[spec(pltpu.VMEM)] * 2,
        out_shape=[array(SUB, rows, LANES), array(SUB, LANES)],
        scratch_shapes=[
                pltpu.VMEM((2 * FACES, SUB * SUB, LANES), F32),
            *face_lists(),
        ],
        compiler_params=params(),
        cost_estimate=traffic(rows, 5),
        name="first_sums",
    )(links, geo, native)


SPLIT_PARTS = 4


def is_odd():
    return lax.rem(lax.axis_index("space"), 2) == 1


def first_rows_kernel(native_hbm, native_ref, far_any, near_any, far_ref, near_ref, sems, far_sems, near_sems):
    rows = native_ref.shape[0]
    part = rows // SPLIT_PARTS
    copies = [
        pltpu.make_async_copy(
            native_hbm.at[pl.ds(i * part, part)], native_ref.at[pl.ds(i * part, part)], sems.at[i]
        )
        for i in range(SPLIT_PARTS)
    ]
    for c in copies:
        c.start()
    odd = is_odd()
    far = jnp.where(odd, SUB - REACH, 0)
    near = jnp.where(odd, 0, SUB - REACH)
    groups = part // (SUB * SUB)
    out = []

    for i, c in enumerate(copies):
        c.wait()

        def group(j, _):
            for r in range(REACH):
                at = at_rows(j * SUB)
                far_ref[r, at, :] = native_ref[pl.ds(j * SUB * SUB + far + r, SUB, stride=SUB), :]
                near_ref[r, at, :] = native_ref[pl.ds(j * SUB * SUB + near + r, SUB, stride=SUB), :]
            return 0

        lax.fori_loop(i * groups, (i + 1) * groups, group, 0, unroll=unroll(groups, 8))
        at = pl.ds(i * groups * SUB, groups * SUB)
        out.append(pltpu.make_async_copy(far_ref.at[:, at], far_any.at[:, at], far_sems.at[i]))
        out.append(pltpu.make_async_copy(near_ref.at[:, at], near_any.at[:, at], near_sems.at[i]))
        out[-2].start()
        out[-1].start()
    for c in out:
        c.wait()


def first_rows(native):
    rows = native.shape[0] // SUB
    halo = (REACH, rows, LANES)
    return pl.pallas_call(
        first_rows_kernel,
        in_specs=[spec(pltpu.HBM)],
        out_specs=[spec(pltpu.VMEM), spec(pl.ANY), spec(pl.ANY)],
        out_shape=[array(*native.shape), array(*halo), array(*halo)],
        scratch_shapes=[pltpu.VMEM(halo, F32)] * 2 + [pltpu.SemaphoreType.DMA((SPLIT_PARTS,))] * 3,
        compiler_params=params(),
        cost_estimate=traffic(rows, 4),
        name="first_rows",
    )(pltpu.with_memory_space_constraint(native, pltpu.HBM))


def geometry_kernel(links_ref, geo_ref, pairs_ref, cells, faces):
    rows = pairs_ref.shape[1]
    planes = rows // CHUNKS
    first = splat(geo_ref, FIRST, 0)

    def clear(j, _):
        for p in range(pairs_ref.shape[0]):
            pairs_ref[p, at_rows(j * SUB), :] = jnp.zeros((SUB, LANES), F32)
        return 0

    lax.fori_loop(0, rows // SUB, clear, 0, unroll=4)

    def remote(i, _):
        g, k = cells[i], faces[i]
        j = links_ref[k, g]
        edge = g - (SUB - REACH)
        before = g * REACH - g * (g - 1) // 2 + (j + REACH) - g
        after = len(BEFORE_PAIRS) + edge * (edge + 1) // 2 + j - SUB
        at_pair = jnp.where(j < 0, before, after)
        scale = -TIME_STEP / splat(geo_ref, VOL, g)
        v0, v1, v2 = [scale * x for x in face_coefficients(geo_ref, k, g)]
        base = []
        for t in range(TILES):
            xb, xc = tile_nodes(t)
            base.append(v1 * xb + v2 * xc)

        def plane(a, _):
            sa = v0 * (first + a.astype(F32) * H)
            for t in range(TILES):
                at = at_rows((a * TILES + t) * SUB)
                pairs_ref[at_pair, at, :] = pairs_ref[at_pair, at, :] + jnp.maximum(sa + base[t], 0.0)
            return 0

        lax.fori_loop(0, planes, plane, 0, unroll=unroll(planes, 8))
        return 0

    lax.fori_loop(0, list_faces(links_ref, is_remote, cells, faces), remote, 0)


def geometry(links, geo, rows):
    return pl.pallas_call(
        geometry_kernel,
        in_specs=[spec(pltpu.SMEM), spec(pltpu.VMEM)],
        out_specs=spec(pltpu.VMEM),
        out_shape=array(2 * len(BEFORE_PAIRS), rows, LANES),
        scratch_shapes=face_lists(),
        compiler_params=params(),
        cost_estimate=traffic(rows, 4),
        name="geometry",
    )(links, geo)


def gather_sums(tile):
    size = lax.axis_size("vel")
    if size not in (2, 4):
        return [lax.psum(tile, "vel")]
    others = [lax.ppermute(tile, "vel", [(i, i ^ s) for i in range(size)]) for s in range(1, size)]
    return [tile, *others]


def exchanged_sums(tile):
    size = lax.axis_size("vel")
    parts = lax.all_to_all(jnp.broadcast_to(tile, (size, SUB, LANES)), "vel", 0, 0)
    return [parts]


def add_tiles(refs):
    tiles = [r[...] for r in refs] if len(refs[0].shape) == 2 else [refs[0][i] for i in range(refs[0].shape[0])]
    while len(tiles) > 1:
        tiles = [tiles[i] + tiles[i + 1] for i in range(0, len(tiles), 2)]
    return tiles[0]


def quantities(tile):
    m = [WEIGHT * column(tile, p) for p in range(13)]
    n = m[0]
    rn = 1.0 / n
    u = [m[1 + i] * rn for i in range(3)]
    uu = u[0] * u[0] + u[1] * u[1] + u[2] * u[2]
    trace = m[4] + m[5] + m[6]
    width = trace - n * uu
    temperature = width * rn * (1.0 / 3.0)
    second = [[m[4], m[7], m[8]], [m[7], m[5], m[9]], [m[8], m[9], m[6]]]
    q = []
    for i in range(3):
        across = u[0] * second[i][0] + u[1] * second[i][1] + u[2] * second[i][2]
        q.append(0.5 * (m[10 + i] - 2.0 * across - u[i] * trace + 2.0 * uu * m[1 + i]))
    return n, u, temperature, q


def macro_kernel(*refs):
    out_ref = refs[-1]
    n, u, temperature, q = quantities(add_tiles(refs[:-1]))
    lane, sub = lane_iota(), sub_iota()
    for i, x in enumerate((n, *u, temperature, *q)):
        row = jnp.sum(jnp.where(lane == sub, x, 0.0), axis=0, keepdims=True)
        out_ref[pl.ds(i, 1), :] = row[:, :SUB]


def macro(tiles):
    return pl.pallas_call(
        macro_kernel,
        in_specs=[spec(pltpu.VMEM)] * len(tiles),
        out_specs=spec(pltpu.VMEM),
        out_shape=array(8, SUB),
        compiler_params=params(1),
        name="macro",
    )(*tiles)


def flux_kernel(links_ref, geo_ref, f_ref, out_ref, coef, source, face):
    planes = f_ref.shape[1] // CHUNKS
    scale = -TIME_STEP / geo_ref[VOL]
    for i in range(3):
        whole = None
        for k in range(FACES):
            x = scale * geo_ref[FV + FACES * i + k]
            coef[FACES * i + k] = x
            whole = x if whole is None else whole + x
        coef[3 * FACES + i] = whole

    def cell(g, _):
        count = 0
        for k in range(FACES):
            j = links_ref[k, g]
            source[count] = j
            face[count] = k
            count = count + jnp.logical_and(j >= 0, j < SUB).astype(jnp.int32)
        for n in range(FACES + 1):

            @pl.when(count == n)
            def _():
                own_faces(g, n)

        return 0

    def own_faces(g, n):
        at_source = [source[i] for i in range(n)]
        weight = [[splat(coef, FACES * i + face[k], g) for i in range(3)] for k in range(n)]
        whole = [splat(coef, 3 * FACES + i, g) for i in range(3)]
        x0 = splat(geo_ref, FIRST, g)
        base, stay = [], []
        for t in range(TILES):
            xb, xc = tile_nodes(t)
            base.append([w[1] * xb + w[2] * xc for w in weight])
            stay.append(1.0 + whole[1] * xb + whole[2] * xc)

        def plane(a, _):
            xa = x0 + a.astype(F32) * H
            sa = [w[0] * xa for w in weight]
            stay_a = whole[0] * xa
            for t in range(TILES):
                at = at_rows((a * TILES + t) * SUB)
                f = f_ref[g, at, :]
                acc = f * (stay_a + stay[t])
                for k in range(n):
                    acc = acc + jnp.maximum(sa[k] + base[t][k], 0.0) * (f_ref[at_source[k], at, :] - f)
                out_ref[g, at, :] = acc
            return 0

        lax.fori_loop(0, planes, plane, 0, unroll=unroll(planes, 8))

    lax.fori_loop(0, SUB, cell, 0)


def flux(links, geo, f):
    return pl.pallas_call(
        flux_kernel,
        in_specs=[spec(pltpu.SMEM), spec(pltpu.VMEM), spec(pltpu.VMEM)],
        out_specs=spec(pltpu.VMEM),
        out_shape=array(*f.shape),
        scratch_shapes=[
            pltpu.VMEM((3 * FACES + 3, SUB, LANES), F32),
            pltpu.SMEM((FACES + 1,), jnp.int32),
            pltpu.SMEM((FACES + 1,), jnp.int32),
        ],
        compiler_params=params(),
        cost_estimate=traffic(f.shape[1], 7),
        name="flux",
    )(links, geo, f)


def target_kernel(count, links_ref, geo_ref, absorbed_in, *refs):
    sums_refs, (f_ref, part_ref, out_ref, sum_out, ta, coef, cells, faces) = refs[:count], refs[count:]
    planes = f_ref.shape[1] // CHUNKS
    sums = add_tiles(sums_refs)
    sum_out[...] = sums
    absorbed = sums if absorbed_in is None else absorbed_in[...]
    n, u, temperature, q = quantities(sums)
    rt = 1.0 / temperature
    rate = TIME_STEP * n * temperature / (SHEAR * jnp.exp(POWER * jnp.log(temperature)))
    height = rate * n * rt * jnp.sqrt(rt)
    slope = (1.0 / 3.0) / (5.0 * n * temperature * temperature)
    coef[0] = rate
    coef[1] = rt
    coef[2], coef[3] = u[1], u[2]
    coef[4], coef[5] = slope * q[1], slope * q[2]
    for k in range(FACES):
        wall = geo_ref[WALL + k] > 0.5
        coef[6 + k] = column(sums, EMIT + k) / jnp.where(wall, column(absorbed, ABSORB + k), 1.0)
    first = geo_ref[FIRST]

    def plane_table(a, _):
        ca = first + a.astype(F32) * H - u[0]
        za = ca * ca * rt
        ta[0, a] = height * jnp.exp(-0.5 * za)
        ta[1, a] = slope * q[0] * ca
        ta[2, a] = za - 5.0
        return 0

    lax.fori_loop(0, planes, plane_table, 0, unroll=4)

    def cell(g, _):
        rate_g, rtg = splat(coef, 0, g), splat(coef, 1, g)
        ub, uc = splat(coef, 2, g), splat(coef, 3, g)
        qb, qc = splat(coef, 4, g), splat(coef, 5, g)
        bell, heat, zz = [], [], []
        for t in range(TILES):
            xb, xc = tile_nodes(t)
            cb, cc = xb - ub, xc - uc
            z = (cb * cb + cc * cc) * rtg
            bell.append(jnp.exp(-0.5 * z))
            heat.append(cb * qb + cc * qc)
            zz.append(z)

        def plane(a, _):
            height_a, heat_a, z_a = [
                jnp.broadcast_to(ta[i, a, pl.ds(g, 1), :], (SUB, LANES)) for i in range(3)
            ]
            for t in range(TILES):
                where = (g, at_rows((a * TILES + t) * SUB), slice(None))
                f = f_ref[where]
                target = (height_a * bell[t]) * (1.0 + (heat_a + heat[t]) * (z_a + zz[t]))
                out_ref[where] = (part_ref[where] - rate_g * f) + target
            return 0

        lax.fori_loop(0, planes, plane, 0, unroll=unroll(planes, 16))
        return 0

    lax.fori_loop(0, SUB, cell, 0)

    def wall(i, _):
        g, k = cells[i], faces[i]
        x0 = splat(geo_ref, FIRST, g)
        wt = splat(geo_ref, WT, g)
        ratio = splat(coef, 6 + k, g)
        shape = [ratio * x for x in wall_tiles(wt)]
        scale = -TIME_STEP / splat(geo_ref, VOL, g)
        v0, v1, v2 = [scale * x for x in face_coefficients(geo_ref, k, g)]
        base = []
        for t in range(TILES):
            xb, xc = tile_nodes(t)
            base.append(v1 * xb + v2 * xc)

        def plane(a, _):
            xa = x0 + a.astype(F32) * H
            wa = jnp.exp(-0.5 * xa * xa / wt)
            sa = v0 * xa
            for t in range(TILES):
                where = (g, at_rows((a * TILES + t) * SUB), slice(None))
                f = f_ref[where]
                out_ref[where] = out_ref[where] + jnp.maximum(sa + base[t], 0.0) * (wa * shape[t] - f)
            return 0

        lax.fori_loop(0, planes, plane, 0, unroll=unroll(planes, 8))
        return 0

    lax.fori_loop(0, list_faces(links_ref, is_wall, cells, faces), wall, 0)


def add_target(links, geo, absorbed, tiles, f, part):
    rows = f.shape[1]
    vmem = spec(pltpu.VMEM)
    given = [links, geo] + ([] if absorbed is None else [absorbed]) + list(tiles) + [f, part]

    def kernel(links_ref, geo_in, *refs):
        if absorbed is None:
            target_kernel(len(tiles), links_ref, geo_in, None, *refs)
        else:
            target_kernel(len(tiles), links_ref, geo_in, *refs)

    return pl.pallas_call(
        kernel,
        in_specs=[spec(pltpu.SMEM)] + [vmem] * (len(given) - 1),
        out_specs=[vmem] * 2,
        out_shape=[array(*part.shape), array(SUB, LANES)],
        input_output_aliases={len(given) - 1: 0},
        scratch_shapes=[
                pltpu.VMEM((3, rows // CHUNKS, SUB, LANES), F32),
            pltpu.VMEM((6 + FACES, SUB, LANES), F32),
            *face_lists(),
        ],
        compiler_params=params(),
        cost_estimate=traffic(rows, 7),
        name="add_target",
    )(*given)


def halo_terms(pairs_ref, before_ref, after_ref, f_ref, at):
    low, high = [None] * REACH, [None] * REACH
    rows = [before_ref[r, at, :] for r in range(REACH)]
    own = [f_ref[g, at, :] for g in range(REACH)]
    for p, (g, r) in enumerate(BEFORE_PAIRS):
        term = pairs_ref[p, at, :] * (rows[r] - own[g])
        low[g] = term if low[g] is None else low[g] + term
    rows = [after_ref[r, at, :] for r in range(REACH)]
    own = [f_ref[SUB - REACH + e, at, :] for e in range(REACH)]
    p = len(BEFORE_PAIRS)
    for e in range(REACH):
        for r in range(e + 1):
            term = pairs_ref[p, at, :] * (rows[r] - own[e])
            high[e] = term if high[e] is None else high[e] + term
            p += 1
    return low, high


def by_side(far_ref, near_ref, run):
    odd = is_odd()

    @pl.when(odd)
    def _():
        run(near_ref, far_ref)

    @pl.when(jnp.logical_not(odd))
    def _():
        run(far_ref, near_ref)


def edge_kernel(pairs_ref, far_in, near_in, old_ref, part_ref, f_ref, far_out, near_out):
    def run(before_ref, after_ref):
        down_out, up_out = (near_out, far_out) if after_ref is far_in else (far_out, near_out)

        def group(j, _):
            at = at_rows(j * SUB)
            low, high = halo_terms(pairs_ref, before_ref, after_ref, old_ref, at)
            for g in range(REACH):
                x = part_ref[g, at, :] + low[g]
                down_out[g, at, :] = x
                f_ref[g, at, :] = x
                e = SUB - REACH + g
                x = part_ref[e, at, :] + high[g]
                up_out[g, at, :] = x
                f_ref[e, at, :] = x
            return 0

        lax.fori_loop(0, part_ref.shape[1] // SUB, group, 0, unroll=4)

    by_side(far_in, near_in, run)


def edge(pairs, far, near, old, part):
    rows = part.shape[1]
    return pl.pallas_call(
        edge_kernel,
        in_specs=[spec(pltpu.VMEM)] * 5,
        out_specs=[spec(pltpu.VMEM)] * 3,
        out_shape=[array(SUB, rows, LANES), array(REACH, rows, LANES), array(REACH, rows, LANES)],
        input_output_aliases={4: 0},
        compiler_params=params(),
        cost_estimate=traffic(rows, 4),
        name="edge",
    )(pairs, far, near, old, part)


def last_edge_kernel(
    geo_ref, pairs_ref, far_ref, near_ref, f_ref, part_ref, out_hbm, sums_out, native_ref, sems
):
    rows = part_ref.shape[1]
    planes = rows // CHUNKS
    part = rows // SUB // LAST_PARTS

    def copy(i):
        at = pl.ds(i * part * SUB * SUB, part * SUB * SUB)
        return pltpu.make_async_copy(native_ref.at[at], out_hbm.at[at], sems.at[i])

    def run(before_ref, after_ref):
        for i in range(LAST_PARTS):

            def group(j, _):
                at = at_rows(j * SUB)
                low, high = halo_terms(pairs_ref, before_ref, after_ref, f_ref, at)
                terms = low + [None] * (SUB - 2 * REACH) + high
                for g in range(SUB):
                    x = part_ref[g, at, :]
                    where = (pl.ds(j * SUB * SUB + g, SUB, stride=SUB), slice(None))
                    native_ref[where] = x if terms[g] is None else x + terms[g]
                return 0

            lax.fori_loop(i * part, (i + 1) * part, group, 0, unroll=2)
            copy(i).start()

    by_side(far_ref, near_ref, run)
    y = native_polynomial_sums(native_ref, planes)
    sums_out[...] = pack_sums(finish_polynomials(y, geo_ref[FIRST], planes), 0)
    for i in range(LAST_PARTS):
        copy(i).wait()


LAST_PARTS = 4


def last_edge(geo, pairs, far, near, f, part):
    native = (SUB * part.shape[1], LANES)
    return pl.pallas_call(
        last_edge_kernel,
        in_specs=[spec(pltpu.VMEM)] * 6,
        out_specs=[spec(pltpu.HBM), spec(pltpu.VMEM)],
        out_shape=[array(*native), array(SUB, LANES)],
        scratch_shapes=[pltpu.VMEM(native, F32), pltpu.SemaphoreType.DMA((LAST_PARTS,))],
        compiler_params=params(),
        cost_estimate=traffic(part.shape[1], 4),
        name="last_edge",
    )(geo, pairs, far, near, f, part)


def exchange(far, near):
    size = lax.axis_size("space")
    out = []
    for x, start in ((far, 1), (near, 0)):
        pairs = [(i, i + 1) for i in range(start, size - 1, 2)]
        out.append(lax.ppermute(x, "space", pairs + [(j, i) for i, j in pairs]))
    return out


def per_device(particle_profile, neighbors, face_vectors, volumes, wall_temp):
    cells, points = particle_profile.shape
    rows = points // LANES
    plane_count = NV // lax.axis_size("vel")
    native = particle_profile.reshape(cells, rows, LANES).transpose(1, 0, 2).reshape(cells * rows, LANES)
    wall = neighbors < 0
    links = jnp.where(wall, WALL_LINK, neighbors - lax.axis_index("space") * cells)
    own = (links >= 0) & (links < cells)
    first = -SPEED_LIMIT + ((lax.axis_index("vel") * plane_count).astype(F32) + 0.5) * H
    geo = jnp.concatenate(
        [
            face_vectors.reshape(3 * FACES, cells),
            volumes[None],
            wall_temp[None],
            wall.astype(F32),
            own.astype(F32),
            jnp.full((1, cells), first, F32),
        ]
    )
    geo = jnp.broadcast_to(geo[:, :, None], (GEO, cells, LANES))
    native, far, near = first_rows(native)
    far, near = exchange(far, near)
    f, sums = first_sums(links, geo, native)
    tiles = gather_sums(sums)
    pairs = geometry(links, geo, rows)
    part = flux(links, geo, f)
    part, absorbed = add_target(links, geo, None, tiles, f, part)
    f, far, near = edge(pairs, far, near, f, part)
    far, near = exchange(far, near)
    tiles = gather_sums(local_sums(links, geo, f))
    part = flux(links, geo, f)
    part, _ = add_target(links, geo, absorbed, tiles, f, part)
    native, sums = last_edge(geo, pairs, far, near, f, part)
    macro_quantities = macro(exchanged_sums(sums))
    evolved = native.reshape(rows, cells, LANES).transpose(1, 0, 2).reshape(cells, points)
    return evolved, macro_quantities


def solution(mesh):
    return jax.shard_map(
        per_device,
        mesh=mesh,
        in_specs=(
            P("space", "vel"),
            P(None, "space"),
            P(None, None, "space"),
            P("space"),
            P("space"),
        ),
        out_specs=(P("space", "vel"), P(None, "space")),
        check_vma=False,
    )
```

```python
import functools
import math

import jax
import jax.numpy as jnp
from jax import lax
from jax.experimental import pallas as pl
from jax.experimental.pallas import tpu as pltpu
from jax.sharding import PartitionSpec as P

NV = 64
FACES = 6
REACH = 3
STEPS = 2
LANES = 128
SUB = 8

TIME_STEP = 0.015
SHEAR = 0.1
POWER = 0.81
SPEED_LIMIT = 6.0
H = 2.0 * SPEED_LIMIT / NV
WEIGHT = H**3 * (2.0 * math.pi) ** (-1.5)

CHUNKS = NV * NV // LANES
TILES = CHUNKS // SUB

FV, VOL, WT, WALL, LOCAL, FIRST = 0, 18, 19, 20, 26, 32
GEO = 33
WALL_LINK = -64
BEFORE_PAIRS = tuple((g, r) for g in range(REACH) for r in range(g, REACH))
EMIT, ABSORB = 13, 19
SUMS = 25

F32 = jnp.float32


def lane_iota():
    return lax.broadcasted_iota(jnp.int32, (SUB, LANES), 1)


def sub_iota():
    return lax.broadcasted_iota(jnp.int32, (SUB, LANES), 0)


def half_of(lane):
    return (lane >= NV).astype(F32)


def third_component(lane):
    c = jnp.where(lane >= NV, lane - NV, lane).astype(F32)
    return -SPEED_LIMIT + (c + 0.5) * H


def tile_nodes(t):
    lane = lane_iota()
    b = (2 * SUB * t + 2 * sub_iota()).astype(F32) + half_of(lane)
    return -SPEED_LIMIT + (b + 0.5) * H, third_component(lane)


def column(tile, p):
    return jnp.broadcast_to(tile[:, p : p + 1], (SUB, LANES))


def splat(ref, i, g):
    return jnp.broadcast_to(ref[i, pl.ds(g, 1), :], (SUB, LANES))


def total(tile):
    return jnp.broadcast_to(jnp.sum(tile, axis=1, keepdims=True), (SUB, LANES))


def face_coefficients(geo_ref, k, g):
    return [splat(geo_ref, FV + FACES * i + k, g) for i in range(3)]


def at_rows(start, size=SUB):
    return pl.ds(pl.multiple_of(start, SUB), size)


def wall_tiles(wall_temp):
    rt = 1.0 / wall_temp
    scale = rt * jnp.sqrt(rt)
    out = []
    for t in range(TILES):
        xb, xc = tile_nodes(t)
        out.append(scale * jnp.exp(-0.5 * (xb * xb + xc * xc) * rt))
    return out


def pack_sums(arrays, start):
    lane = lane_iota()
    out = jnp.zeros((SUB, LANES), F32)
    for p, x in enumerate(arrays):
        out = jnp.where(lane == start + p, total(x), out)
    return out


def over_sublanes(ref, k):
    out = ref[k, pl.ds(0, SUB, stride=SUB), :]
    for s in range(1, SUB):
        out = out + ref[k, pl.ds(s, SUB, stride=SUB), :]
    return out


def list_faces(links_ref, wanted, cell_ref, face_ref):
    def cell(g, count):
        for k in range(FACES):
            cell_ref[count] = g
            face_ref[count] = k
            count = count + wanted(links_ref[k, g]).astype(jnp.int32)
        return count

    return lax.fori_loop(0, SUB, cell, 0)


def is_wall(j):
    return j == WALL_LINK


def is_remote(j):
    return jnp.logical_or(j >= SUB, jnp.logical_and(j < 0, j != WALL_LINK))


def face_lists():
    return [pltpu.SMEM((FACES * SUB + 1,), jnp.int32)] * 2


def unroll(planes, most):
    return math.gcd(planes, most)


def finish_polynomials(y, first, planes):
    y0, y1, y2, y3, by0, by1, by2, bby0, bby1, bbby0 = y
    m = first + 0.5 * (planes - 1) * H
    c = third_component(lane_iota())
    cc = c * c
    a = y1 + m * y0
    aa = y2 + m * (2.0 * y1 + m * y0)
    aaa = y3 + m * (3.0 * y2 + m * (3.0 * y1 + m * y0))
    ab = by1 + m * by0
    aab = by2 + m * (2.0 * by1 + m * by0)
    abb = bby1 + m * bby0
    return (
        y0,
        a,
        by0,
        c * y0,
        aa,
        bby0,
        cc * y0,
        ab,
        c * a,
        c * by0,
        aaa + abb + cc * a,
        aab + bbby0 + cc * by0,
        c * (aa + bby0 + cc * y0),
    )


def polynomial_sums(f_ref, planes, parts_ref):
    half = planes // 2

    def cell(g, _):
        out = [None] * 10
        for t in range(TILES):
            y0 = y1 = y2 = y3 = None
            for i in range(half):
                d = (i + 0.5) * H
                hi = f_ref[g, pl.ds(((half + i) * TILES + t) * SUB, SUB), :]
                lo = f_ref[g, pl.ds(((half - 1 - i) * TILES + t) * SUB, SUB), :]
                s, r = hi + lo, hi - lo
                if i == 0:
                    y0, y1, y2, y3 = s, d * r, (d * d) * s, (d * d * d) * r
                else:
                    y0, y1, y2, y3 = y0 + s, y1 + d * r, y2 + (d * d) * s, y3 + (d * d * d) * r
            b, _c = tile_nodes(t)
            bb = b * b
            terms = (y0, y1, y2, y3, b * y0, b * y1, b * y2, bb * y0, bb * y1, bb * (b * y0))
            out = [x if o is None else o + x for o, x in zip(out, terms)]
        for p in range(10):
            parts_ref[p, at_rows(g * SUB), :] = out[p]
        return 0

    lax.fori_loop(0, SUB, cell, 0)
    return [over_sublanes(parts_ref, p) for p in range(10)]


def native_polynomial_sums(native_ref, planes):
    half, side = planes // 2, CHUNKS // 2
    zero = jnp.zeros((SUB, LANES), F32)
    acc = [zero] * 10

    def plane(a, acc):
        xa = (a.astype(F32) - 0.5 * (planes - 1)) * H
        b0 = b1 = b2 = b3 = None
        for i in range(side):
            y = (2 * i + 1) * H
            hi = native_ref[at_rows((a * CHUNKS + side + i) * SUB), :]
            lo = native_ref[at_rows((a * CHUNKS + side - 1 - i) * SUB), :]
            s, d = hi + lo, hi - lo
            terms = (s, y * d, (y * y) * s, (y * y * y) * d)
            if i == 0:
                b0, b1, b2, b3 = terms
            else:
                b0, b1, b2, b3 = b0 + terms[0], b1 + terms[1], b2 + terms[2], b3 + terms[3]
        a0, a1, a2 = xa * b0, xa * b1, xa * b2
        aa0 = xa * a0
        new = (b0, a0, aa0, xa * aa0, b1, a1, xa * a1, b2, a2, b3)
        return tuple(x + z for x, z in zip(acc, new))

    g0, a0, aa0, aaa0, g1, a1, aa1, g2, a2, g3 = lax.fori_loop(0, planes, plane, tuple(acc))
    e = (half_of(lane_iota()) - 0.5) * H
    return [
        g0,
        a0,
        aa0,
        aaa0,
        g1 + e * g0,
        a1 + e * a0,
        aa1 + e * aa0,
        g2 + e * (2.0 * g1 + e * g0),
        a2 + e * (2.0 * a1 + e * a0),
        g3 + e * (3.0 * g2 + e * (3.0 * g1 + e * g0)),
    ]


def wall_sums(f_ref, planes, links_ref, geo_ref, sums_ref, cells, faces, with_absorbed):
    sums_ref[...] = jnp.zeros_like(sums_ref)

    def wall(i, _):
        g, k = cells[i], faces[i]
        v0, v1, v2 = face_coefficients(geo_ref, k, g)
        first = splat(geo_ref, FIRST, g)
        base = []
        for t in range(TILES):
            xb, xc = tile_nodes(t)
            base.append(v1 * xb + v2 * xc)
        if with_absorbed:
            wt = splat(geo_ref, WT, g)
            shape = wall_tiles(wt)

        def plane(a, acc):
            out, back = list(acc[0]), list(acc[1])
            xa = first + a.astype(F32) * H
            sa = v0 * xa
            if with_absorbed:
                wa = jnp.exp(-0.5 * xa * xa / wt)
            for t in range(TILES):
                s = sa + base[t]
                f = f_ref[g, at_rows((a * TILES + t) * SUB), :]
                out[t] = out[t] + jnp.maximum(s, 0.0) * f
                if with_absorbed:
                    back[t] = back[t] + jnp.maximum(-s, 0.0) * (wa * shape[t])
            return tuple(out), tuple(back)

        zeros = (jnp.zeros((SUB, LANES), F32),) * TILES
        out, back = lax.fori_loop(0, planes, plane, (zeros, zeros), unroll=unroll(planes, 16))
        at = at_rows(g * SUB)
        sums_ref[k, at, :] = (out[0] + out[1]) + (out[2] + out[3])
        if with_absorbed:
            sums_ref[FACES + k, at, :] = (back[0] + back[1]) + (back[2] + back[3])
        return 0

    lax.fori_loop(0, list_faces(links_ref, is_wall, cells, faces), wall, 0)


def sums_kernel(links_ref, geo_ref, f_ref, sums_out, parts_ref, face_ref, cells, faces):
    planes = f_ref.shape[1] // CHUNKS
    y = polynomial_sums(f_ref, planes, parts_ref)
    packed = pack_sums(finish_polynomials(y, geo_ref[FIRST], planes), 0)
    wall_sums(f_ref, planes, links_ref, geo_ref, face_ref, cells, faces, False)
    sums_out[...] = packed + pack_sums([over_sublanes(face_ref, k) for k in range(FACES)], EMIT)


def first_sums_kernel(links_ref, geo_ref, native_ref, f_ref, sums_out, face_ref, cells, faces):
    rows = f_ref.shape[1]
    planes = rows // CHUNKS

    def group(j, _):
        for g in range(SUB):
            f_ref[g, at_rows(j * SUB), :] = native_ref[pl.ds(j * SUB * SUB + g, SUB, stride=SUB), :]
        return 0

    lax.fori_loop(0, rows // SUB, group, 0, unroll=2)
    y = native_polynomial_sums(native_ref, planes)
    packed = pack_sums(finish_polynomials(y, geo_ref[FIRST], planes), 0)
    wall_sums(f_ref, planes, links_ref, geo_ref, face_ref, cells, faces, True)
    sums_out[...] = packed + pack_sums([over_sublanes(face_ref, k) for k in range(2 * FACES)], EMIT)


def spec(space):
    return pl.BlockSpec(memory_space=space)


def array(*shape):
    return jax.ShapeDtypeStruct(shape, F32)


def params(mib=8):
    return pltpu.CompilerParams(vmem_limit_bytes=mib * 1024 * 1024)


def traffic(rows, profiles):
    size = SUB * rows * LANES
    return pl.CostEstimate(flops=8 * profiles * size, bytes_accessed=4 * profiles * size, transcendentals=0)


def local_sums(links, geo, f):
    return pl.pallas_call(
        sums_kernel,
        in_specs=[spec(pltpu.SMEM), spec(pltpu.VMEM), spec(pltpu.VMEM)],
        out_specs=spec(pltpu.VMEM),
        out_shape=array(SUB, LANES),
        scratch_shapes=[
                pltpu.VMEM((10, SUB * SUB, LANES), F32),
            pltpu.VMEM((FACES, SUB * SUB, LANES), F32),
            *face_lists(),
        ],
        compiler_params=params(),
        cost_estimate=traffic(f.shape[1], 4),
        name="local_sums",
    )(links, geo, f)


def first_sums(links, geo, native):
    rows = native.shape[0] // SUB
    return pl.pallas_call(
        first_sums_kernel,
        in_specs=[spec(pltpu.SMEM), spec(pltpu.VMEM), spec(pltpu.VMEM)],
        out_specs=[spec(pltpu.VMEM)] * 2,
        out_shape=[array(SUB, rows, LANES), array(SUB, LANES)],
        scratch_shapes=[
                pltpu.VMEM((2 * FACES, SUB * SUB, LANES), F32),
            *face_lists(),
        ],
        compiler_params=params(),
        cost_estimate=traffic(rows, 5),
        name="first_sums",
    )(links, geo, native)


SPLIT_PARTS = 4


def is_odd():
    return lax.rem(lax.axis_index("space"), 2) == 1


def first_rows_kernel(native_hbm, native_ref, far_any, near_any, far_ref, near_ref, sems, far_sems, near_sems):
    rows = native_ref.shape[0]
    part = rows // SPLIT_PARTS
    copies = [
        pltpu.make_async_copy(
            native_hbm.at[pl.ds(i * part, part)], native_ref.at[pl.ds(i * part, part)], sems.at[i]
        )
        for i in range(SPLIT_PARTS)
    ]
    for c in copies:
        c.start()
    odd = is_odd()
    far = jnp.where(odd, SUB - REACH, 0)
    near = jnp.where(odd, 0, SUB - REACH)
    groups = part // (SUB * SUB)
    out = []

    for i, c in enumerate(copies):
        c.wait()

        def group(j, _):
            for r in range(REACH):
                at = at_rows(j * SUB)
                far_ref[r, at, :] = native_ref[pl.ds(j * SUB * SUB + far + r, SUB, stride=SUB), :]
                near_ref[r, at, :] = native_ref[pl.ds(j * SUB * SUB + near + r, SUB, stride=SUB), :]
            return 0

        lax.fori_loop(i * groups, (i + 1) * groups, group, 0, unroll=unroll(groups, 8))
        at = pl.ds(i * groups * SUB, groups * SUB)
        out.append(pltpu.make_async_copy(far_ref.at[:, at], far_any.at[:, at], far_sems.at[i]))
        out.append(pltpu.make_async_copy(near_ref.at[:, at], near_any.at[:, at], near_sems.at[i]))
        out[-2].start()
        out[-1].start()
    for c in out:
        c.wait()


def first_rows(native):
    rows = native.shape[0] // SUB
    halo = (REACH, rows, LANES)
    return pl.pallas_call(
        first_rows_kernel,
        in_specs=[spec(pltpu.HBM)],
        out_specs=[spec(pltpu.VMEM), spec(pl.ANY), spec(pl.ANY)],
        out_shape=[array(*native.shape), array(*halo), array(*halo)],
        scratch_shapes=[pltpu.VMEM(halo, F32)] * 2 + [pltpu.SemaphoreType.DMA((SPLIT_PARTS,))] * 3,
        compiler_params=params(),
        cost_estimate=traffic(rows, 4),
        name="first_rows",
    )(pltpu.with_memory_space_constraint(native, pltpu.HBM))


def geometry_kernel(links_ref, geo_ref, pairs_ref, cells, faces):
    rows = pairs_ref.shape[1]
    planes = rows // CHUNKS
    first = splat(geo_ref, FIRST, 0)

    def clear(j, _):
        for p in range(pairs_ref.shape[0]):
            pairs_ref[p, at_rows(j * SUB), :] = jnp.zeros((SUB, LANES), F32)
        return 0

    lax.fori_loop(0, rows // SUB, clear, 0, unroll=4)

    def remote(i, _):
        g, k = cells[i], faces[i]
        j = links_ref[k, g]
        edge = g - (SUB - REACH)
        before = g * REACH - g * (g - 1) // 2 + (j + REACH) - g
        after = len(BEFORE_PAIRS) + edge * (edge + 1) // 2 + j - SUB
        at_pair = jnp.where(j < 0, before, after)
        scale = -TIME_STEP / splat(geo_ref, VOL, g)
        v0, v1, v2 = [scale * x for x in face_coefficients(geo_ref, k, g)]
        base = []
        for t in range(TILES):
            xb, xc = tile_nodes(t)
            base.append(v1 * xb + v2 * xc)

        def plane(a, _):
            sa = v0 * (first + a.astype(F32) * H)
            for t in range(TILES):
                at = at_rows((a * TILES + t) * SUB)
                pairs_ref[at_pair, at, :] = pairs_ref[at_pair, at, :] + jnp.maximum(sa + base[t], 0.0)
            return 0

        lax.fori_loop(0, planes, plane, 0, unroll=unroll(planes, 8))
        return 0

    lax.fori_loop(0, list_faces(links_ref, is_remote, cells, faces), remote, 0)


def geometry(links, geo, rows):
    return pl.pallas_call(
        geometry_kernel,
        in_specs=[spec(pltpu.SMEM), spec(pltpu.VMEM)],
        out_specs=spec(pltpu.VMEM),
        out_shape=array(2 * len(BEFORE_PAIRS), rows, LANES),
        scratch_shapes=face_lists(),
        compiler_params=params(),
        cost_estimate=traffic(rows, 4),
        name="geometry",
    )(links, geo)


def gather_sums(tile):
    size = lax.axis_size("vel")
    if size not in (2, 4):
        return [lax.psum(tile, "vel")]
    others = [lax.ppermute(tile, "vel", [(i, i ^ s) for i in range(size)]) for s in range(1, size)]
    return [tile, *others]


def doubling_sums(tile):
    size = lax.axis_size("vel")
    if size != 4:
        return gather_sums(tile)
    pair = tile + lax.ppermute(tile, "vel", [(i, i ^ 1) for i in range(size)])
    return [pair, lax.ppermute(pair, "vel", [(i, i ^ 2) for i in range(size)])]


def add_tiles(refs):
    tiles = [r[...] for r in refs]
    while len(tiles) > 1:
        tiles = [tiles[i] + tiles[i + 1] for i in range(0, len(tiles), 2)]
    return tiles[0]


def quantities(tile):
    m = [WEIGHT * column(tile, p) for p in range(13)]
    n = m[0]
    rn = 1.0 / n
    u = [m[1 + i] * rn for i in range(3)]
    uu = u[0] * u[0] + u[1] * u[1] + u[2] * u[2]
    trace = m[4] + m[5] + m[6]
    width = trace - n * uu
    temperature = width * rn * (1.0 / 3.0)
    second = [[m[4], m[7], m[8]], [m[7], m[5], m[9]], [m[8], m[9], m[6]]]
    q = []
    for i in range(3):
        across = u[0] * second[i][0] + u[1] * second[i][1] + u[2] * second[i][2]
        q.append(0.5 * (m[10 + i] - 2.0 * across - u[i] * trace + 2.0 * uu * m[1 + i]))
    return n, u, temperature, q


def macro_kernel(*refs):
    out_ref = refs[-1]
    n, u, temperature, q = quantities(add_tiles(refs[:-1]))
    lane, sub = lane_iota(), sub_iota()
    for i, x in enumerate((n, *u, temperature, *q)):
        row = jnp.sum(jnp.where(lane == sub, x, 0.0), axis=0, keepdims=True)
        out_ref[pl.ds(i, 1), :] = row[:, :SUB]


def macro(tiles):
    return pl.pallas_call(
        macro_kernel,
        in_specs=[spec(pltpu.VMEM)] * len(tiles),
        out_specs=spec(pltpu.VMEM),
        out_shape=array(8, SUB),
        compiler_params=params(1),
        name="macro",
    )(*tiles)


def flux_kernel(links_ref, geo_ref, f_ref, out_ref, coef, source, face):
    planes = f_ref.shape[1] // CHUNKS
    scale = -TIME_STEP / geo_ref[VOL]
    for i in range(3):
        whole = None
        for k in range(FACES):
            x = scale * geo_ref[FV + FACES * i + k]
            coef[FACES * i + k] = x
            whole = x if whole is None else whole + x
        coef[3 * FACES + i] = whole

    def cell(g, _):
        count = 0
        for k in range(FACES):
            j = links_ref[k, g]
            source[count] = j
            face[count] = k
            count = count + jnp.logical_and(j >= 0, j < SUB).astype(jnp.int32)
        for n in range(FACES + 1):

            @pl.when(count == n)
            def _():
                own_faces(g, n)

        return 0

    def own_faces(g, n):
        at_source = [source[i] for i in range(n)]
        weight = [[splat(coef, FACES * i + face[k], g) for i in range(3)] for k in range(n)]
        whole = [splat(coef, 3 * FACES + i, g) for i in range(3)]
        x0 = splat(geo_ref, FIRST, g)
        base, stay = [], []
        for t in range(TILES):
            xb, xc = tile_nodes(t)
            base.append([w[1] * xb + w[2] * xc for w in weight])
            stay.append(1.0 + whole[1] * xb + whole[2] * xc)

        def plane(a, _):
            xa = x0 + a.astype(F32) * H
            sa = [w[0] * xa for w in weight]
            stay_a = whole[0] * xa
            for t in range(TILES):
                at = at_rows((a * TILES + t) * SUB)
                f = f_ref[g, at, :]
                acc = f * (stay_a + stay[t])
                for k in range(n):
                    acc = acc + jnp.maximum(sa[k] + base[t][k], 0.0) * (f_ref[at_source[k], at, :] - f)
                out_ref[g, at, :] = acc
            return 0

        lax.fori_loop(0, planes, plane, 0, unroll=unroll(planes, 8))

    lax.fori_loop(0, SUB, cell, 0)


def flux(links, geo, f):
    return pl.pallas_call(
        flux_kernel,
        in_specs=[spec(pltpu.SMEM), spec(pltpu.VMEM), spec(pltpu.VMEM)],
        out_specs=spec(pltpu.VMEM),
        out_shape=array(*f.shape),
        scratch_shapes=[
            pltpu.VMEM((3 * FACES + 3, SUB, LANES), F32),
            pltpu.SMEM((FACES + 1,), jnp.int32),
            pltpu.SMEM((FACES + 1,), jnp.int32),
        ],
        compiler_params=params(),
        cost_estimate=traffic(f.shape[1], 7),
        name="flux",
    )(links, geo, f)


def target_kernel(count, links_ref, geo_ref, absorbed_in, *refs):
    sums_refs, (f_ref, part_ref, out_ref, sum_out, ta, coef, cells, faces) = refs[:count], refs[count:]
    planes = f_ref.shape[1] // CHUNKS
    sums = add_tiles(sums_refs)
    sum_out[...] = sums
    absorbed = sums if absorbed_in is None else absorbed_in[...]
    n, u, temperature, q = quantities(sums)
    rt = 1.0 / temperature
    rate = TIME_STEP * n * temperature / (SHEAR * jnp.exp(POWER * jnp.log(temperature)))
    height = rate * n * rt * jnp.sqrt(rt)
    slope = (1.0 / 3.0) / (5.0 * n * temperature * temperature)
    coef[0] = rate
    coef[1] = rt
    coef[2], coef[3] = u[1], u[2]
    coef[4], coef[5] = slope * q[1], slope * q[2]
    for k in range(FACES):
        wall = geo_ref[WALL + k] > 0.5
        coef[6 + k] = column(sums, EMIT + k) / jnp.where(wall, column(absorbed, ABSORB + k), 1.0)
    first = geo_ref[FIRST]

    def plane_table(a, _):
        ca = first + a.astype(F32) * H - u[0]
        za = ca * ca * rt
        ta[0, a] = height * jnp.exp(-0.5 * za)
        ta[1, a] = slope * q[0] * ca
        ta[2, a] = za - 5.0
        return 0

    lax.fori_loop(0, planes, plane_table, 0, unroll=4)

    def cell(g, _):
        rate_g, rtg = splat(coef, 0, g), splat(coef, 1, g)
        ub, uc = splat(coef, 2, g), splat(coef, 3, g)
        qb, qc = splat(coef, 4, g), splat(coef, 5, g)
        bell, heat, zz = [], [], []
        for t in range(TILES):
            xb, xc = tile_nodes(t)
            cb, cc = xb - ub, xc - uc
            z = (cb * cb + cc * cc) * rtg
            bell.append(jnp.exp(-0.5 * z))
            heat.append(cb * qb + cc * qc)
            zz.append(z)

        def plane(a, _):
            height_a, heat_a, z_a = [
                jnp.broadcast_to(ta[i, a, pl.ds(g, 1), :], (SUB, LANES)) for i in range(3)
            ]
            for t in range(TILES):
                where = (g, at_rows((a * TILES + t) * SUB), slice(None))
                f = f_ref[where]
                target = (height_a * bell[t]) * (1.0 + (heat_a + heat[t]) * (z_a + zz[t]))
                out_ref[where] = (part_ref[where] - rate_g * f) + target
            return 0

        lax.fori_loop(0, planes, plane, 0, unroll=unroll(planes, 16))
        return 0

    lax.fori_loop(0, SUB, cell, 0)

    def wall(i, _):
        g, k = cells[i], faces[i]
        x0 = splat(geo_ref, FIRST, g)
        wt = splat(geo_ref, WT, g)
        ratio = splat(coef, 6 + k, g)
        shape = [ratio * x for x in wall_tiles(wt)]
        scale = -TIME_STEP / splat(geo_ref, VOL, g)
        v0, v1, v2 = [scale * x for x in face_coefficients(geo_ref, k, g)]
        base = []
        for t in range(TILES):
            xb, xc = tile_nodes(t)
            base.append(v1 * xb + v2 * xc)

        def plane(a, _):
            xa = x0 + a.astype(F32) * H
            wa = jnp.exp(-0.5 * xa * xa / wt)
            sa = v0 * xa
            for t in range(TILES):
                where = (g, at_rows((a * TILES + t) * SUB), slice(None))
                f = f_ref[where]
                out_ref[where] = out_ref[where] + jnp.maximum(sa + base[t], 0.0) * (wa * shape[t] - f)
            return 0

        lax.fori_loop(0, planes, plane, 0, unroll=unroll(planes, 8))
        return 0

    lax.fori_loop(0, list_faces(links_ref, is_wall, cells, faces), wall, 0)


def add_target(links, geo, absorbed, tiles, f, part):
    rows = f.shape[1]
    vmem = spec(pltpu.VMEM)
    given = [links, geo] + ([] if absorbed is None else [absorbed]) + list(tiles) + [f, part]

    def kernel(links_ref, geo_in, *refs):
        if absorbed is None:
            target_kernel(len(tiles), links_ref, geo_in, None, *refs)
        else:
            target_kernel(len(tiles), links_ref, geo_in, *refs)

    return pl.pallas_call(
        kernel,
        in_specs=[spec(pltpu.SMEM)] + [vmem] * (len(given) - 1),
        out_specs=[vmem] * 2,
        out_shape=[array(*part.shape), array(SUB, LANES)],
        input_output_aliases={len(given) - 1: 0},
        scratch_shapes=[
                pltpu.VMEM((3, rows // CHUNKS, SUB, LANES), F32),
            pltpu.VMEM((6 + FACES, SUB, LANES), F32),
            *face_lists(),
        ],
        compiler_params=params(),
        cost_estimate=traffic(rows, 7),
        name="add_target",
    )(*given)


def side_terms(high, pairs_ref, halo_ref, f_ref, at):
    terms = [None] * REACH
    rows = [halo_ref[r, at, :] for r in range(REACH)]
    first = SUB - REACH if high else 0
    own = [f_ref[first + e, at, :] for e in range(REACH)]
    count = len(BEFORE_PAIRS)
    pairs = [(e, r) for e in range(REACH) for r in range(e + 1)] if high else BEFORE_PAIRS
    for p, (e, r) in enumerate(pairs):
        term = pairs_ref[p + count if high else p, at, :] * (rows[r] - own[e])
        terms[e] = term if terms[e] is None else terms[e] + term
    return first, terms


def for_side(far, run):
    odd = is_odd()

    @pl.when(odd)
    def _():
        run(far)

    @pl.when(jnp.logical_not(odd))
    def _():
        run(not far)


def edge_kernel(far, pairs_ref, halo_ref, old_ref, part_ref, f_ref, *rows_refs):
    def run(high):
        def group(j, _):
            at = at_rows(j * SUB)
            first, terms = side_terms(high, pairs_ref, halo_ref, old_ref, at)
            for e in range(REACH):
                x = part_ref[first + e, at, :] + terms[e]
                f_ref[first + e, at, :] = x
                for rows_ref in rows_refs:
                    rows_ref[e, at, :] = x
            return 0

        groups = part_ref.shape[1] // SUB
        lax.fori_loop(0, groups, group, 0, unroll=unroll(groups, 8))

    for_side(far, run)


def edge(far, pairs, halo, old, part, keep_rows):
    rows = part.shape[1]
    return pl.pallas_call(
        functools.partial(edge_kernel, far),
        in_specs=[spec(pltpu.VMEM)] * 4,
        out_specs=[spec(pltpu.VMEM)] * (2 if keep_rows else 1),
        out_shape=[array(SUB, rows, LANES), array(REACH, rows, LANES)][: 2 if keep_rows else 1],
        input_output_aliases={3: 0},
        compiler_params=params(),
        cost_estimate=traffic(rows, 2),
        name="far_edge" if far else "near_edge",
    )(pairs, halo, old, part)


def last_edge_kernel(geo_ref, pairs_ref, far_ref, f_ref, part_ref, out_hbm, sums_out, native_ref, sems):
    rows = part_ref.shape[1]
    planes = rows // CHUNKS
    part = rows // SUB // LAST_PARTS

    def copy(i):
        at = pl.ds(i * part * SUB * SUB, part * SUB * SUB)
        return pltpu.make_async_copy(native_ref.at[at], out_hbm.at[at], sems.at[i])

    def run(high):
        for i in range(LAST_PARTS):

            def group(j, _):
                at = at_rows(j * SUB)
                first, terms = side_terms(high, pairs_ref, far_ref, f_ref, at)
                for g in range(SUB):
                    x = part_ref[g, at, :]
                    if 0 <= g - first < REACH:
                        x = x + terms[g - first]
                    native_ref[pl.ds(j * SUB * SUB + g, SUB, stride=SUB), :] = x
                return 0

            lax.fori_loop(i * part, (i + 1) * part, group, 0, unroll=unroll(part, 4))
            copy(i).start()

    for_side(True, run)
    y = native_polynomial_sums(native_ref, planes)
    sums_out[...] = pack_sums(finish_polynomials(y, geo_ref[FIRST], planes), 0)
    for i in range(LAST_PARTS):
        copy(i).wait()


LAST_PARTS = 4


def last_edge(geo, pairs, far, f, part):
    native = (SUB * part.shape[1], LANES)
    return pl.pallas_call(
        last_edge_kernel,
        in_specs=[spec(pltpu.VMEM)] * 5,
        out_specs=[spec(pltpu.HBM), spec(pltpu.VMEM)],
        out_shape=[array(*native), array(SUB, LANES)],
        scratch_shapes=[pltpu.VMEM(native, F32), pltpu.SemaphoreType.DMA((LAST_PARTS,))],
        compiler_params=params(),
        cost_estimate=traffic(part.shape[1], 4),
        name="last_edge",
    )(geo, pairs, far, f, part)


def swap(rows, start):
    pairs = [(i, i + 1) for i in range(start, lax.axis_size("space") - 1, 2)]
    return lax.ppermute(rows, "space", pairs + [(j, i) for i, j in pairs])


def per_device(particle_profile, neighbors, face_vectors, volumes, wall_temp):
    cells, points = particle_profile.shape
    rows = points // LANES
    plane_count = NV // lax.axis_size("vel")
    native = particle_profile.reshape(cells, rows, LANES).transpose(1, 0, 2).reshape(cells * rows, LANES)
    wall = neighbors < 0
    links = jnp.where(wall, WALL_LINK, neighbors - lax.axis_index("space") * cells)
    own = (links >= 0) & (links < cells)
    first = -SPEED_LIMIT + ((lax.axis_index("vel") * plane_count).astype(F32) + 0.5) * H
    geo = jnp.concatenate(
        [
            face_vectors.reshape(3 * FACES, cells),
            volumes[None],
            wall_temp[None],
            wall.astype(F32),
            own.astype(F32),
            jnp.full((1, cells), first, F32),
        ]
    )
    geo = jnp.broadcast_to(geo[:, :, None], (GEO, cells, LANES))
    native, far, near = first_rows(native)
    far, near = swap(far, 1), swap(near, 0)
    f, sums = first_sums(links, geo, native)
    tiles = gather_sums(sums)
    pairs = geometry(links, geo, rows)
    part = flux(links, geo, f)
    part, absorbed = add_target(links, geo, None, tiles, f, part)
    part, near = edge(False, pairs, near, f, part, True)
    near = swap(near, 0)
    f, far = edge(True, pairs, far, f, part, True)
    far = swap(far, 1)
    tiles = gather_sums(local_sums(links, geo, f))
    part = flux(links, geo, f)
    part, _ = add_target(links, geo, absorbed, tiles, f, part)
    (part,) = edge(False, pairs, near, f, part, False)
    native, sums = last_edge(geo, pairs, far, f, part)
    macro_quantities = macro(doubling_sums(sums))
    evolved = native.reshape(rows, cells, LANES).transpose(1, 0, 2).reshape(cells, points)
    return evolved, macro_quantities


def solution(mesh):
    return jax.shard_map(
        per_device,
        mesh=mesh,
        in_specs=(
            P("space", "vel"),
            P(None, "space"),
            P(None, None, "space"),
            P("space"),
            P("space"),
        ),
        out_specs=(P("space", "vel"), P(None, "space")),
        check_vma=False,
    )
```

```python
import functools
import math

import jax
import jax.numpy as jnp
from jax import lax
from jax.experimental import pallas as pl
from jax.experimental.pallas import tpu as pltpu
from jax.sharding import PartitionSpec as P

NV = 64
FACES = 6
REACH = 3
STEPS = 2
LANES = 128
SUB = 8

TIME_STEP = 0.015
SHEAR = 0.1
POWER = 0.81
SPEED_LIMIT = 6.0
H = 2.0 * SPEED_LIMIT / NV
WEIGHT = H**3 * (2.0 * math.pi) ** (-1.5)

CHUNKS = NV * NV // LANES
TILES = CHUNKS // SUB

FV, VOL, WT, WALL, LOCAL, FIRST = 0, 18, 19, 20, 26, 32
GEO = 33
WALL_LINK = -64
BEFORE_PAIRS = tuple((g, r) for g in range(REACH) for r in range(g, REACH))
EMIT, ABSORB = 13, 19
SUMS = 25

F32 = jnp.float32


def lane_iota():
    return lax.broadcasted_iota(jnp.int32, (SUB, LANES), 1)


def sub_iota():
    return lax.broadcasted_iota(jnp.int32, (SUB, LANES), 0)


def half_of(lane):
    return (lane >= NV).astype(F32)


def third_component(lane):
    c = jnp.where(lane >= NV, lane - NV, lane).astype(F32)
    return -SPEED_LIMIT + (c + 0.5) * H


def tile_nodes(t):
    lane = lane_iota()
    b = (2 * SUB * t + 2 * sub_iota()).astype(F32) + half_of(lane)
    return -SPEED_LIMIT + (b + 0.5) * H, third_component(lane)


def column(tile, p):
    return jnp.broadcast_to(tile[:, p : p + 1], (SUB, LANES))


def splat(ref, i, g):
    return jnp.broadcast_to(ref[i, pl.ds(g, 1), :], (SUB, LANES))


def total(tile):
    return jnp.broadcast_to(jnp.sum(tile, axis=1, keepdims=True), (SUB, LANES))


def face_coefficients(geo_ref, k, g):
    return [splat(geo_ref, FV + FACES * i + k, g) for i in range(3)]


def at_rows(start, size=SUB):
    return pl.ds(pl.multiple_of(start, SUB), size)


def wall_tiles(wall_temp):
    rt = 1.0 / wall_temp
    scale = rt * jnp.sqrt(rt)
    out = []
    for t in range(TILES):
        xb, xc = tile_nodes(t)
        out.append(scale * jnp.exp(-0.5 * (xb * xb + xc * xc) * rt))
    return out


def pack_sums(arrays, start):
    lane = lane_iota()
    out = jnp.zeros((SUB, LANES), F32)
    for p, x in enumerate(arrays):
        out = jnp.where(lane == start + p, total(x), out)
    return out


def over_sublanes(ref, k):
    out = ref[k, pl.ds(0, SUB, stride=SUB), :]
    for s in range(1, SUB):
        out = out + ref[k, pl.ds(s, SUB, stride=SUB), :]
    return out


def list_faces(links_ref, wanted, cell_ref, face_ref):
    count = 0
    for g in range(SUB):
        for k in range(FACES):
            cell_ref[count] = g
            face_ref[count] = k
            count = count + wanted(links_ref[k, g]).astype(jnp.int32)
    return count


def is_wall(j):
    return j == WALL_LINK


def is_remote(j):
    return jnp.logical_or(j >= SUB, jnp.logical_and(j < 0, j != WALL_LINK))


def face_lists():
    return [pltpu.SMEM((FACES * SUB + 1,), jnp.int32)] * 2


def unroll(planes, most):
    return math.gcd(planes, most)


def finish_polynomials(y, first, planes):
    y0, y1, y2, y3, by0, by1, by2, bby0, bby1, bbby0 = y
    m = first + 0.5 * (planes - 1) * H
    c = third_component(lane_iota())
    cc = c * c
    a = y1 + m * y0
    aa = y2 + m * (2.0 * y1 + m * y0)
    aaa = y3 + m * (3.0 * y2 + m * (3.0 * y1 + m * y0))
    ab = by1 + m * by0
    aab = by2 + m * (2.0 * by1 + m * by0)
    abb = bby1 + m * bby0
    return (
        y0,
        a,
        by0,
        c * y0,
        aa,
        bby0,
        cc * y0,
        ab,
        c * a,
        c * by0,
        aaa + abb + cc * a,
        aab + bbby0 + cc * by0,
        c * (aa + bby0 + cc * y0),
    )


def polynomial_sums(f_ref, planes, parts_ref):
    half = planes // 2

    def cell(g, _):
        out = [None] * 10
        for t in range(TILES):
            y0 = y1 = y2 = y3 = None
            for i in range(half):
                d = (i + 0.5) * H
                hi = f_ref[g, pl.ds(((half + i) * TILES + t) * SUB, SUB), :]
                lo = f_ref[g, pl.ds(((half - 1 - i) * TILES + t) * SUB, SUB), :]
                s, r = hi + lo, hi - lo
                if i == 0:
                    y0, y1, y2, y3 = s, d * r, (d * d) * s, (d * d * d) * r
                else:
                    y0, y1, y2, y3 = y0 + s, y1 + d * r, y2 + (d * d) * s, y3 + (d * d * d) * r
            b, _c = tile_nodes(t)
            bb = b * b
            terms = (y0, y1, y2, y3, b * y0, b * y1, b * y2, bb * y0, bb * y1, bb * (b * y0))
            out = [x if o is None else o + x for o, x in zip(out, terms)]
        for p in range(10):
            parts_ref[p, at_rows(g * SUB), :] = out[p]
        return 0

    lax.fori_loop(0, SUB, cell, 0)
    return [over_sublanes(parts_ref, p) for p in range(10)]


def native_polynomial_sums(native_ref, planes):
    half, side = planes // 2, CHUNKS // 2
    zero = jnp.zeros((SUB, LANES), F32)
    acc = [zero] * 10

    def plane(a, acc):
        xa = (a.astype(F32) - 0.5 * (planes - 1)) * H
        b0 = b1 = b2 = b3 = None
        for i in range(side):
            y = (2 * i + 1) * H
            hi = native_ref[at_rows((a * CHUNKS + side + i) * SUB), :]
            lo = native_ref[at_rows((a * CHUNKS + side - 1 - i) * SUB), :]
            s, d = hi + lo, hi - lo
            terms = (s, y * d, (y * y) * s, (y * y * y) * d)
            if i == 0:
                b0, b1, b2, b3 = terms
            else:
                b0, b1, b2, b3 = b0 + terms[0], b1 + terms[1], b2 + terms[2], b3 + terms[3]
        a0, a1, a2 = xa * b0, xa * b1, xa * b2
        aa0 = xa * a0
        new = (b0, a0, aa0, xa * aa0, b1, a1, xa * a1, b2, a2, b3)
        return tuple(x + z for x, z in zip(acc, new))

    g0, a0, aa0, aaa0, g1, a1, aa1, g2, a2, g3 = lax.fori_loop(0, planes, plane, tuple(acc))
    e = (half_of(lane_iota()) - 0.5) * H
    return [
        g0,
        a0,
        aa0,
        aaa0,
        g1 + e * g0,
        a1 + e * a0,
        aa1 + e * aa0,
        g2 + e * (2.0 * g1 + e * g0),
        a2 + e * (2.0 * a1 + e * a0),
        g3 + e * (3.0 * g2 + e * (3.0 * g1 + e * g0)),
    ]


def wall_sums(f_ref, planes, links_ref, geo_ref, sums_ref, cells, faces, with_absorbed):
    sums_ref[...] = jnp.zeros_like(sums_ref)

    def wall(i, _):
        g, k = cells[i], faces[i]
        v0, v1, v2 = face_coefficients(geo_ref, k, g)
        first = splat(geo_ref, FIRST, g)
        base = []
        for t in range(TILES):
            xb, xc = tile_nodes(t)
            base.append(v1 * xb + v2 * xc)
        if with_absorbed:
            wt = splat(geo_ref, WT, g)
            shape = wall_tiles(wt)

        def plane(a, acc):
            out, back = list(acc[0]), list(acc[1])
            xa = first + a.astype(F32) * H
            sa = v0 * xa
            if with_absorbed:
                wa = jnp.exp(-0.5 * xa * xa / wt)
            for t in range(TILES):
                s = sa + base[t]
                f = f_ref[g, at_rows((a * TILES + t) * SUB), :]
                out[t] = out[t] + jnp.maximum(s, 0.0) * f
                if with_absorbed:
                    back[t] = back[t] + jnp.maximum(-s, 0.0) * (wa * shape[t])
            return tuple(out), tuple(back)

        zeros = (jnp.zeros((SUB, LANES), F32),) * TILES
        out, back = lax.fori_loop(0, planes, plane, (zeros, zeros), unroll=unroll(planes, 16))
        at = at_rows(g * SUB)
        sums_ref[k, at, :] = (out[0] + out[1]) + (out[2] + out[3])
        if with_absorbed:
            sums_ref[FACES + k, at, :] = (back[0] + back[1]) + (back[2] + back[3])
        return 0

    lax.fori_loop(0, list_faces(links_ref, is_wall, cells, faces), wall, 0)


def sums_kernel(links_ref, geo_ref, f_ref, sums_out, parts_ref, face_ref, cells, faces):
    planes = f_ref.shape[1] // CHUNKS
    y = polynomial_sums(f_ref, planes, parts_ref)
    packed = pack_sums(finish_polynomials(y, geo_ref[FIRST], planes), 0)
    wall_sums(f_ref, planes, links_ref, geo_ref, face_ref, cells, faces, False)
    sums_out[...] = packed + pack_sums([over_sublanes(face_ref, k) for k in range(FACES)], EMIT)


def first_sums_kernel(links_ref, geo_ref, native_ref, f_ref, sums_out, face_ref, cells, faces):
    rows = f_ref.shape[1]
    planes = rows // CHUNKS

    def group(j, _):
        for g in range(SUB):
            f_ref[g, at_rows(j * SUB), :] = native_ref[pl.ds(j * SUB * SUB + g, SUB, stride=SUB), :]
        return 0

    lax.fori_loop(0, rows // SUB, group, 0, unroll=2)
    y = native_polynomial_sums(native_ref, planes)
    packed = pack_sums(finish_polynomials(y, geo_ref[FIRST], planes), 0)
    wall_sums(f_ref, planes, links_ref, geo_ref, face_ref, cells, faces, True)
    sums_out[...] = packed + pack_sums([over_sublanes(face_ref, k) for k in range(2 * FACES)], EMIT)


def spec(space):
    return pl.BlockSpec(memory_space=space)


def array(*shape):
    return jax.ShapeDtypeStruct(shape, F32)


def params(mib=4):
    return pltpu.CompilerParams(vmem_limit_bytes=mib * 1024 * 1024)


def traffic(rows, profiles):
    size = SUB * rows * LANES
    return pl.CostEstimate(flops=8 * profiles * size, bytes_accessed=4 * profiles * size, transcendentals=0)


def local_sums(links, geo, f):
    return pl.pallas_call(
        sums_kernel,
        in_specs=[spec(pltpu.SMEM), spec(pltpu.VMEM), spec(pltpu.VMEM)],
        out_specs=spec(pltpu.VMEM),
        out_shape=array(SUB, LANES),
        scratch_shapes=[
                pltpu.VMEM((10, SUB * SUB, LANES), F32),
            pltpu.VMEM((FACES, SUB * SUB, LANES), F32),
            *face_lists(),
        ],
        compiler_params=params(),
        cost_estimate=traffic(f.shape[1], 4),
        name="local_sums",
    )(links, geo, f)


def first_sums(links, geo, native):
    rows = native.shape[0] // SUB
    return pl.pallas_call(
        first_sums_kernel,
        in_specs=[spec(pltpu.SMEM), spec(pltpu.VMEM), spec(pltpu.VMEM)],
        out_specs=[spec(pltpu.VMEM)] * 2,
        out_shape=[array(SUB, rows, LANES), array(SUB, LANES)],
        scratch_shapes=[
                pltpu.VMEM((2 * FACES, SUB * SUB, LANES), F32),
            *face_lists(),
        ],
        compiler_params=params(),
        cost_estimate=traffic(rows, 5),
        name="first_sums",
    )(links, geo, native)


SPLIT_PARTS = 4


def is_odd():
    return lax.rem(lax.axis_index("space"), 2) == 1


def first_rows_kernel(native_hbm, native_ref, far_any, near_any, far_ref, near_ref, sems, far_sems, near_sems):
    rows = native_ref.shape[0]
    part = rows // SPLIT_PARTS
    copies = [
        pltpu.make_async_copy(
            native_hbm.at[pl.ds(i * part, part)], native_ref.at[pl.ds(i * part, part)], sems.at[i]
        )
        for i in range(SPLIT_PARTS)
    ]
    for c in copies:
        c.start()
    odd = is_odd()
    far = jnp.where(odd, SUB - REACH, 0)
    near = jnp.where(odd, 0, SUB - REACH)
    groups = part // (SUB * SUB)
    out = []

    for i, c in enumerate(copies):
        c.wait()

        def group(j, _):
            for r in range(REACH):
                at = at_rows(j * SUB)
                far_ref[r, at, :] = native_ref[pl.ds(j * SUB * SUB + far + r, SUB, stride=SUB), :]
                near_ref[r, at, :] = native_ref[pl.ds(j * SUB * SUB + near + r, SUB, stride=SUB), :]
            return 0

        lax.fori_loop(i * groups, (i + 1) * groups, group, 0, unroll=unroll(groups, 8))
        at = pl.ds(i * groups * SUB, groups * SUB)
        out.append(pltpu.make_async_copy(far_ref.at[:, at], far_any.at[:, at], far_sems.at[i]))
        out.append(pltpu.make_async_copy(near_ref.at[:, at], near_any.at[:, at], near_sems.at[i]))
        out[-2].start()
        out[-1].start()
    for c in out:
        c.wait()


def first_rows(native):
    rows = native.shape[0] // SUB
    halo = (REACH, rows, LANES)
    return pl.pallas_call(
        first_rows_kernel,
        in_specs=[spec(pltpu.HBM)],
        out_specs=[spec(pltpu.VMEM), spec(pl.ANY), spec(pl.ANY)],
        out_shape=[array(*native.shape), array(*halo), array(*halo)],
        scratch_shapes=[pltpu.VMEM(halo, F32)] * 2 + [pltpu.SemaphoreType.DMA((SPLIT_PARTS,))] * 3,
        compiler_params=params(),
        cost_estimate=traffic(rows, 4),
        name="first_rows",
    )(pltpu.with_memory_space_constraint(native, pltpu.HBM))


def pair_weights(links_ref, geo_ref, pairs_ref, cells, faces):
    rows = pairs_ref.shape[1]
    planes = rows // CHUNKS
    first = splat(geo_ref, FIRST, 0)

    def clear(j, _):
        for p in range(pairs_ref.shape[0]):
            pairs_ref[p, at_rows(j * SUB), :] = jnp.zeros((SUB, LANES), F32)
        return 0

    lax.fori_loop(0, rows // SUB, clear, 0, unroll=4)

    def remote(i, _):
        g, k = cells[i], faces[i]
        j = links_ref[k, g]
        edge = g - (SUB - REACH)
        before = g * REACH - g * (g - 1) // 2 + (j + REACH) - g
        after = len(BEFORE_PAIRS) + edge * (edge + 1) // 2 + j - SUB
        at_pair = jnp.where(j < 0, before, after)
        scale = -TIME_STEP / splat(geo_ref, VOL, g)
        v0, v1, v2 = [scale * x for x in face_coefficients(geo_ref, k, g)]
        base = []
        for t in range(TILES):
            xb, xc = tile_nodes(t)
            base.append(v1 * xb + v2 * xc)

        def plane(a, _):
            sa = v0 * (first + a.astype(F32) * H)
            for t in range(TILES):
                at = at_rows((a * TILES + t) * SUB)
                pairs_ref[at_pair, at, :] = pairs_ref[at_pair, at, :] + jnp.maximum(sa + base[t], 0.0)
            return 0

        lax.fori_loop(0, planes, plane, 0, unroll=unroll(planes, 8))
        return 0

    lax.fori_loop(0, list_faces(links_ref, is_remote, cells, faces), remote, 0)


def gather_sums(tile):
    size = lax.axis_size("vel")
    if size not in (2, 4):
        return [lax.psum(tile, "vel")]
    others = [lax.ppermute(tile, "vel", [(i, i ^ s) for i in range(size)]) for s in range(1, size)]
    return [tile, *others]


def doubling_sums(tile):
    size = lax.axis_size("vel")
    if size != 4:
        return gather_sums(tile)
    pair = tile + lax.ppermute(tile, "vel", [(i, i ^ 1) for i in range(size)])
    return [pair, lax.ppermute(pair, "vel", [(i, i ^ 2) for i in range(size)])]


def add_tiles(refs):
    tiles = [r[...] for r in refs]
    while len(tiles) > 1:
        tiles = [tiles[i] + tiles[i + 1] for i in range(0, len(tiles), 2)]
    return tiles[0]


def quantities(tile):
    m = [WEIGHT * column(tile, p) for p in range(13)]
    n = m[0]
    rn = 1.0 / n
    u = [m[1 + i] * rn for i in range(3)]
    uu = u[0] * u[0] + u[1] * u[1] + u[2] * u[2]
    trace = m[4] + m[5] + m[6]
    width = trace - n * uu
    temperature = width * rn * (1.0 / 3.0)
    second = [[m[4], m[7], m[8]], [m[7], m[5], m[9]], [m[8], m[9], m[6]]]
    q = []
    for i in range(3):
        across = u[0] * second[i][0] + u[1] * second[i][1] + u[2] * second[i][2]
        q.append(0.5 * (m[10 + i] - 2.0 * across - u[i] * trace + 2.0 * uu * m[1 + i]))
    return n, u, temperature, q


def macro_kernel(*refs):
    out_ref = refs[-1]
    n, u, temperature, q = quantities(add_tiles(refs[:-1]))
    lane, sub = lane_iota(), sub_iota()
    for i, x in enumerate((n, *u, temperature, *q)):
        row = jnp.sum(jnp.where(lane == sub, x, 0.0), axis=0, keepdims=True)
        out_ref[pl.ds(i, 1), :] = row[:, :SUB]


def macro(tiles):
    return pl.pallas_call(
        macro_kernel,
        in_specs=[spec(pltpu.VMEM)] * len(tiles),
        out_specs=spec(pltpu.VMEM),
        out_shape=array(8, SUB),
        compiler_params=params(1),
        name="macro",
    )(*tiles)


def flux_kernel(with_pairs, links_ref, geo_ref, f_ref, out_ref, *refs):
    if with_pairs:
        pairs_ref, cells, faces = refs[0], refs[-2], refs[-1]
        pair_weights(links_ref, geo_ref, pairs_ref, cells, faces)
        refs = refs[1:-2]
    coef, bases, stays, source, face = refs
    planes = f_ref.shape[1] // CHUNKS
    scale = -TIME_STEP / geo_ref[VOL]
    for i in range(3):
        whole = None
        for k in range(FACES):
            x = scale * geo_ref[FV + FACES * i + k]
            coef[FACES * i + k] = x
            whole = x if whole is None else whole + x
        coef[3 * FACES + i] = whole

    def table(g, _):
        w = [[splat(coef, FACES * i + k, g) for i in (1, 2)] for k in range(FACES)]
        whole = [splat(coef, 3 * FACES + i, g) for i in (1, 2)]
        for t in range(TILES):
            xb, xc = tile_nodes(t)
            for k in range(FACES):
                bases[k, g * TILES + t] = w[k][0] * xb + w[k][1] * xc
            stays[g * TILES + t] = 1.0 + whole[0] * xb + whole[1] * xc
        return 0

    lax.fori_loop(0, SUB, table, 0, unroll=2)

    def cell(g, _):
        count = 0
        for k in range(FACES):
            j = links_ref[k, g]
            source[count] = j
            face[count] = k
            count = count + jnp.logical_and(j >= 0, j < SUB).astype(jnp.int32)
        for n in range(FACES + 1):

            @pl.when(count == n)
            def _():
                own_faces(g, n)

        return 0

    def own_faces(g, n):
        at_source = [source[i] for i in range(n)]
        first_weight = [splat(coef, face[k], g) for k in range(n)]
        whole = splat(coef, 3 * FACES, g)
        x0 = splat(geo_ref, FIRST, g)
        base = [[bases[face[k], g * TILES + t] for k in range(n)] for t in range(TILES)]
        stay = [stays[g * TILES + t] for t in range(TILES)]

        def plane(a, _):
            xa = x0 + a.astype(F32) * H
            sa = [w * xa for w in first_weight]
            stay_a = whole * xa
            for t in range(TILES):
                at = at_rows((a * TILES + t) * SUB)
                f = f_ref[g, at, :]
                acc = f * (stay_a + stay[t])
                for k in range(n):
                    acc = acc + jnp.maximum(sa[k] + base[t][k], 0.0) * (f_ref[at_source[k], at, :] - f)
                out_ref[g, at, :] = acc
            return 0

        lax.fori_loop(0, planes, plane, 0, unroll=unroll(planes, 8))

    lax.fori_loop(0, SUB, cell, 0)


def flux(with_pairs, links, geo, f):
    rows = f.shape[1]
    pairs = 2 * len(BEFORE_PAIRS)
    return pl.pallas_call(
        functools.partial(flux_kernel, with_pairs),
        in_specs=[spec(pltpu.SMEM), spec(pltpu.VMEM), spec(pltpu.VMEM)],
        out_specs=[spec(pltpu.VMEM)] * (2 if with_pairs else 1),
        out_shape=[array(*f.shape)] + ([array(pairs, rows, LANES)] if with_pairs else []),
        scratch_shapes=[
            pltpu.VMEM((3 * FACES + 3, SUB, LANES), F32),
            pltpu.VMEM((FACES, SUB * TILES, SUB, LANES), F32),
            pltpu.VMEM((SUB * TILES, SUB, LANES), F32),
            pltpu.SMEM((FACES + 1,), jnp.int32),
            pltpu.SMEM((FACES + 1,), jnp.int32),
        ]
        + (face_lists() if with_pairs else []),
        compiler_params=params(),
        cost_estimate=traffic(rows, 9 if with_pairs else 7),
        name="flux",
    )(links, geo, f)


def target_kernel(count, links_ref, geo_ref, absorbed_in, *refs):
    sums_refs, (f_ref, part_ref, out_ref, sum_out, ta, tiles_ref, coef, cells, faces) = refs[:count], refs[count:]
    planes = f_ref.shape[1] // CHUNKS
    sums = add_tiles(sums_refs)
    sum_out[...] = sums
    absorbed = sums if absorbed_in is None else absorbed_in[...]
    n, u, temperature, q = quantities(sums)
    rt = 1.0 / temperature
    rate = TIME_STEP * n * temperature / (SHEAR * jnp.exp(POWER * jnp.log(temperature)))
    height = rate * n * rt * jnp.sqrt(rt)
    slope = (1.0 / 3.0) / (5.0 * n * temperature * temperature)
    coef[0] = rate
    coef[1] = rt
    coef[2], coef[3] = u[1], u[2]
    coef[4], coef[5] = slope * q[1], slope * q[2]
    for k in range(FACES):
        wall = geo_ref[WALL + k] > 0.5
        coef[6 + k] = column(sums, EMIT + k) / jnp.where(wall, column(absorbed, ABSORB + k), 1.0)
    first = geo_ref[FIRST]

    wt = geo_ref[WT]

    def plane_table(a, _):
        xa = first + a.astype(F32) * H
        ca = xa - u[0]
        za = ca * ca * rt
        ta[0, a] = height * jnp.exp(-0.5 * za)
        ta[1, a] = slope * q[0] * ca
        ta[2, a] = za - 5.0
        ta[3, a] = jnp.exp(-0.5 * xa * xa / wt)
        return 0

    lax.fori_loop(0, planes, plane_table, 0, unroll=unroll(planes, 8))

    def tile_table(g, _):
        rtg = splat(coef, 1, g)
        ub, uc = splat(coef, 2, g), splat(coef, 3, g)
        qb, qc = splat(coef, 4, g), splat(coef, 5, g)
        shape = wall_tiles(splat(geo_ref, WT, g))
        for t in range(TILES):
            xb, xc = tile_nodes(t)
            cb, cc = xb - ub, xc - uc
            z = (cb * cb + cc * cc) * rtg
            at = g * TILES + t
            tiles_ref[0, at] = jnp.exp(-0.5 * z)
            tiles_ref[1, at] = cb * qb + cc * qc
            tiles_ref[2, at] = z
            tiles_ref[3, at] = shape[t]
        return 0

    lax.fori_loop(0, SUB, tile_table, 0, unroll=4)

    def at_plane(i, a, g):
        return jnp.broadcast_to(ta[i, a, pl.ds(g, 1), :], (SUB, LANES))

    def cell(g, _):
        rate_g = splat(coef, 0, g)
        bell, heat, zz = [[tiles_ref[i, g * TILES + t] for t in range(TILES)] for i in range(3)]

        def plane(a, _):
            height_a, heat_a, z_a = [at_plane(i, a, g) for i in range(3)]
            for t in range(TILES):
                where = (g, at_rows((a * TILES + t) * SUB), slice(None))
                f = f_ref[where]
                target = (height_a * bell[t]) * (1.0 + (heat_a + heat[t]) * (z_a + zz[t]))
                out_ref[where] = (part_ref[where] - rate_g * f) + target
            return 0

        lax.fori_loop(0, planes, plane, 0, unroll=unroll(planes, 16))
        return 0

    lax.fori_loop(0, SUB, cell, 0)

    def wall(i, _):
        g, k = cells[i], faces[i]
        x0 = splat(geo_ref, FIRST, g)
        ratio = splat(coef, 6 + k, g)
        scale = -TIME_STEP / splat(geo_ref, VOL, g)
        v0, v1, v2 = [scale * x for x in face_coefficients(geo_ref, k, g)]
        base, shape = [], []
        for t in range(TILES):
            xb, xc = tile_nodes(t)
            base.append(v1 * xb + v2 * xc)
            shape.append(ratio * tiles_ref[3, g * TILES + t])

        def plane(a, _):
            wa = at_plane(3, a, g)
            sa = v0 * (x0 + a.astype(F32) * H)
            for t in range(TILES):
                where = (g, at_rows((a * TILES + t) * SUB), slice(None))
                f = f_ref[where]
                out_ref[where] = out_ref[where] + jnp.maximum(sa + base[t], 0.0) * (wa * shape[t] - f)
            return 0

        lax.fori_loop(0, planes, plane, 0, unroll=unroll(planes, 16))
        return 0

    lax.fori_loop(0, list_faces(links_ref, is_wall, cells, faces), wall, 0)


def add_target(links, geo, absorbed, tiles, f, part):
    rows = f.shape[1]
    vmem = spec(pltpu.VMEM)
    given = [links, geo] + ([] if absorbed is None else [absorbed]) + list(tiles) + [f, part]

    def kernel(links_ref, geo_in, *refs):
        if absorbed is None:
            target_kernel(len(tiles), links_ref, geo_in, None, *refs)
        else:
            target_kernel(len(tiles), links_ref, geo_in, *refs)

    return pl.pallas_call(
        kernel,
        in_specs=[spec(pltpu.SMEM)] + [vmem] * (len(given) - 1),
        out_specs=[vmem] * 2,
        out_shape=[array(*part.shape), array(SUB, LANES)],
        input_output_aliases={len(given) - 1: 0},
        scratch_shapes=[
                pltpu.VMEM((4, rows // CHUNKS, SUB, LANES), F32),
            pltpu.VMEM((4, SUB * TILES, SUB, LANES), F32),
            pltpu.VMEM((6 + FACES, SUB, LANES), F32),
            *face_lists(),
        ],
        compiler_params=params(),
        cost_estimate=traffic(rows, 7),
        name="add_target",
    )(*given)


def side_terms(high, pairs_ref, halo_ref, f_ref, at):
    terms = [None] * REACH
    rows = [halo_ref[r, at, :] for r in range(REACH)]
    first = SUB - REACH if high else 0
    own = [f_ref[first + e, at, :] for e in range(REACH)]
    count = len(BEFORE_PAIRS)
    pairs = [(e, r) for e in range(REACH) for r in range(e + 1)] if high else BEFORE_PAIRS
    for p, (e, r) in enumerate(pairs):
        term = pairs_ref[p + count if high else p, at, :] * (rows[r] - own[e])
        terms[e] = term if terms[e] is None else terms[e] + term
    return first, terms


def for_side(far, run):
    odd = is_odd()

    @pl.when(odd)
    def _():
        run(far)

    @pl.when(jnp.logical_not(odd))
    def _():
        run(not far)


def edge_kernel(far, pairs_ref, halo_ref, old_ref, part_ref, f_ref, *rows_refs):
    def run(high):
        def group(j, _):
            at = at_rows(j * SUB)
            first, terms = side_terms(high, pairs_ref, halo_ref, old_ref, at)
            for e in range(REACH):
                x = part_ref[first + e, at, :] + terms[e]
                f_ref[first + e, at, :] = x
                for rows_ref in rows_refs:
                    rows_ref[e, at, :] = x
            return 0

        groups = part_ref.shape[1] // SUB
        lax.fori_loop(0, groups, group, 0, unroll=unroll(groups, 8))

    for_side(far, run)


def edge(far, pairs, halo, old, part, keep_rows):
    rows = part.shape[1]
    return pl.pallas_call(
        functools.partial(edge_kernel, far),
        in_specs=[spec(pltpu.VMEM)] * 4,
        out_specs=[spec(pltpu.VMEM)] * (2 if keep_rows else 1),
        out_shape=[array(SUB, rows, LANES), array(REACH, rows, LANES)][: 2 if keep_rows else 1],
        input_output_aliases={3: 0},
        compiler_params=params(),
        cost_estimate=traffic(rows, 2),
        name="far_edge" if far else "near_edge",
    )(pairs, halo, old, part)


def last_edge_kernel(geo_ref, pairs_ref, far_ref, f_ref, part_ref, out_hbm, sums_out, native_ref, sems):
    rows = part_ref.shape[1]
    planes = rows // CHUNKS
    part = rows // SUB // LAST_PARTS

    def copy(i):
        at = pl.ds(i * part * SUB * SUB, part * SUB * SUB)
        return pltpu.make_async_copy(native_ref.at[at], out_hbm.at[at], sems.at[i])

    def run(high):
        for i in range(LAST_PARTS):

            def group(j, _):
                at = at_rows(j * SUB)
                first, terms = side_terms(high, pairs_ref, far_ref, f_ref, at)
                for g in range(SUB):
                    x = part_ref[g, at, :]
                    if 0 <= g - first < REACH:
                        x = x + terms[g - first]
                    native_ref[pl.ds(j * SUB * SUB + g, SUB, stride=SUB), :] = x
                return 0

            lax.fori_loop(i * part, (i + 1) * part, group, 0, unroll=unroll(part, 4))
            copy(i).start()

    for_side(True, run)
    y = native_polynomial_sums(native_ref, planes)
    sums_out[...] = pack_sums(finish_polynomials(y, geo_ref[FIRST], planes), 0)
    for i in range(LAST_PARTS):
        copy(i).wait()


LAST_PARTS = 4


def last_edge(geo, pairs, far, f, part):
    native = (SUB * part.shape[1], LANES)
    return pl.pallas_call(
        last_edge_kernel,
        in_specs=[spec(pltpu.VMEM)] * 5,
        out_specs=[spec(pltpu.HBM), spec(pltpu.VMEM)],
        out_shape=[array(*native), array(SUB, LANES)],
        scratch_shapes=[pltpu.VMEM(native, F32), pltpu.SemaphoreType.DMA((LAST_PARTS,))],
        compiler_params=params(),
        cost_estimate=traffic(part.shape[1], 4),
        name="last_edge",
    )(geo, pairs, far, f, part)


def swap(rows, start):
    pairs = [(i, i + 1) for i in range(start, lax.axis_size("space") - 1, 2)]
    return lax.ppermute(rows, "space", pairs + [(j, i) for i, j in pairs])


def per_device(particle_profile, neighbors, face_vectors, volumes, wall_temp):
    cells, points = particle_profile.shape
    rows = points // LANES
    plane_count = NV // lax.axis_size("vel")
    native = particle_profile.reshape(cells, rows, LANES).transpose(1, 0, 2).reshape(cells * rows, LANES)
    wall = neighbors < 0
    links = jnp.where(wall, WALL_LINK, neighbors - lax.axis_index("space") * cells)
    own = (links >= 0) & (links < cells)
    first = -SPEED_LIMIT + ((lax.axis_index("vel") * plane_count).astype(F32) + 0.5) * H
    geo = jnp.concatenate(
        [
            face_vectors.reshape(3 * FACES, cells),
            volumes[None],
            wall_temp[None],
            wall.astype(F32),
            own.astype(F32),
            jnp.full((1, cells), first, F32),
        ]
    )
    geo = jnp.broadcast_to(geo[:, :, None], (GEO, cells, LANES))
    native, far, near = first_rows(native)
    far, near = swap(far, 1), swap(near, 0)
    f, sums = first_sums(links, geo, native)
    tiles = gather_sums(sums)
    part, pairs = flux(True, links, geo, f)
    part, absorbed = add_target(links, geo, None, tiles, f, part)
    part, near = edge(False, pairs, near, f, part, True)
    near = swap(near, 0)
    f, far = edge(True, pairs, far, f, part, True)
    far = swap(far, 1)
    tiles = gather_sums(local_sums(links, geo, f))
    (part,) = flux(False, links, geo, f)
    part, _ = add_target(links, geo, absorbed, tiles, f, part)
    (part,) = edge(False, pairs, near, f, part, False)
    native, sums = last_edge(geo, pairs, far, f, part)
    macro_quantities = macro(doubling_sums(sums))
    evolved = native.reshape(rows, cells, LANES).transpose(1, 0, 2).reshape(cells, points)
    return evolved, macro_quantities


def solution(mesh):
    return jax.shard_map(
        per_device,
        mesh=mesh,
        in_specs=(
            P("space", "vel"),
            P(None, "space"),
            P(None, None, "space"),
            P("space"),
            P("space"),
        ),
        out_specs=(P("space", "vel"), P(None, "space")),
        check_vma=False,
    )
```

```python
import functools
import math

import jax
import jax.numpy as jnp
from jax import lax
from jax.experimental import pallas as pl
from jax.experimental.pallas import tpu as pltpu
from jax.sharding import PartitionSpec as P

NV = 64
FACES = 6
REACH = 3
STEPS = 2
LANES = 128
SUB = 8

TIME_STEP = 0.015
SHEAR = 0.1
POWER = 0.81
SPEED_LIMIT = 6.0
H = 2.0 * SPEED_LIMIT / NV
WEIGHT = H**3 * (2.0 * math.pi) ** (-1.5)

CHUNKS = NV * NV // LANES
TILES = CHUNKS // SUB

FV, VOL, WT, WALL, LOCAL, FIRST = 0, 18, 19, 20, 26, 32
GEO = 33
WALL_LINK = -64
BEFORE_PAIRS = tuple((g, r) for g in range(REACH) for r in range(g, REACH))
EMIT, ABSORB = 13, 19
SUMS = 25

F32 = jnp.float32


def lane_iota():
    return lax.broadcasted_iota(jnp.int32, (SUB, LANES), 1)


def sub_iota():
    return lax.broadcasted_iota(jnp.int32, (SUB, LANES), 0)


def half_of(lane):
    return (lane >= NV).astype(F32)


def third_component(lane):
    c = jnp.where(lane >= NV, lane - NV, lane).astype(F32)
    return -SPEED_LIMIT + (c + 0.5) * H


def tile_nodes(t):
    lane = lane_iota()
    b = (2 * SUB * t + 2 * sub_iota()).astype(F32) + half_of(lane)
    return -SPEED_LIMIT + (b + 0.5) * H, third_component(lane)


def column(tile, p):
    return jnp.broadcast_to(tile[:, p : p + 1], (SUB, LANES))


def splat(ref, i, g):
    return jnp.broadcast_to(ref[i, pl.ds(g, 1), :], (SUB, LANES))


def total(tile):
    return jnp.broadcast_to(jnp.sum(tile, axis=1, keepdims=True), (SUB, LANES))


def face_coefficients(geo_ref, k, g):
    return [splat(geo_ref, FV + FACES * i + k, g) for i in range(3)]


def at_rows(start, size=SUB):
    return pl.ds(pl.multiple_of(start, SUB), size)


def wall_tiles(wall_temp):
    rt = 1.0 / wall_temp
    scale = rt * jnp.sqrt(rt)
    out = []
    for t in range(TILES):
        xb, xc = tile_nodes(t)
        out.append(scale * jnp.exp(-0.5 * (xb * xb + xc * xc) * rt))
    return out


def pack_sums(arrays, start):
    lane = lane_iota()
    out = jnp.zeros((SUB, LANES), F32)
    for p, x in enumerate(arrays):
        out = jnp.where(lane == start + p, total(x), out)
    return out


def over_sublanes(ref, k):
    out = ref[k, pl.ds(0, SUB, stride=SUB), :]
    for s in range(1, SUB):
        out = out + ref[k, pl.ds(s, SUB, stride=SUB), :]
    return out


def list_faces(links_ref, wanted, cell_ref, face_ref):
    count = 0
    for g in range(SUB):
        for k in range(FACES):
            cell_ref[count] = g
            face_ref[count] = k
            count = count + wanted(links_ref[k, g]).astype(jnp.int32)
    return count


def is_wall(j):
    return j == WALL_LINK


def is_remote(j):
    return jnp.logical_or(j >= SUB, jnp.logical_and(j < 0, j != WALL_LINK))


def face_lists():
    return [pltpu.SMEM((FACES * SUB + 1,), jnp.int32)] * 2


def unroll(planes, most):
    return math.gcd(planes, most)


def finish_polynomials(y, first, planes):
    y0, y1, y2, y3, by0, by1, by2, bby0, bby1, bbby0 = y
    m = first + 0.5 * (planes - 1) * H
    c = third_component(lane_iota())
    cc = c * c
    a = y1 + m * y0
    aa = y2 + m * (2.0 * y1 + m * y0)
    aaa = y3 + m * (3.0 * y2 + m * (3.0 * y1 + m * y0))
    ab = by1 + m * by0
    aab = by2 + m * (2.0 * by1 + m * by0)
    abb = bby1 + m * bby0
    return (
        y0,
        a,
        by0,
        c * y0,
        aa,
        bby0,
        cc * y0,
        ab,
        c * a,
        c * by0,
        aaa + abb + cc * a,
        aab + bbby0 + cc * by0,
        c * (aa + bby0 + cc * y0),
    )


def polynomial_sums(f_ref, planes, parts_ref, first=0):
    half = planes // 2

    def cell(g, _):
        out = [None] * 10
        for t in range(TILES):
            y0 = y1 = y2 = y3 = None
            for i in range(half):
                d = (i + 0.5) * H
                hi = f_ref[g, pl.ds(((half + i) * TILES + t) * SUB, SUB), :]
                lo = f_ref[g, pl.ds(((half - 1 - i) * TILES + t) * SUB, SUB), :]
                s, r = hi + lo, hi - lo
                if i == 0:
                    y0, y1, y2, y3 = s, d * r, (d * d) * s, (d * d * d) * r
                else:
                    y0, y1, y2, y3 = y0 + s, y1 + d * r, y2 + (d * d) * s, y3 + (d * d * d) * r
            b, _c = tile_nodes(t)
            bb = b * b
            terms = (y0, y1, y2, y3, b * y0, b * y1, b * y2, bb * y0, bb * y1, bb * (b * y0))
            out = [x if o is None else o + x for o, x in zip(out, terms)]
        for p in range(10):
            parts_ref[p, at_rows((first + g) * SUB), :] = out[p]
        return 0

    lax.fori_loop(0, f_ref.shape[0], cell, 0)
    return [over_sublanes(parts_ref, p) for p in range(10)]


def native_polynomial_sums(native_ref, planes):
    half, side = planes // 2, CHUNKS // 2
    zero = jnp.zeros((SUB, LANES), F32)
    acc = [zero] * 10

    def plane(a, acc):
        xa = (a.astype(F32) - 0.5 * (planes - 1)) * H
        b0 = b1 = b2 = b3 = None
        for i in range(side):
            y = (2 * i + 1) * H
            hi = native_ref[at_rows((a * CHUNKS + side + i) * SUB), :]
            lo = native_ref[at_rows((a * CHUNKS + side - 1 - i) * SUB), :]
            s, d = hi + lo, hi - lo
            terms = (s, y * d, (y * y) * s, (y * y * y) * d)
            if i == 0:
                b0, b1, b2, b3 = terms
            else:
                b0, b1, b2, b3 = b0 + terms[0], b1 + terms[1], b2 + terms[2], b3 + terms[3]
        a0, a1, a2 = xa * b0, xa * b1, xa * b2
        aa0 = xa * a0
        new = (b0, a0, aa0, xa * aa0, b1, a1, xa * a1, b2, a2, b3)
        return tuple(x + z for x, z in zip(acc, new))

    g0, a0, aa0, aaa0, g1, a1, aa1, g2, a2, g3 = lax.fori_loop(0, planes, plane, tuple(acc))
    e = (half_of(lane_iota()) - 0.5) * H
    return [
        g0,
        a0,
        aa0,
        aaa0,
        g1 + e * g0,
        a1 + e * a0,
        aa1 + e * aa0,
        g2 + e * (2.0 * g1 + e * g0),
        a2 + e * (2.0 * a1 + e * a0),
        g3 + e * (3.0 * g2 + e * (3.0 * g1 + e * g0)),
    ]


def wall_sums(f_ref, planes, links_ref, geo_ref, sums_ref, cells, faces, with_absorbed):
    sums_ref[...] = jnp.zeros_like(sums_ref)

    def wall(i, _):
        g, k = cells[i], faces[i]
        v0, v1, v2 = face_coefficients(geo_ref, k, g)
        first = splat(geo_ref, FIRST, g)
        base = []
        for t in range(TILES):
            xb, xc = tile_nodes(t)
            base.append(v1 * xb + v2 * xc)
        if with_absorbed:
            wt = splat(geo_ref, WT, g)
            shape = wall_tiles(wt)

        def plane(a, acc):
            out, back = list(acc[0]), list(acc[1])
            xa = first + a.astype(F32) * H
            sa = v0 * xa
            if with_absorbed:
                wa = jnp.exp(-0.5 * xa * xa / wt)
            for t in range(TILES):
                s = sa + base[t]
                f = f_ref[g, at_rows((a * TILES + t) * SUB), :]
                out[t] = out[t] + jnp.maximum(s, 0.0) * f
                if with_absorbed:
                    back[t] = back[t] + jnp.maximum(-s, 0.0) * (wa * shape[t])
            return tuple(out), tuple(back)

        zeros = (jnp.zeros((SUB, LANES), F32),) * TILES
        out, back = lax.fori_loop(0, planes, plane, (zeros, zeros), unroll=unroll(planes, 16))
        at = at_rows(g * SUB)
        sums_ref[k, at, :] = (out[0] + out[1]) + (out[2] + out[3])
        if with_absorbed:
            sums_ref[FACES + k, at, :] = (back[0] + back[1]) + (back[2] + back[3])
        return 0

    lax.fori_loop(0, list_faces(links_ref, is_wall, cells, faces), wall, 0)


def sums_kernel(links_ref, geo_ref, f_ref, sums_out, parts_ref, face_ref, cells, faces):
    planes = f_ref.shape[1] // CHUNKS
    y = polynomial_sums(f_ref, planes, parts_ref)
    packed = pack_sums(finish_polynomials(y, geo_ref[FIRST], planes), 0)
    wall_sums(f_ref, planes, links_ref, geo_ref, face_ref, cells, faces, False)
    sums_out[...] = packed + pack_sums([over_sublanes(face_ref, k) for k in range(FACES)], EMIT)


def first_sums_kernel(links_ref, geo_ref, native_ref, f_ref, sums_out, face_ref, cells, faces):
    rows = f_ref.shape[1]
    planes = rows // CHUNKS

    def group(j, _):
        for g in range(SUB):
            f_ref[g, at_rows(j * SUB), :] = native_ref[pl.ds(j * SUB * SUB + g, SUB, stride=SUB), :]
        return 0

    lax.fori_loop(0, rows // SUB, group, 0, unroll=2)
    y = native_polynomial_sums(native_ref, planes)
    packed = pack_sums(finish_polynomials(y, geo_ref[FIRST], planes), 0)
    wall_sums(f_ref, planes, links_ref, geo_ref, face_ref, cells, faces, True)
    sums_out[...] = packed + pack_sums([over_sublanes(face_ref, k) for k in range(2 * FACES)], EMIT)


def spec(space):
    return pl.BlockSpec(memory_space=space)


def array(*shape):
    return jax.ShapeDtypeStruct(shape, F32)


def params(mib=4):
    return pltpu.CompilerParams(vmem_limit_bytes=mib * 1024 * 1024)


def traffic(rows, profiles):
    size = SUB * rows * LANES
    return pl.CostEstimate(flops=8 * profiles * size, bytes_accessed=4 * profiles * size, transcendentals=0)


def local_sums(links, geo, f):
    return pl.pallas_call(
        sums_kernel,
        in_specs=[spec(pltpu.SMEM), spec(pltpu.VMEM), spec(pltpu.VMEM)],
        out_specs=spec(pltpu.VMEM),
        out_shape=array(SUB, LANES),
        scratch_shapes=[
                pltpu.VMEM((10, SUB * SUB, LANES), F32),
            pltpu.VMEM((FACES, SUB * SUB, LANES), F32),
            *face_lists(),
        ],
        compiler_params=params(),
        cost_estimate=traffic(f.shape[1], 4),
        name="local_sums",
    )(links, geo, f)


def first_sums(links, geo, native):
    rows = native.shape[0] // SUB
    return pl.pallas_call(
        first_sums_kernel,
        in_specs=[spec(pltpu.SMEM), spec(pltpu.VMEM), spec(pltpu.VMEM)],
        out_specs=[spec(pltpu.VMEM)] * 2,
        out_shape=[array(SUB, rows, LANES), array(SUB, LANES)],
        scratch_shapes=[
                pltpu.VMEM((2 * FACES, SUB * SUB, LANES), F32),
            *face_lists(),
        ],
        compiler_params=params(),
        cost_estimate=traffic(rows, 5),
        name="first_sums",
    )(links, geo, native)


SPLIT_PARTS = 8


def is_odd():
    return lax.rem(lax.axis_index("space"), 2) == 1


def first_rows_kernel(native_hbm, native_ref, far_any, near_any, far_ref, near_ref, sems, far_sems, near_sems):
    rows = native_ref.shape[0]
    part = rows // SPLIT_PARTS
    copies = [
        pltpu.make_async_copy(
            native_hbm.at[pl.ds(i * part, part)], native_ref.at[pl.ds(i * part, part)], sems.at[i]
        )
        for i in range(SPLIT_PARTS)
    ]
    for c in copies:
        c.start()
    odd = is_odd()
    far = jnp.where(odd, SUB - REACH, 0)
    near = jnp.where(odd, 0, SUB - REACH)
    groups = part // (SUB * SUB)
    out = []

    for i, c in enumerate(copies):
        c.wait()

        def group(j, _):
            for r in range(REACH):
                at = at_rows(j * SUB)
                far_ref[r, at, :] = native_ref[pl.ds(j * SUB * SUB + far + r, SUB, stride=SUB), :]
                near_ref[r, at, :] = native_ref[pl.ds(j * SUB * SUB + near + r, SUB, stride=SUB), :]
            return 0

        lax.fori_loop(i * groups, (i + 1) * groups, group, 0, unroll=unroll(groups, 8))
        at = pl.ds(i * groups * SUB, groups * SUB)
        out.append(pltpu.make_async_copy(far_ref.at[:, at], far_any.at[:, at], far_sems.at[i]))
        out.append(pltpu.make_async_copy(near_ref.at[:, at], near_any.at[:, at], near_sems.at[i]))
        out[-2].start()
        out[-1].start()
    for c in out:
        c.wait()


def first_rows(native):
    rows = native.shape[0] // SUB
    halo = (REACH, rows, LANES)
    return pl.pallas_call(
        first_rows_kernel,
        in_specs=[spec(pltpu.HBM)],
        out_specs=[spec(pltpu.VMEM), spec(pl.ANY), spec(pl.ANY)],
        out_shape=[array(*native.shape), array(*halo), array(*halo)],
        scratch_shapes=[pltpu.VMEM(halo, F32)] * 2 + [pltpu.SemaphoreType.DMA((SPLIT_PARTS,))] * 3,
        compiler_params=params(),
        cost_estimate=traffic(rows, 4),
        name="first_rows",
    )(pltpu.with_memory_space_constraint(native, pltpu.HBM))


def pair_weights(links_ref, geo_ref, pairs_ref, cells, faces):
    rows = pairs_ref.shape[1]
    planes = rows // CHUNKS
    first = splat(geo_ref, FIRST, 0)

    def clear(j, _):
        for p in range(pairs_ref.shape[0]):
            pairs_ref[p, at_rows(j * SUB), :] = jnp.zeros((SUB, LANES), F32)
        return 0

    lax.fori_loop(0, rows // SUB, clear, 0, unroll=4)

    def remote(i, _):
        g, k = cells[i], faces[i]
        j = links_ref[k, g]
        edge = g - (SUB - REACH)
        before = g * REACH - g * (g - 1) // 2 + (j + REACH) - g
        after = len(BEFORE_PAIRS) + edge * (edge + 1) // 2 + j - SUB
        at_pair = jnp.where(j < 0, before, after)
        scale = -TIME_STEP / splat(geo_ref, VOL, g)
        v0, v1, v2 = [scale * x for x in face_coefficients(geo_ref, k, g)]
        base = []
        for t in range(TILES):
            xb, xc = tile_nodes(t)
            base.append(v1 * xb + v2 * xc)

        def plane(a, _):
            sa = v0 * (first + a.astype(F32) * H)
            for t in range(TILES):
                at = at_rows((a * TILES + t) * SUB)
                pairs_ref[at_pair, at, :] = pairs_ref[at_pair, at, :] + jnp.maximum(sa + base[t], 0.0)
            return 0

        lax.fori_loop(0, planes, plane, 0, unroll=unroll(planes, 8))
        return 0

    lax.fori_loop(0, list_faces(links_ref, is_remote, cells, faces), remote, 0)


def gather_sums(tile):
    size = lax.axis_size("vel")
    if size not in (2, 4):
        return [lax.psum(tile, "vel")]
    others = [lax.ppermute(tile, "vel", [(i, i ^ s) for i in range(size)]) for s in range(1, size)]
    return [tile, *others]


def doubling_sums(tile):
    size = lax.axis_size("vel")
    if size != 4:
        return gather_sums(tile)
    pair = tile + lax.ppermute(tile, "vel", [(i, i ^ 1) for i in range(size)])
    return [pair, lax.ppermute(pair, "vel", [(i, i ^ 2) for i in range(size)])]


def add_tiles(refs):
    tiles = [r[...] for r in refs]
    while len(tiles) > 1:
        tiles = [tiles[i] + tiles[i + 1] for i in range(0, len(tiles), 2)]
    return tiles[0]


def quantities(tile):
    m = [WEIGHT * column(tile, p) for p in range(13)]
    n = m[0]
    rn = 1.0 / n
    u = [m[1 + i] * rn for i in range(3)]
    uu = u[0] * u[0] + u[1] * u[1] + u[2] * u[2]
    trace = m[4] + m[5] + m[6]
    width = trace - n * uu
    temperature = width * rn * (1.0 / 3.0)
    second = [[m[4], m[7], m[8]], [m[7], m[5], m[9]], [m[8], m[9], m[6]]]
    q = []
    for i in range(3):
        across = u[0] * second[i][0] + u[1] * second[i][1] + u[2] * second[i][2]
        q.append(0.5 * (m[10 + i] - 2.0 * across - u[i] * trace + 2.0 * uu * m[1 + i]))
    return n, u, temperature, q


def macro_kernel(*refs):
    out_ref = refs[-1]
    n, u, temperature, q = quantities(add_tiles(refs[:-1]))
    lane, sub = lane_iota(), sub_iota()
    for i, x in enumerate((n, *u, temperature, *q)):
        row = jnp.sum(jnp.where(lane == sub, x, 0.0), axis=0, keepdims=True)
        out_ref[pl.ds(i, 1), :] = row[:, :SUB]


def macro(tiles):
    return pl.pallas_call(
        macro_kernel,
        in_specs=[spec(pltpu.VMEM)] * len(tiles),
        out_specs=spec(pltpu.VMEM),
        out_shape=array(8, SUB),
        compiler_params=params(1),
        name="macro",
    )(*tiles)


def flux_kernel(with_pairs, links_ref, geo_ref, f_ref, out_ref, *refs):
    if with_pairs:
        pairs_ref, cells, faces = refs[0], refs[-2], refs[-1]
        pair_weights(links_ref, geo_ref, pairs_ref, cells, faces)
        refs = refs[1:-2]
    coef, bases, stays, source, face = refs
    planes = f_ref.shape[1] // CHUNKS
    scale = -TIME_STEP / geo_ref[VOL]
    for i in range(3):
        whole = None
        for k in range(FACES):
            x = scale * geo_ref[FV + FACES * i + k]
            coef[FACES * i + k] = x
            whole = x if whole is None else whole + x
        coef[3 * FACES + i] = whole

    def table(g, _):
        w = [[splat(coef, FACES * i + k, g) for i in (1, 2)] for k in range(FACES)]
        whole = [splat(coef, 3 * FACES + i, g) for i in (1, 2)]
        for t in range(TILES):
            xb, xc = tile_nodes(t)
            for k in range(FACES):
                bases[k, g * TILES + t] = w[k][0] * xb + w[k][1] * xc
            stays[g * TILES + t] = 1.0 + whole[0] * xb + whole[1] * xc
        return 0

    lax.fori_loop(0, SUB, table, 0, unroll=2)

    def cell(g, _):
        count = 0
        for k in range(FACES):
            j = links_ref[k, g]
            source[count] = j
            face[count] = k
            count = count + jnp.logical_and(j >= 0, j < SUB).astype(jnp.int32)
        for n in range(FACES + 1):

            @pl.when(count == n)
            def _():
                own_faces(g, n)

        return 0

    def own_faces(g, n):
        at_source = [source[i] for i in range(n)]
        first_weight = [splat(coef, face[k], g) for k in range(n)]
        whole = splat(coef, 3 * FACES, g)
        x0 = splat(geo_ref, FIRST, g)
        base = [[bases[face[k], g * TILES + t] for k in range(n)] for t in range(TILES)]
        stay = [stays[g * TILES + t] for t in range(TILES)]

        def plane(a, _):
            xa = x0 + a.astype(F32) * H
            sa = [w * xa for w in first_weight]
            stay_a = whole * xa
            for t in range(TILES):
                at = at_rows((a * TILES + t) * SUB)
                f = f_ref[g, at, :]
                acc = f * (stay_a + stay[t])
                for k in range(n):
                    acc = acc + jnp.maximum(sa[k] + base[t][k], 0.0) * (f_ref[at_source[k], at, :] - f)
                out_ref[g, at, :] = acc
            return 0

        lax.fori_loop(0, planes, plane, 0, unroll=unroll(planes, 8))

    lax.fori_loop(0, SUB, cell, 0)


def flux(with_pairs, links, geo, f):
    rows = f.shape[1]
    pairs = 2 * len(BEFORE_PAIRS)
    return pl.pallas_call(
        functools.partial(flux_kernel, with_pairs),
        in_specs=[spec(pltpu.SMEM), spec(pltpu.VMEM), spec(pltpu.VMEM)],
        out_specs=[spec(pltpu.VMEM)] * (2 if with_pairs else 1),
        out_shape=[array(*f.shape)] + ([array(pairs, rows, LANES)] if with_pairs else []),
        scratch_shapes=[
            pltpu.VMEM((3 * FACES + 3, SUB, LANES), F32),
            pltpu.VMEM((FACES, SUB * TILES, SUB, LANES), F32),
            pltpu.VMEM((SUB * TILES, SUB, LANES), F32),
            pltpu.SMEM((FACES + 1,), jnp.int32),
            pltpu.SMEM((FACES + 1,), jnp.int32),
        ]
        + (face_lists() if with_pairs else []),
        compiler_params=params(),
        cost_estimate=traffic(rows, 9 if with_pairs else 7),
        name="flux",
    )(links, geo, f)


def target_kernel(count, links_ref, geo_ref, absorbed_in, *refs):
    sums_refs, (f_ref, part_ref, out_ref, *sum_out, ta, tiles_ref, coef, cells, faces) = refs[:count], refs[count:]
    planes = f_ref.shape[1] // CHUNKS
    sums = add_tiles(sums_refs)
    for ref in sum_out:
        ref[...] = sums
    absorbed = sums if absorbed_in is None else absorbed_in[...]
    n, u, temperature, q = quantities(sums)
    rt = 1.0 / temperature
    rate = TIME_STEP * n * temperature / (SHEAR * jnp.exp(POWER * jnp.log(temperature)))
    height = rate * n * rt * jnp.sqrt(rt)
    slope = (1.0 / 3.0) / (5.0 * n * temperature * temperature)
    coef[0] = rate
    coef[1] = rt
    coef[2], coef[3] = u[1], u[2]
    coef[4], coef[5] = slope * q[1], slope * q[2]
    for k in range(FACES):
        wall = geo_ref[WALL + k] > 0.5
        coef[6 + k] = column(sums, EMIT + k) / jnp.where(wall, column(absorbed, ABSORB + k), 1.0)
    first = geo_ref[FIRST]

    wt = geo_ref[WT]

    def plane_table(a, _):
        xa = first + a.astype(F32) * H
        ca = xa - u[0]
        za = ca * ca * rt
        ta[0, a] = height * jnp.exp(-0.5 * za)
        ta[1, a] = slope * q[0] * ca
        ta[2, a] = za - 5.0
        ta[3, a] = jnp.exp(-0.5 * xa * xa / wt)
        return 0

    lax.fori_loop(0, planes, plane_table, 0, unroll=unroll(planes, 8))

    def tile_table(g, _):
        rtg = splat(coef, 1, g)
        ub, uc = splat(coef, 2, g), splat(coef, 3, g)
        qb, qc = splat(coef, 4, g), splat(coef, 5, g)
        shape = wall_tiles(splat(geo_ref, WT, g))
        for t in range(TILES):
            xb, xc = tile_nodes(t)
            cb, cc = xb - ub, xc - uc
            z = (cb * cb + cc * cc) * rtg
            at = g * TILES + t
            tiles_ref[0, at] = jnp.exp(-0.5 * z)
            tiles_ref[1, at] = cb * qb + cc * qc
            tiles_ref[2, at] = z
            tiles_ref[3, at] = shape[t]
        return 0

    lax.fori_loop(0, SUB, tile_table, 0, unroll=4)

    def at_plane(i, a, g):
        return jnp.broadcast_to(ta[i, a, pl.ds(g, 1), :], (SUB, LANES))

    def cell(g, _):
        rate_g = splat(coef, 0, g)
        bell, heat, zz = [[tiles_ref[i, g * TILES + t] for t in range(TILES)] for i in range(3)]

        def plane(a, _):
            height_a, heat_a, z_a = [at_plane(i, a, g) for i in range(3)]
            for t in range(TILES):
                where = (g, at_rows((a * TILES + t) * SUB), slice(None))
                f = f_ref[where]
                target = (height_a * bell[t]) * (1.0 + (heat_a + heat[t]) * (z_a + zz[t]))
                out_ref[where] = (part_ref[where] - rate_g * f) + target
            return 0

        lax.fori_loop(0, planes, plane, 0, unroll=unroll(planes, 16))
        return 0

    lax.fori_loop(0, SUB, cell, 0)

    def wall(i, _):
        g, k = cells[i], faces[i]
        x0 = splat(geo_ref, FIRST, g)
        ratio = splat(coef, 6 + k, g)
        scale = -TIME_STEP / splat(geo_ref, VOL, g)
        v0, v1, v2 = [scale * x for x in face_coefficients(geo_ref, k, g)]
        base, shape = [], []
        for t in range(TILES):
            xb, xc = tile_nodes(t)
            base.append(v1 * xb + v2 * xc)
            shape.append(ratio * tiles_ref[3, g * TILES + t])

        def plane(a, _):
            wa = at_plane(3, a, g)
            sa = v0 * (x0 + a.astype(F32) * H)
            for t in range(TILES):
                where = (g, at_rows((a * TILES + t) * SUB), slice(None))
                f = f_ref[where]
                out_ref[where] = out_ref[where] + jnp.maximum(sa + base[t], 0.0) * (wa * shape[t] - f)
            return 0

        lax.fori_loop(0, planes, plane, 0, unroll=unroll(planes, 16))
        return 0

    lax.fori_loop(0, list_faces(links_ref, is_wall, cells, faces), wall, 0)


def add_target(links, geo, absorbed, tiles, f, part):
    rows = f.shape[1]
    vmem = spec(pltpu.VMEM)
    given = [links, geo] + ([] if absorbed is None else [absorbed]) + list(tiles) + [f, part]

    def kernel(links_ref, geo_in, *refs):
        if absorbed is None:
            target_kernel(len(tiles), links_ref, geo_in, None, *refs)
        else:
            target_kernel(len(tiles), links_ref, geo_in, *refs)

    return pl.pallas_call(
        kernel,
        in_specs=[spec(pltpu.SMEM)] + [vmem] * (len(given) - 1),
        out_specs=[vmem] * (2 if absorbed is None else 1),
        out_shape=[array(*part.shape)] + ([array(SUB, LANES)] if absorbed is None else []),
        input_output_aliases={len(given) - 1: 0},
        scratch_shapes=[
                pltpu.VMEM((4, rows // CHUNKS, SUB, LANES), F32),
            pltpu.VMEM((4, SUB * TILES, SUB, LANES), F32),
            pltpu.VMEM((6 + FACES, SUB, LANES), F32),
            *face_lists(),
        ],
        compiler_params=params(),
        cost_estimate=traffic(rows, 7),
        name="add_target",
    )(*given)


def side_terms(high, pairs_ref, halo_ref, f_ref, at):
    terms = [None] * REACH
    rows = [halo_ref[r, at, :] for r in range(REACH)]
    first = SUB - REACH if high else 0
    own = [f_ref[first + e, at, :] for e in range(REACH)]
    count = len(BEFORE_PAIRS)
    pairs = [(e, r) for e in range(REACH) for r in range(e + 1)] if high else BEFORE_PAIRS
    for p, (e, r) in enumerate(pairs):
        term = pairs_ref[p + count if high else p, at, :] * (rows[r] - own[e])
        terms[e] = term if terms[e] is None else terms[e] + term
    return first, terms


def for_side(far, run):
    odd = is_odd()

    @pl.when(odd)
    def _():
        run(far)

    @pl.when(jnp.logical_not(odd))
    def _():
        run(not far)


def add_side(far, pairs_ref, halo_ref, old_ref, part_ref, f_ref, rows_ref):
    def run(high):
        def group(j, _):
            at = at_rows(j * SUB)
            first, terms = side_terms(high, pairs_ref, halo_ref, old_ref, at)
            for e in range(REACH):
                x = part_ref[first + e, at, :] + terms[e]
                f_ref[first + e, at, :] = x
                if rows_ref is not None:
                    rows_ref[e, at, :] = x
            return 0

        groups = part_ref.shape[1] // SUB
        lax.fori_loop(0, groups, group, 0, unroll=unroll(groups, 8))

    for_side(far, run)


def edge(far, pairs, halo, old, part):
    rows = part.shape[1]
    return pl.pallas_call(
        functools.partial(add_side, far),
        in_specs=[spec(pltpu.VMEM)] * 4,
        out_specs=[spec(pltpu.VMEM)] * 2,
        out_shape=[array(SUB, rows, LANES), array(REACH, rows, LANES)],
        input_output_aliases={3: 0},
        compiler_params=params(),
        cost_estimate=traffic(rows, 2),
        name="far_edge" if far else "near_edge",
    )(pairs, halo, old, part)


def last_near_kernel(geo_ref, pairs_ref, halo_ref, old_ref, part_ref, f_ref, sums_out, parts_ref):
    add_side(False, pairs_ref, halo_ref, old_ref, part_ref, f_ref, None)
    planes = f_ref.shape[1] // CHUNKS
    y = polynomial_sums(f_ref, planes, parts_ref)
    sums_out[...] = pack_sums(finish_polynomials(y, geo_ref[FIRST], planes), 0)


def last_near(geo, pairs, near, old, part):
    rows = part.shape[1]
    return pl.pallas_call(
        last_near_kernel,
        in_specs=[spec(pltpu.VMEM)] * 5,
        out_specs=[spec(pltpu.VMEM)] * 2,
        out_shape=[array(SUB, rows, LANES), array(SUB, LANES)],
        input_output_aliases={4: 0},
        scratch_shapes=[pltpu.VMEM((10, SUB * SUB, LANES), F32)],
        compiler_params=params(),
        cost_estimate=traffic(rows, 3),
        name="last_near",
    )(geo, pairs, near, old, part)


def last_far_kernel(geo_ref, pairs_ref, halo_ref, old_ref, sums_in, terms_ref, sums_out, parts_ref):
    rows = old_ref.shape[1]
    planes = rows // CHUNKS
    parts_ref[...] = jnp.zeros_like(parts_ref)

    def run(high):
        def group(j, _):
            at = at_rows(j * SUB)
            _first, terms = side_terms(high, pairs_ref, halo_ref, old_ref, at)
            for e in range(REACH):
                terms_ref[e, at, :] = terms[e]
            return 0

        lax.fori_loop(0, rows // SUB, group, 0, unroll=unroll(rows // SUB, 8))
        y = polynomial_sums(terms_ref, planes, parts_ref, SUB - REACH if high else 0)
        sums_out[...] = sums_in[...] + pack_sums(finish_polynomials(y, geo_ref[FIRST], planes), 0)

    for_side(True, run)


def last_far(geo, pairs, far, old, sums):
    rows = old.shape[1]
    return pl.pallas_call(
        last_far_kernel,
        in_specs=[spec(pltpu.VMEM)] * 5,
        out_specs=[spec(pltpu.VMEM)] * 2,
        out_shape=[array(REACH, rows, LANES), array(SUB, LANES)],
        scratch_shapes=[pltpu.VMEM((10, SUB * SUB, LANES), F32)],
        compiler_params=params(),
        cost_estimate=traffic(rows, 2),
        name="last_far",
    )(geo, pairs, far, old, sums)


LAST_PARTS = 4


def result_kernel(part_ref, terms_ref, out_hbm, native_ref, sems):
    part = part_ref.shape[1] // SUB // LAST_PARTS

    def copy(i):
        at = pl.ds(i * part * SUB * SUB, part * SUB * SUB)
        return pltpu.make_async_copy(native_ref.at[at], out_hbm.at[at], sems.at[i])

    def run(high):
        first = SUB - REACH if high else 0
        for i in range(LAST_PARTS):

            def group(j, _):
                at = at_rows(j * SUB)
                for g in range(SUB):
                    x = part_ref[g, at, :]
                    if 0 <= g - first < REACH:
                        x = x + terms_ref[g - first, at, :]
                    native_ref[pl.ds(j * SUB * SUB + g, SUB, stride=SUB), :] = x
                return 0

            lax.fori_loop(i * part, (i + 1) * part, group, 0, unroll=unroll(part, 4))
            copy(i).start()

    for_side(True, run)
    for i in range(LAST_PARTS):
        copy(i).wait()


def result(part, terms):
    rows = part.shape[1]
    native = (SUB * rows, LANES)
    return pl.pallas_call(
        result_kernel,
        in_specs=[spec(pltpu.VMEM)] * 2,
        out_specs=spec(pltpu.HBM),
        out_shape=array(*native),
        scratch_shapes=[pltpu.VMEM(native, F32), pltpu.SemaphoreType.DMA((LAST_PARTS,))],
        compiler_params=params(),
        cost_estimate=traffic(rows, 3),
        name="result",
    )(part, terms)


def swap(rows, start):
    pairs = [(i, i + 1) for i in range(start, lax.axis_size("space") - 1, 2)]
    return lax.ppermute(rows, "space", pairs + [(j, i) for i, j in pairs])


def per_device(particle_profile, neighbors, face_vectors, volumes, wall_temp):
    cells, points = particle_profile.shape
    rows = points // LANES
    plane_count = NV // lax.axis_size("vel")
    native = particle_profile.reshape(cells, rows, LANES).transpose(1, 0, 2).reshape(cells * rows, LANES)
    wall = neighbors < 0
    links = jnp.where(wall, WALL_LINK, neighbors - lax.axis_index("space") * cells)
    own = (links >= 0) & (links < cells)
    first = -SPEED_LIMIT + ((lax.axis_index("vel") * plane_count).astype(F32) + 0.5) * H
    geo = jnp.concatenate(
        [
            face_vectors.reshape(3 * FACES, cells),
            volumes[None],
            wall_temp[None],
            wall.astype(F32),
            own.astype(F32),
            jnp.full((1, cells), first, F32),
        ]
    )
    geo = jnp.broadcast_to(geo[:, :, None], (GEO, cells, LANES))
    native, far, near = first_rows(native)
    far, near = swap(far, 1), swap(near, 0)
    f, sums = first_sums(links, geo, native)
    tiles = gather_sums(sums)
    part, pairs = flux(True, links, geo, f)
    part, absorbed = add_target(links, geo, None, tiles, f, part)
    part, near = edge(False, pairs, near, f, part)
    near = swap(near, 0)
    f, far = edge(True, pairs, far, f, part)
    far = swap(far, 1)
    tiles = gather_sums(local_sums(links, geo, f))
    (part,) = flux(False, links, geo, f)
    (part,) = add_target(links, geo, absorbed, tiles, f, part)
    part, sums = last_near(geo, pairs, near, f, part)
    terms, sums = last_far(geo, pairs, far, f, sums)
    tiles = doubling_sums(sums)
    native = result(part, terms)
    macro_quantities = macro(tiles)
    evolved = native.reshape(rows, cells, LANES).transpose(1, 0, 2).reshape(cells, points)
    return evolved, macro_quantities


def solution(mesh):
    return jax.shard_map(
        per_device,
        mesh=mesh,
        in_specs=(
            P("space", "vel"),
            P(None, "space"),
            P(None, None, "space"),
            P("space"),
            P("space"),
        ),
        out_specs=(P("space", "vel"), P(None, "space")),
        check_vma=False,
    )
```

```python
import functools
import math

import jax
import jax.numpy as jnp
from jax import lax
from jax.experimental import pallas as pl
from jax.experimental.pallas import tpu as pltpu
from jax.sharding import PartitionSpec as P

NV = 64
FACES = 6
REACH = 3
STEPS = 2
LANES = 128
SUB = 8

TIME_STEP = 0.015
SHEAR = 0.1
POWER = 0.81
SPEED_LIMIT = 6.0
H = 2.0 * SPEED_LIMIT / NV
WEIGHT = H**3 * (2.0 * math.pi) ** (-1.5)

CHUNKS = NV * NV // LANES
TILES = CHUNKS // SUB

FV, VOL, WT, WALL, LOCAL, FIRST = 0, 18, 19, 20, 26, 32
GEO = 33
WALL_LINK = -64
BEFORE_PAIRS = tuple((g, r) for g in range(REACH) for r in range(g, REACH))
EMIT, ABSORB = 13, 19
SUMS = 25

F32 = jnp.float32


def lane_iota():
    return lax.broadcasted_iota(jnp.int32, (SUB, LANES), 1)


def sub_iota():
    return lax.broadcasted_iota(jnp.int32, (SUB, LANES), 0)


def half_of(lane):
    return (lane >= NV).astype(F32)


def third_component(lane):
    c = jnp.where(lane >= NV, lane - NV, lane).astype(F32)
    return -SPEED_LIMIT + (c + 0.5) * H


def tile_nodes(t):
    lane = lane_iota()
    b = (2 * SUB * t + 2 * sub_iota()).astype(F32) + half_of(lane)
    return -SPEED_LIMIT + (b + 0.5) * H, third_component(lane)


def column(tile, p):
    return jnp.broadcast_to(tile[:, p : p + 1], (SUB, LANES))


def splat(ref, i, g):
    return jnp.broadcast_to(ref[i, pl.ds(g, 1), :], (SUB, LANES))


def total(tile):
    return jnp.broadcast_to(jnp.sum(tile, axis=1, keepdims=True), (SUB, LANES))


def face_coefficients(geo_ref, k, g):
    return [splat(geo_ref, FV + FACES * i + k, g) for i in range(3)]


def at_rows(start, size=SUB):
    return pl.ds(pl.multiple_of(start, SUB), size)


def wall_tiles(wall_temp):
    rt = 1.0 / wall_temp
    scale = rt * jnp.sqrt(rt)
    out = []
    for t in range(TILES):
        xb, xc = tile_nodes(t)
        out.append(scale * jnp.exp(-0.5 * (xb * xb + xc * xc) * rt))
    return out


def pack_sums(arrays, start):
    lane = lane_iota()
    out = jnp.zeros((SUB, LANES), F32)
    for p, x in enumerate(arrays):
        out = jnp.where(lane == start + p, total(x), out)
    return out


def over_sublanes(ref, k):
    out = ref[k, pl.ds(0, SUB, stride=SUB), :]
    for s in range(1, SUB):
        out = out + ref[k, pl.ds(s, SUB, stride=SUB), :]
    return out


def list_faces(links_ref, wanted, cell_ref, face_ref):
    count = 0
    for g in range(SUB):
        for k in range(FACES):
            cell_ref[count] = g
            face_ref[count] = k
            count = count + wanted(links_ref[k, g]).astype(jnp.int32)
    return count


def is_wall(j):
    return j == WALL_LINK


def is_remote(j):
    return jnp.logical_or(j >= SUB, jnp.logical_and(j < 0, j != WALL_LINK))


def face_lists():
    return [pltpu.SMEM((FACES * SUB + 1,), jnp.int32)] * 2


def unroll(planes, most):
    return math.gcd(planes, most)


def finish_polynomials(y, first, planes):
    y0, y1, y2, y3, by0, by1, by2, bby0, bby1, bbby0 = y
    m = first + 0.5 * (planes - 1) * H
    c = third_component(lane_iota())
    cc = c * c
    a = y1 + m * y0
    aa = y2 + m * (2.0 * y1 + m * y0)
    aaa = y3 + m * (3.0 * y2 + m * (3.0 * y1 + m * y0))
    ab = by1 + m * by0
    aab = by2 + m * (2.0 * by1 + m * by0)
    abb = bby1 + m * bby0
    return (
        y0,
        a,
        by0,
        c * y0,
        aa,
        bby0,
        cc * y0,
        ab,
        c * a,
        c * by0,
        aaa + abb + cc * a,
        aab + bbby0 + cc * by0,
        c * (aa + bby0 + cc * y0),
    )


def polynomial_sums(f_ref, planes, parts_ref, first=0):
    half = planes // 2

    def cell(g, _):
        out = [None] * 10
        for t in range(TILES):
            y0 = y1 = y2 = y3 = None
            for i in range(half):
                d = (i + 0.5) * H
                hi = f_ref[g, pl.ds(((half + i) * TILES + t) * SUB, SUB), :]
                lo = f_ref[g, pl.ds(((half - 1 - i) * TILES + t) * SUB, SUB), :]
                s, r = hi + lo, hi - lo
                if i == 0:
                    y0, y1, y2, y3 = s, d * r, (d * d) * s, (d * d * d) * r
                else:
                    y0, y1, y2, y3 = y0 + s, y1 + d * r, y2 + (d * d) * s, y3 + (d * d * d) * r
            b, _c = tile_nodes(t)
            bb = b * b
            terms = (y0, y1, y2, y3, b * y0, b * y1, b * y2, bb * y0, bb * y1, bb * (b * y0))
            out = [x if o is None else o + x for o, x in zip(out, terms)]
        for p in range(10):
            parts_ref[p, at_rows((first + g) * SUB), :] = out[p]
        return 0

    lax.fori_loop(0, f_ref.shape[0], cell, 0)
    return [over_sublanes(parts_ref, p) for p in range(10)]


def native_polynomial_sums(native_ref, planes):
    half, side = planes // 2, CHUNKS // 2
    zero = jnp.zeros((SUB, LANES), F32)
    acc = [zero] * 10

    def plane(a, acc):
        xa = (a.astype(F32) - 0.5 * (planes - 1)) * H
        b0 = b1 = b2 = b3 = None
        for i in range(side):
            y = (2 * i + 1) * H
            hi = native_ref[at_rows((a * CHUNKS + side + i) * SUB), :]
            lo = native_ref[at_rows((a * CHUNKS + side - 1 - i) * SUB), :]
            s, d = hi + lo, hi - lo
            terms = (s, y * d, (y * y) * s, (y * y * y) * d)
            if i == 0:
                b0, b1, b2, b3 = terms
            else:
                b0, b1, b2, b3 = b0 + terms[0], b1 + terms[1], b2 + terms[2], b3 + terms[3]
        a0, a1, a2 = xa * b0, xa * b1, xa * b2
        aa0 = xa * a0
        new = (b0, a0, aa0, xa * aa0, b1, a1, xa * a1, b2, a2, b3)
        return tuple(x + z for x, z in zip(acc, new))

    g0, a0, aa0, aaa0, g1, a1, aa1, g2, a2, g3 = lax.fori_loop(0, planes, plane, tuple(acc))
    e = (half_of(lane_iota()) - 0.5) * H
    return [
        g0,
        a0,
        aa0,
        aaa0,
        g1 + e * g0,
        a1 + e * a0,
        aa1 + e * aa0,
        g2 + e * (2.0 * g1 + e * g0),
        a2 + e * (2.0 * a1 + e * a0),
        g3 + e * (3.0 * g2 + e * (3.0 * g1 + e * g0)),
    ]


def wall_sums(f_ref, planes, links_ref, geo_ref, sums_ref, cells, faces, with_absorbed):
    sums_ref[...] = jnp.zeros_like(sums_ref)

    def wall(i, _):
        g, k = cells[i], faces[i]
        v0, v1, v2 = face_coefficients(geo_ref, k, g)
        first = splat(geo_ref, FIRST, g)
        base = []
        for t in range(TILES):
            xb, xc = tile_nodes(t)
            base.append(v1 * xb + v2 * xc)
        if with_absorbed:
            wt = splat(geo_ref, WT, g)
            shape = wall_tiles(wt)

        def plane(a, acc):
            out, back = list(acc[0]), list(acc[1])
            xa = first + a.astype(F32) * H
            sa = v0 * xa
            if with_absorbed:
                wa = jnp.exp(-0.5 * xa * xa / wt)
            for t in range(TILES):
                s = sa + base[t]
                f = f_ref[g, at_rows((a * TILES + t) * SUB), :]
                out[t] = out[t] + jnp.maximum(s, 0.0) * f
                if with_absorbed:
                    back[t] = back[t] + jnp.maximum(-s, 0.0) * (wa * shape[t])
            return tuple(out), tuple(back)

        zeros = (jnp.zeros((SUB, LANES), F32),) * TILES
        out, back = lax.fori_loop(0, planes, plane, (zeros, zeros), unroll=unroll(planes, 16))
        at = at_rows(g * SUB)
        sums_ref[k, at, :] = (out[0] + out[1]) + (out[2] + out[3])
        if with_absorbed:
            sums_ref[FACES + k, at, :] = (back[0] + back[1]) + (back[2] + back[3])
        return 0

    lax.fori_loop(0, list_faces(links_ref, is_wall, cells, faces), wall, 0)


def sums_kernel(links_ref, geo_ref, f_ref, sums_out, parts_ref, face_ref, cells, faces):
    planes = f_ref.shape[1] // CHUNKS
    y = polynomial_sums(f_ref, planes, parts_ref)
    packed = pack_sums(finish_polynomials(y, geo_ref[FIRST], planes), 0)
    wall_sums(f_ref, planes, links_ref, geo_ref, face_ref, cells, faces, False)
    sums_out[...] = packed + pack_sums([over_sublanes(face_ref, k) for k in range(FACES)], EMIT)


def first_sums_kernel(links_ref, geo_ref, native_ref, f_ref, sums_out, face_ref, cells, faces):
    rows = f_ref.shape[1]
    planes = rows // CHUNKS

    def group(j, _):
        for g in range(SUB):
            f_ref[g, at_rows(j * SUB), :] = native_ref[pl.ds(j * SUB * SUB + g, SUB, stride=SUB), :]
        return 0

    lax.fori_loop(0, rows // SUB, group, 0, unroll=2)
    y = native_polynomial_sums(native_ref, planes)
    packed = pack_sums(finish_polynomials(y, geo_ref[FIRST], planes), 0)
    wall_sums(f_ref, planes, links_ref, geo_ref, face_ref, cells, faces, True)
    sums_out[...] = packed + pack_sums([over_sublanes(face_ref, k) for k in range(2 * FACES)], EMIT)


def spec(space):
    return pl.BlockSpec(memory_space=space)


def array(*shape):
    return jax.ShapeDtypeStruct(shape, F32)


def params(mib=4):
    return pltpu.CompilerParams(vmem_limit_bytes=mib * 1024 * 1024)


def traffic(rows, profiles):
    size = SUB * rows * LANES
    return pl.CostEstimate(flops=8 * profiles * size, bytes_accessed=4 * profiles * size, transcendentals=0)


def local_sums(links, geo, f):
    return pl.pallas_call(
        sums_kernel,
        in_specs=[spec(pltpu.SMEM), spec(pltpu.VMEM), spec(pltpu.VMEM)],
        out_specs=spec(pltpu.VMEM),
        out_shape=array(SUB, LANES),
        scratch_shapes=[
                pltpu.VMEM((10, SUB * SUB, LANES), F32),
            pltpu.VMEM((FACES, SUB * SUB, LANES), F32),
            *face_lists(),
        ],
        compiler_params=params(),
        cost_estimate=traffic(f.shape[1], 4),
        name="local_sums",
    )(links, geo, f)


def first_sums(links, geo, native):
    rows = native.shape[0] // SUB
    return pl.pallas_call(
        first_sums_kernel,
        in_specs=[spec(pltpu.SMEM), spec(pltpu.VMEM), spec(pltpu.VMEM)],
        out_specs=[spec(pltpu.VMEM)] * 2,
        out_shape=[array(SUB, rows, LANES), array(SUB, LANES)],
        scratch_shapes=[
                pltpu.VMEM((2 * FACES, SUB * SUB, LANES), F32),
            *face_lists(),
        ],
        compiler_params=params(),
        cost_estimate=traffic(rows, 5),
        name="first_sums",
    )(links, geo, native)


def is_odd():
    return lax.rem(lax.axis_index("space"), 2) == 1


def first_rows_kernel(native_hbm, native_ref, far_any, near_any, sem, far_sems, near_sems):
    whole = pltpu.make_async_copy(native_hbm, native_ref, sem)

    def copies(far, near):
        out = []
        for r in range(REACH):
            out.append(pltpu.make_async_copy(native_hbm.at[:, far + r, :], far_any.at[r], far_sems.at[r]))
            out.append(pltpu.make_async_copy(native_hbm.at[:, near + r, :], near_any.at[r], near_sems.at[r]))
        return out

    odd = is_odd()

    @pl.when(odd)
    def _():
        for c in copies(SUB - REACH, 0):
            c.start()

    @pl.when(jnp.logical_not(odd))
    def _():
        for c in copies(0, SUB - REACH):
            c.start()

    whole.start()
    for c in copies(0, SUB - REACH):
        c.wait()
    whole.wait()


def first_rows(native):
    rows = native.shape[0]
    halo = (REACH, rows, LANES)
    return pl.pallas_call(
        first_rows_kernel,
        in_specs=[spec(pltpu.HBM)],
        out_specs=[spec(pltpu.VMEM), spec(pl.ANY), spec(pl.ANY)],
        out_shape=[array(*native.shape), array(*halo), array(*halo)],
        scratch_shapes=[pltpu.SemaphoreType.DMA] + [pltpu.SemaphoreType.DMA((REACH,))] * 2,
        compiler_params=params(),
        cost_estimate=traffic(rows, 4),
        name="first_rows",
    )(pltpu.with_memory_space_constraint(native, pltpu.HBM))


def pair_weights(links_ref, geo_ref, pairs_ref, cells, faces):
    rows = pairs_ref.shape[1]
    planes = rows // CHUNKS
    first = splat(geo_ref, FIRST, 0)

    def clear(j, _):
        for p in range(pairs_ref.shape[0]):
            pairs_ref[p, at_rows(j * SUB), :] = jnp.zeros((SUB, LANES), F32)
        return 0

    lax.fori_loop(0, rows // SUB, clear, 0, unroll=4)

    def remote(i, _):
        g, k = cells[i], faces[i]
        j = links_ref[k, g]
        edge = g - (SUB - REACH)
        before = g * REACH - g * (g - 1) // 2 + (j + REACH) - g
        after = len(BEFORE_PAIRS) + edge * (edge + 1) // 2 + j - SUB
        at_pair = jnp.where(j < 0, before, after)
        scale = -TIME_STEP / splat(geo_ref, VOL, g)
        v0, v1, v2 = [scale * x for x in face_coefficients(geo_ref, k, g)]
        base = []
        for t in range(TILES):
            xb, xc = tile_nodes(t)
            base.append(v1 * xb + v2 * xc)

        def plane(a, _):
            sa = v0 * (first + a.astype(F32) * H)
            for t in range(TILES):
                at = at_rows((a * TILES + t) * SUB)
                pairs_ref[at_pair, at, :] = pairs_ref[at_pair, at, :] + jnp.maximum(sa + base[t], 0.0)
            return 0

        lax.fori_loop(0, planes, plane, 0, unroll=unroll(planes, 8))
        return 0

    lax.fori_loop(0, list_faces(links_ref, is_remote, cells, faces), remote, 0)


def gather_sums(tile):
    size = lax.axis_size("vel")
    if size not in (2, 4):
        return [lax.psum(tile, "vel")]
    others = [lax.ppermute(tile, "vel", [(i, i ^ s) for i in range(size)]) for s in range(1, size)]
    return [tile, *others]


def doubling_sums(tile):
    size = lax.axis_size("vel")
    if size != 4:
        return gather_sums(tile)
    pair = tile + lax.ppermute(tile, "vel", [(i, i ^ 1) for i in range(size)])
    return [pair, lax.ppermute(pair, "vel", [(i, i ^ 2) for i in range(size)])]


def add_tiles(refs):
    tiles = [r[...] for r in refs]
    while len(tiles) > 1:
        tiles = [tiles[i] + tiles[i + 1] for i in range(0, len(tiles), 2)]
    return tiles[0]


def quantities(tile):
    m = [WEIGHT * column(tile, p) for p in range(13)]
    n = m[0]
    rn = 1.0 / n
    u = [m[1 + i] * rn for i in range(3)]
    uu = u[0] * u[0] + u[1] * u[1] + u[2] * u[2]
    trace = m[4] + m[5] + m[6]
    width = trace - n * uu
    temperature = width * rn * (1.0 / 3.0)
    second = [[m[4], m[7], m[8]], [m[7], m[5], m[9]], [m[8], m[9], m[6]]]
    q = []
    for i in range(3):
        across = u[0] * second[i][0] + u[1] * second[i][1] + u[2] * second[i][2]
        q.append(0.5 * (m[10 + i] - 2.0 * across - u[i] * trace + 2.0 * uu * m[1 + i]))
    return n, u, temperature, q


def macro_kernel(*refs):
    out_ref = refs[-1]
    n, u, temperature, q = quantities(add_tiles(refs[:-1]))
    lane, sub = lane_iota(), sub_iota()
    for i, x in enumerate((n, *u, temperature, *q)):
        row = jnp.sum(jnp.where(lane == sub, x, 0.0), axis=0, keepdims=True)
        out_ref[pl.ds(i, 1), :] = row[:, :SUB]


def macro(tiles):
    return pl.pallas_call(
        macro_kernel,
        in_specs=[spec(pltpu.VMEM)] * len(tiles),
        out_specs=spec(pltpu.VMEM),
        out_shape=array(8, SUB),
        compiler_params=params(1),
        name="macro",
    )(*tiles)


def flux_kernel(with_pairs, links_ref, geo_ref, f_ref, out_ref, *refs):
    if with_pairs:
        pairs_ref, cells, faces = refs[0], refs[-2], refs[-1]
        pair_weights(links_ref, geo_ref, pairs_ref, cells, faces)
        refs = refs[1:-2]
    coef, bases, stays, source, face = refs
    planes = f_ref.shape[1] // CHUNKS
    scale = -TIME_STEP / geo_ref[VOL]
    for i in range(3):
        whole = None
        for k in range(FACES):
            x = scale * geo_ref[FV + FACES * i + k]
            coef[FACES * i + k] = x
            whole = x if whole is None else whole + x
        coef[3 * FACES + i] = whole

    def table(g, _):
        w = [[splat(coef, FACES * i + k, g) for i in (1, 2)] for k in range(FACES)]
        whole = [splat(coef, 3 * FACES + i, g) for i in (1, 2)]
        for t in range(TILES):
            xb, xc = tile_nodes(t)
            for k in range(FACES):
                bases[k, g * TILES + t] = w[k][0] * xb + w[k][1] * xc
            stays[g * TILES + t] = 1.0 + whole[0] * xb + whole[1] * xc
        return 0

    lax.fori_loop(0, SUB, table, 0, unroll=2)

    def cell(g, _):
        count = 0
        for k in range(FACES):
            j = links_ref[k, g]
            source[count] = j
            face[count] = k
            count = count + jnp.logical_and(j >= 0, j < SUB).astype(jnp.int32)
        for n in range(FACES + 1):

            @pl.when(count == n)
            def _():
                own_faces(g, n)

        return 0

    def own_faces(g, n):
        at_source = [source[i] for i in range(n)]
        first_weight = [splat(coef, face[k], g) for k in range(n)]
        whole = splat(coef, 3 * FACES, g)
        x0 = splat(geo_ref, FIRST, g)
        base = [[bases[face[k], g * TILES + t] for k in range(n)] for t in range(TILES)]
        stay = [stays[g * TILES + t] for t in range(TILES)]

        def plane(a, _):
            xa = x0 + a.astype(F32) * H
            sa = [w * xa for w in first_weight]
            stay_a = whole * xa
            for t in range(TILES):
                at = at_rows((a * TILES + t) * SUB)
                f = f_ref[g, at, :]
                acc = f * (stay_a + stay[t])
                for k in range(n):
                    acc = acc + jnp.maximum(sa[k] + base[t][k], 0.0) * (f_ref[at_source[k], at, :] - f)
                out_ref[g, at, :] = acc
            return 0

        lax.fori_loop(0, planes, plane, 0, unroll=unroll(planes, 8))

    lax.fori_loop(0, SUB, cell, 0)


def flux(with_pairs, links, geo, f):
    rows = f.shape[1]
    pairs = 2 * len(BEFORE_PAIRS)
    return pl.pallas_call(
        functools.partial(flux_kernel, with_pairs),
        in_specs=[spec(pltpu.SMEM), spec(pltpu.VMEM), spec(pltpu.VMEM)],
        out_specs=[spec(pltpu.VMEM)] * (2 if with_pairs else 1),
        out_shape=[array(*f.shape)] + ([array(pairs, rows, LANES)] if with_pairs else []),
        scratch_shapes=[
            pltpu.VMEM((3 * FACES + 3, SUB, LANES), F32),
            pltpu.VMEM((FACES, SUB * TILES, SUB, LANES), F32),
            pltpu.VMEM((SUB * TILES, SUB, LANES), F32),
            pltpu.SMEM((FACES + 1,), jnp.int32),
            pltpu.SMEM((FACES + 1,), jnp.int32),
        ]
        + (face_lists() if with_pairs else []),
        compiler_params=params(),
        cost_estimate=traffic(rows, 9 if with_pairs else 7),
        name="flux",
    )(links, geo, f)


def target_kernel(count, links_ref, geo_ref, absorbed_in, *refs):
    sums_refs, (f_ref, part_ref, out_ref, *sum_out, ta, tiles_ref, coef, cells, faces) = refs[:count], refs[count:]
    planes = f_ref.shape[1] // CHUNKS
    sums = add_tiles(sums_refs)
    for ref in sum_out:
        ref[...] = sums
    absorbed = sums if absorbed_in is None else absorbed_in[...]
    n, u, temperature, q = quantities(sums)
    rt = 1.0 / temperature
    rate = TIME_STEP * n * temperature / (SHEAR * jnp.exp(POWER * jnp.log(temperature)))
    height = rate * n * rt * jnp.sqrt(rt)
    slope = (1.0 / 3.0) / (5.0 * n * temperature * temperature)
    coef[0] = rate
    coef[1] = rt
    coef[2], coef[3] = u[1], u[2]
    coef[4], coef[5] = slope * q[1], slope * q[2]
    for k in range(FACES):
        wall = geo_ref[WALL + k] > 0.5
        coef[6 + k] = column(sums, EMIT + k) / jnp.where(wall, column(absorbed, ABSORB + k), 1.0)
    first = geo_ref[FIRST]

    wt = geo_ref[WT]

    def plane_table(a, _):
        xa = first + a.astype(F32) * H
        ca = xa - u[0]
        za = ca * ca * rt
        ta[0, a] = height * jnp.exp(-0.5 * za)
        ta[1, a] = slope * q[0] * ca
        ta[2, a] = za - 5.0
        ta[3, a] = jnp.exp(-0.5 * xa * xa / wt)
        return 0

    lax.fori_loop(0, planes, plane_table, 0, unroll=unroll(planes, 8))

    def tile_table(g, _):
        rtg = splat(coef, 1, g)
        ub, uc = splat(coef, 2, g), splat(coef, 3, g)
        qb, qc = splat(coef, 4, g), splat(coef, 5, g)
        shape = wall_tiles(splat(geo_ref, WT, g))
        for t in range(TILES):
            xb, xc = tile_nodes(t)
            cb, cc = xb - ub, xc - uc
            z = (cb * cb + cc * cc) * rtg
            at = g * TILES + t
            tiles_ref[0, at] = jnp.exp(-0.5 * z)
            tiles_ref[1, at] = cb * qb + cc * qc
            tiles_ref[2, at] = z
            tiles_ref[3, at] = shape[t]
        return 0

    lax.fori_loop(0, SUB, tile_table, 0, unroll=4)

    def at_plane(i, a, g):
        return jnp.broadcast_to(ta[i, a, pl.ds(g, 1), :], (SUB, LANES))

    def cell(g, _):
        rate_g = splat(coef, 0, g)
        bell, heat, zz = [[tiles_ref[i, g * TILES + t] for t in range(TILES)] for i in range(3)]

        def plane(a, _):
            height_a, heat_a, z_a = [at_plane(i, a, g) for i in range(3)]
            for t in range(TILES):
                where = (g, at_rows((a * TILES + t) * SUB), slice(None))
                f = f_ref[where]
                target = (height_a * bell[t]) * (1.0 + (heat_a + heat[t]) * (z_a + zz[t]))
                out_ref[where] = (part_ref[where] - rate_g * f) + target
            return 0

        lax.fori_loop(0, planes, plane, 0, unroll=unroll(planes, 16))
        return 0

    lax.fori_loop(0, SUB, cell, 0)

    def wall(i, _):
        g, k = cells[i], faces[i]
        x0 = splat(geo_ref, FIRST, g)
        ratio = splat(coef, 6 + k, g)
        scale = -TIME_STEP / splat(geo_ref, VOL, g)
        v0, v1, v2 = [scale * x for x in face_coefficients(geo_ref, k, g)]
        base, shape = [], []
        for t in range(TILES):
            xb, xc = tile_nodes(t)
            base.append(v1 * xb + v2 * xc)
            shape.append(ratio * tiles_ref[3, g * TILES + t])

        def plane(a, _):
            wa = at_plane(3, a, g)
            sa = v0 * (x0 + a.astype(F32) * H)
            for t in range(TILES):
                where = (g, at_rows((a * TILES + t) * SUB), slice(None))
                f = f_ref[where]
                out_ref[where] = out_ref[where] + jnp.maximum(sa + base[t], 0.0) * (wa * shape[t] - f)
            return 0

        lax.fori_loop(0, planes, plane, 0, unroll=unroll(planes, 16))
        return 0

    lax.fori_loop(0, list_faces(links_ref, is_wall, cells, faces), wall, 0)


def add_target(links, geo, absorbed, tiles, f, part):
    rows = f.shape[1]
    vmem = spec(pltpu.VMEM)
    given = [links, geo] + ([] if absorbed is None else [absorbed]) + list(tiles) + [f, part]

    def kernel(links_ref, geo_in, *refs):
        if absorbed is None:
            target_kernel(len(tiles), links_ref, geo_in, None, *refs)
        else:
            target_kernel(len(tiles), links_ref, geo_in, *refs)

    return pl.pallas_call(
        kernel,
        in_specs=[spec(pltpu.SMEM)] + [vmem] * (len(given) - 1),
        out_specs=[vmem] * (2 if absorbed is None else 1),
        out_shape=[array(*part.shape)] + ([array(SUB, LANES)] if absorbed is None else []),
        input_output_aliases={len(given) - 1: 0},
        scratch_shapes=[
                pltpu.VMEM((4, rows // CHUNKS, SUB, LANES), F32),
            pltpu.VMEM((4, SUB * TILES, SUB, LANES), F32),
            pltpu.VMEM((6 + FACES, SUB, LANES), F32),
            *face_lists(),
        ],
        compiler_params=params(),
        cost_estimate=traffic(rows, 7),
        name="add_target",
    )(*given)


def side_terms(high, pairs_ref, halo_ref, f_ref, at):
    terms = [None] * REACH
    rows = [halo_ref[r, at, :] for r in range(REACH)]
    first = SUB - REACH if high else 0
    own = [f_ref[first + e, at, :] for e in range(REACH)]
    count = len(BEFORE_PAIRS)
    pairs = [(e, r) for e in range(REACH) for r in range(e + 1)] if high else BEFORE_PAIRS
    for p, (e, r) in enumerate(pairs):
        term = pairs_ref[p + count if high else p, at, :] * (rows[r] - own[e])
        terms[e] = term if terms[e] is None else terms[e] + term
    return first, terms


def for_side(far, run):
    odd = is_odd()

    @pl.when(odd)
    def _():
        run(far)

    @pl.when(jnp.logical_not(odd))
    def _():
        run(not far)


def add_side(far, pairs_ref, halo_ref, old_ref, part_ref, f_ref, rows_ref):
    def run(high):
        def group(j, _):
            at = at_rows(j * SUB)
            first, terms = side_terms(high, pairs_ref, halo_ref, old_ref, at)
            for e in range(REACH):
                x = part_ref[first + e, at, :] + terms[e]
                f_ref[first + e, at, :] = x
                if rows_ref is not None:
                    rows_ref[e, at, :] = x
            return 0

        groups = part_ref.shape[1] // SUB
        lax.fori_loop(0, groups, group, 0, unroll=unroll(groups, 8))

    for_side(far, run)


def edge(far, pairs, halo, old, part):
    rows = part.shape[1]
    return pl.pallas_call(
        functools.partial(add_side, far),
        in_specs=[spec(pltpu.VMEM)] * 4,
        out_specs=[spec(pltpu.VMEM)] * 2,
        out_shape=[array(SUB, rows, LANES), array(REACH, rows, LANES)],
        input_output_aliases={3: 0},
        compiler_params=params(),
        cost_estimate=traffic(rows, 2),
        name="far_edge" if far else "near_edge",
    )(pairs, halo, old, part)


def last_near_kernel(geo_ref, pairs_ref, halo_ref, old_ref, part_ref, f_ref, sums_out, parts_ref):
    add_side(False, pairs_ref, halo_ref, old_ref, part_ref, f_ref, None)
    planes = f_ref.shape[1] // CHUNKS
    y = polynomial_sums(f_ref, planes, parts_ref)
    sums_out[...] = pack_sums(finish_polynomials(y, geo_ref[FIRST], planes), 0)


def last_near(geo, pairs, near, old, part):
    rows = part.shape[1]
    return pl.pallas_call(
        last_near_kernel,
        in_specs=[spec(pltpu.VMEM)] * 5,
        out_specs=[spec(pltpu.VMEM)] * 2,
        out_shape=[array(SUB, rows, LANES), array(SUB, LANES)],
        input_output_aliases={4: 0},
        scratch_shapes=[pltpu.VMEM((10, SUB * SUB, LANES), F32)],
        compiler_params=params(),
        cost_estimate=traffic(rows, 3),
        name="last_near",
    )(geo, pairs, near, old, part)


def last_far_kernel(geo_ref, pairs_ref, halo_ref, old_ref, sums_in, terms_ref, sums_out, parts_ref):
    rows = old_ref.shape[1]
    planes = rows // CHUNKS
    parts_ref[...] = jnp.zeros_like(parts_ref)

    def run(high):
        def group(j, _):
            at = at_rows(j * SUB)
            _first, terms = side_terms(high, pairs_ref, halo_ref, old_ref, at)
            for e in range(REACH):
                terms_ref[e, at, :] = terms[e]
            return 0

        lax.fori_loop(0, rows // SUB, group, 0, unroll=unroll(rows // SUB, 8))
        y = polynomial_sums(terms_ref, planes, parts_ref, SUB - REACH if high else 0)
        sums_out[...] = sums_in[...] + pack_sums(finish_polynomials(y, geo_ref[FIRST], planes), 0)

    for_side(True, run)


def last_far(geo, pairs, far, old, sums):
    rows = old.shape[1]
    return pl.pallas_call(
        last_far_kernel,
        in_specs=[spec(pltpu.VMEM)] * 5,
        out_specs=[spec(pltpu.VMEM)] * 2,
        out_shape=[array(REACH, rows, LANES), array(SUB, LANES)],
        scratch_shapes=[pltpu.VMEM((10, SUB * SUB, LANES), F32)],
        compiler_params=params(),
        cost_estimate=traffic(rows, 2),
        name="last_far",
    )(geo, pairs, far, old, sums)


LAST_PARTS = 4


def result_kernel(part_ref, terms_ref, out_hbm, native_ref, sems):
    part = part_ref.shape[1] // SUB // LAST_PARTS

    def copy(i):
        at = pl.ds(i * part * SUB * SUB, part * SUB * SUB)
        return pltpu.make_async_copy(native_ref.at[at], out_hbm.at[at], sems.at[i])

    def run(high):
        first = SUB - REACH if high else 0
        for i in range(LAST_PARTS):

            def group(j, _):
                at = at_rows(j * SUB)
                for g in range(SUB):
                    x = part_ref[g, at, :]
                    if 0 <= g - first < REACH:
                        x = x + terms_ref[g - first, at, :]
                    native_ref[pl.ds(j * SUB * SUB + g, SUB, stride=SUB), :] = x
                return 0

            lax.fori_loop(i * part, (i + 1) * part, group, 0, unroll=unroll(part, 4))
            copy(i).start()

    for_side(True, run)
    for i in range(LAST_PARTS):
        copy(i).wait()


def result(part, terms):
    rows = part.shape[1]
    native = (SUB * rows, LANES)
    return pl.pallas_call(
        result_kernel,
        in_specs=[spec(pltpu.VMEM)] * 2,
        out_specs=spec(pltpu.HBM),
        out_shape=array(*native),
        scratch_shapes=[pltpu.VMEM(native, F32), pltpu.SemaphoreType.DMA((LAST_PARTS,))],
        compiler_params=params(),
        cost_estimate=traffic(rows, 3),
        name="result",
    )(part, terms)


def swap(rows, start):
    pairs = [(i, i + 1) for i in range(start, lax.axis_size("space") - 1, 2)]
    return lax.ppermute(rows, "space", pairs + [(j, i) for i, j in pairs])


def per_device(particle_profile, neighbors, face_vectors, volumes, wall_temp):
    cells, points = particle_profile.shape
    rows = points // LANES
    plane_count = NV // lax.axis_size("vel")
    native = particle_profile.reshape(cells, rows, LANES).transpose(1, 0, 2)
    wall = neighbors < 0
    links = jnp.where(wall, WALL_LINK, neighbors - lax.axis_index("space") * cells)
    own = (links >= 0) & (links < cells)
    first = -SPEED_LIMIT + ((lax.axis_index("vel") * plane_count).astype(F32) + 0.5) * H
    geo = jnp.concatenate(
        [
            face_vectors.reshape(3 * FACES, cells),
            volumes[None],
            wall_temp[None],
            wall.astype(F32),
            own.astype(F32),
            jnp.full((1, cells), first, F32),
        ]
    )
    geo = jnp.broadcast_to(geo[:, :, None], (GEO, cells, LANES))
    native, far, near = first_rows(native)
    far, near = swap(far, 1), swap(near, 0)
    f, sums = first_sums(links, geo, native.reshape(rows * cells, LANES))
    tiles = gather_sums(sums)
    part, pairs = flux(True, links, geo, f)
    part, absorbed = add_target(links, geo, None, tiles, f, part)
    part, near = edge(False, pairs, near, f, part)
    near = swap(near, 0)
    f, far = edge(True, pairs, far, f, part)
    far = swap(far, 1)
    tiles = gather_sums(local_sums(links, geo, f))
    (part,) = flux(False, links, geo, f)
    (part,) = add_target(links, geo, absorbed, tiles, f, part)
    part, sums = last_near(geo, pairs, near, f, part)
    terms, sums = last_far(geo, pairs, far, f, sums)
    tiles = doubling_sums(sums)
    native = result(part, terms)
    macro_quantities = macro(tiles)
    evolved = native.reshape(rows, cells, LANES).transpose(1, 0, 2).reshape(cells, points)
    return evolved, macro_quantities


def solution(mesh):
    return jax.shard_map(
        per_device,
        mesh=mesh,
        in_specs=(
            P("space", "vel"),
            P(None, "space"),
            P(None, None, "space"),
            P("space"),
            P("space"),
        ),
        out_specs=(P("space", "vel"), P(None, "space")),
        check_vma=False,
    )
```

```python
import functools
import math

import jax
import jax.numpy as jnp
from jax import lax
from jax.experimental import pallas as pl
from jax.experimental.pallas import tpu as pltpu
from jax.sharding import PartitionSpec as P

NV = 64
FACES = 6
REACH = 3
STEPS = 2
LANES = 128
SUB = 8

TIME_STEP = 0.015
SHEAR = 0.1
POWER = 0.81
SPEED_LIMIT = 6.0
H = 2.0 * SPEED_LIMIT / NV
WEIGHT = H**3 * (2.0 * math.pi) ** (-1.5)

CHUNKS = NV * NV // LANES
TILES = CHUNKS // SUB

FV, VOL, WT, WALL, LOCAL, FIRST = 0, 18, 19, 20, 26, 32
GEO = 33
WALL_LINK = -64
BEFORE_PAIRS = tuple((g, r) for g in range(REACH) for r in range(g, REACH))
EMIT, ABSORB = 13, 19
SUMS = 25

F32 = jnp.float32


def lane_iota():
    return lax.broadcasted_iota(jnp.int32, (SUB, LANES), 1)


def sub_iota():
    return lax.broadcasted_iota(jnp.int32, (SUB, LANES), 0)


def half_of(lane):
    return (lane >= NV).astype(F32)


def third_component(lane):
    c = jnp.where(lane >= NV, lane - NV, lane).astype(F32)
    return -SPEED_LIMIT + (c + 0.5) * H


def tile_nodes(t):
    lane = lane_iota()
    b = (2 * SUB * t + 2 * sub_iota()).astype(F32) + half_of(lane)
    return -SPEED_LIMIT + (b + 0.5) * H, third_component(lane)


def column(tile, p):
    return jnp.broadcast_to(tile[:, p : p + 1], (SUB, LANES))


def splat(ref, i, g):
    return jnp.broadcast_to(ref[i, pl.ds(g, 1), :], (SUB, LANES))


def total(tile):
    return jnp.broadcast_to(jnp.sum(tile, axis=1, keepdims=True), (SUB, LANES))


def face_coefficients(geo_ref, k, g):
    return [splat(geo_ref, FV + FACES * i + k, g) for i in range(3)]


def at_rows(start, size=SUB):
    return pl.ds(pl.multiple_of(start, SUB), size)


def wall_tiles(wall_temp):
    rt = 1.0 / wall_temp
    scale = rt * jnp.sqrt(rt)
    out = []
    for t in range(TILES):
        xb, xc = tile_nodes(t)
        out.append(scale * jnp.exp(-0.5 * (xb * xb + xc * xc) * rt))
    return out


def pack_sums(arrays, start):
    lane = lane_iota()
    out = jnp.zeros((SUB, LANES), F32)
    for p, x in enumerate(arrays):
        out = jnp.where(lane == start + p, total(x), out)
    return out


def over_sublanes(ref, k):
    out = ref[k, pl.ds(0, SUB, stride=SUB), :]
    for s in range(1, SUB):
        out = out + ref[k, pl.ds(s, SUB, stride=SUB), :]
    return out


def list_faces(links_ref, wanted, cell_ref, face_ref):
    count = 0
    for g in range(SUB):
        for k in range(FACES):
            cell_ref[count] = g
            face_ref[count] = k
            count = count + wanted(links_ref[k, g]).astype(jnp.int32)
    return count


def is_wall(j):
    return j == WALL_LINK


def is_remote(j):
    return jnp.logical_or(j >= SUB, jnp.logical_and(j < 0, j != WALL_LINK))


def face_lists():
    return [pltpu.SMEM((FACES * SUB + 1,), jnp.int32)] * 2


def unroll(planes, most):
    return math.gcd(planes, most)


def finish_polynomials(y, first, planes):
    y0, y1, y2, y3, by0, by1, by2, bby0, bby1, bbby0 = y
    m = first + 0.5 * (planes - 1) * H
    c = third_component(lane_iota())
    cc = c * c
    a = y1 + m * y0
    aa = y2 + m * (2.0 * y1 + m * y0)
    aaa = y3 + m * (3.0 * y2 + m * (3.0 * y1 + m * y0))
    ab = by1 + m * by0
    aab = by2 + m * (2.0 * by1 + m * by0)
    abb = bby1 + m * bby0
    return (
        y0,
        a,
        by0,
        c * y0,
        aa,
        bby0,
        cc * y0,
        ab,
        c * a,
        c * by0,
        aaa + abb + cc * a,
        aab + bbby0 + cc * by0,
        c * (aa + bby0 + cc * y0),
    )


def polynomial_sums(f_ref, planes, parts_ref, first=0):
    half = planes // 2

    def cell(g, _):
        out = [None] * 10
        for t in range(TILES):
            y0 = y1 = y2 = y3 = None
            for i in range(half):
                d = (i + 0.5) * H
                hi = f_ref[g, pl.ds(((half + i) * TILES + t) * SUB, SUB), :]
                lo = f_ref[g, pl.ds(((half - 1 - i) * TILES + t) * SUB, SUB), :]
                s, r = hi + lo, hi - lo
                if i == 0:
                    y0, y1, y2, y3 = s, d * r, (d * d) * s, (d * d * d) * r
                else:
                    y0, y1, y2, y3 = y0 + s, y1 + d * r, y2 + (d * d) * s, y3 + (d * d * d) * r
            b, _c = tile_nodes(t)
            bb = b * b
            terms = (y0, y1, y2, y3, b * y0, b * y1, b * y2, bb * y0, bb * y1, bb * (b * y0))
            out = [x if o is None else o + x for o, x in zip(out, terms)]
        for p in range(10):
            parts_ref[p, at_rows((first + g) * SUB), :] = out[p]
        return 0

    lax.fori_loop(0, f_ref.shape[0], cell, 0)
    return [over_sublanes(parts_ref, p) for p in range(10)]


def native_polynomial_sums(native_ref, planes):
    half, side = planes // 2, CHUNKS // 2
    zero = jnp.zeros((SUB, LANES), F32)
    acc = [zero] * 10

    def plane(a, acc):
        xa = (a.astype(F32) - 0.5 * (planes - 1)) * H
        b0 = b1 = b2 = b3 = None
        for i in range(side):
            y = (2 * i + 1) * H
            hi = native_ref[at_rows((a * CHUNKS + side + i) * SUB), :]
            lo = native_ref[at_rows((a * CHUNKS + side - 1 - i) * SUB), :]
            s, d = hi + lo, hi - lo
            terms = (s, y * d, (y * y) * s, (y * y * y) * d)
            if i == 0:
                b0, b1, b2, b3 = terms
            else:
                b0, b1, b2, b3 = b0 + terms[0], b1 + terms[1], b2 + terms[2], b3 + terms[3]
        a0, a1, a2 = xa * b0, xa * b1, xa * b2
        aa0 = xa * a0
        new = (b0, a0, aa0, xa * aa0, b1, a1, xa * a1, b2, a2, b3)
        return tuple(x + z for x, z in zip(acc, new))

    g0, a0, aa0, aaa0, g1, a1, aa1, g2, a2, g3 = lax.fori_loop(0, planes, plane, tuple(acc))
    e = (half_of(lane_iota()) - 0.5) * H
    return [
        g0,
        a0,
        aa0,
        aaa0,
        g1 + e * g0,
        a1 + e * a0,
        aa1 + e * aa0,
        g2 + e * (2.0 * g1 + e * g0),
        a2 + e * (2.0 * a1 + e * a0),
        g3 + e * (3.0 * g2 + e * (3.0 * g1 + e * g0)),
    ]


def wall_sums(f_ref, planes, links_ref, geo_ref, sums_ref, cells, faces, with_absorbed):
    sums_ref[...] = jnp.zeros_like(sums_ref)

    def wall(i, _):
        g, k = cells[i], faces[i]
        v0, v1, v2 = face_coefficients(geo_ref, k, g)
        first = splat(geo_ref, FIRST, g)
        base = []
        for t in range(TILES):
            xb, xc = tile_nodes(t)
            base.append(v1 * xb + v2 * xc)
        if with_absorbed:
            wt = splat(geo_ref, WT, g)
            shape = wall_tiles(wt)

        def plane(a, acc):
            out, back = list(acc[0]), list(acc[1])
            xa = first + a.astype(F32) * H
            sa = v0 * xa
            if with_absorbed:
                wa = jnp.exp(-0.5 * xa * xa / wt)
            for t in range(TILES):
                s = sa + base[t]
                f = f_ref[g, at_rows((a * TILES + t) * SUB), :]
                out[t] = out[t] + jnp.maximum(s, 0.0) * f
                if with_absorbed:
                    back[t] = back[t] + jnp.maximum(-s, 0.0) * (wa * shape[t])
            return tuple(out), tuple(back)

        zeros = (jnp.zeros((SUB, LANES), F32),) * TILES
        out, back = lax.fori_loop(0, planes, plane, (zeros, zeros), unroll=unroll(planes, 16))
        at = at_rows(g * SUB)
        sums_ref[k, at, :] = (out[0] + out[1]) + (out[2] + out[3])
        if with_absorbed:
            sums_ref[FACES + k, at, :] = (back[0] + back[1]) + (back[2] + back[3])
        return 0

    lax.fori_loop(0, list_faces(links_ref, is_wall, cells, faces), wall, 0)


def sums_kernel(links_ref, geo_ref, f_ref, sums_out, parts_ref, face_ref, cells, faces):
    planes = f_ref.shape[1] // CHUNKS
    y = polynomial_sums(f_ref, planes, parts_ref)
    packed = pack_sums(finish_polynomials(y, geo_ref[FIRST], planes), 0)
    wall_sums(f_ref, planes, links_ref, geo_ref, face_ref, cells, faces, False)
    sums_out[...] = packed + pack_sums([over_sublanes(face_ref, k) for k in range(FACES)], EMIT)


def first_sums_kernel(links_ref, geo_ref, native_ref, f_ref, sums_out, face_ref, cells, faces):
    rows = f_ref.shape[1]
    planes = rows // CHUNKS

    def group(j, _):
        for g in range(SUB):
            f_ref[g, at_rows(j * SUB), :] = native_ref[pl.ds(j * SUB * SUB + g, SUB, stride=SUB), :]
        return 0

    lax.fori_loop(0, rows // SUB, group, 0, unroll=2)
    y = native_polynomial_sums(native_ref, planes)
    packed = pack_sums(finish_polynomials(y, geo_ref[FIRST], planes), 0)
    wall_sums(f_ref, planes, links_ref, geo_ref, face_ref, cells, faces, True)
    sums_out[...] = packed + pack_sums([over_sublanes(face_ref, k) for k in range(2 * FACES)], EMIT)


def spec(space):
    return pl.BlockSpec(memory_space=space)


def array(*shape):
    return jax.ShapeDtypeStruct(shape, F32)


def params(mib=4):
    return pltpu.CompilerParams(vmem_limit_bytes=mib * 1024 * 1024)


def traffic(rows, profiles):
    size = SUB * rows * LANES
    return pl.CostEstimate(flops=8 * profiles * size, bytes_accessed=4 * profiles * size, transcendentals=0)


def local_sums(links, geo, f):
    return pl.pallas_call(
        sums_kernel,
        in_specs=[spec(pltpu.SMEM), spec(pltpu.VMEM), spec(pltpu.VMEM)],
        out_specs=spec(pltpu.VMEM),
        out_shape=array(SUB, LANES),
        scratch_shapes=[
                pltpu.VMEM((10, SUB * SUB, LANES), F32),
            pltpu.VMEM((FACES, SUB * SUB, LANES), F32),
            *face_lists(),
        ],
        compiler_params=params(),
        cost_estimate=traffic(f.shape[1], 4),
        name="local_sums",
    )(links, geo, f)


def first_sums(links, geo, native):
    rows = native.shape[0] // SUB
    return pl.pallas_call(
        first_sums_kernel,
        in_specs=[spec(pltpu.SMEM), spec(pltpu.VMEM), spec(pltpu.VMEM)],
        out_specs=[spec(pltpu.VMEM)] * 2,
        out_shape=[array(SUB, rows, LANES), array(SUB, LANES)],
        scratch_shapes=[
                pltpu.VMEM((2 * FACES, SUB * SUB, LANES), F32),
            *face_lists(),
        ],
        compiler_params=params(),
        cost_estimate=traffic(rows, 5),
        name="first_sums",
    )(links, geo, native)


SPLIT_PARTS = 8


def is_odd():
    return lax.rem(lax.axis_index("space"), 2) == 1


def first_rows_kernel(native_hbm, native_ref, far_any, near_any, far_ref, near_ref, sems, far_sems, near_sems):
    rows = native_ref.shape[0]
    part = rows // SPLIT_PARTS
    copies = [
        pltpu.make_async_copy(
            native_hbm.at[pl.ds(i * part, part)], native_ref.at[pl.ds(i * part, part)], sems.at[i]
        )
        for i in range(SPLIT_PARTS)
    ]
    for c in copies:
        c.start()
    odd = is_odd()
    far = jnp.where(odd, SUB - REACH, 0)
    near = jnp.where(odd, 0, SUB - REACH)
    groups = part // (SUB * SUB)
    out = []

    for i, c in enumerate(copies):
        c.wait()

        def group(j, _):
            for r in range(REACH):
                at = at_rows(j * SUB)
                far_ref[r, at, :] = native_ref[pl.ds(j * SUB * SUB + far + r, SUB, stride=SUB), :]
                near_ref[r, at, :] = native_ref[pl.ds(j * SUB * SUB + near + r, SUB, stride=SUB), :]
            return 0

        lax.fori_loop(i * groups, (i + 1) * groups, group, 0, unroll=unroll(groups, 8))
        at = pl.ds(i * groups * SUB, groups * SUB)
        out.append(pltpu.make_async_copy(far_ref.at[:, at], far_any.at[:, at], far_sems.at[i]))
        out.append(pltpu.make_async_copy(near_ref.at[:, at], near_any.at[:, at], near_sems.at[i]))
        out[-2].start()
        out[-1].start()
    for c in out:
        c.wait()


def first_rows(native):
    rows = native.shape[0] // SUB
    halo = (REACH, rows, LANES)
    return pl.pallas_call(
        first_rows_kernel,
        in_specs=[spec(pltpu.HBM)],
        out_specs=[spec(pltpu.VMEM), spec(pl.ANY), spec(pl.ANY)],
        out_shape=[array(*native.shape), array(*halo), array(*halo)],
        scratch_shapes=[pltpu.VMEM(halo, F32)] * 2 + [pltpu.SemaphoreType.DMA((SPLIT_PARTS,))] * 3,
        compiler_params=params(),
        cost_estimate=traffic(rows, 4),
        name="first_rows",
    )(pltpu.with_memory_space_constraint(native, pltpu.HBM))


def pair_weights(links_ref, geo_ref, pairs_ref, cells, faces):
    rows = pairs_ref.shape[1]
    planes = rows // CHUNKS
    first = splat(geo_ref, FIRST, 0)

    def clear(j, _):
        for p in range(pairs_ref.shape[0]):
            pairs_ref[p, at_rows(j * SUB), :] = jnp.zeros((SUB, LANES), F32)
        return 0

    lax.fori_loop(0, rows // SUB, clear, 0, unroll=4)

    def remote(i, _):
        g, k = cells[i], faces[i]
        j = links_ref[k, g]
        edge = g - (SUB - REACH)
        before = g * REACH - g * (g - 1) // 2 + (j + REACH) - g
        after = len(BEFORE_PAIRS) + edge * (edge + 1) // 2 + j - SUB
        at_pair = jnp.where(j < 0, before, after)
        scale = -TIME_STEP / splat(geo_ref, VOL, g)
        v0, v1, v2 = [scale * x for x in face_coefficients(geo_ref, k, g)]
        base = []
        for t in range(TILES):
            xb, xc = tile_nodes(t)
            base.append(v1 * xb + v2 * xc)

        def plane(a, _):
            sa = v0 * (first + a.astype(F32) * H)
            for t in range(TILES):
                at = at_rows((a * TILES + t) * SUB)
                pairs_ref[at_pair, at, :] = pairs_ref[at_pair, at, :] + jnp.maximum(sa + base[t], 0.0)
            return 0

        lax.fori_loop(0, planes, plane, 0, unroll=unroll(planes, 8))
        return 0

    lax.fori_loop(0, list_faces(links_ref, is_remote, cells, faces), remote, 0)


def gather_sums(tile):
    size = lax.axis_size("vel")
    if size not in (2, 4):
        return [lax.psum(tile, "vel")]
    others = [lax.ppermute(tile, "vel", [(i, i ^ s) for i in range(size)]) for s in range(1, size)]
    return [tile, *others]


def doubling_sums(tile):
    size = lax.axis_size("vel")
    if size != 4:
        return gather_sums(tile)
    pair = tile + lax.ppermute(tile, "vel", [(i, i ^ 1) for i in range(size)])
    return [pair, lax.ppermute(pair, "vel", [(i, i ^ 2) for i in range(size)])]


def add_tiles(refs):
    tiles = [r[...] for r in refs]
    while len(tiles) > 1:
        tiles = [tiles[i] + tiles[i + 1] for i in range(0, len(tiles), 2)]
    return tiles[0]


def quantities(tile):
    m = [WEIGHT * column(tile, p) for p in range(13)]
    n = m[0]
    rn = 1.0 / n
    u = [m[1 + i] * rn for i in range(3)]
    uu = u[0] * u[0] + u[1] * u[1] + u[2] * u[2]
    trace = m[4] + m[5] + m[6]
    width = trace - n * uu
    temperature = width * rn * (1.0 / 3.0)
    second = [[m[4], m[7], m[8]], [m[7], m[5], m[9]], [m[8], m[9], m[6]]]
    q = []
    for i in range(3):
        across = u[0] * second[i][0] + u[1] * second[i][1] + u[2] * second[i][2]
        q.append(0.5 * (m[10 + i] - 2.0 * across - u[i] * trace + 2.0 * uu * m[1 + i]))
    return n, u, temperature, q


def macro_kernel(*refs):
    out_ref = refs[-1]
    n, u, temperature, q = quantities(add_tiles(refs[:-1]))
    lane, sub = lane_iota(), sub_iota()
    for i, x in enumerate((n, *u, temperature, *q)):
        row = jnp.sum(jnp.where(lane == sub, x, 0.0), axis=0, keepdims=True)
        out_ref[pl.ds(i, 1), :] = row[:, :SUB]


def macro(tiles):
    return pl.pallas_call(
        macro_kernel,
        in_specs=[spec(pltpu.VMEM)] * len(tiles),
        out_specs=spec(pltpu.VMEM),
        out_shape=array(8, SUB),
        compiler_params=params(1),
        name="macro",
    )(*tiles)


def flux_kernel(with_pairs, links_ref, geo_ref, f_ref, out_ref, *refs):
    if with_pairs:
        pairs_ref, cells, faces = refs[0], refs[-2], refs[-1]
        pair_weights(links_ref, geo_ref, pairs_ref, cells, faces)
        refs = refs[1:-2]
    coef, bases, stays, source, face = refs
    planes = f_ref.shape[1] // CHUNKS
    scale = -TIME_STEP / geo_ref[VOL]
    for i in range(3):
        whole = None
        for k in range(FACES):
            x = scale * geo_ref[FV + FACES * i + k]
            coef[FACES * i + k] = x
            whole = x if whole is None else whole + x
        coef[3 * FACES + i] = whole

    def table(g, _):
        w = [[splat(coef, FACES * i + k, g) for i in (1, 2)] for k in range(FACES)]
        whole = [splat(coef, 3 * FACES + i, g) for i in (1, 2)]
        for t in range(TILES):
            xb, xc = tile_nodes(t)
            for k in range(FACES):
                bases[k, g * TILES + t] = w[k][0] * xb + w[k][1] * xc
            stays[g * TILES + t] = 1.0 + whole[0] * xb + whole[1] * xc
        return 0

    lax.fori_loop(0, SUB, table, 0, unroll=2)

    def cell(g, _):
        count = 0
        for k in range(FACES):
            j = links_ref[k, g]
            source[count] = j
            face[count] = k
            count = count + jnp.logical_and(j >= 0, j < SUB).astype(jnp.int32)
        for n in range(FACES + 1):

            @pl.when(count == n)
            def _():
                own_faces(g, n)

        return 0

    def own_faces(g, n):
        at_source = [source[i] for i in range(n)]
        first_weight = [splat(coef, face[k], g) for k in range(n)]
        whole = splat(coef, 3 * FACES, g)
        x0 = splat(geo_ref, FIRST, g)
        base = [[bases[face[k], g * TILES + t] for k in range(n)] for t in range(TILES)]
        stay = [stays[g * TILES + t] for t in range(TILES)]

        def plane(a, _):
            xa = x0 + a.astype(F32) * H
            sa = [w * xa for w in first_weight]
            stay_a = whole * xa
            for t in range(TILES):
                at = at_rows((a * TILES + t) * SUB)
                f = f_ref[g, at, :]
                acc = f * (stay_a + stay[t])
                for k in range(n):
                    acc = acc + jnp.maximum(sa[k] + base[t][k], 0.0) * (f_ref[at_source[k], at, :] - f)
                out_ref[g, at, :] = acc
            return 0

        lax.fori_loop(0, planes, plane, 0, unroll=unroll(planes, 8))

    lax.fori_loop(0, SUB, cell, 0)


def flux(with_pairs, links, geo, f):
    rows = f.shape[1]
    pairs = 2 * len(BEFORE_PAIRS)
    return pl.pallas_call(
        functools.partial(flux_kernel, with_pairs),
        in_specs=[spec(pltpu.SMEM), spec(pltpu.VMEM), spec(pltpu.VMEM)],
        out_specs=[spec(pltpu.VMEM)] * (2 if with_pairs else 1),
        out_shape=[array(*f.shape)] + ([array(pairs, rows, LANES)] if with_pairs else []),
        scratch_shapes=[
            pltpu.VMEM((3 * FACES + 3, SUB, LANES), F32),
            pltpu.VMEM((FACES, SUB * TILES, SUB, LANES), F32),
            pltpu.VMEM((SUB * TILES, SUB, LANES), F32),
            pltpu.SMEM((FACES + 1,), jnp.int32),
            pltpu.SMEM((FACES + 1,), jnp.int32),
        ]
        + (face_lists() if with_pairs else []),
        compiler_params=params(),
        cost_estimate=traffic(rows, 9 if with_pairs else 7),
        name="flux",
    )(links, geo, f)


def target_kernel(count, links_ref, geo_ref, absorbed_in, *refs):
    sums_refs, (f_ref, part_ref, out_ref, *sum_out, ta, tiles_ref, coef, cells, faces) = refs[:count], refs[count:]
    planes = f_ref.shape[1] // CHUNKS
    sums = add_tiles(sums_refs)
    for ref in sum_out:
        ref[...] = sums
    absorbed = sums if absorbed_in is None else absorbed_in[...]
    n, u, temperature, q = quantities(sums)
    rt = 1.0 / temperature
    rate = TIME_STEP * n * temperature / (SHEAR * jnp.exp(POWER * jnp.log(temperature)))
    height = rate * n * rt * jnp.sqrt(rt)
    slope = (1.0 / 3.0) / (5.0 * n * temperature * temperature)
    coef[0] = rate
    coef[1] = rt
    coef[2], coef[3] = u[1], u[2]
    coef[4], coef[5] = slope * q[1], slope * q[2]
    for k in range(FACES):
        wall = geo_ref[WALL + k] > 0.5
        coef[6 + k] = column(sums, EMIT + k) / jnp.where(wall, column(absorbed, ABSORB + k), 1.0)
    first = geo_ref[FIRST]

    wt = geo_ref[WT]

    def plane_table(a, _):
        xa = first + a.astype(F32) * H
        ca = xa - u[0]
        za = ca * ca * rt
        ta[0, a] = height * jnp.exp(-0.5 * za)
        ta[1, a] = slope * q[0] * ca
        ta[2, a] = za - 5.0
        ta[3, a] = jnp.exp(-0.5 * xa * xa / wt)
        return 0

    lax.fori_loop(0, planes, plane_table, 0, unroll=unroll(planes, 8))

    def tile_table(g, _):
        rtg = splat(coef, 1, g)
        ub, uc = splat(coef, 2, g), splat(coef, 3, g)
        qb, qc = splat(coef, 4, g), splat(coef, 5, g)
        shape = wall_tiles(splat(geo_ref, WT, g))
        for t in range(TILES):
            xb, xc = tile_nodes(t)
            cb, cc = xb - ub, xc - uc
            z = (cb * cb + cc * cc) * rtg
            at = g * TILES + t
            tiles_ref[0, at] = jnp.exp(-0.5 * z)
            tiles_ref[1, at] = cb * qb + cc * qc
            tiles_ref[2, at] = z
            tiles_ref[3, at] = shape[t]
        return 0

    lax.fori_loop(0, SUB, tile_table, 0, unroll=4)

    def at_plane(i, a, g):
        return jnp.broadcast_to(ta[i, a, pl.ds(g, 1), :], (SUB, LANES))

    def cell(g, _):
        rate_g = splat(coef, 0, g)
        bell, heat, zz = [[tiles_ref[i, g * TILES + t] for t in range(TILES)] for i in range(3)]

        def plane(a, _):
            height_a, heat_a, z_a = [at_plane(i, a, g) for i in range(3)]
            for t in range(TILES):
                where = (g, at_rows((a * TILES + t) * SUB), slice(None))
                f = f_ref[where]
                target = (height_a * bell[t]) * (1.0 + (heat_a + heat[t]) * (z_a + zz[t]))
                out_ref[where] = (part_ref[where] - rate_g * f) + target
            return 0

        lax.fori_loop(0, planes, plane, 0, unroll=unroll(planes, 16))
        return 0

    lax.fori_loop(0, SUB, cell, 0)

    def wall(i, _):
        g, k = cells[i], faces[i]
        x0 = splat(geo_ref, FIRST, g)
        ratio = splat(coef, 6 + k, g)
        scale = -TIME_STEP / splat(geo_ref, VOL, g)
        v0, v1, v2 = [scale * x for x in face_coefficients(geo_ref, k, g)]
        base, shape = [], []
        for t in range(TILES):
            xb, xc = tile_nodes(t)
            base.append(v1 * xb + v2 * xc)
            shape.append(ratio * tiles_ref[3, g * TILES + t])

        def plane(a, _):
            wa = at_plane(3, a, g)
            sa = v0 * (x0 + a.astype(F32) * H)
            for t in range(TILES):
                where = (g, at_rows((a * TILES + t) * SUB), slice(None))
                f = f_ref[where]
                out_ref[where] = out_ref[where] + jnp.maximum(sa + base[t], 0.0) * (wa * shape[t] - f)
            return 0

        lax.fori_loop(0, planes, plane, 0, unroll=unroll(planes, 16))
        return 0

    lax.fori_loop(0, list_faces(links_ref, is_wall, cells, faces), wall, 0)


def add_target(links, geo, absorbed, tiles, f, part):
    rows = f.shape[1]
    vmem = spec(pltpu.VMEM)
    given = [links, geo] + ([] if absorbed is None else [absorbed]) + list(tiles) + [f, part]

    def kernel(links_ref, geo_in, *refs):
        if absorbed is None:
            target_kernel(len(tiles), links_ref, geo_in, None, *refs)
        else:
            target_kernel(len(tiles), links_ref, geo_in, *refs)

    return pl.pallas_call(
        kernel,
        in_specs=[spec(pltpu.SMEM)] + [vmem] * (len(given) - 1),
        out_specs=[vmem] * (2 if absorbed is None else 1),
        out_shape=[array(*part.shape)] + ([array(SUB, LANES)] if absorbed is None else []),
        input_output_aliases={len(given) - 1: 0},
        scratch_shapes=[
                pltpu.VMEM((4, rows // CHUNKS, SUB, LANES), F32),
            pltpu.VMEM((4, SUB * TILES, SUB, LANES), F32),
            pltpu.VMEM((6 + FACES, SUB, LANES), F32),
            *face_lists(),
        ],
        compiler_params=params(),
        cost_estimate=traffic(rows, 7),
        name="add_target",
    )(*given)


def side_terms(high, pairs_ref, halo_ref, f_ref, at):
    terms = [None] * REACH
    rows = [halo_ref[r, at, :] for r in range(REACH)]
    first = SUB - REACH if high else 0
    own = [f_ref[first + e, at, :] for e in range(REACH)]
    count = len(BEFORE_PAIRS)
    pairs = [(e, r) for e in range(REACH) for r in range(e + 1)] if high else BEFORE_PAIRS
    for p, (e, r) in enumerate(pairs):
        term = pairs_ref[p + count if high else p, at, :] * (rows[r] - own[e])
        terms[e] = term if terms[e] is None else terms[e] + term
    return first, terms


def for_side(far, run):
    odd = is_odd()

    @pl.when(odd)
    def _():
        run(far)

    @pl.when(jnp.logical_not(odd))
    def _():
        run(not far)


def add_side(far, pairs_ref, halo_ref, old_ref, part_ref, f_ref, rows_ref):
    def run(high):
        def group(j, _):
            at = at_rows(j * SUB)
            first, terms = side_terms(high, pairs_ref, halo_ref, old_ref, at)
            for e in range(REACH):
                x = part_ref[first + e, at, :] + terms[e]
                f_ref[first + e, at, :] = x
                if rows_ref is not None:
                    rows_ref[e, at, :] = x
            return 0

        groups = part_ref.shape[1] // SUB
        lax.fori_loop(0, groups, group, 0, unroll=unroll(groups, 8))

    for_side(far, run)


def edge(far, pairs, halo, old, part):
    rows = part.shape[1]
    return pl.pallas_call(
        functools.partial(add_side, far),
        in_specs=[spec(pltpu.VMEM)] * 4,
        out_specs=[spec(pltpu.VMEM)] * 2,
        out_shape=[array(SUB, rows, LANES), array(REACH, rows, LANES)],
        input_output_aliases={3: 0},
        compiler_params=params(),
        cost_estimate=traffic(rows, 2),
        name="far_edge" if far else "near_edge",
    )(pairs, halo, old, part)


def last_near_kernel(geo_ref, pairs_ref, halo_ref, old_ref, part_ref, f_ref, sums_out, parts_ref):
    add_side(False, pairs_ref, halo_ref, old_ref, part_ref, f_ref, None)
    planes = f_ref.shape[1] // CHUNKS
    y = polynomial_sums(f_ref, planes, parts_ref)
    sums_out[...] = pack_sums(finish_polynomials(y, geo_ref[FIRST], planes), 0)


def last_near(geo, pairs, near, old, part):
    rows = part.shape[1]
    return pl.pallas_call(
        last_near_kernel,
        in_specs=[spec(pltpu.VMEM)] * 5,
        out_specs=[spec(pltpu.VMEM)] * 2,
        out_shape=[array(SUB, rows, LANES), array(SUB, LANES)],
        input_output_aliases={4: 0},
        scratch_shapes=[pltpu.VMEM((10, SUB * SUB, LANES), F32)],
        compiler_params=params(),
        cost_estimate=traffic(rows, 3),
        name="last_near",
    )(geo, pairs, near, old, part)


def last_far_kernel(
    geo_ref, pairs_ref, to_odd_ref, to_even_ref, old_ref, sums_in, terms_ref, sums_out, parts_ref
):
    rows = old_ref.shape[1]
    planes = rows // CHUNKS
    parts_ref[...] = jnp.zeros_like(parts_ref)

    def run(high):
        halo_ref = to_odd_ref if high else to_even_ref

        def group(j, _):
            at = at_rows(j * SUB)
            _first, terms = side_terms(high, pairs_ref, halo_ref, old_ref, at)
            for e in range(REACH):
                terms_ref[e, at, :] = terms[e]
            return 0

        lax.fori_loop(0, rows // SUB, group, 0, unroll=unroll(rows // SUB, 8))
        y = polynomial_sums(terms_ref, planes, parts_ref, SUB - REACH if high else 0)
        sums_out[...] = sums_in[...] + pack_sums(finish_polynomials(y, geo_ref[FIRST], planes), 0)

    for_side(True, run)


def last_far(geo, pairs, far, old, sums):
    rows = old.shape[1]
    return pl.pallas_call(
        last_far_kernel,
        in_specs=[spec(pltpu.VMEM)] * 6,
        out_specs=[spec(pltpu.VMEM)] * 2,
        out_shape=[array(REACH, rows, LANES), array(SUB, LANES)],
        scratch_shapes=[pltpu.VMEM((10, SUB * SUB, LANES), F32)],
        compiler_params=params(),
        cost_estimate=traffic(rows, 2),
        name="last_far",
    )(geo, pairs, far[1], far[0], old, sums)


LAST_PARTS = 4


def result_kernel(part_ref, terms_ref, out_hbm, native_ref, sems):
    part = part_ref.shape[1] // SUB // LAST_PARTS

    def copy(i):
        at = pl.ds(i * part * SUB * SUB, part * SUB * SUB)
        return pltpu.make_async_copy(native_ref.at[at], out_hbm.at[at], sems.at[i])

    def run(high):
        first = SUB - REACH if high else 0
        for i in range(LAST_PARTS):

            def group(j, _):
                at = at_rows(j * SUB)
                for g in range(SUB):
                    x = part_ref[g, at, :]
                    if 0 <= g - first < REACH:
                        x = x + terms_ref[g - first, at, :]
                    native_ref[pl.ds(j * SUB * SUB + g, SUB, stride=SUB), :] = x
                return 0

            lax.fori_loop(i * part, (i + 1) * part, group, 0, unroll=unroll(part, 4))
            copy(i).start()

    for_side(True, run)
    for i in range(LAST_PARTS):
        copy(i).wait()


def result(part, terms):
    rows = part.shape[1]
    native = (SUB * rows, LANES)
    return pl.pallas_call(
        result_kernel,
        in_specs=[spec(pltpu.VMEM)] * 2,
        out_specs=spec(pltpu.HBM),
        out_shape=array(*native),
        scratch_shapes=[pltpu.VMEM(native, F32), pltpu.SemaphoreType.DMA((LAST_PARTS,))],
        compiler_params=params(),
        cost_estimate=traffic(rows, 3),
        name="result",
    )(part, terms)


def swap(rows, start):
    pairs = [(i, i + 1) for i in range(start, lax.axis_size("space") - 1, 2)]
    return lax.ppermute(rows, "space", pairs + [(j, i) for i, j in pairs])


def swap_far_one_way(rows):
    pairs = [(i, i + 1) for i in range(1, lax.axis_size("space") - 1, 2)]
    to_odd = lax.ppermute(rows, "space", [(j, i) for i, j in pairs])
    return lax.ppermute(rows, "space", pairs), to_odd


def per_device(particle_profile, neighbors, face_vectors, volumes, wall_temp):
    cells, points = particle_profile.shape
    rows = points // LANES
    plane_count = NV // lax.axis_size("vel")
    native = particle_profile.reshape(cells, rows, LANES).transpose(1, 0, 2).reshape(cells * rows, LANES)
    wall = neighbors < 0
    links = jnp.where(wall, WALL_LINK, neighbors - lax.axis_index("space") * cells)
    own = (links >= 0) & (links < cells)
    first = -SPEED_LIMIT + ((lax.axis_index("vel") * plane_count).astype(F32) + 0.5) * H
    geo = jnp.concatenate(
        [
            face_vectors.reshape(3 * FACES, cells),
            volumes[None],
            wall_temp[None],
            wall.astype(F32),
            own.astype(F32),
            jnp.full((1, cells), first, F32),
        ]
    )
    geo = jnp.broadcast_to(geo[:, :, None], (GEO, cells, LANES))
    native, far, near = first_rows(native)
    far, near = swap(far, 1), swap(near, 0)
    f, sums = first_sums(links, geo, native)
    tiles = gather_sums(sums)
    part, pairs = flux(True, links, geo, f)
    part, absorbed = add_target(links, geo, None, tiles, f, part)
    part, near = edge(False, pairs, near, f, part)
    near = swap(near, 0)
    f, far = edge(True, pairs, far, f, part)
    far = swap_far_one_way(far)
    tiles = gather_sums(local_sums(links, geo, f))
    (part,) = flux(False, links, geo, f)
    (part,) = add_target(links, geo, absorbed, tiles, f, part)
    part, sums = last_near(geo, pairs, near, f, part)
    terms, sums = last_far(geo, pairs, far, f, sums)
    tiles = doubling_sums(sums)
    native = result(part, terms)
    macro_quantities = macro(tiles)
    evolved = native.reshape(rows, cells, LANES).transpose(1, 0, 2).reshape(cells, points)
    return evolved, macro_quantities


def solution(mesh):
    return jax.shard_map(
        per_device,
        mesh=mesh,
        in_specs=(
            P("space", "vel"),
            P(None, "space"),
            P(None, None, "space"),
            P("space"),
            P("space"),
        ),
        out_specs=(P("space", "vel"), P(None, "space")),
        check_vma=False,
    )
```

```python
import functools
import math

import jax
import jax.numpy as jnp
from jax import lax
from jax.experimental import pallas as pl
from jax.experimental.pallas import tpu as pltpu
from jax.sharding import PartitionSpec as P

NV = 64
FACES = 6
REACH = 3
STEPS = 2
LANES = 128
SUB = 8

TIME_STEP = 0.015
SHEAR = 0.1
POWER = 0.81
SPEED_LIMIT = 6.0
H = 2.0 * SPEED_LIMIT / NV
WEIGHT = H**3 * (2.0 * math.pi) ** (-1.5)

CHUNKS = NV * NV // LANES
TILES = CHUNKS // SUB

FV, VOL, WT, WALL, LOCAL, FIRST = 0, 18, 19, 20, 26, 32
GEO = 33
WALL_LINK = -64
BEFORE_PAIRS = tuple((g, r) for g in range(REACH) for r in range(g, REACH))
EMIT, ABSORB = 13, 19
SUMS = 25

F32 = jnp.float32


def lane_iota():
    return lax.broadcasted_iota(jnp.int32, (SUB, LANES), 1)


def sub_iota():
    return lax.broadcasted_iota(jnp.int32, (SUB, LANES), 0)


def half_of(lane):
    return (lane >= NV).astype(F32)


def third_component(lane):
    c = jnp.where(lane >= NV, lane - NV, lane).astype(F32)
    return -SPEED_LIMIT + (c + 0.5) * H


def tile_nodes(t):
    lane = lane_iota()
    b = (2 * SUB * t + 2 * sub_iota()).astype(F32) + half_of(lane)
    return -SPEED_LIMIT + (b + 0.5) * H, third_component(lane)


def column(tile, p):
    return jnp.broadcast_to(tile[:, p : p + 1], (SUB, LANES))


def splat(ref, i, g):
    return jnp.broadcast_to(ref[i, pl.ds(g, 1), :], (SUB, LANES))


def total(tile):
    return jnp.broadcast_to(jnp.sum(tile, axis=1, keepdims=True), (SUB, LANES))


def face_coefficients(geo_ref, k, g):
    return [splat(geo_ref, FV + FACES * i + k, g) for i in range(3)]


def at_rows(start, size=SUB):
    return pl.ds(pl.multiple_of(start, SUB), size)


def wall_tiles(wall_temp):
    rt = 1.0 / wall_temp
    scale = rt * jnp.sqrt(rt)
    out = []
    for t in range(TILES):
        xb, xc = tile_nodes(t)
        out.append(scale * jnp.exp(-0.5 * (xb * xb + xc * xc) * rt))
    return out


def pack_sums(arrays, start):
    lane = lane_iota()
    out = jnp.zeros((SUB, LANES), F32)
    for p, x in enumerate(arrays):
        out = jnp.where(lane == start + p, total(x), out)
    return out


def over_sublanes(ref, k):
    out = ref[k, pl.ds(0, SUB, stride=SUB), :]
    for s in range(1, SUB):
        out = out + ref[k, pl.ds(s, SUB, stride=SUB), :]
    return out


def list_faces(links_ref, wanted, cell_ref, face_ref):
    count = 0
    for g in range(SUB):
        for k in range(FACES):
            cell_ref[count] = g
            face_ref[count] = k
            count = count + wanted(links_ref[k, g]).astype(jnp.int32)
    return count


def is_wall(j):
    return j == WALL_LINK


def is_remote(j):
    return jnp.logical_or(j >= SUB, jnp.logical_and(j < 0, j != WALL_LINK))


def face_lists():
    return [pltpu.SMEM((FACES * SUB + 1,), jnp.int32)] * 2


def unroll(planes, most):
    return math.gcd(planes, most)


def finish_polynomials(y, first, planes):
    y0, y1, y2, y3, by0, by1, by2, bby0, bby1, bbby0 = y
    m = first + 0.5 * (planes - 1) * H
    c = third_component(lane_iota())
    cc = c * c
    a = y1 + m * y0
    aa = y2 + m * (2.0 * y1 + m * y0)
    aaa = y3 + m * (3.0 * y2 + m * (3.0 * y1 + m * y0))
    ab = by1 + m * by0
    aab = by2 + m * (2.0 * by1 + m * by0)
    abb = bby1 + m * bby0
    return (
        y0,
        a,
        by0,
        c * y0,
        aa,
        bby0,
        cc * y0,
        ab,
        c * a,
        c * by0,
        aaa + abb + cc * a,
        aab + bbby0 + cc * by0,
        c * (aa + bby0 + cc * y0),
    )


def polynomial_sums(f_ref, planes, parts_ref, first=0):
    half = planes // 2

    def cell(g, _):
        out = [None] * 10
        for t in range(TILES):
            y0 = y1 = y2 = y3 = None
            for i in range(half):
                d = (i + 0.5) * H
                hi = f_ref[g, pl.ds(((half + i) * TILES + t) * SUB, SUB), :]
                lo = f_ref[g, pl.ds(((half - 1 - i) * TILES + t) * SUB, SUB), :]
                s, r = hi + lo, hi - lo
                if i == 0:
                    y0, y1, y2, y3 = s, d * r, (d * d) * s, (d * d * d) * r
                else:
                    y0, y1, y2, y3 = y0 + s, y1 + d * r, y2 + (d * d) * s, y3 + (d * d * d) * r
            b, _c = tile_nodes(t)
            bb = b * b
            terms = (y0, y1, y2, y3, b * y0, b * y1, b * y2, bb * y0, bb * y1, bb * (b * y0))
            out = [x if o is None else o + x for o, x in zip(out, terms)]
        for p in range(10):
            parts_ref[p, at_rows((first + g) * SUB), :] = out[p]
        return 0

    lax.fori_loop(0, f_ref.shape[0], cell, 0)
    return [over_sublanes(parts_ref, p) for p in range(10)]


def native_polynomial_sums(native_ref, planes):
    half, side = planes // 2, CHUNKS // 2
    zero = jnp.zeros((SUB, LANES), F32)
    acc = [zero] * 10

    def plane(a, acc):
        xa = (a.astype(F32) - 0.5 * (planes - 1)) * H
        b0 = b1 = b2 = b3 = None
        for i in range(side):
            y = (2 * i + 1) * H
            hi = native_ref[at_rows((a * CHUNKS + side + i) * SUB), :]
            lo = native_ref[at_rows((a * CHUNKS + side - 1 - i) * SUB), :]
            s, d = hi + lo, hi - lo
            terms = (s, y * d, (y * y) * s, (y * y * y) * d)
            if i == 0:
                b0, b1, b2, b3 = terms
            else:
                b0, b1, b2, b3 = b0 + terms[0], b1 + terms[1], b2 + terms[2], b3 + terms[3]
        a0, a1, a2 = xa * b0, xa * b1, xa * b2
        aa0 = xa * a0
        new = (b0, a0, aa0, xa * aa0, b1, a1, xa * a1, b2, a2, b3)
        return tuple(x + z for x, z in zip(acc, new))

    g0, a0, aa0, aaa0, g1, a1, aa1, g2, a2, g3 = lax.fori_loop(0, planes, plane, tuple(acc))
    e = (half_of(lane_iota()) - 0.5) * H
    return [
        g0,
        a0,
        aa0,
        aaa0,
        g1 + e * g0,
        a1 + e * a0,
        aa1 + e * aa0,
        g2 + e * (2.0 * g1 + e * g0),
        a2 + e * (2.0 * a1 + e * a0),
        g3 + e * (3.0 * g2 + e * (3.0 * g1 + e * g0)),
    ]


def wall_sums(f_ref, planes, links_ref, geo_ref, sums_ref, cells, faces, with_absorbed):
    sums_ref[...] = jnp.zeros_like(sums_ref)

    def wall(i, _):
        g, k = cells[i], faces[i]
        v0, v1, v2 = face_coefficients(geo_ref, k, g)
        first = splat(geo_ref, FIRST, g)
        base = []
        for t in range(TILES):
            xb, xc = tile_nodes(t)
            base.append(v1 * xb + v2 * xc)
        if with_absorbed:
            wt = splat(geo_ref, WT, g)
            shape = wall_tiles(wt)

        def plane(a, acc):
            out, back = list(acc[0]), list(acc[1])
            xa = first + a.astype(F32) * H
            sa = v0 * xa
            if with_absorbed:
                wa = jnp.exp(-0.5 * xa * xa / wt)
            for t in range(TILES):
                s = sa + base[t]
                f = f_ref[g, at_rows((a * TILES + t) * SUB), :]
                out[t] = out[t] + jnp.maximum(s, 0.0) * f
                if with_absorbed:
                    back[t] = back[t] + jnp.maximum(-s, 0.0) * (wa * shape[t])
            return tuple(out), tuple(back)

        zeros = (jnp.zeros((SUB, LANES), F32),) * TILES
        out, back = lax.fori_loop(0, planes, plane, (zeros, zeros), unroll=unroll(planes, 16))
        at = at_rows(g * SUB)
        sums_ref[k, at, :] = (out[0] + out[1]) + (out[2] + out[3])
        if with_absorbed:
            sums_ref[FACES + k, at, :] = (back[0] + back[1]) + (back[2] + back[3])
        return 0

    lax.fori_loop(0, list_faces(links_ref, is_wall, cells, faces), wall, 0)


def sums_kernel(links_ref, geo_ref, f_ref, sums_out, parts_ref, face_ref, cells, faces):
    planes = f_ref.shape[1] // CHUNKS
    y = polynomial_sums(f_ref, planes, parts_ref)
    packed = pack_sums(finish_polynomials(y, geo_ref[FIRST], planes), 0)
    wall_sums(f_ref, planes, links_ref, geo_ref, face_ref, cells, faces, False)
    sums_out[...] = packed + pack_sums([over_sublanes(face_ref, k) for k in range(FACES)], EMIT)


def first_sums_kernel(links_ref, geo_ref, native_ref, f_ref, sums_out, face_ref, cells, faces):
    rows = f_ref.shape[1]
    planes = rows // CHUNKS

    def group(j, _):
        for g in range(SUB):
            f_ref[g, at_rows(j * SUB), :] = native_ref[pl.ds(j * SUB * SUB + g, SUB, stride=SUB), :]
        return 0

    lax.fori_loop(0, rows // SUB, group, 0, unroll=2)
    y = native_polynomial_sums(native_ref, planes)
    packed = pack_sums(finish_polynomials(y, geo_ref[FIRST], planes), 0)
    wall_sums(f_ref, planes, links_ref, geo_ref, face_ref, cells, faces, True)
    sums_out[...] = packed + pack_sums([over_sublanes(face_ref, k) for k in range(2 * FACES)], EMIT)


def spec(space):
    return pl.BlockSpec(memory_space=space)


def array(*shape):
    return jax.ShapeDtypeStruct(shape, F32)


def params(mib=4):
    return pltpu.CompilerParams(vmem_limit_bytes=mib * 1024 * 1024)


def traffic(rows, profiles):
    size = SUB * rows * LANES
    return pl.CostEstimate(flops=8 * profiles * size, bytes_accessed=4 * profiles * size, transcendentals=0)


def local_sums(links, geo, f):
    return pl.pallas_call(
        sums_kernel,
        in_specs=[spec(pltpu.SMEM), spec(pltpu.VMEM), spec(pltpu.VMEM)],
        out_specs=spec(pltpu.VMEM),
        out_shape=array(SUB, LANES),
        scratch_shapes=[
                pltpu.VMEM((10, SUB * SUB, LANES), F32),
            pltpu.VMEM((FACES, SUB * SUB, LANES), F32),
            *face_lists(),
        ],
        compiler_params=params(),
        cost_estimate=traffic(f.shape[1], 4),
        name="local_sums",
    )(links, geo, f)


def first_sums(links, geo, native):
    rows = native.shape[0] // SUB
    return pl.pallas_call(
        first_sums_kernel,
        in_specs=[spec(pltpu.SMEM), spec(pltpu.VMEM), spec(pltpu.VMEM)],
        out_specs=[spec(pltpu.VMEM)] * 2,
        out_shape=[array(SUB, rows, LANES), array(SUB, LANES)],
        scratch_shapes=[
                pltpu.VMEM((2 * FACES, SUB * SUB, LANES), F32),
            *face_lists(),
        ],
        compiler_params=params(),
        cost_estimate=traffic(rows, 5),
        name="first_sums",
    )(links, geo, native)


SPLIT_PARTS = 8


def is_odd():
    return lax.rem(lax.axis_index("space"), 2) == 1


def first_rows_kernel(native_hbm, native_ref, far_any, near_any, far_ref, near_ref, sems, far_sems, near_sems):
    rows = native_ref.shape[0]
    part = rows // SPLIT_PARTS
    copies = [
        pltpu.make_async_copy(
            native_hbm.at[pl.ds(i * part, part)], native_ref.at[pl.ds(i * part, part)], sems.at[i]
        )
        for i in range(SPLIT_PARTS)
    ]
    for c in copies:
        c.start()
    odd = is_odd()
    far = jnp.where(odd, SUB - REACH, 0)
    near = jnp.where(odd, 0, SUB - REACH)
    groups = part // (SUB * SUB)
    out = []

    for i, c in enumerate(copies):
        c.wait()

        def group(j, _):
            for r in range(REACH):
                at = at_rows(j * SUB)
                far_ref[r, at, :] = native_ref[pl.ds(j * SUB * SUB + far + r, SUB, stride=SUB), :]
                near_ref[r, at, :] = native_ref[pl.ds(j * SUB * SUB + near + r, SUB, stride=SUB), :]
            return 0

        lax.fori_loop(i * groups, (i + 1) * groups, group, 0, unroll=unroll(groups, 8))
        at = pl.ds(i * groups * SUB, groups * SUB)
        out.append(pltpu.make_async_copy(far_ref.at[:, at], far_any.at[:, at], far_sems.at[i]))
        out.append(pltpu.make_async_copy(near_ref.at[:, at], near_any.at[:, at], near_sems.at[i]))
        out[-2].start()
        out[-1].start()
    for c in out:
        c.wait()


def first_rows(native):
    rows = native.shape[0] // SUB
    halo = (REACH, rows, LANES)
    return pl.pallas_call(
        first_rows_kernel,
        in_specs=[spec(pltpu.HBM)],
        out_specs=[spec(pltpu.VMEM), spec(pl.ANY), spec(pl.ANY)],
        out_shape=[array(*native.shape), array(*halo), array(*halo)],
        scratch_shapes=[pltpu.VMEM(halo, F32)] * 2 + [pltpu.SemaphoreType.DMA((SPLIT_PARTS,))] * 3,
        compiler_params=params(),
        cost_estimate=traffic(rows, 4),
        name="first_rows",
    )(pltpu.with_memory_space_constraint(native, pltpu.HBM))


def pair_weights(links_ref, geo_ref, pairs_ref, cells, faces):
    rows = pairs_ref.shape[1]
    planes = rows // CHUNKS
    first = splat(geo_ref, FIRST, 0)

    def clear(j, _):
        for p in range(pairs_ref.shape[0]):
            pairs_ref[p, at_rows(j * SUB), :] = jnp.zeros((SUB, LANES), F32)
        return 0

    lax.fori_loop(0, rows // SUB, clear, 0, unroll=4)

    def remote(i, _):
        g, k = cells[i], faces[i]
        j = links_ref[k, g]
        edge = g - (SUB - REACH)
        before = g * REACH - g * (g - 1) // 2 + (j + REACH) - g
        after = len(BEFORE_PAIRS) + edge * (edge + 1) // 2 + j - SUB
        at_pair = jnp.where(j < 0, before, after)
        scale = -TIME_STEP / splat(geo_ref, VOL, g)
        v0, v1, v2 = [scale * x for x in face_coefficients(geo_ref, k, g)]
        base = []
        for t in range(TILES):
            xb, xc = tile_nodes(t)
            base.append(v1 * xb + v2 * xc)

        def plane(a, _):
            sa = v0 * (first + a.astype(F32) * H)
            for t in range(TILES):
                at = at_rows((a * TILES + t) * SUB)
                pairs_ref[at_pair, at, :] = pairs_ref[at_pair, at, :] + jnp.maximum(sa + base[t], 0.0)
            return 0

        lax.fori_loop(0, planes, plane, 0, unroll=unroll(planes, 8))
        return 0

    lax.fori_loop(0, list_faces(links_ref, is_remote, cells, faces), remote, 0)


def gather_sums(tile):
    size = lax.axis_size("vel")
    if size not in (2, 4):
        return [lax.psum(tile, "vel")]
    others = [lax.ppermute(tile, "vel", [(i, i ^ s) for i in range(size)]) for s in range(1, size)]
    return [tile, *reversed(others)]


def doubling_sums(tile):
    size = lax.axis_size("vel")
    if size != 4:
        return gather_sums(tile)
    pair = tile + lax.ppermute(tile, "vel", [(i, i ^ 1) for i in range(size)])
    return [pair, lax.ppermute(pair, "vel", [(i, i ^ 2) for i in range(size)])]


def add_tiles(refs):
    tiles = [r[...] for r in refs]
    tiles = tiles[:1] + tiles[:0:-1]
    while len(tiles) > 1:
        tiles = [tiles[i] + tiles[i + 1] for i in range(0, len(tiles), 2)]
    return tiles[0]


def quantities(tile):
    m = [WEIGHT * column(tile, p) for p in range(13)]
    n = m[0]
    rn = 1.0 / n
    u = [m[1 + i] * rn for i in range(3)]
    uu = u[0] * u[0] + u[1] * u[1] + u[2] * u[2]
    trace = m[4] + m[5] + m[6]
    width = trace - n * uu
    temperature = width * rn * (1.0 / 3.0)
    second = [[m[4], m[7], m[8]], [m[7], m[5], m[9]], [m[8], m[9], m[6]]]
    q = []
    for i in range(3):
        across = u[0] * second[i][0] + u[1] * second[i][1] + u[2] * second[i][2]
        q.append(0.5 * (m[10 + i] - 2.0 * across - u[i] * trace + 2.0 * uu * m[1 + i]))
    return n, u, temperature, q


def macro_kernel(*refs):
    out_ref = refs[-1]
    n, u, temperature, q = quantities(add_tiles(refs[:-1]))
    lane, sub = lane_iota(), sub_iota()
    for i, x in enumerate((n, *u, temperature, *q)):
        row = jnp.sum(jnp.where(lane == sub, x, 0.0), axis=0, keepdims=True)
        out_ref[pl.ds(i, 1), :] = row[:, :SUB]


def macro(tiles):
    return pl.pallas_call(
        macro_kernel,
        in_specs=[spec(pltpu.VMEM)] * len(tiles),
        out_specs=spec(pltpu.VMEM),
        out_shape=array(8, SUB),
        compiler_params=params(1),
        name="macro",
    )(*tiles)


def flux_kernel(with_pairs, links_ref, geo_ref, f_ref, out_ref, *refs):
    if with_pairs:
        pairs_ref, cells, faces = refs[0], refs[-2], refs[-1]
        pair_weights(links_ref, geo_ref, pairs_ref, cells, faces)
        refs = refs[1:-2]
    coef, bases, stays, source, face = refs
    planes = f_ref.shape[1] // CHUNKS
    scale = -TIME_STEP / geo_ref[VOL]
    for i in range(3):
        whole = None
        for k in range(FACES):
            x = scale * geo_ref[FV + FACES * i + k]
            coef[FACES * i + k] = x
            whole = x if whole is None else whole + x
        coef[3 * FACES + i] = whole

    def table(g, _):
        w = [[splat(coef, FACES * i + k, g) for i in (1, 2)] for k in range(FACES)]
        whole = [splat(coef, 3 * FACES + i, g) for i in (1, 2)]
        for t in range(TILES):
            xb, xc = tile_nodes(t)
            for k in range(FACES):
                bases[k, g * TILES + t] = w[k][0] * xb + w[k][1] * xc
            stays[g * TILES + t] = 1.0 + whole[0] * xb + whole[1] * xc
        return 0

    lax.fori_loop(0, SUB, table, 0, unroll=2)

    def cell(g, _):
        count = 0
        for k in range(FACES):
            j = links_ref[k, g]
            source[count] = j
            face[count] = k
            count = count + jnp.logical_and(j >= 0, j < SUB).astype(jnp.int32)
        for n in range(FACES + 1):

            @pl.when(count == n)
            def _():
                own_faces(g, n)

        return 0

    def own_faces(g, n):
        at_source = [source[i] for i in range(n)]
        first_weight = [splat(coef, face[k], g) for k in range(n)]
        whole = splat(coef, 3 * FACES, g)
        x0 = splat(geo_ref, FIRST, g)
        base = [[bases[face[k], g * TILES + t] for k in range(n)] for t in range(TILES)]
        stay = [stays[g * TILES + t] for t in range(TILES)]

        def plane(a, _):
            xa = x0 + a.astype(F32) * H
            sa = [w * xa for w in first_weight]
            stay_a = whole * xa
            for t in range(TILES):
                at = at_rows((a * TILES + t) * SUB)
                f = f_ref[g, at, :]
                acc = f * (stay_a + stay[t])
                for k in range(n):
                    acc = acc + jnp.maximum(sa[k] + base[t][k], 0.0) * (f_ref[at_source[k], at, :] - f)
                out_ref[g, at, :] = acc
            return 0

        lax.fori_loop(0, planes, plane, 0, unroll=unroll(planes, 8))

    lax.fori_loop(0, SUB, cell, 0)


def flux(with_pairs, links, geo, f):
    rows = f.shape[1]
    pairs = 2 * len(BEFORE_PAIRS)
    return pl.pallas_call(
        functools.partial(flux_kernel, with_pairs),
        in_specs=[spec(pltpu.SMEM), spec(pltpu.VMEM), spec(pltpu.VMEM)],
        out_specs=[spec(pltpu.VMEM)] * (2 if with_pairs else 1),
        out_shape=[array(*f.shape)] + ([array(pairs, rows, LANES)] if with_pairs else []),
        scratch_shapes=[
            pltpu.VMEM((3 * FACES + 3, SUB, LANES), F32),
            pltpu.VMEM((FACES, SUB * TILES, SUB, LANES), F32),
            pltpu.VMEM((SUB * TILES, SUB, LANES), F32),
            pltpu.SMEM((FACES + 1,), jnp.int32),
            pltpu.SMEM((FACES + 1,), jnp.int32),
        ]
        + (face_lists() if with_pairs else []),
        compiler_params=params(),
        cost_estimate=traffic(rows, 9 if with_pairs else 7),
        name="flux",
    )(links, geo, f)


def target_kernel(count, links_ref, geo_ref, absorbed_in, *refs):
    sums_refs, (f_ref, part_ref, out_ref, *sum_out, ta, tiles_ref, coef, cells, faces) = refs[:count], refs[count:]
    planes = f_ref.shape[1] // CHUNKS
    sums = add_tiles(sums_refs)
    for ref in sum_out:
        ref[...] = sums
    absorbed = sums if absorbed_in is None else absorbed_in[...]
    n, u, temperature, q = quantities(sums)
    rt = 1.0 / temperature
    rate = TIME_STEP * n * temperature / (SHEAR * jnp.exp(POWER * jnp.log(temperature)))
    height = rate * n * rt * jnp.sqrt(rt)
    slope = (1.0 / 3.0) / (5.0 * n * temperature * temperature)
    coef[0] = rate
    coef[1] = rt
    coef[2], coef[3] = u[1], u[2]
    coef[4], coef[5] = slope * q[1], slope * q[2]
    for k in range(FACES):
        wall = geo_ref[WALL + k] > 0.5
        coef[6 + k] = column(sums, EMIT + k) / jnp.where(wall, column(absorbed, ABSORB + k), 1.0)
    first = geo_ref[FIRST]

    wt = geo_ref[WT]

    def plane_table(a, _):
        xa = first + a.astype(F32) * H
        ca = xa - u[0]
        za = ca * ca * rt
        ta[0, a] = height * jnp.exp(-0.5 * za)
        ta[1, a] = slope * q[0] * ca
        ta[2, a] = za - 5.0
        ta[3, a] = jnp.exp(-0.5 * xa * xa / wt)
        return 0

    lax.fori_loop(0, planes, plane_table, 0, unroll=unroll(planes, 8))

    def tile_table(g, _):
        rtg = splat(coef, 1, g)
        ub, uc = splat(coef, 2, g), splat(coef, 3, g)
        qb, qc = splat(coef, 4, g), splat(coef, 5, g)
        shape = wall_tiles(splat(geo_ref, WT, g))
        for t in range(TILES):
            xb, xc = tile_nodes(t)
            cb, cc = xb - ub, xc - uc
            z = (cb * cb + cc * cc) * rtg
            at = g * TILES + t
            tiles_ref[0, at] = jnp.exp(-0.5 * z)
            tiles_ref[1, at] = cb * qb + cc * qc
            tiles_ref[2, at] = z
            tiles_ref[3, at] = shape[t]
        return 0

    lax.fori_loop(0, SUB, tile_table, 0, unroll=4)

    def at_plane(i, a, g):
        return jnp.broadcast_to(ta[i, a, pl.ds(g, 1), :], (SUB, LANES))

    def cell(g, _):
        rate_g = splat(coef, 0, g)
        bell, heat, zz = [[tiles_ref[i, g * TILES + t] for t in range(TILES)] for i in range(3)]

        def plane(a, _):
            height_a, heat_a, z_a = [at_plane(i, a, g) for i in range(3)]
            for t in range(TILES):
                where = (g, at_rows((a * TILES + t) * SUB), slice(None))
                f = f_ref[where]
                target = (height_a * bell[t]) * (1.0 + (heat_a + heat[t]) * (z_a + zz[t]))
                out_ref[where] = (part_ref[where] - rate_g * f) + target
            return 0

        lax.fori_loop(0, planes, plane, 0, unroll=unroll(planes, 16))
        return 0

    lax.fori_loop(0, SUB, cell, 0)

    def wall(i, _):
        g, k = cells[i], faces[i]
        x0 = splat(geo_ref, FIRST, g)
        ratio = splat(coef, 6 + k, g)
        scale = -TIME_STEP / splat(geo_ref, VOL, g)
        v0, v1, v2 = [scale * x for x in face_coefficients(geo_ref, k, g)]
        base, shape = [], []
        for t in range(TILES):
            xb, xc = tile_nodes(t)
            base.append(v1 * xb + v2 * xc)
            shape.append(ratio * tiles_ref[3, g * TILES + t])

        def plane(a, _):
            wa = at_plane(3, a, g)
            sa = v0 * (x0 + a.astype(F32) * H)
            for t in range(TILES):
                where = (g, at_rows((a * TILES + t) * SUB), slice(None))
                f = f_ref[where]
                out_ref[where] = out_ref[where] + jnp.maximum(sa + base[t], 0.0) * (wa * shape[t] - f)
            return 0

        lax.fori_loop(0, planes, plane, 0, unroll=unroll(planes, 16))
        return 0

    lax.fori_loop(0, list_faces(links_ref, is_wall, cells, faces), wall, 0)


def add_target(links, geo, absorbed, tiles, f, part):
    rows = f.shape[1]
    vmem = spec(pltpu.VMEM)
    given = [links, geo] + ([] if absorbed is None else [absorbed]) + list(tiles) + [f, part]

    def kernel(links_ref, geo_in, *refs):
        if absorbed is None:
            target_kernel(len(tiles), links_ref, geo_in, None, *refs)
        else:
            target_kernel(len(tiles), links_ref, geo_in, *refs)

    return pl.pallas_call(
        kernel,
        in_specs=[spec(pltpu.SMEM)] + [vmem] * (len(given) - 1),
        out_specs=[vmem] * (2 if absorbed is None else 1),
        out_shape=[array(*part.shape)] + ([array(SUB, LANES)] if absorbed is None else []),
        input_output_aliases={len(given) - 1: 0},
        scratch_shapes=[
                pltpu.VMEM((4, rows // CHUNKS, SUB, LANES), F32),
            pltpu.VMEM((4, SUB * TILES, SUB, LANES), F32),
            pltpu.VMEM((6 + FACES, SUB, LANES), F32),
            *face_lists(),
        ],
        compiler_params=params(),
        cost_estimate=traffic(rows, 7),
        name="add_target",
    )(*given)


def side_terms(high, pairs_ref, halo_ref, f_ref, at):
    terms = [None] * REACH
    rows = [halo_ref[r, at, :] for r in range(REACH)]
    first = SUB - REACH if high else 0
    own = [f_ref[first + e, at, :] for e in range(REACH)]
    count = len(BEFORE_PAIRS)
    pairs = [(e, r) for e in range(REACH) for r in range(e + 1)] if high else BEFORE_PAIRS
    for p, (e, r) in enumerate(pairs):
        term = pairs_ref[p + count if high else p, at, :] * (rows[r] - own[e])
        terms[e] = term if terms[e] is None else terms[e] + term
    return first, terms


def for_side(far, run):
    odd = is_odd()

    @pl.when(odd)
    def _():
        run(far)

    @pl.when(jnp.logical_not(odd))
    def _():
        run(not far)


def add_side(far, pairs_ref, halo_ref, old_ref, part_ref, f_ref, rows_ref):
    def run(high):
        def group(j, _):
            at = at_rows(j * SUB)
            first, terms = side_terms(high, pairs_ref, halo_ref, old_ref, at)
            for e in range(REACH):
                x = part_ref[first + e, at, :] + terms[e]
                f_ref[first + e, at, :] = x
                if rows_ref is not None:
                    rows_ref[e, at, :] = x
            return 0

        groups = part_ref.shape[1] // SUB
        lax.fori_loop(0, groups, group, 0, unroll=unroll(groups, 8))

    for_side(far, run)


def edge(far, pairs, halo, old, part):
    rows = part.shape[1]
    return pl.pallas_call(
        functools.partial(add_side, far),
        in_specs=[spec(pltpu.VMEM)] * 4,
        out_specs=[spec(pltpu.VMEM)] * 2,
        out_shape=[array(SUB, rows, LANES), array(REACH, rows, LANES)],
        input_output_aliases={3: 0},
        compiler_params=params(),
        cost_estimate=traffic(rows, 2),
        name="far_edge" if far else "near_edge",
    )(pairs, halo, old, part)


def last_near_kernel(geo_ref, pairs_ref, halo_ref, old_ref, part_ref, f_ref, sums_out, parts_ref):
    add_side(False, pairs_ref, halo_ref, old_ref, part_ref, f_ref, None)
    planes = f_ref.shape[1] // CHUNKS
    y = polynomial_sums(f_ref, planes, parts_ref)
    sums_out[...] = pack_sums(finish_polynomials(y, geo_ref[FIRST], planes), 0)


def last_near(geo, pairs, near, old, part):
    rows = part.shape[1]
    return pl.pallas_call(
        last_near_kernel,
        in_specs=[spec(pltpu.VMEM)] * 5,
        out_specs=[spec(pltpu.VMEM)] * 2,
        out_shape=[array(SUB, rows, LANES), array(SUB, LANES)],
        input_output_aliases={4: 0},
        scratch_shapes=[pltpu.VMEM((10, SUB * SUB, LANES), F32)],
        compiler_params=params(),
        cost_estimate=traffic(rows, 3),
        name="last_near",
    )(geo, pairs, near, old, part)


def last_far_kernel(count, geo_ref, pairs_ref, *refs):
    halos, (old_ref, sums_in, terms_ref, sums_out, parts_ref) = refs[:count], refs[count:]
    rows = old_ref.shape[1]
    planes = rows // CHUNKS
    parts_ref[...] = jnp.zeros_like(parts_ref)

    def run(high):
        def add(halo_ref):
            def group(j, _):
                at = at_rows(j * SUB)
                _first, terms = side_terms(high, pairs_ref, halo_ref, old_ref, at)
                for e in range(REACH):
                    terms_ref[e, at, :] = terms[e]
                return 0

            lax.fori_loop(0, rows // SUB, group, 0, unroll=unroll(rows // SUB, 8))

        if count == 1 or not high:
            add(halos[0])
        else:
            late = lax.axis_index("space") == LATE_FLOW[1]

            @pl.when(late)
            def _():
                add(halos[1])

            @pl.when(jnp.logical_not(late))
            def _():
                add(halos[0])

        y = polynomial_sums(terms_ref, planes, parts_ref, SUB - REACH if high else 0)
        sums_out[...] = sums_in[...] + pack_sums(finish_polynomials(y, geo_ref[FIRST], planes), 0)

    for_side(True, run)


def last_far(geo, pairs, halos, old, sums):
    rows = old.shape[1]
    return pl.pallas_call(
        functools.partial(last_far_kernel, len(halos)),
        in_specs=[spec(pltpu.VMEM)] * (4 + len(halos)),
        out_specs=[spec(pltpu.VMEM)] * 2,
        out_shape=[array(REACH, rows, LANES), array(SUB, LANES)],
        scratch_shapes=[pltpu.VMEM((10, SUB * SUB, LANES), F32)],
        compiler_params=params(),
        cost_estimate=traffic(rows, 2),
        name="last_far",
    )(geo, pairs, *halos, old, sums)


LAST_PARTS = 4


def result_kernel(part_ref, terms_ref, out_hbm, native_ref, sems):
    part = part_ref.shape[1] // SUB // LAST_PARTS

    def copy(i):
        at = pl.ds(i * part * SUB * SUB, part * SUB * SUB)
        return pltpu.make_async_copy(native_ref.at[at], out_hbm.at[at], sems.at[i])

    def run(high):
        first = SUB - REACH if high else 0
        for i in range(LAST_PARTS):

            def group(j, _):
                at = at_rows(j * SUB)
                for g in range(SUB):
                    x = part_ref[g, at, :]
                    if 0 <= g - first < REACH:
                        x = x + terms_ref[g - first, at, :]
                    native_ref[pl.ds(j * SUB * SUB + g, SUB, stride=SUB), :] = x
                return 0

            lax.fori_loop(i * part, (i + 1) * part, group, 0, unroll=unroll(part, 4))
            copy(i).start()

    for_side(True, run)
    for i in range(LAST_PARTS):
        copy(i).wait()


def result(part, terms):
    rows = part.shape[1]
    native = (SUB * rows, LANES)
    return pl.pallas_call(
        result_kernel,
        in_specs=[spec(pltpu.VMEM)] * 2,
        out_specs=spec(pltpu.HBM),
        out_shape=array(*native),
        scratch_shapes=[pltpu.VMEM(native, F32), pltpu.SemaphoreType.DMA((LAST_PARTS,))],
        compiler_params=params(),
        cost_estimate=traffic(rows, 3),
        name="result",
    )(part, terms)


LATE_SLABS = 8
LATE_FLOW = (2, 1)


def swap(rows, start, without=()):
    pairs = [(i, i + 1) for i in range(start, lax.axis_size("space") - 1, 2)]
    pairs = pairs + [(j, i) for i, j in pairs]
    return lax.ppermute(rows, "space", [p for p in pairs if p not in without])


def late_flow(rows, after):
    rows, _ = lax.optimization_barrier((rows, after))
    return lax.ppermute(rows, "space", [LATE_FLOW])


def per_device(particle_profile, neighbors, face_vectors, volumes, wall_temp):
    cells, points = particle_profile.shape
    rows = points // LANES
    plane_count = NV // lax.axis_size("vel")
    native = particle_profile.reshape(cells, rows, LANES).transpose(1, 0, 2).reshape(cells * rows, LANES)
    wall = neighbors < 0
    links = jnp.where(wall, WALL_LINK, neighbors - lax.axis_index("space") * cells)
    own = (links >= 0) & (links < cells)
    first = -SPEED_LIMIT + ((lax.axis_index("vel") * plane_count).astype(F32) + 0.5) * H
    geo = jnp.concatenate(
        [
            face_vectors.reshape(3 * FACES, cells),
            volumes[None],
            wall_temp[None],
            wall.astype(F32),
            own.astype(F32),
            jnp.full((1, cells), first, F32),
        ]
    )
    geo = jnp.broadcast_to(geo[:, :, None], (GEO, cells, LANES))
    native, far, near = first_rows(native)
    far, near = swap(far, 1), swap(near, 0)
    f, sums = first_sums(links, geo, native)
    tiles = gather_sums(sums)
    part, pairs = flux(True, links, geo, f)
    part, absorbed = add_target(links, geo, None, tiles, f, part)
    part, near = edge(False, pairs, near, f, part)
    near = swap(near, 0)
    f, far = edge(True, pairs, far, f, part)
    sums = local_sums(links, geo, f)
    if lax.axis_size("space") == LATE_SLABS:
        halos = [swap(far, 1, (LATE_FLOW,)), late_flow(far, sums)]
        sums, near = lax.optimization_barrier((sums, near))
    else:
        halos = [swap(far, 1)]
    tiles = gather_sums(sums)
    (part,) = flux(False, links, geo, f)
    (part,) = add_target(links, geo, absorbed, tiles, f, part)
    part, sums = last_near(geo, pairs, near, f, part)
    terms, sums = last_far(geo, pairs, halos, f, sums)
    tiles = doubling_sums(sums)
    native = result(part, terms)
    macro_quantities = macro(tiles)
    evolved = native.reshape(rows, cells, LANES).transpose(1, 0, 2).reshape(cells, points)
    return evolved, macro_quantities


def solution(mesh):
    return jax.shard_map(
        per_device,
        mesh=mesh,
        in_specs=(
            P("space", "vel"),
            P(None, "space"),
            P(None, None, "space"),
            P("space"),
            P("space"),
        ),
        out_specs=(P("space", "vel"), P(None, "space")),
        check_vma=False,
    )
```

```python
import functools
import math

import jax
import jax.numpy as jnp
from jax import lax
from jax.experimental import pallas as pl
from jax.experimental.pallas import tpu as pltpu
from jax.sharding import PartitionSpec as P

NV = 64
FACES = 6
REACH = 3
STEPS = 2
LANES = 128
SUB = 8

TIME_STEP = 0.015
SHEAR = 0.1
POWER = 0.81
SPEED_LIMIT = 6.0
H = 2.0 * SPEED_LIMIT / NV
WEIGHT = H**3 * (2.0 * math.pi) ** (-1.5)

CHUNKS = NV * NV // LANES
TILES = CHUNKS // SUB

FV, VOL, WT, WALL, LOCAL, FIRST = 0, 18, 19, 20, 26, 32
GEO = 33
WALL_LINK = -64
BEFORE_PAIRS = tuple((g, r) for g in range(REACH) for r in range(g, REACH))
EMIT, ABSORB = 13, 19
SUMS = 25

F32 = jnp.float32


def lane_iota():
    return lax.broadcasted_iota(jnp.int32, (SUB, LANES), 1)


def sub_iota():
    return lax.broadcasted_iota(jnp.int32, (SUB, LANES), 0)


def half_of(lane):
    return (lane >= NV).astype(F32)


def third_component(lane):
    c = jnp.where(lane >= NV, lane - NV, lane).astype(F32)
    return -SPEED_LIMIT + (c + 0.5) * H


def tile_nodes(t):
    lane = lane_iota()
    b = (2 * SUB * t + 2 * sub_iota()).astype(F32) + half_of(lane)
    return -SPEED_LIMIT + (b + 0.5) * H, third_component(lane)


def column(tile, p):
    return jnp.broadcast_to(tile[:, p : p + 1], (SUB, LANES))


def splat(ref, i, g):
    return jnp.broadcast_to(ref[i, pl.ds(g, 1), :], (SUB, LANES))


def total(tile):
    return jnp.broadcast_to(jnp.sum(tile, axis=1, keepdims=True), (SUB, LANES))


def face_coefficients(geo_ref, k, g):
    return [splat(geo_ref, FV + FACES * i + k, g) for i in range(3)]


def at_rows(start, size=SUB):
    return pl.ds(pl.multiple_of(start, SUB), size)


def wall_tiles(wall_temp):
    rt = 1.0 / wall_temp
    scale = rt * jnp.sqrt(rt)
    out = []
    for t in range(TILES):
        xb, xc = tile_nodes(t)
        out.append(scale * jnp.exp(-0.5 * (xb * xb + xc * xc) * rt))
    return out


def pack_sums(arrays, start):
    lane = lane_iota()
    out = jnp.zeros((SUB, LANES), F32)
    for p, x in enumerate(arrays):
        out = jnp.where(lane == start + p, total(x), out)
    return out


def over_sublanes(ref, k):
    out = ref[k, pl.ds(0, SUB, stride=SUB), :]
    for s in range(1, SUB):
        out = out + ref[k, pl.ds(s, SUB, stride=SUB), :]
    return out


def list_faces(links_ref, wanted, cell_ref, face_ref):
    count = 0
    for g in range(SUB):
        for k in range(FACES):
            cell_ref[count] = g
            face_ref[count] = k
            count = count + wanted(links_ref[k, g]).astype(jnp.int32)
    return count


def is_wall(j):
    return j == WALL_LINK


def is_remote(j):
    return jnp.logical_or(j >= SUB, jnp.logical_and(j < 0, j != WALL_LINK))


def face_lists():
    return [pltpu.SMEM((FACES * SUB + 1,), jnp.int32)] * 2


def unroll(planes, most):
    return math.gcd(planes, most)


def finish_polynomials(y, first, planes):
    y0, y1, y2, y3, by0, by1, by2, bby0, bby1, bbby0 = y
    m = first + 0.5 * (planes - 1) * H
    c = third_component(lane_iota())
    cc = c * c
    a = y1 + m * y0
    aa = y2 + m * (2.0 * y1 + m * y0)
    aaa = y3 + m * (3.0 * y2 + m * (3.0 * y1 + m * y0))
    ab = by1 + m * by0
    aab = by2 + m * (2.0 * by1 + m * by0)
    abb = bby1 + m * bby0
    return (
        y0,
        a,
        by0,
        c * y0,
        aa,
        bby0,
        cc * y0,
        ab,
        c * a,
        c * by0,
        aaa + abb + cc * a,
        aab + bbby0 + cc * by0,
        c * (aa + bby0 + cc * y0),
    )


def polynomial_sums(f_ref, planes, parts_ref, first=0):
    half = planes // 2

    def cell(g, _):
        out = [None] * 10
        for t in range(TILES):
            y0 = y1 = y2 = y3 = None
            for i in range(half):
                d = (i + 0.5) * H
                hi = f_ref[g, pl.ds(((half + i) * TILES + t) * SUB, SUB), :]
                lo = f_ref[g, pl.ds(((half - 1 - i) * TILES + t) * SUB, SUB), :]
                s, r = hi + lo, hi - lo
                if i == 0:
                    y0, y1, y2, y3 = s, d * r, (d * d) * s, (d * d * d) * r
                else:
                    y0, y1, y2, y3 = y0 + s, y1 + d * r, y2 + (d * d) * s, y3 + (d * d * d) * r
            b, _c = tile_nodes(t)
            bb = b * b
            terms = (y0, y1, y2, y3, b * y0, b * y1, b * y2, bb * y0, bb * y1, bb * (b * y0))
            out = [x if o is None else o + x for o, x in zip(out, terms)]
        for p in range(10):
            parts_ref[p, at_rows((first + g) * SUB), :] = out[p]
        return 0

    lax.fori_loop(0, f_ref.shape[0], cell, 0)
    return [over_sublanes(parts_ref, p) for p in range(10)]


def native_polynomial_sums(native_ref, planes):
    half, side = planes // 2, CHUNKS // 2
    zero = jnp.zeros((SUB, LANES), F32)
    acc = [zero] * 10

    def plane(a, acc):
        xa = (a.astype(F32) - 0.5 * (planes - 1)) * H
        b0 = b1 = b2 = b3 = None
        for i in range(side):
            y = (2 * i + 1) * H
            hi = native_ref[at_rows((a * CHUNKS + side + i) * SUB), :]
            lo = native_ref[at_rows((a * CHUNKS + side - 1 - i) * SUB), :]
            s, d = hi + lo, hi - lo
            terms = (s, y * d, (y * y) * s, (y * y * y) * d)
            if i == 0:
                b0, b1, b2, b3 = terms
            else:
                b0, b1, b2, b3 = b0 + terms[0], b1 + terms[1], b2 + terms[2], b3 + terms[3]
        a0, a1, a2 = xa * b0, xa * b1, xa * b2
        aa0 = xa * a0
        new = (b0, a0, aa0, xa * aa0, b1, a1, xa * a1, b2, a2, b3)
        return tuple(x + z for x, z in zip(acc, new))

    g0, a0, aa0, aaa0, g1, a1, aa1, g2, a2, g3 = lax.fori_loop(0, planes, plane, tuple(acc))
    e = (half_of(lane_iota()) - 0.5) * H
    return [
        g0,
        a0,
        aa0,
        aaa0,
        g1 + e * g0,
        a1 + e * a0,
        aa1 + e * aa0,
        g2 + e * (2.0 * g1 + e * g0),
        a2 + e * (2.0 * a1 + e * a0),
        g3 + e * (3.0 * g2 + e * (3.0 * g1 + e * g0)),
    ]


def wall_sums(f_ref, planes, links_ref, geo_ref, sums_ref, cells, faces, with_absorbed):
    sums_ref[...] = jnp.zeros_like(sums_ref)

    def wall(i, _):
        g, k = cells[i], faces[i]
        v0, v1, v2 = face_coefficients(geo_ref, k, g)
        first = splat(geo_ref, FIRST, g)
        base = []
        for t in range(TILES):
            xb, xc = tile_nodes(t)
            base.append(v1 * xb + v2 * xc)
        if with_absorbed:
            wt = splat(geo_ref, WT, g)
            shape = wall_tiles(wt)

        def plane(a, acc):
            out, back = list(acc[0]), list(acc[1])
            xa = first + a.astype(F32) * H
            sa = v0 * xa
            if with_absorbed:
                wa = jnp.exp(-0.5 * xa * xa / wt)
            for t in range(TILES):
                s = sa + base[t]
                f = f_ref[g, at_rows((a * TILES + t) * SUB), :]
                out[t] = out[t] + jnp.maximum(s, 0.0) * f
                if with_absorbed:
                    back[t] = back[t] + jnp.maximum(-s, 0.0) * (wa * shape[t])
            return tuple(out), tuple(back)

        zeros = (jnp.zeros((SUB, LANES), F32),) * TILES
        out, back = lax.fori_loop(0, planes, plane, (zeros, zeros), unroll=unroll(planes, 16))
        at = at_rows(g * SUB)
        sums_ref[k, at, :] = (out[0] + out[1]) + (out[2] + out[3])
        if with_absorbed:
            sums_ref[FACES + k, at, :] = (back[0] + back[1]) + (back[2] + back[3])
        return 0

    lax.fori_loop(0, list_faces(links_ref, is_wall, cells, faces), wall, 0)


def sums_kernel(links_ref, geo_ref, f_ref, sums_out, parts_ref, face_ref, cells, faces):
    planes = f_ref.shape[1] // CHUNKS
    y = polynomial_sums(f_ref, planes, parts_ref)
    packed = pack_sums(finish_polynomials(y, geo_ref[FIRST], planes), 0)
    wall_sums(f_ref, planes, links_ref, geo_ref, face_ref, cells, faces, False)
    sums_out[...] = packed + pack_sums([over_sublanes(face_ref, k) for k in range(FACES)], EMIT)


def first_sums_kernel(links_ref, geo_ref, native_ref, f_ref, sums_out, face_ref, cells, faces):
    rows = f_ref.shape[1]
    planes = rows // CHUNKS

    def group(j, _):
        for g in range(SUB):
            f_ref[g, at_rows(j * SUB), :] = native_ref[pl.ds(j * SUB * SUB + g, SUB, stride=SUB), :]
        return 0

    lax.fori_loop(0, rows // SUB, group, 0, unroll=2)
    y = native_polynomial_sums(native_ref, planes)
    packed = pack_sums(finish_polynomials(y, geo_ref[FIRST], planes), 0)
    wall_sums(f_ref, planes, links_ref, geo_ref, face_ref, cells, faces, True)
    sums_out[...] = packed + pack_sums([over_sublanes(face_ref, k) for k in range(2 * FACES)], EMIT)


def spec(space):
    return pl.BlockSpec(memory_space=space)


def array(*shape):
    return jax.ShapeDtypeStruct(shape, F32)


def params(mib=4):
    return pltpu.CompilerParams(vmem_limit_bytes=mib * 1024 * 1024)


def traffic(rows, profiles):
    size = SUB * rows * LANES
    return pl.CostEstimate(flops=8 * profiles * size, bytes_accessed=4 * profiles * size, transcendentals=0)


def local_sums(links, geo, f):
    return pl.pallas_call(
        sums_kernel,
        in_specs=[spec(pltpu.SMEM), spec(pltpu.VMEM), spec(pltpu.VMEM)],
        out_specs=spec(pltpu.VMEM),
        out_shape=array(SUB, LANES),
        scratch_shapes=[
                pltpu.VMEM((10, SUB * SUB, LANES), F32),
            pltpu.VMEM((FACES, SUB * SUB, LANES), F32),
            *face_lists(),
        ],
        compiler_params=params(),
        cost_estimate=traffic(f.shape[1], 4),
        name="local_sums",
    )(links, geo, f)


def first_sums(links, geo, native):
    rows = native.shape[0] // SUB
    return pl.pallas_call(
        first_sums_kernel,
        in_specs=[spec(pltpu.SMEM), spec(pltpu.VMEM), spec(pltpu.VMEM)],
        out_specs=[spec(pltpu.VMEM)] * 2,
        out_shape=[array(SUB, rows, LANES), array(SUB, LANES)],
        scratch_shapes=[
                pltpu.VMEM((2 * FACES, SUB * SUB, LANES), F32),
            *face_lists(),
        ],
        compiler_params=params(),
        cost_estimate=traffic(rows, 5),
        name="first_sums",
    )(links, geo, native)


SPLIT_PARTS = 8


def is_odd():
    return lax.rem(lax.axis_index("space"), 2) == 1


def first_rows_kernel(native_hbm, native_ref, far_any, near_any, far_ref, near_ref, sems, far_sems, near_sems):
    rows = native_ref.shape[0]
    part = rows // SPLIT_PARTS
    copies = [
        pltpu.make_async_copy(
            native_hbm.at[pl.ds(i * part, part)], native_ref.at[pl.ds(i * part, part)], sems.at[i]
        )
        for i in range(SPLIT_PARTS)
    ]
    for c in copies:
        c.start()
    odd = is_odd()
    far = jnp.where(odd, SUB - REACH, 0)
    near = jnp.where(odd, 0, SUB - REACH)
    groups = part // (SUB * SUB)
    out = []

    for i, c in enumerate(copies):
        c.wait()

        def group(j, _):
            for r in range(REACH):
                at = at_rows(j * SUB)
                far_ref[r, at, :] = native_ref[pl.ds(j * SUB * SUB + far + r, SUB, stride=SUB), :]
                near_ref[r, at, :] = native_ref[pl.ds(j * SUB * SUB + near + r, SUB, stride=SUB), :]
            return 0

        lax.fori_loop(i * groups, (i + 1) * groups, group, 0, unroll=unroll(groups, 8))
        at = pl.ds(i * groups * SUB, groups * SUB)
        out.append(pltpu.make_async_copy(far_ref.at[:, at], far_any.at[:, at], far_sems.at[i]))
        out.append(pltpu.make_async_copy(near_ref.at[:, at], near_any.at[:, at], near_sems.at[i]))
        out[-2].start()
        out[-1].start()
    for c in out:
        c.wait()


def first_rows(native):
    rows = native.shape[0] // SUB
    halo = (REACH, rows, LANES)
    return pl.pallas_call(
        first_rows_kernel,
        in_specs=[spec(pltpu.HBM)],
        out_specs=[spec(pltpu.VMEM), spec(pl.ANY), spec(pl.ANY)],
        out_shape=[array(*native.shape), array(*halo), array(*halo)],
        scratch_shapes=[pltpu.VMEM(halo, F32)] * 2 + [pltpu.SemaphoreType.DMA((SPLIT_PARTS,))] * 3,
        compiler_params=params(),
        cost_estimate=traffic(rows, 4),
        name="first_rows",
    )(pltpu.with_memory_space_constraint(native, pltpu.HBM))


def pair_weights(links_ref, geo_ref, pairs_ref, cells, faces):
    rows = pairs_ref.shape[1]
    planes = rows // CHUNKS
    first = splat(geo_ref, FIRST, 0)

    def clear(j, _):
        for p in range(pairs_ref.shape[0]):
            pairs_ref[p, at_rows(j * SUB), :] = jnp.zeros((SUB, LANES), F32)
        return 0

    lax.fori_loop(0, rows // SUB, clear, 0, unroll=4)

    def remote(i, _):
        g, k = cells[i], faces[i]
        j = links_ref[k, g]
        edge = g - (SUB - REACH)
        before = g * REACH - g * (g - 1) // 2 + (j + REACH) - g
        after = len(BEFORE_PAIRS) + edge * (edge + 1) // 2 + j - SUB
        at_pair = jnp.where(j < 0, before, after)
        scale = -TIME_STEP / splat(geo_ref, VOL, g)
        v0, v1, v2 = [scale * x for x in face_coefficients(geo_ref, k, g)]
        base = []
        for t in range(TILES):
            xb, xc = tile_nodes(t)
            base.append(v1 * xb + v2 * xc)

        def plane(a, _):
            sa = v0 * (first + a.astype(F32) * H)
            for t in range(TILES):
                at = at_rows((a * TILES + t) * SUB)
                pairs_ref[at_pair, at, :] = pairs_ref[at_pair, at, :] + jnp.maximum(sa + base[t], 0.0)
            return 0

        lax.fori_loop(0, planes, plane, 0, unroll=unroll(planes, 8))
        return 0

    lax.fori_loop(0, list_faces(links_ref, is_remote, cells, faces), remote, 0)


def gather_sums(tile):
    size = lax.axis_size("vel")
    if size not in (2, 4):
        return [lax.psum(tile, "vel")]
    others = [lax.ppermute(tile, "vel", [(i, i ^ s) for i in range(size)]) for s in range(1, size)]
    return [tile, *reversed(others)]


def doubling_sums(tile):
    size = lax.axis_size("vel")
    if size != 4:
        return gather_sums(tile)
    pair = tile + lax.ppermute(tile, "vel", [(i, i ^ 1) for i in range(size)])
    return [pair, lax.ppermute(pair, "vel", [(i, i ^ 2) for i in range(size)])]


def add_tiles(refs):
    tiles = [r[...] for r in refs]
    tiles = tiles[:1] + tiles[:0:-1]
    while len(tiles) > 1:
        tiles = [tiles[i] + tiles[i + 1] for i in range(0, len(tiles), 2)]
    return tiles[0]


def quantities(tile):
    m = [WEIGHT * column(tile, p) for p in range(13)]
    n = m[0]
    rn = 1.0 / n
    u = [m[1 + i] * rn for i in range(3)]
    uu = u[0] * u[0] + u[1] * u[1] + u[2] * u[2]
    trace = m[4] + m[5] + m[6]
    width = trace - n * uu
    temperature = width * rn * (1.0 / 3.0)
    second = [[m[4], m[7], m[8]], [m[7], m[5], m[9]], [m[8], m[9], m[6]]]
    q = []
    for i in range(3):
        across = u[0] * second[i][0] + u[1] * second[i][1] + u[2] * second[i][2]
        q.append(0.5 * (m[10 + i] - 2.0 * across - u[i] * trace + 2.0 * uu * m[1 + i]))
    return n, u, temperature, q


def macro_kernel(*refs):
    out_ref = refs[-1]
    n, u, temperature, q = quantities(add_tiles(refs[:-1]))
    lane, sub = lane_iota(), sub_iota()
    for i, x in enumerate((n, *u, temperature, *q)):
        row = jnp.sum(jnp.where(lane == sub, x, 0.0), axis=0, keepdims=True)
        out_ref[pl.ds(i, 1), :] = row[:, :SUB]


def macro(tiles):
    return pl.pallas_call(
        macro_kernel,
        in_specs=[spec(pltpu.VMEM)] * len(tiles),
        out_specs=spec(pltpu.VMEM),
        out_shape=array(8, SUB),
        compiler_params=params(1),
        name="macro",
    )(*tiles)


def flux_kernel(with_pairs, links_ref, geo_ref, f_ref, out_ref, *refs):
    if with_pairs:
        pairs_ref, cells, faces = refs[0], refs[-2], refs[-1]
        pair_weights(links_ref, geo_ref, pairs_ref, cells, faces)
        refs = refs[1:-2]
    coef, bases, stays, source, face = refs
    planes = f_ref.shape[1] // CHUNKS
    scale = -TIME_STEP / geo_ref[VOL]
    for i in range(3):
        whole = None
        for k in range(FACES):
            x = scale * geo_ref[FV + FACES * i + k]
            coef[FACES * i + k] = x
            whole = x if whole is None else whole + x
        coef[3 * FACES + i] = whole

    def table(g, _):
        w = [[splat(coef, FACES * i + k, g) for i in (1, 2)] for k in range(FACES)]
        whole = [splat(coef, 3 * FACES + i, g) for i in (1, 2)]
        for t in range(TILES):
            xb, xc = tile_nodes(t)
            for k in range(FACES):
                bases[k, g * TILES + t] = w[k][0] * xb + w[k][1] * xc
            stays[g * TILES + t] = 1.0 + whole[0] * xb + whole[1] * xc
        return 0

    lax.fori_loop(0, SUB, table, 0, unroll=2)

    def cell(g, _):
        count = 0
        for k in range(FACES):
            j = links_ref[k, g]
            source[count] = j
            face[count] = k
            count = count + jnp.logical_and(j >= 0, j < SUB).astype(jnp.int32)
        for n in range(FACES + 1):

            @pl.when(count == n)
            def _():
                own_faces(g, n)

        return 0

    def own_faces(g, n):
        at_source = [source[i] for i in range(n)]
        first_weight = [splat(coef, face[k], g) for k in range(n)]
        whole = splat(coef, 3 * FACES, g)
        x0 = splat(geo_ref, FIRST, g)
        base = [[bases[face[k], g * TILES + t] for k in range(n)] for t in range(TILES)]
        stay = [stays[g * TILES + t] for t in range(TILES)]

        def plane(a, _):
            xa = x0 + a.astype(F32) * H
            sa = [w * xa for w in first_weight]
            stay_a = whole * xa
            for t in range(TILES):
                at = at_rows((a * TILES + t) * SUB)
                f = f_ref[g, at, :]
                acc = f * (stay_a + stay[t])
                for k in range(n):
                    acc = acc + jnp.maximum(sa[k] + base[t][k], 0.0) * (f_ref[at_source[k], at, :] - f)
                out_ref[g, at, :] = acc
            return 0

        lax.fori_loop(0, planes, plane, 0, unroll=unroll(planes, 8))

    lax.fori_loop(0, SUB, cell, 0)


def flux(with_pairs, links, geo, f):
    rows = f.shape[1]
    pairs = 2 * len(BEFORE_PAIRS)
    return pl.pallas_call(
        functools.partial(flux_kernel, with_pairs),
        in_specs=[spec(pltpu.SMEM), spec(pltpu.VMEM), spec(pltpu.VMEM)],
        out_specs=[spec(pltpu.VMEM)] * (2 if with_pairs else 1),
        out_shape=[array(*f.shape)] + ([array(pairs, rows, LANES)] if with_pairs else []),
        scratch_shapes=[
            pltpu.VMEM((3 * FACES + 3, SUB, LANES), F32),
            pltpu.VMEM((FACES, SUB * TILES, SUB, LANES), F32),
            pltpu.VMEM((SUB * TILES, SUB, LANES), F32),
            pltpu.SMEM((FACES + 1,), jnp.int32),
            pltpu.SMEM((FACES + 1,), jnp.int32),
        ]
        + (face_lists() if with_pairs else []),
        compiler_params=params(),
        cost_estimate=traffic(rows, 9 if with_pairs else 7),
        name="flux",
    )(links, geo, f)


def target_kernel(count, links_ref, geo_ref, absorbed_in, *refs):
    sums_refs, (f_ref, part_ref, out_ref, *sum_out, ta, tiles_ref, coef, cells, faces) = refs[:count], refs[count:]
    planes = f_ref.shape[1] // CHUNKS
    sums = add_tiles(sums_refs)
    for ref in sum_out:
        ref[...] = sums
    absorbed = sums if absorbed_in is None else absorbed_in[...]
    n, u, temperature, q = quantities(sums)
    rt = 1.0 / temperature
    rate = TIME_STEP * n * temperature / (SHEAR * jnp.exp(POWER * jnp.log(temperature)))
    height = rate * n * rt * jnp.sqrt(rt)
    slope = (1.0 / 3.0) / (5.0 * n * temperature * temperature)
    coef[0] = rate
    coef[1] = rt
    coef[2], coef[3] = u[1], u[2]
    coef[4], coef[5] = slope * q[1], slope * q[2]
    for k in range(FACES):
        wall = geo_ref[WALL + k] > 0.5
        coef[6 + k] = column(sums, EMIT + k) / jnp.where(wall, column(absorbed, ABSORB + k), 1.0)
    first = geo_ref[FIRST]

    wt = geo_ref[WT]

    def plane_table(a, _):
        xa = first + a.astype(F32) * H
        ca = xa - u[0]
        za = ca * ca * rt
        ta[0, a] = height * jnp.exp(-0.5 * za)
        ta[1, a] = slope * q[0] * ca
        ta[2, a] = za - 5.0
        ta[3, a] = jnp.exp(-0.5 * xa * xa / wt)
        return 0

    lax.fori_loop(0, planes, plane_table, 0, unroll=unroll(planes, 8))

    def tile_table(g, _):
        rtg = splat(coef, 1, g)
        ub, uc = splat(coef, 2, g), splat(coef, 3, g)
        qb, qc = splat(coef, 4, g), splat(coef, 5, g)
        shape = wall_tiles(splat(geo_ref, WT, g))
        for t in range(TILES):
            xb, xc = tile_nodes(t)
            cb, cc = xb - ub, xc - uc
            z = (cb * cb + cc * cc) * rtg
            at = g * TILES + t
            tiles_ref[0, at] = jnp.exp(-0.5 * z)
            tiles_ref[1, at] = cb * qb + cc * qc
            tiles_ref[2, at] = z
            tiles_ref[3, at] = shape[t]
        return 0

    lax.fori_loop(0, SUB, tile_table, 0, unroll=4)

    def at_plane(i, a, g):
        return jnp.broadcast_to(ta[i, a, pl.ds(g, 1), :], (SUB, LANES))

    def cell(g, _):
        rate_g = splat(coef, 0, g)
        bell, heat, zz = [[tiles_ref[i, g * TILES + t] for t in range(TILES)] for i in range(3)]

        def plane(a, _):
            height_a, heat_a, z_a = [at_plane(i, a, g) for i in range(3)]
            for t in range(TILES):
                where = (g, at_rows((a * TILES + t) * SUB), slice(None))
                f = f_ref[where]
                target = (height_a * bell[t]) * (1.0 + (heat_a + heat[t]) * (z_a + zz[t]))
                out_ref[where] = (part_ref[where] - rate_g * f) + target
            return 0

        lax.fori_loop(0, planes, plane, 0, unroll=unroll(planes, 16))
        return 0

    lax.fori_loop(0, SUB, cell, 0)

    def wall(i, _):
        g, k = cells[i], faces[i]
        x0 = splat(geo_ref, FIRST, g)
        ratio = splat(coef, 6 + k, g)
        scale = -TIME_STEP / splat(geo_ref, VOL, g)
        v0, v1, v2 = [scale * x for x in face_coefficients(geo_ref, k, g)]
        base, shape = [], []
        for t in range(TILES):
            xb, xc = tile_nodes(t)
            base.append(v1 * xb + v2 * xc)
            shape.append(ratio * tiles_ref[3, g * TILES + t])

        def plane(a, _):
            wa = at_plane(3, a, g)
            sa = v0 * (x0 + a.astype(F32) * H)
            for t in range(TILES):
                where = (g, at_rows((a * TILES + t) * SUB), slice(None))
                f = f_ref[where]
                out_ref[where] = out_ref[where] + jnp.maximum(sa + base[t], 0.0) * (wa * shape[t] - f)
            return 0

        lax.fori_loop(0, planes, plane, 0, unroll=unroll(planes, 16))
        return 0

    lax.fori_loop(0, list_faces(links_ref, is_wall, cells, faces), wall, 0)


def add_target(links, geo, absorbed, tiles, f, part):
    rows = f.shape[1]
    vmem = spec(pltpu.VMEM)
    given = [links, geo] + ([] if absorbed is None else [absorbed]) + list(tiles) + [f, part]

    def kernel(links_ref, geo_in, *refs):
        if absorbed is None:
            target_kernel(len(tiles), links_ref, geo_in, None, *refs)
        else:
            target_kernel(len(tiles), links_ref, geo_in, *refs)

    return pl.pallas_call(
        kernel,
        in_specs=[spec(pltpu.SMEM)] + [vmem] * (len(given) - 1),
        out_specs=[vmem] * (2 if absorbed is None else 1),
        out_shape=[array(*part.shape)] + ([array(SUB, LANES)] if absorbed is None else []),
        input_output_aliases={len(given) - 1: 0},
        scratch_shapes=[
                pltpu.VMEM((4, rows // CHUNKS, SUB, LANES), F32),
            pltpu.VMEM((4, SUB * TILES, SUB, LANES), F32),
            pltpu.VMEM((6 + FACES, SUB, LANES), F32),
            *face_lists(),
        ],
        compiler_params=params(),
        cost_estimate=traffic(rows, 7),
        name="add_target",
    )(*given)


def side_terms(high, pairs_ref, halo_ref, f_ref, at):
    terms = [None] * REACH
    rows = [halo_ref[r, at, :] for r in range(REACH)]
    first = SUB - REACH if high else 0
    own = [f_ref[first + e, at, :] for e in range(REACH)]
    count = len(BEFORE_PAIRS)
    pairs = [(e, r) for e in range(REACH) for r in range(e + 1)] if high else BEFORE_PAIRS
    for p, (e, r) in enumerate(pairs):
        term = pairs_ref[p + count if high else p, at, :] * (rows[r] - own[e])
        terms[e] = term if terms[e] is None else terms[e] + term
    return first, terms


def for_side(far, run):
    odd = is_odd()

    @pl.when(odd)
    def _():
        run(far)

    @pl.when(jnp.logical_not(odd))
    def _():
        run(not far)


def add_side(far, pairs_ref, halo_ref, old_ref, part_ref, f_ref, rows_ref):
    def run(high):
        def group(j, _):
            at = at_rows(j * SUB)
            first, terms = side_terms(high, pairs_ref, halo_ref, old_ref, at)
            for e in range(REACH):
                x = part_ref[first + e, at, :] + terms[e]
                f_ref[first + e, at, :] = x
                if rows_ref is not None:
                    rows_ref[e, at, :] = x
            return 0

        groups = part_ref.shape[1] // SUB
        lax.fori_loop(0, groups, group, 0, unroll=unroll(groups, 8))

    for_side(far, run)


def edge(far, pairs, halo, old, part):
    rows = part.shape[1]
    return pl.pallas_call(
        functools.partial(add_side, far),
        in_specs=[spec(pltpu.VMEM)] * 4,
        out_specs=[spec(pltpu.VMEM)] * 2,
        out_shape=[array(SUB, rows, LANES), array(REACH, rows, LANES)],
        input_output_aliases={3: 0},
        compiler_params=params(),
        cost_estimate=traffic(rows, 2),
        name="far_edge" if far else "near_edge",
    )(pairs, halo, old, part)


def last_near_kernel(geo_ref, pairs_ref, halo_ref, old_ref, part_ref, f_ref, sums_out, parts_ref):
    add_side(False, pairs_ref, halo_ref, old_ref, part_ref, f_ref, None)
    planes = f_ref.shape[1] // CHUNKS
    y = polynomial_sums(f_ref, planes, parts_ref)
    sums_out[...] = pack_sums(finish_polynomials(y, geo_ref[FIRST], planes), 0)


def last_near(geo, pairs, near, old, part):
    rows = part.shape[1]
    return pl.pallas_call(
        last_near_kernel,
        in_specs=[spec(pltpu.VMEM)] * 5,
        out_specs=[spec(pltpu.VMEM)] * 2,
        out_shape=[array(SUB, rows, LANES), array(SUB, LANES)],
        input_output_aliases={4: 0},
        scratch_shapes=[pltpu.VMEM((10, SUB * SUB, LANES), F32)],
        compiler_params=params(),
        cost_estimate=traffic(rows, 3),
        name="last_near",
    )(geo, pairs, near, old, part)


def last_far_kernel(count, geo_ref, pairs_ref, *refs):
    halos, (old_ref, sums_in, terms_ref, sums_out, parts_ref) = refs[:count], refs[count:]
    rows = old_ref.shape[1]
    planes = rows // CHUNKS
    parts_ref[...] = jnp.zeros_like(parts_ref)

    def run(high):
        def add(halo_ref):
            def group(j, _):
                at = at_rows(j * SUB)
                _first, terms = side_terms(high, pairs_ref, halo_ref, old_ref, at)
                for e in range(REACH):
                    terms_ref[e, at, :] = terms[e]
                return 0

            lax.fori_loop(0, rows // SUB, group, 0, unroll=unroll(rows // SUB, 8))

        if count == 1 or not high:
            add(halos[-1])
        else:
            late = lax.axis_index("space") == LATE_FLOW[1]

            @pl.when(late)
            def _():
                add(halos[0])

            @pl.when(jnp.logical_not(late))
            def _():
                add(halos[-1])

        y = polynomial_sums(terms_ref, planes, parts_ref, SUB - REACH if high else 0)
        sums_out[...] = sums_in[...] + pack_sums(finish_polynomials(y, geo_ref[FIRST], planes), 0)

    for_side(True, run)


def last_far(geo, pairs, halos, old, sums):
    rows = old.shape[1]
    return pl.pallas_call(
        functools.partial(last_far_kernel, len(halos)),
        in_specs=[spec(pltpu.VMEM)] * (4 + len(halos)),
        out_specs=[spec(pltpu.VMEM)] * 2,
        out_shape=[array(REACH, rows, LANES), array(SUB, LANES)],
        scratch_shapes=[pltpu.VMEM((10, SUB * SUB, LANES), F32)],
        compiler_params=params(),
        cost_estimate=traffic(rows, 2),
        name="last_far",
    )(geo, pairs, *halos, old, sums)


LAST_PARTS = 4


def result_kernel(part_ref, terms_ref, out_hbm, native_ref, sems):
    part = part_ref.shape[1] // SUB // LAST_PARTS

    def copy(i):
        at = pl.ds(i * part * SUB * SUB, part * SUB * SUB)
        return pltpu.make_async_copy(native_ref.at[at], out_hbm.at[at], sems.at[i])

    def run(high):
        first = SUB - REACH if high else 0
        for i in range(LAST_PARTS):

            def group(j, _):
                at = at_rows(j * SUB)
                for g in range(SUB):
                    x = part_ref[g, at, :]
                    if 0 <= g - first < REACH:
                        x = x + terms_ref[g - first, at, :]
                    native_ref[pl.ds(j * SUB * SUB + g, SUB, stride=SUB), :] = x
                return 0

            lax.fori_loop(i * part, (i + 1) * part, group, 0, unroll=unroll(part, 4))
            copy(i).start()

    for_side(True, run)
    for i in range(LAST_PARTS):
        copy(i).wait()


def result(part, terms):
    rows = part.shape[1]
    native = (SUB * rows, LANES)
    return pl.pallas_call(
        result_kernel,
        in_specs=[spec(pltpu.VMEM)] * 2,
        out_specs=spec(pltpu.HBM),
        out_shape=array(*native),
        scratch_shapes=[pltpu.VMEM(native, F32), pltpu.SemaphoreType.DMA((LAST_PARTS,))],
        compiler_params=params(),
        cost_estimate=traffic(rows, 3),
        name="result",
    )(part, terms)


LATE_SLABS = 8
LATE_FLOW = (2, 1)


def swap(rows, start, without=()):
    pairs = [(i, i + 1) for i in range(start, lax.axis_size("space") - 1, 2)]
    pairs = pairs + [(j, i) for i, j in pairs]
    return lax.ppermute(rows, "space", [p for p in pairs if p not in without])


def late_flow(rows):
    return lax.ppermute(rows, "space", [LATE_FLOW])


def per_device(particle_profile, neighbors, face_vectors, volumes, wall_temp):
    cells, points = particle_profile.shape
    rows = points // LANES
    plane_count = NV // lax.axis_size("vel")
    native = particle_profile.reshape(cells, rows, LANES).transpose(1, 0, 2).reshape(cells * rows, LANES)
    wall = neighbors < 0
    links = jnp.where(wall, WALL_LINK, neighbors - lax.axis_index("space") * cells)
    own = (links >= 0) & (links < cells)
    first = -SPEED_LIMIT + ((lax.axis_index("vel") * plane_count).astype(F32) + 0.5) * H
    geo = jnp.concatenate(
        [
            face_vectors.reshape(3 * FACES, cells),
            volumes[None],
            wall_temp[None],
            wall.astype(F32),
            own.astype(F32),
            jnp.full((1, cells), first, F32),
        ]
    )
    geo = jnp.broadcast_to(geo[:, :, None], (GEO, cells, LANES))
    native, far, near = first_rows(native)
    far, near = swap(far, 1), swap(near, 0)
    f, sums = first_sums(links, geo, native)
    tiles = gather_sums(sums)
    part, pairs = flux(True, links, geo, f)
    part, absorbed = add_target(links, geo, None, tiles, f, part)
    part, near = edge(False, pairs, near, f, part)
    near = swap(near, 0)
    f, far = edge(True, pairs, far, f, part)
    sums = local_sums(links, geo, f)
    if lax.axis_size("space") == LATE_SLABS:
        halos = [late_flow(far), swap(far, 1, (LATE_FLOW,))]
        sums, near = lax.optimization_barrier((sums, near))
    else:
        halos = [swap(far, 1)]
    tiles = gather_sums(sums)
    (part,) = flux(False, links, geo, f)
    (part,) = add_target(links, geo, absorbed, tiles, f, part)
    part, sums = last_near(geo, pairs, near, f, part)
    terms, sums = last_far(geo, pairs, halos, f, sums)
    tiles = doubling_sums(sums)
    native = result(part, terms)
    macro_quantities = macro(tiles)
    evolved = native.reshape(rows, cells, LANES).transpose(1, 0, 2).reshape(cells, points)
    return evolved, macro_quantities


def solution(mesh):
    return jax.shard_map(
        per_device,
        mesh=mesh,
        in_specs=(
            P("space", "vel"),
            P(None, "space"),
            P(None, None, "space"),
            P("space"),
            P("space"),
        ),
        out_specs=(P("space", "vel"), P(None, "space")),
        check_vma=False,
    )
```

```python
import functools
import math

import jax
import jax.numpy as jnp
from jax import lax
from jax.experimental import pallas as pl
from jax.experimental.pallas import tpu as pltpu
from jax.sharding import PartitionSpec as P

NV = 64
FACES = 6
REACH = 3
STEPS = 2
LANES = 128
SUB = 8

TIME_STEP = 0.015
SHEAR = 0.1
POWER = 0.81
SPEED_LIMIT = 6.0
H = 2.0 * SPEED_LIMIT / NV
WEIGHT = H**3 * (2.0 * math.pi) ** (-1.5)

CHUNKS = NV * NV // LANES
TILES = CHUNKS // SUB

FV, VOL, WT, WALL, LOCAL, FIRST = 0, 18, 19, 20, 26, 32
GEO = 33
WALL_LINK = -64
BEFORE_PAIRS = tuple((g, r) for g in range(REACH) for r in range(g, REACH))
EMIT, ABSORB = 13, 19
SUMS = 25

F32 = jnp.float32


def lane_iota():
    return lax.broadcasted_iota(jnp.int32, (SUB, LANES), 1)


def sub_iota():
    return lax.broadcasted_iota(jnp.int32, (SUB, LANES), 0)


def half_of(lane):
    return (lane >= NV).astype(F32)


def third_component(lane):
    c = jnp.where(lane >= NV, lane - NV, lane).astype(F32)
    return -SPEED_LIMIT + (c + 0.5) * H


def tile_nodes(t):
    lane = lane_iota()
    b = (2 * SUB * t + 2 * sub_iota()).astype(F32) + half_of(lane)
    return -SPEED_LIMIT + (b + 0.5) * H, third_component(lane)


def column(tile, p):
    return jnp.broadcast_to(tile[:, p : p + 1], (SUB, LANES))


def splat(ref, i, g):
    return jnp.broadcast_to(ref[i, pl.ds(g, 1), :], (SUB, LANES))


def total(tile):
    return jnp.broadcast_to(jnp.sum(tile, axis=1, keepdims=True), (SUB, LANES))


def face_coefficients(geo_ref, k, g):
    return [splat(geo_ref, FV + FACES * i + k, g) for i in range(3)]


def at_rows(start, size=SUB):
    return pl.ds(pl.multiple_of(start, SUB), size)


def wall_tiles(wall_temp):
    rt = 1.0 / wall_temp
    scale = rt * jnp.sqrt(rt)
    out = []
    for t in range(TILES):
        xb, xc = tile_nodes(t)
        out.append(scale * jnp.exp(-0.5 * (xb * xb + xc * xc) * rt))
    return out


def pack_sums(arrays, start):
    lane = lane_iota()
    out = jnp.zeros((SUB, LANES), F32)
    for p, x in enumerate(arrays):
        out = jnp.where(lane == start + p, total(x), out)
    return out


def over_sublanes(ref, k):
    out = ref[k, pl.ds(0, SUB, stride=SUB), :]
    for s in range(1, SUB):
        out = out + ref[k, pl.ds(s, SUB, stride=SUB), :]
    return out


def list_faces(links_ref, wanted, cell_ref, face_ref):
    count = 0
    for g in range(SUB):
        for k in range(FACES):
            cell_ref[count] = g
            face_ref[count] = k
            count = count + wanted(links_ref[k, g]).astype(jnp.int32)
    return count


def is_wall(j):
    return j == WALL_LINK


def is_remote(j):
    return jnp.logical_or(j >= SUB, jnp.logical_and(j < 0, j != WALL_LINK))


def face_lists():
    return [pltpu.SMEM((FACES * SUB + 1,), jnp.int32)] * 2


def unroll(planes, most):
    return math.gcd(planes, most)


def finish_polynomials(y, first, planes):
    y0, y1, y2, y3, by0, by1, by2, bby0, bby1, bbby0 = y
    m = first + 0.5 * (planes - 1) * H
    c = third_component(lane_iota())
    cc = c * c
    a = y1 + m * y0
    aa = y2 + m * (2.0 * y1 + m * y0)
    aaa = y3 + m * (3.0 * y2 + m * (3.0 * y1 + m * y0))
    ab = by1 + m * by0
    aab = by2 + m * (2.0 * by1 + m * by0)
    abb = bby1 + m * bby0
    return (
        y0,
        a,
        by0,
        c * y0,
        aa,
        bby0,
        cc * y0,
        ab,
        c * a,
        c * by0,
        aaa + abb + cc * a,
        aab + bbby0 + cc * by0,
        c * (aa + bby0 + cc * y0),
    )


def polynomial_sums(f_ref, planes, parts_ref, first=0):
    half = planes // 2

    def cell(g, _):
        out = [None] * 10
        for t in range(TILES):
            y0 = y1 = y2 = y3 = None
            for i in range(half):
                d = (i + 0.5) * H
                hi = f_ref[g, pl.ds(((half + i) * TILES + t) * SUB, SUB), :]
                lo = f_ref[g, pl.ds(((half - 1 - i) * TILES + t) * SUB, SUB), :]
                s, r = hi + lo, hi - lo
                if i == 0:
                    y0, y1, y2, y3 = s, d * r, (d * d) * s, (d * d * d) * r
                else:
                    y0, y1, y2, y3 = y0 + s, y1 + d * r, y2 + (d * d) * s, y3 + (d * d * d) * r
            b, _c = tile_nodes(t)
            bb = b * b
            terms = (y0, y1, y2, y3, b * y0, b * y1, b * y2, bb * y0, bb * y1, bb * (b * y0))
            out = [x if o is None else o + x for o, x in zip(out, terms)]
        for p in range(10):
            parts_ref[p, at_rows((first + g) * SUB), :] = out[p]
        return 0

    lax.fori_loop(0, f_ref.shape[0], cell, 0)
    return [over_sublanes(parts_ref, p) for p in range(10)]


def native_polynomial_sums(native_ref, planes):
    half, side = planes // 2, CHUNKS // 2
    zero = jnp.zeros((SUB, LANES), F32)
    acc = [zero] * 10

    def plane(a, acc):
        xa = (a.astype(F32) - 0.5 * (planes - 1)) * H
        b0 = b1 = b2 = b3 = None
        for i in range(side):
            y = (2 * i + 1) * H
            hi = native_ref[at_rows((a * CHUNKS + side + i) * SUB), :]
            lo = native_ref[at_rows((a * CHUNKS + side - 1 - i) * SUB), :]
            s, d = hi + lo, hi - lo
            terms = (s, y * d, (y * y) * s, (y * y * y) * d)
            if i == 0:
                b0, b1, b2, b3 = terms
            else:
                b0, b1, b2, b3 = b0 + terms[0], b1 + terms[1], b2 + terms[2], b3 + terms[3]
        a0, a1, a2 = xa * b0, xa * b1, xa * b2
        aa0 = xa * a0
        new = (b0, a0, aa0, xa * aa0, b1, a1, xa * a1, b2, a2, b3)
        return tuple(x + z for x, z in zip(acc, new))

    g0, a0, aa0, aaa0, g1, a1, aa1, g2, a2, g3 = lax.fori_loop(0, planes, plane, tuple(acc))
    e = (half_of(lane_iota()) - 0.5) * H
    return [
        g0,
        a0,
        aa0,
        aaa0,
        g1 + e * g0,
        a1 + e * a0,
        aa1 + e * aa0,
        g2 + e * (2.0 * g1 + e * g0),
        a2 + e * (2.0 * a1 + e * a0),
        g3 + e * (3.0 * g2 + e * (3.0 * g1 + e * g0)),
    ]


def wall_sums(f_ref, planes, links_ref, geo_ref, sums_ref, cells, faces, with_absorbed):
    sums_ref[...] = jnp.zeros_like(sums_ref)

    def wall(i, _):
        g, k = cells[i], faces[i]
        v0, v1, v2 = face_coefficients(geo_ref, k, g)
        first = splat(geo_ref, FIRST, g)
        base = []
        for t in range(TILES):
            xb, xc = tile_nodes(t)
            base.append(v1 * xb + v2 * xc)
        if with_absorbed:
            wt = splat(geo_ref, WT, g)
            shape = wall_tiles(wt)

        def plane(a, acc):
            out, back = list(acc[0]), list(acc[1])
            xa = first + a.astype(F32) * H
            sa = v0 * xa
            if with_absorbed:
                wa = jnp.exp(-0.5 * xa * xa / wt)
            for t in range(TILES):
                s = sa + base[t]
                f = f_ref[g, at_rows((a * TILES + t) * SUB), :]
                out[t] = out[t] + jnp.maximum(s, 0.0) * f
                if with_absorbed:
                    back[t] = back[t] + jnp.maximum(-s, 0.0) * (wa * shape[t])
            return tuple(out), tuple(back)

        zeros = (jnp.zeros((SUB, LANES), F32),) * TILES
        out, back = lax.fori_loop(0, planes, plane, (zeros, zeros), unroll=unroll(planes, 16))
        at = at_rows(g * SUB)
        sums_ref[k, at, :] = (out[0] + out[1]) + (out[2] + out[3])
        if with_absorbed:
            sums_ref[FACES + k, at, :] = (back[0] + back[1]) + (back[2] + back[3])
        return 0

    lax.fori_loop(0, list_faces(links_ref, is_wall, cells, faces), wall, 0)


def sums_kernel(links_ref, geo_ref, f_ref, sums_out, parts_ref, face_ref, cells, faces):
    planes = f_ref.shape[1] // CHUNKS
    y = polynomial_sums(f_ref, planes, parts_ref)
    packed = pack_sums(finish_polynomials(y, geo_ref[FIRST], planes), 0)
    wall_sums(f_ref, planes, links_ref, geo_ref, face_ref, cells, faces, False)
    sums_out[...] = packed + pack_sums([over_sublanes(face_ref, k) for k in range(FACES)], EMIT)


def first_sums_kernel(links_ref, geo_ref, native_ref, f_ref, sums_out, face_ref, cells, faces):
    rows = f_ref.shape[1]
    planes = rows // CHUNKS

    def group(j, _):
        for g in range(SUB):
            f_ref[g, at_rows(j * SUB), :] = native_ref[pl.ds(j * SUB * SUB + g, SUB, stride=SUB), :]
        return 0

    lax.fori_loop(0, rows // SUB, group, 0, unroll=2)
    y = native_polynomial_sums(native_ref, planes)
    packed = pack_sums(finish_polynomials(y, geo_ref[FIRST], planes), 0)
    wall_sums(f_ref, planes, links_ref, geo_ref, face_ref, cells, faces, True)
    sums_out[...] = packed + pack_sums([over_sublanes(face_ref, k) for k in range(2 * FACES)], EMIT)


def spec(space):
    return pl.BlockSpec(memory_space=space)


def array(*shape):
    return jax.ShapeDtypeStruct(shape, F32)


def params(mib=4):
    return pltpu.CompilerParams(vmem_limit_bytes=mib * 1024 * 1024)


def traffic(rows, profiles):
    size = SUB * rows * LANES
    return pl.CostEstimate(flops=8 * profiles * size, bytes_accessed=4 * profiles * size, transcendentals=0)


def local_sums(links, geo, f):
    return pl.pallas_call(
        sums_kernel,
        in_specs=[spec(pltpu.SMEM), spec(pltpu.VMEM), spec(pltpu.VMEM)],
        out_specs=spec(pltpu.VMEM),
        out_shape=array(SUB, LANES),
        scratch_shapes=[
                pltpu.VMEM((10, SUB * SUB, LANES), F32),
            pltpu.VMEM((FACES, SUB * SUB, LANES), F32),
            *face_lists(),
        ],
        compiler_params=params(),
        cost_estimate=traffic(f.shape[1], 4),
        name="local_sums",
    )(links, geo, f)


def first_sums(links, geo, native):
    rows = native.shape[0] // SUB
    return pl.pallas_call(
        first_sums_kernel,
        in_specs=[spec(pltpu.SMEM), spec(pltpu.VMEM), spec(pltpu.VMEM)],
        out_specs=[spec(pltpu.VMEM)] * 2,
        out_shape=[array(SUB, rows, LANES), array(SUB, LANES)],
        scratch_shapes=[
                pltpu.VMEM((2 * FACES, SUB * SUB, LANES), F32),
            *face_lists(),
        ],
        compiler_params=params(),
        cost_estimate=traffic(rows, 5),
        name="first_sums",
    )(links, geo, native)


SPLIT_PARTS = 8


def is_odd():
    return lax.rem(lax.axis_index("space"), 2) == 1


def first_rows_kernel(native_hbm, native_ref, far_any, near_any, far_ref, near_ref, sems, far_sems, near_sems):
    rows = native_ref.shape[0]
    part = rows // SPLIT_PARTS
    copies = [
        pltpu.make_async_copy(
            native_hbm.at[pl.ds(i * part, part)], native_ref.at[pl.ds(i * part, part)], sems.at[i]
        )
        for i in range(SPLIT_PARTS)
    ]
    for c in copies:
        c.start()
    odd = is_odd()
    far = jnp.where(odd, SUB - REACH, 0)
    near = jnp.where(odd, 0, SUB - REACH)
    groups = part // (SUB * SUB)
    out = []

    for i, c in enumerate(copies):
        c.wait()

        def group(j, _):
            for r in range(REACH):
                at = at_rows(j * SUB)
                far_ref[r, at, :] = native_ref[pl.ds(j * SUB * SUB + far + r, SUB, stride=SUB), :]
                near_ref[r, at, :] = native_ref[pl.ds(j * SUB * SUB + near + r, SUB, stride=SUB), :]
            return 0

        lax.fori_loop(i * groups, (i + 1) * groups, group, 0, unroll=unroll(groups, 8))
        at = pl.ds(i * groups * SUB, groups * SUB)
        out.append(pltpu.make_async_copy(far_ref.at[:, at], far_any.at[:, at], far_sems.at[i]))
        out.append(pltpu.make_async_copy(near_ref.at[:, at], near_any.at[:, at], near_sems.at[i]))
        out[-2].start()
        out[-1].start()
    for c in out:
        c.wait()


def first_rows(native):
    rows = native.shape[0] // SUB
    halo = (REACH, rows, LANES)
    return pl.pallas_call(
        first_rows_kernel,
        in_specs=[spec(pltpu.HBM)],
        out_specs=[spec(pltpu.VMEM), spec(pl.ANY), spec(pl.ANY)],
        out_shape=[array(*native.shape), array(*halo), array(*halo)],
        scratch_shapes=[pltpu.VMEM(halo, F32)] * 2 + [pltpu.SemaphoreType.DMA((SPLIT_PARTS,))] * 3,
        compiler_params=params(),
        cost_estimate=traffic(rows, 4),
        name="first_rows",
    )(pltpu.with_memory_space_constraint(native, pltpu.HBM))


def pair_weights(links_ref, geo_ref, pairs_ref, cells, faces):
    rows = pairs_ref.shape[1]
    planes = rows // CHUNKS
    first = splat(geo_ref, FIRST, 0)

    def clear(j, _):
        for p in range(pairs_ref.shape[0]):
            pairs_ref[p, at_rows(j * SUB), :] = jnp.zeros((SUB, LANES), F32)
        return 0

    lax.fori_loop(0, rows // SUB, clear, 0, unroll=4)

    def remote(i, _):
        g, k = cells[i], faces[i]
        j = links_ref[k, g]
        edge = g - (SUB - REACH)
        before = g * REACH - g * (g - 1) // 2 + (j + REACH) - g
        after = len(BEFORE_PAIRS) + edge * (edge + 1) // 2 + j - SUB
        at_pair = jnp.where(j < 0, before, after)
        scale = -TIME_STEP / splat(geo_ref, VOL, g)
        v0, v1, v2 = [scale * x for x in face_coefficients(geo_ref, k, g)]
        base = []
        for t in range(TILES):
            xb, xc = tile_nodes(t)
            base.append(v1 * xb + v2 * xc)

        def plane(a, _):
            sa = v0 * (first + a.astype(F32) * H)
            for t in range(TILES):
                at = at_rows((a * TILES + t) * SUB)
                pairs_ref[at_pair, at, :] = pairs_ref[at_pair, at, :] + jnp.maximum(sa + base[t], 0.0)
            return 0

        lax.fori_loop(0, planes, plane, 0, unroll=unroll(planes, 8))
        return 0

    lax.fori_loop(0, list_faces(links_ref, is_remote, cells, faces), remote, 0)


def gather_sums(tile):
    size = lax.axis_size("vel")
    if size not in (2, 4):
        return [lax.psum(tile, "vel")]
    others = [lax.ppermute(tile, "vel", [(i, i ^ s) for i in range(size)]) for s in range(1, size)]
    return [tile, *others]


def doubling_sums(tile):
    size = lax.axis_size("vel")
    if size != 4:
        return gather_sums(tile)
    pair = tile + lax.ppermute(tile, "vel", [(i, i ^ 1) for i in range(size)])
    return [pair, lax.ppermute(pair, "vel", [(i, i ^ 2) for i in range(size)])]


def add_tiles(refs):
    tiles = [r[...] for r in refs]
    while len(tiles) > 1:
        tiles = [tiles[i] + tiles[i + 1] for i in range(0, len(tiles), 2)]
    return tiles[0]


def quantities(tile):
    m = [WEIGHT * column(tile, p) for p in range(13)]
    n = m[0]
    rn = 1.0 / n
    u = [m[1 + i] * rn for i in range(3)]
    uu = u[0] * u[0] + u[1] * u[1] + u[2] * u[2]
    trace = m[4] + m[5] + m[6]
    width = trace - n * uu
    temperature = width * rn * (1.0 / 3.0)
    second = [[m[4], m[7], m[8]], [m[7], m[5], m[9]], [m[8], m[9], m[6]]]
    q = []
    for i in range(3):
        across = u[0] * second[i][0] + u[1] * second[i][1] + u[2] * second[i][2]
        q.append(0.5 * (m[10 + i] - 2.0 * across - u[i] * trace + 2.0 * uu * m[1 + i]))
    return n, u, temperature, q


def macro_kernel(*refs):
    out_ref = refs[-1]
    n, u, temperature, q = quantities(add_tiles(refs[:-1]))
    lane, sub = lane_iota(), sub_iota()
    for i, x in enumerate((n, *u, temperature, *q)):
        row = jnp.sum(jnp.where(lane == sub, x, 0.0), axis=0, keepdims=True)
        out_ref[pl.ds(i, 1), :] = row[:, :SUB]


def macro(tiles):
    return pl.pallas_call(
        macro_kernel,
        in_specs=[spec(pltpu.VMEM)] * len(tiles),
        out_specs=spec(pltpu.VMEM),
        out_shape=array(8, SUB),
        compiler_params=params(1),
        name="macro",
    )(*tiles)


def flux_kernel(with_pairs, links_ref, geo_ref, f_ref, out_ref, *refs):
    if with_pairs:
        pairs_ref, cells, faces = refs[0], refs[-2], refs[-1]
        pair_weights(links_ref, geo_ref, pairs_ref, cells, faces)
        refs = refs[1:-2]
    coef, bases, stays, source, face = refs
    planes = f_ref.shape[1] // CHUNKS
    scale = -TIME_STEP / geo_ref[VOL]
    for i in range(3):
        whole = None
        for k in range(FACES):
            x = scale * geo_ref[FV + FACES * i + k]
            coef[FACES * i + k] = x
            whole = x if whole is None else whole + x
        coef[3 * FACES + i] = whole

    def table(g, _):
        w = [[splat(coef, FACES * i + k, g) for i in (1, 2)] for k in range(FACES)]
        whole = [splat(coef, 3 * FACES + i, g) for i in (1, 2)]
        for t in range(TILES):
            xb, xc = tile_nodes(t)
            for k in range(FACES):
                bases[k, g * TILES + t] = w[k][0] * xb + w[k][1] * xc
            stays[g * TILES + t] = 1.0 + whole[0] * xb + whole[1] * xc
        return 0

    lax.fori_loop(0, SUB, table, 0, unroll=2)

    def cell(g, _):
        count = 0
        for k in range(FACES):
            j = links_ref[k, g]
            source[count] = j
            face[count] = k
            count = count + jnp.logical_and(j >= 0, j < SUB).astype(jnp.int32)
        for n in range(FACES + 1):

            @pl.when(count == n)
            def _():
                own_faces(g, n)

        return 0

    def own_faces(g, n):
        at_source = [source[i] for i in range(n)]
        first_weight = [splat(coef, face[k], g) for k in range(n)]
        whole = splat(coef, 3 * FACES, g)
        x0 = splat(geo_ref, FIRST, g)
        base = [[bases[face[k], g * TILES + t] for k in range(n)] for t in range(TILES)]
        stay = [stays[g * TILES + t] for t in range(TILES)]

        def plane(a, _):
            xa = x0 + a.astype(F32) * H
            sa = [w * xa for w in first_weight]
            stay_a = whole * xa
            for t in range(TILES):
                at = at_rows((a * TILES + t) * SUB)
                f = f_ref[g, at, :]
                acc = f * (stay_a + stay[t])
                for k in range(n):
                    acc = acc + jnp.maximum(sa[k] + base[t][k], 0.0) * (f_ref[at_source[k], at, :] - f)
                out_ref[g, at, :] = acc
            return 0

        lax.fori_loop(0, planes, plane, 0, unroll=unroll(planes, 8))

    lax.fori_loop(0, SUB, cell, 0)


def flux(with_pairs, links, geo, f):
    rows = f.shape[1]
    pairs = 2 * len(BEFORE_PAIRS)
    return pl.pallas_call(
        functools.partial(flux_kernel, with_pairs),
        in_specs=[spec(pltpu.SMEM), spec(pltpu.VMEM), spec(pltpu.VMEM)],
        out_specs=[spec(pltpu.VMEM)] * (2 if with_pairs else 1),
        out_shape=[array(*f.shape)] + ([array(pairs, rows, LANES)] if with_pairs else []),
        scratch_shapes=[
            pltpu.VMEM((3 * FACES + 3, SUB, LANES), F32),
            pltpu.VMEM((FACES, SUB * TILES, SUB, LANES), F32),
            pltpu.VMEM((SUB * TILES, SUB, LANES), F32),
            pltpu.SMEM((FACES + 1,), jnp.int32),
            pltpu.SMEM((FACES + 1,), jnp.int32),
        ]
        + (face_lists() if with_pairs else []),
        compiler_params=params(),
        cost_estimate=traffic(rows, 9 if with_pairs else 7),
        name="flux",
    )(links, geo, f)


def target_kernel(count, links_ref, geo_ref, absorbed_in, *refs):
    sums_refs, (f_ref, part_ref, out_ref, *sum_out, tiles_ref, coef, cells, faces) = refs[:count], refs[count:]
    planes = f_ref.shape[1] // CHUNKS
    sums = add_tiles(sums_refs)
    for ref in sum_out:
        ref[...] = sums
    absorbed = sums if absorbed_in is None else absorbed_in[...]
    n, u, temperature, q = quantities(sums)
    rt = 1.0 / temperature
    rate = TIME_STEP * n * temperature / (SHEAR * jnp.exp(POWER * jnp.log(temperature)))
    height = rate * n * rt * jnp.sqrt(rt)
    slope = (1.0 / 3.0) / (5.0 * n * temperature * temperature)
    coef[0] = rate
    coef[1] = rt
    coef[2], coef[3] = u[1], u[2]
    coef[4], coef[5] = slope * q[1], slope * q[2]
    coef[6], coef[7], coef[8] = u[0], slope * q[0], height
    for k in range(FACES):
        wall = geo_ref[WALL + k] > 0.5
        coef[9 + k] = column(sums, EMIT + k) / jnp.where(wall, column(absorbed, ABSORB + k), 1.0)

    def tile_table(g, _):
        rtg = splat(coef, 1, g)
        ub, uc = splat(coef, 2, g), splat(coef, 3, g)
        qb, qc = splat(coef, 4, g), splat(coef, 5, g)
        shape = wall_tiles(splat(geo_ref, WT, g))
        for t in range(TILES):
            xb, xc = tile_nodes(t)
            cb, cc = xb - ub, xc - uc
            z = (cb * cb + cc * cc) * rtg
            at = g * TILES + t
            tiles_ref[0, at] = jnp.exp(-0.5 * z)
            tiles_ref[1, at] = cb * qb + cc * qc
            tiles_ref[2, at] = z
            tiles_ref[3, at] = shape[t]
        return 0

    lax.fori_loop(0, SUB, tile_table, 0, unroll=4)

    def cell(g, _):
        rate_g, rtg, u0, q0, height_g = [splat(coef, i, g) for i in (0, 1, 6, 7, 8)]
        x0 = splat(geo_ref, FIRST, g) - u0
        bell, heat, zz = [[tiles_ref[i, g * TILES + t] for t in range(TILES)] for i in range(3)]

        def plane(a, _):
            ca = x0 + a.astype(F32) * H
            za = ca * ca * rtg
            height_a = height_g * jnp.exp(-0.5 * za)
            heat_a = q0 * ca
            z_a = za - 5.0
            for t in range(TILES):
                where = (g, at_rows((a * TILES + t) * SUB), slice(None))
                f = f_ref[where]
                target = (height_a * bell[t]) * (1.0 + (heat_a + heat[t]) * (z_a + zz[t]))
                out_ref[where] = (part_ref[where] - rate_g * f) + target
            return 0

        lax.fori_loop(0, planes, plane, 0, unroll=unroll(planes, 16))
        return 0

    lax.fori_loop(0, SUB, cell, 0)

    def wall(i, _):
        g, k = cells[i], faces[i]
        x0 = splat(geo_ref, FIRST, g)
        ratio = splat(coef, 9 + k, g)
        scale = -TIME_STEP / splat(geo_ref, VOL, g)
        v0, v1, v2 = [scale * x for x in face_coefficients(geo_ref, k, g)]
        base, shape = [], []
        for t in range(TILES):
            xb, xc = tile_nodes(t)
            base.append(v1 * xb + v2 * xc)
            shape.append(ratio * tiles_ref[3, g * TILES + t])

        rt_wall = -0.5 / splat(geo_ref, WT, g)

        def plane(a, _):
            xa = x0 + a.astype(F32) * H
            wa = jnp.exp(xa * xa * rt_wall)
            sa = v0 * xa
            for t in range(TILES):
                where = (g, at_rows((a * TILES + t) * SUB), slice(None))
                f = f_ref[where]
                out_ref[where] = out_ref[where] + jnp.maximum(sa + base[t], 0.0) * (wa * shape[t] - f)
            return 0

        lax.fori_loop(0, planes, plane, 0, unroll=unroll(planes, 16))
        return 0

    lax.fori_loop(0, list_faces(links_ref, is_wall, cells, faces), wall, 0)


def add_target(links, geo, absorbed, tiles, f, part):
    rows = f.shape[1]
    vmem = spec(pltpu.VMEM)
    given = [links, geo] + ([] if absorbed is None else [absorbed]) + list(tiles) + [f, part]

    def kernel(links_ref, geo_in, *refs):
        if absorbed is None:
            target_kernel(len(tiles), links_ref, geo_in, None, *refs)
        else:
            target_kernel(len(tiles), links_ref, geo_in, *refs)

    return pl.pallas_call(
        kernel,
        in_specs=[spec(pltpu.SMEM)] + [vmem] * (len(given) - 1),
        out_specs=[vmem] * (2 if absorbed is None else 1),
        out_shape=[array(*part.shape)] + ([array(SUB, LANES)] if absorbed is None else []),
        input_output_aliases={len(given) - 1: 0},
        scratch_shapes=[
                pltpu.VMEM((4, SUB * TILES, SUB, LANES), F32),
            pltpu.VMEM((9 + FACES, SUB, LANES), F32),
            *face_lists(),
        ],
        compiler_params=params(),
        cost_estimate=traffic(rows, 7),
        name="add_target",
    )(*given)


def side_terms(high, pairs_ref, halo_ref, f_ref, at):
    terms = [None] * REACH
    rows = [halo_ref[r, at, :] for r in range(REACH)]
    first = SUB - REACH if high else 0
    own = [f_ref[first + e, at, :] for e in range(REACH)]
    count = len(BEFORE_PAIRS)
    pairs = [(e, r) for e in range(REACH) for r in range(e + 1)] if high else BEFORE_PAIRS
    for p, (e, r) in enumerate(pairs):
        term = pairs_ref[p + count if high else p, at, :] * (rows[r] - own[e])
        terms[e] = term if terms[e] is None else terms[e] + term
    return first, terms


def for_side(far, run):
    odd = is_odd()

    @pl.when(odd)
    def _():
        run(far)

    @pl.when(jnp.logical_not(odd))
    def _():
        run(not far)


def add_side(far, pairs_ref, halo_ref, old_ref, part_ref, f_ref, rows_ref, ready=None):
    def run(high):
        def group(j, _):
            at = at_rows(j * SUB)
            first, terms = side_terms(high, pairs_ref, halo_ref, old_ref, at)
            for e in range(REACH):
                x = part_ref[first + e, at, :] + terms[e]
                f_ref[first + e, at, :] = x
                if rows_ref is not None:
                    rows_ref[e, at, :] = x
            return 0

        groups = part_ref.shape[1] // SUB
        parts = 1 if ready is None else EDGE_PARTS
        for i in range(parts):
            if ready is not None:
                ready(i)
            count = groups // parts
            lax.fori_loop(i * count, (i + 1) * count, group, 0, unroll=unroll(count, 8))

    for_side(far, run)


EDGE_PARTS = 4


def near_edge_kernel(pairs_ref, halo_any, old_ref, part_ref, f_ref, rows_ref, halo_ref, sems):
    size = halo_ref.shape[1] // EDGE_PARTS

    def copy(i):
        at = pl.ds(i * size, size)
        return pltpu.make_async_copy(halo_any.at[:, at], halo_ref.at[:, at], sems.at[i])

    for i in range(EDGE_PARTS):
        copy(i).start()
    add_side(False, pairs_ref, halo_ref, old_ref, part_ref, f_ref, rows_ref, lambda i: copy(i).wait())


def edge(far, pairs, halo, old, part):
    rows = part.shape[1]
    return pl.pallas_call(
        functools.partial(add_side, True) if far else near_edge_kernel,
        in_specs=[spec(pltpu.VMEM), spec(pltpu.VMEM if far else pl.ANY), spec(pltpu.VMEM), spec(pltpu.VMEM)],
        out_specs=[spec(pltpu.VMEM)] * 2,
        out_shape=[array(SUB, rows, LANES), array(REACH, rows, LANES)],
        input_output_aliases={3: 0},
        scratch_shapes=[] if far else [pltpu.VMEM(halo.shape, F32), pltpu.SemaphoreType.DMA((EDGE_PARTS,))],
        compiler_params=params(),
        cost_estimate=traffic(rows, 2),
        name="far_edge" if far else "near_edge",
    )(pairs, halo, old, part)


def last_near_kernel(geo_ref, pairs_ref, halo_ref, old_ref, part_ref, f_ref, sums_out, parts_ref):
    add_side(False, pairs_ref, halo_ref, old_ref, part_ref, f_ref, None)
    planes = f_ref.shape[1] // CHUNKS
    y = polynomial_sums(f_ref, planes, parts_ref)
    sums_out[...] = pack_sums(finish_polynomials(y, geo_ref[FIRST], planes), 0)


def last_near(geo, pairs, near, old, part):
    rows = part.shape[1]
    return pl.pallas_call(
        last_near_kernel,
        in_specs=[spec(pltpu.VMEM)] * 5,
        out_specs=[spec(pltpu.VMEM)] * 2,
        out_shape=[array(SUB, rows, LANES), array(SUB, LANES)],
        input_output_aliases={4: 0},
        scratch_shapes=[pltpu.VMEM((10, SUB * SUB, LANES), F32)],
        compiler_params=params(),
        cost_estimate=traffic(rows, 3),
        name="last_near",
    )(geo, pairs, near, old, part)


def last_far_kernel(geo_ref, pairs_ref, halo_ref, old_ref, sums_in, terms_ref, sums_out, parts_ref):
    rows = old_ref.shape[1]
    planes = rows // CHUNKS
    parts_ref[...] = jnp.zeros_like(parts_ref)

    def run(high):
        def group(j, _):
            at = at_rows(j * SUB)
            _first, terms = side_terms(high, pairs_ref, halo_ref, old_ref, at)
            for e in range(REACH):
                terms_ref[e, at, :] = terms[e]
            return 0

        lax.fori_loop(0, rows // SUB, group, 0, unroll=unroll(rows // SUB, 8))
        y = polynomial_sums(terms_ref, planes, parts_ref, SUB - REACH if high else 0)
        sums_out[...] = sums_in[...] + pack_sums(finish_polynomials(y, geo_ref[FIRST], planes), 0)

    for_side(True, run)


def last_far(geo, pairs, far, old, sums):
    rows = old.shape[1]
    return pl.pallas_call(
        last_far_kernel,
        in_specs=[spec(pltpu.VMEM)] * 5,
        out_specs=[spec(pltpu.VMEM)] * 2,
        out_shape=[array(REACH, rows, LANES), array(SUB, LANES)],
        scratch_shapes=[pltpu.VMEM((10, SUB * SUB, LANES), F32)],
        compiler_params=params(),
        cost_estimate=traffic(rows, 2),
        name="last_far",
    )(geo, pairs, far, old, sums)


LAST_PARTS = 4


def result_kernel(part_ref, terms_ref, out_hbm, native_ref, sems):
    part = part_ref.shape[1] // SUB // LAST_PARTS

    def copy(i):
        at = pl.ds(i * part * SUB * SUB, part * SUB * SUB)
        return pltpu.make_async_copy(native_ref.at[at], out_hbm.at[at], sems.at[i])

    def run(high):
        first = SUB - REACH if high else 0
        for i in range(LAST_PARTS):

            def group(j, _):
                at = at_rows(j * SUB)
                for g in range(SUB):
                    x = part_ref[g, at, :]
                    if 0 <= g - first < REACH:
                        x = x + terms_ref[g - first, at, :]
                    native_ref[pl.ds(j * SUB * SUB + g, SUB, stride=SUB), :] = x
                return 0

            lax.fori_loop(i * part, (i + 1) * part, group, 0, unroll=unroll(part, 4))
            copy(i).start()

    for_side(True, run)
    for i in range(LAST_PARTS):
        copy(i).wait()


def result(part, terms):
    rows = part.shape[1]
    native = (SUB * rows, LANES)
    return pl.pallas_call(
        result_kernel,
        in_specs=[spec(pltpu.VMEM)] * 2,
        out_specs=spec(pltpu.HBM),
        out_shape=array(*native),
        scratch_shapes=[pltpu.VMEM(native, F32), pltpu.SemaphoreType.DMA((LAST_PARTS,))],
        compiler_params=params(),
        cost_estimate=traffic(rows, 3),
        name="result",
    )(part, terms)


def swap(rows, start):
    pairs = [(i, i + 1) for i in range(start, lax.axis_size("space") - 1, 2)]
    return lax.ppermute(rows, "space", pairs + [(j, i) for i, j in pairs])


def per_device(particle_profile, neighbors, face_vectors, volumes, wall_temp):
    cells, points = particle_profile.shape
    rows = points // LANES
    plane_count = NV // lax.axis_size("vel")
    native = particle_profile.reshape(cells, rows, LANES).transpose(1, 0, 2).reshape(cells * rows, LANES)
    wall = neighbors < 0
    links = jnp.where(wall, WALL_LINK, neighbors - lax.axis_index("space") * cells)
    own = (links >= 0) & (links < cells)
    first = -SPEED_LIMIT + ((lax.axis_index("vel") * plane_count).astype(F32) + 0.5) * H
    geo = jnp.concatenate(
        [
            face_vectors.reshape(3 * FACES, cells),
            volumes[None],
            wall_temp[None],
            wall.astype(F32),
            own.astype(F32),
            jnp.full((1, cells), first, F32),
        ]
    )
    geo = jnp.broadcast_to(geo[:, :, None], (GEO, cells, LANES))
    native, far, near = first_rows(native)
    far, near = swap(far, 1), swap(near, 0)
    f, sums = first_sums(links, geo, native)
    tiles = gather_sums(sums)
    part, pairs = flux(True, links, geo, f)
    part, absorbed = add_target(links, geo, None, tiles, f, part)
    part, near = edge(False, pairs, near, f, part)
    near = swap(near, 0)
    f, far = edge(True, pairs, far, f, part)
    far = swap(far, 1)
    tiles = gather_sums(local_sums(links, geo, f))
    (part,) = flux(False, links, geo, f)
    (part,) = add_target(links, geo, absorbed, tiles, f, part)
    part, sums = last_near(geo, pairs, near, f, part)
    terms, sums = last_far(geo, pairs, far, f, sums)
    tiles = doubling_sums(sums)
    native = result(part, terms)
    macro_quantities = macro(tiles)
    evolved = native.reshape(rows, cells, LANES).transpose(1, 0, 2).reshape(cells, points)
    return evolved, macro_quantities


def solution(mesh):
    return jax.shard_map(
        per_device,
        mesh=mesh,
        in_specs=(
            P("space", "vel"),
            P(None, "space"),
            P(None, None, "space"),
            P("space"),
            P("space"),
        ),
        out_specs=(P("space", "vel"), P(None, "space")),
        check_vma=False,
    )
```

```python
import functools
import math

import jax
import jax.numpy as jnp
from jax import lax
from jax.experimental import pallas as pl
from jax.experimental.pallas import tpu as pltpu
from jax.sharding import PartitionSpec as P

NV = 64
FACES = 6
REACH = 3
STEPS = 2
LANES = 128
SUB = 8

TIME_STEP = 0.015
SHEAR = 0.1
POWER = 0.81
SPEED_LIMIT = 6.0
H = 2.0 * SPEED_LIMIT / NV
WEIGHT = H**3 * (2.0 * math.pi) ** (-1.5)

CHUNKS = NV * NV // LANES
TILES = CHUNKS // SUB

FV, VOL, WT, WALL, LOCAL, FIRST = 0, 18, 19, 20, 26, 32
GEO = 33
WALL_LINK = -64
BEFORE_PAIRS = tuple((g, r) for g in range(REACH) for r in range(g, REACH))
EMIT, ABSORB = 13, 19
SUMS = 25

F32 = jnp.float32


def lane_iota():
    return lax.broadcasted_iota(jnp.int32, (SUB, LANES), 1)


def sub_iota():
    return lax.broadcasted_iota(jnp.int32, (SUB, LANES), 0)


def half_of(lane):
    return (lane >= NV).astype(F32)


def third_component(lane):
    c = jnp.where(lane >= NV, lane - NV, lane).astype(F32)
    return -SPEED_LIMIT + (c + 0.5) * H


def tile_nodes(t):
    lane = lane_iota()
    b = (2 * SUB * t + 2 * sub_iota()).astype(F32) + half_of(lane)
    return -SPEED_LIMIT + (b + 0.5) * H, third_component(lane)


def column(tile, p):
    return jnp.broadcast_to(tile[:, p : p + 1], (SUB, LANES))


def splat(ref, i, g):
    return jnp.broadcast_to(ref[i, pl.ds(g, 1), :], (SUB, LANES))


def total(tile):
    return jnp.broadcast_to(jnp.sum(tile, axis=1, keepdims=True), (SUB, LANES))


def face_coefficients(geo_ref, k, g):
    return [splat(geo_ref, FV + FACES * i + k, g) for i in range(3)]


def at_rows(start, size=SUB):
    return pl.ds(pl.multiple_of(start, SUB), size)


def wall_tiles(wall_temp):
    rt = 1.0 / wall_temp
    scale = rt * jnp.sqrt(rt)
    out = []
    for t in range(TILES):
        xb, xc = tile_nodes(t)
        out.append(scale * jnp.exp(-0.5 * (xb * xb + xc * xc) * rt))
    return out


def pack_sums(arrays, start):
    lane = lane_iota()
    out = jnp.zeros((SUB, LANES), F32)
    for p, x in enumerate(arrays):
        out = jnp.where(lane == start + p, total(x), out)
    return out


def over_sublanes(ref, k):
    out = ref[k, pl.ds(0, SUB, stride=SUB), :]
    for s in range(1, SUB):
        out = out + ref[k, pl.ds(s, SUB, stride=SUB), :]
    return out


def list_faces(links_ref, wanted, cell_ref, face_ref):
    count = 0
    for g in range(SUB):
        for k in range(FACES):
            cell_ref[count] = g
            face_ref[count] = k
            count = count + wanted(links_ref[k, g]).astype(jnp.int32)
    return count


def is_wall(j):
    return j == WALL_LINK


def is_remote(j):
    return jnp.logical_or(j >= SUB, jnp.logical_and(j < 0, j != WALL_LINK))


def face_lists():
    return [pltpu.SMEM((FACES * SUB + 1,), jnp.int32)] * 2


def unroll(planes, most):
    return math.gcd(planes, most)


def finish_polynomials(y, first, planes):
    y0, y1, y2, y3, by0, by1, by2, bby0, bby1, bbby0 = y
    m = first + 0.5 * (planes - 1) * H
    c = third_component(lane_iota())
    cc = c * c
    a = y1 + m * y0
    aa = y2 + m * (2.0 * y1 + m * y0)
    aaa = y3 + m * (3.0 * y2 + m * (3.0 * y1 + m * y0))
    ab = by1 + m * by0
    aab = by2 + m * (2.0 * by1 + m * by0)
    abb = bby1 + m * bby0
    return (
        y0,
        a,
        by0,
        c * y0,
        aa,
        bby0,
        cc * y0,
        ab,
        c * a,
        c * by0,
        aaa + abb + cc * a,
        aab + bbby0 + cc * by0,
        c * (aa + bby0 + cc * y0),
    )


def polynomial_sums(f_ref, planes, parts_ref, first=0):
    half = planes // 2

    def cell(g, _):
        out = [None] * 10
        for t in range(TILES):
            y0 = y1 = y2 = y3 = None
            for i in range(half):
                d = (i + 0.5) * H
                hi = f_ref[g, pl.ds(((half + i) * TILES + t) * SUB, SUB), :]
                lo = f_ref[g, pl.ds(((half - 1 - i) * TILES + t) * SUB, SUB), :]
                s, r = hi + lo, hi - lo
                if i == 0:
                    y0, y1, y2, y3 = s, d * r, (d * d) * s, (d * d * d) * r
                else:
                    y0, y1, y2, y3 = y0 + s, y1 + d * r, y2 + (d * d) * s, y3 + (d * d * d) * r
            b, _c = tile_nodes(t)
            bb = b * b
            terms = (y0, y1, y2, y3, b * y0, b * y1, b * y2, bb * y0, bb * y1, bb * (b * y0))
            out = [x if o is None else o + x for o, x in zip(out, terms)]
        for p in range(10):
            parts_ref[p, at_rows((first + g) * SUB), :] = out[p]
        return 0

    lax.fori_loop(0, f_ref.shape[0], cell, 0)
    return [over_sublanes(parts_ref, p) for p in range(10)]


def native_polynomial_sums(native_ref, planes):
    half, side = planes // 2, CHUNKS // 2
    zero = jnp.zeros((SUB, LANES), F32)
    acc = [zero] * 10

    def plane(a, acc):
        xa = (a.astype(F32) - 0.5 * (planes - 1)) * H
        b0 = b1 = b2 = b3 = None
        for i in range(side):
            y = (2 * i + 1) * H
            hi = native_ref[at_rows((a * CHUNKS + side + i) * SUB), :]
            lo = native_ref[at_rows((a * CHUNKS + side - 1 - i) * SUB), :]
            s, d = hi + lo, hi - lo
            terms = (s, y * d, (y * y) * s, (y * y * y) * d)
            if i == 0:
                b0, b1, b2, b3 = terms
            else:
                b0, b1, b2, b3 = b0 + terms[0], b1 + terms[1], b2 + terms[2], b3 + terms[3]
        a0, a1, a2 = xa * b0, xa * b1, xa * b2
        aa0 = xa * a0
        new = (b0, a0, aa0, xa * aa0, b1, a1, xa * a1, b2, a2, b3)
        return tuple(x + z for x, z in zip(acc, new))

    g0, a0, aa0, aaa0, g1, a1, aa1, g2, a2, g3 = lax.fori_loop(0, planes, plane, tuple(acc))
    e = (half_of(lane_iota()) - 0.5) * H
    return [
        g0,
        a0,
        aa0,
        aaa0,
        g1 + e * g0,
        a1 + e * a0,
        aa1 + e * aa0,
        g2 + e * (2.0 * g1 + e * g0),
        a2 + e * (2.0 * a1 + e * a0),
        g3 + e * (3.0 * g2 + e * (3.0 * g1 + e * g0)),
    ]


def wall_sums(f_ref, planes, links_ref, geo_ref, sums_ref, cells, faces, with_absorbed):
    sums_ref[...] = jnp.zeros_like(sums_ref)

    def wall(i, _):
        g, k = cells[i], faces[i]
        v0, v1, v2 = face_coefficients(geo_ref, k, g)
        first = splat(geo_ref, FIRST, g)
        base = []
        for t in range(TILES):
            xb, xc = tile_nodes(t)
            base.append(v1 * xb + v2 * xc)
        if with_absorbed:
            wt = splat(geo_ref, WT, g)
            shape = wall_tiles(wt)

        def plane(a, acc):
            out, back = list(acc[0]), list(acc[1])
            xa = first + a.astype(F32) * H
            sa = v0 * xa
            if with_absorbed:
                wa = jnp.exp(-0.5 * xa * xa / wt)
            for t in range(TILES):
                s = sa + base[t]
                f = f_ref[g, at_rows((a * TILES + t) * SUB), :]
                out[t] = out[t] + jnp.maximum(s, 0.0) * f
                if with_absorbed:
                    back[t] = back[t] + jnp.maximum(-s, 0.0) * (wa * shape[t])
            return tuple(out), tuple(back)

        zeros = (jnp.zeros((SUB, LANES), F32),) * TILES
        out, back = lax.fori_loop(0, planes, plane, (zeros, zeros), unroll=unroll(planes, 16))
        at = at_rows(g * SUB)
        sums_ref[k, at, :] = (out[0] + out[1]) + (out[2] + out[3])
        if with_absorbed:
            sums_ref[FACES + k, at, :] = (back[0] + back[1]) + (back[2] + back[3])
        return 0

    lax.fori_loop(0, list_faces(links_ref, is_wall, cells, faces), wall, 0)


def sums_kernel(links_ref, geo_ref, f_ref, sums_out, parts_ref, face_ref, cells, faces):
    planes = f_ref.shape[1] // CHUNKS
    y = polynomial_sums(f_ref, planes, parts_ref)
    packed = pack_sums(finish_polynomials(y, geo_ref[FIRST], planes), 0)
    wall_sums(f_ref, planes, links_ref, geo_ref, face_ref, cells, faces, False)
    sums_out[...] = packed + pack_sums([over_sublanes(face_ref, k) for k in range(FACES)], EMIT)


def first_sums_kernel(links_ref, geo_ref, native_ref, f_ref, sums_out, face_ref, cells, faces):
    rows = f_ref.shape[1]
    planes = rows // CHUNKS

    def group(j, _):
        for g in range(SUB):
            f_ref[g, at_rows(j * SUB), :] = native_ref[pl.ds(j * SUB * SUB + g, SUB, stride=SUB), :]
        return 0

    lax.fori_loop(0, rows // SUB, group, 0, unroll=2)
    y = native_polynomial_sums(native_ref, planes)
    packed = pack_sums(finish_polynomials(y, geo_ref[FIRST], planes), 0)
    wall_sums(f_ref, planes, links_ref, geo_ref, face_ref, cells, faces, True)
    sums_out[...] = packed + pack_sums([over_sublanes(face_ref, k) for k in range(2 * FACES)], EMIT)


def spec(space):
    return pl.BlockSpec(memory_space=space)


def array(*shape):
    return jax.ShapeDtypeStruct(shape, F32)


def params(mib=4):
    return pltpu.CompilerParams(vmem_limit_bytes=mib * 1024 * 1024)


def traffic(rows, profiles):
    size = SUB * rows * LANES
    return pl.CostEstimate(flops=8 * profiles * size, bytes_accessed=4 * profiles * size, transcendentals=0)


def local_sums(links, geo, f):
    return pl.pallas_call(
        sums_kernel,
        in_specs=[spec(pltpu.SMEM), spec(pltpu.VMEM), spec(pltpu.VMEM)],
        out_specs=spec(pltpu.VMEM),
        out_shape=array(SUB, LANES),
        scratch_shapes=[
                pltpu.VMEM((10, SUB * SUB, LANES), F32),
            pltpu.VMEM((FACES, SUB * SUB, LANES), F32),
            *face_lists(),
        ],
        compiler_params=params(),
        cost_estimate=traffic(f.shape[1], 4),
        name="local_sums",
    )(links, geo, f)


def first_sums(links, geo, native):
    rows = native.shape[0] // SUB
    return pl.pallas_call(
        first_sums_kernel,
        in_specs=[spec(pltpu.SMEM), spec(pltpu.VMEM), spec(pltpu.VMEM)],
        out_specs=[spec(pltpu.VMEM)] * 2,
        out_shape=[array(SUB, rows, LANES), array(SUB, LANES)],
        scratch_shapes=[
                pltpu.VMEM((2 * FACES, SUB * SUB, LANES), F32),
            *face_lists(),
        ],
        compiler_params=params(),
        cost_estimate=traffic(rows, 5),
        name="first_sums",
    )(links, geo, native)


SPLIT_PARTS = 8


def is_odd():
    return lax.rem(lax.axis_index("space"), 2) == 1


def first_rows_kernel(native_hbm, native_ref, far_any, near_any, far_ref, near_ref, sems, far_sems, near_sems):
    rows = native_ref.shape[0]
    part = rows // SPLIT_PARTS
    copies = [
        pltpu.make_async_copy(
            native_hbm.at[pl.ds(i * part, part)], native_ref.at[pl.ds(i * part, part)], sems.at[i]
        )
        for i in range(SPLIT_PARTS)
    ]
    for c in copies:
        c.start()
    odd = is_odd()
    far = jnp.where(odd, SUB - REACH, 0)
    near = jnp.where(odd, 0, SUB - REACH)
    groups = part // (SUB * SUB)
    out = []

    for i, c in enumerate(copies):
        c.wait()

        def group(j, _):
            for r in range(REACH):
                at = at_rows(j * SUB)
                far_ref[r, at, :] = native_ref[pl.ds(j * SUB * SUB + far + r, SUB, stride=SUB), :]
                near_ref[r, at, :] = native_ref[pl.ds(j * SUB * SUB + near + r, SUB, stride=SUB), :]
            return 0

        lax.fori_loop(i * groups, (i + 1) * groups, group, 0, unroll=unroll(groups, 8))
        at = pl.ds(i * groups * SUB, groups * SUB)
        out.append(pltpu.make_async_copy(far_ref.at[:, at], far_any.at[:, at], far_sems.at[i]))
        out.append(pltpu.make_async_copy(near_ref.at[:, at], near_any.at[:, at], near_sems.at[i]))
        out[-2].start()
        out[-1].start()
    for c in out:
        c.wait()


def first_rows(native):
    rows = native.shape[0] // SUB
    halo = (REACH, rows, LANES)
    return pl.pallas_call(
        first_rows_kernel,
        in_specs=[spec(pltpu.HBM)],
        out_specs=[spec(pltpu.VMEM), spec(pl.ANY), spec(pl.ANY)],
        out_shape=[array(*native.shape), array(*halo), array(*halo)],
        scratch_shapes=[pltpu.VMEM(halo, F32)] * 2 + [pltpu.SemaphoreType.DMA((SPLIT_PARTS,))] * 3,
        compiler_params=params(),
        cost_estimate=traffic(rows, 4),
        name="first_rows",
    )(pltpu.with_memory_space_constraint(native, pltpu.HBM))


def pair_weights(links_ref, geo_ref, pairs_ref, cells, faces):
    rows = pairs_ref.shape[1]
    planes = rows // CHUNKS
    first = splat(geo_ref, FIRST, 0)

    def clear(j, _):
        for p in range(pairs_ref.shape[0]):
            pairs_ref[p, at_rows(j * SUB), :] = jnp.zeros((SUB, LANES), F32)
        return 0

    lax.fori_loop(0, rows // SUB, clear, 0, unroll=4)

    def remote(i, _):
        g, k = cells[i], faces[i]
        j = links_ref[k, g]
        edge = g - (SUB - REACH)
        before = g * REACH - g * (g - 1) // 2 + (j + REACH) - g
        after = len(BEFORE_PAIRS) + edge * (edge + 1) // 2 + j - SUB
        at_pair = jnp.where(j < 0, before, after)
        scale = -TIME_STEP / splat(geo_ref, VOL, g)
        v0, v1, v2 = [scale * x for x in face_coefficients(geo_ref, k, g)]
        base = []
        for t in range(TILES):
            xb, xc = tile_nodes(t)
            base.append(v1 * xb + v2 * xc)

        def plane(a, _):
            sa = v0 * (first + a.astype(F32) * H)
            for t in range(TILES):
                at = at_rows((a * TILES + t) * SUB)
                pairs_ref[at_pair, at, :] = pairs_ref[at_pair, at, :] + jnp.maximum(sa + base[t], 0.0)
            return 0

        lax.fori_loop(0, planes, plane, 0, unroll=unroll(planes, 8))
        return 0

    lax.fori_loop(0, list_faces(links_ref, is_remote, cells, faces), remote, 0)


def gather_sums(tile):
    size = lax.axis_size("vel")
    if size not in (2, 4):
        return [lax.psum(tile, "vel")]
    others = [lax.ppermute(tile, "vel", [(i, i ^ s) for i in range(size)]) for s in range(1, size)]
    return [tile, *others]


def doubling_sums(tile):
    size = lax.axis_size("vel")
    if size != 4:
        return gather_sums(tile)
    pair = tile + lax.ppermute(tile, "vel", [(i, i ^ 1) for i in range(size)])
    return [pair, lax.ppermute(pair, "vel", [(i, i ^ 2) for i in range(size)])]


def add_tiles(refs):
    tiles = [r[...] for r in refs]
    while len(tiles) > 1:
        tiles = [tiles[i] + tiles[i + 1] for i in range(0, len(tiles), 2)]
    return tiles[0]


def quantities(tile):
    m = [WEIGHT * column(tile, p) for p in range(13)]
    n = m[0]
    rn = 1.0 / n
    u = [m[1 + i] * rn for i in range(3)]
    uu = u[0] * u[0] + u[1] * u[1] + u[2] * u[2]
    trace = m[4] + m[5] + m[6]
    width = trace - n * uu
    temperature = width * rn * (1.0 / 3.0)
    second = [[m[4], m[7], m[8]], [m[7], m[5], m[9]], [m[8], m[9], m[6]]]
    q = []
    for i in range(3):
        across = u[0] * second[i][0] + u[1] * second[i][1] + u[2] * second[i][2]
        q.append(0.5 * (m[10 + i] - 2.0 * across - u[i] * trace + 2.0 * uu * m[1 + i]))
    return n, u, temperature, q


def macro_kernel(*refs):
    out_ref = refs[-1]
    n, u, temperature, q = quantities(add_tiles(refs[:-1]))
    lane, sub = lane_iota(), sub_iota()
    for i, x in enumerate((n, *u, temperature, *q)):
        row = jnp.sum(jnp.where(lane == sub, x, 0.0), axis=0, keepdims=True)
        out_ref[pl.ds(i, 1), :] = row[:, :SUB]


def macro(tiles):
    return pl.pallas_call(
        macro_kernel,
        in_specs=[spec(pltpu.VMEM)] * len(tiles),
        out_specs=spec(pltpu.VMEM),
        out_shape=array(8, SUB),
        compiler_params=params(1),
        name="macro",
    )(*tiles)


def flux_kernel(with_pairs, links_ref, geo_ref, f_ref, out_ref, *refs):
    if with_pairs:
        pairs_ref, cells, faces = refs[0], refs[-2], refs[-1]
        pair_weights(links_ref, geo_ref, pairs_ref, cells, faces)
        refs = refs[1:-2]
    coef, bases, stays, source, face = refs
    planes = f_ref.shape[1] // CHUNKS
    scale = -TIME_STEP / geo_ref[VOL]
    for i in range(3):
        whole = None
        for k in range(FACES):
            x = scale * geo_ref[FV + FACES * i + k]
            coef[FACES * i + k] = x
            whole = x if whole is None else whole + x
        coef[3 * FACES + i] = whole

    def table(g, _):
        w = [[splat(coef, FACES * i + k, g) for i in (1, 2)] for k in range(FACES)]
        whole = [splat(coef, 3 * FACES + i, g) for i in (1, 2)]
        for t in range(TILES):
            xb, xc = tile_nodes(t)
            for k in range(FACES):
                bases[k, g * TILES + t] = w[k][0] * xb + w[k][1] * xc
            stays[g * TILES + t] = 1.0 + whole[0] * xb + whole[1] * xc
        return 0

    lax.fori_loop(0, SUB, table, 0, unroll=2)

    def cell(g, _):
        count = 0
        for k in range(FACES):
            j = links_ref[k, g]
            source[count] = j
            face[count] = k
            count = count + jnp.logical_and(j >= 0, j < SUB).astype(jnp.int32)
        for n in range(FACES + 1):

            @pl.when(count == n)
            def _():
                own_faces(g, n)

        return 0

    def own_faces(g, n):
        at_source = [source[i] for i in range(n)]
        first_weight = [splat(coef, face[k], g) for k in range(n)]
        whole = splat(coef, 3 * FACES, g)
        x0 = splat(geo_ref, FIRST, g)
        base = [[bases[face[k], g * TILES + t] for k in range(n)] for t in range(TILES)]
        stay = [stays[g * TILES + t] for t in range(TILES)]

        def plane(a, _):
            xa = x0 + a.astype(F32) * H
            sa = [w * xa for w in first_weight]
            stay_a = whole * xa
            for t in range(TILES):
                at = at_rows((a * TILES + t) * SUB)
                f = f_ref[g, at, :]
                acc = f * (stay_a + stay[t])
                for k in range(n):
                    acc = acc + jnp.maximum(sa[k] + base[t][k], 0.0) * (f_ref[at_source[k], at, :] - f)
                out_ref[g, at, :] = acc
            return 0

        lax.fori_loop(0, planes, plane, 0, unroll=unroll(planes, 8))

    lax.fori_loop(0, SUB, cell, 0)


def flux(with_pairs, links, geo, f):
    rows = f.shape[1]
    pairs = 2 * len(BEFORE_PAIRS)
    return pl.pallas_call(
        functools.partial(flux_kernel, with_pairs),
        in_specs=[spec(pltpu.SMEM), spec(pltpu.VMEM), spec(pltpu.VMEM)],
        out_specs=[spec(pltpu.VMEM)] * (2 if with_pairs else 1),
        out_shape=[array(*f.shape)] + ([array(pairs, rows, LANES)] if with_pairs else []),
        scratch_shapes=[
            pltpu.VMEM((3 * FACES + 3, SUB, LANES), F32),
            pltpu.VMEM((FACES, SUB * TILES, SUB, LANES), F32),
            pltpu.VMEM((SUB * TILES, SUB, LANES), F32),
            pltpu.SMEM((FACES + 1,), jnp.int32),
            pltpu.SMEM((FACES + 1,), jnp.int32),
        ]
        + (face_lists() if with_pairs else []),
        compiler_params=params(),
        cost_estimate=traffic(rows, 9 if with_pairs else 7),
        name="flux",
    )(links, geo, f)


def target_kernel(count, links_ref, geo_ref, absorbed_in, *refs):
    sums_refs, (f_ref, part_ref, out_ref, *sum_out, tiles_ref, coef, cells, faces) = refs[:count], refs[count:]
    planes = f_ref.shape[1] // CHUNKS
    sums = add_tiles(sums_refs)
    for ref in sum_out:
        ref[...] = sums
    absorbed = sums if absorbed_in is None else absorbed_in[...]
    n, u, temperature, q = quantities(sums)
    rt = 1.0 / temperature
    rate = TIME_STEP * n * temperature / (SHEAR * jnp.exp(POWER * jnp.log(temperature)))
    height = rate * n * rt * jnp.sqrt(rt)
    slope = (1.0 / 3.0) / (5.0 * n * temperature * temperature)
    coef[0] = rate
    coef[1] = rt
    coef[2], coef[3] = u[1], u[2]
    coef[4], coef[5] = slope * q[1], slope * q[2]
    coef[6], coef[7], coef[8] = u[0], slope * q[0], height
    for k in range(FACES):
        wall = geo_ref[WALL + k] > 0.5
        coef[9 + k] = column(sums, EMIT + k) / jnp.where(wall, column(absorbed, ABSORB + k), 1.0)

    def tile_table(g, _):
        rtg = splat(coef, 1, g)
        ub, uc = splat(coef, 2, g), splat(coef, 3, g)
        qb, qc = splat(coef, 4, g), splat(coef, 5, g)
        shape = wall_tiles(splat(geo_ref, WT, g))
        for t in range(TILES):
            xb, xc = tile_nodes(t)
            cb, cc = xb - ub, xc - uc
            z = (cb * cb + cc * cc) * rtg
            at = g * TILES + t
            tiles_ref[0, at] = jnp.exp(-0.5 * z)
            tiles_ref[1, at] = cb * qb + cc * qc
            tiles_ref[2, at] = z
            tiles_ref[3, at] = shape[t]
        return 0

    lax.fori_loop(0, SUB, tile_table, 0, unroll=4)

    def cell(g, _):
        rate_g, rtg, u0, q0, height_g = [splat(coef, i, g) for i in (0, 1, 6, 7, 8)]
        x0 = splat(geo_ref, FIRST, g) - u0
        bell, heat, zz = [[tiles_ref[i, g * TILES + t] for t in range(TILES)] for i in range(3)]

        def plane(a, _):
            ca = x0 + a.astype(F32) * H
            za = ca * ca * rtg
            height_a = height_g * jnp.exp(-0.5 * za)
            heat_a = q0 * ca
            z_a = za - 5.0
            for t in range(TILES):
                where = (g, at_rows((a * TILES + t) * SUB), slice(None))
                f = f_ref[where]
                target = (height_a * bell[t]) * (1.0 + (heat_a + heat[t]) * (z_a + zz[t]))
                out_ref[where] = (part_ref[where] - rate_g * f) + target
            return 0

        lax.fori_loop(0, planes, plane, 0, unroll=unroll(planes, 16))
        return 0

    lax.fori_loop(0, SUB, cell, 0)

    def wall(i, _):
        g, k = cells[i], faces[i]
        x0 = splat(geo_ref, FIRST, g)
        ratio = splat(coef, 9 + k, g)
        scale = -TIME_STEP / splat(geo_ref, VOL, g)
        v0, v1, v2 = [scale * x for x in face_coefficients(geo_ref, k, g)]
        base, shape = [], []
        for t in range(TILES):
            xb, xc = tile_nodes(t)
            base.append(v1 * xb + v2 * xc)
            shape.append(ratio * tiles_ref[3, g * TILES + t])

        rt_wall = -0.5 / splat(geo_ref, WT, g)

        def plane(a, _):
            xa = x0 + a.astype(F32) * H
            wa = jnp.exp(xa * xa * rt_wall)
            sa = v0 * xa
            for t in range(TILES):
                where = (g, at_rows((a * TILES + t) * SUB), slice(None))
                f = f_ref[where]
                out_ref[where] = out_ref[where] + jnp.maximum(sa + base[t], 0.0) * (wa * shape[t] - f)
            return 0

        lax.fori_loop(0, planes, plane, 0, unroll=unroll(planes, 16))
        return 0

    lax.fori_loop(0, list_faces(links_ref, is_wall, cells, faces), wall, 0)


def add_target(links, geo, absorbed, tiles, f, part):
    rows = f.shape[1]
    vmem = spec(pltpu.VMEM)
    given = [links, geo] + ([] if absorbed is None else [absorbed]) + list(tiles) + [f, part]

    def kernel(links_ref, geo_in, *refs):
        if absorbed is None:
            target_kernel(len(tiles), links_ref, geo_in, None, *refs)
        else:
            target_kernel(len(tiles), links_ref, geo_in, *refs)

    return pl.pallas_call(
        kernel,
        in_specs=[spec(pltpu.SMEM)] + [vmem] * (len(given) - 1),
        out_specs=[vmem] * (2 if absorbed is None else 1),
        out_shape=[array(*part.shape)] + ([array(SUB, LANES)] if absorbed is None else []),
        input_output_aliases={len(given) - 1: 0},
        scratch_shapes=[
                pltpu.VMEM((4, SUB * TILES, SUB, LANES), F32),
            pltpu.VMEM((9 + FACES, SUB, LANES), F32),
            *face_lists(),
        ],
        compiler_params=params(),
        cost_estimate=traffic(rows, 7),
        name="add_target",
    )(*given)


def side_terms(high, pairs_ref, halo_ref, f_ref, at):
    terms = [None] * REACH
    rows = [halo_ref[r, at, :] for r in range(REACH)]
    first = SUB - REACH if high else 0
    own = [f_ref[first + e, at, :] for e in range(REACH)]
    count = len(BEFORE_PAIRS)
    pairs = [(e, r) for e in range(REACH) for r in range(e + 1)] if high else BEFORE_PAIRS
    for p, (e, r) in enumerate(pairs):
        term = pairs_ref[p + count if high else p, at, :] * (rows[r] - own[e])
        terms[e] = term if terms[e] is None else terms[e] + term
    return first, terms


def for_side(far, run):
    odd = is_odd()

    @pl.when(odd)
    def _():
        run(far)

    @pl.when(jnp.logical_not(odd))
    def _():
        run(not far)


def add_side(far, pairs_ref, halo_ref, old_ref, part_ref, f_ref, rows_ref, ready=None):
    def run(high):
        def group(j, _):
            at = at_rows(j * SUB)
            first, terms = side_terms(high, pairs_ref, halo_ref, old_ref, at)
            for e in range(REACH):
                x = part_ref[first + e, at, :] + terms[e]
                f_ref[first + e, at, :] = x
                if rows_ref is not None:
                    rows_ref[e, at, :] = x
            return 0

        groups = part_ref.shape[1] // SUB
        parts = 1 if ready is None else EDGE_PARTS
        for i in range(parts):
            if ready is not None:
                ready(i)
            count = groups // parts
            lax.fori_loop(i * count, (i + 1) * count, group, 0, unroll=unroll(count, 8))

    for_side(far, run)


EDGE_PARTS = 4


def near_edge_kernel(pairs_ref, halo_any, old_ref, part_ref, f_ref, rows_ref, halo_ref, sems):
    size = halo_ref.shape[1] // EDGE_PARTS

    def copy(i):
        at = pl.ds(i * size, size)
        return pltpu.make_async_copy(halo_any.at[:, at], halo_ref.at[:, at], sems.at[i])

    for i in range(EDGE_PARTS):
        copy(i).start()
    add_side(False, pairs_ref, halo_ref, old_ref, part_ref, f_ref, rows_ref, lambda i: copy(i).wait())


def far_edge_kernel(count, pairs_ref, *refs):
    halos, rest = refs[:count], refs[count:]
    if count == 1:
        add_side(True, pairs_ref, halos[0], *rest)
        return
    me = lax.axis_index("space")
    late = me < 0
    for _, last in LATE_FLOWS:
        late = jnp.logical_or(late, me == last)
    for halo_ref, wanted in ((halos[0], late), (halos[1], jnp.logical_not(late))):

        @pl.when(wanted)
        def _():
            add_side(True, pairs_ref, halo_ref, *rest)


def edge(far, pairs, halos, old, part):
    rows = part.shape[1]
    return pl.pallas_call(
        functools.partial(far_edge_kernel, len(halos)) if far else near_edge_kernel,
        in_specs=[spec(pltpu.VMEM)]
        + [spec(pltpu.VMEM if far else pl.ANY)] * len(halos)
        + [spec(pltpu.VMEM), spec(pltpu.VMEM)],
        out_specs=[spec(pltpu.VMEM)] * 2,
        out_shape=[array(SUB, rows, LANES), array(REACH, rows, LANES)],
        input_output_aliases={len(halos) + 2: 0},
        scratch_shapes=[] if far else [pltpu.VMEM(halos[0].shape, F32), pltpu.SemaphoreType.DMA((EDGE_PARTS,))],
        compiler_params=params(),
        cost_estimate=traffic(rows, 2),
        name="far_edge" if far else "near_edge",
    )(pairs, *halos, old, part)


def last_near_kernel(geo_ref, pairs_ref, halo_ref, old_ref, part_ref, f_ref, sums_out, parts_ref):
    add_side(False, pairs_ref, halo_ref, old_ref, part_ref, f_ref, None)
    planes = f_ref.shape[1] // CHUNKS
    y = polynomial_sums(f_ref, planes, parts_ref)
    sums_out[...] = pack_sums(finish_polynomials(y, geo_ref[FIRST], planes), 0)


def last_near(geo, pairs, near, old, part):
    rows = part.shape[1]
    return pl.pallas_call(
        last_near_kernel,
        in_specs=[spec(pltpu.VMEM)] * 5,
        out_specs=[spec(pltpu.VMEM)] * 2,
        out_shape=[array(SUB, rows, LANES), array(SUB, LANES)],
        input_output_aliases={4: 0},
        scratch_shapes=[pltpu.VMEM((10, SUB * SUB, LANES), F32)],
        compiler_params=params(),
        cost_estimate=traffic(rows, 3),
        name="last_near",
    )(geo, pairs, near, old, part)


def last_far_kernel(geo_ref, pairs_ref, halo_ref, old_ref, sums_in, terms_ref, sums_out, parts_ref):
    rows = old_ref.shape[1]
    planes = rows // CHUNKS
    parts_ref[...] = jnp.zeros_like(parts_ref)

    def run(high):
        def group(j, _):
            at = at_rows(j * SUB)
            _first, terms = side_terms(high, pairs_ref, halo_ref, old_ref, at)
            for e in range(REACH):
                terms_ref[e, at, :] = terms[e]
            return 0

        lax.fori_loop(0, rows // SUB, group, 0, unroll=unroll(rows // SUB, 8))
        y = polynomial_sums(terms_ref, planes, parts_ref, SUB - REACH if high else 0)
        sums_out[...] = sums_in[...] + pack_sums(finish_polynomials(y, geo_ref[FIRST], planes), 0)

    for_side(True, run)


def last_far(geo, pairs, far, old, sums):
    rows = old.shape[1]
    return pl.pallas_call(
        last_far_kernel,
        in_specs=[spec(pltpu.VMEM)] * 5,
        out_specs=[spec(pltpu.VMEM)] * 2,
        out_shape=[array(REACH, rows, LANES), array(SUB, LANES)],
        scratch_shapes=[pltpu.VMEM((10, SUB * SUB, LANES), F32)],
        compiler_params=params(),
        cost_estimate=traffic(rows, 2),
        name="last_far",
    )(geo, pairs, far, old, sums)


LAST_PARTS = 4


def result_kernel(part_ref, terms_ref, out_hbm, native_ref, sems):
    part = part_ref.shape[1] // SUB // LAST_PARTS

    def copy(i):
        at = pl.ds(i * part * SUB * SUB, part * SUB * SUB)
        return pltpu.make_async_copy(native_ref.at[at], out_hbm.at[at], sems.at[i])

    def run(high):
        first = SUB - REACH if high else 0
        for i in range(LAST_PARTS):

            def group(j, _):
                at = at_rows(j * SUB)
                for g in range(SUB):
                    x = part_ref[g, at, :]
                    if 0 <= g - first < REACH:
                        x = x + terms_ref[g - first, at, :]
                    native_ref[pl.ds(j * SUB * SUB + g, SUB, stride=SUB), :] = x
                return 0

            lax.fori_loop(i * part, (i + 1) * part, group, 0, unroll=unroll(part, 4))
            copy(i).start()

    for_side(True, run)
    for i in range(LAST_PARTS):
        copy(i).wait()


def result(part, terms):
    rows = part.shape[1]
    native = (SUB * rows, LANES)
    return pl.pallas_call(
        result_kernel,
        in_specs=[spec(pltpu.VMEM)] * 2,
        out_specs=spec(pltpu.HBM),
        out_shape=array(*native),
        scratch_shapes=[pltpu.VMEM(native, F32), pltpu.SemaphoreType.DMA((LAST_PARTS,))],
        compiler_params=params(),
        cost_estimate=traffic(rows, 3),
        name="result",
    )(part, terms)


LATE_SLABS = 8
LATE_FLOWS = ((2, 1), (5, 6))


def swap(rows, start, without=()):
    pairs = [(i, i + 1) for i in range(start, lax.axis_size("space") - 1, 2)]
    pairs = pairs + [(j, i) for i, j in pairs]
    return lax.ppermute(rows, "space", [p for p in pairs if p not in without])


def swap_far(rows):
    if lax.axis_size("space") != LATE_SLABS:
        return [swap(rows, 1)]
    return [lax.ppermute(rows, "space", LATE_FLOWS), swap(rows, 1, LATE_FLOWS)]


def per_device(particle_profile, neighbors, face_vectors, volumes, wall_temp):
    cells, points = particle_profile.shape
    rows = points // LANES
    plane_count = NV // lax.axis_size("vel")
    native = particle_profile.reshape(cells, rows, LANES).transpose(1, 0, 2).reshape(cells * rows, LANES)
    wall = neighbors < 0
    links = jnp.where(wall, WALL_LINK, neighbors - lax.axis_index("space") * cells)
    own = (links >= 0) & (links < cells)
    first = -SPEED_LIMIT + ((lax.axis_index("vel") * plane_count).astype(F32) + 0.5) * H
    geo = jnp.concatenate(
        [
            face_vectors.reshape(3 * FACES, cells),
            volumes[None],
            wall_temp[None],
            wall.astype(F32),
            own.astype(F32),
            jnp.full((1, cells), first, F32),
        ]
    )
    geo = jnp.broadcast_to(geo[:, :, None], (GEO, cells, LANES))
    native, far, near = first_rows(native)
    far, near = swap_far(far), swap(near, 0)
    f, sums = first_sums(links, geo, native)
    sums, near = lax.optimization_barrier((sums, near))
    tiles = gather_sums(sums)
    part, pairs = flux(True, links, geo, f)
    part, absorbed = add_target(links, geo, None, tiles, f, part)
    part, near = edge(False, pairs, [near], f, part)
    near = swap(near, 0)
    f, far = edge(True, pairs, far, f, part)
    far = swap(far, 1)
    tiles = gather_sums(local_sums(links, geo, f))
    (part,) = flux(False, links, geo, f)
    (part,) = add_target(links, geo, absorbed, tiles, f, part)
    part, sums = last_near(geo, pairs, near, f, part)
    terms, sums = last_far(geo, pairs, far, f, sums)
    tiles = doubling_sums(sums)
    native = result(part, terms)
    macro_quantities = macro(tiles)
    evolved = native.reshape(rows, cells, LANES).transpose(1, 0, 2).reshape(cells, points)
    return evolved, macro_quantities


def solution(mesh):
    return jax.shard_map(
        per_device,
        mesh=mesh,
        in_specs=(
            P("space", "vel"),
            P(None, "space"),
            P(None, None, "space"),
            P("space"),
            P("space"),
        ),
        out_specs=(P("space", "vel"), P(None, "space")),
        check_vma=False,
    )
```

```python
import functools
import math

import jax
import jax.numpy as jnp
from jax import lax
from jax.experimental import pallas as pl
from jax.experimental.pallas import tpu as pltpu
from jax.sharding import PartitionSpec as P

NV = 64
FACES = 6
REACH = 3
STEPS = 2
LANES = 128
SUB = 8

TIME_STEP = 0.015
SHEAR = 0.1
POWER = 0.81
SPEED_LIMIT = 6.0
H = 2.0 * SPEED_LIMIT / NV
WEIGHT = H**3 * (2.0 * math.pi) ** (-1.5)

CHUNKS = NV * NV // LANES
TILES = CHUNKS // SUB

FV, VOL, WT, WALL, LOCAL, FIRST = 0, 18, 19, 20, 26, 32
GEO = 33
WALL_LINK = -64
BEFORE_PAIRS = tuple((g, r) for g in range(REACH) for r in range(g, REACH))
EMIT, ABSORB = 13, 19
SUMS = 25

F32 = jnp.float32


def lane_iota():
    return lax.broadcasted_iota(jnp.int32, (SUB, LANES), 1)


def sub_iota():
    return lax.broadcasted_iota(jnp.int32, (SUB, LANES), 0)


def half_of(lane):
    return (lane >= NV).astype(F32)


def third_component(lane):
    c = jnp.where(lane >= NV, lane - NV, lane).astype(F32)
    return -SPEED_LIMIT + (c + 0.5) * H


def tile_nodes(t):
    lane = lane_iota()
    b = (2 * SUB * t + 2 * sub_iota()).astype(F32) + half_of(lane)
    return -SPEED_LIMIT + (b + 0.5) * H, third_component(lane)


def column(tile, p):
    return jnp.broadcast_to(tile[:, p : p + 1], (SUB, LANES))


def splat(ref, i, g):
    return jnp.broadcast_to(ref[i, pl.ds(g, 1), :], (SUB, LANES))


def total(tile):
    return jnp.broadcast_to(jnp.sum(tile, axis=1, keepdims=True), (SUB, LANES))


def face_coefficients(geo_ref, k, g):
    return [splat(geo_ref, FV + FACES * i + k, g) for i in range(3)]


def at_rows(start, size=SUB):
    return pl.ds(pl.multiple_of(start, SUB), size)


def wall_tiles(wall_temp):
    rt = 1.0 / wall_temp
    scale = rt * jnp.sqrt(rt)
    out = []
    for t in range(TILES):
        xb, xc = tile_nodes(t)
        out.append(scale * jnp.exp(-0.5 * (xb * xb + xc * xc) * rt))
    return out


def pack_sums(arrays, start):
    lane = lane_iota()
    out = jnp.zeros((SUB, LANES), F32)
    for p, x in enumerate(arrays):
        out = jnp.where(lane == start + p, total(x), out)
    return out


def over_sublanes(ref, k):
    out = ref[k, pl.ds(0, SUB, stride=SUB), :]
    for s in range(1, SUB):
        out = out + ref[k, pl.ds(s, SUB, stride=SUB), :]
    return out


def list_faces(links_ref, wanted, cell_ref, face_ref):
    count = 0
    for g in range(SUB):
        for k in range(FACES):
            cell_ref[count] = g
            face_ref[count] = k
            count = count + wanted(links_ref[k, g]).astype(jnp.int32)
    return count


def is_wall(j):
    return j == WALL_LINK


def is_remote(j):
    return jnp.logical_or(j >= SUB, jnp.logical_and(j < 0, j != WALL_LINK))


def face_lists():
    return [pltpu.SMEM((FACES * SUB + 1,), jnp.int32)] * 2


def unroll(planes, most):
    return math.gcd(planes, most)


def finish_polynomials(y, first, planes):
    y0, y1, y2, y3, by0, by1, by2, bby0, bby1, bbby0 = y
    m = first + 0.5 * (planes - 1) * H
    c = third_component(lane_iota())
    cc = c * c
    a = y1 + m * y0
    aa = y2 + m * (2.0 * y1 + m * y0)
    aaa = y3 + m * (3.0 * y2 + m * (3.0 * y1 + m * y0))
    ab = by1 + m * by0
    aab = by2 + m * (2.0 * by1 + m * by0)
    abb = bby1 + m * bby0
    return (
        y0,
        a,
        by0,
        c * y0,
        aa,
        bby0,
        cc * y0,
        ab,
        c * a,
        c * by0,
        aaa + abb + cc * a,
        aab + bbby0 + cc * by0,
        c * (aa + bby0 + cc * y0),
    )


def polynomial_sums(f_ref, planes, parts_ref, first=0):
    half = planes // 2

    def cell(g, _):
        out = [None] * 10
        for t in range(TILES):
            y0 = y1 = y2 = y3 = None
            for i in range(half):
                d = (i + 0.5) * H
                hi = f_ref[g, pl.ds(((half + i) * TILES + t) * SUB, SUB), :]
                lo = f_ref[g, pl.ds(((half - 1 - i) * TILES + t) * SUB, SUB), :]
                s, r = hi + lo, hi - lo
                if i == 0:
                    y0, y1, y2, y3 = s, d * r, (d * d) * s, (d * d * d) * r
                else:
                    y0, y1, y2, y3 = y0 + s, y1 + d * r, y2 + (d * d) * s, y3 + (d * d * d) * r
            b, _c = tile_nodes(t)
            bb = b * b
            terms = (y0, y1, y2, y3, b * y0, b * y1, b * y2, bb * y0, bb * y1, bb * (b * y0))
            out = [x if o is None else o + x for o, x in zip(out, terms)]
        for p in range(10):
            parts_ref[p, at_rows((first + g) * SUB), :] = out[p]
        return 0

    lax.fori_loop(0, f_ref.shape[0], cell, 0)
    return [over_sublanes(parts_ref, p) for p in range(10)]


def native_polynomial_sums(native_ref, planes):
    half, side = planes // 2, CHUNKS // 2
    zero = jnp.zeros((SUB, LANES), F32)
    acc = [zero] * 10

    def plane(a, acc):
        xa = (a.astype(F32) - 0.5 * (planes - 1)) * H
        b0 = b1 = b2 = b3 = None
        for i in range(side):
            y = (2 * i + 1) * H
            hi = native_ref[at_rows((a * CHUNKS + side + i) * SUB), :]
            lo = native_ref[at_rows((a * CHUNKS + side - 1 - i) * SUB), :]
            s, d = hi + lo, hi - lo
            terms = (s, y * d, (y * y) * s, (y * y * y) * d)
            if i == 0:
                b0, b1, b2, b3 = terms
            else:
                b0, b1, b2, b3 = b0 + terms[0], b1 + terms[1], b2 + terms[2], b3 + terms[3]
        a0, a1, a2 = xa * b0, xa * b1, xa * b2
        aa0 = xa * a0
        new = (b0, a0, aa0, xa * aa0, b1, a1, xa * a1, b2, a2, b3)
        return tuple(x + z for x, z in zip(acc, new))

    g0, a0, aa0, aaa0, g1, a1, aa1, g2, a2, g3 = lax.fori_loop(0, planes, plane, tuple(acc))
    e = (half_of(lane_iota()) - 0.5) * H
    return [
        g0,
        a0,
        aa0,
        aaa0,
        g1 + e * g0,
        a1 + e * a0,
        aa1 + e * aa0,
        g2 + e * (2.0 * g1 + e * g0),
        a2 + e * (2.0 * a1 + e * a0),
        g3 + e * (3.0 * g2 + e * (3.0 * g1 + e * g0)),
    ]


def wall_sums(f_ref, planes, links_ref, geo_ref, sums_ref, cells, faces, with_absorbed):
    sums_ref[...] = jnp.zeros_like(sums_ref)

    def wall(i, _):
        g, k = cells[i], faces[i]
        v0, v1, v2 = face_coefficients(geo_ref, k, g)
        first = splat(geo_ref, FIRST, g)
        base = []
        for t in range(TILES):
            xb, xc = tile_nodes(t)
            base.append(v1 * xb + v2 * xc)
        if with_absorbed:
            wt = splat(geo_ref, WT, g)
            shape = wall_tiles(wt)

        def plane(a, acc):
            out, back = list(acc[0]), list(acc[1])
            xa = first + a.astype(F32) * H
            sa = v0 * xa
            if with_absorbed:
                wa = jnp.exp(-0.5 * xa * xa / wt)
            for t in range(TILES):
                s = sa + base[t]
                f = f_ref[g, at_rows((a * TILES + t) * SUB), :]
                out[t] = out[t] + jnp.maximum(s, 0.0) * f
                if with_absorbed:
                    back[t] = back[t] + jnp.maximum(-s, 0.0) * (wa * shape[t])
            return tuple(out), tuple(back)

        zeros = (jnp.zeros((SUB, LANES), F32),) * TILES
        out, back = lax.fori_loop(0, planes, plane, (zeros, zeros), unroll=unroll(planes, 16))
        at = at_rows(g * SUB)
        sums_ref[k, at, :] = (out[0] + out[1]) + (out[2] + out[3])
        if with_absorbed:
            sums_ref[FACES + k, at, :] = (back[0] + back[1]) + (back[2] + back[3])
        return 0

    lax.fori_loop(0, list_faces(links_ref, is_wall, cells, faces), wall, 0)


def sums_kernel(links_ref, geo_ref, f_ref, sums_out, parts_ref, face_ref, cells, faces):
    planes = f_ref.shape[1] // CHUNKS
    y = polynomial_sums(f_ref, planes, parts_ref)
    packed = pack_sums(finish_polynomials(y, geo_ref[FIRST], planes), 0)
    wall_sums(f_ref, planes, links_ref, geo_ref, face_ref, cells, faces, False)
    sums_out[...] = packed + pack_sums([over_sublanes(face_ref, k) for k in range(FACES)], EMIT)


def first_sums_kernel(links_ref, geo_ref, native_ref, f_ref, sums_out, face_ref, cells, faces):
    rows = f_ref.shape[1]
    planes = rows // CHUNKS

    def group(j, _):
        for g in range(SUB):
            f_ref[g, at_rows(j * SUB), :] = native_ref[pl.ds(j * SUB * SUB + g, SUB, stride=SUB), :]
        return 0

    lax.fori_loop(0, rows // SUB, group, 0, unroll=2)
    y = native_polynomial_sums(native_ref, planes)
    packed = pack_sums(finish_polynomials(y, geo_ref[FIRST], planes), 0)
    wall_sums(f_ref, planes, links_ref, geo_ref, face_ref, cells, faces, True)
    sums_out[...] = packed + pack_sums([over_sublanes(face_ref, k) for k in range(2 * FACES)], EMIT)


def spec(space):
    return pl.BlockSpec(memory_space=space)


def array(*shape):
    return jax.ShapeDtypeStruct(shape, F32)


def params(mib=4):
    return pltpu.CompilerParams(vmem_limit_bytes=mib * 1024 * 1024)


def traffic(rows, profiles):
    size = SUB * rows * LANES
    return pl.CostEstimate(flops=8 * profiles * size, bytes_accessed=4 * profiles * size, transcendentals=0)


def local_sums(links, geo, f):
    return pl.pallas_call(
        sums_kernel,
        in_specs=[spec(pltpu.SMEM), spec(pltpu.VMEM), spec(pltpu.VMEM)],
        out_specs=spec(pltpu.VMEM),
        out_shape=array(SUB, LANES),
        scratch_shapes=[
                pltpu.VMEM((10, SUB * SUB, LANES), F32),
            pltpu.VMEM((FACES, SUB * SUB, LANES), F32),
            *face_lists(),
        ],
        compiler_params=params(),
        cost_estimate=traffic(f.shape[1], 4),
        name="local_sums",
    )(links, geo, f)


def first_sums(links, geo, native):
    rows = native.shape[0] // SUB
    return pl.pallas_call(
        first_sums_kernel,
        in_specs=[spec(pltpu.SMEM), spec(pltpu.VMEM), spec(pltpu.VMEM)],
        out_specs=[spec(pltpu.VMEM)] * 2,
        out_shape=[array(SUB, rows, LANES), array(SUB, LANES)],
        scratch_shapes=[
                pltpu.VMEM((2 * FACES, SUB * SUB, LANES), F32),
            *face_lists(),
        ],
        compiler_params=params(),
        cost_estimate=traffic(rows, 5),
        name="first_sums",
    )(links, geo, native)


SPLIT_PARTS = 8


def is_odd():
    return lax.rem(lax.axis_index("space"), 2) == 1


def first_rows_kernel(native_hbm, native_ref, far_any, near_any, far_ref, near_ref, sems, far_sems, near_sems):
    rows = native_ref.shape[0]
    part = rows // SPLIT_PARTS
    copies = [
        pltpu.make_async_copy(
            native_hbm.at[pl.ds(i * part, part)], native_ref.at[pl.ds(i * part, part)], sems.at[i]
        )
        for i in range(SPLIT_PARTS)
    ]
    for c in copies:
        c.start()
    odd = is_odd()
    far = jnp.where(odd, SUB - REACH, 0)
    near = jnp.where(odd, 0, SUB - REACH)
    groups = part // (SUB * SUB)
    out = []

    for i, c in enumerate(copies):
        c.wait()

        def group(j, _):
            for r in range(REACH):
                at = at_rows(j * SUB)
                far_ref[r, at, :] = native_ref[pl.ds(j * SUB * SUB + far + r, SUB, stride=SUB), :]
                near_ref[r, at, :] = native_ref[pl.ds(j * SUB * SUB + near + r, SUB, stride=SUB), :]
            return 0

        lax.fori_loop(i * groups, (i + 1) * groups, group, 0, unroll=unroll(groups, 8))
        at = pl.ds(i * groups * SUB, groups * SUB)
        out.append(pltpu.make_async_copy(far_ref.at[:, at], far_any.at[:, at], far_sems.at[i]))
        out.append(pltpu.make_async_copy(near_ref.at[:, at], near_any.at[:, at], near_sems.at[i]))
        out[-2].start()
        out[-1].start()
    for c in out:
        c.wait()


def first_rows(native):
    rows = native.shape[0] // SUB
    halo = (REACH, rows, LANES)
    return pl.pallas_call(
        first_rows_kernel,
        in_specs=[spec(pltpu.HBM)],
        out_specs=[spec(pltpu.VMEM), spec(pl.ANY), spec(pl.ANY)],
        out_shape=[array(*native.shape), array(*halo), array(*halo)],
        scratch_shapes=[pltpu.VMEM(halo, F32)] * 2 + [pltpu.SemaphoreType.DMA((SPLIT_PARTS,))] * 3,
        compiler_params=params(),
        cost_estimate=traffic(rows, 4),
        name="first_rows",
    )(pltpu.with_memory_space_constraint(native, pltpu.HBM))


def pair_weights(links_ref, geo_ref, pairs_ref, cells, faces):
    rows = pairs_ref.shape[1]
    planes = rows // CHUNKS
    first = splat(geo_ref, FIRST, 0)

    def clear(j, _):
        for p in range(pairs_ref.shape[0]):
            pairs_ref[p, at_rows(j * SUB), :] = jnp.zeros((SUB, LANES), F32)
        return 0

    lax.fori_loop(0, rows // SUB, clear, 0, unroll=4)

    def remote(i, _):
        g, k = cells[i], faces[i]
        j = links_ref[k, g]
        edge = g - (SUB - REACH)
        before = g * REACH - g * (g - 1) // 2 + (j + REACH) - g
        after = len(BEFORE_PAIRS) + edge * (edge + 1) // 2 + j - SUB
        at_pair = jnp.where(j < 0, before, after)
        scale = -TIME_STEP / splat(geo_ref, VOL, g)
        v0, v1, v2 = [scale * x for x in face_coefficients(geo_ref, k, g)]
        base = []
        for t in range(TILES):
            xb, xc = tile_nodes(t)
            base.append(v1 * xb + v2 * xc)

        def plane(a, _):
            sa = v0 * (first + a.astype(F32) * H)
            for t in range(TILES):
                at = at_rows((a * TILES + t) * SUB)
                pairs_ref[at_pair, at, :] = pairs_ref[at_pair, at, :] + jnp.maximum(sa + base[t], 0.0)
            return 0

        lax.fori_loop(0, planes, plane, 0, unroll=unroll(planes, 8))
        return 0

    lax.fori_loop(0, list_faces(links_ref, is_remote, cells, faces), remote, 0)


def gather_sums(tile):
    size = lax.axis_size("vel")
    if size not in (2, 4):
        return [lax.psum(tile, "vel")]
    others = [lax.ppermute(tile, "vel", [(i, i ^ s) for i in range(size)]) for s in range(1, size)]
    return [tile, *others]


def add_tiles(refs):
    tiles = [r[...] for r in refs]
    while len(tiles) > 1:
        tiles = [tiles[i] + tiles[i + 1] for i in range(0, len(tiles), 2)]
    return tiles[0]


def quantities(tile):
    m = [WEIGHT * column(tile, p) for p in range(13)]
    n = m[0]
    rn = 1.0 / n
    u = [m[1 + i] * rn for i in range(3)]
    uu = u[0] * u[0] + u[1] * u[1] + u[2] * u[2]
    trace = m[4] + m[5] + m[6]
    width = trace - n * uu
    temperature = width * rn * (1.0 / 3.0)
    second = [[m[4], m[7], m[8]], [m[7], m[5], m[9]], [m[8], m[9], m[6]]]
    q = []
    for i in range(3):
        across = u[0] * second[i][0] + u[1] * second[i][1] + u[2] * second[i][2]
        q.append(0.5 * (m[10 + i] - 2.0 * across - u[i] * trace + 2.0 * uu * m[1 + i]))
    return n, u, temperature, q


def macro_kernel(*refs):
    out_ref = refs[-1]
    n, u, temperature, q = quantities(add_tiles(refs[:-1]))
    lane, sub = lane_iota(), sub_iota()
    for i, x in enumerate((n, *u, temperature, *q)):
        row = jnp.sum(jnp.where(lane == sub, x, 0.0), axis=0, keepdims=True)
        out_ref[pl.ds(i, 1), :] = row[:, :SUB]


def macro(tiles):
    return pl.pallas_call(
        macro_kernel,
        in_specs=[spec(pltpu.VMEM)] * len(tiles),
        out_specs=spec(pltpu.VMEM),
        out_shape=array(8, SUB),
        compiler_params=params(1),
        name="macro",
    )(*tiles)


def flux_kernel(with_pairs, links_ref, geo_ref, f_ref, out_ref, *refs):
    if with_pairs:
        pairs_ref, cells, faces = refs[0], refs[-2], refs[-1]
        pair_weights(links_ref, geo_ref, pairs_ref, cells, faces)
        refs = refs[1:-2]
    coef, bases, stays, source, face = refs
    planes = f_ref.shape[1] // CHUNKS
    scale = -TIME_STEP / geo_ref[VOL]
    for i in range(3):
        whole = None
        for k in range(FACES):
            x = scale * geo_ref[FV + FACES * i + k]
            coef[FACES * i + k] = x
            whole = x if whole is None else whole + x
        coef[3 * FACES + i] = whole

    def table(g, _):
        w = [[splat(coef, FACES * i + k, g) for i in (1, 2)] for k in range(FACES)]
        whole = [splat(coef, 3 * FACES + i, g) for i in (1, 2)]
        for t in range(TILES):
            xb, xc = tile_nodes(t)
            for k in range(FACES):
                bases[k, g * TILES + t] = w[k][0] * xb + w[k][1] * xc
            stays[g * TILES + t] = 1.0 + whole[0] * xb + whole[1] * xc
        return 0

    lax.fori_loop(0, SUB, table, 0, unroll=2)

    def cell(g, _):
        count = 0
        for k in range(FACES):
            j = links_ref[k, g]
            source[count] = j
            face[count] = k
            count = count + jnp.logical_and(j >= 0, j < SUB).astype(jnp.int32)
        for n in range(FACES + 1):

            @pl.when(count == n)
            def _():
                own_faces(g, n)

        return 0

    def own_faces(g, n):
        at_source = [source[i] for i in range(n)]
        first_weight = [splat(coef, face[k], g) for k in range(n)]
        whole = splat(coef, 3 * FACES, g)
        x0 = splat(geo_ref, FIRST, g)
        base = [[bases[face[k], g * TILES + t] for k in range(n)] for t in range(TILES)]
        stay = [stays[g * TILES + t] for t in range(TILES)]

        def plane(a, _):
            xa = x0 + a.astype(F32) * H
            sa = [w * xa for w in first_weight]
            stay_a = whole * xa
            for t in range(TILES):
                at = at_rows((a * TILES + t) * SUB)
                f = f_ref[g, at, :]
                acc = f * (stay_a + stay[t])
                for k in range(n):
                    acc = acc + jnp.maximum(sa[k] + base[t][k], 0.0) * (f_ref[at_source[k], at, :] - f)
                out_ref[g, at, :] = acc
            return 0

        lax.fori_loop(0, planes, plane, 0, unroll=unroll(planes, 8))

    lax.fori_loop(0, SUB, cell, 0)


def flux(with_pairs, links, geo, f):
    rows = f.shape[1]
    pairs = 2 * len(BEFORE_PAIRS)
    return pl.pallas_call(
        functools.partial(flux_kernel, with_pairs),
        in_specs=[spec(pltpu.SMEM), spec(pltpu.VMEM), spec(pltpu.VMEM)],
        out_specs=[spec(pltpu.VMEM)] * (2 if with_pairs else 1),
        out_shape=[array(*f.shape)] + ([array(pairs, rows, LANES)] if with_pairs else []),
        scratch_shapes=[
            pltpu.VMEM((3 * FACES + 3, SUB, LANES), F32),
            pltpu.VMEM((FACES, SUB * TILES, SUB, LANES), F32),
            pltpu.VMEM((SUB * TILES, SUB, LANES), F32),
            pltpu.SMEM((FACES + 1,), jnp.int32),
            pltpu.SMEM((FACES + 1,), jnp.int32),
        ]
        + (face_lists() if with_pairs else []),
        compiler_params=params(),
        cost_estimate=traffic(rows, 9 if with_pairs else 7),
        name="flux",
    )(links, geo, f)


def target_kernel(count, links_ref, geo_ref, absorbed_in, *refs):
    sums_refs, (f_ref, part_ref, out_ref, *sum_out, tiles_ref, coef, cells, faces) = refs[:count], refs[count:]
    planes = f_ref.shape[1] // CHUNKS
    sums = add_tiles(sums_refs)
    for ref in sum_out:
        ref[...] = sums
    absorbed = sums if absorbed_in is None else absorbed_in[...]
    n, u, temperature, q = quantities(sums)
    rt = 1.0 / temperature
    rate = TIME_STEP * n * temperature / (SHEAR * jnp.exp(POWER * jnp.log(temperature)))
    height = rate * n * rt * jnp.sqrt(rt)
    slope = (1.0 / 3.0) / (5.0 * n * temperature * temperature)
    coef[0] = rate
    coef[1] = rt
    coef[2], coef[3] = u[1], u[2]
    coef[4], coef[5] = slope * q[1], slope * q[2]
    coef[6], coef[7], coef[8] = u[0], slope * q[0], height
    for k in range(FACES):
        wall = geo_ref[WALL + k] > 0.5
        coef[9 + k] = column(sums, EMIT + k) / jnp.where(wall, column(absorbed, ABSORB + k), 1.0)

    def tile_table(g, _):
        rtg = splat(coef, 1, g)
        ub, uc = splat(coef, 2, g), splat(coef, 3, g)
        qb, qc = splat(coef, 4, g), splat(coef, 5, g)
        shape = wall_tiles(splat(geo_ref, WT, g))
        for t in range(TILES):
            xb, xc = tile_nodes(t)
            cb, cc = xb - ub, xc - uc
            z = (cb * cb + cc * cc) * rtg
            at = g * TILES + t
            tiles_ref[0, at] = jnp.exp(-0.5 * z)
            tiles_ref[1, at] = cb * qb + cc * qc
            tiles_ref[2, at] = z
            tiles_ref[3, at] = shape[t]
        return 0

    lax.fori_loop(0, SUB, tile_table, 0, unroll=4)

    def cell(g, _):
        rate_g, rtg, u0, q0, height_g = [splat(coef, i, g) for i in (0, 1, 6, 7, 8)]
        x0 = splat(geo_ref, FIRST, g) - u0
        bell, heat, zz = [[tiles_ref[i, g * TILES + t] for t in range(TILES)] for i in range(3)]

        def plane(a, _):
            ca = x0 + a.astype(F32) * H
            za = ca * ca * rtg
            height_a = height_g * jnp.exp(-0.5 * za)
            heat_a = q0 * ca
            z_a = za - 5.0
            for t in range(TILES):
                where = (g, at_rows((a * TILES + t) * SUB), slice(None))
                f = f_ref[where]
                target = (height_a * bell[t]) * (1.0 + (heat_a + heat[t]) * (z_a + zz[t]))
                out_ref[where] = (part_ref[where] - rate_g * f) + target
            return 0

        lax.fori_loop(0, planes, plane, 0, unroll=unroll(planes, 16))
        return 0

    lax.fori_loop(0, SUB, cell, 0)

    def wall(i, _):
        g, k = cells[i], faces[i]
        x0 = splat(geo_ref, FIRST, g)
        ratio = splat(coef, 9 + k, g)
        scale = -TIME_STEP / splat(geo_ref, VOL, g)
        v0, v1, v2 = [scale * x for x in face_coefficients(geo_ref, k, g)]
        base, shape = [], []
        for t in range(TILES):
            xb, xc = tile_nodes(t)
            base.append(v1 * xb + v2 * xc)
            shape.append(ratio * tiles_ref[3, g * TILES + t])

        rt_wall = -0.5 / splat(geo_ref, WT, g)

        def plane(a, _):
            xa = x0 + a.astype(F32) * H
            wa = jnp.exp(xa * xa * rt_wall)
            sa = v0 * xa
            for t in range(TILES):
                where = (g, at_rows((a * TILES + t) * SUB), slice(None))
                f = f_ref[where]
                out_ref[where] = out_ref[where] + jnp.maximum(sa + base[t], 0.0) * (wa * shape[t] - f)
            return 0

        lax.fori_loop(0, planes, plane, 0, unroll=unroll(planes, 16))
        return 0

    lax.fori_loop(0, list_faces(links_ref, is_wall, cells, faces), wall, 0)


def add_target(links, geo, absorbed, tiles, f, part):
    rows = f.shape[1]
    vmem = spec(pltpu.VMEM)
    given = [links, geo] + ([] if absorbed is None else [absorbed]) + list(tiles) + [f, part]

    def kernel(links_ref, geo_in, *refs):
        if absorbed is None:
            target_kernel(len(tiles), links_ref, geo_in, None, *refs)
        else:
            target_kernel(len(tiles), links_ref, geo_in, *refs)

    return pl.pallas_call(
        kernel,
        in_specs=[spec(pltpu.SMEM)] + [vmem] * (len(given) - 1),
        out_specs=[vmem] * (2 if absorbed is None else 1),
        out_shape=[array(*part.shape)] + ([array(SUB, LANES)] if absorbed is None else []),
        input_output_aliases={len(given) - 1: 0},
        scratch_shapes=[
                pltpu.VMEM((4, SUB * TILES, SUB, LANES), F32),
            pltpu.VMEM((9 + FACES, SUB, LANES), F32),
            *face_lists(),
        ],
        compiler_params=params(),
        cost_estimate=traffic(rows, 7),
        name="add_target",
    )(*given)


def side_terms(high, pairs_ref, halo_ref, f_ref, at):
    terms = [None] * REACH
    rows = [halo_ref[r, at, :] for r in range(REACH)]
    first = SUB - REACH if high else 0
    own = [f_ref[first + e, at, :] for e in range(REACH)]
    count = len(BEFORE_PAIRS)
    pairs = [(e, r) for e in range(REACH) for r in range(e + 1)] if high else BEFORE_PAIRS
    for p, (e, r) in enumerate(pairs):
        term = pairs_ref[p + count if high else p, at, :] * (rows[r] - own[e])
        terms[e] = term if terms[e] is None else terms[e] + term
    return first, terms


def for_side(far, run):
    odd = is_odd()

    @pl.when(odd)
    def _():
        run(far)

    @pl.when(jnp.logical_not(odd))
    def _():
        run(not far)


def add_side(far, pairs_ref, halo_ref, old_ref, part_ref, f_ref, rows_ref, ready=None):
    def run(high):
        def group(j, _):
            at = at_rows(j * SUB)
            first, terms = side_terms(high, pairs_ref, halo_ref, old_ref, at)
            for e in range(REACH):
                x = part_ref[first + e, at, :] + terms[e]
                f_ref[first + e, at, :] = x
                if rows_ref is not None:
                    rows_ref[e, at, :] = x
            return 0

        groups = part_ref.shape[1] // SUB
        parts = 1 if ready is None else EDGE_PARTS
        for i in range(parts):
            if ready is not None:
                ready(i)
            count = groups // parts
            lax.fori_loop(i * count, (i + 1) * count, group, 0, unroll=unroll(count, 8))

    for_side(far, run)


EDGE_PARTS = 4


def near_edge_kernel(pairs_ref, halo_any, old_ref, part_ref, f_ref, rows_ref, halo_ref, sems):
    size = halo_ref.shape[1] // EDGE_PARTS

    def copy(i):
        at = pl.ds(i * size, size)
        return pltpu.make_async_copy(halo_any.at[:, at], halo_ref.at[:, at], sems.at[i])

    for i in range(EDGE_PARTS):
        copy(i).start()
    add_side(False, pairs_ref, halo_ref, old_ref, part_ref, f_ref, rows_ref, lambda i: copy(i).wait())


def edge(far, pairs, halo, old, part):
    rows = part.shape[1]
    return pl.pallas_call(
        functools.partial(add_side, True) if far else near_edge_kernel,
        in_specs=[spec(pltpu.VMEM), spec(pltpu.VMEM if far else pl.ANY), spec(pltpu.VMEM), spec(pltpu.VMEM)],
        out_specs=[spec(pltpu.VMEM)] * 2,
        out_shape=[array(SUB, rows, LANES), array(REACH, rows, LANES)],
        input_output_aliases={3: 0},
        scratch_shapes=[] if far else [pltpu.VMEM(halo.shape, F32), pltpu.SemaphoreType.DMA((EDGE_PARTS,))],
        compiler_params=params(),
        cost_estimate=traffic(rows, 2),
        name="far_edge" if far else "near_edge",
    )(pairs, halo, old, part)


def last_near_kernel(geo_ref, pairs_ref, halo_ref, old_ref, part_ref, f_ref, sums_out, parts_ref):
    add_side(False, pairs_ref, halo_ref, old_ref, part_ref, f_ref, None)
    planes = f_ref.shape[1] // CHUNKS
    y = polynomial_sums(f_ref, planes, parts_ref)
    sums_out[...] = pack_sums(finish_polynomials(y, geo_ref[FIRST], planes), 0)


def last_near(geo, pairs, near, old, part):
    rows = part.shape[1]
    return pl.pallas_call(
        last_near_kernel,
        in_specs=[spec(pltpu.VMEM)] * 5,
        out_specs=[spec(pltpu.VMEM)] * 2,
        out_shape=[array(SUB, rows, LANES), array(SUB, LANES)],
        input_output_aliases={4: 0},
        scratch_shapes=[pltpu.VMEM((10, SUB * SUB, LANES), F32)],
        compiler_params=params(),
        cost_estimate=traffic(rows, 3),
        name="last_near",
    )(geo, pairs, near, old, part)


def last_far_kernel(geo_ref, pairs_ref, halo_ref, old_ref, sums_in, terms_ref, sums_out, parts_ref):
    rows = old_ref.shape[1]
    planes = rows // CHUNKS
    parts_ref[...] = jnp.zeros_like(parts_ref)

    def run(high):
        def group(j, _):
            at = at_rows(j * SUB)
            _first, terms = side_terms(high, pairs_ref, halo_ref, old_ref, at)
            for e in range(REACH):
                terms_ref[e, at, :] = terms[e]
            return 0

        lax.fori_loop(0, rows // SUB, group, 0, unroll=unroll(rows // SUB, 8))
        y = polynomial_sums(terms_ref, planes, parts_ref, SUB - REACH if high else 0)
        sums_out[...] = sums_in[...] + pack_sums(finish_polynomials(y, geo_ref[FIRST], planes), 0)

    for_side(True, run)


def last_far(geo, pairs, far, old, sums):
    rows = old.shape[1]
    return pl.pallas_call(
        last_far_kernel,
        in_specs=[spec(pltpu.VMEM)] * 5,
        out_specs=[spec(pltpu.VMEM)] * 2,
        out_shape=[array(REACH, rows, LANES), array(SUB, LANES)],
        scratch_shapes=[pltpu.VMEM((10, SUB * SUB, LANES), F32)],
        compiler_params=params(),
        cost_estimate=traffic(rows, 2),
        name="last_far",
    )(geo, pairs, far, old, sums)


LAST_PARTS = 4


def result_kernel(part_ref, terms_ref, out_hbm, native_ref, sems):
    part = part_ref.shape[1] // SUB // LAST_PARTS

    def copy(i):
        at = pl.ds(i * part * SUB * SUB, part * SUB * SUB)
        return pltpu.make_async_copy(native_ref.at[at], out_hbm.at[at], sems.at[i])

    def run(high):
        first = SUB - REACH if high else 0
        for i in range(LAST_PARTS):

            def group(j, _):
                at = at_rows(j * SUB)
                for g in range(SUB):
                    x = part_ref[g, at, :]
                    if 0 <= g - first < REACH:
                        x = x + terms_ref[g - first, at, :]
                    native_ref[pl.ds(j * SUB * SUB + g, SUB, stride=SUB), :] = x
                return 0

            lax.fori_loop(i * part, (i + 1) * part, group, 0, unroll=unroll(part, 4))
            copy(i).start()

    for_side(True, run)
    for i in range(LAST_PARTS):
        copy(i).wait()


def result(part, terms):
    rows = part.shape[1]
    native = (SUB * rows, LANES)
    return pl.pallas_call(
        result_kernel,
        in_specs=[spec(pltpu.VMEM)] * 2,
        out_specs=spec(pltpu.HBM),
        out_shape=array(*native),
        scratch_shapes=[pltpu.VMEM(native, F32), pltpu.SemaphoreType.DMA((LAST_PARTS,))],
        compiler_params=params(),
        cost_estimate=traffic(rows, 3),
        name="result",
    )(part, terms)


def swap(rows, start):
    pairs = [(i, i + 1) for i in range(start, lax.axis_size("space") - 1, 2)]
    return lax.ppermute(rows, "space", pairs + [(j, i) for i, j in pairs])


def per_device(particle_profile, neighbors, face_vectors, volumes, wall_temp):
    cells, points = particle_profile.shape
    rows = points // LANES
    plane_count = NV // lax.axis_size("vel")
    native = particle_profile.reshape(cells, rows, LANES).transpose(1, 0, 2).reshape(cells * rows, LANES)
    wall = neighbors < 0
    links = jnp.where(wall, WALL_LINK, neighbors - lax.axis_index("space") * cells)
    own = (links >= 0) & (links < cells)
    first = -SPEED_LIMIT + ((lax.axis_index("vel") * plane_count).astype(F32) + 0.5) * H
    geo = jnp.concatenate(
        [
            face_vectors.reshape(3 * FACES, cells),
            volumes[None],
            wall_temp[None],
            wall.astype(F32),
            own.astype(F32),
            jnp.full((1, cells), first, F32),
        ]
    )
    geo = jnp.broadcast_to(geo[:, :, None], (GEO, cells, LANES))
    native, far, near = first_rows(native)
    far, near = swap(far, 1), swap(near, 0)
    f, sums = first_sums(links, geo, native)
    tiles = gather_sums(sums)
    part, pairs = flux(True, links, geo, f)
    part, absorbed = add_target(links, geo, None, tiles, f, part)
    part, near = edge(False, pairs, near, f, part)
    near = swap(near, 0)
    f, far = edge(True, pairs, far, f, part)
    far = swap(far, 1)
    tiles = gather_sums(local_sums(links, geo, f))
    (part,) = flux(False, links, geo, f)
    (part,) = add_target(links, geo, absorbed, tiles, f, part)
    part, sums = last_near(geo, pairs, near, f, part)
    terms, sums = last_far(geo, pairs, far, f, sums)
    tiles = gather_sums(sums)
    native = result(part, terms)
    macro_quantities = macro(tiles)
    evolved = native.reshape(rows, cells, LANES).transpose(1, 0, 2).reshape(cells, points)
    return evolved, macro_quantities


def solution(mesh):
    return jax.shard_map(
        per_device,
        mesh=mesh,
        in_specs=(
            P("space", "vel"),
            P(None, "space"),
            P(None, None, "space"),
            P("space"),
            P("space"),
        ),
        out_specs=(P("space", "vel"), P(None, "space")),
        check_vma=False,
    )
```

```python
import functools
import math

import jax
import jax.numpy as jnp
from jax import lax
from jax.experimental import pallas as pl
from jax.experimental.pallas import tpu as pltpu
from jax.sharding import PartitionSpec as P

NV = 64
FACES = 6
REACH = 3
STEPS = 2
LANES = 128
SUB = 8
SPARE = SUB

TIME_STEP = 0.015
SHEAR = 0.1
POWER = 0.81
SPEED_LIMIT = 6.0
H = 2.0 * SPEED_LIMIT / NV
WEIGHT = H**3 * (2.0 * math.pi) ** (-1.5)

CHUNKS = NV * NV // LANES
TILES = CHUNKS // SUB

FV, VOL, WT, WALL, LOCAL, FIRST = 0, 18, 19, 20, 26, 32
GEO = 33
WALL_LINK = -64
BEFORE_PAIRS = tuple((g, r) for g in range(REACH) for r in range(g, REACH))
EMIT, ABSORB = 13, 19
SUMS = 25

F32 = jnp.float32


def lane_iota():
    return lax.broadcasted_iota(jnp.int32, (SUB, LANES), 1)


def sub_iota():
    return lax.broadcasted_iota(jnp.int32, (SUB, LANES), 0)


def half_of(lane):
    return (lane >= NV).astype(F32)


def third_component(lane):
    c = jnp.where(lane >= NV, lane - NV, lane).astype(F32)
    return -SPEED_LIMIT + (c + 0.5) * H


def tile_nodes(t):
    lane = lane_iota()
    b = (2 * SUB * t + 2 * sub_iota()).astype(F32) + half_of(lane)
    return -SPEED_LIMIT + (b + 0.5) * H, third_component(lane)


def column(tile, p):
    return jnp.broadcast_to(tile[:, p : p + 1], (SUB, LANES))


def splat(ref, i, g):
    return jnp.broadcast_to(ref[i, pl.ds(g, 1), :], (SUB, LANES))


def total(tile):
    return jnp.broadcast_to(jnp.sum(tile, axis=1, keepdims=True), (SUB, LANES))


def face_coefficients(geo_ref, k, g):
    return [splat(geo_ref, FV + FACES * i + k, g) for i in range(3)]


def at_rows(start, size=SUB):
    return pl.ds(pl.multiple_of(start, SUB), size)


def wall_tiles(wall_temp):
    rt = 1.0 / wall_temp
    scale = rt * jnp.sqrt(rt)
    out = []
    for t in range(TILES):
        xb, xc = tile_nodes(t)
        out.append(scale * jnp.exp(-0.5 * (xb * xb + xc * xc) * rt))
    return out


def pack_sums(arrays, start):
    lane = lane_iota()
    out = jnp.zeros((SUB, LANES), F32)
    for p, x in enumerate(arrays):
        out = jnp.where(lane == start + p, total(x), out)
    return out


def over_sublanes(ref, k):
    out = ref[k, pl.ds(0, SUB, stride=SUB), :]
    for s in range(1, SUB):
        out = out + ref[k, pl.ds(s, SUB, stride=SUB), :]
    return out


def list_faces(links_ref, wanted, cell_ref, face_ref):
    count = 0
    for g in range(SUB):
        for k in range(FACES):
            cell_ref[count] = g
            face_ref[count] = k
            count = count + wanted(links_ref[k, g]).astype(jnp.int32)
    return count


def is_wall(j):
    return j == WALL_LINK


def is_remote(j):
    return jnp.logical_or(j >= SUB, jnp.logical_and(j < 0, j != WALL_LINK))


def face_lists():
    return [pltpu.SMEM((FACES * SUB + 1,), jnp.int32)] * 2


def unroll(planes, most):
    return math.gcd(planes, most)


def finish_polynomials(y, first, planes):
    y0, y1, y2, y3, by0, by1, by2, bby0, bby1, bbby0 = y
    m = first + 0.5 * (planes - 1) * H
    c = third_component(lane_iota())
    cc = c * c
    a = y1 + m * y0
    aa = y2 + m * (2.0 * y1 + m * y0)
    aaa = y3 + m * (3.0 * y2 + m * (3.0 * y1 + m * y0))
    ab = by1 + m * by0
    aab = by2 + m * (2.0 * by1 + m * by0)
    abb = bby1 + m * bby0
    return (
        y0,
        a,
        by0,
        c * y0,
        aa,
        bby0,
        cc * y0,
        ab,
        c * a,
        c * by0,
        aaa + abb + cc * a,
        aab + bbby0 + cc * by0,
        c * (aa + bby0 + cc * y0),
    )


def polynomial_sums(f_ref, planes, parts_ref, first=0):
    half = planes // 2

    def cell(g, _):
        out = [None] * 10
        for t in range(TILES):
            y0 = y1 = y2 = y3 = None
            for i in range(half):
                d = (i + 0.5) * H
                hi = f_ref[g, pl.ds(((half + i) * TILES + t) * SUB, SUB), :]
                lo = f_ref[g, pl.ds(((half - 1 - i) * TILES + t) * SUB, SUB), :]
                s, r = hi + lo, hi - lo
                if i == 0:
                    y0, y1, y2, y3 = s, d * r, (d * d) * s, (d * d * d) * r
                else:
                    y0, y1, y2, y3 = y0 + s, y1 + d * r, y2 + (d * d) * s, y3 + (d * d * d) * r
            b, _c = tile_nodes(t)
            bb = b * b
            terms = (y0, y1, y2, y3, b * y0, b * y1, b * y2, bb * y0, bb * y1, bb * (b * y0))
            out = [x if o is None else o + x for o, x in zip(out, terms)]
        for p in range(10):
            parts_ref[p, at_rows((first + g) * SUB), :] = out[p]
        return 0

    lax.fori_loop(0, f_ref.shape[0], cell, 0)
    return [over_sublanes(parts_ref, p) for p in range(10)]


def native_polynomial_sums(native_ref, planes):
    half, side = planes // 2, CHUNKS // 2
    zero = jnp.zeros((SUB, LANES), F32)
    acc = [zero] * 10

    def plane(a, acc):
        xa = (a.astype(F32) - 0.5 * (planes - 1)) * H
        b0 = b1 = b2 = b3 = None
        for i in range(side):
            y = (2 * i + 1) * H
            hi = native_ref[at_rows((a * CHUNKS + side + i) * SUB), :]
            lo = native_ref[at_rows((a * CHUNKS + side - 1 - i) * SUB), :]
            s, d = hi + lo, hi - lo
            terms = (s, y * d, (y * y) * s, (y * y * y) * d)
            if i == 0:
                b0, b1, b2, b3 = terms
            else:
                b0, b1, b2, b3 = b0 + terms[0], b1 + terms[1], b2 + terms[2], b3 + terms[3]
        a0, a1, a2 = xa * b0, xa * b1, xa * b2
        aa0 = xa * a0
        new = (b0, a0, aa0, xa * aa0, b1, a1, xa * a1, b2, a2, b3)
        return tuple(x + z for x, z in zip(acc, new))

    g0, a0, aa0, aaa0, g1, a1, aa1, g2, a2, g3 = lax.fori_loop(0, planes, plane, tuple(acc))
    e = (half_of(lane_iota()) - 0.5) * H
    return [
        g0,
        a0,
        aa0,
        aaa0,
        g1 + e * g0,
        a1 + e * a0,
        aa1 + e * aa0,
        g2 + e * (2.0 * g1 + e * g0),
        a2 + e * (2.0 * a1 + e * a0),
        g3 + e * (3.0 * g2 + e * (3.0 * g1 + e * g0)),
    ]


def wall_sums(f_ref, planes, links_ref, geo_ref, sums_ref, cells, faces, with_absorbed):
    sums_ref[...] = jnp.zeros_like(sums_ref)

    def wall(i, _):
        g, k = cells[i], faces[i]
        v0, v1, v2 = face_coefficients(geo_ref, k, g)
        first = splat(geo_ref, FIRST, g)
        base = []
        for t in range(TILES):
            xb, xc = tile_nodes(t)
            base.append(v1 * xb + v2 * xc)
        if with_absorbed:
            wt = splat(geo_ref, WT, g)
            shape = wall_tiles(wt)

        def plane(a, acc):
            out, back = list(acc[0]), list(acc[1])
            xa = first + a.astype(F32) * H
            sa = v0 * xa
            if with_absorbed:
                wa = jnp.exp(-0.5 * xa * xa / wt)
            for t in range(TILES):
                s = sa + base[t]
                f = f_ref[g, at_rows((a * TILES + t) * SUB), :]
                out[t] = out[t] + jnp.maximum(s, 0.0) * f
                if with_absorbed:
                    back[t] = back[t] + jnp.maximum(-s, 0.0) * (wa * shape[t])
            return tuple(out), tuple(back)

        zeros = (jnp.zeros((SUB, LANES), F32),) * TILES
        out, back = lax.fori_loop(0, planes, plane, (zeros, zeros), unroll=unroll(planes, 16))
        at = at_rows(g * SUB)
        sums_ref[k, at, :] = (out[0] + out[1]) + (out[2] + out[3])
        if with_absorbed:
            sums_ref[FACES + k, at, :] = (back[0] + back[1]) + (back[2] + back[3])
        return 0

    lax.fori_loop(0, list_faces(links_ref, is_wall, cells, faces), wall, 0)


def sums_kernel(links_ref, geo_ref, f_ref, sums_out, parts_ref, face_ref, cells, faces):
    planes = f_ref.shape[1] // CHUNKS
    y = polynomial_sums(f_ref, planes, parts_ref)
    packed = pack_sums(finish_polynomials(y, geo_ref[FIRST], planes), 0)
    wall_sums(f_ref, planes, links_ref, geo_ref, face_ref, cells, faces, False)
    sums_out[...] = packed + pack_sums([over_sublanes(face_ref, k) for k in range(FACES)], EMIT)


def first_sums_kernel(links_ref, geo_ref, native_ref, f_ref, sums_out, face_ref, cells, faces):
    rows = f_ref.shape[1]
    planes = rows // CHUNKS

    def group(j, _):
        for g in range(SUB):
            f_ref[g, at_rows(j * SUB), :] = native_ref[pl.ds(j * SUB * SUB + g, SUB, stride=SUB), :]
        return 0

    lax.fori_loop(0, rows // SUB, group, 0, unroll=2)
    y = native_polynomial_sums(native_ref, planes)
    packed = pack_sums(finish_polynomials(y, geo_ref[FIRST], planes), 0)
    wall_sums(f_ref, planes, links_ref, geo_ref, face_ref, cells, faces, True)
    sums_out[...] = packed + pack_sums([over_sublanes(face_ref, k) for k in range(2 * FACES)], EMIT)


def spec(space):
    return pl.BlockSpec(memory_space=space)


def array(*shape):
    return jax.ShapeDtypeStruct(shape, F32)


def params(mib=4):
    return pltpu.CompilerParams(vmem_limit_bytes=mib * 1024 * 1024)


def traffic(rows, profiles):
    size = SUB * rows * LANES
    return pl.CostEstimate(flops=8 * profiles * size, bytes_accessed=4 * profiles * size, transcendentals=0)


def local_sums(links, geo, f):
    return pl.pallas_call(
        sums_kernel,
        in_specs=[spec(pltpu.SMEM), spec(pltpu.VMEM), spec(pltpu.VMEM)],
        out_specs=spec(pltpu.VMEM),
        out_shape=array(SUB, LANES),
        scratch_shapes=[
                pltpu.VMEM((10, SUB * SUB + SPARE, LANES), F32),
            pltpu.VMEM((FACES, SUB * SUB + SPARE, LANES), F32),
            *face_lists(),
        ],
        compiler_params=params(),
        cost_estimate=traffic(f.shape[1], 4),
        name="local_sums",
    )(links, geo, f)


def first_sums(links, geo, native):
    rows = (native.shape[0] - SPARE) // SUB
    return pl.pallas_call(
        first_sums_kernel,
        in_specs=[spec(pltpu.SMEM), spec(pltpu.VMEM), spec(pltpu.VMEM)],
        out_specs=[spec(pltpu.VMEM)] * 2,
        out_shape=[array(SUB, rows, LANES), array(SUB, LANES)],
        scratch_shapes=[
                pltpu.VMEM((2 * FACES, SUB * SUB + SPARE, LANES), F32),
            *face_lists(),
        ],
        compiler_params=params(),
        cost_estimate=traffic(rows, 5),
        name="first_sums",
    )(links, geo, native)


SPLIT_PARTS = 8


def is_odd():
    return lax.rem(lax.axis_index("space"), 2) == 1


def first_rows_kernel(native_hbm, native_ref, far_any, near_any, far_ref, near_ref, sems, far_sems, near_sems):
    rows = native_hbm.shape[0]
    part = rows // SPLIT_PARTS
    copies = [
        pltpu.make_async_copy(
            native_hbm.at[pl.ds(i * part, part)], native_ref.at[pl.ds(i * part, part)], sems.at[i]
        )
        for i in range(SPLIT_PARTS)
    ]
    for c in copies:
        c.start()
    odd = is_odd()
    far = jnp.where(odd, SUB - REACH, 0)
    near = jnp.where(odd, 0, SUB - REACH)
    groups = part // (SUB * SUB)
    out = []

    for i, c in enumerate(copies):
        c.wait()

        def group(j, _):
            for r in range(REACH):
                at = at_rows(j * SUB)
                far_ref[r, at, :] = native_ref[pl.ds(j * SUB * SUB + far + r, SUB, stride=SUB), :]
                near_ref[r, at, :] = native_ref[pl.ds(j * SUB * SUB + near + r, SUB, stride=SUB), :]
            return 0

        lax.fori_loop(i * groups, (i + 1) * groups, group, 0, unroll=unroll(groups, 8))
        at = pl.ds(i * groups * SUB, groups * SUB)
        out.append(pltpu.make_async_copy(far_ref.at[:, at], far_any.at[:, at], far_sems.at[i]))
        out.append(pltpu.make_async_copy(near_ref.at[:, at], near_any.at[:, at], near_sems.at[i]))
        out[-2].start()
        out[-1].start()
    for c in out:
        c.wait()


def first_rows(native):
    rows = native.shape[0] // SUB
    halo = (REACH, rows, LANES)
    return pl.pallas_call(
        first_rows_kernel,
        in_specs=[spec(pltpu.HBM)],
        out_specs=[spec(pltpu.VMEM), spec(pl.ANY), spec(pl.ANY)],
        out_shape=[array(native.shape[0] + SPARE, LANES), array(*halo), array(*halo)],
        scratch_shapes=[pltpu.VMEM(halo, F32)] * 2 + [pltpu.SemaphoreType.DMA((SPLIT_PARTS,))] * 3,
        compiler_params=params(),
        cost_estimate=traffic(rows, 4),
        name="first_rows",
    )(pltpu.with_memory_space_constraint(native, pltpu.HBM))


def pair_weights(links_ref, geo_ref, pairs_ref, cells, faces):
    rows = pairs_ref.shape[1]
    planes = rows // CHUNKS
    first = splat(geo_ref, FIRST, 0)

    def clear(j, _):
        for p in range(pairs_ref.shape[0]):
            pairs_ref[p, at_rows(j * SUB), :] = jnp.zeros((SUB, LANES), F32)
        return 0

    lax.fori_loop(0, rows // SUB, clear, 0, unroll=4)

    def remote(i, _):
        g, k = cells[i], faces[i]
        j = links_ref[k, g]
        edge = g - (SUB - REACH)
        before = g * REACH - g * (g - 1) // 2 + (j + REACH) - g
        after = len(BEFORE_PAIRS) + edge * (edge + 1) // 2 + j - SUB
        at_pair = jnp.where(j < 0, before, after)
        scale = -TIME_STEP / splat(geo_ref, VOL, g)
        v0, v1, v2 = [scale * x for x in face_coefficients(geo_ref, k, g)]
        base = []
        for t in range(TILES):
            xb, xc = tile_nodes(t)
            base.append(v1 * xb + v2 * xc)

        def plane(a, _):
            sa = v0 * (first + a.astype(F32) * H)
            for t in range(TILES):
                at = at_rows((a * TILES + t) * SUB)
                pairs_ref[at_pair, at, :] = pairs_ref[at_pair, at, :] + jnp.maximum(sa + base[t], 0.0)
            return 0

        lax.fori_loop(0, planes, plane, 0, unroll=unroll(planes, 8))
        return 0

    lax.fori_loop(0, list_faces(links_ref, is_remote, cells, faces), remote, 0)


def gather_sums(tile):
    size = lax.axis_size("vel")
    if size not in (2, 4):
        return [lax.psum(tile, "vel")]
    others = [lax.ppermute(tile, "vel", [(i, i ^ s) for i in range(size)]) for s in range(1, size)]
    return [tile, *others]


def doubling_sums(tile):
    size = lax.axis_size("vel")
    if size != 4:
        return gather_sums(tile)
    pair = tile + lax.ppermute(tile, "vel", [(i, i ^ 1) for i in range(size)])
    return [pair, lax.ppermute(pair, "vel", [(i, i ^ 2) for i in range(size)])]


def add_tiles(refs):
    tiles = [r[...] for r in refs]
    while len(tiles) > 1:
        tiles = [tiles[i] + tiles[i + 1] for i in range(0, len(tiles), 2)]
    return tiles[0]


def quantities(tile):
    m = [WEIGHT * column(tile, p) for p in range(13)]
    n = m[0]
    rn = 1.0 / n
    u = [m[1 + i] * rn for i in range(3)]
    uu = u[0] * u[0] + u[1] * u[1] + u[2] * u[2]
    trace = m[4] + m[5] + m[6]
    width = trace - n * uu
    temperature = width * rn * (1.0 / 3.0)
    second = [[m[4], m[7], m[8]], [m[7], m[5], m[9]], [m[8], m[9], m[6]]]
    q = []
    for i in range(3):
        across = u[0] * second[i][0] + u[1] * second[i][1] + u[2] * second[i][2]
        q.append(0.5 * (m[10 + i] - 2.0 * across - u[i] * trace + 2.0 * uu * m[1 + i]))
    return n, u, temperature, q


def macro_kernel(*refs):
    out_ref = refs[-1]
    n, u, temperature, q = quantities(add_tiles(refs[:-1]))
    lane, sub = lane_iota(), sub_iota()
    for i, x in enumerate((n, *u, temperature, *q)):
        row = jnp.sum(jnp.where(lane == sub, x, 0.0), axis=0, keepdims=True)
        out_ref[pl.ds(i, 1), :] = row[:, :SUB]


def macro(tiles):
    return pl.pallas_call(
        macro_kernel,
        in_specs=[spec(pltpu.VMEM)] * len(tiles),
        out_specs=spec(pltpu.VMEM),
        out_shape=array(8, SUB),
        compiler_params=params(1),
        name="macro",
    )(*tiles)


def flux_kernel(with_pairs, links_ref, geo_ref, f_ref, out_ref, *refs):
    if with_pairs:
        pairs_ref, cells, faces = refs[0], refs[-2], refs[-1]
        pair_weights(links_ref, geo_ref, pairs_ref, cells, faces)
        refs = refs[1:-2]
    coef, bases, stays, source, face = refs
    planes = f_ref.shape[1] // CHUNKS
    scale = -TIME_STEP / geo_ref[VOL]
    for i in range(3):
        whole = None
        for k in range(FACES):
            x = scale * geo_ref[FV + FACES * i + k]
            coef[FACES * i + k] = x
            whole = x if whole is None else whole + x
        coef[3 * FACES + i] = whole

    def table(g, _):
        w = [[splat(coef, FACES * i + k, g) for i in (1, 2)] for k in range(FACES)]
        whole = [splat(coef, 3 * FACES + i, g) for i in (1, 2)]
        for t in range(TILES):
            xb, xc = tile_nodes(t)
            for k in range(FACES):
                bases[k, g * TILES + t] = w[k][0] * xb + w[k][1] * xc
            stays[g * TILES + t] = 1.0 + whole[0] * xb + whole[1] * xc
        return 0

    lax.fori_loop(0, SUB, table, 0, unroll=2)

    def cell(g, _):
        count = 0
        for k in range(FACES):
            j = links_ref[k, g]
            source[count] = j
            face[count] = k
            count = count + jnp.logical_and(j >= 0, j < SUB).astype(jnp.int32)
        for n in range(FACES + 1):

            @pl.when(count == n)
            def _():
                own_faces(g, n)

        return 0

    def own_faces(g, n):
        at_source = [source[i] for i in range(n)]
        first_weight = [splat(coef, face[k], g) for k in range(n)]
        whole = splat(coef, 3 * FACES, g)
        x0 = splat(geo_ref, FIRST, g)
        base = [[bases[face[k], g * TILES + t] for k in range(n)] for t in range(TILES)]
        stay = [stays[g * TILES + t] for t in range(TILES)]

        def plane(a, _):
            xa = x0 + a.astype(F32) * H
            sa = [w * xa for w in first_weight]
            stay_a = whole * xa
            for t in range(TILES):
                at = at_rows((a * TILES + t) * SUB)
                f = f_ref[g, at, :]
                acc = f * (stay_a + stay[t])
                for k in range(n):
                    acc = acc + jnp.maximum(sa[k] + base[t][k], 0.0) * (f_ref[at_source[k], at, :] - f)
                out_ref[g, at, :] = acc
            return 0

        lax.fori_loop(0, planes, plane, 0, unroll=unroll(planes, 8))

    lax.fori_loop(0, SUB, cell, 0)


def flux(with_pairs, links, geo, f):
    rows = f.shape[1]
    pairs = 2 * len(BEFORE_PAIRS)
    return pl.pallas_call(
        functools.partial(flux_kernel, with_pairs),
        in_specs=[spec(pltpu.SMEM), spec(pltpu.VMEM), spec(pltpu.VMEM)],
        out_specs=[spec(pltpu.VMEM)] * (2 if with_pairs else 1),
        out_shape=[array(*f.shape)] + ([array(pairs, rows, LANES)] if with_pairs else []),
        scratch_shapes=[
            pltpu.VMEM((3 * FACES + 3, SUB, LANES), F32),
            pltpu.VMEM((FACES, SUB * TILES, SUB, LANES), F32),
            pltpu.VMEM((SUB * TILES, SUB, LANES), F32),
            pltpu.SMEM((FACES + 1,), jnp.int32),
            pltpu.SMEM((FACES + 1,), jnp.int32),
        ]
        + (face_lists() if with_pairs else []),
        compiler_params=params(),
        cost_estimate=traffic(rows, 9 if with_pairs else 7),
        name="flux",
    )(links, geo, f)


def target_kernel(count, links_ref, geo_ref, absorbed_in, *refs):
    sums_refs, (f_ref, part_ref, out_ref, *sum_out, tiles_ref, coef, cells, faces) = refs[:count], refs[count:]
    planes = f_ref.shape[1] // CHUNKS
    sums = add_tiles(sums_refs)
    for ref in sum_out:
        ref[...] = sums
    absorbed = sums if absorbed_in is None else absorbed_in[...]
    n, u, temperature, q = quantities(sums)
    rt = 1.0 / temperature
    rate = TIME_STEP * n * temperature / (SHEAR * jnp.exp(POWER * jnp.log(temperature)))
    height = rate * n * rt * jnp.sqrt(rt)
    slope = (1.0 / 3.0) / (5.0 * n * temperature * temperature)
    coef[0] = rate
    coef[1] = rt
    coef[2], coef[3] = u[1], u[2]
    coef[4], coef[5] = slope * q[1], slope * q[2]
    coef[6], coef[7], coef[8] = u[0], slope * q[0], height
    for k in range(FACES):
        wall = geo_ref[WALL + k] > 0.5
        coef[9 + k] = column(sums, EMIT + k) / jnp.where(wall, column(absorbed, ABSORB + k), 1.0)

    def tile_table(g, _):
        rtg = splat(coef, 1, g)
        ub, uc = splat(coef, 2, g), splat(coef, 3, g)
        qb, qc = splat(coef, 4, g), splat(coef, 5, g)
        shape = wall_tiles(splat(geo_ref, WT, g))
        for t in range(TILES):
            xb, xc = tile_nodes(t)
            cb, cc = xb - ub, xc - uc
            z = (cb * cb + cc * cc) * rtg
            at = g * TILES + t
            tiles_ref[0, at] = jnp.exp(-0.5 * z)
            tiles_ref[1, at] = cb * qb + cc * qc
            tiles_ref[2, at] = z
            tiles_ref[3, at] = shape[t]
        return 0

    lax.fori_loop(0, SUB, tile_table, 0, unroll=4)

    def cell(g, _):
        rate_g, rtg, u0, q0, height_g = [splat(coef, i, g) for i in (0, 1, 6, 7, 8)]
        x0 = splat(geo_ref, FIRST, g) - u0
        bell, heat, zz = [[tiles_ref[i, g * TILES + t] for t in range(TILES)] for i in range(3)]

        def plane(a, _):
            ca = x0 + a.astype(F32) * H
            za = ca * ca * rtg
            height_a = height_g * jnp.exp(-0.5 * za)
            heat_a = q0 * ca
            z_a = za - 5.0
            for t in range(TILES):
                where = (g, at_rows((a * TILES + t) * SUB), slice(None))
                f = f_ref[where]
                target = (height_a * bell[t]) * (1.0 + (heat_a + heat[t]) * (z_a + zz[t]))
                out_ref[where] = (part_ref[where] - rate_g * f) + target
            return 0

        lax.fori_loop(0, planes, plane, 0, unroll=unroll(planes, 16))
        return 0

    lax.fori_loop(0, SUB, cell, 0)

    def wall(i, _):
        g, k = cells[i], faces[i]
        x0 = splat(geo_ref, FIRST, g)
        ratio = splat(coef, 9 + k, g)
        scale = -TIME_STEP / splat(geo_ref, VOL, g)
        v0, v1, v2 = [scale * x for x in face_coefficients(geo_ref, k, g)]
        base, shape = [], []
        for t in range(TILES):
            xb, xc = tile_nodes(t)
            base.append(v1 * xb + v2 * xc)
            shape.append(ratio * tiles_ref[3, g * TILES + t])

        rt_wall = -0.5 / splat(geo_ref, WT, g)

        def plane(a, _):
            xa = x0 + a.astype(F32) * H
            wa = jnp.exp(xa * xa * rt_wall)
            sa = v0 * xa
            for t in range(TILES):
                where = (g, at_rows((a * TILES + t) * SUB), slice(None))
                f = f_ref[where]
                out_ref[where] = out_ref[where] + jnp.maximum(sa + base[t], 0.0) * (wa * shape[t] - f)
            return 0

        lax.fori_loop(0, planes, plane, 0, unroll=unroll(planes, 16))
        return 0

    lax.fori_loop(0, list_faces(links_ref, is_wall, cells, faces), wall, 0)


def add_target(links, geo, absorbed, tiles, f, part):
    rows = f.shape[1]
    vmem = spec(pltpu.VMEM)
    given = [links, geo] + ([] if absorbed is None else [absorbed]) + list(tiles) + [f, part]

    def kernel(links_ref, geo_in, *refs):
        if absorbed is None:
            target_kernel(len(tiles), links_ref, geo_in, None, *refs)
        else:
            target_kernel(len(tiles), links_ref, geo_in, *refs)

    return pl.pallas_call(
        kernel,
        in_specs=[spec(pltpu.SMEM)] + [vmem] * (len(given) - 1),
        out_specs=[vmem] * (2 if absorbed is None else 1),
        out_shape=[array(*part.shape)] + ([array(SUB, LANES)] if absorbed is None else []),
        input_output_aliases={len(given) - 1: 0},
        scratch_shapes=[
                pltpu.VMEM((4, SUB * TILES, SUB, LANES), F32),
            pltpu.VMEM((9 + FACES, SUB, LANES), F32),
            *face_lists(),
        ],
        compiler_params=params(),
        cost_estimate=traffic(rows, 7),
        name="add_target",
    )(*given)


def side_terms(high, pairs_ref, halo_ref, f_ref, at):
    terms = [None] * REACH
    rows = [halo_ref[r, at, :] for r in range(REACH)]
    first = SUB - REACH if high else 0
    own = [f_ref[first + e, at, :] for e in range(REACH)]
    count = len(BEFORE_PAIRS)
    pairs = [(e, r) for e in range(REACH) for r in range(e + 1)] if high else BEFORE_PAIRS
    for p, (e, r) in enumerate(pairs):
        term = pairs_ref[p + count if high else p, at, :] * (rows[r] - own[e])
        terms[e] = term if terms[e] is None else terms[e] + term
    return first, terms


def for_side(far, run):
    odd = is_odd()

    @pl.when(odd)
    def _():
        run(far)

    @pl.when(jnp.logical_not(odd))
    def _():
        run(not far)


def add_side(far, pairs_ref, halo_ref, old_ref, part_ref, f_ref, rows_ref, ready=None):
    def run(high):
        def group(j, _):
            at = at_rows(j * SUB)
            first, terms = side_terms(high, pairs_ref, halo_ref, old_ref, at)
            for e in range(REACH):
                x = part_ref[first + e, at, :] + terms[e]
                f_ref[first + e, at, :] = x
                if rows_ref is not None:
                    rows_ref[e, at, :] = x
            return 0

        groups = part_ref.shape[1] // SUB
        parts = 1 if ready is None else EDGE_PARTS
        for i in range(parts):
            if ready is not None:
                ready(i)
            count = groups // parts
            lax.fori_loop(i * count, (i + 1) * count, group, 0, unroll=unroll(count, 8))

    for_side(far, run)


EDGE_PARTS = 4


def near_edge_kernel(pairs_ref, halo_any, old_ref, part_ref, f_ref, rows_ref, halo_ref, sems):
    size = halo_ref.shape[1] // EDGE_PARTS

    def copy(i):
        at = pl.ds(i * size, size)
        return pltpu.make_async_copy(halo_any.at[:, at], halo_ref.at[:, at], sems.at[i])

    for i in range(EDGE_PARTS):
        copy(i).start()
    add_side(False, pairs_ref, halo_ref, old_ref, part_ref, f_ref, rows_ref, lambda i: copy(i).wait())


def edge(far, pairs, halo, old, part):
    rows = part.shape[1]
    return pl.pallas_call(
        functools.partial(add_side, True) if far else near_edge_kernel,
        in_specs=[spec(pltpu.VMEM), spec(pltpu.VMEM if far else pl.ANY), spec(pltpu.VMEM), spec(pltpu.VMEM)],
        out_specs=[spec(pltpu.VMEM)] * 2,
        out_shape=[array(SUB, rows, LANES), array(REACH, rows, LANES)],
        input_output_aliases={3: 0},
        scratch_shapes=[] if far else [pltpu.VMEM(halo.shape, F32), pltpu.SemaphoreType.DMA((EDGE_PARTS,))],
        compiler_params=params(),
        cost_estimate=traffic(rows, 2),
        name="far_edge" if far else "near_edge",
    )(pairs, halo, old, part)


def last_near_kernel(geo_ref, pairs_ref, halo_ref, old_ref, part_ref, f_ref, sums_out, parts_ref):
    add_side(False, pairs_ref, halo_ref, old_ref, part_ref, f_ref, None)
    planes = f_ref.shape[1] // CHUNKS
    y = polynomial_sums(f_ref, planes, parts_ref)
    sums_out[...] = pack_sums(finish_polynomials(y, geo_ref[FIRST], planes), 0)


def last_near(geo, pairs, near, old, part):
    rows = part.shape[1]
    return pl.pallas_call(
        last_near_kernel,
        in_specs=[spec(pltpu.VMEM)] * 5,
        out_specs=[spec(pltpu.VMEM)] * 2,
        out_shape=[array(SUB, rows, LANES), array(SUB, LANES)],
        input_output_aliases={4: 0},
        scratch_shapes=[pltpu.VMEM((10, SUB * SUB + SPARE, LANES), F32)],
        compiler_params=params(),
        cost_estimate=traffic(rows, 3),
        name="last_near",
    )(geo, pairs, near, old, part)


def last_far_kernel(geo_ref, pairs_ref, halo_ref, old_ref, sums_in, terms_ref, sums_out, parts_ref):
    rows = old_ref.shape[1]
    planes = rows // CHUNKS
    parts_ref[...] = jnp.zeros_like(parts_ref)

    def run(high):
        def group(j, _):
            at = at_rows(j * SUB)
            _first, terms = side_terms(high, pairs_ref, halo_ref, old_ref, at)
            for e in range(REACH):
                terms_ref[e, at, :] = terms[e]
            return 0

        lax.fori_loop(0, rows // SUB, group, 0, unroll=unroll(rows // SUB, 8))
        y = polynomial_sums(terms_ref, planes, parts_ref, SUB - REACH if high else 0)
        sums_out[...] = sums_in[...] + pack_sums(finish_polynomials(y, geo_ref[FIRST], planes), 0)

    for_side(True, run)


def last_far(geo, pairs, far, old, sums):
    rows = old.shape[1]
    return pl.pallas_call(
        last_far_kernel,
        in_specs=[spec(pltpu.VMEM)] * 5,
        out_specs=[spec(pltpu.VMEM)] * 2,
        out_shape=[array(REACH, rows, LANES), array(SUB, LANES)],
        scratch_shapes=[pltpu.VMEM((10, SUB * SUB + SPARE, LANES), F32)],
        compiler_params=params(),
        cost_estimate=traffic(rows, 2),
        name="last_far",
    )(geo, pairs, far, old, sums)


LAST_PARTS = 4


def result_kernel(part_ref, terms_ref, out_hbm, native_ref, sems):
    part = part_ref.shape[1] // SUB // LAST_PARTS

    def copy(i):
        at = pl.ds(i * part * SUB * SUB, part * SUB * SUB)
        return pltpu.make_async_copy(native_ref.at[at], out_hbm.at[at], sems.at[i])

    def run(high):
        first = SUB - REACH if high else 0
        for i in range(LAST_PARTS):

            def group(j, _):
                at = at_rows(j * SUB)
                for g in range(SUB):
                    x = part_ref[g, at, :]
                    if 0 <= g - first < REACH:
                        x = x + terms_ref[g - first, at, :]
                    native_ref[pl.ds(j * SUB * SUB + g, SUB, stride=SUB), :] = x
                return 0

            lax.fori_loop(i * part, (i + 1) * part, group, 0, unroll=unroll(part, 4))
            copy(i).start()

    for_side(True, run)
    for i in range(LAST_PARTS):
        copy(i).wait()


def result(part, terms):
    rows = part.shape[1]
    native = (SUB * rows, LANES)
    return pl.pallas_call(
        result_kernel,
        in_specs=[spec(pltpu.VMEM)] * 2,
        out_specs=spec(pltpu.HBM),
        out_shape=array(*native),
        scratch_shapes=[pltpu.VMEM((SUB * rows + SPARE, LANES), F32), pltpu.SemaphoreType.DMA((LAST_PARTS,))],
        compiler_params=params(),
        cost_estimate=traffic(rows, 3),
        name="result",
    )(part, terms)


def swap(rows, start):
    pairs = [(i, i + 1) for i in range(start, lax.axis_size("space") - 1, 2)]
    return lax.ppermute(rows, "space", pairs + [(j, i) for i, j in pairs])


def per_device(particle_profile, neighbors, face_vectors, volumes, wall_temp):
    cells, points = particle_profile.shape
    rows = points // LANES
    plane_count = NV // lax.axis_size("vel")
    native = particle_profile.reshape(cells, rows, LANES).transpose(1, 0, 2).reshape(cells * rows, LANES)
    wall = neighbors < 0
    links = jnp.where(wall, WALL_LINK, neighbors - lax.axis_index("space") * cells)
    own = (links >= 0) & (links < cells)
    first = -SPEED_LIMIT + ((lax.axis_index("vel") * plane_count).astype(F32) + 0.5) * H
    geo = jnp.concatenate(
        [
            face_vectors.reshape(3 * FACES, cells),
            volumes[None],
            wall_temp[None],
            wall.astype(F32),
            own.astype(F32),
            jnp.full((1, cells), first, F32),
        ]
    )
    geo = jnp.broadcast_to(geo[:, :, None], (GEO, cells, LANES))
    native, far, near = first_rows(native)
    far, near = swap(far, 1), swap(near, 0)
    f, sums = first_sums(links, geo, native)
    tiles = gather_sums(sums)
    part, pairs = flux(True, links, geo, f)
    part, absorbed = add_target(links, geo, None, tiles, f, part)
    part, near = edge(False, pairs, near, f, part)
    near = swap(near, 0)
    f, far = edge(True, pairs, far, f, part)
    far = swap(far, 1)
    tiles = gather_sums(local_sums(links, geo, f))
    (part,) = flux(False, links, geo, f)
    (part,) = add_target(links, geo, absorbed, tiles, f, part)
    part, sums = last_near(geo, pairs, near, f, part)
    terms, sums = last_far(geo, pairs, far, f, sums)
    tiles = doubling_sums(sums)
    native = result(part, terms)
    macro_quantities = macro(tiles)
    evolved = native.reshape(rows, cells, LANES).transpose(1, 0, 2).reshape(cells, points)
    return evolved, macro_quantities


def solution(mesh):
    return jax.shard_map(
        per_device,
        mesh=mesh,
        in_specs=(
            P("space", "vel"),
            P(None, "space"),
            P(None, None, "space"),
            P("space"),
            P("space"),
        ),
        out_specs=(P("space", "vel"), P(None, "space")),
        check_vma=False,
    )
```

```python
import functools
import math

import jax
import jax.numpy as jnp
from jax import lax
from jax.experimental import pallas as pl
from jax.experimental.pallas import tpu as pltpu
from jax.sharding import PartitionSpec as P

NV = 64
FACES = 6
REACH = 3
STEPS = 2
LANES = 128
SUB = 8
SPARE = SUB

TIME_STEP = 0.015
SHEAR = 0.1
POWER = 0.81
SPEED_LIMIT = 6.0
H = 2.0 * SPEED_LIMIT / NV
WEIGHT = H**3 * (2.0 * math.pi) ** (-1.5)

CHUNKS = NV * NV // LANES
TILES = CHUNKS // SUB

FV, VOL, WT, WALL, LOCAL, FIRST = 0, 18, 19, 20, 26, 32
GEO = 33
WALL_LINK = -64
BEFORE_PAIRS = tuple((g, r) for g in range(REACH) for r in range(g, REACH))
EMIT, ABSORB = 13, 19
SUMS = 25

F32 = jnp.float32


def lane_iota():
    return lax.broadcasted_iota(jnp.int32, (SUB, LANES), 1)


def sub_iota():
    return lax.broadcasted_iota(jnp.int32, (SUB, LANES), 0)


def half_of(lane):
    return (lane >= NV).astype(F32)


def third_component(lane):
    c = jnp.where(lane >= NV, lane - NV, lane).astype(F32)
    return -SPEED_LIMIT + (c + 0.5) * H


def tile_nodes(t):
    lane = lane_iota()
    b = (2 * SUB * t + 2 * sub_iota()).astype(F32) + half_of(lane)
    return -SPEED_LIMIT + (b + 0.5) * H, third_component(lane)


def column(tile, p):
    return jnp.broadcast_to(tile[:, p : p + 1], (SUB, LANES))


def splat(ref, i, g):
    return jnp.broadcast_to(ref[i, pl.ds(g, 1), :], (SUB, LANES))


def total(tile):
    return jnp.broadcast_to(jnp.sum(tile, axis=1, keepdims=True), (SUB, LANES))


def face_coefficients(geo_ref, k, g):
    return [splat(geo_ref, FV + FACES * i + k, g) for i in range(3)]


def at_rows(start, size=SUB):
    return pl.ds(pl.multiple_of(start, SUB), size)


def wall_tiles(wall_temp):
    rt = 1.0 / wall_temp
    scale = rt * jnp.sqrt(rt)
    out = []
    for t in range(TILES):
        xb, xc = tile_nodes(t)
        out.append(scale * jnp.exp(-0.5 * (xb * xb + xc * xc) * rt))
    return out


def pack_sums(arrays, start):
    lane = lane_iota()
    out = jnp.zeros((SUB, LANES), F32)
    for p, x in enumerate(arrays):
        out = jnp.where(lane == start + p, total(x), out)
    return out


def over_sublanes(ref, k):
    out = ref[k, pl.ds(0, SUB, stride=SUB), :]
    for s in range(1, SUB):
        out = out + ref[k, pl.ds(s, SUB, stride=SUB), :]
    return out


def list_faces(links_ref, wanted, cell_ref, face_ref):
    count = 0
    for g in range(SUB):
        for k in range(FACES):
            cell_ref[count] = g
            face_ref[count] = k
            count = count + wanted(links_ref[k, g]).astype(jnp.int32)
    return count


def is_wall(j):
    return j == WALL_LINK


def is_remote(j):
    return jnp.logical_or(j >= SUB, jnp.logical_and(j < 0, j != WALL_LINK))


def face_lists():
    return [pltpu.SMEM((FACES * SUB + 1,), jnp.int32)] * 2


def unroll(planes, most):
    return math.gcd(planes, most)


def finish_polynomials(y, first, planes):
    y0, y1, y2, y3, by0, by1, by2, bby0, bby1, bbby0 = y
    m = first + 0.5 * (planes - 1) * H
    c = third_component(lane_iota())
    cc = c * c
    a = y1 + m * y0
    aa = y2 + m * (2.0 * y1 + m * y0)
    aaa = y3 + m * (3.0 * y2 + m * (3.0 * y1 + m * y0))
    ab = by1 + m * by0
    aab = by2 + m * (2.0 * by1 + m * by0)
    abb = bby1 + m * bby0
    return (
        y0,
        a,
        by0,
        c * y0,
        aa,
        bby0,
        cc * y0,
        ab,
        c * a,
        c * by0,
        aaa + abb + cc * a,
        aab + bbby0 + cc * by0,
        c * (aa + bby0 + cc * y0),
    )


def polynomial_sums(f_ref, planes, parts_ref, first=0):
    half = planes // 2

    def cell(g, _):
        out = [None] * 10
        for t in range(TILES):
            y0 = y1 = y2 = y3 = None
            for i in range(half):
                d = (i + 0.5) * H
                hi = f_ref[g, pl.ds(((half + i) * TILES + t) * SUB, SUB), :]
                lo = f_ref[g, pl.ds(((half - 1 - i) * TILES + t) * SUB, SUB), :]
                s, r = hi + lo, hi - lo
                if i == 0:
                    y0, y1, y2, y3 = s, d * r, (d * d) * s, (d * d * d) * r
                else:
                    y0, y1, y2, y3 = y0 + s, y1 + d * r, y2 + (d * d) * s, y3 + (d * d * d) * r
            b, _c = tile_nodes(t)
            bb = b * b
            terms = (y0, y1, y2, y3, b * y0, b * y1, b * y2, bb * y0, bb * y1, bb * (b * y0))
            out = [x if o is None else o + x for o, x in zip(out, terms)]
        for p in range(10):
            parts_ref[p, at_rows((first + g) * SUB), :] = out[p]
        return 0

    lax.fori_loop(0, f_ref.shape[0], cell, 0)
    return [over_sublanes(parts_ref, p) for p in range(10)]


def native_polynomial_sums(native_ref, planes):
    half, side = planes // 2, CHUNKS // 2
    zero = jnp.zeros((SUB, LANES), F32)
    acc = [zero] * 10

    def plane(a, acc):
        xa = (a.astype(F32) - 0.5 * (planes - 1)) * H
        b0 = b1 = b2 = b3 = None
        for i in range(side):
            y = (2 * i + 1) * H
            hi = native_ref[at_rows((a * CHUNKS + side + i) * SUB), :]
            lo = native_ref[at_rows((a * CHUNKS + side - 1 - i) * SUB), :]
            s, d = hi + lo, hi - lo
            terms = (s, y * d, (y * y) * s, (y * y * y) * d)
            if i == 0:
                b0, b1, b2, b3 = terms
            else:
                b0, b1, b2, b3 = b0 + terms[0], b1 + terms[1], b2 + terms[2], b3 + terms[3]
        a0, a1, a2 = xa * b0, xa * b1, xa * b2
        aa0 = xa * a0
        new = (b0, a0, aa0, xa * aa0, b1, a1, xa * a1, b2, a2, b3)
        return tuple(x + z for x, z in zip(acc, new))

    g0, a0, aa0, aaa0, g1, a1, aa1, g2, a2, g3 = lax.fori_loop(0, planes, plane, tuple(acc))
    e = (half_of(lane_iota()) - 0.5) * H
    return [
        g0,
        a0,
        aa0,
        aaa0,
        g1 + e * g0,
        a1 + e * a0,
        aa1 + e * aa0,
        g2 + e * (2.0 * g1 + e * g0),
        a2 + e * (2.0 * a1 + e * a0),
        g3 + e * (3.0 * g2 + e * (3.0 * g1 + e * g0)),
    ]


def wall_sums(f_ref, planes, links_ref, geo_ref, sums_ref, cells, faces, with_absorbed):
    sums_ref[...] = jnp.zeros_like(sums_ref)

    def wall(i, _):
        g, k = cells[i], faces[i]
        v0, v1, v2 = face_coefficients(geo_ref, k, g)
        first = splat(geo_ref, FIRST, g)
        base = []
        for t in range(TILES):
            xb, xc = tile_nodes(t)
            base.append(v1 * xb + v2 * xc)
        if with_absorbed:
            wt = splat(geo_ref, WT, g)
            shape = wall_tiles(wt)

        def plane(a, acc):
            out, back = list(acc[0]), list(acc[1])
            xa = first + a.astype(F32) * H
            sa = v0 * xa
            if with_absorbed:
                wa = jnp.exp(-0.5 * xa * xa / wt)
            for t in range(TILES):
                s = sa + base[t]
                f = f_ref[g, at_rows((a * TILES + t) * SUB), :]
                out[t] = out[t] + jnp.maximum(s, 0.0) * f
                if with_absorbed:
                    back[t] = back[t] + jnp.maximum(-s, 0.0) * (wa * shape[t])
            return tuple(out), tuple(back)

        zeros = (jnp.zeros((SUB, LANES), F32),) * TILES
        out, back = lax.fori_loop(0, planes, plane, (zeros, zeros), unroll=unroll(planes, 16))
        at = at_rows(g * SUB)
        sums_ref[k, at, :] = (out[0] + out[1]) + (out[2] + out[3])
        if with_absorbed:
            sums_ref[FACES + k, at, :] = (back[0] + back[1]) + (back[2] + back[3])
        return 0

    lax.fori_loop(0, list_faces(links_ref, is_wall, cells, faces), wall, 0)


def sums_kernel(links_ref, geo_ref, f_ref, sums_out, parts_ref, face_ref, cells, faces):
    planes = f_ref.shape[1] // CHUNKS
    y = polynomial_sums(f_ref, planes, parts_ref)
    packed = pack_sums(finish_polynomials(y, geo_ref[FIRST], planes), 0)
    wall_sums(f_ref, planes, links_ref, geo_ref, face_ref, cells, faces, False)
    sums_out[...] = packed + pack_sums([over_sublanes(face_ref, k) for k in range(FACES)], EMIT)


def first_sums_kernel(links_ref, geo_ref, native_ref, f_ref, sums_out, face_ref, cells, faces):
    rows = f_ref.shape[1]
    planes = rows // CHUNKS

    def group(j, _):
        for g in range(SUB):
            f_ref[g, at_rows(j * SUB), :] = native_ref[pl.ds(j * SUB * SUB + g, SUB, stride=SUB), :]
        return 0

    lax.fori_loop(0, rows // SUB, group, 0, unroll=2)
    y = native_polynomial_sums(native_ref, planes)
    packed = pack_sums(finish_polynomials(y, geo_ref[FIRST], planes), 0)
    wall_sums(f_ref, planes, links_ref, geo_ref, face_ref, cells, faces, True)
    sums_out[...] = packed + pack_sums([over_sublanes(face_ref, k) for k in range(2 * FACES)], EMIT)


def spec(space):
    return pl.BlockSpec(memory_space=space)


def array(*shape):
    return jax.ShapeDtypeStruct(shape, F32)


def params(mib=4):
    return pltpu.CompilerParams(vmem_limit_bytes=mib * 1024 * 1024)


def traffic(rows, profiles):
    size = SUB * rows * LANES
    return pl.CostEstimate(flops=8 * profiles * size, bytes_accessed=4 * profiles * size, transcendentals=0)


def local_sums(links, geo, f):
    return pl.pallas_call(
        sums_kernel,
        in_specs=[spec(pltpu.SMEM), spec(pltpu.VMEM), spec(pltpu.VMEM)],
        out_specs=spec(pltpu.VMEM),
        out_shape=array(SUB, LANES),
        scratch_shapes=[
                pltpu.VMEM((10, SUB * SUB + SPARE, LANES), F32),
            pltpu.VMEM((FACES, SUB * SUB + SPARE, LANES), F32),
            *face_lists(),
        ],
        compiler_params=params(),
        cost_estimate=traffic(f.shape[1], 4),
        name="local_sums",
    )(links, geo, f)


def first_sums(links, geo, native):
    rows = (native.shape[0] - SPARE) // SUB
    return pl.pallas_call(
        first_sums_kernel,
        in_specs=[spec(pltpu.SMEM), spec(pltpu.VMEM), spec(pltpu.VMEM)],
        out_specs=[spec(pltpu.VMEM)] * 2,
        out_shape=[array(SUB, rows, LANES), array(SUB, LANES)],
        scratch_shapes=[
                pltpu.VMEM((2 * FACES, SUB * SUB + SPARE, LANES), F32),
            *face_lists(),
        ],
        compiler_params=params(),
        cost_estimate=traffic(rows, 5),
        name="first_sums",
    )(links, geo, native)


SPLIT_PARTS = 8


def is_odd():
    return lax.rem(lax.axis_index("space"), 2) == 1


def first_rows_kernel(native_hbm, native_ref, far_any, near_any, far_ref, near_ref, sems, far_sems, near_sems):
    rows = native_hbm.shape[0]
    part = rows // SPLIT_PARTS
    copies = [
        pltpu.make_async_copy(
            native_hbm.at[pl.ds(i * part, part)], native_ref.at[pl.ds(i * part, part)], sems.at[i]
        )
        for i in range(SPLIT_PARTS)
    ]
    for i, c in enumerate(copies):
        c.start(priority=i % 2)
    odd = is_odd()
    far = jnp.where(odd, SUB - REACH, 0)
    near = jnp.where(odd, 0, SUB - REACH)
    groups = part // (SUB * SUB)
    out = []

    for i, c in enumerate(copies):
        c.wait()

        def group(j, _):
            for r in range(REACH):
                at = at_rows(j * SUB)
                far_ref[r, at, :] = native_ref[pl.ds(j * SUB * SUB + far + r, SUB, stride=SUB), :]
                near_ref[r, at, :] = native_ref[pl.ds(j * SUB * SUB + near + r, SUB, stride=SUB), :]
            return 0

        lax.fori_loop(i * groups, (i + 1) * groups, group, 0, unroll=unroll(groups, 8))
        at = pl.ds(i * groups * SUB, groups * SUB)
        out.append(pltpu.make_async_copy(far_ref.at[:, at], far_any.at[:, at], far_sems.at[i]))
        out.append(pltpu.make_async_copy(near_ref.at[:, at], near_any.at[:, at], near_sems.at[i]))
        out[-2].start()
        out[-1].start()
    for c in out:
        c.wait()


def first_rows(native):
    rows = native.shape[0] // SUB
    halo = (REACH, rows, LANES)
    return pl.pallas_call(
        first_rows_kernel,
        in_specs=[spec(pltpu.HBM)],
        out_specs=[spec(pltpu.VMEM), spec(pl.ANY), spec(pl.ANY)],
        out_shape=[array(native.shape[0] + SPARE, LANES), array(*halo), array(*halo)],
        scratch_shapes=[pltpu.VMEM(halo, F32)] * 2 + [pltpu.SemaphoreType.DMA((SPLIT_PARTS,))] * 3,
        compiler_params=params(),
        cost_estimate=traffic(rows, 4),
        name="first_rows",
    )(pltpu.with_memory_space_constraint(native, pltpu.HBM))


def pair_weights(links_ref, geo_ref, pairs_ref, cells, faces):
    rows = pairs_ref.shape[1]
    planes = rows // CHUNKS
    first = splat(geo_ref, FIRST, 0)

    def clear(j, _):
        for p in range(pairs_ref.shape[0]):
            pairs_ref[p, at_rows(j * SUB), :] = jnp.zeros((SUB, LANES), F32)
        return 0

    lax.fori_loop(0, rows // SUB, clear, 0, unroll=4)

    def remote(i, _):
        g, k = cells[i], faces[i]
        j = links_ref[k, g]
        edge = g - (SUB - REACH)
        before = g * REACH - g * (g - 1) // 2 + (j + REACH) - g
        after = len(BEFORE_PAIRS) + edge * (edge + 1) // 2 + j - SUB
        at_pair = jnp.where(j < 0, before, after)
        scale = -TIME_STEP / splat(geo_ref, VOL, g)
        v0, v1, v2 = [scale * x for x in face_coefficients(geo_ref, k, g)]
        base = []
        for t in range(TILES):
            xb, xc = tile_nodes(t)
            base.append(v1 * xb + v2 * xc)

        def plane(a, _):
            sa = v0 * (first + a.astype(F32) * H)
            for t in range(TILES):
                at = at_rows((a * TILES + t) * SUB)
                pairs_ref[at_pair, at, :] = pairs_ref[at_pair, at, :] + jnp.maximum(sa + base[t], 0.0)
            return 0

        lax.fori_loop(0, planes, plane, 0, unroll=unroll(planes, 8))
        return 0

    lax.fori_loop(0, list_faces(links_ref, is_remote, cells, faces), remote, 0)


def gather_sums(tile):
    size = lax.axis_size("vel")
    if size not in (2, 4):
        return [lax.psum(tile, "vel")]
    others = [lax.ppermute(tile, "vel", [(i, i ^ s) for i in range(size)]) for s in range(1, size)]
    return [tile, *others]


def doubling_sums(tile):
    size = lax.axis_size("vel")
    if size != 4:
        return gather_sums(tile)
    pair = tile + lax.ppermute(tile, "vel", [(i, i ^ 1) for i in range(size)])
    return [pair, lax.ppermute(pair, "vel", [(i, i ^ 2) for i in range(size)])]


def add_tiles(refs):
    tiles = [r[...] for r in refs]
    while len(tiles) > 1:
        tiles = [tiles[i] + tiles[i + 1] for i in range(0, len(tiles), 2)]
    return tiles[0]


def quantities(tile):
    m = [WEIGHT * column(tile, p) for p in range(13)]
    n = m[0]
    rn = 1.0 / n
    u = [m[1 + i] * rn for i in range(3)]
    uu = u[0] * u[0] + u[1] * u[1] + u[2] * u[2]
    trace = m[4] + m[5] + m[6]
    width = trace - n * uu
    temperature = width * rn * (1.0 / 3.0)
    second = [[m[4], m[7], m[8]], [m[7], m[5], m[9]], [m[8], m[9], m[6]]]
    q = []
    for i in range(3):
        across = u[0] * second[i][0] + u[1] * second[i][1] + u[2] * second[i][2]
        q.append(0.5 * (m[10 + i] - 2.0 * across - u[i] * trace + 2.0 * uu * m[1 + i]))
    return n, u, temperature, q


def macro_kernel(*refs):
    out_ref = refs[-1]
    n, u, temperature, q = quantities(add_tiles(refs[:-1]))
    lane, sub = lane_iota(), sub_iota()
    for i, x in enumerate((n, *u, temperature, *q)):
        row = jnp.sum(jnp.where(lane == sub, x, 0.0), axis=0, keepdims=True)
        out_ref[pl.ds(i, 1), :] = row[:, :SUB]


def macro(tiles):
    return pl.pallas_call(
        macro_kernel,
        in_specs=[spec(pltpu.VMEM)] * len(tiles),
        out_specs=spec(pltpu.VMEM),
        out_shape=array(8, SUB),
        compiler_params=params(1),
        name="macro",
    )(*tiles)


def flux_kernel(with_pairs, links_ref, geo_ref, f_ref, out_ref, *refs):
    if with_pairs:
        pairs_ref, cells, faces = refs[0], refs[-2], refs[-1]
        pair_weights(links_ref, geo_ref, pairs_ref, cells, faces)
        refs = refs[1:-2]
    coef, bases, stays, source, face = refs
    planes = f_ref.shape[1] // CHUNKS
    scale = -TIME_STEP / geo_ref[VOL]
    for i in range(3):
        whole = None
        for k in range(FACES):
            x = scale * geo_ref[FV + FACES * i + k]
            coef[FACES * i + k] = x
            whole = x if whole is None else whole + x
        coef[3 * FACES + i] = whole

    def table(g, _):
        w = [[splat(coef, FACES * i + k, g) for i in (1, 2)] for k in range(FACES)]
        whole = [splat(coef, 3 * FACES + i, g) for i in (1, 2)]
        for t in range(TILES):
            xb, xc = tile_nodes(t)
            for k in range(FACES):
                bases[k, g * TILES + t] = w[k][0] * xb + w[k][1] * xc
            stays[g * TILES + t] = 1.0 + whole[0] * xb + whole[1] * xc
        return 0

    lax.fori_loop(0, SUB, table, 0, unroll=2)

    def cell(g, _):
        count = 0
        for k in range(FACES):
            j = links_ref[k, g]
            source[count] = j
            face[count] = k
            count = count + jnp.logical_and(j >= 0, j < SUB).astype(jnp.int32)
        for n in range(FACES + 1):

            @pl.when(count == n)
            def _():
                own_faces(g, n)

        return 0

    def own_faces(g, n):
        at_source = [source[i] for i in range(n)]
        first_weight = [splat(coef, face[k], g) for k in range(n)]
        whole = splat(coef, 3 * FACES, g)
        x0 = splat(geo_ref, FIRST, g)
        base = [[bases[face[k], g * TILES + t] for k in range(n)] for t in range(TILES)]
        stay = [stays[g * TILES + t] for t in range(TILES)]

        def plane(a, _):
            xa = x0 + a.astype(F32) * H
            sa = [w * xa for w in first_weight]
            stay_a = whole * xa
            for t in range(TILES):
                at = at_rows((a * TILES + t) * SUB)
                f = f_ref[g, at, :]
                acc = f * (stay_a + stay[t])
                for k in range(n):
                    acc = acc + jnp.maximum(sa[k] + base[t][k], 0.0) * (f_ref[at_source[k], at, :] - f)
                out_ref[g, at, :] = acc
            return 0

        lax.fori_loop(0, planes, plane, 0, unroll=unroll(planes, 8))

    lax.fori_loop(0, SUB, cell, 0)


def flux(with_pairs, links, geo, f):
    rows = f.shape[1]
    pairs = 2 * len(BEFORE_PAIRS)
    return pl.pallas_call(
        functools.partial(flux_kernel, with_pairs),
        in_specs=[spec(pltpu.SMEM), spec(pltpu.VMEM), spec(pltpu.VMEM)],
        out_specs=[spec(pltpu.VMEM)] * (2 if with_pairs else 1),
        out_shape=[array(*f.shape)] + ([array(pairs, rows, LANES)] if with_pairs else []),
        scratch_shapes=[
            pltpu.VMEM((3 * FACES + 3, SUB, LANES), F32),
            pltpu.VMEM((FACES, SUB * TILES, SUB, LANES), F32),
            pltpu.VMEM((SUB * TILES, SUB, LANES), F32),
            pltpu.SMEM((FACES + 1,), jnp.int32),
            pltpu.SMEM((FACES + 1,), jnp.int32),
        ]
        + (face_lists() if with_pairs else []),
        compiler_params=params(),
        cost_estimate=traffic(rows, 9 if with_pairs else 7),
        name="flux",
    )(links, geo, f)


def target_kernel(count, links_ref, geo_ref, absorbed_in, *refs):
    sums_refs, (f_ref, part_ref, out_ref, *sum_out, tiles_ref, coef, cells, faces) = refs[:count], refs[count:]
    planes = f_ref.shape[1] // CHUNKS
    sums = add_tiles(sums_refs)
    for ref in sum_out:
        ref[...] = sums
    absorbed = sums if absorbed_in is None else absorbed_in[...]
    n, u, temperature, q = quantities(sums)
    rt = 1.0 / temperature
    rate = TIME_STEP * n * temperature / (SHEAR * jnp.exp(POWER * jnp.log(temperature)))
    height = rate * n * rt * jnp.sqrt(rt)
    slope = (1.0 / 3.0) / (5.0 * n * temperature * temperature)
    coef[0] = rate
    coef[1] = rt
    coef[2], coef[3] = u[1], u[2]
    coef[4], coef[5] = slope * q[1], slope * q[2]
    coef[6], coef[7], coef[8] = u[0], slope * q[0], height
    for k in range(FACES):
        wall = geo_ref[WALL + k] > 0.5
        coef[9 + k] = column(sums, EMIT + k) / jnp.where(wall, column(absorbed, ABSORB + k), 1.0)

    def tile_table(g, _):
        rtg = splat(coef, 1, g)
        ub, uc = splat(coef, 2, g), splat(coef, 3, g)
        qb, qc = splat(coef, 4, g), splat(coef, 5, g)
        shape = wall_tiles(splat(geo_ref, WT, g))
        for t in range(TILES):
            xb, xc = tile_nodes(t)
            cb, cc = xb - ub, xc - uc
            z = (cb * cb + cc * cc) * rtg
            at = g * TILES + t
            tiles_ref[0, at] = jnp.exp(-0.5 * z)
            tiles_ref[1, at] = cb * qb + cc * qc
            tiles_ref[2, at] = z
            tiles_ref[3, at] = shape[t]
        return 0

    lax.fori_loop(0, SUB, tile_table, 0, unroll=4)

    def cell(g, _):
        rate_g, rtg, u0, q0, height_g = [splat(coef, i, g) for i in (0, 1, 6, 7, 8)]
        x0 = splat(geo_ref, FIRST, g) - u0
        bell, heat, zz = [[tiles_ref[i, g * TILES + t] for t in range(TILES)] for i in range(3)]

        def plane(a, _):
            ca = x0 + a.astype(F32) * H
            za = ca * ca * rtg
            height_a = height_g * jnp.exp(-0.5 * za)
            heat_a = q0 * ca
            z_a = za - 5.0
            for t in range(TILES):
                where = (g, at_rows((a * TILES + t) * SUB), slice(None))
                f = f_ref[where]
                target = (height_a * bell[t]) * (1.0 + (heat_a + heat[t]) * (z_a + zz[t]))
                out_ref[where] = (part_ref[where] - rate_g * f) + target
            return 0

        lax.fori_loop(0, planes, plane, 0, unroll=unroll(planes, 16))
        return 0

    lax.fori_loop(0, SUB, cell, 0)

    def wall(i, _):
        g, k = cells[i], faces[i]
        x0 = splat(geo_ref, FIRST, g)
        ratio = splat(coef, 9 + k, g)
        scale = -TIME_STEP / splat(geo_ref, VOL, g)
        v0, v1, v2 = [scale * x for x in face_coefficients(geo_ref, k, g)]
        base, shape = [], []
        for t in range(TILES):
            xb, xc = tile_nodes(t)
            base.append(v1 * xb + v2 * xc)
            shape.append(ratio * tiles_ref[3, g * TILES + t])

        rt_wall = -0.5 / splat(geo_ref, WT, g)

        def plane(a, _):
            xa = x0 + a.astype(F32) * H
            wa = jnp.exp(xa * xa * rt_wall)
            sa = v0 * xa
            for t in range(TILES):
                where = (g, at_rows((a * TILES + t) * SUB), slice(None))
                f = f_ref[where]
                out_ref[where] = out_ref[where] + jnp.maximum(sa + base[t], 0.0) * (wa * shape[t] - f)
            return 0

        lax.fori_loop(0, planes, plane, 0, unroll=unroll(planes, 16))
        return 0

    lax.fori_loop(0, list_faces(links_ref, is_wall, cells, faces), wall, 0)


def add_target(links, geo, absorbed, tiles, f, part):
    rows = f.shape[1]
    vmem = spec(pltpu.VMEM)
    given = [links, geo] + ([] if absorbed is None else [absorbed]) + list(tiles) + [f, part]

    def kernel(links_ref, geo_in, *refs):
        if absorbed is None:
            target_kernel(len(tiles), links_ref, geo_in, None, *refs)
        else:
            target_kernel(len(tiles), links_ref, geo_in, *refs)

    return pl.pallas_call(
        kernel,
        in_specs=[spec(pltpu.SMEM)] + [vmem] * (len(given) - 1),
        out_specs=[vmem] * (2 if absorbed is None else 1),
        out_shape=[array(*part.shape)] + ([array(SUB, LANES)] if absorbed is None else []),
        input_output_aliases={len(given) - 1: 0},
        scratch_shapes=[
                pltpu.VMEM((4, SUB * TILES, SUB, LANES), F32),
            pltpu.VMEM((9 + FACES, SUB, LANES), F32),
            *face_lists(),
        ],
        compiler_params=params(),
        cost_estimate=traffic(rows, 7),
        name="add_target",
    )(*given)


def side_terms(high, pairs_ref, halo_ref, f_ref, at):
    terms = [None] * REACH
    rows = [halo_ref[r, at, :] for r in range(REACH)]
    first = SUB - REACH if high else 0
    own = [f_ref[first + e, at, :] for e in range(REACH)]
    count = len(BEFORE_PAIRS)
    pairs = [(e, r) for e in range(REACH) for r in range(e + 1)] if high else BEFORE_PAIRS
    for p, (e, r) in enumerate(pairs):
        term = pairs_ref[p + count if high else p, at, :] * (rows[r] - own[e])
        terms[e] = term if terms[e] is None else terms[e] + term
    return first, terms


def for_side(far, run):
    odd = is_odd()

    @pl.when(odd)
    def _():
        run(far)

    @pl.when(jnp.logical_not(odd))
    def _():
        run(not far)


def add_side(far, pairs_ref, halo_ref, old_ref, part_ref, f_ref, rows_ref, ready=None):
    def run(high):
        def group(j, _):
            at = at_rows(j * SUB)
            first, terms = side_terms(high, pairs_ref, halo_ref, old_ref, at)
            for e in range(REACH):
                x = part_ref[first + e, at, :] + terms[e]
                f_ref[first + e, at, :] = x
                if rows_ref is not None:
                    rows_ref[e, at, :] = x
            return 0

        groups = part_ref.shape[1] // SUB
        parts = 1 if ready is None else EDGE_PARTS
        for i in range(parts):
            if ready is not None:
                ready(i)
            count = groups // parts
            lax.fori_loop(i * count, (i + 1) * count, group, 0, unroll=unroll(count, 8))

    for_side(far, run)


EDGE_PARTS = 4


def near_edge_kernel(pairs_ref, halo_any, old_ref, part_ref, f_ref, rows_ref, halo_ref, sems):
    size = halo_ref.shape[1] // EDGE_PARTS

    def copy(i):
        at = pl.ds(i * size, size)
        return pltpu.make_async_copy(halo_any.at[:, at], halo_ref.at[:, at], sems.at[i])

    for i in range(EDGE_PARTS):
        copy(i).start()
    add_side(False, pairs_ref, halo_ref, old_ref, part_ref, f_ref, rows_ref, lambda i: copy(i).wait())


def edge(far, pairs, halo, old, part):
    rows = part.shape[1]
    return pl.pallas_call(
        functools.partial(add_side, True) if far else near_edge_kernel,
        in_specs=[spec(pltpu.VMEM), spec(pltpu.VMEM if far else pl.ANY), spec(pltpu.VMEM), spec(pltpu.VMEM)],
        out_specs=[spec(pltpu.VMEM)] * 2,
        out_shape=[array(SUB, rows, LANES), array(REACH, rows, LANES)],
        input_output_aliases={3: 0},
        scratch_shapes=[] if far else [pltpu.VMEM(halo.shape, F32), pltpu.SemaphoreType.DMA((EDGE_PARTS,))],
        compiler_params=params(),
        cost_estimate=traffic(rows, 2),
        name="far_edge" if far else "near_edge",
    )(pairs, halo, old, part)


def last_near_kernel(geo_ref, pairs_ref, halo_ref, old_ref, part_ref, f_ref, sums_out, parts_ref):
    add_side(False, pairs_ref, halo_ref, old_ref, part_ref, f_ref, None)
    planes = f_ref.shape[1] // CHUNKS
    y = polynomial_sums(f_ref, planes, parts_ref)
    sums_out[...] = pack_sums(finish_polynomials(y, geo_ref[FIRST], planes), 0)


def last_near(geo, pairs, near, old, part):
    rows = part.shape[1]
    return pl.pallas_call(
        last_near_kernel,
        in_specs=[spec(pltpu.VMEM)] * 5,
        out_specs=[spec(pltpu.VMEM)] * 2,
        out_shape=[array(SUB, rows, LANES), array(SUB, LANES)],
        input_output_aliases={4: 0},
        scratch_shapes=[pltpu.VMEM((10, SUB * SUB + SPARE, LANES), F32)],
        compiler_params=params(),
        cost_estimate=traffic(rows, 3),
        name="last_near",
    )(geo, pairs, near, old, part)


def last_far_kernel(geo_ref, pairs_ref, halo_ref, old_ref, sums_in, terms_ref, sums_out, parts_ref):
    rows = old_ref.shape[1]
    planes = rows // CHUNKS
    parts_ref[...] = jnp.zeros_like(parts_ref)

    def run(high):
        def group(j, _):
            at = at_rows(j * SUB)
            _first, terms = side_terms(high, pairs_ref, halo_ref, old_ref, at)
            for e in range(REACH):
                terms_ref[e, at, :] = terms[e]
            return 0

        lax.fori_loop(0, rows // SUB, group, 0, unroll=unroll(rows // SUB, 8))
        y = polynomial_sums(terms_ref, planes, parts_ref, SUB - REACH if high else 0)
        sums_out[...] = sums_in[...] + pack_sums(finish_polynomials(y, geo_ref[FIRST], planes), 0)

    for_side(True, run)


def last_far(geo, pairs, far, old, sums):
    rows = old.shape[1]
    return pl.pallas_call(
        last_far_kernel,
        in_specs=[spec(pltpu.VMEM)] * 5,
        out_specs=[spec(pltpu.VMEM)] * 2,
        out_shape=[array(REACH, rows, LANES), array(SUB, LANES)],
        scratch_shapes=[pltpu.VMEM((10, SUB * SUB + SPARE, LANES), F32)],
        compiler_params=params(),
        cost_estimate=traffic(rows, 2),
        name="last_far",
    )(geo, pairs, far, old, sums)


LAST_PARTS = 4


def result_kernel(part_ref, terms_ref, out_hbm, native_ref, sems):
    part = part_ref.shape[1] // SUB // LAST_PARTS

    def copy(i):
        at = pl.ds(i * part * SUB * SUB, part * SUB * SUB)
        return pltpu.make_async_copy(native_ref.at[at], out_hbm.at[at], sems.at[i])

    def run(high):
        first = SUB - REACH if high else 0
        for i in range(LAST_PARTS):

            def group(j, _):
                at = at_rows(j * SUB)
                for g in range(SUB):
                    x = part_ref[g, at, :]
                    if 0 <= g - first < REACH:
                        x = x + terms_ref[g - first, at, :]
                    native_ref[pl.ds(j * SUB * SUB + g, SUB, stride=SUB), :] = x
                return 0

            lax.fori_loop(i * part, (i + 1) * part, group, 0, unroll=unroll(part, 4))
            copy(i).start()

    for_side(True, run)
    for i in range(LAST_PARTS):
        copy(i).wait()


def result(part, terms):
    rows = part.shape[1]
    native = (SUB * rows, LANES)
    return pl.pallas_call(
        result_kernel,
        in_specs=[spec(pltpu.VMEM)] * 2,
        out_specs=spec(pltpu.HBM),
        out_shape=array(*native),
        scratch_shapes=[pltpu.VMEM((SUB * rows + SPARE, LANES), F32), pltpu.SemaphoreType.DMA((LAST_PARTS,))],
        compiler_params=params(),
        cost_estimate=traffic(rows, 3),
        name="result",
    )(part, terms)


def swap(rows, start):
    pairs = [(i, i + 1) for i in range(start, lax.axis_size("space") - 1, 2)]
    return lax.ppermute(rows, "space", pairs + [(j, i) for i, j in pairs])


def per_device(particle_profile, neighbors, face_vectors, volumes, wall_temp):
    cells, points = particle_profile.shape
    rows = points // LANES
    plane_count = NV // lax.axis_size("vel")
    native = particle_profile.reshape(cells, rows, LANES).transpose(1, 0, 2).reshape(cells * rows, LANES)
    wall = neighbors < 0
    links = jnp.where(wall, WALL_LINK, neighbors - lax.axis_index("space") * cells)
    own = (links >= 0) & (links < cells)
    first = -SPEED_LIMIT + ((lax.axis_index("vel") * plane_count).astype(F32) + 0.5) * H
    geo = jnp.concatenate(
        [
            face_vectors.reshape(3 * FACES, cells),
            volumes[None],
            wall_temp[None],
            wall.astype(F32),
            own.astype(F32),
            jnp.full((1, cells), first, F32),
        ]
    )
    geo = jnp.broadcast_to(geo[:, :, None], (GEO, cells, LANES))
    native, far, near = first_rows(native)
    far, near = swap(far, 1), swap(near, 0)
    f, sums = first_sums(links, geo, native)
    tiles = gather_sums(sums)
    part, pairs = flux(True, links, geo, f)
    part, absorbed = add_target(links, geo, None, tiles, f, part)
    part, near = edge(False, pairs, near, f, part)
    near = swap(near, 0)
    f, far = edge(True, pairs, far, f, part)
    far = swap(far, 1)
    tiles = gather_sums(local_sums(links, geo, f))
    (part,) = flux(False, links, geo, f)
    (part,) = add_target(links, geo, absorbed, tiles, f, part)
    part, sums = last_near(geo, pairs, near, f, part)
    terms, sums = last_far(geo, pairs, far, f, sums)
    tiles = doubling_sums(sums)
    native = result(part, terms)
    macro_quantities = macro(tiles)
    evolved = native.reshape(rows, cells, LANES).transpose(1, 0, 2).reshape(cells, points)
    return evolved, macro_quantities


def solution(mesh):
    return jax.shard_map(
        per_device,
        mesh=mesh,
        in_specs=(
            P("space", "vel"),
            P(None, "space"),
            P(None, None, "space"),
            P("space"),
            P("space"),
        ),
        out_specs=(P("space", "vel"), P(None, "space")),
        check_vma=False,
    )
```

```python
import functools
import math

import jax
import jax.numpy as jnp
from jax import lax
from jax.experimental import pallas as pl
from jax.experimental.pallas import tpu as pltpu
from jax.sharding import PartitionSpec as P

NV = 64
FACES = 6
REACH = 3
STEPS = 2
LANES = 128
SUB = 8
SPARE = SUB

TIME_STEP = 0.015
SHEAR = 0.1
POWER = 0.81
SPEED_LIMIT = 6.0
H = 2.0 * SPEED_LIMIT / NV
WEIGHT = H**3 * (2.0 * math.pi) ** (-1.5)

CHUNKS = NV * NV // LANES
TILES = CHUNKS // SUB

FV, VOL, WT, WALL, LOCAL, FIRST = 0, 18, 19, 20, 26, 32
GEO = 33
WALL_LINK = -64
BEFORE_PAIRS = tuple((g, r) for g in range(REACH) for r in range(g, REACH))
EMIT, ABSORB = 13, 19
SUMS = 25

F32 = jnp.float32


def lane_iota():
    return lax.broadcasted_iota(jnp.int32, (SUB, LANES), 1)


def sub_iota():
    return lax.broadcasted_iota(jnp.int32, (SUB, LANES), 0)


def half_of(lane):
    return (lane >= NV).astype(F32)


def third_component(lane):
    c = jnp.where(lane >= NV, lane - NV, lane).astype(F32)
    return -SPEED_LIMIT + (c + 0.5) * H


def tile_nodes(t):
    lane = lane_iota()
    b = (2 * SUB * t + 2 * sub_iota()).astype(F32) + half_of(lane)
    return -SPEED_LIMIT + (b + 0.5) * H, third_component(lane)


def column(tile, p):
    return jnp.broadcast_to(tile[:, p : p + 1], (SUB, LANES))


def splat(ref, i, g):
    return jnp.broadcast_to(ref[i, pl.ds(g, 1), :], (SUB, LANES))


def total(tile):
    return jnp.broadcast_to(jnp.sum(tile, axis=1, keepdims=True), (SUB, LANES))


def face_coefficients(geo_ref, k, g):
    return [splat(geo_ref, FV + FACES * i + k, g) for i in range(3)]


def at_rows(start, size=SUB):
    return pl.ds(pl.multiple_of(start, SUB), size)


def wall_tiles(wall_temp):
    rt = 1.0 / wall_temp
    scale = rt * jnp.sqrt(rt)
    out = []
    for t in range(TILES):
        xb, xc = tile_nodes(t)
        out.append(scale * jnp.exp(-0.5 * (xb * xb + xc * xc) * rt))
    return out


def pack_sums(arrays, start):
    lane = lane_iota()
    out = jnp.zeros((SUB, LANES), F32)
    for p, x in enumerate(arrays):
        out = jnp.where(lane == start + p, total(x), out)
    return out


def over_sublanes(ref, k):
    out = ref[k, pl.ds(0, SUB, stride=SUB), :]
    for s in range(1, SUB):
        out = out + ref[k, pl.ds(s, SUB, stride=SUB), :]
    return out


def list_faces(links_ref, wanted, cell_ref, face_ref):
    count = 0
    for g in range(SUB):
        for k in range(FACES):
            cell_ref[count] = g
            face_ref[count] = k
            count = count + wanted(links_ref[k, g]).astype(jnp.int32)
    return count


def is_wall(j):
    return j == WALL_LINK


def is_remote(j):
    return jnp.logical_or(j >= SUB, jnp.logical_and(j < 0, j != WALL_LINK))


def face_lists():
    return [pltpu.SMEM((FACES * SUB + 1,), jnp.int32)] * 2


def unroll(planes, most):
    return math.gcd(planes, most)


def finish_polynomials(y, first, planes):
    y0, y1, y2, y3, by0, by1, by2, bby0, bby1, bbby0 = y
    m = first + 0.5 * (planes - 1) * H
    c = third_component(lane_iota())
    cc = c * c
    a = y1 + m * y0
    aa = y2 + m * (2.0 * y1 + m * y0)
    aaa = y3 + m * (3.0 * y2 + m * (3.0 * y1 + m * y0))
    ab = by1 + m * by0
    aab = by2 + m * (2.0 * by1 + m * by0)
    abb = bby1 + m * bby0
    return (
        y0,
        a,
        by0,
        c * y0,
        aa,
        bby0,
        cc * y0,
        ab,
        c * a,
        c * by0,
        aaa + abb + cc * a,
        aab + bbby0 + cc * by0,
        c * (aa + bby0 + cc * y0),
    )


def polynomial_sums(f_ref, planes, parts_ref, first=0):
    half = planes // 2

    def cell(g, _):
        out = [None] * 10
        for t in range(TILES):
            y0 = y1 = y2 = y3 = None
            for i in range(half):
                d = (i + 0.5) * H
                hi = f_ref[g, pl.ds(((half + i) * TILES + t) * SUB, SUB), :]
                lo = f_ref[g, pl.ds(((half - 1 - i) * TILES + t) * SUB, SUB), :]
                s, r = hi + lo, hi - lo
                if i == 0:
                    y0, y1, y2, y3 = s, d * r, (d * d) * s, (d * d * d) * r
                else:
                    y0, y1, y2, y3 = y0 + s, y1 + d * r, y2 + (d * d) * s, y3 + (d * d * d) * r
            b, _c = tile_nodes(t)
            bb = b * b
            terms = (y0, y1, y2, y3, b * y0, b * y1, b * y2, bb * y0, bb * y1, bb * (b * y0))
            out = [x if o is None else o + x for o, x in zip(out, terms)]
        for p in range(10):
            parts_ref[p, at_rows((first + g) * SUB), :] = out[p]
        return 0

    lax.fori_loop(0, f_ref.shape[0], cell, 0)
    return [over_sublanes(parts_ref, p) for p in range(10)]


def native_polynomial_sums(native_ref, planes):
    half, side = planes // 2, CHUNKS // 2
    zero = jnp.zeros((SUB, LANES), F32)
    acc = [zero] * 10

    def plane(a, acc):
        xa = (a.astype(F32) - 0.5 * (planes - 1)) * H
        b0 = b1 = b2 = b3 = None
        for i in range(side):
            y = (2 * i + 1) * H
            hi = native_ref[at_rows((a * CHUNKS + side + i) * SUB), :]
            lo = native_ref[at_rows((a * CHUNKS + side - 1 - i) * SUB), :]
            s, d = hi + lo, hi - lo
            terms = (s, y * d, (y * y) * s, (y * y * y) * d)
            if i == 0:
                b0, b1, b2, b3 = terms
            else:
                b0, b1, b2, b3 = b0 + terms[0], b1 + terms[1], b2 + terms[2], b3 + terms[3]
        a0, a1, a2 = xa * b0, xa * b1, xa * b2
        aa0 = xa * a0
        new = (b0, a0, aa0, xa * aa0, b1, a1, xa * a1, b2, a2, b3)
        return tuple(x + z for x, z in zip(acc, new))

    g0, a0, aa0, aaa0, g1, a1, aa1, g2, a2, g3 = lax.fori_loop(0, planes, plane, tuple(acc))
    e = (half_of(lane_iota()) - 0.5) * H
    return [
        g0,
        a0,
        aa0,
        aaa0,
        g1 + e * g0,
        a1 + e * a0,
        aa1 + e * aa0,
        g2 + e * (2.0 * g1 + e * g0),
        a2 + e * (2.0 * a1 + e * a0),
        g3 + e * (3.0 * g2 + e * (3.0 * g1 + e * g0)),
    ]


def wall_sums(f_ref, planes, links_ref, geo_ref, sums_ref, cells, faces, with_absorbed):
    sums_ref[...] = jnp.zeros_like(sums_ref)

    def wall(i, _):
        g, k = cells[i], faces[i]
        v0, v1, v2 = face_coefficients(geo_ref, k, g)
        first = splat(geo_ref, FIRST, g)
        base = []
        for t in range(TILES):
            xb, xc = tile_nodes(t)
            base.append(v1 * xb + v2 * xc)
        if with_absorbed:
            wt = splat(geo_ref, WT, g)
            shape = wall_tiles(wt)

        def plane(a, acc):
            out, back = list(acc[0]), list(acc[1])
            xa = first + a.astype(F32) * H
            sa = v0 * xa
            if with_absorbed:
                wa = jnp.exp(-0.5 * xa * xa / wt)
            for t in range(TILES):
                s = sa + base[t]
                f = f_ref[g, at_rows((a * TILES + t) * SUB), :]
                out[t] = out[t] + jnp.maximum(s, 0.0) * f
                if with_absorbed:
                    back[t] = back[t] + jnp.maximum(-s, 0.0) * (wa * shape[t])
            return tuple(out), tuple(back)

        zeros = (jnp.zeros((SUB, LANES), F32),) * TILES
        out, back = lax.fori_loop(0, planes, plane, (zeros, zeros), unroll=unroll(planes, 16))
        at = at_rows(g * SUB)
        sums_ref[k, at, :] = (out[0] + out[1]) + (out[2] + out[3])
        if with_absorbed:
            sums_ref[FACES + k, at, :] = (back[0] + back[1]) + (back[2] + back[3])
        return 0

    lax.fori_loop(0, list_faces(links_ref, is_wall, cells, faces), wall, 0)


def sums_kernel(links_ref, geo_ref, f_ref, sums_out, parts_ref, face_ref, cells, faces):
    planes = f_ref.shape[1] // CHUNKS
    y = polynomial_sums(f_ref, planes, parts_ref)
    packed = pack_sums(finish_polynomials(y, geo_ref[FIRST], planes), 0)
    wall_sums(f_ref, planes, links_ref, geo_ref, face_ref, cells, faces, False)
    sums_out[...] = packed + pack_sums([over_sublanes(face_ref, k) for k in range(FACES)], EMIT)


def first_sums_kernel(links_ref, geo_ref, native_ref, f_ref, sums_out, face_ref, cells, faces):
    rows = f_ref.shape[1]
    planes = rows // CHUNKS

    def group(j, _):
        for g in range(SUB):
            f_ref[g, at_rows(j * SUB), :] = native_ref[pl.ds(j * SUB * SUB + g, SUB, stride=SUB), :]
        return 0

    lax.fori_loop(0, rows // SUB, group, 0, unroll=2)
    y = native_polynomial_sums(native_ref, planes)
    packed = pack_sums(finish_polynomials(y, geo_ref[FIRST], planes), 0)
    wall_sums(f_ref, planes, links_ref, geo_ref, face_ref, cells, faces, True)
    sums_out[...] = packed + pack_sums([over_sublanes(face_ref, k) for k in range(2 * FACES)], EMIT)


def spec(space):
    return pl.BlockSpec(memory_space=space)


def array(*shape):
    return jax.ShapeDtypeStruct(shape, F32)


def params(mib=4):
    return pltpu.CompilerParams(vmem_limit_bytes=mib * 1024 * 1024)


def traffic(rows, profiles):
    size = SUB * rows * LANES
    return pl.CostEstimate(flops=8 * profiles * size, bytes_accessed=4 * profiles * size, transcendentals=0)


def local_sums(links, geo, f):
    return pl.pallas_call(
        sums_kernel,
        in_specs=[spec(pltpu.SMEM), spec(pltpu.VMEM), spec(pltpu.VMEM)],
        out_specs=spec(pltpu.VMEM),
        out_shape=array(SUB, LANES),
        scratch_shapes=[
                pltpu.VMEM((10, SUB * SUB + SPARE, LANES), F32),
            pltpu.VMEM((FACES, SUB * SUB + SPARE, LANES), F32),
            *face_lists(),
        ],
        compiler_params=params(),
        cost_estimate=traffic(f.shape[1], 4),
        name="local_sums",
    )(links, geo, f)


def first_sums(links, geo, native):
    rows = (native.shape[0] - SPARE) // SUB
    return pl.pallas_call(
        first_sums_kernel,
        in_specs=[spec(pltpu.SMEM), spec(pltpu.VMEM), spec(pltpu.VMEM)],
        out_specs=[spec(pltpu.VMEM)] * 2,
        out_shape=[array(SUB, rows, LANES), array(SUB, LANES)],
        scratch_shapes=[
                pltpu.VMEM((2 * FACES, SUB * SUB + SPARE, LANES), F32),
            *face_lists(),
        ],
        compiler_params=params(),
        cost_estimate=traffic(rows, 5),
        name="first_sums",
    )(links, geo, native)


SPLIT_PARTS = 8


def is_odd():
    return lax.rem(lax.axis_index("space"), 2) == 1


def first_rows_kernel(native_hbm, native_ref, far_any, near_any, far_ref, near_ref, sems, far_sems, near_sems):
    rows = native_hbm.shape[0]
    part = rows // SPLIT_PARTS
    copies = [
        pltpu.make_async_copy(
            native_hbm.at[pl.ds(i * part, part)], native_ref.at[pl.ds(i * part, part)], sems.at[i]
        )
        for i in range(SPLIT_PARTS)
    ]
    for c in copies:
        c.start()
    odd = is_odd()
    far = jnp.where(odd, SUB - REACH, 0)
    near = jnp.where(odd, 0, SUB - REACH)
    groups = part // (SUB * SUB)
    out = []

    for i, c in enumerate(copies):
        c.wait()

        def group(j, _):
            for r in range(REACH):
                at = at_rows(j * SUB)
                far_ref[r, at, :] = native_ref[pl.ds(j * SUB * SUB + far + r, SUB, stride=SUB), :]
                near_ref[r, at, :] = native_ref[pl.ds(j * SUB * SUB + near + r, SUB, stride=SUB), :]
            return 0

        lax.fori_loop(i * groups, (i + 1) * groups, group, 0, unroll=unroll(groups, 8))
        at = pl.ds(i * groups * SUB, groups * SUB)
        out.append(pltpu.make_async_copy(far_ref.at[:, at], far_any.at[:, at], far_sems.at[i]))
        out.append(pltpu.make_async_copy(near_ref.at[:, at], near_any.at[:, at], near_sems.at[i]))
        out[-2].start()
        out[-1].start()
    for c in out:
        c.wait()


def first_rows(native):
    rows = native.shape[0] // SUB
    halo = (REACH, rows, LANES)
    return pl.pallas_call(
        first_rows_kernel,
        in_specs=[spec(pltpu.HBM)],
        out_specs=[spec(pltpu.VMEM), spec(pl.ANY), spec(pl.ANY)],
        out_shape=[array(native.shape[0] + SPARE, LANES), array(*halo), array(*halo)],
        scratch_shapes=[pltpu.VMEM(halo, F32)] * 2 + [pltpu.SemaphoreType.DMA((SPLIT_PARTS,))] * 3,
        compiler_params=params(),
        cost_estimate=traffic(rows, 4),
        name="first_rows",
    )(pltpu.with_memory_space_constraint(native, pltpu.HBM))


def pair_weights(links_ref, geo_ref, pairs_ref, cells, faces):
    rows = pairs_ref.shape[1]
    planes = rows // CHUNKS
    first = splat(geo_ref, FIRST, 0)

    def clear(j, _):
        for p in range(pairs_ref.shape[0]):
            pairs_ref[p, at_rows(j * SUB), :] = jnp.zeros((SUB, LANES), F32)
        return 0

    lax.fori_loop(0, rows // SUB, clear, 0, unroll=4)

    def remote(i, _):
        g, k = cells[i], faces[i]
        j = links_ref[k, g]
        edge = g - (SUB - REACH)
        before = g * REACH - g * (g - 1) // 2 + (j + REACH) - g
        after = len(BEFORE_PAIRS) + edge * (edge + 1) // 2 + j - SUB
        at_pair = jnp.where(j < 0, before, after)
        scale = -TIME_STEP / splat(geo_ref, VOL, g)
        v0, v1, v2 = [scale * x for x in face_coefficients(geo_ref, k, g)]
        base = []
        for t in range(TILES):
            xb, xc = tile_nodes(t)
            base.append(v1 * xb + v2 * xc)

        def plane(a, _):
            sa = v0 * (first + a.astype(F32) * H)
            for t in range(TILES):
                at = at_rows((a * TILES + t) * SUB)
                pairs_ref[at_pair, at, :] = pairs_ref[at_pair, at, :] + jnp.maximum(sa + base[t], 0.0)
            return 0

        lax.fori_loop(0, planes, plane, 0, unroll=unroll(planes, 8))
        return 0

    lax.fori_loop(0, list_faces(links_ref, is_remote, cells, faces), remote, 0)


def gather_sums(tile):
    size = lax.axis_size("vel")
    if size not in (2, 4):
        return [lax.psum(tile, "vel")]
    others = [lax.ppermute(tile, "vel", [(i, i ^ s) for i in range(size)]) for s in range(1, size)]
    return [tile, *others]


def doubling_sums(tile):
    size = lax.axis_size("vel")
    if size != 4:
        return gather_sums(tile)
    pair = tile + lax.ppermute(tile, "vel", [(i, i ^ 1) for i in range(size)])
    return [pair, lax.ppermute(pair, "vel", [(i, i ^ 2) for i in range(size)])]


def add_tiles(refs):
    tiles = [r[...] for r in refs]
    while len(tiles) > 1:
        tiles = [tiles[i] + tiles[i + 1] for i in range(0, len(tiles), 2)]
    return tiles[0]


def quantities(sums):
    m = [WEIGHT * x for x in sums]
    n = m[0]
    rn = 1.0 / n
    u = [m[1 + i] * rn for i in range(3)]
    uu = u[0] * u[0] + u[1] * u[1] + u[2] * u[2]
    trace = m[4] + m[5] + m[6]
    width = trace - n * uu
    temperature = width * rn * (1.0 / 3.0)
    second = [[m[4], m[7], m[8]], [m[7], m[5], m[9]], [m[8], m[9], m[6]]]
    q = []
    for i in range(3):
        across = u[0] * second[i][0] + u[1] * second[i][1] + u[2] * second[i][2]
        q.append(0.5 * (m[10 + i] - 2.0 * across - u[i] * trace + 2.0 * uu * m[1 + i]))
    return n, u, temperature, q


def macro_kernel(*refs):
    out_ref = refs[-1]
    by_sum = jnp.transpose(add_tiles(refs[:-1]))
    n, u, temperature, q = quantities([by_sum[p : p + 1, :] for p in range(13)])
    for i, x in enumerate((n, *u, temperature, *q)):
        out_ref[pl.ds(i, 1), :] = x


def macro(tiles):
    return pl.pallas_call(
        macro_kernel,
        in_specs=[spec(pltpu.VMEM)] * len(tiles),
        out_specs=spec(pltpu.VMEM),
        out_shape=array(8, SUB),
        compiler_params=params(1),
        name="macro",
    )(*tiles)


def flux_kernel(with_pairs, links_ref, geo_ref, f_ref, out_ref, *refs):
    if with_pairs:
        pairs_ref, cells, faces = refs[0], refs[-2], refs[-1]
        pair_weights(links_ref, geo_ref, pairs_ref, cells, faces)
        refs = refs[1:-2]
    coef, bases, stays, source, face = refs
    planes = f_ref.shape[1] // CHUNKS
    scale = -TIME_STEP / geo_ref[VOL]
    for i in range(3):
        whole = None
        for k in range(FACES):
            x = scale * geo_ref[FV + FACES * i + k]
            coef[FACES * i + k] = x
            whole = x if whole is None else whole + x
        coef[3 * FACES + i] = whole

    def table(g, _):
        w = [[splat(coef, FACES * i + k, g) for i in (1, 2)] for k in range(FACES)]
        whole = [splat(coef, 3 * FACES + i, g) for i in (1, 2)]
        for t in range(TILES):
            xb, xc = tile_nodes(t)
            for k in range(FACES):
                bases[k, g * TILES + t] = w[k][0] * xb + w[k][1] * xc
            stays[g * TILES + t] = 1.0 + whole[0] * xb + whole[1] * xc
        return 0

    lax.fori_loop(0, SUB, table, 0, unroll=2)

    def cell(g, _):
        count = 0
        for k in range(FACES):
            j = links_ref[k, g]
            source[count] = j
            face[count] = k
            count = count + jnp.logical_and(j >= 0, j < SUB).astype(jnp.int32)
        for n in range(FACES + 1):

            @pl.when(count == n)
            def _():
                own_faces(g, n)

        return 0

    def own_faces(g, n):
        at_source = [source[i] for i in range(n)]
        first_weight = [splat(coef, face[k], g) for k in range(n)]
        whole = splat(coef, 3 * FACES, g)
        x0 = splat(geo_ref, FIRST, g)
        base = [[bases[face[k], g * TILES + t] for k in range(n)] for t in range(TILES)]
        stay = [stays[g * TILES + t] for t in range(TILES)]

        def plane(a, _):
            xa = x0 + a.astype(F32) * H
            sa = [w * xa for w in first_weight]
            stay_a = whole * xa
            for t in range(TILES):
                at = at_rows((a * TILES + t) * SUB)
                f = f_ref[g, at, :]
                acc = f * (stay_a + stay[t])
                for k in range(n):
                    acc = acc + jnp.maximum(sa[k] + base[t][k], 0.0) * (f_ref[at_source[k], at, :] - f)
                out_ref[g, at, :] = acc
            return 0

        lax.fori_loop(0, planes, plane, 0, unroll=unroll(planes, 8))

    lax.fori_loop(0, SUB, cell, 0)


def flux(with_pairs, links, geo, f):
    rows = f.shape[1]
    pairs = 2 * len(BEFORE_PAIRS)
    return pl.pallas_call(
        functools.partial(flux_kernel, with_pairs),
        in_specs=[spec(pltpu.SMEM), spec(pltpu.VMEM), spec(pltpu.VMEM)],
        out_specs=[spec(pltpu.VMEM)] * (2 if with_pairs else 1),
        out_shape=[array(*f.shape)] + ([array(pairs, rows, LANES)] if with_pairs else []),
        scratch_shapes=[
            pltpu.VMEM((3 * FACES + 3, SUB, LANES), F32),
            pltpu.VMEM((FACES, SUB * TILES, SUB, LANES), F32),
            pltpu.VMEM((SUB * TILES, SUB, LANES), F32),
            pltpu.SMEM((FACES + 1,), jnp.int32),
            pltpu.SMEM((FACES + 1,), jnp.int32),
        ]
        + (face_lists() if with_pairs else []),
        compiler_params=params(),
        cost_estimate=traffic(rows, 9 if with_pairs else 7),
        name="flux",
    )(links, geo, f)


def target_kernel(count, links_ref, geo_ref, absorbed_in, *refs):
    sums_refs, (f_ref, part_ref, out_ref, *sum_out, tiles_ref, coef, cells, faces) = refs[:count], refs[count:]
    planes = f_ref.shape[1] // CHUNKS
    sums = add_tiles(sums_refs)
    for ref in sum_out:
        ref[...] = sums
    absorbed = sums if absorbed_in is None else absorbed_in[...]
    n, u, temperature, q = quantities([column(sums, p) for p in range(13)])
    rt = 1.0 / temperature
    rate = TIME_STEP * n * temperature / (SHEAR * jnp.exp(POWER * jnp.log(temperature)))
    height = rate * n * rt * jnp.sqrt(rt)
    slope = (1.0 / 3.0) / (5.0 * n * temperature * temperature)
    coef[0] = rate
    coef[1] = rt
    coef[2], coef[3] = u[1], u[2]
    coef[4], coef[5] = slope * q[1], slope * q[2]
    coef[6], coef[7], coef[8] = u[0], slope * q[0], height
    for k in range(FACES):
        wall = geo_ref[WALL + k] > 0.5
        coef[9 + k] = column(sums, EMIT + k) / jnp.where(wall, column(absorbed, ABSORB + k), 1.0)

    def tile_table(g, _):
        rtg = splat(coef, 1, g)
        ub, uc = splat(coef, 2, g), splat(coef, 3, g)
        qb, qc = splat(coef, 4, g), splat(coef, 5, g)
        shape = wall_tiles(splat(geo_ref, WT, g))
        for t in range(TILES):
            xb, xc = tile_nodes(t)
            cb, cc = xb - ub, xc - uc
            z = (cb * cb + cc * cc) * rtg
            at = g * TILES + t
            tiles_ref[0, at] = jnp.exp(-0.5 * z)
            tiles_ref[1, at] = cb * qb + cc * qc
            tiles_ref[2, at] = z
            tiles_ref[3, at] = shape[t]
        return 0

    lax.fori_loop(0, SUB, tile_table, 0, unroll=4)

    def cell(g, _):
        rate_g, rtg, u0, q0, height_g = [splat(coef, i, g) for i in (0, 1, 6, 7, 8)]
        x0 = splat(geo_ref, FIRST, g) - u0
        bell, heat, zz = [[tiles_ref[i, g * TILES + t] for t in range(TILES)] for i in range(3)]

        def plane(a, _):
            ca = x0 + a.astype(F32) * H
            za = ca * ca * rtg
            height_a = height_g * jnp.exp(-0.5 * za)
            heat_a = q0 * ca
            z_a = za - 5.0
            for t in range(TILES):
                where = (g, at_rows((a * TILES + t) * SUB), slice(None))
                f = f_ref[where]
                target = (height_a * bell[t]) * (1.0 + (heat_a + heat[t]) * (z_a + zz[t]))
                out_ref[where] = (part_ref[where] - rate_g * f) + target
            return 0

        lax.fori_loop(0, planes, plane, 0, unroll=unroll(planes, 16))
        return 0

    lax.fori_loop(0, SUB, cell, 0)

    def wall(i, _):
        g, k = cells[i], faces[i]
        x0 = splat(geo_ref, FIRST, g)
        ratio = splat(coef, 9 + k, g)
        scale = -TIME_STEP / splat(geo_ref, VOL, g)
        v0, v1, v2 = [scale * x for x in face_coefficients(geo_ref, k, g)]
        base, shape = [], []
        for t in range(TILES):
            xb, xc = tile_nodes(t)
            base.append(v1 * xb + v2 * xc)
            shape.append(ratio * tiles_ref[3, g * TILES + t])

        rt_wall = -0.5 / splat(geo_ref, WT, g)

        def plane(a, _):
            xa = x0 + a.astype(F32) * H
            wa = jnp.exp(xa * xa * rt_wall)
            sa = v0 * xa
            for t in range(TILES):
                where = (g, at_rows((a * TILES + t) * SUB), slice(None))
                f = f_ref[where]
                out_ref[where] = out_ref[where] + jnp.maximum(sa + base[t], 0.0) * (wa * shape[t] - f)
            return 0

        lax.fori_loop(0, planes, plane, 0, unroll=unroll(planes, 16))
        return 0

    lax.fori_loop(0, list_faces(links_ref, is_wall, cells, faces), wall, 0)


def add_target(links, geo, absorbed, tiles, f, part):
    rows = f.shape[1]
    vmem = spec(pltpu.VMEM)
    given = [links, geo] + ([] if absorbed is None else [absorbed]) + list(tiles) + [f, part]

    def kernel(links_ref, geo_in, *refs):
        if absorbed is None:
            target_kernel(len(tiles), links_ref, geo_in, None, *refs)
        else:
            target_kernel(len(tiles), links_ref, geo_in, *refs)

    return pl.pallas_call(
        kernel,
        in_specs=[spec(pltpu.SMEM)] + [vmem] * (len(given) - 1),
        out_specs=[vmem] * (2 if absorbed is None else 1),
        out_shape=[array(*part.shape)] + ([array(SUB, LANES)] if absorbed is None else []),
        input_output_aliases={len(given) - 1: 0},
        scratch_shapes=[
                pltpu.VMEM((4, SUB * TILES, SUB, LANES), F32),
            pltpu.VMEM((9 + FACES, SUB, LANES), F32),
            *face_lists(),
        ],
        compiler_params=params(),
        cost_estimate=traffic(rows, 7),
        name="add_target",
    )(*given)


def side_terms(high, pairs_ref, halo_ref, f_ref, at):
    terms = [None] * REACH
    rows = [halo_ref[r, at, :] for r in range(REACH)]
    first = SUB - REACH if high else 0
    own = [f_ref[first + e, at, :] for e in range(REACH)]
    count = len(BEFORE_PAIRS)
    pairs = [(e, r) for e in range(REACH) for r in range(e + 1)] if high else BEFORE_PAIRS
    for p, (e, r) in enumerate(pairs):
        term = pairs_ref[p + count if high else p, at, :] * (rows[r] - own[e])
        terms[e] = term if terms[e] is None else terms[e] + term
    return first, terms


def for_side(far, run):
    odd = is_odd()

    @pl.when(odd)
    def _():
        run(far)

    @pl.when(jnp.logical_not(odd))
    def _():
        run(not far)


def add_side(far, pairs_ref, halo_ref, old_ref, part_ref, f_ref, rows_ref, ready=None):
    def run(high):
        def group(j, _):
            at = at_rows(j * SUB)
            first, terms = side_terms(high, pairs_ref, halo_ref, old_ref, at)
            for e in range(REACH):
                x = part_ref[first + e, at, :] + terms[e]
                f_ref[first + e, at, :] = x
                if rows_ref is not None:
                    rows_ref[e, at, :] = x
            return 0

        groups = part_ref.shape[1] // SUB
        parts = 1 if ready is None else EDGE_PARTS
        for i in range(parts):
            if ready is not None:
                ready(i)
            count = groups // parts
            lax.fori_loop(i * count, (i + 1) * count, group, 0, unroll=unroll(count, 8))

    for_side(far, run)


EDGE_PARTS = 4


def near_edge_kernel(pairs_ref, halo_any, old_ref, part_ref, f_ref, rows_ref, halo_ref, sems):
    size = halo_ref.shape[1] // EDGE_PARTS

    def copy(i):
        at = pl.ds(i * size, size)
        return pltpu.make_async_copy(halo_any.at[:, at], halo_ref.at[:, at], sems.at[i])

    for i in range(EDGE_PARTS):
        copy(i).start()
    add_side(False, pairs_ref, halo_ref, old_ref, part_ref, f_ref, rows_ref, lambda i: copy(i).wait())


def edge(far, pairs, halo, old, part):
    rows = part.shape[1]
    return pl.pallas_call(
        functools.partial(add_side, True) if far else near_edge_kernel,
        in_specs=[spec(pltpu.VMEM), spec(pltpu.VMEM if far else pl.ANY), spec(pltpu.VMEM), spec(pltpu.VMEM)],
        out_specs=[spec(pltpu.VMEM)] * 2,
        out_shape=[array(SUB, rows, LANES), array(REACH, rows, LANES)],
        input_output_aliases={3: 0},
        scratch_shapes=[] if far else [pltpu.VMEM(halo.shape, F32), pltpu.SemaphoreType.DMA((EDGE_PARTS,))],
        compiler_params=params(),
        cost_estimate=traffic(rows, 2),
        name="far_edge" if far else "near_edge",
    )(pairs, halo, old, part)


def last_near_kernel(geo_ref, pairs_ref, halo_ref, old_ref, part_ref, f_ref, sums_out, parts_ref):
    add_side(False, pairs_ref, halo_ref, old_ref, part_ref, f_ref, None)
    planes = f_ref.shape[1] // CHUNKS
    y = polynomial_sums(f_ref, planes, parts_ref)
    sums_out[...] = pack_sums(finish_polynomials(y, geo_ref[FIRST], planes), 0)


def last_near(geo, pairs, near, old, part):
    rows = part.shape[1]
    return pl.pallas_call(
        last_near_kernel,
        in_specs=[spec(pltpu.VMEM)] * 5,
        out_specs=[spec(pltpu.VMEM)] * 2,
        out_shape=[array(SUB, rows, LANES), array(SUB, LANES)],
        input_output_aliases={4: 0},
        scratch_shapes=[pltpu.VMEM((10, SUB * SUB + SPARE, LANES), F32)],
        compiler_params=params(),
        cost_estimate=traffic(rows, 3),
        name="last_near",
    )(geo, pairs, near, old, part)


def last_far_kernel(geo_ref, pairs_ref, halo_ref, old_ref, sums_in, terms_ref, sums_out, parts_ref):
    rows = old_ref.shape[1]
    planes = rows // CHUNKS
    parts_ref[...] = jnp.zeros_like(parts_ref)

    def run(high):
        def group(j, _):
            at = at_rows(j * SUB)
            _first, terms = side_terms(high, pairs_ref, halo_ref, old_ref, at)
            for e in range(REACH):
                terms_ref[e, at, :] = terms[e]
            return 0

        lax.fori_loop(0, rows // SUB, group, 0, unroll=unroll(rows // SUB, 8))
        y = polynomial_sums(terms_ref, planes, parts_ref, SUB - REACH if high else 0)
        sums_out[...] = sums_in[...] + pack_sums(finish_polynomials(y, geo_ref[FIRST], planes), 0)

    for_side(True, run)


def last_far(geo, pairs, far, old, sums):
    rows = old.shape[1]
    return pl.pallas_call(
        last_far_kernel,
        in_specs=[spec(pltpu.VMEM)] * 5,
        out_specs=[spec(pltpu.VMEM)] * 2,
        out_shape=[array(REACH, rows, LANES), array(SUB, LANES)],
        scratch_shapes=[pltpu.VMEM((10, SUB * SUB + SPARE, LANES), F32)],
        compiler_params=params(),
        cost_estimate=traffic(rows, 2),
        name="last_far",
    )(geo, pairs, far, old, sums)


LAST_PARTS = 4


def result_kernel(part_ref, terms_ref, out_hbm, native_ref, sems):
    part = part_ref.shape[1] // SUB // LAST_PARTS

    def copy(i):
        at = pl.ds(i * part * SUB * SUB, part * SUB * SUB)
        return pltpu.make_async_copy(native_ref.at[at], out_hbm.at[at], sems.at[i])

    def run(high):
        first = SUB - REACH if high else 0
        for i in range(LAST_PARTS):

            def group(j, _):
                at = at_rows(j * SUB)
                for g in range(SUB):
                    x = part_ref[g, at, :]
                    if 0 <= g - first < REACH:
                        x = x + terms_ref[g - first, at, :]
                    native_ref[pl.ds(j * SUB * SUB + g, SUB, stride=SUB), :] = x
                return 0

            lax.fori_loop(i * part, (i + 1) * part, group, 0, unroll=unroll(part, 4))
            copy(i).start()

    for_side(True, run)
    for i in range(LAST_PARTS):
        copy(i).wait()


def result(part, terms):
    rows = part.shape[1]
    native = (SUB * rows, LANES)
    return pl.pallas_call(
        result_kernel,
        in_specs=[spec(pltpu.VMEM)] * 2,
        out_specs=spec(pltpu.HBM),
        out_shape=array(*native),
        scratch_shapes=[pltpu.VMEM((SUB * rows + SPARE, LANES), F32), pltpu.SemaphoreType.DMA((LAST_PARTS,))],
        compiler_params=params(),
        cost_estimate=traffic(rows, 3),
        name="result",
    )(part, terms)


def swap(rows, start):
    pairs = [(i, i + 1) for i in range(start, lax.axis_size("space") - 1, 2)]
    return lax.ppermute(rows, "space", pairs + [(j, i) for i, j in pairs])


def per_device(particle_profile, neighbors, face_vectors, volumes, wall_temp):
    cells, points = particle_profile.shape
    rows = points // LANES
    plane_count = NV // lax.axis_size("vel")
    native = particle_profile.reshape(cells, rows, LANES).transpose(1, 0, 2).reshape(cells * rows, LANES)
    wall = neighbors < 0
    links = jnp.where(wall, WALL_LINK, neighbors - lax.axis_index("space") * cells)
    own = (links >= 0) & (links < cells)
    first = -SPEED_LIMIT + ((lax.axis_index("vel") * plane_count).astype(F32) + 0.5) * H
    geo = jnp.concatenate(
        [
            face_vectors.reshape(3 * FACES, cells),
            volumes[None],
            wall_temp[None],
            wall.astype(F32),
            own.astype(F32),
            jnp.full((1, cells), first, F32),
        ]
    )
    geo = jnp.broadcast_to(geo[:, :, None], (GEO, cells, LANES))
    native, far, near = first_rows(native)
    far, near = swap(far, 1), swap(near, 0)
    f, sums = first_sums(links, geo, native)
    tiles = gather_sums(sums)
    part, pairs = flux(True, links, geo, f)
    part, absorbed = add_target(links, geo, None, tiles, f, part)
    part, near = edge(False, pairs, near, f, part)
    near = swap(near, 0)
    f, far = edge(True, pairs, far, f, part)
    far = swap(far, 1)
    tiles = gather_sums(local_sums(links, geo, f))
    (part,) = flux(False, links, geo, f)
    (part,) = add_target(links, geo, absorbed, tiles, f, part)
    part, sums = last_near(geo, pairs, near, f, part)
    terms, sums = last_far(geo, pairs, far, f, sums)
    tiles = doubling_sums(sums)
    native = result(part, terms)
    macro_quantities = macro(tiles)
    evolved = native.reshape(rows, cells, LANES).transpose(1, 0, 2).reshape(cells, points)
    return evolved, macro_quantities


def solution(mesh):
    return jax.shard_map(
        per_device,
        mesh=mesh,
        in_specs=(
            P("space", "vel"),
            P(None, "space"),
            P(None, None, "space"),
            P("space"),
            P("space"),
        ),
        out_specs=(P("space", "vel"), P(None, "space")),
        check_vma=False,
    )
```

```python
import functools
import math

import jax
import jax.numpy as jnp
from jax import lax
from jax.experimental import pallas as pl
from jax.experimental.pallas import tpu as pltpu
from jax.sharding import PartitionSpec as P

NV = 64
FACES = 6
REACH = 3
STEPS = 2
LANES = 128
SUB = 8
SPARE = SUB

TIME_STEP = 0.015
SHEAR = 0.1
POWER = 0.81
SPEED_LIMIT = 6.0
H = 2.0 * SPEED_LIMIT / NV
WEIGHT = H**3 * (2.0 * math.pi) ** (-1.5)

CHUNKS = NV * NV // LANES
TILES = CHUNKS // SUB

FV, VOL, WT, WALL, LOCAL, FIRST = 0, 18, 19, 20, 26, 32
GEO = 33
WALL_LINK = -64
BEFORE_PAIRS = tuple((g, r) for g in range(REACH) for r in range(g, REACH))
EMIT, ABSORB = 13, 19
SUMS = 25

F32 = jnp.float32


def lane_iota():
    return lax.broadcasted_iota(jnp.int32, (SUB, LANES), 1)


def sub_iota():
    return lax.broadcasted_iota(jnp.int32, (SUB, LANES), 0)


def half_of(lane):
    return (lane >= NV).astype(F32)


def third_component(lane):
    c = jnp.where(lane >= NV, lane - NV, lane).astype(F32)
    return -SPEED_LIMIT + (c + 0.5) * H


def tile_nodes(t):
    lane = lane_iota()
    b = (2 * SUB * t + 2 * sub_iota()).astype(F32) + half_of(lane)
    return -SPEED_LIMIT + (b + 0.5) * H, third_component(lane)


def column(tile, p):
    return jnp.broadcast_to(tile[:, p : p + 1], (SUB, LANES))


def splat(ref, i, g):
    return jnp.broadcast_to(ref[i, pl.ds(g, 1), :], (SUB, LANES))


def total(tile):
    return jnp.broadcast_to(jnp.sum(tile, axis=1, keepdims=True), (SUB, LANES))


def face_coefficients(geo_ref, k, g):
    return [splat(geo_ref, FV + FACES * i + k, g) for i in range(3)]


def at_rows(start, size=SUB):
    return pl.ds(pl.multiple_of(start, SUB), size)


def wall_tiles(wall_temp):
    rt = 1.0 / wall_temp
    scale = rt * jnp.sqrt(rt)
    out = []
    for t in range(TILES):
        xb, xc = tile_nodes(t)
        out.append(scale * jnp.exp(-0.5 * (xb * xb + xc * xc) * rt))
    return out


def pack_sums(arrays, start):
    lane = lane_iota()
    out = jnp.zeros((SUB, LANES), F32)
    for p, x in enumerate(arrays):
        out = jnp.where(lane == start + p, total(x), out)
    return out


def over_sublanes(ref, k):
    out = ref[k, pl.ds(0, SUB, stride=SUB), :]
    for s in range(1, SUB):
        out = out + ref[k, pl.ds(s, SUB, stride=SUB), :]
    return out


def list_faces(links_ref, wanted, cell_ref, face_ref):
    count = 0
    for g in range(SUB):
        for k in range(FACES):
            cell_ref[count] = g
            face_ref[count] = k
            count = count + wanted(links_ref[k, g]).astype(jnp.int32)
    return count


def is_wall(j):
    return j == WALL_LINK


def is_remote(j):
    return jnp.logical_or(j >= SUB, jnp.logical_and(j < 0, j != WALL_LINK))


def face_lists():
    return [pltpu.SMEM((FACES * SUB + 1,), jnp.int32)] * 2


def unroll(planes, most):
    return math.gcd(planes, most)


def finish_polynomials(y, first, planes):
    y0, y1, y2, y3, by0, by1, by2, bby0, bby1, bbby0 = y
    m = first + 0.5 * (planes - 1) * H
    c = third_component(lane_iota())
    cc = c * c
    a = y1 + m * y0
    aa = y2 + m * (2.0 * y1 + m * y0)
    aaa = y3 + m * (3.0 * y2 + m * (3.0 * y1 + m * y0))
    ab = by1 + m * by0
    aab = by2 + m * (2.0 * by1 + m * by0)
    abb = bby1 + m * bby0
    return (
        y0,
        a,
        by0,
        c * y0,
        aa,
        bby0,
        cc * y0,
        ab,
        c * a,
        c * by0,
        aaa + abb + cc * a,
        aab + bbby0 + cc * by0,
        c * (aa + bby0 + cc * y0),
    )


def polynomial_sums(f_ref, planes, parts_ref, first=0):
    half = planes // 2

    def cell(g, _):
        out = [None] * 10
        for t in range(TILES):
            y0 = y1 = y2 = y3 = None
            for i in range(half):
                d = (i + 0.5) * H
                hi = f_ref[g, pl.ds(((half + i) * TILES + t) * SUB, SUB), :]
                lo = f_ref[g, pl.ds(((half - 1 - i) * TILES + t) * SUB, SUB), :]
                s, r = hi + lo, hi - lo
                if i == 0:
                    y0, y1, y2, y3 = s, d * r, (d * d) * s, (d * d * d) * r
                else:
                    y0, y1, y2, y3 = y0 + s, y1 + d * r, y2 + (d * d) * s, y3 + (d * d * d) * r
            b, _c = tile_nodes(t)
            bb = b * b
            terms = (y0, y1, y2, y3, b * y0, b * y1, b * y2, bb * y0, bb * y1, bb * (b * y0))
            out = [x if o is None else o + x for o, x in zip(out, terms)]
        for p in range(10):
            parts_ref[p, at_rows((first + g) * SUB), :] = out[p]
        return 0

    lax.fori_loop(0, f_ref.shape[0], cell, 0)
    return [over_sublanes(parts_ref, p) for p in range(10)]


def native_polynomial_sums(native_ref, planes):
    half, side = planes // 2, CHUNKS // 2
    zero = jnp.zeros((SUB, LANES), F32)
    acc = [zero] * 10

    def plane(a, acc):
        xa = (a.astype(F32) - 0.5 * (planes - 1)) * H
        b0 = b1 = b2 = b3 = None
        for i in range(side):
            y = (2 * i + 1) * H
            hi = native_ref[at_rows((a * CHUNKS + side + i) * SUB), :]
            lo = native_ref[at_rows((a * CHUNKS + side - 1 - i) * SUB), :]
            s, d = hi + lo, hi - lo
            terms = (s, y * d, (y * y) * s, (y * y * y) * d)
            if i == 0:
                b0, b1, b2, b3 = terms
            else:
                b0, b1, b2, b3 = b0 + terms[0], b1 + terms[1], b2 + terms[2], b3 + terms[3]
        a0, a1, a2 = xa * b0, xa * b1, xa * b2
        aa0 = xa * a0
        new = (b0, a0, aa0, xa * aa0, b1, a1, xa * a1, b2, a2, b3)
        return tuple(x + z for x, z in zip(acc, new))

    g0, a0, aa0, aaa0, g1, a1, aa1, g2, a2, g3 = lax.fori_loop(0, planes, plane, tuple(acc))
    e = (half_of(lane_iota()) - 0.5) * H
    return [
        g0,
        a0,
        aa0,
        aaa0,
        g1 + e * g0,
        a1 + e * a0,
        aa1 + e * aa0,
        g2 + e * (2.0 * g1 + e * g0),
        a2 + e * (2.0 * a1 + e * a0),
        g3 + e * (3.0 * g2 + e * (3.0 * g1 + e * g0)),
    ]


def wall_sums(f_ref, planes, links_ref, geo_ref, sums_ref, cells, faces, with_absorbed):
    sums_ref[...] = jnp.zeros_like(sums_ref)

    def wall(i, _):
        g, k = cells[i], faces[i]
        v0, v1, v2 = face_coefficients(geo_ref, k, g)
        first = splat(geo_ref, FIRST, g)
        base = []
        for t in range(TILES):
            xb, xc = tile_nodes(t)
            base.append(v1 * xb + v2 * xc)
        if with_absorbed:
            wt = splat(geo_ref, WT, g)
            shape = wall_tiles(wt)

        def plane(a, acc):
            out, back = list(acc[0]), list(acc[1])
            xa = first + a.astype(F32) * H
            sa = v0 * xa
            if with_absorbed:
                wa = jnp.exp(-0.5 * xa * xa / wt)
            for t in range(TILES):
                s = sa + base[t]
                f = f_ref[g, at_rows((a * TILES + t) * SUB), :]
                out[t] = out[t] + jnp.maximum(s, 0.0) * f
                if with_absorbed:
                    back[t] = back[t] + jnp.maximum(-s, 0.0) * (wa * shape[t])
            return tuple(out), tuple(back)

        zeros = (jnp.zeros((SUB, LANES), F32),) * TILES
        out, back = lax.fori_loop(0, planes, plane, (zeros, zeros), unroll=unroll(planes, 16))
        at = at_rows(g * SUB)
        sums_ref[k, at, :] = (out[0] + out[1]) + (out[2] + out[3])
        if with_absorbed:
            sums_ref[FACES + k, at, :] = (back[0] + back[1]) + (back[2] + back[3])
        return 0

    lax.fori_loop(0, list_faces(links_ref, is_wall, cells, faces), wall, 0)


def sums_kernel(links_ref, geo_ref, f_ref, sums_out, parts_ref, face_ref, cells, faces):
    planes = f_ref.shape[1] // CHUNKS
    y = polynomial_sums(f_ref, planes, parts_ref)
    packed = pack_sums(finish_polynomials(y, geo_ref[FIRST], planes), 0)
    wall_sums(f_ref, planes, links_ref, geo_ref, face_ref, cells, faces, False)
    sums_out[...] = packed + pack_sums([over_sublanes(face_ref, k) for k in range(FACES)], EMIT)


def first_sums_kernel(links_ref, geo_ref, native_ref, f_ref, sums_out, face_ref, cells, faces):
    rows = f_ref.shape[1]
    planes = rows // CHUNKS

    def group(j, _):
        for g in range(SUB):
            f_ref[g, at_rows(j * SUB), :] = native_ref[pl.ds(j * SUB * SUB + g, SUB, stride=SUB), :]
        return 0

    lax.fori_loop(0, rows // SUB, group, 0, unroll=2)
    y = native_polynomial_sums(native_ref, planes)
    packed = pack_sums(finish_polynomials(y, geo_ref[FIRST], planes), 0)
    wall_sums(f_ref, planes, links_ref, geo_ref, face_ref, cells, faces, True)
    sums_out[...] = packed + pack_sums([over_sublanes(face_ref, k) for k in range(2 * FACES)], EMIT)


def spec(space):
    return pl.BlockSpec(memory_space=space)


def array(*shape):
    return jax.ShapeDtypeStruct(shape, F32)


def params(mib=4):
    return pltpu.CompilerParams(vmem_limit_bytes=mib * 1024 * 1024)


def traffic(rows, profiles):
    size = SUB * rows * LANES
    return pl.CostEstimate(flops=8 * profiles * size, bytes_accessed=4 * profiles * size, transcendentals=0)


def local_sums(links, geo, f):
    return pl.pallas_call(
        sums_kernel,
        in_specs=[spec(pltpu.SMEM), spec(pltpu.VMEM), spec(pltpu.VMEM)],
        out_specs=spec(pltpu.VMEM),
        out_shape=array(SUB, LANES),
        scratch_shapes=[
                pltpu.VMEM((10, SUB * SUB + SPARE, LANES), F32),
            pltpu.VMEM((FACES, SUB * SUB + SPARE, LANES), F32),
            *face_lists(),
        ],
        compiler_params=params(),
        cost_estimate=traffic(f.shape[1], 4),
        name="local_sums",
    )(links, geo, f)


def first_sums(links, geo, native):
    rows = (native.shape[0] - SPARE) // SUB
    return pl.pallas_call(
        first_sums_kernel,
        in_specs=[spec(pltpu.SMEM), spec(pltpu.VMEM), spec(pltpu.VMEM)],
        out_specs=[spec(pltpu.VMEM)] * 2,
        out_shape=[array(SUB, rows, LANES), array(SUB, LANES)],
        scratch_shapes=[
                pltpu.VMEM((2 * FACES, SUB * SUB + SPARE, LANES), F32),
            *face_lists(),
        ],
        compiler_params=params(),
        cost_estimate=traffic(rows, 5),
        name="first_sums",
    )(links, geo, native)


SPLIT_PARTS = 8


def is_odd():
    return lax.rem(lax.axis_index("space"), 2) == 1


def first_rows_kernel(native_hbm, native_ref, far_any, near_any, far_ref, near_ref, sems, far_sems, near_sems):
    rows = native_hbm.shape[0]
    part = rows // SPLIT_PARTS
    copies = [
        pltpu.make_async_copy(
            native_hbm.at[pl.ds(i * part, part)], native_ref.at[pl.ds(i * part, part)], sems.at[i]
        )
        for i in range(SPLIT_PARTS)
    ]
    for c in copies:
        c.start()
    odd = is_odd()
    far = jnp.where(odd, SUB - REACH, 0)
    near = jnp.where(odd, 0, SUB - REACH)
    groups = part // (SUB * SUB)
    out = []

    for i, c in enumerate(copies):
        c.wait()

        def group(j, _):
            for r in range(REACH):
                at = at_rows(j * SUB)
                far_ref[r, at, :] = native_ref[pl.ds(j * SUB * SUB + far + r, SUB, stride=SUB), :]
                near_ref[r, at, :] = native_ref[pl.ds(j * SUB * SUB + near + r, SUB, stride=SUB), :]
            return 0

        lax.fori_loop(i * groups, (i + 1) * groups, group, 0, unroll=unroll(groups, 8))
        at = pl.ds(i * groups * SUB, groups * SUB)
        out.append(pltpu.make_async_copy(far_ref.at[:, at], far_any.at[:, at], far_sems.at[i]))
        out.append(pltpu.make_async_copy(near_ref.at[:, at], near_any.at[:, at], near_sems.at[i]))
        out[-2].start()
        out[-1].start()
    for c in out:
        c.wait()


def first_rows(native):
    rows = native.shape[0] // SUB
    halo = (REACH, rows, LANES)
    return pl.pallas_call(
        first_rows_kernel,
        in_specs=[spec(pltpu.HBM)],
        out_specs=[spec(pltpu.VMEM), spec(pl.ANY), spec(pl.ANY)],
        out_shape=[array(native.shape[0] + SPARE, LANES), array(*halo), array(*halo)],
        scratch_shapes=[pltpu.VMEM(halo, F32)] * 2 + [pltpu.SemaphoreType.DMA((SPLIT_PARTS,))] * 3,
        compiler_params=params(),
        cost_estimate=traffic(rows, 4),
        name="first_rows",
    )(pltpu.with_memory_space_constraint(native, pltpu.HBM))


def pair_weights(links_ref, geo_ref, pairs_ref, cells, faces):
    rows = pairs_ref.shape[1]
    planes = rows // CHUNKS
    first = splat(geo_ref, FIRST, 0)

    def clear(j, _):
        for p in range(pairs_ref.shape[0]):
            pairs_ref[p, at_rows(j * SUB), :] = jnp.zeros((SUB, LANES), F32)
        return 0

    lax.fori_loop(0, rows // SUB, clear, 0, unroll=4)

    def remote(i, _):
        g, k = cells[i], faces[i]
        j = links_ref[k, g]
        edge = g - (SUB - REACH)
        before = g * REACH - g * (g - 1) // 2 + (j + REACH) - g
        after = len(BEFORE_PAIRS) + edge * (edge + 1) // 2 + j - SUB
        at_pair = jnp.where(j < 0, before, after)
        scale = -TIME_STEP / splat(geo_ref, VOL, g)
        v0, v1, v2 = [scale * x for x in face_coefficients(geo_ref, k, g)]
        base = []
        for t in range(TILES):
            xb, xc = tile_nodes(t)
            base.append(v1 * xb + v2 * xc)

        def plane(a, _):
            sa = v0 * (first + a.astype(F32) * H)
            for t in range(TILES):
                at = at_rows((a * TILES + t) * SUB)
                pairs_ref[at_pair, at, :] = pairs_ref[at_pair, at, :] + jnp.maximum(sa + base[t], 0.0)
            return 0

        lax.fori_loop(0, planes, plane, 0, unroll=unroll(planes, 8))
        return 0

    lax.fori_loop(0, list_faces(links_ref, is_remote, cells, faces), remote, 0)


def gather_sums(tile):
    size = lax.axis_size("vel")
    if size not in (2, 4):
        return [lax.psum(tile, "vel")]
    others = [lax.ppermute(tile, "vel", [(i, i ^ s) for i in range(size)]) for s in range(1, size)]
    return [tile, *others]


def doubling_sums(tile):
    size = lax.axis_size("vel")
    if size != 4:
        return gather_sums(tile)
    pair = tile + lax.ppermute(tile, "vel", [(i, i ^ 1) for i in range(size)])
    return [pair, lax.ppermute(pair, "vel", [(i, i ^ 2) for i in range(size)])]


def add_tiles(refs):
    tiles = [r[...] for r in refs]
    while len(tiles) > 1:
        tiles = [tiles[i] + tiles[i + 1] for i in range(0, len(tiles), 2)]
    return tiles[0]


def quantities(sums):
    m = [WEIGHT * x for x in sums]
    n = m[0]
    rn = 1.0 / n
    u = [m[1 + i] * rn for i in range(3)]
    uu = u[0] * u[0] + u[1] * u[1] + u[2] * u[2]
    trace = m[4] + m[5] + m[6]
    width = trace - n * uu
    temperature = width * rn * (1.0 / 3.0)
    second = [[m[4], m[7], m[8]], [m[7], m[5], m[9]], [m[8], m[9], m[6]]]
    q = []
    for i in range(3):
        across = u[0] * second[i][0] + u[1] * second[i][1] + u[2] * second[i][2]
        q.append(0.5 * (m[10 + i] - 2.0 * across - u[i] * trace + 2.0 * uu * m[1 + i]))
    return n, u, temperature, q


def macro(tiles):
    by_sum = sum(tiles[1:], tiles[0])[:, :13].T
    n, u, temperature, q = quantities([by_sum[p] for p in range(13)])
    return jnp.stack([n, *u, temperature, *q])


def flux_kernel(with_pairs, links_ref, geo_ref, f_ref, out_ref, *refs):
    if with_pairs:
        pairs_ref, cells, faces = refs[0], refs[-2], refs[-1]
        pair_weights(links_ref, geo_ref, pairs_ref, cells, faces)
        refs = refs[1:-2]
    coef, bases, stays, source, face = refs
    planes = f_ref.shape[1] // CHUNKS
    scale = -TIME_STEP / geo_ref[VOL]
    for i in range(3):
        whole = None
        for k in range(FACES):
            x = scale * geo_ref[FV + FACES * i + k]
            coef[FACES * i + k] = x
            whole = x if whole is None else whole + x
        coef[3 * FACES + i] = whole

    def table(g, _):
        w = [[splat(coef, FACES * i + k, g) for i in (1, 2)] for k in range(FACES)]
        whole = [splat(coef, 3 * FACES + i, g) for i in (1, 2)]
        for t in range(TILES):
            xb, xc = tile_nodes(t)
            for k in range(FACES):
                bases[k, g * TILES + t] = w[k][0] * xb + w[k][1] * xc
            stays[g * TILES + t] = 1.0 + whole[0] * xb + whole[1] * xc
        return 0

    lax.fori_loop(0, SUB, table, 0, unroll=2)

    def cell(g, _):
        count = 0
        for k in range(FACES):
            j = links_ref[k, g]
            source[count] = j
            face[count] = k
            count = count + jnp.logical_and(j >= 0, j < SUB).astype(jnp.int32)
        for n in range(FACES + 1):

            @pl.when(count == n)
            def _():
                own_faces(g, n)

        return 0

    def own_faces(g, n):
        at_source = [source[i] for i in range(n)]
        first_weight = [splat(coef, face[k], g) for k in range(n)]
        whole = splat(coef, 3 * FACES, g)
        x0 = splat(geo_ref, FIRST, g)
        base = [[bases[face[k], g * TILES + t] for k in range(n)] for t in range(TILES)]
        stay = [stays[g * TILES + t] for t in range(TILES)]

        def plane(a, _):
            xa = x0 + a.astype(F32) * H
            sa = [w * xa for w in first_weight]
            stay_a = whole * xa
            for t in range(TILES):
                at = at_rows((a * TILES + t) * SUB)
                f = f_ref[g, at, :]
                acc = f * (stay_a + stay[t])
                for k in range(n):
                    acc = acc + jnp.maximum(sa[k] + base[t][k], 0.0) * (f_ref[at_source[k], at, :] - f)
                out_ref[g, at, :] = acc
            return 0

        lax.fori_loop(0, planes, plane, 0, unroll=unroll(planes, 8))

    lax.fori_loop(0, SUB, cell, 0)


def flux(with_pairs, links, geo, f):
    rows = f.shape[1]
    pairs = 2 * len(BEFORE_PAIRS)
    return pl.pallas_call(
        functools.partial(flux_kernel, with_pairs),
        in_specs=[spec(pltpu.SMEM), spec(pltpu.VMEM), spec(pltpu.VMEM)],
        out_specs=[spec(pltpu.VMEM)] * (2 if with_pairs else 1),
        out_shape=[array(*f.shape)] + ([array(pairs, rows, LANES)] if with_pairs else []),
        scratch_shapes=[
            pltpu.VMEM((3 * FACES + 3, SUB, LANES), F32),
            pltpu.VMEM((FACES, SUB * TILES, SUB, LANES), F32),
            pltpu.VMEM((SUB * TILES, SUB, LANES), F32),
            pltpu.SMEM((FACES + 1,), jnp.int32),
            pltpu.SMEM((FACES + 1,), jnp.int32),
        ]
        + (face_lists() if with_pairs else []),
        compiler_params=params(),
        cost_estimate=traffic(rows, 9 if with_pairs else 7),
        name="flux",
    )(links, geo, f)


def target_kernel(count, links_ref, geo_ref, absorbed_in, *refs):
    sums_refs, (f_ref, part_ref, out_ref, *sum_out, tiles_ref, coef, cells, faces) = refs[:count], refs[count:]
    planes = f_ref.shape[1] // CHUNKS
    sums = add_tiles(sums_refs)
    for ref in sum_out:
        ref[...] = sums
    absorbed = sums if absorbed_in is None else absorbed_in[...]
    n, u, temperature, q = quantities([column(sums, p) for p in range(13)])
    rt = 1.0 / temperature
    rate = TIME_STEP * n * temperature / (SHEAR * jnp.exp(POWER * jnp.log(temperature)))
    height = rate * n * rt * jnp.sqrt(rt)
    slope = (1.0 / 3.0) / (5.0 * n * temperature * temperature)
    coef[0] = rate
    coef[1] = rt
    coef[2], coef[3] = u[1], u[2]
    coef[4], coef[5] = slope * q[1], slope * q[2]
    coef[6], coef[7], coef[8] = u[0], slope * q[0], height
    for k in range(FACES):
        wall = geo_ref[WALL + k] > 0.5
        coef[9 + k] = column(sums, EMIT + k) / jnp.where(wall, column(absorbed, ABSORB + k), 1.0)

    def tile_table(g, _):
        rtg = splat(coef, 1, g)
        ub, uc = splat(coef, 2, g), splat(coef, 3, g)
        qb, qc = splat(coef, 4, g), splat(coef, 5, g)
        shape = wall_tiles(splat(geo_ref, WT, g))
        for t in range(TILES):
            xb, xc = tile_nodes(t)
            cb, cc = xb - ub, xc - uc
            z = (cb * cb + cc * cc) * rtg
            at = g * TILES + t
            tiles_ref[0, at] = jnp.exp(-0.5 * z)
            tiles_ref[1, at] = cb * qb + cc * qc
            tiles_ref[2, at] = z
            tiles_ref[3, at] = shape[t]
        return 0

    lax.fori_loop(0, SUB, tile_table, 0, unroll=4)

    def cell(g, _):
        rate_g, rtg, u0, q0, height_g = [splat(coef, i, g) for i in (0, 1, 6, 7, 8)]
        x0 = splat(geo_ref, FIRST, g) - u0
        bell, heat, zz = [[tiles_ref[i, g * TILES + t] for t in range(TILES)] for i in range(3)]

        def plane(a, _):
            ca = x0 + a.astype(F32) * H
            za = ca * ca * rtg
            height_a = height_g * jnp.exp(-0.5 * za)
            heat_a = q0 * ca
            z_a = za - 5.0
            for t in range(TILES):
                where = (g, at_rows((a * TILES + t) * SUB), slice(None))
                f = f_ref[where]
                target = (height_a * bell[t]) * (1.0 + (heat_a + heat[t]) * (z_a + zz[t]))
                out_ref[where] = (part_ref[where] - rate_g * f) + target
            return 0

        lax.fori_loop(0, planes, plane, 0, unroll=unroll(planes, 16))
        return 0

    lax.fori_loop(0, SUB, cell, 0)

    def wall(i, _):
        g, k = cells[i], faces[i]
        x0 = splat(geo_ref, FIRST, g)
        ratio = splat(coef, 9 + k, g)
        scale = -TIME_STEP / splat(geo_ref, VOL, g)
        v0, v1, v2 = [scale * x for x in face_coefficients(geo_ref, k, g)]
        base, shape = [], []
        for t in range(TILES):
            xb, xc = tile_nodes(t)
            base.append(v1 * xb + v2 * xc)
            shape.append(ratio * tiles_ref[3, g * TILES + t])

        rt_wall = -0.5 / splat(geo_ref, WT, g)

        def plane(a, _):
            xa = x0 + a.astype(F32) * H
            wa = jnp.exp(xa * xa * rt_wall)
            sa = v0 * xa
            for t in range(TILES):
                where = (g, at_rows((a * TILES + t) * SUB), slice(None))
                f = f_ref[where]
                out_ref[where] = out_ref[where] + jnp.maximum(sa + base[t], 0.0) * (wa * shape[t] - f)
            return 0

        lax.fori_loop(0, planes, plane, 0, unroll=unroll(planes, 16))
        return 0

    lax.fori_loop(0, list_faces(links_ref, is_wall, cells, faces), wall, 0)


def add_target(links, geo, absorbed, tiles, f, part):
    rows = f.shape[1]
    vmem = spec(pltpu.VMEM)
    given = [links, geo] + ([] if absorbed is None else [absorbed]) + list(tiles) + [f, part]

    def kernel(links_ref, geo_in, *refs):
        if absorbed is None:
            target_kernel(len(tiles), links_ref, geo_in, None, *refs)
        else:
            target_kernel(len(tiles), links_ref, geo_in, *refs)

    return pl.pallas_call(
        kernel,
        in_specs=[spec(pltpu.SMEM)] + [vmem] * (len(given) - 1),
        out_specs=[vmem] * (2 if absorbed is None else 1),
        out_shape=[array(*part.shape)] + ([array(SUB, LANES)] if absorbed is None else []),
        input_output_aliases={len(given) - 1: 0},
        scratch_shapes=[
                pltpu.VMEM((4, SUB * TILES, SUB, LANES), F32),
            pltpu.VMEM((9 + FACES, SUB, LANES), F32),
            *face_lists(),
        ],
        compiler_params=params(),
        cost_estimate=traffic(rows, 7),
        name="add_target",
    )(*given)


def side_terms(high, pairs_ref, halo_ref, f_ref, at):
    terms = [None] * REACH
    rows = [halo_ref[r, at, :] for r in range(REACH)]
    first = SUB - REACH if high else 0
    own = [f_ref[first + e, at, :] for e in range(REACH)]
    count = len(BEFORE_PAIRS)
    pairs = [(e, r) for e in range(REACH) for r in range(e + 1)] if high else BEFORE_PAIRS
    for p, (e, r) in enumerate(pairs):
        term = pairs_ref[p + count if high else p, at, :] * (rows[r] - own[e])
        terms[e] = term if terms[e] is None else terms[e] + term
    return first, terms


def for_side(far, run):
    odd = is_odd()

    @pl.when(odd)
    def _():
        run(far)

    @pl.when(jnp.logical_not(odd))
    def _():
        run(not far)


def add_side(far, pairs_ref, halo_ref, old_ref, part_ref, f_ref, rows_ref, ready=None):
    def run(high):
        def group(j, _):
            at = at_rows(j * SUB)
            first, terms = side_terms(high, pairs_ref, halo_ref, old_ref, at)
            for e in range(REACH):
                x = part_ref[first + e, at, :] + terms[e]
                f_ref[first + e, at, :] = x
                if rows_ref is not None:
                    rows_ref[e, at, :] = x
            return 0

        groups = part_ref.shape[1] // SUB
        parts = 1 if ready is None else EDGE_PARTS
        for i in range(parts):
            if ready is not None:
                ready(i)
            count = groups // parts
            lax.fori_loop(i * count, (i + 1) * count, group, 0, unroll=unroll(count, 8))

    for_side(far, run)


EDGE_PARTS = 4


def near_edge_kernel(pairs_ref, halo_any, old_ref, part_ref, f_ref, rows_ref, halo_ref, sems):
    size = halo_ref.shape[1] // EDGE_PARTS

    def copy(i):
        at = pl.ds(i * size, size)
        return pltpu.make_async_copy(halo_any.at[:, at], halo_ref.at[:, at], sems.at[i])

    for i in range(EDGE_PARTS):
        copy(i).start()
    add_side(False, pairs_ref, halo_ref, old_ref, part_ref, f_ref, rows_ref, lambda i: copy(i).wait())


def edge(far, pairs, halo, old, part):
    rows = part.shape[1]
    return pl.pallas_call(
        functools.partial(add_side, True) if far else near_edge_kernel,
        in_specs=[spec(pltpu.VMEM), spec(pltpu.VMEM if far else pl.ANY), spec(pltpu.VMEM), spec(pltpu.VMEM)],
        out_specs=[spec(pltpu.VMEM)] * 2,
        out_shape=[array(SUB, rows, LANES), array(REACH, rows, LANES)],
        input_output_aliases={3: 0},
        scratch_shapes=[] if far else [pltpu.VMEM(halo.shape, F32), pltpu.SemaphoreType.DMA((EDGE_PARTS,))],
        compiler_params=params(),
        cost_estimate=traffic(rows, 2),
        name="far_edge" if far else "near_edge",
    )(pairs, halo, old, part)


def last_near_kernel(geo_ref, pairs_ref, halo_ref, old_ref, part_ref, f_ref, sums_out, parts_ref):
    add_side(False, pairs_ref, halo_ref, old_ref, part_ref, f_ref, None)
    planes = f_ref.shape[1] // CHUNKS
    y = polynomial_sums(f_ref, planes, parts_ref)
    sums_out[...] = pack_sums(finish_polynomials(y, geo_ref[FIRST], planes), 0)


def last_near(geo, pairs, near, old, part):
    rows = part.shape[1]
    return pl.pallas_call(
        last_near_kernel,
        in_specs=[spec(pltpu.VMEM)] * 5,
        out_specs=[spec(pltpu.VMEM)] * 2,
        out_shape=[array(SUB, rows, LANES), array(SUB, LANES)],
        input_output_aliases={4: 0},
        scratch_shapes=[pltpu.VMEM((10, SUB * SUB + SPARE, LANES), F32)],
        compiler_params=params(),
        cost_estimate=traffic(rows, 3),
        name="last_near",
    )(geo, pairs, near, old, part)


def last_far_kernel(geo_ref, pairs_ref, halo_ref, old_ref, sums_in, terms_ref, sums_out, parts_ref):
    rows = old_ref.shape[1]
    planes = rows // CHUNKS
    parts_ref[...] = jnp.zeros_like(parts_ref)

    def run(high):
        def group(j, _):
            at = at_rows(j * SUB)
            _first, terms = side_terms(high, pairs_ref, halo_ref, old_ref, at)
            for e in range(REACH):
                terms_ref[e, at, :] = terms[e]
            return 0

        lax.fori_loop(0, rows // SUB, group, 0, unroll=unroll(rows // SUB, 8))
        y = polynomial_sums(terms_ref, planes, parts_ref, SUB - REACH if high else 0)
        sums_out[...] = sums_in[...] + pack_sums(finish_polynomials(y, geo_ref[FIRST], planes), 0)

    for_side(True, run)


def last_far(geo, pairs, far, old, sums):
    rows = old.shape[1]
    return pl.pallas_call(
        last_far_kernel,
        in_specs=[spec(pltpu.VMEM)] * 5,
        out_specs=[spec(pltpu.VMEM)] * 2,
        out_shape=[array(REACH, rows, LANES), array(SUB, LANES)],
        scratch_shapes=[pltpu.VMEM((10, SUB * SUB + SPARE, LANES), F32)],
        compiler_params=params(),
        cost_estimate=traffic(rows, 2),
        name="last_far",
    )(geo, pairs, far, old, sums)


LAST_PARTS = 4


def result_kernel(part_ref, terms_ref, out_hbm, native_ref, sems):
    part = part_ref.shape[1] // SUB // LAST_PARTS

    def copy(i):
        at = pl.ds(i * part * SUB * SUB, part * SUB * SUB)
        return pltpu.make_async_copy(native_ref.at[at], out_hbm.at[at], sems.at[i])

    def run(high):
        first = SUB - REACH if high else 0
        for i in range(LAST_PARTS):

            def group(j, _):
                at = at_rows(j * SUB)
                for g in range(SUB):
                    x = part_ref[g, at, :]
                    if 0 <= g - first < REACH:
                        x = x + terms_ref[g - first, at, :]
                    native_ref[pl.ds(j * SUB * SUB + g, SUB, stride=SUB), :] = x
                return 0

            lax.fori_loop(i * part, (i + 1) * part, group, 0, unroll=unroll(part, 4))
            copy(i).start()

    for_side(True, run)
    for i in range(LAST_PARTS):
        copy(i).wait()


def result(part, terms):
    rows = part.shape[1]
    native = (SUB * rows, LANES)
    return pl.pallas_call(
        result_kernel,
        in_specs=[spec(pltpu.VMEM)] * 2,
        out_specs=spec(pltpu.HBM),
        out_shape=array(*native),
        scratch_shapes=[pltpu.VMEM((SUB * rows + SPARE, LANES), F32), pltpu.SemaphoreType.DMA((LAST_PARTS,))],
        compiler_params=params(),
        cost_estimate=traffic(rows, 3),
        name="result",
    )(part, terms)


def swap(rows, start):
    pairs = [(i, i + 1) for i in range(start, lax.axis_size("space") - 1, 2)]
    return lax.ppermute(rows, "space", pairs + [(j, i) for i, j in pairs])


def per_device(particle_profile, neighbors, face_vectors, volumes, wall_temp):
    cells, points = particle_profile.shape
    rows = points // LANES
    plane_count = NV // lax.axis_size("vel")
    native = particle_profile.reshape(cells, rows, LANES).transpose(1, 0, 2).reshape(cells * rows, LANES)
    wall = neighbors < 0
    links = jnp.where(wall, WALL_LINK, neighbors - lax.axis_index("space") * cells)
    own = (links >= 0) & (links < cells)
    first = -SPEED_LIMIT + ((lax.axis_index("vel") * plane_count).astype(F32) + 0.5) * H
    geo = jnp.concatenate(
        [
            face_vectors.reshape(3 * FACES, cells),
            volumes[None],
            wall_temp[None],
            wall.astype(F32),
            own.astype(F32),
            jnp.full((1, cells), first, F32),
        ]
    )
    geo = jnp.broadcast_to(geo[:, :, None], (GEO, cells, LANES))
    native, far, near = first_rows(native)
    far, near = swap(far, 1), swap(near, 0)
    f, sums = first_sums(links, geo, native)
    tiles = gather_sums(sums)
    part, pairs = flux(True, links, geo, f)
    part, absorbed = add_target(links, geo, None, tiles, f, part)
    part, near = edge(False, pairs, near, f, part)
    near = swap(near, 0)
    f, far = edge(True, pairs, far, f, part)
    far = swap(far, 1)
    tiles = gather_sums(local_sums(links, geo, f))
    (part,) = flux(False, links, geo, f)
    (part,) = add_target(links, geo, absorbed, tiles, f, part)
    part, sums = last_near(geo, pairs, near, f, part)
    terms, sums = last_far(geo, pairs, far, f, sums)
    tiles = doubling_sums(sums)
    native = result(part, terms)
    macro_quantities = macro(tiles)
    evolved = native.reshape(rows, cells, LANES).transpose(1, 0, 2).reshape(cells, points)
    return evolved, macro_quantities


def solution(mesh):
    return jax.shard_map(
        per_device,
        mesh=mesh,
        in_specs=(
            P("space", "vel"),
            P(None, "space"),
            P(None, None, "space"),
            P("space"),
            P("space"),
        ),
        out_specs=(P("space", "vel"), P(None, "space")),
        check_vma=False,
    )
```
